32 devices in a mesh: section: 2 (over y), blk: 4 (over z), fsdp: 4 (over x, core).
Axes of the slice: x: 2, y: 2, z: 4, core: 2. Of those that a mesh axis runs over, the one named last changes fastest.
Arguments:
- tokens_in: bfloat16 [8, 1024, 896], P('fsdp', 'blk'), may hold values from -6 to 6
- positions: int32 [8, 1024], P('fsdp', 'blk'), may hold values from 0 to 511, as said below
- doc_ids: int32 [8, 1024], P('fsdp'), may hold values from 0 to 3, as said below
- out_grad: bfloat16 [8, 1024, 896], P('fsdp', 'blk'), may hold values from -6 to 6
- norm1_gain: float32 [2, 896], P('section'), may hold values from 0.25 to 1.75
- w_qkv: bfloat16 [2, 896, 1152], P('section', ('blk', 'fsdp')), may hold values from -0.1875 to 0.1875
- b_qkv: float32 [2, 1152], P('section'), may hold values from -1.25 to 1.25
- w_out: bfloat16 [2, 896, 896], P('section', ('blk', 'fsdp')), may hold values from -0.75 to 0.75
- norm2_gain: float32 [2, 896], P('section'), may hold values from 0.25 to 1.75
- w_gate_up: bfloat16 [2, 896, 9728], P('section', ('blk', 'fsdp')), may hold values from -0.1875 to 0.1875
- w_down: bfloat16 [2, 4864, 896], P('section', ('blk', 'fsdp')), may hold values from -0.078125 to 0.078125
Outputs:
- block_out: float32 [2, 8, 1024, 896], P('section', 'fsdp', 'blk')
- input_grad: float32 [2, 8, 1024, 896], P('section', 'fsdp', 'blk')
- grad_norm1_gain: float32 [2, 896], P('section')
- grad_w_qkv: float32 [2, 896, 1152], P('section', ('blk', 'fsdp'))
- grad_b_qkv: float32 [2, 1152], P('section')
- grad_w_out: float32 [2, 896, 896], P('section', ('blk', 'fsdp'))
- grad_norm2_gain: float32 [2, 896], P('section')
- grad_w_gate_up: float32 [2, 896, 9728], P('section', ('blk', 'fsdp'))
- grad_w_down: float32 [2, 4864, 896], P('section', ('blk', 'fsdp'))
The draws below stay inside these ranges and needn't reach their ends.
Inputs may be any that keep to these rules, and one draw needn't show every extreme that they name: `doc_ids`: each token's document number within its sequence: never falling, four documents in every sequence, exactly one of them of 512 tokens. `positions`: each token's place within its document, 0 at the document's first token.
All inputs are finite; a program needn't handle non-finite values.
Results may differ from the reference program's by a relative error of at most 0.017.
Values may be sent and summed in bfloat16 or wider, within the bound.
A program may use at most 320 MiB of HBM per device.

```python
import math
import jax
import jax.numpy as jnp
from jax import lax

D = 896
H = 14
KVH = 2
HD = 64
FF = 4864
L = 1024
QKV = 1152
SEQS = 8


def document_layout(key):
    base_key = jax.random.fold_in(key, 11)
    key_one, key_two, key_three = jax.random.split(base_key, 3)
    quarter = L // 4
    length_one = jax.random.randint(key_one, (SEQS, 1), 1, quarter)
    length_two = jax.random.randint(key_two, (SEQS, 1), 1, quarter)
    length_three = L // 2 - length_one - length_two
    pieces = jnp.concatenate([length_one, length_two, length_three], axis=1).astype(jnp.int32)
    filler = jnp.zeros((SEQS, 1), jnp.int32)
    before_long = jnp.concatenate([pieces, filler], axis=1)
    after_long = jnp.concatenate([filler, pieces], axis=1)
    longest = jax.random.randint(key_three, (SEQS, 1), 0, 4)
    slot_ids = jnp.arange(4, dtype=jnp.int32)[None, :]
    lengths = jnp.where(slot_ids == longest, L // 2, jnp.where(slot_ids < longest, before_long, after_long)).astype(jnp.int32)
    doc_ends = jnp.cumsum(lengths, axis=1)
    doc_starts = doc_ends - lengths
    token_index = jnp.arange(L, dtype=jnp.int32)
    documents = jnp.sum((token_index[None, :, None] >= doc_ends[:, None, :]).astype(jnp.int32), axis=2)
    one_hot = documents[:, :, None] == slot_ids[None, :, :]
    offsets = jnp.sum(jnp.where(one_hot, doc_starts[:, None, :], 0), axis=2)
    places = token_index[None, :] - offsets
    return (documents.astype(jnp.int32), places.astype(jnp.int32))


def draw_positions(key, part):
    return document_layout(key)[1]


def draw_doc_ids(key, part):
    return document_layout(key)[0]


def steps_of(rng, extent, cuts, least, largest):
    loudness, own = 1.0, jax.random.fold_in(rng, 6)
    for dim, parts in cuts:
        steps = jnp.exp(jax.random.uniform(jax.random.fold_in(own, dim), (parts,), jnp.float32, least / len(cuts), largest / len(cuts)))
        loudness = loudness * jnp.repeat(steps, extent[dim] // parts).reshape([-1 if axis == dim else 1 for axis in range(len(extent))])
    return loudness


def bell_draw(stream_key, dims, deviation, limit, cuts=(), kind=jnp.bfloat16):
    level = steps_of(stream_key, dims, cuts, -0.22, 0.18) if cuts else 1.0
    result = jax.random.normal(stream_key, dims, jnp.float32) * deviation * level
    return jnp.minimum(jnp.maximum(result, -limit), limit).astype(kind)


def setup_inputs(seed: int = 0) -> dict:
    key_of = jax.random.split(jax.random.key(seed), 12)
    return {
        "tokens_in": bell_draw(key_of[0], (SEQS, L, D), 1.0, 6.0, ((0, 4), (1, 4))),
        "positions": draw_positions(jax.random.fold_in(key_of[11], 71), 0),
        "doc_ids": draw_doc_ids(jax.random.fold_in(key_of[11], 71), 0),
        "out_grad": bell_draw(key_of[3], (SEQS, L, D), 1.0, 6.0, ((0, 4), (1, 4))),
        "norm1_gain": jnp.clip(1.0 + 0.15 * jax.random.normal(key_of[4], (2, D), jnp.float32), 0.25, 1.75),
        "w_qkv": bell_draw(key_of[5], (2, D, QKV), D ** -0.5, 0.1875, ((0, 2), (1, 16))),
        "b_qkv": bell_draw(key_of[6], (2, QKV), 0.2, 1.25, ((0, 2),), jnp.float32),
        "w_out": bell_draw(key_of[7], (2, H * HD, D), (D // 16) ** -0.5, 0.75, ((0, 2), (1, 16))),
        "norm2_gain": jnp.clip(1.0 + 0.15 * jax.random.normal(key_of[8], (2, D), jnp.float32), 0.25, 1.75),
        "w_gate_up": bell_draw(key_of[9], (2, D, 2 * FF), D ** -0.5, 0.1875, ((0, 2), (1, 16))),
        "w_down": bell_draw(key_of[10], (2, FF, D), FF ** -0.5, 0.078125, ((0, 2), (1, 16))),
    }


@jax.custom_vjp
def low(v):
    return lax.optimization_barrier(v.astype(jnp.bfloat16)).astype(jnp.float32)

@jax.custom_vjp
def low_back(v):
    return v

def low_keep(v):
    return (low(v), None)

def low_pass(kept, grad):
    return (grad,)

def back_keep(v):
    return (v, None)

def back_low(kept, grad):
    return (low(grad),)
low.defvjp(low_keep, low_pass)
low_back.defvjp(back_keep, back_low)

def matmul(left, right):
    return jnp.dot(left, right, precision=lax.Precision.HIGHEST, preferred_element_type=jnp.float32)

def normalize(values, gain):
    return values * lax.rsqrt(lax.optimization_barrier(jnp.mean(values * values, axis=-1, keepdims=True)) + 1e-06) * gain

def angles(positions):
    half_size = HD // 2
    freq = jnp.exp(jnp.arange(half_size, dtype=jnp.float32) * (-2.0 / HD) * math.log(1000000.0))
    phase = positions.astype(jnp.float32)[:, None] * freq[None, :]
    return (jnp.cos(phase)[:, None, :], jnp.sin(phase)[:, None, :])

def rotate(values, cos_part, sin_part):
    half_size = values.shape[-1] // 2
    part_one = values[..., :half_size]
    part_two = values[..., half_size:]
    return jnp.concatenate([part_one * cos_part - part_two * sin_part, part_two * cos_part + part_one * sin_part], axis=-1)

def allowed_keys(docs, row_start, row_count):
    query_rows = row_start + jnp.arange(row_count, dtype=jnp.int32)
    query_docs = lax.dynamic_slice_in_dim(docs, row_start, row_count)
    key_rows = jnp.arange(docs.shape[0], dtype=jnp.int32)
    return (key_rows[None, :] <= query_rows[:, None]) & (docs[None, :] == query_docs[:, None])

def attend(queries, key_heads, value_heads, docs):
    group_size = H // KVH
    block_rows = min(512, L)
    head_scale = HD ** (-0.5)
    query_blocks = queries.reshape(L // block_rows, block_rows, KVH, group_size, HD)
    block_starts = jnp.arange(L // block_rows, dtype=jnp.int32) * block_rows

    def one_block(block_args):
        query_block, row_start = block_args
        scores = jnp.einsum('tgjd,kgd->gjtk', query_block, key_heads, precision=lax.Precision.HIGHEST) * head_scale
        scores = low_back(scores)
        allowed = allowed_keys(docs, row_start, block_rows)
        scores = jnp.where(allowed[None, None], scores, -1e+30)
        top_score = lax.optimization_barrier(jnp.max(scores, axis=-1, keepdims=True))
        exponent = jnp.exp(scores - top_score)
        probabilities = low(exponent / lax.optimization_barrier(jnp.sum(exponent, axis=-1, keepdims=True)))
        return jnp.einsum('gjtk,kgd->tgjd', probabilities, value_heads, precision=lax.Precision.HIGHEST)
    attended = lax.map(jax.checkpoint(one_block), (query_blocks, block_starts))
    return attended.reshape(L, H * HD)

def layer(hidden, positions, docs, params):
    gain_one, weight_qkv, bias_qkv, weight_out, gain_two, weight_gate_up, weight_down = params
    attn_width = H * HD
    normed = low(normalize(hidden, gain_one))
    joined = low_back(matmul(normed, weight_qkv) + bias_qkv)
    cos_part, sin_part = angles(positions)
    queries = low(rotate(joined[:, :attn_width].reshape(L, H, HD), cos_part, sin_part))
    key_heads = low(rotate(joined[:, attn_width:attn_width + KVH * HD].reshape(L, KVH, HD), cos_part, sin_part))
    value_heads = low(joined[:, attn_width + KVH * HD:].reshape(L, KVH, HD))
    mixed_low = low(low_back(attend(queries, key_heads, value_heads, docs)))
    residual = hidden + low_back(matmul(mixed_low, weight_out))
    normed_two = low(normalize(residual, gain_two))
    gate_up = low_back(matmul(normed_two, weight_gate_up))
    gate_part = gate_up[:, :FF]
    up_part = gate_up[:, FF:]
    inner_low = low(gate_part * jax.nn.sigmoid(gate_part) * up_part)
    return residual + low_back(matmul(inner_low, weight_down))

def reference(tokens_in, positions, doc_ids, out_grad, norm1_gain, w_qkv, b_qkv, w_out, norm2_gain, w_gate_up, w_down):

    def section_params(section_number):
        return (norm1_gain[section_number], w_qkv[section_number].astype(jnp.float32), b_qkv[section_number], w_out[section_number].astype(jnp.float32), norm2_gain[section_number], w_gate_up[section_number].astype(jnp.float32), w_down[section_number].astype(jnp.float32))
    lower_params = section_params(0)
    upper_params = section_params(1)
    inputs = tokens_in.astype(jnp.float32)
    probe = jnp.zeros(inputs.shape, jnp.float32)

    def forward(inputs, probe, lower_params, upper_params):

        def per_sequence(seq_args):
            seq_in, seq_probe, seq_positions, seq_docs = seq_args
            lower_out = layer(seq_in, seq_positions, seq_docs, lower_params)
            upper_in = low_back(low(lower_out)) + seq_probe
            upper_out = layer(upper_in, seq_positions, seq_docs, upper_params)
            return (upper_out, lower_out)
        upper_out, lower_out = lax.map(per_sequence, (inputs, probe, positions, doc_ids))
        return (upper_out, lower_out)
    upper_out, pullback, lower_out = jax.vjp(forward, inputs, probe, lower_params, upper_params, has_aux=True)
    grad_inputs, grad_probe, grad_lower, grad_upper = pullback(out_grad.astype(jnp.float32))
    block_out = jnp.stack([lower_out, upper_out])
    input_grad = jnp.stack([grad_inputs, grad_probe])
    stacked = [jnp.stack([lower_grad, upper_grad]) for lower_grad, upper_grad in zip(grad_lower, grad_upper)]
    return (block_out, input_grad, stacked[0], stacked[1], stacked[2], stacked[3], stacked[4], stacked[5], stacked[6])
```

```python
import functools
import math

import jax
import jax.numpy as jnp
from jax import lax
from jax.experimental import pallas as pl
from jax.experimental.pallas import tpu as pltpu
from jax.sharding import PartitionSpec as P

H = 14
KVH = 2
HD = 64
GROUP = H // KVH
LONGEST = 512
NEG = -1e30
BF = jnp.bfloat16
F32 = jnp.float32
MESH = pl.DeviceIdType.MESH
VMEM_LIMIT = 60 * 2**20
VM = pl.BlockSpec(memory_space=pltpu.VMEM)
AN = pl.BlockSpec(memory_space=pl.ANY)


def nn(a, b):
    return lax.dot_general(a, b, (((1,), (0,)), ((), ())), preferred_element_type=F32)


def nt(a, b):
    return lax.dot_general(a, b, (((1,), (1,)), ((), ())), preferred_element_type=F32)


def tn(a, b):
    return lax.dot_general(a, b, (((0,), (0,)), ((), ())), preferred_element_type=F32)


def other(f):
    return f + 1 - 2 * (f % 2)


class Place:
    def __init__(self, dims):
        self.ns, self.nb, self.nf = dims
        self.count = self.ns * self.nf
        self.s = lax.axis_index("section")
        self.b = lax.axis_index("blk")
        self.f = lax.axis_index("fsdp")
        self.me = self.s * self.nf + self.f
        self.two_level = self.ns == 2 and self.nf == 4

    def plane(self, e):
        q = (self.me + e) % self.count
        return (q // self.nf, self.b, q % self.nf)

    def slot_from(self, e):
        return (self.me + self.count - e) % self.count

    def along(self, d):
        return (self.s, (self.b + d) % self.nb, self.f)

    def mates(self):
        s, b, f = (self.s, self.b, self.f)
        xf = (f + 2) % 4
        return ((s, b, other(f)), (s, b, xf), (1 - s, b, f))

    def slots(self):
        s, f = (self.s, self.f)
        xf = (f + 2) % 4
        t = 1 - s
        return (
            s * 4 + f,
            s * 4 + other(f),
            s * 4 + xf,
            t * 4 + f,
            s * 4 + other(xf),
            t * 4 + other(f),
            t * 4 + xf,
            t * 4 + other(xf),
        )


def pick(i, values):
    total = 0
    for k, v in enumerate(values):
        total = total + jnp.where(i == k, v, 0)
    return total


def greet(place, plane, along):
    barrier = pltpu.get_barrier_semaphore()
    count = 0
    if plane:
        if place.two_level and plane == "mates":
            targets = list(place.mates())
        else:
            targets = [place.plane(e) for e in range(1, place.count)]
        for t in targets:
            pl.semaphore_signal(barrier, 1, device_id=t, device_id_type=MESH)
        count += len(targets)
    if along:
        for d in range(1, place.nb):
            pl.semaphore_signal(barrier, 1, device_id=place.along(d), device_id_type=MESH)
        count += place.nb - 1
    pl.semaphore_wait(barrier, count)


def remote(src, dst, ssem, rsem, device):
    return pltpu.make_async_remote_copy(
        src_ref=src,
        dst_ref=dst,
        send_sem=ssem,
        recv_sem=rsem,
        device_id=device,
        device_id_type=MESH,
    )


class PlaneGather:
    def __init__(self, place, slot, ssem, rsem):
        self.place, self.slot, self.ssem, self.rsem = (place, slot, ssem, rsem)
        if place.two_level:
            self.order = place.slots()
        else:
            self.order = tuple(place.slot_from(e) for e in range(place.count))

    def copy(self, k, q, device):
        v = self.slot(q)
        return remote(v, v, self.ssem.at[k], self.rsem.at[k], device)

    def start(self):
        pc = self.place
        if pc.two_level:
            core, xm, ym = pc.mates()
            self.copy(1, self.order[0], xm).start()
            self.copy(2, self.order[0], ym).start()
            self.copy(0, self.order[0], core).start()
        else:
            for e in range(1, pc.count):
                self.copy(e - 1, self.order[0], pc.plane(e)).start()

    def waited(self, k):
        self.copy(k, self.order[k + 1], self.place.plane(1)).wait_recv()

    def before(self, step):
        if step == 0:
            return
        pc = self.place
        if not pc.two_level:
            self.waited(step - 1)
            return
        core, xm, ym = pc.mates()
        c = pc.f % 2
        if step == 2:
            self.waited(1)
            self.copy(3, self.order[2], core).start()
            self.waited(2)
            self.copy(4, self.order[3], core).start()
            which = c * self.order[3] + (1 - c) * self.order[2]
            far = (
                c * xm[0] + (1 - c) * ym[0],
                pc.b,
                c * xm[2] + (1 - c) * ym[2],
            )
            self.copy(5, which, far).start()
        elif step == 3:
            return
        elif step == 6:
            self.waited(5)
            self.copy(6, self.order[6], core).start()
        else:
            self.waited(step - 1)

    def finish(self):
        n = self.place.count - 1
        for k in range(n):
            self.copy(k, self.order[0], self.place.plane(1)).wait_send()


class PlaneScatter:
    def __init__(self, place, near, away, back, hop, ssem, rsem):
        self.place = place
        self.near, self.away, self.back, self.hop = (near, away, back, hop)
        self.ssem, self.rsem = (ssem, rsem)

    def put(self, step, value):
        pc = self.place
        if not pc.two_level:
            @pl.when(step == 0)
            def _():
                self.near[0] = value

            @pl.when(step > 0)
            def _():
                e = pc.count - step
                self.away[e - 1] = value.astype(BF)
                q = (pc.me + e) % pc.count
                remote(
                    self.away.at[e - 1],
                    self.back.at[e - 1],
                    self.ssem.at[e - 1],
                    self.rsem.at[e - 1],
                    (q // pc.nf, pc.b, q % pc.nf),
                ).start()
            return
        core, xm, ym = pc.mates()
        here = (step == 0) | (step == 2) | (step == 3) | (step == 6)
        q = pick(step, (0, 0, 1, 2, 1, 2, 3, 3))

        @pl.when(here)
        def _():
            self.near[q] = value

        @pl.when(jnp.logical_not(here))
        def _():
            self.away[q] = value.astype(BF)
            self.core_copy(q).start()

    def core_copy(self, q):
        core = self.place.mates()[0]
        return remote(self.away.at[q], self.back.at[q], self.ssem.at[q], self.rsem.at[q], core)

    def hop_copy(self, k, device):
        return remote(
            self.hop.at[k], self.hop.at[k + 3], self.ssem.at[4 + k], self.rsem.at[4 + k], device
        )

    def targets(self):
        pc = self.place
        core, xm, ym = pc.mates()
        c = pc.f % 2
        first = (c * xm[0] + (1 - c) * ym[0], pc.b, c * xm[2] + (1 - c) * ym[2])
        second = (c * ym[0] + (1 - c) * xm[0], pc.b, c * ym[2] + (1 - c) * xm[2])
        return (first, second)

    def early(self):
        pc = self.place
        if not pc.two_level:
            return
        c = pc.f % 2
        first, second = self.targets()
        self.core_copy(1).wait_recv()
        self.core_copy(2).wait_recv()
        q = c * 1 + (1 - c) * 2
        self.hop[0] = (self.near[q] + self.back[q].astype(F32)).astype(BF)
        self.hop_copy(0, first).start()

    def diagonal(self):
        pc = self.place
        if not pc.two_level:
            return
        first, second = self.targets()
        self.core_copy(3).wait_recv()
        self.hop[1] = (self.near[3] + self.back[3].astype(F32)).astype(BF)
        self.hop_copy(1, first).start()

    def result(self, store):
        pc = self.place
        if not pc.two_level:
            total = self.near[0]
            for e in range(1, pc.count):
                remote(self.away.at[e - 1], self.back.at[e - 1], self.ssem.at[e - 1],
                       self.rsem.at[e - 1], pc.plane(e)).wait()
                total = total + self.back[e - 1].astype(F32)
            store(total)
            return
        c = pc.f % 2
        first, second = self.targets()
        self.hop_copy(1, first).wait_recv()
        q = c * 2 + (1 - c) * 1
        self.hop[2] = (
            self.near[q] + self.back[q].astype(F32) + self.hop[4].astype(F32)
        ).astype(BF)
        self.hop_copy(2, second).start()
        self.core_copy(0).wait_recv()
        self.hop_copy(0, first).wait_recv()
        part = self.near[0] + self.back[0].astype(F32) + self.hop[3].astype(F32)
        self.near[0] = part
        self.hop_copy(2, second).wait_recv()
        store(self.near[0] + self.hop[5].astype(F32))
        for q in range(4):
            self.core_copy(q).wait_send()
        self.hop_copy(0, first).wait_send()
        self.hop_copy(1, first).wait_send()
        self.hop_copy(2, second).wait_send()


def scatter_scratch(dims, rows, cols):
    count = dims[0] * dims[2]
    if dims[0] == 2 and dims[2] == 4:
        near, away, hops, sems = (4, 4, 6, 7)
    else:
        near, away, hops, sems = (1, count - 1, 1, count - 1)
    return [
        pltpu.VMEM((near, rows, cols), F32),
        pltpu.VMEM((away, rows, cols), BF),
        pltpu.VMEM((away, rows, cols), BF),
        pltpu.VMEM((hops, rows, cols), BF),
        pltpu.SemaphoreType.DMA((sems,)),
        pltpu.SemaphoreType.DMA((sems,)),
    ]


def call(kernel, name, cid, outs, out_specs, in_specs, scratch, args):
    params = pltpu.CompilerParams(
        collective_id=cid, has_side_effects=True, vmem_limit_bytes=VMEM_LIMIT
    )
    return pl.pallas_call(
        kernel,
        name=name,
        out_shape=outs,
        in_specs=in_specs,
        out_specs=out_specs,
        scratch_shapes=scratch,
        compiler_params=params,
    )(*args)


def gather_weights_kernel(dims, gu, wd, qo, gu_all, wd_all, qo_all, lsem, ps, pr, zs, zr, qs, qr):
    pc = Place(dims)
    ns, nb, nf = dims
    greet(pc, "all", True)
    local = [
        pltpu.make_async_copy(qo, qo_all.at[pc.s, pc.f, pc.b], lsem.at[0]),
        pltpu.make_async_copy(gu.at[pc.s, pc.f], gu_all.at[pc.s, pc.b, pc.f], lsem.at[1]),
        pltpu.make_async_copy(wd.at[pc.s], wd_all.at[pc.s, pc.b], lsem.at[2]),
    ]
    mine = qo_all.at[pc.s, pc.f, pc.b]
    firsts = [remote(qo, mine, qs.at[d - 1], qr.at[d - 1], pc.along(d)) for d in range(1, nb)]
    for c in firsts:
        c.start()
    for c in local:
        c.start()
    plane = []
    for e in range(1, pc.count):
        t = pc.plane(e)
        plane.append(
            remote(gu.at[t[0], t[2]], gu_all.at[pc.s, pc.b, pc.f], ps.at[e - 1], pr.at[e - 1], t)
        )
    for d in range(1, ns):
        y = (pc.s + d) % ns
        k = pc.count - 1 + d - 1
        plane.append(
            remote(wd.at[y], wd_all.at[pc.s, pc.b], ps.at[k], pr.at[k], (y, pc.b, pc.f))
        )
    for c in plane:
        c.start()
    for c in local:
        c.wait()
    for c in firsts:
        c.wait()
    base = nb - 1
    gather = PlaneGather(
        pc,
        lambda q: qo_all.at[q // nf, q % nf],
        qs.at[pl.ds(base, pc.count - 1)],
        qr.at[pl.ds(base, pc.count - 1)],
    )
    gather.start()
    for c in plane:
        c.wait()
    lines = []
    k = 0
    for d in range(1, nb):
        for l in range(ns):
            for ref in (gu_all, wd_all):
                lines.append(
                    remote(ref.at[l, pc.b], ref.at[l, pc.b], zs.at[k], zr.at[k], pc.along(d))
                )
                k += 1
    for c in lines:
        c.start()
    for step in range(pc.count):
        gather.before(step)
    gather.finish()
    for c in lines:
        c.wait()


def gather_weights(dims, gu, wd, qo):
    ns, nb, nf = dims
    count = ns * nf
    half, width = wd.shape[1:]
    outs = (
        jax.ShapeDtypeStruct((ns, nb) + gu.shape[1:], BF),
        jax.ShapeDtypeStruct((ns, nb, half, width), BF),
        jax.ShapeDtypeStruct((ns, nf, nb) + qo.shape, BF),
    )
    dma = pltpu.SemaphoreType.DMA
    n_plane = count - 1 + ns - 1
    n_line = (nb - 1) * ns * 2
    n_qo = nb - 1 + count - 1
    return call(
        functools.partial(gather_weights_kernel, dims),
        "gather_weights",
        0,
        outs,
        [AN] * 3,
        [AN] * 3,
        [dma((3,)), dma((n_plane,)), dma((n_plane,)), dma((n_line,)), dma((n_line,)),
         dma((n_qo,)), dma((n_qo,))],
        (gu, wd, qo),
    )


def rms(values):
    return lax.rsqrt(jnp.mean(values * values, axis=0, keepdims=True) + 1e-06)


def attention_forward_kernel(
    dims, nk, h_ref, w_ref, wo_ref, bias_ref, g1_ref, g2_ref, cos_ref, sin_ref, mask_ref,
    normed_ref, q_ref, kv_ref, lse_ref, mixed_ref, res_ref, n2_ref,
    joined, ssem, rsem,
):
    pc = Place(dims)
    width, rows = h_ref.shape
    hidden = h_ref[...]
    normed = (hidden * rms(hidden) * g1_ref[...]).astype(BF)
    normed_ref[...] = normed
    joined[...] = tn(w_ref[...], normed) + bias_ref[...]
    cos_part = cos_ref[...]
    sin_part = sin_ref[...]
    half = HD // 2
    greet(pc, None, True)

    def turned(row):
        u1 = joined[pl.ds(row, half), :]
        u2 = joined[pl.ds(row + half, half), :]
        return (u1 * cos_part - u2 * sin_part, u2 * cos_part + u1 * sin_part)

    for g in range(KVH):
        r1, r2 = turned((H + g) * HD)
        kv_ref[0, g, :half, :] = r1.astype(BF)
        kv_ref[0, g, half:, :] = r2.astype(BF)
        v0 = (H + KVH + g) * HD
        kv_ref[0, KVH + g] = joined[v0 : v0 + HD, :].astype(BF)
    sends = [
        remote(kv_ref.at[0], kv_ref.at[j], ssem.at[j - 1], rsem.at[j - 1], pc.along(j))
        for j in range(1, nk)
    ]
    for c in sends:
        c.start()
    scale = HD**-0.5
    for head in range(H):
        r1, r2 = turned(head * HD)
        q_ref[head, :half, :] = (r1 * scale).astype(BF)
        q_ref[head, half:, :] = (r2 * scale).astype(BF)
    for c in sends:
        c.wait()
    for g in range(KVH):
        keys = [kv_ref[j, g].T for j in range(nk)]
        values = [kv_ref[j, KVH + g] for j in range(nk)]

        def one_head(i, carry):
            head = g * GROUP + i
            q = q_ref[head]
            s = [nn(keys[j], q) + mask_ref[j] for j in range(nk)]
            top = s[0].max(axis=0, keepdims=True)
            for j in range(1, nk):
                top = jnp.maximum(top, s[j].max(axis=0, keepdims=True))
            e = [jnp.exp(x - top) for x in s]
            total = e[0].sum(axis=0, keepdims=True)
            for j in range(1, nk):
                total = total + e[j].sum(axis=0, keepdims=True)
            out = nn(values[0], e[0].astype(BF))
            for j in range(1, nk):
                out = out + nn(values[j], e[j].astype(BF))
            lse_ref[head] = top + jnp.log(total)
            mixed_ref[head] = (out / total).astype(BF)
            return carry

        lax.fori_loop(0, GROUP, one_head, 0)
    mixed = mixed_ref[...].reshape(H * HD, rows)
    residual = h_ref[...] + tn(wo_ref[...], mixed)
    res_ref[...] = residual
    n2_ref[...] = (residual * rms(residual) * g2_ref[...]).astype(BF)


def attention_forward(dims, nk, cid, hidden, w, wo, bias, g1, g2, cos_part, sin_part, mask):
    width, rows = hidden.shape
    sds = jax.ShapeDtypeStruct
    outs = (
        sds((width, rows), BF),
        sds((H, HD, rows), BF),
        sds((nk, 2 * KVH, HD, rows), BF),
        sds((H, 1, rows), F32),
        sds((H, HD, rows), BF),
        sds((width, rows), F32),
        sds((width, rows), BF),
    )
    dma = pltpu.SemaphoreType.DMA
    return call(
        functools.partial(attention_forward_kernel, dims, nk),
        "attention_forward",
        cid,
        outs,
        [VM] * 7,
        [VM] * 9,
        [pltpu.VMEM((w.shape[1], rows), F32), dma((nk - 1,)), dma((nk - 1,))],
        (hidden, w, wo, bias, g1, g2, cos_part, sin_part, mask),
    )


def folded(v):
    out = v[:, :128]
    for k in range(1, v.shape[1] // 128):
        out = out + v[:, k * 128 : (k + 1) * 128]
    return out


def attention_backward_kernel(
    dims, nk, g_ref, w_ref, wo_ref, g1_ref, cos_ref, sin_ref, mask_ref,
    h_ref, normed_ref, q_ref, kv_ref, lse_ref, mixed_ref,
    gh_ref, dw_ref, dwo_ref, dg1_ref, db_ref,
    dmix, dkv, out_kv, in_kv, gj, ssem, rsem,
):
    pc = Place(dims)
    width, rows = h_ref.shape
    greet(pc, None, True)
    grl = g_ref[...].astype(BF)
    dmix[...] = nn(wo_ref[...], grl).astype(BF).reshape(dmix.shape)
    dwo_ref[...] = nt(mixed_ref[...].reshape(H * HD, rows), grl).astype(BF)
    cos_part = cos_ref[...]
    sin_part = sin_ref[...]
    half = HD // 2
    scale = HD**-0.5
    dkv[...] = jnp.zeros_like(dkv)

    def unturned(d1, d2):
        return (d1 * cos_part + d2 * sin_part, d2 * cos_part - d1 * sin_part)

    for g in range(KVH):
        keys_t = [kv_ref[j, g] for j in range(nk)]
        keys = [k.T for k in keys_t]
        values = [kv_ref[j, KVH + g].T for j in range(nk)]

        def one_head(i, carry):
            head = g * GROUP + i
            q = q_ref[head]
            do = dmix[head]
            lse = lse_ref[head]
            p = [jnp.exp(nn(keys[j], q) + mask_ref[j] - lse) for j in range(nk)]
            dp = [nn(values[j], do) for j in range(nk)]
            delta = (p[0] * dp[0]).sum(axis=0, keepdims=True)
            for j in range(1, nk):
                delta = delta + (p[j] * dp[j]).sum(axis=0, keepdims=True)
            dq = jnp.zeros((HD, rows), F32)
            for j in range(nk):
                ds = (p[j] * (dp[j] - delta)).astype(BF)
                dkv[j, g] += nt(q, ds)
                dkv[j, KVH + g] += nt(do, p[j].astype(BF))
                dq = dq + nn(keys_t[j], ds)
            dq = dq * scale
            r1, r2 = unturned(dq[:half], dq[half:])
            gj[pl.ds(pl.multiple_of(head * HD, HD), half), :] = r1.astype(BF)
            gj[pl.ds(pl.multiple_of(head * HD + half, half), half), :] = r2.astype(BF)
            return carry

        lax.fori_loop(0, GROUP, one_head, 0)
    for j in range(1, nk):
        out_kv[j - 1] = dkv[j].astype(BF)
    sends = [
        remote(out_kv.at[j - 1], in_kv.at[j - 1], ssem.at[j - 1], rsem.at[j - 1],
               pc.along(pc.nb - j))
        for j in range(1, nk)
    ]
    for c in sends:
        c.start()
    for c in sends:
        c.wait()
    own = dkv[0]
    for j in range(1, nk):
        own = own + in_kv[j - 1].astype(F32)
    for g in range(KVH):
        r1, r2 = unturned(own[g, :half], own[g, half:])
        k0 = (H + g) * HD
        gj[k0 : k0 + half, :] = r1.astype(BF)
        gj[k0 + half : k0 + HD, :] = r2.astype(BF)
        v0 = (H + KVH + g) * HD
        gj[v0 : v0 + HD, :] = own[KVH + g].astype(BF)
    gjv = gj[...]
    db_ref[...] = folded(gjv.astype(F32))
    dw_ref[...] = nt(normed_ref[...], gjv).astype(BF)
    gn = nn(w_ref[...], gjv)
    hidden = h_ref[...]
    scale_one = rms(hidden)
    unit = hidden * scale_one
    dg1_ref[...] = folded(gn * unit)
    u = gn * g1_ref[...]
    gh_ref[...] = g_ref[...] + scale_one * (u - unit * jnp.mean(u * unit, axis=0, keepdims=True))


def attention_backward(dims, nk, cid, g, w, wo, g1, cos_part, sin_part, mask, hidden, normed, q,
                       kv, lse, mixed):
    width, rows = hidden.shape
    sds = jax.ShapeDtypeStruct
    outs = (
        sds((width, rows), F32),
        sds(w.shape, BF),
        sds(wo.shape, BF),
        sds((width, 128), F32),
        sds((w.shape[1], 128), F32),
    )
    dma = pltpu.SemaphoreType.DMA
    block = (2 * KVH, HD, rows)
    return call(
        functools.partial(attention_backward_kernel, dims, nk),
        "attention_backward",
        cid,
        outs,
        [VM] * 5,
        [VM] * 13,
        [
            pltpu.VMEM((H, HD, rows), BF),
            pltpu.VMEM((nk,) + block, F32),
            pltpu.VMEM((nk - 1,) + block, BF),
            pltpu.VMEM((nk - 1,) + block, BF),
            pltpu.VMEM((w.shape[1], rows), BF),
            dma((nk - 1,)),
            dma((nk - 1,)),
        ],
        (g, w, wo, g1, cos_part, sin_part, mask, hidden, normed, q, kv, lse, mixed),
    )


def steps_of(count):
    return (5, count - 1)


def lanes(slot, rows):
    return pl.ds(pl.multiple_of(slot * rows, rows), rows)


def transpose_into(dst, src):
    cols = src.shape[1]
    for c0 in range(0, cols, 128):
        c1 = min(c0 + 128, cols)
        dst[c0:c1, :] = src[:, c0:c1].T


def feed_forward_kernel(
    dims, x_ref, res_ref, wgu_ref, wd_ref,
    out_ref, x_all, gu_all,
    wgu_t, wd_t, gu, inner, near, away, back, hop, ss, sr, gs, gr,
):
    pc = Place(dims)
    width, rows = x_ref.shape
    ff = wd_ref.shape[0]
    greet(pc, "mates", False)
    gather = PlaneGather(pc, lambda q: x_all.at[:, lanes(q, rows)], gs, gr)
    scatter = PlaneScatter(pc, near, away, back, hop, ss, sr)
    x_all[:, lanes(pc.me, rows)] = x_ref[...]
    gather.start()
    transpose_into(wgu_t, wgu_ref)
    transpose_into(wd_t, wd_ref)
    neighbours, last = steps_of(pc.count)
    chunk = 32 if ff % 32 == 0 else 16

    def step_body(step, carry):
        for k in range(pc.count):
            @pl.when(step == k)
            def _():
                gather.before(k)

        slot = pick(step, gather.order)
        sl = lanes(slot, rows)
        gu[...] = nn(wgu_t[...], x_all[:, sl])

        def act(i, c):
            r = pl.multiple_of(i * chunk, chunk)
            gate = gu[pl.ds(r, chunk), :]
            up = gu[pl.ds(ff + r, chunk), :]
            gu_all[pl.ds(r, chunk), sl] = gate.astype(BF)
            gu_all[pl.ds(ff + r, chunk), sl] = up.astype(BF)
            inner[pl.ds(r, chunk), :] = (gate * jax.nn.sigmoid(gate) * up).astype(BF)
            return c

        lax.fori_loop(0, ff // chunk, act, 0)
        scatter.put(step, nn(wd_t[...], inner[...]))

        @pl.when(step == neighbours)
        def _():
            scatter.early()

        return carry

    lax.fori_loop(0, pc.count, step_body, 0)
    scatter.diagonal()

    def store(total):
        out_ref[...] = res_ref[...] + total

    scatter.result(store)
    gather.finish()


def feed_forward(dims, cid, x, residual, wgu, wd):
    width, rows = x.shape
    count = dims[0] * dims[2]
    two_ff, ff = (wgu.shape[1], wd.shape[0])
    sds = jax.ShapeDtypeStruct
    dma = pltpu.SemaphoreType.DMA
    return call(
        functools.partial(feed_forward_kernel, dims),
        "feed_forward",
        cid,
        (
            sds((width, rows), F32),
            sds((width, count * rows), BF),
            sds((two_ff, count * rows), BF),
        ),
        [VM] * 3,
        [VM] * 4,
        [
            pltpu.VMEM((two_ff, width), BF),
            pltpu.VMEM((width, ff), BF),
            pltpu.VMEM((two_ff, rows), F32),
            pltpu.VMEM((ff, rows), BF),
        ]
        + scatter_scratch(dims, width, rows)
        + [dma((count - 1,)), dma((count - 1,))],
        (x, residual, wgu, wd),
    )


def feed_backward_kernel(
    dims, g_ref, res_ref, x_all, gu_all, wgu_ref, wd_ref, g2_ref,
    gr_ref, dwgu_ref, dwd_ref, dg2_ref,
    g_all, inner, ggu, gi, near, away, back, hop, ss, sr, gs, gr,
):
    pc = Place(dims)
    width, rows = g_ref.shape
    ff = wd_ref.shape[0]
    greet(pc, "mates", False)
    gather = PlaneGather(pc, lambda q: g_all.at[:, lanes(q, rows)], gs, gr)
    scatter = PlaneScatter(pc, near, away, back, hop, ss, sr)
    g_all[:, lanes(pc.me, rows)] = g_ref[...].astype(BF)
    gather.start()
    neighbours, last = steps_of(pc.count)
    chunk = 32 if ff % 32 == 0 else 16

    def step_body(step, carry):
        for k in range(pc.count):
            @pl.when(step == k)
            def _():
                gather.before(k)

        slot = pick(step, gather.order)
        sl = lanes(slot, rows)
        gi[...] = nn(wd_ref[...], g_all[:, sl])

        def act(i, c):
            r = pl.multiple_of(i * chunk, chunk)
            gate = gu_all[pl.ds(r, chunk), sl].astype(F32)
            up = gu_all[pl.ds(ff + r, chunk), sl].astype(F32)
            grad = gi[pl.ds(r, chunk), :]
            sig = jax.nn.sigmoid(gate)
            silu = gate * sig
            inner[pl.ds(r, chunk), sl] = (silu * up).astype(BF)
            ggu[pl.ds(r, chunk), sl] = (grad * up * sig * (1.0 + gate * (1.0 - sig))).astype(BF)
            ggu[pl.ds(ff + r, chunk), sl] = (grad * silu).astype(BF)
            return c

        lax.fori_loop(0, ff // chunk, act, 0)
        scatter.put(step, nn(wgu_ref[...], ggu[:, sl]))

        @pl.when(step == neighbours)
        def _():
            scatter.early()

        return carry

    lax.fori_loop(0, pc.count, step_body, 0)
    scatter.diagonal()
    part = width // 2
    for r in range(2):
        dwgu_ref[r * part : (r + 1) * part, :] = nt(
            x_all[r * part : (r + 1) * part, :], ggu[...]
        ).astype(BF)
    dwd_ref[...] = nt(inner[...], g_all[...]).astype(BF)

    def store(total):
        residual = res_ref[...]
        scale_two = rms(residual)
        unit = residual * scale_two
        dg2_ref[...] = folded(total * unit)
        u = total * g2_ref[...]
        gr_ref[...] = g_ref[...] + scale_two * (
            u - unit * jnp.mean(u * unit, axis=0, keepdims=True)
        )

    scatter.result(store)
    gather.finish()


def feed_backward(dims, cid, g, residual, x_all, gu_all, wgu, wd, g2):
    width, rows = g.shape
    count = dims[0] * dims[2]
    two_ff, ff = (wgu.shape[1], wd.shape[0])
    sds = jax.ShapeDtypeStruct
    dma = pltpu.SemaphoreType.DMA
    return call(
        functools.partial(feed_backward_kernel, dims),
        "feed_backward",
        cid,
        (
            sds((width, rows), F32),
            sds(wgu.shape, BF),
            sds(wd.shape, BF),
            sds((width, 128), F32),
        ),
        [VM] * 4,
        [VM] * 7,
        [
            pltpu.VMEM((width, count * rows), BF),
            pltpu.VMEM((ff, count * rows), BF),
            pltpu.VMEM((two_ff, count * rows), BF),
            pltpu.VMEM((ff, rows), F32),
        ]
        + scatter_scratch(dims, width, rows)
        + [dma((count - 1,)), dma((count - 1,))],
        (g, residual, x_all, gu_all, wgu, wd, g2),
    )


def line_exchange_kernel(dims, count, *refs):
    pc = Place(dims)
    ins, outs, (lsem, ss, sr) = (refs[:count], refs[count : 2 * count], refs[2 * count :])
    greet(pc, None, True)
    copies = []
    k = 0
    for i in range(count):
        copies.append(
            pltpu.make_async_copy(ins[i].at[pc.b], outs[i].at[pc.b], lsem.at[i])
        )
        for d in range(1, pc.nb):
            t = pc.along(d)
            copies.append(remote(ins[i].at[t[1]], outs[i].at[pc.b], ss.at[k], sr.at[k], t))
            k += 1
    for c in copies:
        c.start()
    for c in copies:
        c.wait()


def line_exchange(dims, cid, arrays):
    n = len(arrays)
    dma = pltpu.SemaphoreType.DMA
    total = n * (dims[1] - 1)
    return call(
        functools.partial(line_exchange_kernel, dims, n),
        "line_exchange",
        cid,
        tuple(jax.ShapeDtypeStruct(a.shape, a.dtype) for a in arrays),
        [AN] * n,
        [AN] * n,
        [dma((n,)), dma((total,)), dma((total,))],
        tuple(arrays),
    )


def plane_exchange_kernel(dims, gu, wd, gu_out, wd_out, lsem, ss, sr):
    pc = Place(dims)
    greet(pc, "all", False)
    copies = [
        pltpu.make_async_copy(gu.at[pc.me], gu_out.at[pc.me], lsem.at[0]),
        pltpu.make_async_copy(wd.at[pc.s], wd_out.at[pc.s], lsem.at[1]),
    ]
    for e in range(1, pc.count):
        t = pc.plane(e)
        copies.append(
            remote(gu.at[t[0] * pc.nf + t[2]], gu_out.at[pc.me], ss.at[e - 1], sr.at[e - 1], t)
        )
    for d in range(1, pc.ns):
        k = pc.count - 1 + d - 1
        y = (pc.s + d) % pc.ns
        copies.append(remote(wd.at[y], wd_out.at[pc.s], ss.at[k], sr.at[k], (y, pc.b, pc.f)))
    for c in copies:
        c.start()
    for c in copies:
        c.wait()


def plane_exchange(dims, cid, gu, wd):
    dma = pltpu.SemaphoreType.DMA
    total = dims[0] * dims[2] - 1 + dims[0] - 1
    return call(
        functools.partial(plane_exchange_kernel, dims),
        "plane_exchange",
        cid,
        tuple(jax.ShapeDtypeStruct(a.shape, a.dtype) for a in (gu, wd)),
        [AN] * 2,
        [AN] * 2,
        [dma((2,)), dma((total,)), dma((total,))],
        (gu, wd),
    )


def small_reduce_kernel(
    dims, qo_ref, small_ref, qo_out, small_out,
    half_sum, z_out, z_in, sm_in, sm_mid, sm_line, near, away, back, hop, ss, sr, ps, pr, zs, zr, ws, wr,
):
    pc = Place(dims)
    ns, nb, nf = dims
    greet(pc, "all", True)
    smalls = [
        remote(small_ref, sm_in.at[e - 1], ps.at[e - 1], pr.at[e - 1], pc.plane(e))
        for e in range(1, pc.count)
    ]
    for c in smalls:
        c.start()
    scatter = PlaneScatter(pc, near, away, back, hop, ss, sr)
    if pc.two_level:
        order = pc.slots()
    else:
        order = tuple(pc.slot_from(e) for e in range(pc.count))
    neighbours, last = steps_of(pc.count)

    def step_body(step, carry):
        slot = pick(step, order)
        scatter.put(step, qo_ref[slot].astype(F32))

        @pl.when(step == neighbours)
        def _():
            scatter.early()

        return carry

    lax.fori_loop(0, pc.count, step_body, 0)
    scatter.diagonal()
    total = small_ref[...]
    for e, c in enumerate(smalls):
        c.wait()
        total = total + sm_in[e]
    sm_mid[...] = total
    lines = [
        remote(sm_mid, sm_line.at[d - 1], ws.at[d - 1], wr.at[d - 1], pc.along(d))
        for d in range(1, nb)
    ]
    for c in lines:
        c.start()

    def store(value):
        half_sum[...] = value

    scatter.result(store)
    part = half_sum.shape[0] // nb
    z_out[...] = half_sum[...].astype(BF).reshape(z_out.shape)
    sends = []
    for d in range(1, nb):
        t = pc.along(d)
        sends.append(
            remote(z_out.at[t[1]], z_in.at[d - 1], zs.at[d - 1], zr.at[d - 1], t)
        )
    for c in sends:
        c.start()
    mine = z_out[pc.b].astype(F32)
    for d, c in enumerate(sends):
        c.wait()
        mine = mine + z_in[d].astype(F32)
    qo_out[...] = mine
    total = sm_mid[...]
    for d, c in enumerate(lines):
        c.wait()
        total = total + sm_line[d]
    small_out[...] = total


def small_reduce(dims, cid, qo, small, dr):
    ns, nb, nf = dims
    count = ns * nf
    cols = qo.shape[2]
    sds = jax.ShapeDtypeStruct
    dma = pltpu.SemaphoreType.DMA
    return call(
        functools.partial(small_reduce_kernel, dims),
        "small_reduce",
        cid,
        (sds((dr, cols), F32), sds(small.shape, F32)),
        [VM] * 2,
        [VM] * 2,
        [
            pltpu.VMEM((nb * dr, cols), F32),
            pltpu.VMEM((nb, dr, cols), BF),
            pltpu.VMEM((nb - 1, dr, cols), BF),
            pltpu.VMEM((count - 1,) + small.shape, F32),
            pltpu.VMEM(small.shape, F32),
            pltpu.VMEM((nb - 1,) + small.shape, F32),
        ]
        + scatter_scratch(dims, nb * dr, cols)
        + [dma((count - 1,)), dma((count - 1,))]
        + [dma((nb - 1,))] * 4,
        (qo, small),
    )


def shards(
    dims,
    tokens_in,
    positions,
    doc_ids,
    out_grad,
    norm1_gain,
    w_qkv,
    b_qkv,
    w_out,
    norm2_gain,
    w_gate_up,
    w_down,
):
    ns, nb, nf = dims
    seqs, rows, width = tokens_in.shape
    length = doc_ids.shape[1]
    s = lax.axis_index("section")
    b = lax.axis_index("blk")
    dr = w_qkv.shape[1]
    qkv = w_qkv.shape[2]
    fr = w_down.shape[1]
    half = fr // ns
    ff = nb * half
    nk = min(nb, 1 + (LONGEST - 1 + rows - 1) // rows)

    gu = w_gate_up[0].reshape(dr, 2, nb, nf, ns, half).transpose(4, 3, 0, 1, 2, 5)
    gu = gu.reshape(ns, nf, dr, 2 * ff)
    wd = w_down[0].reshape(ns, half, width)
    qo = jnp.concatenate([w_qkv[0], w_out[0]], axis=1)
    gu_all, wd_all, qo_all = gather_weights(dims, gu, wd, qo)
    wgu = gu_all.reshape(ns, width, 2 * ff)
    wdn = wd_all.reshape(ns, ff, width)
    qo_all = qo_all.transpose(0, 2, 1, 3, 4).reshape(ns, width, qkv + width)
    wq = qo_all[:, :, :qkv]
    wo = qo_all[:, :, qkv:]

    small_in = jnp.concatenate([norm1_gain[0], norm2_gain[0], b_qkv[0]])
    small_all = lax.all_gather(small_in, "section", axis=0, tiled=False)
    g1 = small_all[:, :width, None]
    g2 = small_all[:, width : 2 * width, None]
    bias = small_all[:, 2 * width :, None]

    tokens = lax.dynamic_index_in_dim(tokens_in, s, 0, keepdims=False)
    cot = lax.dynamic_index_in_dim(out_grad, s, 0, keepdims=False)
    pos = lax.dynamic_index_in_dim(positions, s, 0, keepdims=False)
    docs = lax.dynamic_index_in_dim(doc_ids, s, 0, keepdims=False)
    freq = jnp.exp(jnp.arange(HD // 2, dtype=F32) * (-2.0 / HD) * math.log(1000000.0))
    phase = freq[:, None] * pos.astype(F32)[None, :]
    cos_part, sin_part = (jnp.cos(phase), jnp.sin(phase))
    query_rows = b * rows + jnp.arange(rows, dtype=jnp.int32)
    query_docs = lax.dynamic_slice_in_dim(docs, b * rows, rows)
    masks = []
    for j in range(nk):
        key_rows = (b - j) * rows + jnp.arange(rows, dtype=jnp.int32)
        start = lax.rem(b - j + nb, nb) * rows
        key_docs = lax.dynamic_slice_in_dim(docs, start, rows)
        live = (
            (key_rows[:, None] >= 0)
            & (key_rows[:, None] <= query_rows[None, :])
            & (key_docs[:, None] == query_docs[None, :])
        )
        masks.append(jnp.where(live, 0.0, NEG).astype(F32))
    mask = jnp.stack(masks)

    hidden = tokens.T.astype(F32)
    saved = []
    outputs = []
    for l in range(ns):
        normed, q, kv, lse, mixed, residual, n2 = attention_forward(
            dims, nk, 1 + l, hidden, wq[l], wo[l], bias[l], g1[l], g2[l], cos_part, sin_part, mask
        )
        out, x_all, gu_saved = feed_forward(dims, 3 + l, n2, residual, wgu[l], wdn[l])
        saved.append((hidden, normed, q, kv, lse, mixed, residual, x_all, gu_saved))
        outputs.append(out)
        hidden = out.astype(BF).astype(F32)
    g = cot.T.astype(F32)
    grads = [None] * ns
    line_in = []
    qo_terms = [None] * ns
    small_terms = [None] * ns
    for l in reversed(range(ns)):
        hidden, normed, q, kv, lse, mixed, residual, x_all, gu_saved = saved[l]
        gres, dwgu, dwd, dg2 = feed_backward(
            dims, 5 + l, g, residual, x_all, gu_saved, wgu[l], wdn[l], g2[l]
        )
        gh, dwq, dwo, dg1, db = attention_backward(
            dims, nk, 7 + l, gres, wq[l], wo[l], g1[l], cos_part, sin_part, mask, hidden, normed, q,
            kv, lse, mixed,
        )
        grads[l] = gh
        g = gh.astype(BF).astype(F32)
        line_in.append((dwgu.reshape(nb, nf * dr, 2 * ff), dwd.reshape(nb, half, width)))
        qo_terms[l] = jnp.concatenate([dwq, dwo], axis=1)
        small_terms[l] = jnp.concatenate([dg1.sum(1), dg2.sum(1), db.sum(1)])
    line_in.reverse()

    got = line_exchange(dims, 9, [a for pair in line_in for a in pair])
    summed = [a.astype(F32).sum(0) for a in got]
    gu_send = jnp.stack([summed[2 * l].reshape(nf, dr, 2 * ff) for l in range(ns)]).astype(BF)
    wd_send = jnp.stack([summed[2 * l + 1] for l in range(ns)]).astype(BF)
    gu_got, wd_got = plane_exchange(dims, 10, gu_send.reshape(ns * nf, dr, 2 * ff), wd_send)
    grad_gu = gu_got.reshape(ns, nf, dr, 2, nb, half).transpose(2, 3, 4, 1, 0, 5)
    grad_gu = grad_gu.reshape(dr, w_gate_up.shape[2]).astype(F32)
    grad_wd = wd_got.reshape(fr, width).astype(F32)
    qo_send = jnp.stack(qo_terms).reshape(ns, nb, nf, dr, qkv + width)
    qo_send = qo_send.transpose(0, 2, 1, 3, 4).reshape(ns * nf, nb * dr, qkv + width)
    small = jnp.stack(small_terms)
    small_size = small.shape[1]
    padded = -(-small_size // 1024) * 1024
    small = jnp.pad(small, ((0, 0), (0, padded - small_size))).reshape(-1, 128)
    grad_qo, small_sum = small_reduce(dims, 11, qo_send, small, dr)
    small_sum = small_sum.reshape(ns, padded)
    mine = lax.dynamic_index_in_dim(small_sum, s, 0, keepdims=False)

    def both(values):
        own = jnp.stack(values)
        keep = lax.dynamic_index_in_dim(own, s, 0, keepdims=False)
        give = lax.dynamic_index_in_dim(own, 1 - s, 0, keepdims=False)
        take = lax.ppermute(give.astype(BF), "section", [(0, 1), (1, 0)]).astype(F32)
        first = jnp.where(s == 0, keep, take).T
        second = jnp.where(s == 0, take, keep).T
        return jnp.stack([first, second])[None]

    return (
        both(outputs),
        both(grads),
        mine[None, :width],
        grad_qo[None, :, :qkv],
        mine[None, 2 * width : 2 * width + qkv],
        grad_qo[None, :, qkv:],
        mine[None, width : 2 * width],
        grad_gu[None],
        grad_wd[None],
    )


def solution(mesh):
    dims = (mesh.shape["section"], mesh.shape["blk"], mesh.shape["fsdp"])
    return jax.shard_map(
        functools.partial(shards, dims),
        mesh=mesh,
        in_specs=(
            P("fsdp", "blk", None),
            P("fsdp", "blk"),
            P("fsdp", None),
            P("fsdp", "blk", None),
            P("section", None),
            P("section", ("blk", "fsdp"), None),
            P("section", None),
            P("section", ("blk", "fsdp"), None),
            P("section", None),
            P("section", ("blk", "fsdp"), None),
            P("section", ("blk", "fsdp"), None),
        ),
        out_specs=(
            P("section", "fsdp", "blk", None),
            P("section", "fsdp", "blk", None),
            P("section", None),
            P("section", ("blk", "fsdp"), None),
            P("section", None),
            P("section", ("blk", "fsdp"), None),
            P("section", None),
            P("section", ("blk", "fsdp"), None),
            P("section", ("blk", "fsdp"), None),
        ),
        check_vma=False,
    )
```

```python
import functools
import math

import jax
import jax.numpy as jnp
from jax import lax
from jax.experimental import pallas as pl
from jax.experimental.pallas import tpu as pltpu
from jax.sharding import PartitionSpec as P

H = 14
KVH = 2
HD = 64
GROUP = H // KVH
LONGEST = 512
NEG = -1e30
BF = jnp.bfloat16
F32 = jnp.float32
MESH = pl.DeviceIdType.MESH
VMEM_LIMIT = 60 * 2**20
VM = pl.BlockSpec(memory_space=pltpu.VMEM)
AN = pl.BlockSpec(memory_space=pl.ANY)


def nn(a, b):
    return lax.dot_general(a, b, (((1,), (0,)), ((), ())), preferred_element_type=F32)


def nt(a, b):
    return lax.dot_general(a, b, (((1,), (1,)), ((), ())), preferred_element_type=F32)


def tn(a, b):
    return lax.dot_general(a, b, (((0,), (0,)), ((), ())), preferred_element_type=F32)


def other(f):
    return f + 1 - 2 * (f % 2)


class Place:
    def __init__(self, dims):
        self.ns, self.nb, self.nf = dims
        self.count = self.ns * self.nf
        self.s = lax.axis_index("section")
        self.b = lax.axis_index("blk")
        self.f = lax.axis_index("fsdp")
        self.me = self.s * self.nf + self.f
        self.two_level = self.ns == 2 and self.nf == 4

    def plane(self, e):
        q = (self.me + e) % self.count
        return (q // self.nf, self.b, q % self.nf)

    def slot_from(self, e):
        return (self.me + self.count - e) % self.count

    def along(self, d):
        return (self.s, (self.b + d) % self.nb, self.f)

    def mates(self):
        s, b, f = (self.s, self.b, self.f)
        xf = (f + 2) % 4
        return ((s, b, other(f)), (s, b, xf), (1 - s, b, f))

    def slots(self):
        s, f = (self.s, self.f)
        xf = (f + 2) % 4
        t = 1 - s
        return (
            s * 4 + f,
            s * 4 + other(f),
            s * 4 + xf,
            t * 4 + f,
            s * 4 + other(xf),
            t * 4 + other(f),
            t * 4 + xf,
            t * 4 + other(xf),
        )


def pick(i, values):
    total = 0
    for k, v in enumerate(values):
        total = total + jnp.where(i == k, v, 0)
    return total


def greet(place, plane, along):
    barrier = pltpu.get_barrier_semaphore()
    count = 0
    if plane:
        if place.two_level and plane == "mates":
            targets = list(place.mates())
        else:
            targets = [place.plane(e) for e in range(1, place.count)]
        for t in targets:
            pl.semaphore_signal(barrier, 1, device_id=t, device_id_type=MESH)
        count += len(targets)
    if along:
        for d in range(1, place.nb):
            pl.semaphore_signal(barrier, 1, device_id=place.along(d), device_id_type=MESH)
        count += place.nb - 1
    pl.semaphore_wait(barrier, count)


def remote(src, dst, ssem, rsem, device):
    return pltpu.make_async_remote_copy(
        src_ref=src,
        dst_ref=dst,
        send_sem=ssem,
        recv_sem=rsem,
        device_id=device,
        device_id_type=MESH,
    )


class PlaneGather:
    def __init__(self, place, slot, ssem, rsem):
        self.place, self.slot, self.ssem, self.rsem = (place, slot, ssem, rsem)
        if place.two_level:
            self.order = place.slots()
        else:
            self.order = tuple(place.slot_from(e) for e in range(place.count))

    def copy(self, k, q, device):
        v = self.slot(q)
        return remote(v, v, self.ssem.at[k], self.rsem.at[k], device)

    def start(self):
        pc = self.place
        if pc.two_level:
            core, xm, ym = pc.mates()
            self.copy(1, self.order[0], xm).start()
            self.copy(2, self.order[0], ym).start()
            self.copy(0, self.order[0], core).start()
        else:
            for e in range(1, pc.count):
                self.copy(e - 1, self.order[0], pc.plane(e)).start()

    def waited(self, k):
        self.copy(k, self.order[k + 1], self.place.plane(1)).wait_recv()

    def before(self, step):
        if step == 0:
            return
        pc = self.place
        if not pc.two_level:
            self.waited(step - 1)
            return
        core, xm, ym = pc.mates()
        c = pc.f % 2
        if step == 2:
            self.waited(1)
            self.copy(3, self.order[2], core).start()
            self.waited(2)
            self.copy(4, self.order[3], core).start()
            which = c * self.order[3] + (1 - c) * self.order[2]
            far = (
                c * xm[0] + (1 - c) * ym[0],
                pc.b,
                c * xm[2] + (1 - c) * ym[2],
            )
            self.copy(5, which, far).start()
        elif step == 3:
            return
        elif step == 6:
            self.waited(5)
            self.copy(6, self.order[6], core).start()
        else:
            self.waited(step - 1)

    def finish(self):
        n = self.place.count - 1
        for k in range(n):
            self.copy(k, self.order[0], self.place.plane(1)).wait_send()


class PlaneScatter:
    def __init__(self, place, near, away, back, hop, ssem, rsem):
        self.place = place
        self.near, self.away, self.back, self.hop = (near, away, back, hop)
        self.ssem, self.rsem = (ssem, rsem)

    def put(self, step, value):
        pc = self.place
        if not pc.two_level:
            @pl.when(step == 0)
            def _():
                self.near[0] = value

            @pl.when(step > 0)
            def _():
                e = pc.count - step
                self.away[e - 1] = value.astype(BF)
                q = (pc.me + e) % pc.count
                remote(
                    self.away.at[e - 1],
                    self.back.at[e - 1],
                    self.ssem.at[e - 1],
                    self.rsem.at[e - 1],
                    (q // pc.nf, pc.b, q % pc.nf),
                ).start()
            return
        core, xm, ym = pc.mates()
        here = (step == 0) | (step == 2) | (step == 3) | (step == 6)
        q = pick(step, (0, 0, 1, 2, 1, 2, 3, 3))

        @pl.when(here)
        def _():
            self.near[q] = value

        @pl.when(jnp.logical_not(here))
        def _():
            self.away[q] = value.astype(BF)
            self.core_copy(q).start()

    def core_copy(self, q):
        core = self.place.mates()[0]
        return remote(self.away.at[q], self.back.at[q], self.ssem.at[q], self.rsem.at[q], core)

    def hop_copy(self, k, device):
        return remote(
            self.hop.at[k], self.hop.at[k + 3], self.ssem.at[4 + k], self.rsem.at[4 + k], device
        )

    def targets(self):
        pc = self.place
        core, xm, ym = pc.mates()
        c = pc.f % 2
        first = (c * xm[0] + (1 - c) * ym[0], pc.b, c * xm[2] + (1 - c) * ym[2])
        second = (c * ym[0] + (1 - c) * xm[0], pc.b, c * ym[2] + (1 - c) * xm[2])
        return (first, second)

    def early(self):
        pc = self.place
        if not pc.two_level:
            return
        c = pc.f % 2
        first, second = self.targets()
        self.core_copy(1).wait_recv()
        self.core_copy(2).wait_recv()
        q = c * 1 + (1 - c) * 2
        self.hop[0] = (self.near[q] + self.back[q].astype(F32)).astype(BF)
        self.hop_copy(0, first).start()

    def diagonal(self):
        pc = self.place
        if not pc.two_level:
            return
        first, second = self.targets()
        self.core_copy(3).wait_recv()
        self.hop[1] = (self.near[3] + self.back[3].astype(F32)).astype(BF)
        self.hop_copy(1, first).start()

    def result(self, store):
        pc = self.place
        if not pc.two_level:
            total = self.near[0]
            for e in range(1, pc.count):
                remote(self.away.at[e - 1], self.back.at[e - 1], self.ssem.at[e - 1],
                       self.rsem.at[e - 1], pc.plane(e)).wait()
                total = total + self.back[e - 1].astype(F32)
            store(total)
            return
        c = pc.f % 2
        first, second = self.targets()
        self.hop_copy(1, first).wait_recv()
        q = c * 2 + (1 - c) * 1
        self.hop[2] = (
            self.near[q] + self.back[q].astype(F32) + self.hop[4].astype(F32)
        ).astype(BF)
        self.hop_copy(2, second).start()
        self.core_copy(0).wait_recv()
        self.hop_copy(0, first).wait_recv()
        part = self.near[0] + self.back[0].astype(F32) + self.hop[3].astype(F32)
        self.near[0] = part
        self.hop_copy(2, second).wait_recv()
        store(self.near[0] + self.hop[5].astype(F32))
        for q in range(4):
            self.core_copy(q).wait_send()
        self.hop_copy(0, first).wait_send()
        self.hop_copy(1, first).wait_send()
        self.hop_copy(2, second).wait_send()


class LineGather:
    def __init__(self, place, piece, out, sems):
        lsem, ss, sr = sems
        own = out.at[place.b]
        self.copies = [pltpu.make_async_copy(piece, own, lsem)]
        for d in range(1, place.nb):
            self.copies.append(remote(piece, own, ss.at[d - 1], sr.at[d - 1], place.along(d)))

    def start(self):
        for c in self.copies:
            c.start()

    def finish(self):
        for c in self.copies:
            c.wait()


class LineExchange(LineGather):
    def __init__(self, place, parts, out, sems):
        lsem, ss, sr = sems
        own = out(place.b)
        self.copies = [pltpu.make_async_copy(parts(place.b), own, lsem)]
        for d in range(1, place.nb):
            t = place.along(d)
            self.copies.append(remote(parts(t[1]), own, ss.at[d - 1], sr.at[d - 1], t))


def line_sems(dims):
    dma = pltpu.SemaphoreType.DMA
    return [dma(()), dma((dims[1] - 1,)), dma((dims[1] - 1,))]


def riders_of(place, specs, ins, outs, sems):
    out = []
    for i, spec in enumerate(specs):
        mine = sems[3 * i : 3 * i + 3]
        if spec[0] == "gather":
            piece = ins[i] if spec[1] is None else ins[i].at[spec[1]]
            out.append(LineGather(place, piece, outs[i], mine))
        else:
            lo, hi = spec[1]
            out.append(
                LineExchange(
                    place,
                    lambda t, r=ins[i]: r.at[t, lo:hi],
                    lambda t, r=outs[i]: r.at[t],
                    mine,
                )
            )
    return out


def rider_shapes(dims, specs, arrays):
    out = []
    for spec, a in zip(specs, arrays):
        if spec[0] == "gather":
            shape = a.shape if spec[1] is None else a.shape[1:]
            out.append(jax.ShapeDtypeStruct((dims[1],) + shape, a.dtype))
        else:
            lo, hi = spec[1]
            out.append(jax.ShapeDtypeStruct((a.shape[0], hi - lo) + a.shape[2:], a.dtype))
    return out


def scatter_scratch(dims, *block):
    count = dims[0] * dims[2]
    if dims[0] == 2 and dims[2] == 4:
        near, away, hops, sems = (4, 4, 6, 7)
    else:
        near, away, hops, sems = (1, count - 1, 1, count - 1)
    return [
        pltpu.VMEM((near,) + block, F32),
        pltpu.VMEM((away,) + block, BF),
        pltpu.VMEM((away,) + block, BF),
        pltpu.VMEM((hops,) + block, BF),
        pltpu.SemaphoreType.DMA((sems,)),
        pltpu.SemaphoreType.DMA((sems,)),
    ]


def call(kernel, name, cid, outs, out_specs, in_specs, scratch, args):
    params = pltpu.CompilerParams(
        collective_id=cid, has_side_effects=True, vmem_limit_bytes=VMEM_LIMIT
    )
    return pl.pallas_call(
        kernel,
        name=name,
        out_shape=outs,
        in_specs=in_specs,
        out_specs=out_specs,
        scratch_shapes=scratch,
        compiler_params=params,
    )(*args)


def column_start(dims, part, b, f, y, half):
    ns, nb, nf = dims
    return part * nb * nf * ns * half + ((b * nf + f) * ns + y) * half


def gather_weights_kernel(
    dims, w_ref, wd, qo, small, gup, wdp, gu_first, qo_all, small_all,
    pack, lsem, ps, pr, zs, zr, qs, qr, ms, mr, *rest
):
    pc = Place(dims)
    ns, nb, nf = dims
    half = wd.shape[1]
    greet(pc, "all", True)
    firsts = []
    for d in range(1, nb):
        firsts.append(
            remote(qo, qo_all.at[pc.s, pc.b, pc.f], zs.at[d - 1], zr.at[d - 1], pc.along(d))
        )
        firsts[-1].start()
    local = [
        pltpu.make_async_copy(qo, qo_all.at[pc.s, pc.b, pc.f], lsem.at[0]),
        pltpu.make_async_copy(wd.at[pc.s], wdp.at[pc.s], lsem.at[1]),
        pltpu.make_async_copy(small, small_all.at[pc.s], lsem.at[2]),
    ]
    for c in local:
        c.start()
    across = []
    for d in range(1, ns):
        y = (pc.s + d) % ns
        t = (y, pc.b, pc.f)
        across.append(remote(wd.at[y], wdp.at[pc.s], ms.at[2 * d - 2], mr.at[2 * d - 2], t))
        across.append(remote(small, small_all.at[pc.s], ms.at[2 * d - 1], mr.at[2 * d - 1], t))
    for c in across:
        c.start()
    for y in range(ns):
        for f in range(nf):
            pieces = []
            for part in range(2):
                for b in range(nb):
                    c0 = column_start(dims, part, b, f, y, half)
                    pieces.append(w_ref[0, :, c0 : c0 + half])
            pack[y, f] = jnp.concatenate(pieces, axis=1)
    own = pltpu.make_async_copy(pack.at[pc.s, pc.f], gup.at[pc.s, pc.f], lsem.at[3])
    own.start()
    plane = []
    for e in range(1, pc.count):
        t = pc.plane(e)
        plane.append(
            remote(pack.at[t[0], t[2]], gup.at[pc.s, pc.f], ps.at[e - 1], pr.at[e - 1], t)
        )
    for c in plane:
        c.start()
    n = pc.count - 1
    gathers = []
    for d in range(nb):
        b = (pc.b + nb - d) % nb
        gathers.append(
            PlaneGather(
                pc,
                lambda q, b=b: qo_all.at[q // nf, b, q % nf],
                qs.at[pl.ds(d * n, n)],
                qr.at[pl.ds(d * n, n)],
            )
        )
    local[0].wait()
    gathers[0].start()
    own.wait()
    for c in plane:
        c.wait()
    line = LineGather(pc, gup.at[0], gu_first, rest)
    line.start()
    for d in range(1, nb):
        firsts[d - 1].wait()
        gathers[d].start()
        for step in range(1, min(6, pc.count)):
            gathers[d - 1].before(step)
    for step in range(1, min(6, pc.count)):
        gathers[nb - 1].before(step)
    for step in range(min(6, pc.count), pc.count):
        for g in gathers:
            g.before(step)
    for g in gathers:
        g.finish()
    for c in local[1:]:
        c.wait()
    for c in across:
        c.wait()
    line.finish()


def gather_weights(dims, w, wd, qo, small):
    ns, nb, nf = dims
    count = ns * nf
    half, width = wd.shape[1:]
    dr = qo.shape[0]
    two_ff = 2 * nb * half
    sds = jax.ShapeDtypeStruct
    outs = (
        sds((ns, nf, dr, two_ff), BF),
        sds((ns, half, width), BF),
        sds((nb, nf, dr, two_ff), BF),
        sds((ns, nb, nf) + qo.shape, BF),
        sds((ns,) + small.shape, F32),
    )
    dma = pltpu.SemaphoreType.DMA
    return call(
        functools.partial(gather_weights_kernel, dims),
        "gather_weights",
        0,
        outs,
        [AN] * 5,
        [VM, AN, AN, AN],
        [
            pltpu.VMEM((ns, nf, dr, two_ff), BF),
            dma((4,)),
            dma((count - 1,)),
            dma((count - 1,)),
            dma((nb - 1,)),
            dma((nb - 1,)),
            dma((nb * (count - 1),)),
            dma((nb * (count - 1),)),
            dma((2 * (ns - 1),)),
            dma((2 * (ns - 1),)),
        ]
        + line_sems(dims),
        (w, wd, qo, small),
    )


def rms(values):
    return lax.rsqrt(jnp.mean(values * values, axis=0, keepdims=True) + 1e-06)


def column(rows_t, first, count):
    return jnp.concatenate([rows_t[:, k : k + 1] for k in range(first, first + count)], axis=0)


def rows_of(values):
    v = folded(values)
    return jnp.concatenate(
        [v[k : k + 128].T.sum(axis=0, keepdims=True) for k in range(0, v.shape[0], 128)], axis=0
    )


def folded(v):
    out = v[:, :128]
    for k in range(1, v.shape[1] // 128):
        out = out + v[:, k * 128 : (k + 1) * 128]
    return out


def fill_masks(pc, mask, meta_t, query_docs):
    nk, rows = mask.shape[:2]
    key_i = lax.broadcasted_iota(jnp.int32, (rows, rows), 0)
    query_i = lax.broadcasted_iota(jnp.int32, (rows, rows), 1)
    per = rows // 128
    for j in range(nk):
        same = column(meta_t, j * per, per) == query_docs
        if j == 0:
            live = same & (key_i <= query_i)
        else:
            live = same & (key_i < (pc.b - j + 1) * rows)
        mask[j] = jnp.where(live, 0.0, NEG)


def load_qo(qo_all, layer, w, wo, sems):
    cols = w.shape[1]
    c1 = pltpu.make_async_copy(qo_all.at[layer, :, 0:cols], w, sems.at[0])
    c2 = pltpu.make_async_copy(qo_all.at[layer, :, cols : cols + wo.shape[1]], wo, sems.at[1])
    c1.start()
    c2.start()
    return (c1, c2)


def gains_of(small_t, width, qkv):
    n = width // 128
    return (
        column(small_t, 0, n),
        column(small_t, n, n),
        column(small_t, 2 * n, qkv // 128),
    )


def padded_t(v):
    n = v.shape[0]
    return jnp.concatenate([v, jnp.zeros((128 - n, 128), v.dtype)], axis=0).T


def attention_forward_kernel(
    dims, nk, layer, specs, h_ref, small_ref, meta_ref, docs_ref, cos_ref, sin_ref, qo_all, *refs
):
    n = len(specs)
    ins, refs = (refs[:n], refs[n:])
    normed_ref, q_ref, kv_ref, lse_ref, mixed_ref, res_ref, n2_ref = refs[:7]
    outs, refs = (refs[7 : 7 + n], refs[7 + n :])
    w, wo, mask, joined, ssem, rsem, qsem = refs[:7]
    pc = Place(dims)
    width, rows = h_ref.shape
    loads = load_qo(qo_all, layer, w, wo, qsem)
    greet(pc, None, True)
    riders = riders_of(pc, specs, ins, outs, refs[7:])
    g1, g2, bias = gains_of(padded_t(small_ref[layer]), width, w.shape[1])
    hidden = h_ref[...].astype(BF).astype(F32)
    normed = (hidden * rms(hidden) * g1).astype(BF)
    normed_ref[...] = normed
    fill_masks(pc, mask, padded_t(meta_ref[...]), docs_ref[...])
    loads[0].wait()
    joined[...] = tn(w[...], normed) + bias
    cos_part = cos_ref[...]
    sin_part = sin_ref[...]
    half = HD // 2

    def turned(row):
        u1 = joined[pl.ds(row, half), :]
        u2 = joined[pl.ds(row + half, half), :]
        return (u1 * cos_part - u2 * sin_part, u2 * cos_part + u1 * sin_part)

    for g in range(KVH):
        r1, r2 = turned((H + g) * HD)
        kv_ref[0, g, :half, :] = r1.astype(BF)
        kv_ref[0, g, half:, :] = r2.astype(BF)
        v0 = (H + KVH + g) * HD
        kv_ref[0, KVH + g] = joined[v0 : v0 + HD, :].astype(BF)
    sends = [
        remote(kv_ref.at[0], kv_ref.at[j], ssem.at[j - 1], rsem.at[j - 1], pc.along(j))
        for j in range(1, nk)
    ]
    for c in sends:
        c.start()
    for r in riders:
        r.start()
    scale = HD**-0.5
    for head in range(H):
        r1, r2 = turned(head * HD)
        q_ref[head, :half, :] = (r1 * scale).astype(BF)
        q_ref[head, half:, :] = (r2 * scale).astype(BF)
    for c in sends:
        c.wait()
    for g in range(KVH):
        keys = [kv_ref[j, g].T for j in range(nk)]
        values = [kv_ref[j, KVH + g] for j in range(nk)]

        def one_head(i, carry):
            head = g * GROUP + i
            q = q_ref[head]
            s = [nn(keys[j], q) + mask[j] for j in range(nk)]
            top = s[0].max(axis=0, keepdims=True)
            for j in range(1, nk):
                top = jnp.maximum(top, s[j].max(axis=0, keepdims=True))
            e = [jnp.exp(x - top) for x in s]
            total = e[0].sum(axis=0, keepdims=True)
            for j in range(1, nk):
                total = total + e[j].sum(axis=0, keepdims=True)
            out = nn(values[0], e[0].astype(BF))
            for j in range(1, nk):
                out = out + nn(values[j], e[j].astype(BF))
            lse_ref[head] = top + jnp.log(total)
            mixed_ref[head] = (out / total).astype(BF)
            return carry

        lax.fori_loop(0, GROUP, one_head, 0)
    mixed = mixed_ref[...].reshape(H * HD, rows)
    loads[1].wait()
    residual = hidden + tn(wo[...], mixed)
    res_ref[...] = residual
    n2_ref[...] = (residual * rms(residual) * g2).astype(BF)
    for r in riders:
        r.finish()


def attention_forward(dims, nk, cid, layer, hidden, small, meta, docs, cos_part, sin_part, qo_all,
                      specs, riders):
    width, rows = hidden.shape
    qkv = qo_all.shape[2] - width
    sds = jax.ShapeDtypeStruct
    outs = [
        sds((width, rows), BF),
        sds((H, HD, rows), BF),
        sds((nk, 2 * KVH, HD, rows), BF),
        sds((H, 1, rows), F32),
        sds((H, HD, rows), BF),
        sds((width, rows), F32),
        sds((width, rows), BF),
    ] + rider_shapes(dims, specs, riders)
    dma = pltpu.SemaphoreType.DMA
    n = len(specs)
    out = call(
        functools.partial(attention_forward_kernel, dims, nk, layer, specs),
        "attention_forward",
        cid,
        tuple(outs),
        [VM] * 7 + [AN] * n,
        [VM] * 6 + [AN] * (1 + n),
        [
            pltpu.VMEM((width, qkv), BF),
            pltpu.VMEM((width, width), BF),
            pltpu.VMEM((nk, rows, rows), F32),
            pltpu.VMEM((qkv, rows), F32),
            dma((nk - 1,)),
            dma((nk - 1,)),
            dma((2,)),
        ]
        + line_sems(dims) * n,
        (hidden, small, meta, docs, cos_part, sin_part, qo_all, *riders),
    )
    return (out[:7], out[7:])


def attention_backward_kernel(
    dims, nk, layer, specs, g_ref, small_ref, meta_ref, docs_ref, cos_ref, sin_ref,
    h_ref, normed_ref, q_ref, kv_ref, lse_ref, mixed_ref, qo_all, *refs
):
    n = len(specs)
    ins, refs = (refs[:n], refs[n:])
    gh_ref, dqo_ref, dsmall_ref = refs[:3]
    outs, refs = (refs[3 : 3 + n], refs[3 + n :])
    w, wo, mask, dmix, dkv, out_kv, in_kv, gj, ssem, rsem, qsem = refs[:11]
    pc = Place(dims)
    width, rows = h_ref.shape
    qkv = w.shape[1]
    loads = load_qo(qo_all, layer, w, wo, qsem)
    greet(pc, None, True)
    riders = riders_of(pc, specs, ins, outs, refs[11:])
    for r in riders:
        r.start()
    g1 = column(padded_t(small_ref[layer]), 0, width // 128)
    fill_masks(pc, mask, padded_t(meta_ref[...]), docs_ref[...])
    grl = g_ref[...].astype(BF)
    loads[1].wait()
    dmix[...] = nn(wo[...], grl).astype(BF).reshape(dmix.shape)
    dqo_ref[:, qkv:] = nt(mixed_ref[...].reshape(H * HD, rows), grl).astype(BF)
    cos_part = cos_ref[...]
    sin_part = sin_ref[...]
    half = HD // 2
    scale = HD**-0.5
    dkv[...] = jnp.zeros_like(dkv)

    def unturned(d1, d2):
        return (d1 * cos_part + d2 * sin_part, d2 * cos_part - d1 * sin_part)

    for g in range(KVH):
        keys_t = [kv_ref[j, g] for j in range(nk)]
        keys = [k.T for k in keys_t]
        values = [kv_ref[j, KVH + g].T for j in range(nk)]

        def one_head(i, carry):
            head = g * GROUP + i
            q = q_ref[head]
            do = dmix[head]
            lse = lse_ref[head]
            p = [jnp.exp(nn(keys[j], q) + mask[j] - lse) for j in range(nk)]
            dp = [nn(values[j], do) for j in range(nk)]
            delta = (p[0] * dp[0]).sum(axis=0, keepdims=True)
            for j in range(1, nk):
                delta = delta + (p[j] * dp[j]).sum(axis=0, keepdims=True)
            dq = jnp.zeros((HD, rows), F32)
            for j in range(nk):
                ds = (p[j] * (dp[j] - delta)).astype(BF)
                dkv[j, g] += nt(q, ds)
                dkv[j, KVH + g] += nt(do, p[j].astype(BF))
                dq = dq + nn(keys_t[j], ds)
            dq = dq * scale
            r1, r2 = unturned(dq[:half], dq[half:])
            gj[pl.ds(pl.multiple_of(head * HD, HD), half), :] = r1.astype(BF)
            gj[pl.ds(pl.multiple_of(head * HD + half, half), half), :] = r2.astype(BF)
            return carry

        lax.fori_loop(0, GROUP, one_head, 0)
    for j in range(1, nk):
        out_kv[j - 1] = dkv[j].astype(BF)
    sends = [
        remote(out_kv.at[j - 1], in_kv.at[j - 1], ssem.at[j - 1], rsem.at[j - 1],
               pc.along(pc.nb - j))
        for j in range(1, nk)
    ]
    for c in sends:
        c.start()
    for c in sends:
        c.wait()
    own = dkv[0]
    for j in range(1, nk):
        own = own + in_kv[j - 1].astype(F32)
    for g in range(KVH):
        r1, r2 = unturned(own[g, :half], own[g, half:])
        k0 = (H + g) * HD
        gj[k0 : k0 + half, :] = r1.astype(BF)
        gj[k0 + half : k0 + HD, :] = r2.astype(BF)
        v0 = (H + KVH + g) * HD
        gj[v0 : v0 + HD, :] = own[KVH + g].astype(BF)
    gjv = gj[...]
    n1 = width // 128
    dsmall_ref[n1 : n1 + qkv // 128, :] = rows_of(gjv.astype(F32))
    loads[0].wait()
    dqo_ref[:, :qkv] = nt(normed_ref[...], gjv).astype(BF)
    gn = nn(w[...], gjv)
    hidden = h_ref[...].astype(BF).astype(F32)
    scale_one = rms(hidden)
    unit = hidden * scale_one
    dsmall_ref[:n1, :] = rows_of(gn * unit)
    u = gn * g1
    gh_ref[...] = g_ref[...] + scale_one * (u - unit * jnp.mean(u * unit, axis=0, keepdims=True))
    for r in riders:
        r.finish()


def attention_backward(dims, nk, cid, layer, g, small, meta, docs, cos_part, sin_part, hidden,
                       normed, q, kv, lse, mixed, qo_all, specs, riders):
    width, rows = hidden.shape
    qkv = qo_all.shape[2] - width
    sds = jax.ShapeDtypeStruct
    outs = [
        sds((width, rows), F32),
        sds((width, qkv + width), BF),
        sds(((width + qkv) // 128, 128), F32),
    ] + rider_shapes(dims, specs, riders)
    dma = pltpu.SemaphoreType.DMA
    block = (2 * KVH, HD, rows)
    n = len(specs)
    out = call(
        functools.partial(attention_backward_kernel, dims, nk, layer, specs),
        "attention_backward",
        cid,
        tuple(outs),
        [VM] * 3 + [AN] * n,
        [VM] * 12 + [AN] * (1 + n),
        [
            pltpu.VMEM((width, qkv), BF),
            pltpu.VMEM((width, width), BF),
            pltpu.VMEM((nk, rows, rows), F32),
            pltpu.VMEM((H, HD, rows), BF),
            pltpu.VMEM((nk,) + block, F32),
            pltpu.VMEM((nk - 1,) + block, BF),
            pltpu.VMEM((nk - 1,) + block, BF),
            pltpu.VMEM((qkv, rows), BF),
            dma((nk - 1,)),
            dma((nk - 1,)),
            dma((2,)),
        ]
        + line_sems(dims) * n,
        (g, small, meta, docs, cos_part, sin_part, hidden, normed, q, kv, lse, mixed, qo_all,
         *riders),
    )
    return (out[:3], out[3:])


def steps_of(count):
    return (5, count - 1)


def lanes(slot, rows):
    return pl.ds(pl.multiple_of(slot * rows, rows), rows)


def transpose_into(dst, src):
    cols = src.shape[1]
    for c0 in range(0, cols, 128):
        c1 = min(c0 + 128, cols)
        dst[c0:c1, :] = src[:, c0:c1].T


def feed_forward_kernel(dims, specs, x_ref, res_ref, wgu_ref, wd_ref, *refs):
    n = len(specs)
    ins, refs = (refs[:n], refs[n:])
    out_ref, x_all, gu_all = refs[:3]
    outs, refs = (refs[3 : 3 + n], refs[3 + n :])
    wgu_t, wd_t, gu, inner, near, away, back, hop, ss, sr, gs, gr = refs[:12]
    pc = Place(dims)
    width, rows = x_ref.shape
    ff = wd_ref.shape[0]
    greet(pc, "mates", n > 0)
    riders = riders_of(pc, specs, ins, outs, refs[12:])
    gather = PlaneGather(pc, lambda q: x_all.at[:, lanes(q, rows)], gs, gr)
    scatter = PlaneScatter(pc, near, away, back, hop, ss, sr)
    x_all[:, lanes(pc.me, rows)] = x_ref[...]
    gather.start()
    for r in riders:
        r.start()
    transpose_into(wgu_t, wgu_ref)
    transpose_into(wd_t, wd_ref)
    neighbours, last = steps_of(pc.count)
    chunk = 32 if ff % 32 == 0 else 16

    def step_body(step, carry):
        for k in range(pc.count):
            @pl.when(step == k)
            def _():
                gather.before(k)

        slot = pick(step, gather.order)
        sl = lanes(slot, rows)
        gu[...] = nn(wgu_t[...], x_all[:, sl])

        def act(i, c):
            r = pl.multiple_of(i * chunk, chunk)
            gate = gu[pl.ds(r, chunk), :]
            up = gu[pl.ds(ff + r, chunk), :]
            gu_all[pl.ds(r, chunk), sl] = gate.astype(BF)
            gu_all[pl.ds(ff + r, chunk), sl] = up.astype(BF)
            inner[pl.ds(r, chunk), :] = (gate * jax.nn.sigmoid(gate) * up).astype(BF)
            return c

        lax.fori_loop(0, ff // chunk, act, 0)
        scatter.put(step, nn(wd_t[...], inner[...]))

        @pl.when(step == neighbours)
        def _():
            scatter.early()

        return carry

    lax.fori_loop(0, pc.count, step_body, 0)
    scatter.diagonal()

    def store(total):
        out_ref[...] = res_ref[...] + total

    scatter.result(store)
    gather.finish()
    for r in riders:
        r.finish()


def feed_forward(dims, cid, x, residual, wgu, wd, specs, riders):
    width, rows = x.shape
    count = dims[0] * dims[2]
    two_ff, ff = (wgu.shape[1], wd.shape[0])
    sds = jax.ShapeDtypeStruct
    dma = pltpu.SemaphoreType.DMA
    n = len(specs)
    out = call(
        functools.partial(feed_forward_kernel, dims, specs),
        "feed_forward",
        cid,
        (
            sds((width, rows), F32),
            sds((width, count * rows), BF),
            sds((two_ff, count * rows), BF),
            *rider_shapes(dims, specs, riders),
        ),
        [VM] * 3 + [AN] * n,
        [VM] * 4 + [AN] * n,
        [
            pltpu.VMEM((two_ff, width), BF),
            pltpu.VMEM((width, ff), BF),
            pltpu.VMEM((two_ff, rows), F32),
            pltpu.VMEM((ff, rows), BF),
        ]
        + scatter_scratch(dims, width, rows)
        + [dma((count - 1,)), dma((count - 1,))]
        + line_sems(dims) * n,
        (x, residual, wgu, wd, *riders),
    )
    return (out[:3], out[3:])


def feed_backward_kernel(
    dims, layer, specs, g_ref, res_ref, x_all, gu_all, wgu_ref, wd_ref, small_ref, *refs
):
    n = len(specs)
    ins, refs = (refs[:n], refs[n:])
    gr_ref, dwgu_ref, dwd_ref, dsmall_ref = refs[:4]
    outs, refs = (refs[4 : 4 + n], refs[4 + n :])
    g_all, inner, ggu, gi, near, away, back, hop, ss, sr, gs, gr = refs[:12]
    pc = Place(dims)
    width, rows = g_ref.shape
    ff = wd_ref.shape[0]
    greet(pc, "mates", n > 0)
    riders = riders_of(pc, specs, ins, outs, refs[12:])
    gather = PlaneGather(pc, lambda q: g_all.at[:, lanes(q, rows)], gs, gr)
    scatter = PlaneScatter(pc, near, away, back, hop, ss, sr)
    g_all[:, lanes(pc.me, rows)] = g_ref[...].astype(BF)
    gather.start()
    for r in riders:
        r.start()
    neighbours, last = steps_of(pc.count)
    chunk = 32 if ff % 32 == 0 else 16

    def step_body(step, carry):
        for k in range(pc.count):
            @pl.when(step == k)
            def _():
                gather.before(k)

        slot = pick(step, gather.order)
        sl = lanes(slot, rows)
        gi[...] = nn(wd_ref[...], g_all[:, sl])

        def act(i, c):
            r = pl.multiple_of(i * chunk, chunk)
            gate = gu_all[pl.ds(r, chunk), sl].astype(F32)
            up = gu_all[pl.ds(ff + r, chunk), sl].astype(F32)
            grad = gi[pl.ds(r, chunk), :]
            sig = jax.nn.sigmoid(gate)
            silu = gate * sig
            inner[pl.ds(r, chunk), sl] = (silu * up).astype(BF)
            ggu[pl.ds(r, chunk), sl] = (grad * up * sig * (1.0 + gate * (1.0 - sig))).astype(BF)
            ggu[pl.ds(ff + r, chunk), sl] = (grad * silu).astype(BF)
            return c

        lax.fori_loop(0, ff // chunk, act, 0)
        scatter.put(step, nn(wgu_ref[...], ggu[:, sl]))

        @pl.when(step == neighbours)
        def _():
            scatter.early()

        return carry

    lax.fori_loop(0, pc.count, step_body, 0)
    scatter.diagonal()
    part = width // 2
    for r in range(2):
        dwgu_ref[r * part : (r + 1) * part, :] = nt(
            x_all[r * part : (r + 1) * part, :], ggu[...]
        ).astype(BF)
    dwd_ref[...] = nt(inner[...], g_all[...]).astype(BF)

    def store(total):
        residual = res_ref[...]
        scale_two = rms(residual)
        unit = residual * scale_two
        n1 = width // 128
        dsmall_ref[...] = rows_of(total * unit)
        u = total * column(padded_t(small_ref[layer]), n1, n1)
        gr_ref[...] = g_ref[...].astype(BF).astype(F32) + scale_two * (
            u - unit * jnp.mean(u * unit, axis=0, keepdims=True)
        )

    scatter.result(store)
    gather.finish()
    for r in riders:
        r.finish()


def feed_backward(dims, cid, layer, g, residual, x_all, gu_all, wgu, wd, small, specs, riders):
    width, rows = g.shape
    count = dims[0] * dims[2]
    two_ff, ff = (wgu.shape[1], wd.shape[0])
    sds = jax.ShapeDtypeStruct
    dma = pltpu.SemaphoreType.DMA
    n = len(specs)
    out = call(
        functools.partial(feed_backward_kernel, dims, layer, specs),
        "feed_backward",
        cid,
        (
            sds((width, rows), F32),
            sds(wgu.shape, BF),
            sds(wd.shape, BF),
            sds((width // 128, 128), F32),
            *rider_shapes(dims, specs, riders),
        ),
        [VM] * 4 + [AN] * n,
        [VM] * 7 + [AN] * n,
        [
            pltpu.VMEM((width, count * rows), BF),
            pltpu.VMEM((ff, count * rows), BF),
            pltpu.VMEM((two_ff, count * rows), BF),
            pltpu.VMEM((ff, rows), F32),
        ]
        + scatter_scratch(dims, width, rows)
        + [dma((count - 1,)), dma((count - 1,))]
        + line_sems(dims) * n,
        (g, residual, x_all, gu_all, wgu, wd, small, *riders),
    )
    return (out[:4], out[4:])


def reduce_kernel(
    dims, cut, qo0, qo1, sa0, sa1, sb0, sb1, gu1, wd1, wd0, gu0a, gu0,
    qo_out, small_out, gu_got, wd_got,
    buf1, bufa, buf0, bufw, gsum, wsum, small, sm_in, sm_mid, sm_line, z_out, z_in, half_sum,
    lsem, ps, pr, gs, gr, ws, wr, ls, lr, zs, zr, near, away, back, hop, ss, sr, *rest
):
    pc = Place(dims)
    ns, nb, nf = dims
    greet(pc, "all", True)
    line = LineExchange(pc, lambda t: gu0.at[t, cut:nf], lambda t: buf0.at[t], rest)
    line.start()
    loads = [
        pltpu.make_async_copy(gu1, buf1, lsem.at[0]),
        pltpu.make_async_copy(gu0a, bufa, lsem.at[1]),
        pltpu.make_async_copy(wd0, bufw.at[0], lsem.at[2]),
        pltpu.make_async_copy(wd1, bufw.at[1], lsem.at[3]),
    ]
    for c in loads:
        c.start()
    n1 = sb0.shape[0]
    per = small.shape[0] // ns
    nr = sa0.shape[0] + n1
    small[...] = jnp.zeros_like(small)
    for l, (a, g) in enumerate(((sa0, sb0), (sa1, sb1))):
        small[l * per : l * per + n1] = a[0:n1]
        small[l * per + n1 : l * per + 2 * n1] = g[...]
        small[l * per + 2 * n1 : l * per + nr] = a[n1 : a.shape[0]]
    smalls = [
        remote(small, sm_in.at[e - 1], ls.at[e - 1], lr.at[e - 1], pc.plane(e))
        for e in range(1, pc.count)
    ]
    for c in smalls:
        c.start()
    scatter = PlaneScatter(pc, near, away, back, hop, ss, sr)
    if pc.two_level:
        order = pc.slots()
    else:
        order = tuple(pc.slot_from(e) for e in range(pc.count))
    neighbours, last = steps_of(pc.count)

    def step_body(step, carry):
        slot = pick(step, order)
        f = slot % nf
        for l, ref in enumerate((qo0, qo1)):
            @pl.when(slot // nf == l)
            def _():
                scatter.put(step, ref[:, f].astype(F32))

        @pl.when(step == neighbours)
        def _():
            scatter.early()

        return carry

    lax.fori_loop(0, pc.count, step_body, 0)
    scatter.diagonal()

    def send_rows(l, f):
        e = (l * nf + f - pc.me + pc.count) % pc.count

        @pl.when(e != 0)
        def _():
            remote(
                gsum.at[l, f], gu_got.at[pc.me], ps.at[e - 1], pr.at[e - 1], (l, pc.b, f)
            ).start()

        @pl.when(e == 0)
        def _():
            pltpu.make_async_copy(gsum.at[l, f], gu_got.at[pc.me], lsem.at[4]).start()

    def total_of(buf):
        total = buf[0].astype(F32)
        for t in range(1, nb):
            total = total + buf[t].astype(F32)
        return total.astype(BF)

    loads[0].wait()
    for f in range(nf):
        gsum[1, f] = total_of(buf1.at[:, f])
        send_rows(1, f)
    loads[2].wait()
    loads[3].wait()
    wsum[0] = total_of(bufw.at[0])
    wsum[1] = total_of(bufw.at[1])
    own = pltpu.make_async_copy(wsum.at[pc.s], wd_got.at[pc.s], lsem.at[5])
    own.start()
    across = []
    for d in range(1, ns):
        y = (pc.s + d) % ns
        across.append(
            remote(wsum.at[y], wd_got.at[pc.s], ws.at[d - 1], wr.at[d - 1], (y, pc.b, pc.f))
        )
        across[-1].start()
    loads[1].wait()
    for f in range(cut):
        gsum[0, f] = total_of(bufa.at[:, f])
        send_rows(0, f)
    total = small[...]
    for e, c in enumerate(smalls):
        c.wait()
        total = total + sm_in[e]
    sm_mid[...] = total
    m = nb - 1
    lines = [
        remote(sm_mid, sm_line.at[d - 1], zs.at[m + d - 1], zr.at[m + d - 1], pc.along(d))
        for d in range(1, nb)
    ]
    for c in lines:
        c.start()

    def store(value):
        half_sum[...] = value

    scatter.result(store)
    z_out[...] = half_sum[...].astype(BF)
    sends = []
    for d in range(1, nb):
        t = pc.along(d)
        sends.append(remote(z_out.at[t[1]], z_in.at[d - 1], zs.at[d - 1], zr.at[d - 1], t))
    for c in sends:
        c.start()
    line.finish()
    for f in range(cut, nf):
        gsum[0, f] = total_of(buf0.at[:, f - cut])
        send_rows(0, f)
    mine = z_out[pc.b].astype(F32)
    for d, c in enumerate(sends):
        c.wait()
        mine = mine + z_in[d].astype(F32)
    qo_out[...] = mine
    total = sm_mid[...]
    for d, c in enumerate(lines):
        c.wait()
        total = total + sm_line[d]
    small_out[...] = total
    for k in range(pc.count - 1):
        c = remote(gsum.at[0, 0], gu_got.at[pc.me], ps.at[k], pr.at[k], pc.plane(1))
        c.wait()
    pltpu.make_async_copy(gsum.at[0, 0], gu_got.at[pc.me], lsem.at[4]).wait()
    own.wait()
    for c in across:
        c.wait()


def reduce_gradients(dims, cid, cut, qo0, qo1, smalls, gu1, wd1, wd0, gu0a, gu0):
    ns, nb, nf = dims
    count = ns * nf
    dr, cols = qo0.shape[2:]
    two_ff = gu0.shape[3]
    half, width = wd0.shape[1:]
    rows = smalls[0].shape[0] + smalls[2].shape[0]
    small = (ns * (-(-rows // 8) * 8), 128)
    sds = jax.ShapeDtypeStruct
    dma = pltpu.SemaphoreType.DMA
    return call(
        functools.partial(reduce_kernel, dims, cut),
        "reduce_gradients",
        cid,
        (
            sds((dr, cols), F32),
            sds(small, F32),
            sds((count, dr, two_ff), BF),
            sds((ns, half, width), BF),
        ),
        [VM] * 4,
        [VM] * 6 + [AN] * 5,
        [
            pltpu.VMEM((nb, nf, dr, two_ff), BF),
            pltpu.VMEM((nb, cut, dr, two_ff), BF),
            pltpu.VMEM((nb, nf - cut, dr, two_ff), BF),
            pltpu.VMEM((ns, nb, half, width), BF),
            pltpu.VMEM((ns, nf, dr, two_ff), BF),
            pltpu.VMEM((ns, half, width), BF),
            pltpu.VMEM(small, F32),
            pltpu.VMEM((count - 1,) + small, F32),
            pltpu.VMEM(small, F32),
            pltpu.VMEM((nb - 1,) + small, F32),
            pltpu.VMEM((nb, dr, cols), BF),
            pltpu.VMEM((nb - 1, dr, cols), BF),
            pltpu.VMEM((nb, dr, cols), F32),
            dma((6,)),
            dma((count - 1,)),
            dma((count - 1,)),
            dma((1,)),
            dma((1,)),
            dma((ns - 1,)),
            dma((ns - 1,)),
            dma((count - 1,)),
            dma((count - 1,)),
            dma((2 * (nb - 1),)),
            dma((2 * (nb - 1),)),
        ]
        + scatter_scratch(dims, nb, dr, cols)
        + line_sems(dims),
        (qo0, qo1, *smalls, gu1, wd1, wd0, gu0a, gu0),
    )


def lay_out_kernel(
    dims, gu, wd, qo, small, out0, out1, gh0, gh1, take_out, take_grad,
    block_out, input_grad, g1, wqkv, bqkv, wout, g2, wgu, wdn
):
    ns, nb, nf = dims
    half = wd.shape[1]
    s = lax.axis_index("section")
    qkv = wqkv.shape[2]
    width = wout.shape[2]
    wqkv[0] = qo[:, :qkv]
    wout[0] = qo[:, qkv:]
    for y in range(ns):
        wdn[0, y * half : (y + 1) * half, :] = wd[y].astype(F32)
        for f in range(nf):
            got = gu[y * nf + f].astype(F32)
            for part in range(2):
                for b in range(nb):
                    c0 = column_start(dims, part, b, f, y, half)
                    k0 = (part * nb + b) * half
                    wgu[0, :, c0 : c0 + half] = got[:, k0 : k0 + half]
    n1 = width // 128
    per = small.shape[0] // ns
    rows = small[pl.ds(pl.multiple_of(s * per, 8), per), :]
    for k in range(n1):
        g1[0:1, k * 128 : (k + 1) * 128] = rows[k : k + 1]
        g2[0:1, k * 128 : (k + 1) * 128] = rows[n1 + k : n1 + k + 1]
    for k in range(qkv // 128):
        bqkv[0:1, k * 128 : (k + 1) * 128] = rows[2 * n1 + k : 2 * n1 + k + 1]
    for out, pair, take in (
        (block_out, (out0, out1), take_out),
        (input_grad, (gh0, gh1), take_grad),
    ):
        for l in range(ns):
            @pl.when(s == l)
            def _():
                out[0, l] = pair[l][...].T
                out[0, 1 - l] = take[...].T.astype(F32)


def lay_out(dims, qkv, args):
    ns, nb, nf = dims
    gu, wd, qo = args[:3]
    width, rows = args[4].shape
    dr = qo.shape[0]
    sds = jax.ShapeDtypeStruct
    tokens = sds((1, ns, rows, width), F32)
    return pl.pallas_call(
        functools.partial(lay_out_kernel, dims),
        name="lay_out",
        out_shape=(
            tokens,
            tokens,
            sds((1, width), F32),
            sds((1, dr, qkv), F32),
            sds((1, qkv), F32),
            sds((1, dr, width), F32),
            sds((1, width), F32),
            sds((1, dr, gu.shape[0] * gu.shape[2]), F32),
            sds((1, ns * wd.shape[1], width), F32),
        ),
        in_specs=[VM] * len(args),
        out_specs=[VM] * 9,
        compiler_params=pltpu.CompilerParams(vmem_limit_bytes=VMEM_LIMIT),
    )(*args)


def shards(
    dims,
    tokens_in,
    positions,
    doc_ids,
    out_grad,
    norm1_gain,
    w_qkv,
    b_qkv,
    w_out,
    norm2_gain,
    w_gate_up,
    w_down,
):
    ns, nb, nf = dims
    seqs, rows, width = tokens_in.shape
    s = lax.axis_index("section")
    b = lax.axis_index("blk")
    dr = w_qkv.shape[1]
    qkv = w_qkv.shape[2]
    fr = w_down.shape[1]
    half = fr // ns
    ff = nb * half
    nk = min(nb, 1 + (LONGEST - 1 + rows - 1) // rows)

    tokens = lax.dynamic_index_in_dim(tokens_in, s, 0, keepdims=False)
    cot = lax.dynamic_index_in_dim(out_grad, s, 0, keepdims=False)
    pos = lax.dynamic_index_in_dim(positions, s, 0, keepdims=False)
    docs = lax.dynamic_index_in_dim(doc_ids, s, 0, keepdims=False).astype(F32)
    freq = jnp.exp(jnp.arange(HD // 2, dtype=F32) * (-2.0 / HD) * math.log(1000000.0))
    phase = freq[:, None] * pos.astype(F32)[None, :]
    cos_part, sin_part = (jnp.cos(phase), jnp.sin(phase))
    docs = docs.reshape(nb, rows)
    picked = (b - jnp.arange(nk) + nb) % nb
    meta = jnp.take(docs, picked, axis=0).reshape(nk * rows // 128, 128)
    query_docs = lax.dynamic_slice_in_dim(docs, b, 1)
    hidden = tokens.T.astype(F32)
    g = cot.T.astype(F32)

    wd = w_down[0].reshape(ns, half, width)
    qo = jnp.concatenate([w_qkv[0], w_out[0]], axis=1)
    small = jnp.concatenate([norm1_gain[0], norm2_gain[0], b_qkv[0]])
    total = -(-small.shape[0] // 1024) * 1024
    small = jnp.pad(small, (0, total - small.shape[0])).reshape(-1, 128)
    gup, wdp, gu_first, qo_all, small_all = gather_weights(dims, w_gate_up, wd, qo, small)
    qo_all = qo_all.reshape(ns, width, qkv + width)
    wide = (width, 2 * ff)

    common = (small_all, meta, query_docs, cos_part, sin_part, qo_all)
    a0, (wd0,) = attention_forward(dims, nk, 1, 0, hidden, *common, (("gather", 0),), (wdp,))
    wd0 = wd0.reshape(ff, width)
    wgu0 = gu_first.reshape(wide)
    f0, (gu1,) = feed_forward(dims, 3, a0[6], a0[5], wgu0, wd0, (("gather", 1),), (gup,))
    wgu1 = gu1.reshape(wide)
    a1, (wd1,) = attention_forward(dims, nk, 2, 1, f0[0], *common, (("gather", 1),), (wdp,))
    wd1 = wd1.reshape(ff, width)
    f1, _ = feed_forward(dims, 4, a1[6], a1[5], wgu1, wd1, (), ())

    line_gu = (nb, nf, dr, 2 * ff)
    line_wd = (nb, half, width)
    everything = (0, half)
    cut = max(1, nf // 4)
    b1, _ = feed_backward(dims, 5, 1, g, a1[5], f1[1], f1[2], wgu1, wd1, small_all, (), ())
    ab1, (dwd1,) = attention_backward(
        dims, nk, 7, 1, b1[0], *common[:5], f0[0], *a1[:5], qo_all,
        (("exchange", everything),), (b1[2].reshape(line_wd),),
    )
    b0, (dgu1,) = feed_backward(
        dims, 6, 0, ab1[0], a0[5], f0[1], f0[2], wgu0, wd0, small_all,
        (("exchange", (0, nf)),), (b1[1].reshape(line_gu),),
    )
    dgu0 = b0[1].reshape(line_gu)
    ab0, (dwd0, dgu0a) = attention_backward(
        dims, nk, 8, 0, b0[0], *common[:5], hidden, *a0[:5], qo_all,
        (("exchange", everything), ("exchange", (0, cut))), (b0[2].reshape(line_wd), dgu0),
    )

    def swapped(values):
        give = jnp.where(s == 0, values[1], values[0]).astype(BF)
        return lax.ppermute(give, "section", [(0, 1), (1, 0)])

    take_out = swapped((f0[0], f1[0]))
    take_grad = swapped((ab0[0], ab1[0]))
    line_qo = (nb, nf, dr, qkv + width)
    grad_qo, small_sum, gu_got, wd_got = reduce_gradients(
        dims, 9, cut, ab0[1].reshape(line_qo), ab1[1].reshape(line_qo),
        (ab0[2], ab1[2], b0[3], b1[3]), dgu1, dwd1, dwd0, dgu0a, dgu0,
    )
    return lay_out(
        dims,
        qkv,
        (gu_got, wd_got, grad_qo, small_sum, f0[0], f1[0], ab0[0], ab1[0], take_out, take_grad),
    )


def solution(mesh):
    dims = (mesh.shape["section"], mesh.shape["blk"], mesh.shape["fsdp"])
    return jax.shard_map(
        functools.partial(shards, dims),
        mesh=mesh,
        in_specs=(
            P("fsdp", "blk", None),
            P("fsdp", "blk"),
            P("fsdp", None),
            P("fsdp", "blk", None),
            P("section", None),
            P("section", ("blk", "fsdp"), None),
            P("section", None),
            P("section", ("blk", "fsdp"), None),
            P("section", None),
            P("section", ("blk", "fsdp"), None),
            P("section", ("blk", "fsdp"), None),
        ),
        out_specs=(
            P("section", "fsdp", "blk", None),
            P("section", "fsdp", "blk", None),
            P("section", None),
            P("section", ("blk", "fsdp"), None),
            P("section", None),
            P("section", ("blk", "fsdp"), None),
            P("section", None),
            P("section", ("blk", "fsdp"), None),
            P("section", ("blk", "fsdp"), None),
        ),
        check_vma=False,
    )
```

```python
import functools
import math

import jax
import jax.numpy as jnp
from jax import lax
from jax.experimental import pallas as pl
from jax.experimental.pallas import tpu as pltpu
from jax.sharding import PartitionSpec as P

H = 14
KVH = 2
HD = 64
GROUP = H // KVH
LONGEST = 512
NEG = -1e30
BF = jnp.bfloat16
F32 = jnp.float32
MESH = pl.DeviceIdType.MESH
VMEM_LIMIT = 60 * 2**20
VM = pl.BlockSpec(memory_space=pltpu.VMEM)
AN = pl.BlockSpec(memory_space=pl.ANY)


def nn(a, b):
    return lax.dot_general(a, b, (((1,), (0,)), ((), ())), preferred_element_type=F32)


def nt(a, b):
    return lax.dot_general(a, b, (((1,), (1,)), ((), ())), preferred_element_type=F32)


def tn(a, b):
    return lax.dot_general(a, b, (((0,), (0,)), ((), ())), preferred_element_type=F32)


def other(f):
    return f + 1 - 2 * (f % 2)


class Place:
    def __init__(self, dims):
        self.ns, self.nb, self.nf = dims
        self.count = self.ns * self.nf
        self.s = lax.axis_index("section")
        self.b = lax.axis_index("blk")
        self.f = lax.axis_index("fsdp")
        self.me = self.s * self.nf + self.f
        self.two_level = self.ns == 2 and self.nf == 4

    def plane(self, e):
        q = (self.me + e) % self.count
        return (q // self.nf, self.b, q % self.nf)

    def slot_from(self, e):
        return (self.me + self.count - e) % self.count

    def along(self, d):
        return (self.s, (self.b + d) % self.nb, self.f)

    def mates(self):
        s, b, f = (self.s, self.b, self.f)
        xf = (f + 2) % 4
        return ((s, b, other(f)), (s, b, xf), (1 - s, b, f))

    def slots(self):
        s, f = (self.s, self.f)
        xf = (f + 2) % 4
        t = 1 - s
        return (
            s * 4 + f,
            s * 4 + other(f),
            s * 4 + xf,
            t * 4 + f,
            s * 4 + other(xf),
            t * 4 + other(f),
            t * 4 + xf,
            t * 4 + other(xf),
        )


def pick(i, values):
    total = 0
    for k, v in enumerate(values):
        total = total + jnp.where(i == k, v, 0)
    return total


def greet(place, plane, along):
    barrier = pltpu.get_barrier_semaphore()
    count = 0
    if plane:
        if place.two_level and plane == "mates":
            targets = list(place.mates())
        else:
            targets = [place.plane(e) for e in range(1, place.count)]
        for t in targets:
            pl.semaphore_signal(barrier, 1, device_id=t, device_id_type=MESH)
        count += len(targets)
    if along:
        for d in range(1, place.nb):
            pl.semaphore_signal(barrier, 1, device_id=place.along(d), device_id_type=MESH)
        count += place.nb - 1
    pl.semaphore_wait(barrier, count)


def remote(src, dst, ssem, rsem, device):
    return pltpu.make_async_remote_copy(
        src_ref=src,
        dst_ref=dst,
        send_sem=ssem,
        recv_sem=rsem,
        device_id=device,
        device_id_type=MESH,
    )


class PlaneGather:
    def __init__(self, place, slot, ssem, rsem):
        self.place, self.slot, self.ssem, self.rsem = (place, slot, ssem, rsem)
        if place.two_level:
            self.order = place.slots()
        else:
            self.order = tuple(place.slot_from(e) for e in range(place.count))

    def copy(self, k, q, device):
        v = self.slot(q)
        return remote(v, v, self.ssem.at[k], self.rsem.at[k], device)

    def start(self):
        pc = self.place
        if pc.two_level:
            core, xm, ym = pc.mates()
            self.copy(1, self.order[0], xm).start()
            self.copy(2, self.order[0], ym).start()
            self.copy(0, self.order[0], core).start()
        else:
            for e in range(1, pc.count):
                self.copy(e - 1, self.order[0], pc.plane(e)).start()

    def waited(self, k):
        self.copy(k, self.order[k + 1], self.place.plane(1)).wait_recv()

    def before(self, step):
        if step == 0:
            return
        pc = self.place
        if not pc.two_level:
            self.waited(step - 1)
            return
        core, xm, ym = pc.mates()
        c = pc.f % 2
        if step == 2:
            self.waited(1)
            self.copy(3, self.order[2], core).start()
            self.waited(2)
            self.copy(4, self.order[3], core).start()
            which = c * self.order[3] + (1 - c) * self.order[2]
            far = (
                c * xm[0] + (1 - c) * ym[0],
                pc.b,
                c * xm[2] + (1 - c) * ym[2],
            )
            self.copy(5, which, far).start()
        elif step == 3:
            return
        elif step == 6:
            self.waited(5)
            self.copy(6, self.order[6], core).start()
        else:
            self.waited(step - 1)

    def finish(self):
        n = self.place.count - 1
        for k in range(n):
            self.copy(k, self.order[0], self.place.plane(1)).wait_send()


class PlaneScatter:
    def __init__(self, place, near, away, back, hop, ssem, rsem):
        self.place = place
        self.near, self.away, self.back, self.hop = (near, away, back, hop)
        self.ssem, self.rsem = (ssem, rsem)

    def put(self, step, value):
        pc = self.place
        if not pc.two_level:
            @pl.when(step == 0)
            def _():
                self.near[0] = value

            @pl.when(step > 0)
            def _():
                e = pc.count - step
                self.away[e - 1] = value.astype(BF)
                q = (pc.me + e) % pc.count
                remote(
                    self.away.at[e - 1],
                    self.back.at[e - 1],
                    self.ssem.at[e - 1],
                    self.rsem.at[e - 1],
                    (q // pc.nf, pc.b, q % pc.nf),
                ).start()
            return
        core, xm, ym = pc.mates()
        here = (step == 0) | (step == 2) | (step == 3) | (step == 6)
        q = pick(step, (0, 0, 1, 2, 1, 2, 3, 3))

        @pl.when(here)
        def _():
            self.near[q] = value

        @pl.when(jnp.logical_not(here))
        def _():
            self.away[q] = value.astype(BF)
            self.core_copy(q).start()

    def core_copy(self, q):
        core = self.place.mates()[0]
        return remote(self.away.at[q], self.back.at[q], self.ssem.at[q], self.rsem.at[q], core)

    def far_copy(self, e):
        return remote(self.away.at[e - 1], self.back.at[e - 1], self.ssem.at[e - 1],
                      self.rsem.at[e - 1], self.place.plane(e))

    def hop_copy(self, k, device):
        return remote(
            self.hop.at[k], self.hop.at[k + 3], self.ssem.at[4 + k], self.rsem.at[4 + k], device
        )

    def targets(self):
        pc = self.place
        core, xm, ym = pc.mates()
        c = pc.f % 2
        first = (c * xm[0] + (1 - c) * ym[0], pc.b, c * xm[2] + (1 - c) * ym[2])
        second = (c * ym[0] + (1 - c) * xm[0], pc.b, c * ym[2] + (1 - c) * xm[2])
        return (first, second)

    def early(self):
        pc = self.place
        if not pc.two_level:
            return
        c = pc.f % 2
        first, second = self.targets()
        self.core_copy(1).wait_recv()
        self.core_copy(2).wait_recv()
        q = c * 1 + (1 - c) * 2
        self.hop[0] = (self.mine(q) + self.back[q].astype(F32)).astype(BF)
        self.hop_copy(0, first).start()

    def diagonal(self):
        pc = self.place
        if not pc.two_level:
            return
        first, second = self.targets()
        self.core_copy(3).wait_recv()
        self.hop[1] = (self.mine(3) + self.back[3].astype(F32)).astype(BF)
        self.hop_copy(1, first).start()

    def mine(self, q):
        return self.near[q]

    def result(self, store):
        self.late()
        self.finish(store)

    def late(self):
        pc = self.place
        if not pc.two_level:
            return
        c = pc.f % 2
        first, second = self.targets()
        self.hop_copy(1, first).wait_recv()
        q = c * 2 + (1 - c) * 1
        self.hop[2] = (
            self.mine(q) + self.back[q].astype(F32) + self.hop[4].astype(F32)
        ).astype(BF)
        self.hop_copy(2, second).start()

    def finish(self, store):
        pc = self.place
        if not pc.two_level:
            total = self.mine(0)
            for e in range(1, pc.count):
                self.far_copy(e).wait()
                total = total + self.back[e - 1].astype(F32)
            store(total)
            return
        first, second = self.targets()
        self.core_copy(0).wait_recv()
        self.hop_copy(0, first).wait_recv()
        self.hop_copy(2, second).wait_recv()
        store(
            self.mine(0)
            + self.back[0].astype(F32)
            + self.hop[3].astype(F32)
            + self.hop[5].astype(F32)
        )
        for q in range(4):
            self.core_copy(q).wait_send()
        self.hop_copy(0, first).wait_send()
        self.hop_copy(1, first).wait_send()
        self.hop_copy(2, second).wait_send()


class ReadyScatter(PlaneScatter):
    def __init__(self, place, parts, back, hop, ssem, rsem):
        super().__init__(place, None, None, back, hop, ssem, rsem)
        self.parts = parts
        if place.two_level:
            o = place.slots()
            self.here = (o[0], o[2], o[3], o[6])
            self.gone = (o[1], o[4], o[5], o[7])

    def mine(self, q):
        if not self.place.two_level:
            return self.parts[self.place.me].astype(F32)
        return self.parts[pick(q, self.here)].astype(F32)

    def core_copy(self, q):
        core = self.place.mates()[0]
        v = self.parts.at[self.gone[q]]
        return remote(v, self.back.at[q], self.ssem.at[q], self.rsem.at[q], core)

    def far_copy(self, e):
        pc = self.place
        v = self.parts.at[(pc.me + e) % pc.count]
        return remote(v, self.back.at[e - 1], self.ssem.at[e - 1], self.rsem.at[e - 1],
                      pc.plane(e))

    def start(self):
        pc = self.place
        if pc.two_level:
            for q in (2, 1, 3, 0):
                self.core_copy(q).start()
        else:
            for e in range(1, pc.count):
                self.far_copy(e).start()


class LineGather:
    def __init__(self, place, piece, out, sems):
        lsem, ss, sr = sems
        own = out.at[place.b]
        self.copies = [pltpu.make_async_copy(piece, own, lsem)]
        for d in range(1, place.nb):
            self.copies.append(remote(piece, own, ss.at[d - 1], sr.at[d - 1], place.along(d)))

    def start(self):
        for c in self.copies:
            c.start()

    def finish(self):
        for c in self.copies:
            c.wait()


class LineExchange(LineGather):
    def __init__(self, place, parts, out, sems):
        lsem, ss, sr = sems
        own = out(place.b)
        self.copies = [pltpu.make_async_copy(parts(place.b), own, lsem)]
        for d in range(1, place.nb):
            t = place.along(d)
            self.copies.append(remote(parts(t[1]), own, ss.at[d - 1], sr.at[d - 1], t))


def line_sems(dims):
    dma = pltpu.SemaphoreType.DMA
    return [dma(()), dma((dims[1] - 1,)), dma((dims[1] - 1,))]


def riders_of(place, specs, ins, outs, sems):
    out = []
    for i, spec in enumerate(specs):
        mine = sems[3 * i : 3 * i + 3]
        if spec[0] == "gather":
            piece = ins[i] if spec[1] is None else ins[i].at[spec[1]]
            out.append(LineGather(place, piece, outs[i], mine))
        else:
            lo, hi = spec[1]
            out.append(
                LineExchange(
                    place,
                    lambda t, r=ins[i]: r.at[t, lo:hi],
                    lambda t, r=outs[i]: r.at[t],
                    mine,
                )
            )
    return out


def rider_shapes(dims, specs, arrays):
    out = []
    for spec, a in zip(specs, arrays):
        if spec[0] == "gather":
            shape = a.shape if spec[1] is None else a.shape[1:]
            out.append(jax.ShapeDtypeStruct((dims[1],) + shape, a.dtype))
        else:
            lo, hi = spec[1]
            out.append(jax.ShapeDtypeStruct((a.shape[0], hi - lo) + a.shape[2:], a.dtype))
    return out


def scatter_scratch(dims, *block):
    count = dims[0] * dims[2]
    if dims[0] == 2 and dims[2] == 4:
        near, away, hops, sems = (4, 4, 6, 7)
    else:
        near, away, hops, sems = (1, count - 1, 1, count - 1)
    return [
        pltpu.VMEM((near,) + block, F32),
        pltpu.VMEM((away,) + block, BF),
        pltpu.VMEM((away,) + block, BF),
        pltpu.VMEM((hops,) + block, BF),
        pltpu.SemaphoreType.DMA((sems,)),
        pltpu.SemaphoreType.DMA((sems,)),
    ]


def call(kernel, name, cid, outs, out_specs, in_specs, scratch, args):
    params = pltpu.CompilerParams(
        collective_id=cid, has_side_effects=True, vmem_limit_bytes=VMEM_LIMIT
    )
    return pl.pallas_call(
        kernel,
        name=name,
        out_shape=outs,
        in_specs=in_specs,
        out_specs=out_specs,
        scratch_shapes=scratch,
        compiler_params=params,
    )(*args)


def column_start(dims, part, b, f, y, half):
    ns, nb, nf = dims
    return part * nb * nf * ns * half + ((b * nf + f) * ns + y) * half


def gather_weights_kernel(
    dims, w_ref, wd, qo, small, gup, wdp, gu_first, qo_all, small_all,
    pack, lsem, ps, pr, zs, zr, qs, qr, ms, mr, *rest
):
    pc = Place(dims)
    ns, nb, nf = dims
    half = wd.shape[1]
    greet(pc, "all", True)
    firsts = []
    for d in range(1, nb):
        firsts.append(
            remote(qo, qo_all.at[pc.s, pc.b, pc.f], zs.at[d - 1], zr.at[d - 1], pc.along(d))
        )
        firsts[-1].start()
    local = [
        pltpu.make_async_copy(qo, qo_all.at[pc.s, pc.b, pc.f], lsem.at[0]),
        pltpu.make_async_copy(wd.at[pc.s], wdp.at[pc.s], lsem.at[1]),
        pltpu.make_async_copy(small, small_all.at[pc.s], lsem.at[2]),
    ]
    for c in local:
        c.start()
    across = []
    for d in range(1, ns):
        y = (pc.s + d) % ns
        t = (y, pc.b, pc.f)
        across.append(remote(wd.at[y], wdp.at[pc.s], ms.at[2 * d - 2], mr.at[2 * d - 2], t))
        across.append(remote(small, small_all.at[pc.s], ms.at[2 * d - 1], mr.at[2 * d - 1], t))
    for c in across:
        c.start()
    for y in range(ns):
        for f in range(nf):
            pieces = []
            for part in range(2):
                for b in range(nb):
                    c0 = column_start(dims, part, b, f, y, half)
                    pieces.append(w_ref[0, :, c0 : c0 + half])
            pack[y, f] = jnp.concatenate(pieces, axis=1)
    own = pltpu.make_async_copy(pack.at[pc.s, pc.f], gup.at[pc.s, pc.f], lsem.at[3])
    own.start()
    plane = []
    for e in range(1, pc.count):
        t = pc.plane(e)
        plane.append(
            remote(pack.at[t[0], t[2]], gup.at[pc.s, pc.f], ps.at[e - 1], pr.at[e - 1], t)
        )
    for c in plane:
        c.start()
    n = pc.count - 1
    gathers = []
    for d in range(nb):
        b = (pc.b + nb - d) % nb
        gathers.append(
            PlaneGather(
                pc,
                lambda q, b=b: qo_all.at[q // nf, b, q % nf],
                qs.at[pl.ds(d * n, n)],
                qr.at[pl.ds(d * n, n)],
            )
        )
    local[0].wait()
    gathers[0].start()
    own.wait()
    for c in plane:
        c.wait()
    line = LineGather(pc, gup.at[0], gu_first, rest)
    line.start()
    for d in range(1, nb):
        firsts[d - 1].wait()
        gathers[d].start()
        for step in range(1, min(6, pc.count)):
            gathers[d - 1].before(step)
    for step in range(1, min(6, pc.count)):
        gathers[nb - 1].before(step)
    for step in range(min(6, pc.count), pc.count):
        for g in gathers:
            g.before(step)
    for g in gathers:
        g.finish()
    for c in local[1:]:
        c.wait()
    for c in across:
        c.wait()
    line.finish()


def gather_weights(dims, w, wd, qo, small):
    ns, nb, nf = dims
    count = ns * nf
    half, width = wd.shape[1:]
    dr = qo.shape[0]
    two_ff = 2 * nb * half
    sds = jax.ShapeDtypeStruct
    outs = (
        sds((ns, nf, dr, two_ff), BF),
        sds((ns, half, width), BF),
        sds((nb, nf, dr, two_ff), BF),
        sds((ns, nb, nf) + qo.shape, BF),
        sds((ns,) + small.shape, F32),
    )
    dma = pltpu.SemaphoreType.DMA
    return call(
        functools.partial(gather_weights_kernel, dims),
        "gather_weights",
        0,
        outs,
        [AN] * 5,
        [VM, AN, AN, AN],
        [
            pltpu.VMEM((ns, nf, dr, two_ff), BF),
            dma((4,)),
            dma((count - 1,)),
            dma((count - 1,)),
            dma((nb - 1,)),
            dma((nb - 1,)),
            dma((nb * (count - 1),)),
            dma((nb * (count - 1),)),
            dma((2 * (ns - 1),)),
            dma((2 * (ns - 1),)),
        ]
        + line_sems(dims),
        (w, wd, qo, small),
    )


def rms(values):
    return lax.rsqrt(jnp.mean(values * values, axis=0, keepdims=True) + 1e-06)


def column(rows_t, first, count):
    return jnp.concatenate([rows_t[:, k : k + 1] for k in range(first, first + count)], axis=0)


def rows_of(values):
    v = folded(values)
    return jnp.concatenate(
        [v[k : k + 128].T.sum(axis=0, keepdims=True) for k in range(0, v.shape[0], 128)], axis=0
    )


def folded(v):
    out = v[:, :128]
    for k in range(1, v.shape[1] // 128):
        out = out + v[:, k * 128 : (k + 1) * 128]
    return out


def fill_masks(pc, mask, meta_t, query_docs):
    nk, rows = mask.shape[:2]
    key_i = lax.broadcasted_iota(jnp.int32, (rows, rows), 0)
    query_i = lax.broadcasted_iota(jnp.int32, (rows, rows), 1)
    per = rows // 128
    for j in range(nk):
        same = column(meta_t, j * per, per) == query_docs
        if j == 0:
            live = same & (key_i <= query_i)
        else:
            live = same & (key_i < (pc.b - j + 1) * rows)
        mask[j] = jnp.where(live, 0.0, NEG)


def load_qo(qo_all, layer, w, wo, sems):
    cols = w.shape[1]
    c1 = pltpu.make_async_copy(qo_all.at[layer, :, 0:cols], w, sems.at[0])
    c2 = pltpu.make_async_copy(qo_all.at[layer, :, cols : cols + wo.shape[1]], wo, sems.at[1])
    c1.start()
    c2.start()
    return (c1, c2)


def gains_of(small_t, width, qkv):
    n = width // 128
    return (
        column(small_t, 0, n),
        column(small_t, n, n),
        column(small_t, 2 * n, qkv // 128),
    )


def padded_t(v):
    n = v.shape[0]
    return jnp.concatenate([v, jnp.zeros((128 - n, 128), v.dtype)], axis=0).T


def attention_forward_kernel(
    dims, nk, layer, specs, carry, h_ref, small_ref, meta_ref, docs_ref, cos_ref, sin_ref, qo_all,
    *refs
):
    n = len(specs)
    if carry:
        block_ref, refs = (refs[0], refs[1:])
    ins, refs = (refs[:n], refs[n:])
    normed_ref, q_ref, kv_ref, lse_ref, mixed_ref, res_ref, n2_ref = refs[:7]
    outs, refs = (refs[7 : 7 + n], refs[7 + n :])
    if carry:
        block_all, refs = (refs[0], refs[1:])
    w, wo, mask, joined, ssem, rsem, qsem = refs[:7]
    refs = refs[7:]
    pc = Place(dims)
    width, rows = h_ref.shape
    loads = load_qo(qo_all, layer, w, wo, qsem)
    greet(pc, "mates" if carry else None, True)
    riders = riders_of(pc, specs, ins, outs, refs[: 3 * n])
    gather = None
    if carry:
        gather = PlaneGather(pc, lambda q: block_all.at[:, lanes(q, rows)], *refs[3 * n :])
        block_all[:, lanes(pc.me, rows)] = block_ref[...]
        gather.start()
    g1, g2, bias = gains_of(padded_t(small_ref[layer]), width, w.shape[1])
    hidden = h_ref[...].astype(BF).astype(F32)
    normed = (hidden * rms(hidden) * g1).astype(BF)
    normed_ref[...] = normed
    fill_masks(pc, mask, padded_t(meta_ref[...]), docs_ref[...])
    loads[0].wait()
    joined[...] = tn(w[...], normed) + bias
    cos_part = cos_ref[...]
    sin_part = sin_ref[...]
    half = HD // 2

    def turned(row):
        u1 = joined[pl.ds(row, half), :]
        u2 = joined[pl.ds(row + half, half), :]
        return (u1 * cos_part - u2 * sin_part, u2 * cos_part + u1 * sin_part)

    for g in range(KVH):
        r1, r2 = turned((H + g) * HD)
        kv_ref[0, g, :half, :] = r1.astype(BF)
        kv_ref[0, g, half:, :] = r2.astype(BF)
        v0 = (H + KVH + g) * HD
        kv_ref[0, KVH + g] = joined[v0 : v0 + HD, :].astype(BF)
    sends = [
        remote(kv_ref.at[0], kv_ref.at[j], ssem.at[j - 1], rsem.at[j - 1], pc.along(j))
        for j in range(1, nk)
    ]
    for c in sends:
        c.start()
    scale = HD**-0.5
    for head in range(H):
        r1, r2 = turned(head * HD)
        q_ref[head, :half, :] = (r1 * scale).astype(BF)
        q_ref[head, half:, :] = (r2 * scale).astype(BF)
    for c in sends:
        c.wait()
    for r in riders:
        r.start()
    for g in range(KVH):
        keys = [kv_ref[j, g].T for j in range(nk)]
        values = [kv_ref[j, KVH + g] for j in range(nk)]

        def one_head(i, carried):
            head = g * GROUP + i
            q = q_ref[head]
            s = [nn(keys[j], q) + mask[j] for j in range(nk)]
            top = s[0].max(axis=0, keepdims=True)
            for j in range(1, nk):
                top = jnp.maximum(top, s[j].max(axis=0, keepdims=True))
            e = [jnp.exp(x - top) for x in s]
            total = e[0].sum(axis=0, keepdims=True)
            for j in range(1, nk):
                total = total + e[j].sum(axis=0, keepdims=True)
            out = nn(values[0], e[0].astype(BF))
            for j in range(1, nk):
                out = out + nn(values[j], e[j].astype(BF))
            lse_ref[head] = top + jnp.log(total)
            mixed_ref[head] = (out / total).astype(BF)
            return carried

        lax.fori_loop(0, GROUP, one_head, 0)
        if carry and g == 0:
            for step in range(1, min(6, pc.count)):
                gather.before(step)
    mixed = mixed_ref[...].reshape(H * HD, rows)
    loads[1].wait()
    residual = hidden + tn(wo[...], mixed)
    res_ref[...] = residual
    n2_ref[...] = (residual * rms(residual) * g2).astype(BF)
    if carry:
        for step in range(min(6, pc.count), pc.count):
            gather.before(step)
        gather.finish()
    for r in riders:
        r.finish()


def attention_forward(dims, nk, cid, layer, hidden, small, meta, docs, cos_part, sin_part, qo_all,
                      specs, riders, block=None):
    width, rows = hidden.shape
    count = dims[0] * dims[2]
    carry = block is not None
    qkv = qo_all.shape[2] - width
    sds = jax.ShapeDtypeStruct
    outs = [
        sds((width, rows), BF),
        sds((H, HD, rows), BF),
        sds((nk, 2 * KVH, HD, rows), BF),
        sds((H, 1, rows), F32),
        sds((H, HD, rows), BF),
        sds((width, rows), F32),
        sds((width, rows), BF),
    ] + rider_shapes(dims, specs, riders)
    dma = pltpu.SemaphoreType.DMA
    n = len(specs)
    if carry:
        outs.append(sds((width, count * rows), BF))
    out = call(
        functools.partial(attention_forward_kernel, dims, nk, layer, specs, carry),
        "attention_forward",
        cid,
        tuple(outs),
        [VM] * 7 + [AN] * n + [VM] * carry,
        [VM] * 6 + [AN] + [VM] * carry + [AN] * n,
        [
            pltpu.VMEM((width, qkv), BF),
            pltpu.VMEM((width, width), BF),
            pltpu.VMEM((nk, rows, rows), F32),
            pltpu.VMEM((qkv, rows), F32),
            dma((nk - 1,)),
            dma((nk - 1,)),
            dma((2,)),
        ]
        + line_sems(dims) * n
        + [dma((count - 1,))] * (2 * carry),
        (hidden, small, meta, docs, cos_part, sin_part, qo_all, *([block] * carry), *riders),
    )
    return (out[:7], out[7:])


def attention_backward_kernel(
    dims, nk, layer, specs, carry, g_ref, small_ref, meta_ref, docs_ref, cos_ref, sin_ref,
    h_ref, normed_ref, q_ref, kv_ref, lse_ref, mixed_ref, qo_all, *refs
):
    n = len(specs)
    if carry:
        parts_ref, res_ref, refs = (refs[0], refs[1], refs[2:])
    ins, refs = (refs[:n], refs[n:])
    gh_ref, dqo_ref, dsmall_ref = refs[:3]
    outs, refs = (refs[3 : 3 + n], refs[3 + n :])
    if carry:
        out_ref, refs = (refs[0], refs[1:])
    w, wo, mask, dmix, dkv, out_kv, in_kv, gj, ssem, rsem, qsem = refs[:11]
    refs = refs[11:]
    pc = Place(dims)
    width, rows = h_ref.shape
    qkv = w.shape[1]
    loads = load_qo(qo_all, layer, w, wo, qsem)
    greet(pc, "mates" if carry else None, True)
    riders = riders_of(pc, specs, ins, outs, refs[: 3 * n])
    scatter = None
    if carry:
        scatter = ReadyScatter(pc, parts_ref, *refs[3 * n :])
        scatter.start()
    for r in riders:
        r.start()
    g1 = column(padded_t(small_ref[layer]), 0, width // 128)
    fill_masks(pc, mask, padded_t(meta_ref[...]), docs_ref[...])
    grl = g_ref[...].astype(BF)
    loads[1].wait()
    dmix[...] = nn(wo[...], grl).astype(BF).reshape(dmix.shape)
    dqo_ref[:, qkv:] = nt(mixed_ref[...].reshape(H * HD, rows), grl).astype(BF)
    if carry:
        scatter.early()
        scatter.diagonal()
    cos_part = cos_ref[...]
    sin_part = sin_ref[...]
    half = HD // 2
    scale = HD**-0.5
    dkv[...] = jnp.zeros_like(dkv)

    def unturned(d1, d2):
        return (d1 * cos_part + d2 * sin_part, d2 * cos_part - d1 * sin_part)

    for g in range(KVH):
        keys_t = [kv_ref[j, g] for j in range(nk)]
        keys = [k.T for k in keys_t]
        values = [kv_ref[j, KVH + g].T for j in range(nk)]

        def one_head(i, carried):
            head = g * GROUP + i
            q = q_ref[head]
            do = dmix[head]
            lse = lse_ref[head]
            p = [jnp.exp(nn(keys[j], q) + mask[j] - lse) for j in range(nk)]
            dp = [nn(values[j], do) for j in range(nk)]
            delta = (p[0] * dp[0]).sum(axis=0, keepdims=True)
            for j in range(1, nk):
                delta = delta + (p[j] * dp[j]).sum(axis=0, keepdims=True)
            dq = jnp.zeros((HD, rows), F32)
            for j in range(nk):
                ds = (p[j] * (dp[j] - delta)).astype(BF)
                dkv[j, g] += nt(q, ds)
                dkv[j, KVH + g] += nt(do, p[j].astype(BF))
                dq = dq + nn(keys_t[j], ds)
            dq = dq * scale
            r1, r2 = unturned(dq[:half], dq[half:])
            gj[pl.ds(pl.multiple_of(head * HD, HD), half), :] = r1.astype(BF)
            gj[pl.ds(pl.multiple_of(head * HD + half, half), half), :] = r2.astype(BF)
            return carried

        lax.fori_loop(0, GROUP, one_head, 0)
        if carry and g == 0:
            scatter.late()
    for j in range(1, nk):
        out_kv[j - 1] = dkv[j].astype(BF)
    sends = [
        remote(out_kv.at[j - 1], in_kv.at[j - 1], ssem.at[j - 1], rsem.at[j - 1],
               pc.along(pc.nb - j))
        for j in range(1, nk)
    ]
    for c in sends:
        c.start()
    for c in sends:
        c.wait()
    own = dkv[0]
    for j in range(1, nk):
        own = own + in_kv[j - 1].astype(F32)
    for g in range(KVH):
        r1, r2 = unturned(own[g, :half], own[g, half:])
        k0 = (H + g) * HD
        gj[k0 : k0 + half, :] = r1.astype(BF)
        gj[k0 + half : k0 + HD, :] = r2.astype(BF)
        v0 = (H + KVH + g) * HD
        gj[v0 : v0 + HD, :] = own[KVH + g].astype(BF)
    gjv = gj[...]
    n1 = width // 128
    dsmall_ref[n1 : n1 + qkv // 128, :] = rows_of(gjv.astype(F32))
    loads[0].wait()
    dqo_ref[:, :qkv] = nt(normed_ref[...], gjv).astype(BF)
    gn = nn(w[...], gjv)
    hidden = h_ref[...].astype(BF).astype(F32)
    scale_one = rms(hidden)
    unit = hidden * scale_one
    dsmall_ref[:n1, :] = rows_of(gn * unit)
    u = gn * g1
    gh_ref[...] = g_ref[...] + scale_one * (u - unit * jnp.mean(u * unit, axis=0, keepdims=True))
    if carry:

        def store(total):
            out_ref[...] = res_ref[...] + total

        scatter.finish(store)
    for r in riders:
        r.finish()


def attention_backward(dims, nk, cid, layer, g, small, meta, docs, cos_part, sin_part, hidden,
                       normed, q, kv, lse, mixed, qo_all, specs, riders, late=()):
    width, rows = hidden.shape
    carry = len(late) > 0
    qkv = qo_all.shape[2] - width
    sds = jax.ShapeDtypeStruct
    outs = [
        sds((width, rows), F32),
        sds((width, qkv + width), BF),
        sds(((width + qkv) // 128, 128), F32),
    ] + rider_shapes(dims, specs, riders)
    dma = pltpu.SemaphoreType.DMA
    block = (2 * KVH, HD, rows)
    n = len(specs)
    if carry:
        outs.append(sds((width, rows), F32))
    out = call(
        functools.partial(attention_backward_kernel, dims, nk, layer, specs, carry),
        "attention_backward",
        cid,
        tuple(outs),
        [VM] * 3 + [AN] * n + [VM] * carry,
        [VM] * 12 + [AN] + [VM] * len(late) + [AN] * n,
        [
            pltpu.VMEM((width, qkv), BF),
            pltpu.VMEM((width, width), BF),
            pltpu.VMEM((nk, rows, rows), F32),
            pltpu.VMEM((H, HD, rows), BF),
            pltpu.VMEM((nk,) + block, F32),
            pltpu.VMEM((nk - 1,) + block, BF),
            pltpu.VMEM((nk - 1,) + block, BF),
            pltpu.VMEM((qkv, rows), BF),
            dma((nk - 1,)),
            dma((nk - 1,)),
            dma((2,)),
        ]
        + line_sems(dims) * n
        + (scatter_scratch(dims, width, rows)[2:] if carry else []),
        (g, small, meta, docs, cos_part, sin_part, hidden, normed, q, kv, lse, mixed, qo_all,
         *late, *riders),
    )
    return (out[:3], out[3:])


def steps_of(count):
    return (5, count - 1)


def lanes(slot, rows):
    return pl.ds(pl.multiple_of(slot * rows, rows), rows)


def transpose_into(dst, src):
    cols = src.shape[1]
    for c0 in range(0, cols, 128):
        c1 = min(c0 + 128, cols)
        dst[c0:c1, :] = src[:, c0:c1].T


def feed_forward_kernel(dims, specs, x_ref, res_ref, wgu_ref, wd_ref, *refs):
    n = len(specs)
    ins, refs = (refs[:n], refs[n:])
    out_ref, x_all, gu_all = refs[:3]
    outs, refs = (refs[3 : 3 + n], refs[3 + n :])
    wgu_t, wd_t, gu, inner, near, away, back, hop, ss, sr, gs, gr = refs[:12]
    pc = Place(dims)
    width, rows = x_ref.shape
    ff = wd_ref.shape[0]
    greet(pc, "mates", n > 0)
    riders = riders_of(pc, specs, ins, outs, refs[12:])
    gather = PlaneGather(pc, lambda q: x_all.at[:, lanes(q, rows)], gs, gr)
    scatter = PlaneScatter(pc, near, away, back, hop, ss, sr)
    x_all[:, lanes(pc.me, rows)] = x_ref[...]
    gather.start()
    for r in riders:
        r.start()
    transpose_into(wgu_t, wgu_ref)
    transpose_into(wd_t, wd_ref)
    neighbours, last = steps_of(pc.count)
    chunk = 32 if ff % 32 == 0 else 16

    def step_body(step, carry):
        for k in range(pc.count):
            @pl.when(step == k)
            def _():
                gather.before(k)

        slot = pick(step, gather.order)
        sl = lanes(slot, rows)
        gu[...] = nn(wgu_t[...], x_all[:, sl])

        def act(i, c):
            r = pl.multiple_of(i * chunk, chunk)
            gate = gu[pl.ds(r, chunk), :]
            up = gu[pl.ds(ff + r, chunk), :]
            gu_all[pl.ds(r, chunk), sl] = gate.astype(BF)
            gu_all[pl.ds(ff + r, chunk), sl] = up.astype(BF)
            inner[pl.ds(r, chunk), :] = (gate * jax.nn.sigmoid(gate) * up).astype(BF)
            return c

        lax.fori_loop(0, ff // chunk, act, 0)
        scatter.put(step, nn(wd_t[...], inner[...]))

        @pl.when(step == neighbours)
        def _():
            scatter.early()

        return carry

    lax.fori_loop(0, pc.count, step_body, 0)
    scatter.diagonal()

    def store(total):
        out_ref[...] = res_ref[...] + total

    scatter.result(store)
    gather.finish()
    for r in riders:
        r.finish()


def feed_forward(dims, cid, x, residual, wgu, wd, specs, riders):
    width, rows = x.shape
    count = dims[0] * dims[2]
    two_ff, ff = (wgu.shape[1], wd.shape[0])
    sds = jax.ShapeDtypeStruct
    dma = pltpu.SemaphoreType.DMA
    n = len(specs)
    out = call(
        functools.partial(feed_forward_kernel, dims, specs),
        "feed_forward",
        cid,
        (
            sds((width, rows), F32),
            sds((width, count * rows), BF),
            sds((two_ff, count * rows), BF),
            *rider_shapes(dims, specs, riders),
        ),
        [VM] * 3 + [AN] * n,
        [VM] * 4 + [AN] * n,
        [
            pltpu.VMEM((two_ff, width), BF),
            pltpu.VMEM((width, ff), BF),
            pltpu.VMEM((two_ff, rows), F32),
            pltpu.VMEM((ff, rows), BF),
        ]
        + scatter_scratch(dims, width, rows)
        + [dma((count - 1,)), dma((count - 1,))]
        + line_sems(dims) * n,
        (x, residual, wgu, wd, *riders),
    )
    return (out[:3], out[3:])


def feed_backward_kernel(
    dims, layer, specs, g_ref, res_ref, x_all, gu_all, wgu_ref, wd_ref, small_ref, *refs
):
    n = len(specs)
    ins, refs = (refs[:n], refs[n:])
    gr_ref, dwgu_ref, dwd_ref, dsmall_ref = refs[:4]
    outs, refs = (refs[4 : 4 + n], refs[4 + n :])
    g_all, inner, ggu, gi, near, away, back, hop, ss, sr, gs, gr = refs[:12]
    pc = Place(dims)
    width, rows = g_ref.shape
    ff = wd_ref.shape[0]
    greet(pc, "mates", n > 0)
    riders = riders_of(pc, specs, ins, outs, refs[12:])
    gather = PlaneGather(pc, lambda q: g_all.at[:, lanes(q, rows)], gs, gr)
    scatter = PlaneScatter(pc, near, away, back, hop, ss, sr)
    g_all[:, lanes(pc.me, rows)] = g_ref[...].astype(BF)
    gather.start()
    for r in riders:
        r.start()
    neighbours, last = steps_of(pc.count)
    chunk = 32 if ff % 32 == 0 else 16

    def step_body(step, carry):
        for k in range(pc.count):
            @pl.when(step == k)
            def _():
                gather.before(k)

        slot = pick(step, gather.order)
        sl = lanes(slot, rows)
        gi[...] = nn(wd_ref[...], g_all[:, sl])

        def act(i, c):
            r = pl.multiple_of(i * chunk, chunk)
            gate = gu_all[pl.ds(r, chunk), sl].astype(F32)
            up = gu_all[pl.ds(ff + r, chunk), sl].astype(F32)
            grad = gi[pl.ds(r, chunk), :]
            sig = jax.nn.sigmoid(gate)
            silu = gate * sig
            inner[pl.ds(r, chunk), sl] = (silu * up).astype(BF)
            ggu[pl.ds(r, chunk), sl] = (grad * up * sig * (1.0 + gate * (1.0 - sig))).astype(BF)
            ggu[pl.ds(ff + r, chunk), sl] = (grad * silu).astype(BF)
            return c

        lax.fori_loop(0, ff // chunk, act, 0)
        scatter.put(step, nn(wgu_ref[...], ggu[:, sl]))

        @pl.when(step == neighbours)
        def _():
            scatter.early()

        return carry

    lax.fori_loop(0, pc.count, step_body, 0)
    scatter.diagonal()
    dwd_ref[...] = nt(inner[...], g_all[...]).astype(BF)
    scatter.late()
    part = width // 2
    for r in range(2):
        dwgu_ref[r * part : (r + 1) * part, :] = nt(
            x_all[r * part : (r + 1) * part, :], ggu[...]
        ).astype(BF)

    def store(total):
        residual = res_ref[...]
        scale_two = rms(residual)
        unit = residual * scale_two
        n1 = width // 128
        dsmall_ref[...] = rows_of(total * unit)
        u = total * column(padded_t(small_ref[layer]), n1, n1)
        gr_ref[...] = g_ref[...].astype(BF).astype(F32) + scale_two * (
            u - unit * jnp.mean(u * unit, axis=0, keepdims=True)
        )

    scatter.finish(store)
    gather.finish()
    for r in riders:
        r.finish()


def feed_backward(dims, cid, layer, g, residual, x_all, gu_all, wgu, wd, small, specs, riders):
    width, rows = g.shape
    count = dims[0] * dims[2]
    two_ff, ff = (wgu.shape[1], wd.shape[0])
    sds = jax.ShapeDtypeStruct
    dma = pltpu.SemaphoreType.DMA
    n = len(specs)
    out = call(
        functools.partial(feed_backward_kernel, dims, layer, specs),
        "feed_backward",
        cid,
        (
            sds((width, rows), F32),
            sds(wgu.shape, BF),
            sds(wd.shape, BF),
            sds((width // 128, 128), F32),
            *rider_shapes(dims, specs, riders),
        ),
        [VM] * 4 + [AN] * n,
        [VM] * 7 + [AN] * n,
        [
            pltpu.VMEM((width, count * rows), BF),
            pltpu.VMEM((ff, count * rows), BF),
            pltpu.VMEM((two_ff, count * rows), BF),
            pltpu.VMEM((ff, rows), F32),
        ]
        + scatter_scratch(dims, width, rows)
        + [dma((count - 1,)), dma((count - 1,))]
        + line_sems(dims) * n,
        (g, residual, x_all, gu_all, wgu, wd, small, *riders),
    )
    return (out[:4], out[4:])


def feed_both_kernel(
    dims, layer, x_ref, res_ref, g_ref, g_all, wgu_ref, wd_ref, small_ref,
    gr_ref, dwgu_ref, dwd_ref, dsmall_ref, parts_ref,
    x_all, inner, ggu, wgu_t, wd_t, gu, gi, near, away, back, hop, ss, sr, gs, gr,
):
    pc = Place(dims)
    width, rows = g_ref.shape
    ff = wd_ref.shape[0]
    greet(pc, "mates", False)
    gather = PlaneGather(pc, lambda q: x_all.at[:, lanes(q, rows)], gs, gr)
    scatter = PlaneScatter(pc, near, away, back, hop, ss, sr)
    x_all[:, lanes(pc.me, rows)] = x_ref[...]
    gather.start()
    transpose_into(wgu_t, wgu_ref)
    transpose_into(wd_t, wd_ref)
    neighbours, last = steps_of(pc.count)
    chunk = 32 if ff % 32 == 0 else 16

    def step_body(step, carry):
        for k in range(pc.count):
            @pl.when(step == k)
            def _():
                gather.before(k)

        slot = pick(step, gather.order)
        sl = lanes(slot, rows)
        gu[...] = nn(wgu_t[...], x_all[:, sl])
        gi[...] = nn(wd_ref[...], g_all[:, sl])

        def act(i, c):
            r = pl.multiple_of(i * chunk, chunk)
            gate = gu[pl.ds(r, chunk), :]
            up = gu[pl.ds(ff + r, chunk), :]
            grad = gi[pl.ds(r, chunk), :]
            sig = jax.nn.sigmoid(gate)
            silu = gate * sig
            inner[pl.ds(r, chunk), sl] = (silu * up).astype(BF)
            ggu[pl.ds(r, chunk), sl] = (grad * up * sig * (1.0 + gate * (1.0 - sig))).astype(BF)
            ggu[pl.ds(ff + r, chunk), sl] = (grad * silu).astype(BF)
            return c

        lax.fori_loop(0, ff // chunk, act, 0)
        scatter.put(step, nn(wgu_ref[...], ggu[:, sl]))

        @pl.when(step == neighbours)
        def _():
            scatter.early()

        @pl.when(step == last)
        def _():
            scatter.diagonal()

        parts_ref[slot] = nn(wd_t[...], inner[:, sl]).astype(BF)
        return carry

    lax.fori_loop(0, pc.count, step_body, 0)
    dwd_ref[...] = nt(inner[...], g_all[...]).astype(BF)
    scatter.late()
    part = width // 2
    for r in range(2):
        dwgu_ref[r * part : (r + 1) * part, :] = nt(
            x_all[r * part : (r + 1) * part, :], ggu[...]
        ).astype(BF)

    def store(total):
        residual = res_ref[...]
        scale_two = rms(residual)
        unit = residual * scale_two
        n1 = width // 128
        dsmall_ref[...] = rows_of(total * unit)
        u = total * column(padded_t(small_ref[layer]), n1, n1)
        gr_ref[...] = g_ref[...].astype(BF).astype(F32) + scale_two * (
            u - unit * jnp.mean(u * unit, axis=0, keepdims=True)
        )

    scatter.finish(store)
    gather.finish()


def feed_both(dims, cid, layer, x, residual, g, g_all, wgu, wd, small):
    width, rows = g.shape
    count = dims[0] * dims[2]
    two_ff, ff = (wgu.shape[1], wd.shape[0])
    sds = jax.ShapeDtypeStruct
    dma = pltpu.SemaphoreType.DMA
    return call(
        functools.partial(feed_both_kernel, dims, layer),
        "feed_both",
        cid,
        (
            sds((width, rows), F32),
            sds(wgu.shape, BF),
            sds(wd.shape, BF),
            sds((width // 128, 128), F32),
            sds((count, width, rows), BF),
        ),
        [VM] * 5,
        [VM] * 7,
        [
            pltpu.VMEM((width, count * rows), BF),
            pltpu.VMEM((ff, count * rows), BF),
            pltpu.VMEM((two_ff, count * rows), BF),
            pltpu.VMEM((two_ff, width), BF),
            pltpu.VMEM((width, ff), BF),
            pltpu.VMEM((two_ff, rows), F32),
            pltpu.VMEM((ff, rows), F32),
        ]
        + scatter_scratch(dims, width, rows)
        + [dma((count - 1,)), dma((count - 1,))],
        (x, residual, g, g_all, wgu, wd, small),
    )


def reduce_kernel(
    dims, cut, qo0, qo1, sa0, sa1, sb0, sb1, gu1, wd1, wd0, gu0a, gu0,
    qo_out, small_out, gu_got, wd_got,
    buf1, bufa, buf0, bufw, gsum, wsum, small, sm_in, sm_mid, sm_line, z_out, z_in, half_sum,
    lsem, ps, pr, gs, gr, ws, wr, ls, lr, zs, zr, near, away, back, hop, ss, sr, *rest
):
    pc = Place(dims)
    ns, nb, nf = dims
    greet(pc, "all", True)
    line = LineExchange(pc, lambda t: gu0.at[t, cut:nf], lambda t: buf0.at[t], rest)
    line.start()
    loads = [
        pltpu.make_async_copy(gu1, buf1, lsem.at[0]),
        pltpu.make_async_copy(gu0a, bufa, lsem.at[1]),
        pltpu.make_async_copy(wd0, bufw.at[0], lsem.at[2]),
        pltpu.make_async_copy(wd1, bufw.at[1], lsem.at[3]),
    ]
    for c in loads:
        c.start()
    n1 = sb0.shape[0]
    per = small.shape[0] // ns
    nr = sa0.shape[0] + n1
    small[...] = jnp.zeros_like(small)
    for l, (a, g) in enumerate(((sa0, sb0), (sa1, sb1))):
        small[l * per : l * per + n1] = a[0:n1]
        small[l * per + n1 : l * per + 2 * n1] = g[...]
        small[l * per + 2 * n1 : l * per + nr] = a[n1 : a.shape[0]]
    smalls = [
        remote(small, sm_in.at[e - 1], ls.at[e - 1], lr.at[e - 1], pc.plane(e))
        for e in range(1, pc.count)
    ]
    for c in smalls:
        c.start()
    scatter = PlaneScatter(pc, near, away, back, hop, ss, sr)
    if pc.two_level:
        order = pc.slots()
    else:
        order = tuple(pc.slot_from(e) for e in range(pc.count))
    neighbours, last = steps_of(pc.count)

    def step_body(step, carry):
        slot = pick(step, order)
        f = slot % nf
        for l, ref in enumerate((qo0, qo1)):
            @pl.when(slot // nf == l)
            def _():
                scatter.put(step, ref[:, f].astype(F32))

        @pl.when(step == neighbours)
        def _():
            scatter.early()

        return carry

    lax.fori_loop(0, pc.count, step_body, 0)
    scatter.diagonal()

    def send_rows(l, f):
        e = (l * nf + f - pc.me + pc.count) % pc.count

        @pl.when(e != 0)
        def _():
            remote(
                gsum.at[l, f], gu_got.at[pc.me], ps.at[e - 1], pr.at[e - 1], (l, pc.b, f)
            ).start()

        @pl.when(e == 0)
        def _():
            pltpu.make_async_copy(gsum.at[l, f], gu_got.at[pc.me], lsem.at[4]).start()

    def total_of(buf):
        total = buf[0].astype(F32)
        for t in range(1, nb):
            total = total + buf[t].astype(F32)
        return total.astype(BF)

    loads[0].wait()
    for f in range(nf):
        gsum[1, f] = total_of(buf1.at[:, f])
        send_rows(1, f)
    loads[2].wait()
    loads[3].wait()
    wsum[0] = total_of(bufw.at[0])
    wsum[1] = total_of(bufw.at[1])
    own = pltpu.make_async_copy(wsum.at[pc.s], wd_got.at[pc.s], lsem.at[5])
    own.start()
    across = []
    for d in range(1, ns):
        y = (pc.s + d) % ns
        across.append(
            remote(wsum.at[y], wd_got.at[pc.s], ws.at[d - 1], wr.at[d - 1], (y, pc.b, pc.f))
        )
        across[-1].start()
    loads[1].wait()
    for f in range(cut):
        gsum[0, f] = total_of(bufa.at[:, f])
        send_rows(0, f)
    total = small[...]
    for e, c in enumerate(smalls):
        c.wait()
        total = total + sm_in[e]
    sm_mid[...] = total
    m = nb - 1
    lines = [
        remote(sm_mid, sm_line.at[d - 1], zs.at[m + d - 1], zr.at[m + d - 1], pc.along(d))
        for d in range(1, nb)
    ]
    for c in lines:
        c.start()

    def store(value):
        half_sum[...] = value

    scatter.result(store)
    z_out[...] = half_sum[...].astype(BF)
    sends = []
    for d in range(1, nb):
        t = pc.along(d)
        sends.append(remote(z_out.at[t[1]], z_in.at[d - 1], zs.at[d - 1], zr.at[d - 1], t))
    for c in sends:
        c.start()
    line.finish()
    for f in range(cut, nf):
        gsum[0, f] = total_of(buf0.at[:, f - cut])
        send_rows(0, f)
    mine = z_out[pc.b].astype(F32)
    for d, c in enumerate(sends):
        c.wait()
        mine = mine + z_in[d].astype(F32)
    qo_out[...] = mine
    total = sm_mid[...]
    for d, c in enumerate(lines):
        c.wait()
        total = total + sm_line[d]
    small_out[...] = total
    for k in range(pc.count - 1):
        c = remote(gsum.at[0, 0], gu_got.at[pc.me], ps.at[k], pr.at[k], pc.plane(1))
        c.wait()
    pltpu.make_async_copy(gsum.at[0, 0], gu_got.at[pc.me], lsem.at[4]).wait()
    own.wait()
    for c in across:
        c.wait()


def reduce_gradients(dims, cid, cut, qo0, qo1, smalls, gu1, wd1, wd0, gu0a, gu0):
    ns, nb, nf = dims
    count = ns * nf
    dr, cols = qo0.shape[2:]
    two_ff = gu0.shape[3]
    half, width = wd0.shape[1:]
    rows = smalls[0].shape[0] + smalls[2].shape[0]
    small = (ns * (-(-rows // 8) * 8), 128)
    sds = jax.ShapeDtypeStruct
    dma = pltpu.SemaphoreType.DMA
    return call(
        functools.partial(reduce_kernel, dims, cut),
        "reduce_gradients",
        cid,
        (
            sds((dr, cols), F32),
            sds(small, F32),
            sds((count, dr, two_ff), BF),
            sds((ns, half, width), BF),
        ),
        [VM] * 4,
        [VM] * 6 + [AN] * 5,
        [
            pltpu.VMEM((nb, nf, dr, two_ff), BF),
            pltpu.VMEM((nb, cut, dr, two_ff), BF),
            pltpu.VMEM((nb, nf - cut, dr, two_ff), BF),
            pltpu.VMEM((ns, nb, half, width), BF),
            pltpu.VMEM((ns, nf, dr, two_ff), BF),
            pltpu.VMEM((ns, half, width), BF),
            pltpu.VMEM(small, F32),
            pltpu.VMEM((count - 1,) + small, F32),
            pltpu.VMEM(small, F32),
            pltpu.VMEM((nb - 1,) + small, F32),
            pltpu.VMEM((nb, dr, cols), BF),
            pltpu.VMEM((nb - 1, dr, cols), BF),
            pltpu.VMEM((nb, dr, cols), F32),
            dma((6,)),
            dma((count - 1,)),
            dma((count - 1,)),
            dma((1,)),
            dma((1,)),
            dma((ns - 1,)),
            dma((ns - 1,)),
            dma((count - 1,)),
            dma((count - 1,)),
            dma((2 * (nb - 1),)),
            dma((2 * (nb - 1),)),
        ]
        + scatter_scratch(dims, nb, dr, cols)
        + line_sems(dims),
        (qo0, qo1, *smalls, gu1, wd1, wd0, gu0a, gu0),
    )


def lay_out_kernel(
    dims, gu, wd, qo, small, out0, out1, gh0, gh1, take_out, take_grad,
    block_out, input_grad, g1, wqkv, bqkv, wout, g2, wgu, wdn
):
    ns, nb, nf = dims
    half = wd.shape[1]
    s = lax.axis_index("section")
    qkv = wqkv.shape[2]
    width = wout.shape[2]
    wqkv[0] = qo[:, :qkv]
    wout[0] = qo[:, qkv:]
    for y in range(ns):
        wdn[0, y * half : (y + 1) * half, :] = wd[y].astype(F32)
        for f in range(nf):
            got = gu[y * nf + f].astype(F32)
            for part in range(2):
                for b in range(nb):
                    c0 = column_start(dims, part, b, f, y, half)
                    k0 = (part * nb + b) * half
                    wgu[0, :, c0 : c0 + half] = got[:, k0 : k0 + half]
    n1 = width // 128
    per = small.shape[0] // ns
    rows = small[pl.ds(pl.multiple_of(s * per, 8), per), :]
    for k in range(n1):
        g1[0:1, k * 128 : (k + 1) * 128] = rows[k : k + 1]
        g2[0:1, k * 128 : (k + 1) * 128] = rows[n1 + k : n1 + k + 1]
    for k in range(qkv // 128):
        bqkv[0:1, k * 128 : (k + 1) * 128] = rows[2 * n1 + k : 2 * n1 + k + 1]
    for out, pair, take in (
        (block_out, (out0, out1), take_out),
        (input_grad, (gh0, gh1), take_grad),
    ):
        for l in range(ns):
            @pl.when(s == l)
            def _():
                out[0, l] = pair[l][...].T
                out[0, 1 - l] = take[...].T.astype(F32)


def lay_out(dims, qkv, args):
    ns, nb, nf = dims
    gu, wd, qo = args[:3]
    width, rows = args[4].shape
    dr = qo.shape[0]
    sds = jax.ShapeDtypeStruct
    tokens = sds((1, ns, rows, width), F32)
    return pl.pallas_call(
        functools.partial(lay_out_kernel, dims),
        name="lay_out",
        out_shape=(
            tokens,
            tokens,
            sds((1, width), F32),
            sds((1, dr, qkv), F32),
            sds((1, qkv), F32),
            sds((1, dr, width), F32),
            sds((1, width), F32),
            sds((1, dr, gu.shape[0] * gu.shape[2]), F32),
            sds((1, ns * wd.shape[1], width), F32),
        ),
        in_specs=[VM] * len(args),
        out_specs=[VM] * 9,
        compiler_params=pltpu.CompilerParams(vmem_limit_bytes=VMEM_LIMIT),
    )(*args)


def shards(
    dims,
    tokens_in,
    positions,
    doc_ids,
    out_grad,
    norm1_gain,
    w_qkv,
    b_qkv,
    w_out,
    norm2_gain,
    w_gate_up,
    w_down,
):
    ns, nb, nf = dims
    seqs, rows, width = tokens_in.shape
    s = lax.axis_index("section")
    b = lax.axis_index("blk")
    dr = w_qkv.shape[1]
    qkv = w_qkv.shape[2]
    fr = w_down.shape[1]
    half = fr // ns
    ff = nb * half
    nk = min(nb, 1 + (LONGEST - 1 + rows - 1) // rows)

    tokens = lax.dynamic_index_in_dim(tokens_in, s, 0, keepdims=False)
    cot = lax.dynamic_index_in_dim(out_grad, s, 0, keepdims=False)
    pos = lax.dynamic_index_in_dim(positions, s, 0, keepdims=False)
    docs = lax.dynamic_index_in_dim(doc_ids, s, 0, keepdims=False).astype(F32)
    freq = jnp.exp(jnp.arange(HD // 2, dtype=F32) * (-2.0 / HD) * math.log(1000000.0))
    phase = freq[:, None] * pos.astype(F32)[None, :]
    cos_part, sin_part = (jnp.cos(phase), jnp.sin(phase))
    docs = docs.reshape(nb, rows)
    picked = (b - jnp.arange(nk) + nb) % nb
    meta = jnp.take(docs, picked, axis=0).reshape(nk * rows // 128, 128)
    query_docs = lax.dynamic_slice_in_dim(docs, b, 1)
    hidden = tokens.T.astype(F32)
    g = cot.T.astype(F32)

    wd = w_down[0].reshape(ns, half, width)
    qo = jnp.concatenate([w_qkv[0], w_out[0]], axis=1)
    small = jnp.concatenate([norm1_gain[0], norm2_gain[0], b_qkv[0]])
    total = -(-small.shape[0] // 1024) * 1024
    small = jnp.pad(small, (0, total - small.shape[0])).reshape(-1, 128)
    gup, wdp, gu_first, qo_all, small_all = gather_weights(dims, w_gate_up, wd, qo, small)
    qo_all = qo_all.reshape(ns, width, qkv + width)
    wide = (width, 2 * ff)

    common = (small_all, meta, query_docs, cos_part, sin_part, qo_all)
    a0, (wd0,) = attention_forward(dims, nk, 1, 0, hidden, *common, (("gather", 0),), (wdp,))
    wd0 = wd0.reshape(ff, width)
    wgu0 = gu_first.reshape(wide)
    f0, (gu1,) = feed_forward(dims, 3, a0[6], a0[5], wgu0, wd0, (("gather", 1),), (gup,))
    wgu1 = gu1.reshape(wide)
    a1, (wd1, g_all) = attention_forward(
        dims, nk, 2, 1, f0[0], *common, (("gather", 1),), (wdp,), cot.T
    )
    wd1 = wd1.reshape(ff, width)

    line_gu = (nb, nf, dr, 2 * ff)
    line_wd = (nb, half, width)
    everything = (0, half)
    cut = max(1, nf // 4)
    b1 = feed_both(dims, 4, 1, a1[6], a1[5], g, g_all, wgu1, wd1, small_all)
    ab1, (dwd1, out1) = attention_backward(
        dims, nk, 7, 1, b1[0], *common[:5], f0[0], *a1[:5], qo_all,
        (("exchange", everything),), (b1[2].reshape(line_wd),), (b1[4], a1[5]),
    )
    b0, (dgu1,) = feed_backward(
        dims, 6, 0, ab1[0], a0[5], f0[1], f0[2], wgu0, wd0, small_all,
        (("exchange", (0, nf)),), (b1[1].reshape(line_gu),),
    )
    dgu0 = b0[1].reshape(line_gu)
    ab0, (dwd0, dgu0a) = attention_backward(
        dims, nk, 8, 0, b0[0], *common[:5], hidden, *a0[:5], qo_all,
        (("exchange", everything), ("exchange", (0, cut))), (b0[2].reshape(line_wd), dgu0),
    )

    def swapped(values):
        give = jnp.where(s == 0, values[1], values[0]).astype(BF)
        return lax.ppermute(give, "section", [(0, 1), (1, 0)])

    take_out = swapped((f0[0], out1))
    take_grad = swapped((ab0[0], ab1[0]))
    line_qo = (nb, nf, dr, qkv + width)
    grad_qo, small_sum, gu_got, wd_got = reduce_gradients(
        dims, 9, cut, ab0[1].reshape(line_qo), ab1[1].reshape(line_qo),
        (ab0[2], ab1[2], b0[3], b1[3]), dgu1, dwd1, dwd0, dgu0a, dgu0,
    )
    return lay_out(
        dims,
        qkv,
        (gu_got, wd_got, grad_qo, small_sum, f0[0], out1, ab0[0], ab1[0], take_out, take_grad),
    )


def solution(mesh):
    dims = (mesh.shape["section"], mesh.shape["blk"], mesh.shape["fsdp"])
    return jax.shard_map(
        functools.partial(shards, dims),
        mesh=mesh,
        in_specs=(
            P("fsdp", "blk", None),
            P("fsdp", "blk"),
            P("fsdp", None),
            P("fsdp", "blk", None),
            P("section", None),
            P("section", ("blk", "fsdp"), None),
            P("section", None),
            P("section", ("blk", "fsdp"), None),
            P("section", None),
            P("section", ("blk", "fsdp"), None),
            P("section", ("blk", "fsdp"), None),
        ),
        out_specs=(
            P("section", "fsdp", "blk", None),
            P("section", "fsdp", "blk", None),
            P("section", None),
            P("section", ("blk", "fsdp"), None),
            P("section", None),
            P("section", ("blk", "fsdp"), None),
            P("section", None),
            P("section", ("blk", "fsdp"), None),
            P("section", ("blk", "fsdp"), None),
        ),
        check_vma=False,
    )
```

```python
import functools
import math

import jax
import jax.numpy as jnp
from jax import lax
from jax.experimental import pallas as pl
from jax.experimental.pallas import tpu as pltpu
from jax.sharding import PartitionSpec as P

H = 14
KVH = 2
HD = 64
GROUP = H // KVH
LONGEST = 512
NEG = -1e30
BF = jnp.bfloat16
F32 = jnp.float32
MESH = pl.DeviceIdType.MESH
VMEM_LIMIT = 60 * 2**20
VM = pl.BlockSpec(memory_space=pltpu.VMEM)
AN = pl.BlockSpec(memory_space=pl.ANY)


def nn(a, b):
    return lax.dot_general(a, b, (((1,), (0,)), ((), ())), preferred_element_type=F32)


def nt(a, b):
    return lax.dot_general(a, b, (((1,), (1,)), ((), ())), preferred_element_type=F32)


def tn(a, b):
    return lax.dot_general(a, b, (((0,), (0,)), ((), ())), preferred_element_type=F32)


def other(f):
    return f + 1 - 2 * (f % 2)


class Place:
    def __init__(self, dims):
        self.ns, self.nb, self.nf = dims
        self.count = self.ns * self.nf
        self.s = lax.axis_index("section")
        self.b = lax.axis_index("blk")
        self.f = lax.axis_index("fsdp")
        self.me = self.s * self.nf + self.f
        self.two_level = self.ns == 2 and self.nf == 4

    def plane(self, e):
        q = (self.me + e) % self.count
        return (q // self.nf, self.b, q % self.nf)

    def slot_from(self, e):
        return (self.me + self.count - e) % self.count

    def along(self, d):
        return (self.s, (self.b + d) % self.nb, self.f)

    def mates(self):
        s, b, f = (self.s, self.b, self.f)
        xf = (f + 2) % 4
        return ((s, b, other(f)), (s, b, xf), (1 - s, b, f))

    def slots(self):
        s, f = (self.s, self.f)
        xf = (f + 2) % 4
        t = 1 - s
        return (
            s * 4 + f,
            s * 4 + other(f),
            s * 4 + xf,
            t * 4 + f,
            s * 4 + other(xf),
            t * 4 + other(f),
            t * 4 + xf,
            t * 4 + other(xf),
        )


def pick(i, values):
    total = 0
    for k, v in enumerate(values):
        total = total + jnp.where(i == k, v, 0)
    return total


def greet(place, plane, along):
    barrier = pltpu.get_barrier_semaphore()
    count = 0
    if plane:
        if place.two_level and plane == "mates":
            targets = list(place.mates())
        else:
            targets = [place.plane(e) for e in range(1, place.count)]
        for t in targets:
            pl.semaphore_signal(barrier, 1, device_id=t, device_id_type=MESH)
        count += len(targets)
    if along:
        for d in range(1, place.nb):
            pl.semaphore_signal(barrier, 1, device_id=place.along(d), device_id_type=MESH)
        count += place.nb - 1
    pl.semaphore_wait(barrier, count)


def remote(src, dst, ssem, rsem, device):
    return pltpu.make_async_remote_copy(
        src_ref=src,
        dst_ref=dst,
        send_sem=ssem,
        recv_sem=rsem,
        device_id=device,
        device_id_type=MESH,
    )


class PlaneGather:
    def __init__(self, place, slot, ssem, rsem):
        self.place, self.slot, self.ssem, self.rsem = (place, slot, ssem, rsem)
        if place.two_level:
            self.order = place.slots()
        else:
            self.order = tuple(place.slot_from(e) for e in range(place.count))

    def copy(self, k, q, device):
        v = self.slot(q)
        return remote(v, v, self.ssem.at[k], self.rsem.at[k], device)

    def start(self):
        pc = self.place
        if pc.two_level:
            core, xm, ym = pc.mates()
            self.copy(1, self.order[0], xm).start()
            self.copy(2, self.order[0], ym).start()
            self.copy(0, self.order[0], core).start()
        else:
            for e in range(1, pc.count):
                self.copy(e - 1, self.order[0], pc.plane(e)).start()

    def waited(self, k):
        self.copy(k, self.order[k + 1], self.place.plane(1)).wait_recv()

    def before(self, step):
        if step == 0:
            return
        pc = self.place
        if not pc.two_level:
            self.waited(step - 1)
            return
        core, xm, ym = pc.mates()
        c = pc.f % 2
        if step == 2:
            self.waited(1)
            self.copy(3, self.order[2], core).start()
            self.waited(2)
            self.copy(4, self.order[3], core).start()
            which = c * self.order[3] + (1 - c) * self.order[2]
            far = (
                c * xm[0] + (1 - c) * ym[0],
                pc.b,
                c * xm[2] + (1 - c) * ym[2],
            )
            self.copy(5, which, far).start()
        elif step == 3:
            return
        elif step == 6:
            self.waited(5)
            self.copy(6, self.order[6], core).start()
        else:
            self.waited(step - 1)

    def finish(self):
        n = self.place.count - 1
        for k in range(n):
            self.copy(k, self.order[0], self.place.plane(1)).wait_send()


class PlaneScatter:
    def __init__(self, place, near, away, back, hop, ssem, rsem):
        self.place = place
        self.near, self.away, self.back, self.hop = (near, away, back, hop)
        self.ssem, self.rsem = (ssem, rsem)

    def put(self, step, value):
        pc = self.place
        if not pc.two_level:
            @pl.when(step == 0)
            def _():
                self.near[0] = value

            @pl.when(step > 0)
            def _():
                e = pc.count - step
                self.away[e - 1] = value.astype(BF)
                q = (pc.me + e) % pc.count
                remote(
                    self.away.at[e - 1],
                    self.back.at[e - 1],
                    self.ssem.at[e - 1],
                    self.rsem.at[e - 1],
                    (q // pc.nf, pc.b, q % pc.nf),
                ).start()
            return
        core, xm, ym = pc.mates()
        here = (step == 0) | (step == 2) | (step == 3) | (step == 6)
        q = pick(step, (0, 0, 1, 2, 1, 2, 3, 3))

        @pl.when(here)
        def _():
            self.near[q] = value

        @pl.when(jnp.logical_not(here))
        def _():
            self.away[q] = value.astype(BF)
            self.core_copy(q).start()

    def core_copy(self, q):
        core = self.place.mates()[0]
        return remote(self.away.at[q], self.back.at[q], self.ssem.at[q], self.rsem.at[q], core)

    def far_copy(self, e):
        return remote(self.away.at[e - 1], self.back.at[e - 1], self.ssem.at[e - 1],
                      self.rsem.at[e - 1], self.place.plane(e))

    def hop_copy(self, k, device):
        return remote(
            self.hop.at[k], self.hop.at[k + 3], self.ssem.at[4 + k], self.rsem.at[4 + k], device
        )

    def targets(self):
        pc = self.place
        core, xm, ym = pc.mates()
        c = pc.f % 2
        first = (c * xm[0] + (1 - c) * ym[0], pc.b, c * xm[2] + (1 - c) * ym[2])
        second = (c * ym[0] + (1 - c) * xm[0], pc.b, c * ym[2] + (1 - c) * xm[2])
        return (first, second)

    def early(self):
        pc = self.place
        if not pc.two_level:
            return
        c = pc.f % 2
        first, second = self.targets()
        self.core_copy(1).wait_recv()
        self.core_copy(2).wait_recv()
        q = c * 1 + (1 - c) * 2
        self.hop[0] = (self.mine(q) + self.back[q].astype(F32)).astype(BF)
        self.hop_copy(0, first).start()

    def diagonal(self):
        pc = self.place
        if not pc.two_level:
            return
        first, second = self.targets()
        self.core_copy(3).wait_recv()
        self.hop[1] = (self.mine(3) + self.back[3].astype(F32)).astype(BF)
        self.hop_copy(1, first).start()

    def mine(self, q):
        return self.near[q]

    def result(self, store):
        self.late()
        self.finish(store)

    def late(self):
        pc = self.place
        if not pc.two_level:
            return
        c = pc.f % 2
        first, second = self.targets()
        self.hop_copy(1, first).wait_recv()
        q = c * 2 + (1 - c) * 1
        self.hop[2] = (
            self.mine(q) + self.back[q].astype(F32) + self.hop[4].astype(F32)
        ).astype(BF)
        self.hop_copy(2, second).start()

    def finish(self, store):
        pc = self.place
        if not pc.two_level:
            total = self.mine(0)
            for e in range(1, pc.count):
                self.far_copy(e).wait()
                total = total + self.back[e - 1].astype(F32)
            store(total)
            return
        first, second = self.targets()
        self.core_copy(0).wait_recv()
        self.hop_copy(0, first).wait_recv()
        self.hop_copy(2, second).wait_recv()
        store(
            self.mine(0)
            + self.back[0].astype(F32)
            + self.hop[3].astype(F32)
            + self.hop[5].astype(F32)
        )
        for q in range(4):
            self.core_copy(q).wait_send()
        self.hop_copy(0, first).wait_send()
        self.hop_copy(1, first).wait_send()
        self.hop_copy(2, second).wait_send()


class ReadyScatter(PlaneScatter):
    def __init__(self, place, parts, back, hop, ssem, rsem):
        super().__init__(place, None, None, back, hop, ssem, rsem)
        self.parts = parts
        if place.two_level:
            o = place.slots()
            self.here = (o[0], o[2], o[3], o[6])
            self.gone = (o[1], o[4], o[5], o[7])

    def mine(self, q):
        if not self.place.two_level:
            return self.parts[self.place.me].astype(F32)
        return self.parts[pick(q, self.here)].astype(F32)

    def core_copy(self, q):
        core = self.place.mates()[0]
        v = self.parts.at[self.gone[q]]
        return remote(v, self.back.at[q], self.ssem.at[q], self.rsem.at[q], core)

    def far_copy(self, e):
        pc = self.place
        v = self.parts.at[(pc.me + e) % pc.count]
        return remote(v, self.back.at[e - 1], self.ssem.at[e - 1], self.rsem.at[e - 1],
                      pc.plane(e))

    def start(self):
        pc = self.place
        if pc.two_level:
            for q in (2, 1, 3, 0):
                self.core_copy(q).start()
        else:
            for e in range(1, pc.count):
                self.far_copy(e).start()


class LineGather:
    def __init__(self, place, piece, out, sems):
        self.place, self.piece, self.out = (place, piece, out)
        self.lsem, self.ss, self.sr = sems
        self.k = 0

    def local(self):
        return pltpu.make_async_copy(self.piece, self.out.at[self.place.b], self.lsem)

    def hop(self, way, k, came):
        pc = self.place
        t = pc.b - way * (k - (0 if came else 1))
        src = self.piece if k == 1 and not came else self.out.at[t]
        i = k - 1 + (0 if way == 1 else pc.nb - 1)
        return remote(
            src, self.out.at[t], self.ss.at[i], self.sr.at[i], (pc.s, pc.b + way, pc.f)
        )

    def sends(self, way, k):
        b, nb = (self.place.b, self.place.nb)
        return (b >= k - 1) & (b < nb - 1) if way == 1 else (b <= nb - k) & (b > 0)

    def comes(self, way, k):
        b, nb = (self.place.b, self.place.nb)
        return b >= k if way == 1 else b <= nb - 1 - k

    def arrived(self, k):
        for way in (1, -1):
            @pl.when(self.comes(way, k))
            def _():
                self.hop(way, k, True).wait_recv()

    def start(self):
        self.local().start()
        self.service()

    def service(self):
        if self.k == self.place.nb - 1:
            return
        self.k += 1
        if self.k > 1:
            self.arrived(self.k - 1)
        for way in (1, -1):
            @pl.when(self.sends(way, self.k))
            def _():
                self.hop(way, self.k, False).start()

    def finish(self):
        last = self.place.nb - 1
        while self.k < last:
            self.service()
        self.arrived(last)
        for k in range(1, last + 1):
            for way in (1, -1):
                @pl.when(self.sends(way, k))
                def _():
                    self.hop(way, k, False).wait_send()
        self.local().wait()


class LineReduce:
    def __init__(self, place, terms, store, sems):
        self.place, self.terms, self.store = (place, terms, store)
        self.out, self.came, self.ss, self.sr = sems
        self.k = 0

    def index(self, way, k):
        return k - 1 + (0 if way == 1 else self.place.nb - 1)

    def hop(self, way, k):
        pc = self.place
        i = self.index(way, k)
        return remote(
            self.out.at[i], self.came.at[i], self.ss.at[i], self.sr.at[i],
            (pc.s, pc.b + way, pc.f),
        )

    def rank(self, way):
        pc = self.place
        return pc.b if way == 1 else pc.nb - 1 - pc.b

    def sends(self, way, k):
        r = self.rank(way)
        return (r < k) & (r < self.place.nb - 1)

    def start(self):
        self.service()

    def service(self):
        nb = self.place.nb
        if self.k == nb - 1:
            return
        self.k += 1
        k = self.k
        for way in (1, -1):
            r = self.rank(way)
            t = nb - k + r if way == 1 else k - 1 - r
            i = self.index(way, k)

            @pl.when(self.sends(way, k) & (r == 0))
            def _():
                self.out[i] = self.terms(t)

            if k > 1:
                @pl.when(self.sends(way, k) & (r > 0))
                def _():
                    self.hop(way, k - 1).wait_recv()
                    total = self.terms(t).astype(F32) + self.came[i - 1].astype(F32)
                    self.out[i] = total.astype(BF)

            @pl.when(self.sends(way, k))
            def _():
                self.hop(way, k).start()

    def finish(self):
        pc = self.place
        last = pc.nb - 1
        while self.k < last:
            self.service()
        right, left = (self.index(1, last), self.index(-1, last))

        @pl.when(pc.b == 0)
        def _():
            self.hop(-1, last).wait_recv()
            self.store(self.terms(pc.b).astype(F32) + self.came[left].astype(F32))

        @pl.when(pc.b == last)
        def _():
            self.hop(1, last).wait_recv()
            self.store(self.terms(pc.b).astype(F32) + self.came[right].astype(F32))

        @pl.when((pc.b > 0) & (pc.b < last))
        def _():
            self.hop(1, last).wait_recv()
            self.hop(-1, last).wait_recv()
            self.store(
                self.terms(pc.b).astype(F32)
                + self.came[right].astype(F32)
                + self.came[left].astype(F32)
            )

        for k in range(1, last + 1):
            for way in (1, -1):
                @pl.when(self.sends(way, k))
                def _():
                    self.hop(way, k).wait_send()


def gather_scratch(dims):
    dma = pltpu.SemaphoreType.DMA
    return [dma(()), dma((2 * (dims[1] - 1),)), dma((2 * (dims[1] - 1),))]


def reduce_scratch(dims, *block):
    dma = pltpu.SemaphoreType.DMA
    n = 2 * (dims[1] - 1)
    return [pltpu.VMEM((n,) + block, BF), pltpu.VMEM((n,) + block, BF), dma((n,)), dma((n,))]


class Riders:
    def __init__(self, dims, specs, arrays):
        self.dims, self.specs, self.arrays = (dims, specs, arrays)
        self.shapes = []
        self.places = []
        self.scratch = []
        self.sizes = []
        for spec, a in zip(specs, arrays):
            if spec[0] == "gather":
                shape = (dims[1],) + a.shape[1:]
                self.places.append(AN)
                scratch = gather_scratch(dims)
            else:
                lo, hi = spec[1]
                shape = (hi - lo,) + a.shape[2:]
                self.places.append(VM)
                scratch = reduce_scratch(dims, *shape)
            self.shapes.append(jax.ShapeDtypeStruct(shape, a.dtype))
            self.scratch += scratch
            self.sizes.append(len(scratch))
        self.count = len(specs)

    def board(self, place, ins, outs, scratch):
        out = []
        for spec, size, a, o in zip(self.specs, self.sizes, ins, outs):
            mine, scratch = (scratch[:size], scratch[size:])
            if spec[0] == "gather":
                out.append(LineGather(place, a.at[spec[1]], o, mine))
            else:
                lo, hi = spec[1]

                def store(value, o=o):
                    o[...] = value.astype(BF)

                out.append(
                    LineReduce(place, lambda t, a=a, lo=lo, hi=hi: a[t, lo:hi], store, mine)
                )
        return (out, scratch)


def each(riders, what):
    for r in riders:
        getattr(r, what)()


def scatter_scratch(dims, *block):
    count = dims[0] * dims[2]
    if dims[0] == 2 and dims[2] == 4:
        near, away, hops, sems = (4, 4, 6, 7)
    else:
        near, away, hops, sems = (1, count - 1, 1, count - 1)
    return [
        pltpu.VMEM((near,) + block, F32),
        pltpu.VMEM((away,) + block, BF),
        pltpu.VMEM((away,) + block, BF),
        pltpu.VMEM((hops,) + block, BF),
        pltpu.SemaphoreType.DMA((sems,)),
        pltpu.SemaphoreType.DMA((sems,)),
    ]


def call(kernel, name, cid, outs, out_specs, in_specs, scratch, args):
    params = pltpu.CompilerParams(
        collective_id=cid, has_side_effects=True, vmem_limit_bytes=VMEM_LIMIT
    )
    return pl.pallas_call(
        kernel,
        name=name,
        out_shape=outs,
        in_specs=in_specs,
        out_specs=out_specs,
        scratch_shapes=scratch,
        compiler_params=params,
    )(*args)


def column_start(dims, part, b, f, y, half):
    ns, nb, nf = dims
    return part * nb * nf * ns * half + ((b * nf + f) * ns + y) * half


def gather_weights_kernel(
    dims, w_ref, wd, qo, small, gup, wdp, gu_first, qo_all, small_all,
    pack, lsem, ps, pr, zs, zr, qs, qr, ms, mr, *rest
):
    pc = Place(dims)
    ns, nb, nf = dims
    half = wd.shape[1]
    greet(pc, "all", True)
    firsts = []
    for d in range(1, nb):
        firsts.append(
            remote(qo, qo_all.at[pc.s, pc.b, pc.f], zs.at[d - 1], zr.at[d - 1], pc.along(d))
        )
        firsts[-1].start()
    local = [
        pltpu.make_async_copy(qo, qo_all.at[pc.s, pc.b, pc.f], lsem.at[0]),
        pltpu.make_async_copy(wd.at[pc.s], wdp.at[pc.s], lsem.at[1]),
        pltpu.make_async_copy(small, small_all.at[pc.s], lsem.at[2]),
    ]
    for c in local:
        c.start()
    across = []
    for d in range(1, ns):
        y = (pc.s + d) % ns
        t = (y, pc.b, pc.f)
        across.append(remote(wd.at[y], wdp.at[pc.s], ms.at[2 * d - 2], mr.at[2 * d - 2], t))
        across.append(remote(small, small_all.at[pc.s], ms.at[2 * d - 1], mr.at[2 * d - 1], t))
    for c in across:
        c.start()
    for y in range(ns):
        for f in range(nf):
            pieces = []
            for part in range(2):
                for b in range(nb):
                    c0 = column_start(dims, part, b, f, y, half)
                    pieces.append(w_ref[0, :, c0 : c0 + half])
            pack[y, f] = jnp.concatenate(pieces, axis=1)
    own = pltpu.make_async_copy(pack.at[pc.s, pc.f], gup.at[pc.s, pc.f], lsem.at[3])
    own.start()
    plane = []
    for e in range(1, pc.count):
        t = pc.plane(e)
        plane.append(
            remote(pack.at[t[0], t[2]], gup.at[pc.s, pc.f], ps.at[e - 1], pr.at[e - 1], t)
        )
    for c in plane:
        c.start()
    n = pc.count - 1
    gathers = []
    for d in range(nb):
        b = (pc.b + nb - d) % nb
        gathers.append(
            PlaneGather(
                pc,
                lambda q, b=b: qo_all.at[q // nf, b, q % nf],
                qs.at[pl.ds(d * n, n)],
                qr.at[pl.ds(d * n, n)],
            )
        )
    local[0].wait()
    gathers[0].start()
    own.wait()
    for c in plane:
        c.wait()
    line = LineGather(pc, gup.at[0], gu_first, rest)
    line.start()
    for d in range(1, nb):
        firsts[d - 1].wait()
        gathers[d].start()
        for step in range(1, min(6, pc.count)):
            gathers[d - 1].before(step)
    line.service()
    for step in range(1, min(6, pc.count)):
        gathers[nb - 1].before(step)
    line.service()
    for step in range(min(6, pc.count), pc.count):
        for g in gathers:
            g.before(step)
    for g in gathers:
        g.finish()
    for c in local[1:]:
        c.wait()
    for c in across:
        c.wait()
    line.finish()


def gather_weights(dims, w, wd, qo, small):
    ns, nb, nf = dims
    count = ns * nf
    half, width = wd.shape[1:]
    dr = qo.shape[0]
    two_ff = 2 * nb * half
    sds = jax.ShapeDtypeStruct
    outs = (
        sds((ns, nf, dr, two_ff), BF),
        sds((ns, half, width), BF),
        sds((nb, nf, dr, two_ff), BF),
        sds((ns, nb, nf) + qo.shape, BF),
        sds((ns,) + small.shape, F32),
    )
    dma = pltpu.SemaphoreType.DMA
    return call(
        functools.partial(gather_weights_kernel, dims),
        "gather_weights",
        0,
        outs,
        [AN] * 5,
        [VM, AN, AN, AN],
        [
            pltpu.VMEM((ns, nf, dr, two_ff), BF),
            dma((4,)),
            dma((count - 1,)),
            dma((count - 1,)),
            dma((nb - 1,)),
            dma((nb - 1,)),
            dma((nb * (count - 1),)),
            dma((nb * (count - 1),)),
            dma((2 * (ns - 1),)),
            dma((2 * (ns - 1),)),
        ]
        + gather_scratch(dims),
        (w, wd, qo, small),
    )


def rms(values):
    return lax.rsqrt(jnp.mean(values * values, axis=0, keepdims=True) + 1e-06)


def column(rows_t, first, count):
    return jnp.concatenate([rows_t[:, k : k + 1] for k in range(first, first + count)], axis=0)


def rows_of(values):
    v = folded(values)
    return jnp.concatenate(
        [v[k : k + 128].T.sum(axis=0, keepdims=True) for k in range(0, v.shape[0], 128)], axis=0
    )


def folded(v):
    out = v[:, :128]
    for k in range(1, v.shape[1] // 128):
        out = out + v[:, k * 128 : (k + 1) * 128]
    return out


def fill_masks(pc, mask, meta_t, query_docs):
    nk, rows = mask.shape[:2]
    key_i = lax.broadcasted_iota(jnp.int32, (rows, rows), 0)
    query_i = lax.broadcasted_iota(jnp.int32, (rows, rows), 1)
    per = rows // 128
    for j in range(nk):
        same = column(meta_t, j * per, per) == query_docs
        if j == 0:
            live = same & (key_i <= query_i)
        else:
            live = same & (key_i < (pc.b - j + 1) * rows)
        mask[j] = jnp.where(live, 0.0, NEG)


def load_qo(qo_all, layer, w, wo, sems):
    cols = w.shape[1]
    c1 = pltpu.make_async_copy(qo_all.at[layer, :, 0:cols], w, sems.at[0])
    c2 = pltpu.make_async_copy(qo_all.at[layer, :, cols : cols + wo.shape[1]], wo, sems.at[1])
    c1.start()
    c2.start()
    return (c1, c2)


def gains_of(small_t, width, qkv):
    n = width // 128
    return (
        column(small_t, 0, n),
        column(small_t, n, n),
        column(small_t, 2 * n, qkv // 128),
    )


def padded_t(v):
    n = v.shape[0]
    return jnp.concatenate([v, jnp.zeros((128 - n, 128), v.dtype)], axis=0).T


def attention_forward_kernel(
    dims, nk, layer, plan, carry, h_ref, small_ref, meta_ref, docs_ref, cos_ref, sin_ref, qo_all,
    *refs
):
    n = plan.count
    if carry:
        block_ref, refs = (refs[0], refs[1:])
    ins, refs = (refs[:n], refs[n:])
    normed_ref, q_ref, kv_ref, lse_ref, mixed_ref, res_ref, n2_ref = refs[:7]
    outs, refs = (refs[7 : 7 + n], refs[7 + n :])
    if carry:
        block_all, refs = (refs[0], refs[1:])
    w, wo, mask, joined, ssem, rsem, qsem = refs[:7]
    refs = refs[7:]
    pc = Place(dims)
    width, rows = h_ref.shape
    loads = load_qo(qo_all, layer, w, wo, qsem)
    greet(pc, "mates" if carry else None, True)
    riders, refs = plan.board(pc, ins, outs, refs)
    gather = None
    if carry:
        gather = PlaneGather(pc, lambda q: block_all.at[:, lanes(q, rows)], *refs)
        block_all[:, lanes(pc.me, rows)] = block_ref[...]
        gather.start()
    g1, g2, bias = gains_of(padded_t(small_ref[layer]), width, w.shape[1])
    hidden = h_ref[...].astype(BF).astype(F32)
    normed = (hidden * rms(hidden) * g1).astype(BF)
    normed_ref[...] = normed
    fill_masks(pc, mask, padded_t(meta_ref[...]), docs_ref[...])
    loads[0].wait()
    joined[...] = tn(w[...], normed) + bias
    cos_part = cos_ref[...]
    sin_part = sin_ref[...]
    half = HD // 2

    def turned(row):
        u1 = joined[pl.ds(row, half), :]
        u2 = joined[pl.ds(row + half, half), :]
        return (u1 * cos_part - u2 * sin_part, u2 * cos_part + u1 * sin_part)

    for g in range(KVH):
        r1, r2 = turned((H + g) * HD)
        kv_ref[0, g, :half, :] = r1.astype(BF)
        kv_ref[0, g, half:, :] = r2.astype(BF)
        v0 = (H + KVH + g) * HD
        kv_ref[0, KVH + g] = joined[v0 : v0 + HD, :].astype(BF)
    sends = [
        remote(kv_ref.at[0], kv_ref.at[j], ssem.at[j - 1], rsem.at[j - 1], pc.along(j))
        for j in range(1, nk)
    ]
    for c in sends:
        c.start()
    scale = HD**-0.5
    for head in range(H):
        r1, r2 = turned(head * HD)
        q_ref[head, :half, :] = (r1 * scale).astype(BF)
        q_ref[head, half:, :] = (r2 * scale).astype(BF)
    for c in sends:
        c.wait()
    each(riders, "start")
    for g in range(KVH):
        keys = [kv_ref[j, g].T for j in range(nk)]
        values = [kv_ref[j, KVH + g] for j in range(nk)]

        def one_head(i, carried):
            head = g * GROUP + i
            q = q_ref[head]
            s = [nn(keys[j], q) + mask[j] for j in range(nk)]
            top = s[0].max(axis=0, keepdims=True)
            for j in range(1, nk):
                top = jnp.maximum(top, s[j].max(axis=0, keepdims=True))
            e = [jnp.exp(x - top) for x in s]
            total = e[0].sum(axis=0, keepdims=True)
            for j in range(1, nk):
                total = total + e[j].sum(axis=0, keepdims=True)
            out = nn(values[0], e[0].astype(BF))
            for j in range(1, nk):
                out = out + nn(values[j], e[j].astype(BF))
            lse_ref[head] = top + jnp.log(total)
            mixed_ref[head] = (out / total).astype(BF)
            return carried

        lax.fori_loop(0, GROUP, one_head, 0)
        each(riders, "service")
        if carry and g == 0:
            for step in range(1, min(6, pc.count)):
                gather.before(step)
    mixed = mixed_ref[...].reshape(H * HD, rows)
    loads[1].wait()
    residual = hidden + tn(wo[...], mixed)
    res_ref[...] = residual
    n2_ref[...] = (residual * rms(residual) * g2).astype(BF)
    if carry:
        for step in range(min(6, pc.count), pc.count):
            gather.before(step)
        gather.finish()
    each(riders, "finish")


def attention_forward(dims, nk, cid, layer, hidden, small, meta, docs, cos_part, sin_part, qo_all,
                      plan, block=None):
    width, rows = hidden.shape
    count = dims[0] * dims[2]
    carry = block is not None
    qkv = qo_all.shape[2] - width
    sds = jax.ShapeDtypeStruct
    outs = [
        sds((width, rows), BF),
        sds((H, HD, rows), BF),
        sds((nk, 2 * KVH, HD, rows), BF),
        sds((H, 1, rows), F32),
        sds((H, HD, rows), BF),
        sds((width, rows), F32),
        sds((width, rows), BF),
    ] + plan.shapes
    dma = pltpu.SemaphoreType.DMA
    if carry:
        outs.append(sds((width, count * rows), BF))
    out = call(
        functools.partial(attention_forward_kernel, dims, nk, layer, plan, carry),
        "attention_forward",
        cid,
        tuple(outs),
        [VM] * 7 + plan.places + [VM] * carry,
        [VM] * 6 + [AN] + [VM] * carry + plan.places,
        [
            pltpu.VMEM((width, qkv), BF),
            pltpu.VMEM((width, width), BF),
            pltpu.VMEM((nk, rows, rows), F32),
            pltpu.VMEM((qkv, rows), F32),
            dma((nk - 1,)),
            dma((nk - 1,)),
            dma((2,)),
        ]
        + plan.scratch
        + [dma((count - 1,))] * (2 * carry),
        (hidden, small, meta, docs, cos_part, sin_part, qo_all, *([block] * carry), *plan.arrays),
    )
    return (out[:7], out[7:])


def attention_backward_kernel(
    dims, nk, layer, plan, carry, g_ref, small_ref, meta_ref, docs_ref, cos_ref, sin_ref,
    h_ref, normed_ref, q_ref, kv_ref, lse_ref, mixed_ref, qo_all, *refs
):
    n = plan.count
    if carry:
        parts_ref, res_ref, refs = (refs[0], refs[1], refs[2:])
    ins, refs = (refs[:n], refs[n:])
    gh_ref, dqo_ref, dsmall_ref = refs[:3]
    outs, refs = (refs[3 : 3 + n], refs[3 + n :])
    if carry:
        out_ref, refs = (refs[0], refs[1:])
    w, wo, mask, dmix, dkv, out_kv, in_kv, gj, ssem, rsem, qsem = refs[:11]
    refs = refs[11:]
    pc = Place(dims)
    width, rows = h_ref.shape
    qkv = w.shape[1]
    loads = load_qo(qo_all, layer, w, wo, qsem)
    greet(pc, "mates" if carry else None, True)
    riders, refs = plan.board(pc, ins, outs, refs)
    scatter = None
    if carry:
        scatter = ReadyScatter(pc, parts_ref, *refs)
        scatter.start()
    each(riders, "start")
    g1 = column(padded_t(small_ref[layer]), 0, width // 128)
    fill_masks(pc, mask, padded_t(meta_ref[...]), docs_ref[...])
    grl = g_ref[...].astype(BF)
    loads[1].wait()
    dmix[...] = nn(wo[...], grl).astype(BF).reshape(dmix.shape)
    dqo_ref[:, qkv:] = nt(mixed_ref[...].reshape(H * HD, rows), grl).astype(BF)
    if carry:
        scatter.early()
        scatter.diagonal()
    cos_part = cos_ref[...]
    sin_part = sin_ref[...]
    half = HD // 2
    scale = HD**-0.5
    dkv[...] = jnp.zeros_like(dkv)

    def unturned(d1, d2):
        return (d1 * cos_part + d2 * sin_part, d2 * cos_part - d1 * sin_part)

    for g in range(KVH):
        keys_t = [kv_ref[j, g] for j in range(nk)]
        keys = [k.T for k in keys_t]
        values = [kv_ref[j, KVH + g].T for j in range(nk)]

        def one_head(i, carried):
            head = g * GROUP + i
            q = q_ref[head]
            do = dmix[head]
            lse = lse_ref[head]
            p = [jnp.exp(nn(keys[j], q) + mask[j] - lse) for j in range(nk)]
            dp = [nn(values[j], do) for j in range(nk)]
            delta = (p[0] * dp[0]).sum(axis=0, keepdims=True)
            for j in range(1, nk):
                delta = delta + (p[j] * dp[j]).sum(axis=0, keepdims=True)
            dq = jnp.zeros((HD, rows), F32)
            for j in range(nk):
                ds = (p[j] * (dp[j] - delta)).astype(BF)
                dkv[j, g] += nt(q, ds)
                dkv[j, KVH + g] += nt(do, p[j].astype(BF))
                dq = dq + nn(keys_t[j], ds)
            dq = dq * scale
            r1, r2 = unturned(dq[:half], dq[half:])
            gj[pl.ds(pl.multiple_of(head * HD, HD), half), :] = r1.astype(BF)
            gj[pl.ds(pl.multiple_of(head * HD + half, half), half), :] = r2.astype(BF)
            return carried

        lax.fori_loop(0, GROUP, one_head, 0)
        each(riders, "service")
        if carry and g == 0:
            scatter.late()
    for j in range(1, nk):
        out_kv[j - 1] = dkv[j].astype(BF)
    sends = [
        remote(out_kv.at[j - 1], in_kv.at[j - 1], ssem.at[j - 1], rsem.at[j - 1],
               pc.along(pc.nb - j))
        for j in range(1, nk)
    ]
    for c in sends:
        c.start()
    for c in sends:
        c.wait()
    own = dkv[0]
    for j in range(1, nk):
        own = own + in_kv[j - 1].astype(F32)
    for g in range(KVH):
        r1, r2 = unturned(own[g, :half], own[g, half:])
        k0 = (H + g) * HD
        gj[k0 : k0 + half, :] = r1.astype(BF)
        gj[k0 + half : k0 + HD, :] = r2.astype(BF)
        v0 = (H + KVH + g) * HD
        gj[v0 : v0 + HD, :] = own[KVH + g].astype(BF)
    gjv = gj[...]
    n1 = width // 128
    dsmall_ref[n1 : n1 + qkv // 128, :] = rows_of(gjv.astype(F32))
    loads[0].wait()
    dqo_ref[:, :qkv] = nt(normed_ref[...], gjv).astype(BF)
    gn = nn(w[...], gjv)
    hidden = h_ref[...].astype(BF).astype(F32)
    scale_one = rms(hidden)
    unit = hidden * scale_one
    dsmall_ref[:n1, :] = rows_of(gn * unit)
    u = gn * g1
    gh_ref[...] = g_ref[...] + scale_one * (u - unit * jnp.mean(u * unit, axis=0, keepdims=True))
    if carry:

        def store(total):
            out_ref[...] = res_ref[...] + total

        scatter.finish(store)
    each(riders, "finish")


def attention_backward(dims, nk, cid, layer, g, small, meta, docs, cos_part, sin_part, hidden,
                       normed, q, kv, lse, mixed, qo_all, plan, late=()):
    width, rows = hidden.shape
    carry = len(late) > 0
    qkv = qo_all.shape[2] - width
    sds = jax.ShapeDtypeStruct
    outs = [
        sds((width, rows), F32),
        sds((width, qkv + width), BF),
        sds(((width + qkv) // 128, 128), F32),
    ] + plan.shapes
    dma = pltpu.SemaphoreType.DMA
    block = (2 * KVH, HD, rows)
    if carry:
        outs.append(sds((width, rows), F32))
    out = call(
        functools.partial(attention_backward_kernel, dims, nk, layer, plan, carry),
        "attention_backward",
        cid,
        tuple(outs),
        [VM] * 3 + plan.places + [VM] * carry,
        [VM] * 12 + [AN] + [VM] * len(late) + plan.places,
        [
            pltpu.VMEM((width, qkv), BF),
            pltpu.VMEM((width, width), BF),
            pltpu.VMEM((nk, rows, rows), F32),
            pltpu.VMEM((H, HD, rows), BF),
            pltpu.VMEM((nk,) + block, F32),
            pltpu.VMEM((nk - 1,) + block, BF),
            pltpu.VMEM((nk - 1,) + block, BF),
            pltpu.VMEM((qkv, rows), BF),
            dma((nk - 1,)),
            dma((nk - 1,)),
            dma((2,)),
        ]
        + plan.scratch
        + (scatter_scratch(dims, width, rows)[2:] if carry else []),
        (g, small, meta, docs, cos_part, sin_part, hidden, normed, q, kv, lse, mixed, qo_all,
         *late, *plan.arrays),
    )
    return (out[:3], out[3:])


def steps_of(count):
    return (5, count - 1)


def lanes(slot, rows):
    return pl.ds(pl.multiple_of(slot * rows, rows), rows)


def transpose_into(dst, src):
    cols = src.shape[1]
    for c0 in range(0, cols, 128):
        c1 = min(c0 + 128, cols)
        dst[c0:c1, :] = src[:, c0:c1].T


def feed_forward_kernel(dims, plan, x_ref, res_ref, wgu_ref, wd_ref, *refs):
    n = plan.count
    ins, refs = (refs[:n], refs[n:])
    out_ref, x_all, gu_all = refs[:3]
    outs, refs = (refs[3 : 3 + n], refs[3 + n :])
    wgu_t, wd_t, gu, inner, near, away, back, hop, ss, sr, gs, gr = refs[:12]
    pc = Place(dims)
    width, rows = x_ref.shape
    ff = wd_ref.shape[0]
    greet(pc, "mates", n > 0)
    riders, _ = plan.board(pc, ins, outs, refs[12:])
    gather = PlaneGather(pc, lambda q: x_all.at[:, lanes(q, rows)], gs, gr)
    scatter = PlaneScatter(pc, near, away, back, hop, ss, sr)
    x_all[:, lanes(pc.me, rows)] = x_ref[...]
    gather.start()
    each(riders, "start")
    transpose_into(wgu_t, wgu_ref)
    transpose_into(wd_t, wd_ref)
    neighbours, last = steps_of(pc.count)
    chunk = 32 if ff % 32 == 0 else 16

    def step_body(step, carry):
        for k in range(pc.count):
            @pl.when(step == k)
            def _():
                gather.before(k)

        slot = pick(step, gather.order)
        sl = lanes(slot, rows)
        gu[...] = nn(wgu_t[...], x_all[:, sl])

        def act(i, c):
            r = pl.multiple_of(i * chunk, chunk)
            gate = gu[pl.ds(r, chunk), :]
            up = gu[pl.ds(ff + r, chunk), :]
            gu_all[pl.ds(r, chunk), sl] = gate.astype(BF)
            gu_all[pl.ds(ff + r, chunk), sl] = up.astype(BF)
            inner[pl.ds(r, chunk), :] = (gate * jax.nn.sigmoid(gate) * up).astype(BF)
            return c

        lax.fori_loop(0, ff // chunk, act, 0)
        scatter.put(step, nn(wd_t[...], inner[...]))

        @pl.when(step == 3)
        def _():
            each(riders, "service")

        @pl.when(step == neighbours)
        def _():
            scatter.early()

        return carry

    lax.fori_loop(0, pc.count, step_body, 0)
    scatter.diagonal()
    each(riders, "service")

    def store(total):
        out_ref[...] = res_ref[...] + total

    scatter.result(store)
    gather.finish()
    each(riders, "finish")


def feed_forward(dims, cid, x, residual, wgu, wd, plan):
    width, rows = x.shape
    count = dims[0] * dims[2]
    two_ff, ff = (wgu.shape[1], wd.shape[0])
    sds = jax.ShapeDtypeStruct
    dma = pltpu.SemaphoreType.DMA
    out = call(
        functools.partial(feed_forward_kernel, dims, plan),
        "feed_forward",
        cid,
        (
            sds((width, rows), F32),
            sds((width, count * rows), BF),
            sds((two_ff, count * rows), BF),
            *plan.shapes,
        ),
        [VM] * 3 + plan.places,
        [VM] * 4 + plan.places,
        [
            pltpu.VMEM((two_ff, width), BF),
            pltpu.VMEM((width, ff), BF),
            pltpu.VMEM((two_ff, rows), F32),
            pltpu.VMEM((ff, rows), BF),
        ]
        + scatter_scratch(dims, width, rows)
        + [dma((count - 1,)), dma((count - 1,))]
        + plan.scratch,
        (x, residual, wgu, wd, *plan.arrays),
    )
    return (out[:3], out[3:])


def feed_backward_kernel(
    dims, layer, plan, g_ref, res_ref, x_all, gu_all, wgu_ref, wd_ref, small_ref, *refs
):
    n = plan.count
    ins, refs = (refs[:n], refs[n:])
    gr_ref, dwgu_ref, dwd_ref, dsmall_ref = refs[:4]
    outs, refs = (refs[4 : 4 + n], refs[4 + n :])
    g_all, inner, ggu, gi, near, away, back, hop, ss, sr, gs, gr = refs[:12]
    pc = Place(dims)
    width, rows = g_ref.shape
    ff = wd_ref.shape[0]
    greet(pc, "mates", n > 0)
    riders, _ = plan.board(pc, ins, outs, refs[12:])
    gather = PlaneGather(pc, lambda q: g_all.at[:, lanes(q, rows)], gs, gr)
    scatter = PlaneScatter(pc, near, away, back, hop, ss, sr)
    g_all[:, lanes(pc.me, rows)] = g_ref[...].astype(BF)
    gather.start()
    each(riders, "start")
    neighbours, last = steps_of(pc.count)
    chunk = 32 if ff % 32 == 0 else 16

    def step_body(step, carry):
        for k in range(pc.count):
            @pl.when(step == k)
            def _():
                gather.before(k)

        slot = pick(step, gather.order)
        sl = lanes(slot, rows)
        gi[...] = nn(wd_ref[...], g_all[:, sl])

        def act(i, c):
            r = pl.multiple_of(i * chunk, chunk)
            gate = gu_all[pl.ds(r, chunk), sl].astype(F32)
            up = gu_all[pl.ds(ff + r, chunk), sl].astype(F32)
            grad = gi[pl.ds(r, chunk), :]
            sig = jax.nn.sigmoid(gate)
            silu = gate * sig
            inner[pl.ds(r, chunk), sl] = (silu * up).astype(BF)
            ggu[pl.ds(r, chunk), sl] = (grad * up * sig * (1.0 + gate * (1.0 - sig))).astype(BF)
            ggu[pl.ds(ff + r, chunk), sl] = (grad * silu).astype(BF)
            return c

        lax.fori_loop(0, ff // chunk, act, 0)
        scatter.put(step, nn(wgu_ref[...], ggu[:, sl]))

        @pl.when(step == 3)
        def _():
            each(riders, "service")

        @pl.when(step == neighbours)
        def _():
            scatter.early()

        return carry

    lax.fori_loop(0, pc.count, step_body, 0)
    scatter.diagonal()
    each(riders, "service")
    dwd_ref[...] = nt(inner[...], g_all[...]).astype(BF)
    scatter.late()
    part = width // 2
    for r in range(2):
        dwgu_ref[r * part : (r + 1) * part, :] = nt(
            x_all[r * part : (r + 1) * part, :], ggu[...]
        ).astype(BF)

    def store(total):
        residual = res_ref[...]
        scale_two = rms(residual)
        unit = residual * scale_two
        n1 = width // 128
        dsmall_ref[...] = rows_of(total * unit)
        u = total * column(padded_t(small_ref[layer]), n1, n1)
        gr_ref[...] = g_ref[...].astype(BF).astype(F32) + scale_two * (
            u - unit * jnp.mean(u * unit, axis=0, keepdims=True)
        )

    scatter.finish(store)
    gather.finish()
    each(riders, "finish")


def feed_backward(dims, cid, layer, g, residual, x_all, gu_all, wgu, wd, small, plan):
    width, rows = g.shape
    count = dims[0] * dims[2]
    two_ff, ff = (wgu.shape[1], wd.shape[0])
    sds = jax.ShapeDtypeStruct
    dma = pltpu.SemaphoreType.DMA
    out = call(
        functools.partial(feed_backward_kernel, dims, layer, plan),
        "feed_backward",
        cid,
        (
            sds((width, rows), F32),
            sds(wgu.shape, BF),
            sds(wd.shape, BF),
            sds((width // 128, 128), F32),
            *plan.shapes,
        ),
        [VM] * 4 + plan.places,
        [VM] * 7 + plan.places,
        [
            pltpu.VMEM((width, count * rows), BF),
            pltpu.VMEM((ff, count * rows), BF),
            pltpu.VMEM((two_ff, count * rows), BF),
            pltpu.VMEM((ff, rows), F32),
        ]
        + scatter_scratch(dims, width, rows)
        + [dma((count - 1,)), dma((count - 1,))]
        + plan.scratch,
        (g, residual, x_all, gu_all, wgu, wd, small, *plan.arrays),
    )
    return (out[:4], out[4:])


def feed_both_kernel(
    dims, layer, x_ref, res_ref, g_ref, g_all, wgu_ref, wd_ref, small_ref,
    gr_ref, dwgu_ref, dwd_ref, dsmall_ref, parts_ref,
    x_all, inner, ggu, wgu_t, wd_t, gu, gi, near, away, back, hop, ss, sr, gs, gr,
):
    pc = Place(dims)
    width, rows = g_ref.shape
    ff = wd_ref.shape[0]
    greet(pc, "mates", False)
    gather = PlaneGather(pc, lambda q: x_all.at[:, lanes(q, rows)], gs, gr)
    scatter = PlaneScatter(pc, near, away, back, hop, ss, sr)
    x_all[:, lanes(pc.me, rows)] = x_ref[...]
    gather.start()
    transpose_into(wgu_t, wgu_ref)
    transpose_into(wd_t, wd_ref)
    neighbours, last = steps_of(pc.count)
    chunk = 32 if ff % 32 == 0 else 16

    def step_body(step, carry):
        for k in range(pc.count):
            @pl.when(step == k)
            def _():
                gather.before(k)

        slot = pick(step, gather.order)
        sl = lanes(slot, rows)
        gu[...] = nn(wgu_t[...], x_all[:, sl])
        gi[...] = nn(wd_ref[...], g_all[:, sl])

        def act(i, c):
            r = pl.multiple_of(i * chunk, chunk)
            gate = gu[pl.ds(r, chunk), :]
            up = gu[pl.ds(ff + r, chunk), :]
            grad = gi[pl.ds(r, chunk), :]
            sig = jax.nn.sigmoid(gate)
            silu = gate * sig
            inner[pl.ds(r, chunk), sl] = (silu * up).astype(BF)
            ggu[pl.ds(r, chunk), sl] = (grad * up * sig * (1.0 + gate * (1.0 - sig))).astype(BF)
            ggu[pl.ds(ff + r, chunk), sl] = (grad * silu).astype(BF)
            return c

        lax.fori_loop(0, ff // chunk, act, 0)
        scatter.put(step, nn(wgu_ref[...], ggu[:, sl]))

        @pl.when(step == neighbours)
        def _():
            scatter.early()

        @pl.when(step == last)
        def _():
            scatter.diagonal()

        parts_ref[slot] = nn(wd_t[...], inner[:, sl]).astype(BF)
        return carry

    lax.fori_loop(0, pc.count, step_body, 0)
    dwd_ref[...] = nt(inner[...], g_all[...]).astype(BF)
    scatter.late()
    part = width // 2
    for r in range(2):
        dwgu_ref[r * part : (r + 1) * part, :] = nt(
            x_all[r * part : (r + 1) * part, :], ggu[...]
        ).astype(BF)

    def store(total):
        residual = res_ref[...]
        scale_two = rms(residual)
        unit = residual * scale_two
        n1 = width // 128
        dsmall_ref[...] = rows_of(total * unit)
        u = total * column(padded_t(small_ref[layer]), n1, n1)
        gr_ref[...] = g_ref[...].astype(BF).astype(F32) + scale_two * (
            u - unit * jnp.mean(u * unit, axis=0, keepdims=True)
        )

    scatter.finish(store)
    gather.finish()


def feed_both(dims, cid, layer, x, residual, g, g_all, wgu, wd, small):
    width, rows = g.shape
    count = dims[0] * dims[2]
    two_ff, ff = (wgu.shape[1], wd.shape[0])
    sds = jax.ShapeDtypeStruct
    dma = pltpu.SemaphoreType.DMA
    return call(
        functools.partial(feed_both_kernel, dims, layer),
        "feed_both",
        cid,
        (
            sds((width, rows), F32),
            sds(wgu.shape, BF),
            sds(wd.shape, BF),
            sds((width // 128, 128), F32),
            sds((count, width, rows), BF),
        ),
        [VM] * 5,
        [VM] * 7,
        [
            pltpu.VMEM((width, count * rows), BF),
            pltpu.VMEM((ff, count * rows), BF),
            pltpu.VMEM((two_ff, count * rows), BF),
            pltpu.VMEM((two_ff, width), BF),
            pltpu.VMEM((width, ff), BF),
            pltpu.VMEM((two_ff, rows), F32),
            pltpu.VMEM((ff, rows), F32),
        ]
        + scatter_scratch(dims, width, rows)
        + [dma((count - 1,)), dma((count - 1,))],
        (x, residual, g, g_all, wgu, wd, small),
    )


def reduce_kernel(
    dims, cut, qo0, qo1, sa0, sa1, sb0, sb1, gu1, wd1, wd0, gu0a, gu0,
    qo_out, small_out, gu_got, wd_got,
    gsum, small, sm_in, sm_mid, sm_line, z_out,
    lsem, ps, pr, ws, wr, ls, lr, zs, zr, *rest
):
    pc = Place(dims)
    ns, nb, nf = dims
    line_qo = rest[:4]
    line_gu = rest[4:8]
    near, away, back, hop, ss, sr = rest[8:]
    greet(pc, "all", True)

    def keep(value):
        gsum[...] = value.astype(BF)

    line = LineReduce(pc, lambda t: gu0[t, cut:nf], keep, line_gu)
    line.start()
    n1 = sb0.shape[0]
    per = small.shape[0] // ns
    nr = sa0.shape[0] + n1
    small[...] = jnp.zeros_like(small)
    for l, (a, g) in enumerate(((sa0, sb0), (sa1, sb1))):
        small[l * per : l * per + n1] = a[0:n1]
        small[l * per + n1 : l * per + 2 * n1] = g[...]
        small[l * per + 2 * n1 : l * per + nr] = a[n1 : a.shape[0]]
    smalls = [
        remote(small, sm_in.at[e - 1], ls.at[e - 1], lr.at[e - 1], pc.plane(e))
        for e in range(1, pc.count)
    ]
    scatter = PlaneScatter(pc, near, away, back, hop, ss, sr)
    if pc.two_level:
        order = pc.slots()
    else:
        order = tuple(pc.slot_from(e) for e in range(pc.count))
    neighbours, last = steps_of(pc.count)

    def step_body(step, carry):
        slot = pick(step, order)
        f = slot % nf
        for l, ref in enumerate((qo0, qo1)):
            @pl.when(slot // nf == l)
            def _():
                scatter.put(step, ref[:, f].astype(F32))

        @pl.when(step == neighbours)
        def _():
            scatter.early()

        return carry

    lax.fori_loop(0, pc.count, step_body, 0)
    scatter.diagonal()
    for c in smalls:
        c.start()

    def send_rows(l, f, src):
        e = (l * nf + f - pc.me + pc.count) % pc.count

        @pl.when(e != 0)
        def _():
            remote(src, gu_got.at[pc.me], ps.at[e - 1], pr.at[e - 1], (l, pc.b, f)).start()

        @pl.when(e == 0)
        def _():
            pltpu.make_async_copy(src, gu_got.at[pc.me], lsem.at[0]).start()

    line.service()
    for f in range(nf):
        send_rows(1, f, gu1.at[f])
    for f in range(cut):
        send_rows(0, f, gu0a.at[f])
    for l, ref in ((0, wd0), (1, wd1)):
        @pl.when(pc.s == l)
        def _():
            pltpu.make_async_copy(ref, wd_got.at[l], lsem.at[1]).start()

        @pl.when(pc.s != l)
        def _():
            remote(ref, wd_got.at[pc.s], ws.at[0], wr.at[0], (l, pc.b, pc.f)).start()

    scatter.late()
    total = small[...]
    for e, c in enumerate(smalls):
        c.wait()
        total = total + sm_in[e]
    sm_mid[...] = total
    lines = [
        remote(sm_mid, sm_line.at[d - 1], zs.at[d - 1], zr.at[d - 1], pc.along(d))
        for d in range(1, nb)
    ]
    for c in lines:
        c.start()
    line.service()

    def store(value):
        z_out[...] = value.astype(BF)

    scatter.finish(store)

    def leave(value):
        qo_out[...] = value

    ends = LineReduce(pc, lambda t: z_out[t], leave, line_qo)
    ends.start()
    line.finish()
    for f in range(cut, nf):
        send_rows(0, f, gsum.at[f - cut])
    total = sm_mid[...]
    for d, c in enumerate(lines):
        c.wait()
        total = total + sm_line[d]
    small_out[...] = total
    ends.finish()
    for k in range(pc.count - 1):
        remote(gsum.at[0], gu_got.at[pc.me], ps.at[k], pr.at[k], pc.plane(1)).wait()
    pltpu.make_async_copy(gsum.at[0], gu_got.at[pc.me], lsem.at[0]).wait()
    pltpu.make_async_copy(wd0, wd_got.at[pc.s], lsem.at[1]).wait()
    remote(wd0, wd_got.at[pc.s], ws.at[0], wr.at[0], pc.plane(1)).wait()


def reduce_gradients(dims, cid, cut, qo0, qo1, smalls, gu1, wd1, wd0, gu0a, gu0):
    ns, nb, nf = dims
    count = ns * nf
    dr, cols = qo0.shape[2:]
    two_ff = gu0.shape[3]
    half, width = wd0.shape
    rows = smalls[0].shape[0] + smalls[2].shape[0]
    small = (ns * (-(-rows // 8) * 8), 128)
    sds = jax.ShapeDtypeStruct
    dma = pltpu.SemaphoreType.DMA
    return call(
        functools.partial(reduce_kernel, dims, cut),
        "reduce_gradients",
        cid,
        (
            sds((dr, cols), F32),
            sds(small, F32),
            sds((count, dr, two_ff), BF),
            sds((ns, half, width), BF),
        ),
        [VM] * 4,
        [VM] * 11,
        [
            pltpu.VMEM((nf - cut, dr, two_ff), BF),
            pltpu.VMEM(small, F32),
            pltpu.VMEM((count - 1,) + small, F32),
            pltpu.VMEM(small, F32),
            pltpu.VMEM((nb - 1,) + small, F32),
            pltpu.VMEM((nb, dr, cols), BF),
            dma((2,)),
            dma((count - 1,)),
            dma((count - 1,)),
            dma((ns - 1,)),
            dma((ns - 1,)),
            dma((count - 1,)),
            dma((count - 1,)),
            dma((nb - 1,)),
            dma((nb - 1,)),
        ]
        + reduce_scratch(dims, dr, cols)
        + reduce_scratch(dims, nf - cut, dr, two_ff)
        + scatter_scratch(dims, nb, dr, cols),
        (qo0, qo1, *smalls, gu1, wd1, wd0, gu0a, gu0),
    )


def lay_out_kernel(
    dims, gu, wd, qo, small, out0, out1, gh0, gh1, take_out, take_grad,
    block_out, input_grad, g1, wqkv, bqkv, wout, g2, wgu, wdn
):
    ns, nb, nf = dims
    half = wd.shape[1]
    s = lax.axis_index("section")
    qkv = wqkv.shape[2]
    width = wout.shape[2]
    wqkv[0] = qo[:, :qkv]
    wout[0] = qo[:, qkv:]
    for y in range(ns):
        wdn[0, y * half : (y + 1) * half, :] = wd[y].astype(F32)
        for f in range(nf):
            got = gu[y * nf + f].astype(F32)
            for part in range(2):
                for b in range(nb):
                    c0 = column_start(dims, part, b, f, y, half)
                    k0 = (part * nb + b) * half
                    wgu[0, :, c0 : c0 + half] = got[:, k0 : k0 + half]
    n1 = width // 128
    per = small.shape[0] // ns
    rows = small[pl.ds(pl.multiple_of(s * per, 8), per), :]
    for k in range(n1):
        g1[0:1, k * 128 : (k + 1) * 128] = rows[k : k + 1]
        g2[0:1, k * 128 : (k + 1) * 128] = rows[n1 + k : n1 + k + 1]
    for k in range(qkv // 128):
        bqkv[0:1, k * 128 : (k + 1) * 128] = rows[2 * n1 + k : 2 * n1 + k + 1]
    for out, pair, take in (
        (block_out, (out0, out1), take_out),
        (input_grad, (gh0, gh1), take_grad),
    ):
        for l in range(ns):
            @pl.when(s == l)
            def _():
                out[0, l] = pair[l][...].T
                out[0, 1 - l] = take[...].T.astype(F32)


def lay_out(dims, qkv, args):
    ns, nb, nf = dims
    gu, wd, qo = args[:3]
    width, rows = args[4].shape
    dr = qo.shape[0]
    sds = jax.ShapeDtypeStruct
    tokens = sds((1, ns, rows, width), F32)
    return pl.pallas_call(
        functools.partial(lay_out_kernel, dims),
        name="lay_out",
        out_shape=(
            tokens,
            tokens,
            sds((1, width), F32),
            sds((1, dr, qkv), F32),
            sds((1, qkv), F32),
            sds((1, dr, width), F32),
            sds((1, width), F32),
            sds((1, dr, gu.shape[0] * gu.shape[2]), F32),
            sds((1, ns * wd.shape[1], width), F32),
        ),
        in_specs=[VM] * len(args),
        out_specs=[VM] * 9,
        compiler_params=pltpu.CompilerParams(vmem_limit_bytes=VMEM_LIMIT),
    )(*args)


def shards(
    dims,
    tokens_in,
    positions,
    doc_ids,
    out_grad,
    norm1_gain,
    w_qkv,
    b_qkv,
    w_out,
    norm2_gain,
    w_gate_up,
    w_down,
):
    ns, nb, nf = dims
    seqs, rows, width = tokens_in.shape
    s = lax.axis_index("section")
    b = lax.axis_index("blk")
    dr = w_qkv.shape[1]
    qkv = w_qkv.shape[2]
    fr = w_down.shape[1]
    half = fr // ns
    ff = nb * half
    nk = min(nb, 1 + (LONGEST - 1 + rows - 1) // rows)

    tokens = lax.dynamic_index_in_dim(tokens_in, s, 0, keepdims=False)
    cot = lax.dynamic_index_in_dim(out_grad, s, 0, keepdims=False)
    pos = lax.dynamic_index_in_dim(positions, s, 0, keepdims=False)
    docs = lax.dynamic_index_in_dim(doc_ids, s, 0, keepdims=False).astype(F32)
    freq = jnp.exp(jnp.arange(HD // 2, dtype=F32) * (-2.0 / HD) * math.log(1000000.0))
    phase = freq[:, None] * pos.astype(F32)[None, :]
    cos_part, sin_part = (jnp.cos(phase), jnp.sin(phase))
    docs = docs.reshape(nb, rows)
    picked = (b - jnp.arange(nk) + nb) % nb
    meta = jnp.take(docs, picked, axis=0).reshape(nk * rows // 128, 128)
    query_docs = lax.dynamic_slice_in_dim(docs, b, 1)
    hidden = tokens.T.astype(F32)
    g = cot.T.astype(F32)

    wd = w_down[0].reshape(ns, half, width)
    qo = jnp.concatenate([w_qkv[0], w_out[0]], axis=1)
    small = jnp.concatenate([norm1_gain[0], norm2_gain[0], b_qkv[0]])
    total = -(-small.shape[0] // 1024) * 1024
    small = jnp.pad(small, (0, total - small.shape[0])).reshape(-1, 128)
    gup, wdp, gu_first, qo_all, small_all = gather_weights(dims, w_gate_up, wd, qo, small)
    qo_all = qo_all.reshape(ns, width, qkv + width)
    wide = (width, 2 * ff)

    common = (small_all, meta, query_docs, cos_part, sin_part, qo_all)
    def ride(*pairs):
        return Riders(dims, tuple(a for a, _ in pairs), tuple(v for _, v in pairs))

    a0, (wd0,) = attention_forward(dims, nk, 1, 0, hidden, *common, ride((("gather", 0), wdp)))
    wd0 = wd0.reshape(ff, width)
    wgu0 = gu_first.reshape(wide)
    f0, (gu1,) = feed_forward(dims, 3, a0[6], a0[5], wgu0, wd0, ride((("gather", 1), gup)))
    wgu1 = gu1.reshape(wide)
    a1, (wd1, g_all) = attention_forward(
        dims, nk, 2, 1, f0[0], *common, ride((("gather", 1), wdp)), cot.T
    )
    wd1 = wd1.reshape(ff, width)

    line_gu = (nb, nf, dr, 2 * ff)
    line_wd = (nb, half, width)
    everything = (0, half)
    cut = nf // 2
    b1 = feed_both(dims, 4, 1, a1[6], a1[5], g, g_all, wgu1, wd1, small_all)
    ab1, (dwd1, out1) = attention_backward(
        dims, nk, 7, 1, b1[0], *common[:5], f0[0], *a1[:5], qo_all,
        ride((("reduce", everything), b1[2].reshape(line_wd))), (b1[4], a1[5]),
    )
    b0, (dgu1,) = feed_backward(
        dims, 6, 0, ab1[0], a0[5], f0[1], f0[2], wgu0, wd0, small_all,
        ride((("reduce", (0, nf)), b1[1].reshape(line_gu))),
    )
    dgu0 = b0[1].reshape(line_gu)
    ab0, (dwd0, dgu0a) = attention_backward(
        dims, nk, 8, 0, b0[0], *common[:5], hidden, *a0[:5], qo_all,
        ride((("reduce", everything), b0[2].reshape(line_wd)), (("reduce", (0, cut)), dgu0)),
    )

    def swapped(values):
        give = jnp.where(s == 0, values[1], values[0]).astype(BF)
        return lax.ppermute(give, "section", [(0, 1), (1, 0)])

    take_out = swapped((f0[0], out1))
    take_grad = swapped((ab0[0], ab1[0]))
    line_qo = (nb, nf, dr, qkv + width)
    grad_qo, small_sum, gu_got, wd_got = reduce_gradients(
        dims, 9, cut, ab0[1].reshape(line_qo), ab1[1].reshape(line_qo),
        (ab0[2], ab1[2], b0[3], b1[3]), dgu1, dwd1, dwd0, dgu0a, dgu0,
    )
    return lay_out(
        dims,
        qkv,
        (gu_got, wd_got, grad_qo, small_sum, f0[0], out1, ab0[0], ab1[0], take_out, take_grad),
    )


def solution(mesh):
    dims = (mesh.shape["section"], mesh.shape["blk"], mesh.shape["fsdp"])
    return jax.shard_map(
        functools.partial(shards, dims),
        mesh=mesh,
        in_specs=(
            P("fsdp", "blk", None),
            P("fsdp", "blk"),
            P("fsdp", None),
            P("fsdp", "blk", None),
            P("section", None),
            P("section", ("blk", "fsdp"), None),
            P("section", None),
            P("section", ("blk", "fsdp"), None),
            P("section", None),
            P("section", ("blk", "fsdp"), None),
            P("section", ("blk", "fsdp"), None),
        ),
        out_specs=(
            P("section", "fsdp", "blk", None),
            P("section", "fsdp", "blk", None),
            P("section", None),
            P("section", ("blk", "fsdp"), None),
            P("section", None),
            P("section", ("blk", "fsdp"), None),
            P("section", None),
            P("section", ("blk", "fsdp"), None),
            P("section", ("blk", "fsdp"), None),
        ),
        check_vma=False,
    )
```

```python
import functools
import math

import jax
import jax.numpy as jnp
from jax import lax
from jax.experimental import pallas as pl
from jax.experimental.pallas import tpu as pltpu
from jax.sharding import PartitionSpec as P

H = 14
KVH = 2
HD = 64
GROUP = H // KVH
LONGEST = 512
NEG = -1e30
BF = jnp.bfloat16
F32 = jnp.float32
MESH = pl.DeviceIdType.MESH
VMEM_LIMIT = 60 * 2**20
VM = pl.BlockSpec(memory_space=pltpu.VMEM)
AN = pl.BlockSpec(memory_space=pl.ANY)


def nn(a, b):
    return lax.dot_general(a, b, (((1,), (0,)), ((), ())), preferred_element_type=F32)


def nt(a, b):
    return lax.dot_general(a, b, (((1,), (1,)), ((), ())), preferred_element_type=F32)


def tn(a, b):
    return lax.dot_general(a, b, (((0,), (0,)), ((), ())), preferred_element_type=F32)


def other(f):
    return f + 1 - 2 * (f % 2)


class Place:
    def __init__(self, dims):
        self.ns, self.nb, self.nf = dims
        self.count = self.ns * self.nf
        self.s = lax.axis_index("section")
        self.b = lax.axis_index("blk")
        self.f = lax.axis_index("fsdp")
        self.me = self.s * self.nf + self.f
        self.two_level = self.ns == 2 and self.nf == 4

    def plane(self, e):
        q = (self.me + e) % self.count
        return (q // self.nf, self.b, q % self.nf)

    def slot_from(self, e):
        return (self.me + self.count - e) % self.count

    def along(self, d):
        return (self.s, (self.b + d) % self.nb, self.f)

    def mates(self):
        s, b, f = (self.s, self.b, self.f)
        xf = (f + 2) % 4
        return ((s, b, other(f)), (s, b, xf), (1 - s, b, f))

    def slots(self):
        s, f = (self.s, self.f)
        xf = (f + 2) % 4
        t = 1 - s
        return (
            s * 4 + f,
            s * 4 + other(f),
            s * 4 + xf,
            t * 4 + f,
            s * 4 + other(xf),
            t * 4 + other(f),
            t * 4 + xf,
            t * 4 + other(xf),
        )


def pick(i, values):
    total = 0
    for k, v in enumerate(values):
        total = total + jnp.where(i == k, v, 0)
    return total


def greet(place, plane, along):
    barrier = pltpu.get_barrier_semaphore()
    count = 0
    if plane:
        if place.two_level and plane == "mates":
            targets = list(place.mates())
        else:
            targets = [place.plane(e) for e in range(1, place.count)]
        for t in targets:
            pl.semaphore_signal(barrier, 1, device_id=t, device_id_type=MESH)
        count += len(targets)
    if along:
        for d in range(1, place.nb):
            pl.semaphore_signal(barrier, 1, device_id=place.along(d), device_id_type=MESH)
        count += place.nb - 1
    pl.semaphore_wait(barrier, count)


def remote(src, dst, ssem, rsem, device):
    return pltpu.make_async_remote_copy(
        src_ref=src,
        dst_ref=dst,
        send_sem=ssem,
        recv_sem=rsem,
        device_id=device,
        device_id_type=MESH,
    )


class PlaneGather:
    def __init__(self, place, slot, ssem, rsem):
        self.place, self.slot, self.ssem, self.rsem = (place, slot, ssem, rsem)
        if place.two_level:
            self.order = place.slots()
        else:
            self.order = tuple(place.slot_from(e) for e in range(place.count))

    def copy(self, k, q, device):
        v = self.slot(q)
        return remote(v, v, self.ssem.at[k], self.rsem.at[k], device)

    def start(self):
        pc = self.place
        if pc.two_level:
            core, xm, ym = pc.mates()
            self.copy(1, self.order[0], xm).start()
            self.copy(2, self.order[0], ym).start()
            self.copy(0, self.order[0], core).start()
        else:
            for e in range(1, pc.count):
                self.copy(e - 1, self.order[0], pc.plane(e)).start()

    def waited(self, k):
        self.copy(k, self.order[k + 1], self.place.plane(1)).wait_recv()

    def before(self, step):
        if step == 0:
            return
        pc = self.place
        if not pc.two_level:
            self.waited(step - 1)
            return
        core, xm, ym = pc.mates()
        c = pc.f % 2
        if step == 2:
            self.waited(1)
            self.copy(3, self.order[2], core).start()
            self.waited(2)
            self.copy(4, self.order[3], core).start()
            which = c * self.order[3] + (1 - c) * self.order[2]
            far = (
                c * xm[0] + (1 - c) * ym[0],
                pc.b,
                c * xm[2] + (1 - c) * ym[2],
            )
            self.copy(5, which, far).start()
        elif step == 3:
            return
        elif step == 6:
            self.waited(5)
            self.copy(6, self.order[6], core).start()
        else:
            self.waited(step - 1)

    def finish(self):
        n = self.place.count - 1
        for k in range(n):
            self.copy(k, self.order[0], self.place.plane(1)).wait_send()


class PlaneScatter:
    def __init__(self, place, near, away, back, hop, ssem, rsem):
        self.place = place
        self.near, self.away, self.back, self.hop = (near, away, back, hop)
        self.ssem, self.rsem = (ssem, rsem)

    def put(self, step, value):
        pc = self.place
        if not pc.two_level:
            @pl.when(step == 0)
            def _():
                self.near[0] = value

            @pl.when(step > 0)
            def _():
                e = pc.count - step
                self.away[e - 1] = value.astype(BF)
                q = (pc.me + e) % pc.count
                remote(
                    self.away.at[e - 1],
                    self.back.at[e - 1],
                    self.ssem.at[e - 1],
                    self.rsem.at[e - 1],
                    (q // pc.nf, pc.b, q % pc.nf),
                ).start()
            return
        core, xm, ym = pc.mates()
        here = (step == 0) | (step == 2) | (step == 3) | (step == 6)
        q = pick(step, (0, 0, 1, 2, 1, 2, 3, 3))

        @pl.when(here)
        def _():
            self.near[q] = value

        @pl.when(jnp.logical_not(here))
        def _():
            self.away[q] = value.astype(BF)
            self.core_copy(q).start()

    def core_copy(self, q):
        core = self.place.mates()[0]
        return remote(self.away.at[q], self.back.at[q], self.ssem.at[q], self.rsem.at[q], core)

    def far_copy(self, e):
        return remote(self.away.at[e - 1], self.back.at[e - 1], self.ssem.at[e - 1],
                      self.rsem.at[e - 1], self.place.plane(e))

    def hop_copy(self, k, device):
        return remote(
            self.hop.at[k], self.hop.at[k + 3], self.ssem.at[4 + k], self.rsem.at[4 + k], device
        )

    def targets(self):
        pc = self.place
        core, xm, ym = pc.mates()
        c = pc.f % 2
        first = (c * xm[0] + (1 - c) * ym[0], pc.b, c * xm[2] + (1 - c) * ym[2])
        second = (c * ym[0] + (1 - c) * xm[0], pc.b, c * ym[2] + (1 - c) * xm[2])
        return (first, second)

    def early(self):
        pc = self.place
        if not pc.two_level:
            return
        c = pc.f % 2
        first, second = self.targets()
        self.core_copy(1).wait_recv()
        self.core_copy(2).wait_recv()
        q = c * 1 + (1 - c) * 2
        self.hop[0] = (self.mine(q) + self.back[q].astype(F32)).astype(BF)
        self.hop_copy(0, first).start()

    def diagonal(self):
        pc = self.place
        if not pc.two_level:
            return
        first, second = self.targets()
        self.core_copy(3).wait_recv()
        self.hop[1] = (self.mine(3) + self.back[3].astype(F32)).astype(BF)
        self.hop_copy(1, first).start()

    def mine(self, q):
        return self.near[q]

    def result(self, store):
        self.late()
        self.finish(store)

    def late(self):
        pc = self.place
        if not pc.two_level:
            return
        c = pc.f % 2
        first, second = self.targets()
        self.hop_copy(1, first).wait_recv()
        q = c * 2 + (1 - c) * 1
        self.hop[2] = (
            self.mine(q) + self.back[q].astype(F32) + self.hop[4].astype(F32)
        ).astype(BF)
        self.hop_copy(2, second).start()

    def finish(self, store):
        pc = self.place
        if not pc.two_level:
            total = self.mine(0)
            for e in range(1, pc.count):
                self.far_copy(e).wait()
                total = total + self.back[e - 1].astype(F32)
            store(total)
            return
        first, second = self.targets()
        self.core_copy(0).wait_recv()
        self.hop_copy(0, first).wait_recv()
        self.hop_copy(2, second).wait_recv()
        store(
            self.mine(0)
            + self.back[0].astype(F32)
            + self.hop[3].astype(F32)
            + self.hop[5].astype(F32)
        )
        for q in range(4):
            self.core_copy(q).wait_send()
        self.hop_copy(0, first).wait_send()
        self.hop_copy(1, first).wait_send()
        self.hop_copy(2, second).wait_send()


class ReadyScatter(PlaneScatter):
    def __init__(self, place, part, back, hop, ssem, rsem):
        super().__init__(place, None, None, back, hop, ssem, rsem)
        self.part = part
        if place.two_level:
            o = place.slots()
            self.here = (o[0], o[2], o[3], o[6])
            self.gone = (o[1], o[4], o[5], o[7])

    def mine(self, q):
        if not self.place.two_level:
            return self.part(self.place.me)[...].astype(F32)
        return self.part(pick(q, self.here))[...].astype(F32)

    def core_copy(self, q):
        core = self.place.mates()[0]
        v = self.part(self.gone[q])
        return remote(v, self.back.at[q], self.ssem.at[q], self.rsem.at[q], core)

    def far_copy(self, e):
        pc = self.place
        v = self.part((pc.me + e) % pc.count)
        return remote(v, self.back.at[e - 1], self.ssem.at[e - 1], self.rsem.at[e - 1],
                      pc.plane(e))

    def start(self):
        pc = self.place
        if pc.two_level:
            for q in (3, 2, 1, 0):
                self.core_copy(q).start()
        else:
            for e in range(1, pc.count):
                self.far_copy(e).start()


class RowSends:
    def __init__(self, place, layer, out, sems):
        self.place, self.layer, self.out = (place, layer, out)
        self.lsem, self.ss, self.sr = sems

    def copies(self, f, src):
        pc = self.place
        e = (self.layer * pc.nf + f - pc.me + pc.count) % pc.count
        own = self.out.at[pc.me]
        k = (e + pc.count - 1) % pc.count
        away = remote(src, own, self.ss.at[f], self.sr.at[k], (self.layer, pc.b, f))
        return (e, away, pltpu.make_async_copy(src, own, self.lsem))

    def start(self, f, src):
        e, away, local = self.copies(f, src)

        @pl.when(e != 0)
        def _():
            away.start()

        @pl.when(e == 0)
        def _():
            local.start()

    def finish(self, src):
        pc = self.place
        for f in range(pc.nf):
            e, away, local = self.copies(f, src)

            @pl.when(e != 0)
            def _():
                away.wait_send()

            @pl.when(e == 0)
            def _():
                local.wait()

        @pl.when(pc.s == self.layer)
        def _():
            for e in range(1, pc.count):
                q = pc.slot_from(e)
                remote(src, self.out.at[q], self.ss.at[0], self.sr.at[e - 1], pc.plane(e)).wait_recv()


def row_scratch(dims):
    dma = pltpu.SemaphoreType.DMA
    return [dma(()), dma((dims[2],)), dma((dims[0] * dims[2],))]


class LineGather:
    def __init__(self, place, piece, out, sems):
        self.place, self.piece, self.out = (place, piece, out)
        self.lsem, self.ss, self.sr = sems
        self.k = 0

    def local(self):
        return pltpu.make_async_copy(self.piece, self.out.at[self.place.b], self.lsem)

    def hop(self, way, k, came):
        pc = self.place
        t = pc.b - way * (k - (0 if came else 1))
        src = self.piece if k == 1 and not came else self.out.at[t]
        i = k - 1 + (0 if way == 1 else pc.nb - 1)
        return remote(
            src, self.out.at[t], self.ss.at[i], self.sr.at[i], (pc.s, pc.b + way, pc.f)
        )

    def sends(self, way, k):
        b, nb = (self.place.b, self.place.nb)
        return (b >= k - 1) & (b < nb - 1) if way == 1 else (b <= nb - k) & (b > 0)

    def comes(self, way, k):
        b, nb = (self.place.b, self.place.nb)
        return b >= k if way == 1 else b <= nb - 1 - k

    def arrived(self, k):
        for way in (1, -1):
            @pl.when(self.comes(way, k))
            def _():
                self.hop(way, k, True).wait_recv()

    def start(self):
        self.local().start()
        self.service()

    def service(self):
        if self.k == self.place.nb - 1:
            return
        self.k += 1
        if self.k > 1:
            self.arrived(self.k - 1)
        for way in (1, -1):
            @pl.when(self.sends(way, self.k))
            def _():
                self.hop(way, self.k, False).start()

    def finish(self):
        last = self.place.nb - 1
        while self.k < last:
            self.service()
        self.arrived(last)
        for k in range(1, last + 1):
            for way in (1, -1):
                @pl.when(self.sends(way, k))
                def _():
                    self.hop(way, k, False).wait_send()
        self.local().wait()


class LineReduce:
    def __init__(self, place, terms, store, sems):
        self.place, self.terms, self.store = (place, terms, store)
        self.out, self.came, self.ss, self.sr = sems
        self.k = 0

    def index(self, way, k):
        return k - 1 + (0 if way == 1 else self.place.nb - 1)

    def hop(self, way, k):
        pc = self.place
        i = self.index(way, k)
        return remote(
            self.out.at[i], self.came.at[i], self.ss.at[i], self.sr.at[i],
            (pc.s, pc.b + way, pc.f),
        )

    def rank(self, way):
        pc = self.place
        return pc.b if way == 1 else pc.nb - 1 - pc.b

    def sends(self, way, k):
        r = self.rank(way)
        return (r < k) & (r < self.place.nb - 1)

    def start(self):
        self.service()

    def service(self):
        nb = self.place.nb
        if self.k == nb - 1:
            return
        self.k += 1
        k = self.k
        for way in (1, -1):
            r = self.rank(way)
            t = nb - k + r if way == 1 else k - 1 - r
            i = self.index(way, k)

            @pl.when(self.sends(way, k) & (r == 0))
            def _():
                self.out[i] = self.terms(t)

            if k > 1:
                @pl.when(self.sends(way, k) & (r > 0))
                def _():
                    self.hop(way, k - 1).wait_recv()
                    total = self.terms(t).astype(F32) + self.came[i - 1].astype(F32)
                    self.out[i] = total.astype(BF)

            @pl.when(self.sends(way, k))
            def _():
                self.hop(way, k).start()

    def finish(self):
        pc = self.place
        last = pc.nb - 1
        while self.k < last:
            self.service()
        right, left = (self.index(1, last), self.index(-1, last))

        @pl.when(pc.b == 0)
        def _():
            self.hop(-1, last).wait_recv()
            self.store(self.terms(pc.b).astype(F32) + self.came[left].astype(F32))

        @pl.when(pc.b == last)
        def _():
            self.hop(1, last).wait_recv()
            self.store(self.terms(pc.b).astype(F32) + self.came[right].astype(F32))

        @pl.when((pc.b > 0) & (pc.b < last))
        def _():
            self.hop(1, last).wait_recv()
            self.hop(-1, last).wait_recv()
            self.store(
                self.terms(pc.b).astype(F32)
                + self.came[right].astype(F32)
                + self.came[left].astype(F32)
            )

        for k in range(1, last + 1):
            for way in (1, -1):
                @pl.when(self.sends(way, k))
                def _():
                    self.hop(way, k).wait_send()


def gather_scratch(dims):
    dma = pltpu.SemaphoreType.DMA
    return [dma(()), dma((2 * (dims[1] - 1),)), dma((2 * (dims[1] - 1),))]


def reduce_scratch(dims, *block):
    dma = pltpu.SemaphoreType.DMA
    n = 2 * (dims[1] - 1)
    return [pltpu.VMEM((n,) + block, BF), pltpu.VMEM((n,) + block, BF), dma((n,)), dma((n,))]


class Riders:
    def __init__(self, dims, specs, arrays):
        self.dims, self.specs, self.arrays = (dims, specs, arrays)
        self.shapes = []
        self.places = []
        self.scratch = []
        self.sizes = []
        for spec, a in zip(specs, arrays):
            if spec[0] == "gather":
                shape = (dims[1],) + a.shape[1:]
                self.places.append(AN)
                scratch = gather_scratch(dims)
            else:
                lo, hi = spec[1]
                shape = (hi - lo,) + a.shape[2:]
                self.places.append(VM)
                scratch = reduce_scratch(dims, *shape)
            self.shapes.append(jax.ShapeDtypeStruct(shape, a.dtype))
            self.scratch += scratch
            self.sizes.append(len(scratch))
        self.count = len(specs)

    def board(self, place, ins, outs, scratch):
        out = []
        for spec, size, a, o in zip(self.specs, self.sizes, ins, outs):
            mine, scratch = (scratch[:size], scratch[size:])
            if spec[0] == "gather":
                out.append(LineGather(place, a.at[spec[1]], o, mine))
            else:
                lo, hi = spec[1]

                def store(value, o=o):
                    o[...] = value.astype(BF)

                out.append(
                    LineReduce(place, lambda t, a=a, lo=lo, hi=hi: a[t, lo:hi], store, mine)
                )
        return (out, scratch)


def each(riders, what):
    for r in riders:
        getattr(r, what)()


def scatter_scratch(dims, *block):
    count = dims[0] * dims[2]
    if dims[0] == 2 and dims[2] == 4:
        near, away, hops, sems = (4, 4, 6, 7)
    else:
        near, away, hops, sems = (1, count - 1, 1, count - 1)
    return [
        pltpu.VMEM((near,) + block, F32),
        pltpu.VMEM((away,) + block, BF),
        pltpu.VMEM((away,) + block, BF),
        pltpu.VMEM((hops,) + block, BF),
        pltpu.SemaphoreType.DMA((sems,)),
        pltpu.SemaphoreType.DMA((sems,)),
    ]


def call(kernel, name, cid, outs, out_specs, in_specs, scratch, args):
    params = pltpu.CompilerParams(
        collective_id=cid, has_side_effects=True, vmem_limit_bytes=VMEM_LIMIT
    )
    return pl.pallas_call(
        kernel,
        name=name,
        out_shape=outs,
        in_specs=in_specs,
        out_specs=out_specs,
        scratch_shapes=scratch,
        compiler_params=params,
    )(*args)


def column_start(dims, part, b, f, y, half):
    ns, nb, nf = dims
    return part * nb * nf * ns * half + ((b * nf + f) * ns + y) * half


def columns_of(ref, q, nf, wide):
    return ref.at[:, q % nf, :, pl.ds(pl.multiple_of((q // nf) * wide, wide), wide)]


def gather_weights_kernel(
    dims, w_ref, wq_ref, wo_ref, wd, small, gup, wdp, gu_first, qo_first, qz, small_all,
    pack, qcol, qh, lsem, ps, pr, ms, mr, qs, qr, *rest
):
    pc = Place(dims)
    ns, nb, nf = dims
    half = wd.shape[1]
    wide = qh.shape[2]
    greet(pc, "all", True)
    qkv = wq_ref.shape[2]
    full = jnp.concatenate([wq_ref[0], wo_ref[0]], axis=1)
    for y in range(ns):
        qcol[y] = full[:, y * wide : (y + 1) * wide]
    across = []
    for d in range(1, ns):
        y = (pc.s + d) % ns
        t = (y, pc.b, pc.f)
        i = 3 * (d - 1)
        across.append(remote(qcol.at[y], qh.at[pc.s], ms.at[i], mr.at[i], t))
        across.append(remote(wd.at[y], wdp.at[pc.s], ms.at[i + 1], mr.at[i + 1], t))
        across.append(remote(small, small_all.at[pc.s], ms.at[i + 2], mr.at[i + 2], t))
    for c in across:
        c.start()
    qh[pc.s] = qcol[pc.s]
    local = [
        pltpu.make_async_copy(wd.at[pc.s], wdp.at[pc.s], lsem.at[0]),
        pltpu.make_async_copy(small, small_all.at[pc.s], lsem.at[1]),
    ]
    for c in local:
        c.start()
    own = pltpu.make_async_copy(pack.at[pc.s, pc.f], gup.at[pc.s, pc.f], lsem.at[2])

    def piece(y, f):
        e = (y * nf + f - pc.me + pc.count) % pc.count
        k = (e + pc.count - 1) % pc.count
        return (
            e,
            remote(pack.at[y, f], gup.at[pc.s, pc.f], ps.at[k], pr.at[k], (y, pc.b, f)),
        )

    for f in range(nf):
        for y in range(ns):
            pieces = []
            for part in range(2):
                for b in range(nb):
                    c0 = column_start(dims, part, b, f, y, half)
                    pieces.append(w_ref[0, :, c0 : c0 + half])
            pack[y, f] = jnp.concatenate(pieces, axis=1)
            e, c = piece(y, f)

            @pl.when(e != 0)
            def _():
                c.start()

    own.start()
    for d in range(ns - 1):
        across[3 * d].wait()
    line_q = LineGather(pc, qh, qz, rest[0:3])
    line_gu = LineGather(pc, gup.at[0], gu_first, rest[3:6])
    line_q.start()
    line_q.service()
    own.wait()
    for e in range(1, pc.count):
        q = pc.slot_from(e)
        remote(
            pack.at[0, 0], gup.at[q // nf, q % nf], ps.at[e - 1], pr.at[e - 1], pc.plane(e)
        ).wait_recv()
    line_gu.start()
    line_q.service()
    line_q.finish()
    gather = PlaneGather(pc, lambda q: columns_of(qo_first, q, nf, wide), qs, qr)
    fill = pltpu.make_async_copy(qz.at[:, 0], columns_of(qo_first, pc.me, nf, wide), lsem.at[3])
    fill.start()
    fill.wait()
    gather.start()
    line_gu.service()
    for step in range(1, min(6, pc.count)):
        gather.before(step)
    line_gu.service()
    for step in range(min(6, pc.count), pc.count):
        gather.before(step)
    gather.finish()
    for y in range(ns):
        for f in range(nf):
            e, c = piece(y, f)

            @pl.when(e != 0)
            def _():
                c.wait_send()

    for c in local:
        c.wait()
    for i, c in enumerate(across):
        if i % 3:
            c.wait()
    line_gu.finish()


def gather_weights(dims, w, wq, wo, wd, small):
    ns, nb, nf = dims
    count = ns * nf
    half, width = wd.shape[1:]
    dr = wq.shape[1]
    cols = wq.shape[2] + wo.shape[2]
    wide = cols // ns
    two_ff = 2 * nb * half
    sds = jax.ShapeDtypeStruct
    outs = (
        sds((ns, nf, dr, two_ff), BF),
        sds((ns, half, width), BF),
        sds((nb, nf, dr, two_ff), BF),
        sds((nb, nf, dr, cols), BF),
        sds((nb, ns, dr, wide), BF),
        sds((ns,) + small.shape, F32),
    )
    dma = pltpu.SemaphoreType.DMA
    return call(
        functools.partial(gather_weights_kernel, dims),
        "gather_weights",
        0,
        outs,
        [AN] * 6,
        [VM, VM, VM, AN, AN],
        [
            pltpu.VMEM((ns, nf, dr, two_ff), BF),
            pltpu.VMEM((ns, dr, wide), BF),
            pltpu.VMEM((ns, dr, wide), BF),
            dma((4,)),
            dma((count,)),
            dma((count,)),
            dma((3 * (ns - 1),)),
            dma((3 * (ns - 1),)),
            dma((count - 1,)),
            dma((count - 1,)),
        ]
        + gather_scratch(dims) * 2,
        (w, wq, wo, wd, small),
    )


def rms(values):
    return lax.rsqrt(jnp.mean(values * values, axis=0, keepdims=True) + 1e-06)


def column(rows_t, first, count):
    return jnp.concatenate([rows_t[:, k : k + 1] for k in range(first, first + count)], axis=0)


def rows_of(values):
    v = folded(values)
    return jnp.concatenate(
        [v[k : k + 128].T.sum(axis=0, keepdims=True) for k in range(0, v.shape[0], 128)], axis=0
    )


def folded(v):
    out = v[:, :128]
    for k in range(1, v.shape[1] // 128):
        out = out + v[:, k * 128 : (k + 1) * 128]
    return out


def fill_masks(pc, mask, meta_t, query_docs):
    nk, rows = mask.shape[:2]
    key_i = lax.broadcasted_iota(jnp.int32, (rows, rows), 0)
    query_i = lax.broadcasted_iota(jnp.int32, (rows, rows), 1)
    per = rows // 128
    for j in range(nk):
        same = column(meta_t, j * per, per) == query_docs
        if j == 0:
            live = same & (key_i <= query_i)
        else:
            live = same & (key_i < (pc.b - j + 1) * rows)
        mask[j] = jnp.where(live, 0.0, NEG)


def load_qo(qo, w, wo, sems):
    cols = w.shape[1]
    c1 = pltpu.make_async_copy(qo.at[:, 0:cols], w, sems.at[0])
    c2 = pltpu.make_async_copy(qo.at[:, cols : cols + wo.shape[1]], wo, sems.at[1])
    c1.start()
    c2.start()
    return (c1, c2)


def gains_of(small_t, width, qkv):
    n = width // 128
    return (
        column(small_t, 0, n),
        column(small_t, n, n),
        column(small_t, 2 * n, qkv // 128),
    )


def padded_t(v):
    n = v.shape[0]
    return jnp.concatenate([v, jnp.zeros((128 - n, 128), v.dtype)], axis=0).T


def attention_forward_kernel(
    dims, nk, layer, plan, carry, h_ref, small_ref, meta_ref, docs_ref, cos_ref, sin_ref, qo_all,
    *refs
):
    n = plan.count
    if carry:
        block_ref, refs = (refs[0], refs[1:])
    ins, refs = (refs[:n], refs[n:])
    normed_ref, q_ref, kv_ref, lse_ref, mixed_ref, res_ref, n2_ref = refs[:7]
    outs, refs = (refs[7 : 7 + n], refs[7 + n :])
    if carry:
        block_all, refs = (refs[0], refs[1:])
    w, wo, mask, joined, ssem, rsem, qsem = refs[:7]
    refs = refs[7:]
    pc = Place(dims)
    width, rows = h_ref.shape
    loads = load_qo(qo_all, w, wo, qsem)
    greet(pc, "mates" if carry else None, True)
    riders, refs = plan.board(pc, ins, outs, refs)
    if carry == "lanes":
        own = block_ref
        slot = lambda q: block_all.at[:, lanes(q, rows)]
    elif carry == "columns":
        own = block_ref.at[:, 1]
        slot = lambda q: columns_of(block_all, q, pc.nf, block_ref.shape[3])
    gather = None
    if carry:
        gather = PlaneGather(pc, slot, *refs)
        fill = pltpu.make_async_copy(own, slot(pc.me), qsem.at[2])
        fill.start()
        fill.wait()
        gather.start()
    g1, g2, bias = gains_of(padded_t(small_ref[layer]), width, w.shape[1])
    hidden = h_ref[...].astype(BF).astype(F32)
    normed = (hidden * rms(hidden) * g1).astype(BF)
    normed_ref[...] = normed
    fill_masks(pc, mask, padded_t(meta_ref[...]), docs_ref[...])
    loads[0].wait()
    joined[...] = tn(w[...], normed) + bias
    cos_part = cos_ref[...]
    sin_part = sin_ref[...]
    half = HD // 2

    def turned(row):
        u1 = joined[pl.ds(row, half), :]
        u2 = joined[pl.ds(row + half, half), :]
        return (u1 * cos_part - u2 * sin_part, u2 * cos_part + u1 * sin_part)

    for g in range(KVH):
        r1, r2 = turned((H + g) * HD)
        kv_ref[0, g, :half, :] = r1.astype(BF)
        kv_ref[0, g, half:, :] = r2.astype(BF)
        v0 = (H + KVH + g) * HD
        kv_ref[0, KVH + g] = joined[v0 : v0 + HD, :].astype(BF)
    sends = [
        remote(kv_ref.at[0], kv_ref.at[j], ssem.at[j - 1], rsem.at[j - 1], pc.along(j))
        for j in range(1, nk)
    ]
    for c in sends:
        c.start()
    scale = HD**-0.5
    for head in range(H):
        r1, r2 = turned(head * HD)
        q_ref[head, :half, :] = (r1 * scale).astype(BF)
        q_ref[head, half:, :] = (r2 * scale).astype(BF)
    for c in sends:
        c.wait()
    each(riders, "start")
    for g in range(KVH):
        keys = [kv_ref[j, g].T for j in range(nk)]
        values = [kv_ref[j, KVH + g] for j in range(nk)]

        def one_head(i, carried):
            head = g * GROUP + i
            q = q_ref[head]
            s = [nn(keys[j], q) + mask[j] for j in range(nk)]
            top = s[0].max(axis=0, keepdims=True)
            for j in range(1, nk):
                top = jnp.maximum(top, s[j].max(axis=0, keepdims=True))
            e = [jnp.exp(x - top) for x in s]
            total = e[0].sum(axis=0, keepdims=True)
            for j in range(1, nk):
                total = total + e[j].sum(axis=0, keepdims=True)
            out = nn(values[0], e[0].astype(BF))
            for j in range(1, nk):
                out = out + nn(values[j], e[j].astype(BF))
            lse_ref[head] = top + jnp.log(total)
            mixed_ref[head] = (out / total).astype(BF)
            return carried

        lax.fori_loop(0, GROUP, one_head, 0)
        each(riders, "service")
        if carry and g == 0:
            for step in range(1, min(6, pc.count)):
                gather.before(step)
    mixed = mixed_ref[...].reshape(H * HD, rows)
    loads[1].wait()
    residual = hidden + tn(wo[...], mixed)
    res_ref[...] = residual
    n2_ref[...] = (residual * rms(residual) * g2).astype(BF)
    if carry:
        for step in range(min(6, pc.count), pc.count):
            gather.before(step)
        gather.finish()
    each(riders, "finish")


def attention_forward(dims, nk, cid, layer, hidden, small, meta, docs, cos_part, sin_part, qo_all,
                      plan, carry, block):
    width, rows = hidden.shape
    ns, nb, nf = dims
    count = ns * nf
    qkv = qo_all.shape[1] - width
    sds = jax.ShapeDtypeStruct
    outs = [
        sds((width, rows), BF),
        sds((H, HD, rows), BF),
        sds((nk, 2 * KVH, HD, rows), BF),
        sds((H, 1, rows), F32),
        sds((H, HD, rows), BF),
        sds((width, rows), F32),
        sds((width, rows), BF),
    ] + plan.shapes
    dma = pltpu.SemaphoreType.DMA
    if carry == "lanes":
        outs.append(sds((width, count * rows), BF))
    else:
        outs.append(sds((nb, nf, block.shape[2], ns * block.shape[3]), BF))
    out = call(
        functools.partial(attention_forward_kernel, dims, nk, layer, plan, carry),
        "attention_forward",
        cid,
        tuple(outs),
        [VM] * 7 + plan.places + [AN],
        [VM] * 6 + [AN, AN] + plan.places,
        [
            pltpu.VMEM((width, qkv), BF),
            pltpu.VMEM((width, width), BF),
            pltpu.VMEM((nk, rows, rows), F32),
            pltpu.VMEM((qkv, rows), F32),
            dma((nk - 1,)),
            dma((nk - 1,)),
            dma((3,)),
        ]
        + plan.scratch
        + [dma((count - 1,))] * 2,
        (hidden, small, meta, docs, cos_part, sin_part, qo_all, block, *plan.arrays),
    )
    return (out[:7], out[7:])


def attention_backward_kernel(
    dims, nk, layer, plan, carry, g_ref, small_ref, meta_ref, docs_ref, cos_ref, sin_ref,
    h_ref, normed_ref, q_ref, kv_ref, lse_ref, mixed_ref, qo_all, *refs
):
    n = plan.count
    parts_ref, more_ref, refs = (refs[0], refs[1], refs[2:])
    ins, refs = (refs[:n], refs[n:])
    gh_ref, dqo_ref, dsmall_ref = refs[:3]
    outs, refs = (refs[3 : 3 + n], refs[3 + n :])
    out_ref, refs = (refs[0], refs[1:])
    if carry == "columns":
        rows_ref, refs = (refs[0], refs[1:])
    w, wo, mask, dmix, dkv, out_kv, in_kv, gj, ssem, rsem, qsem = refs[:11]
    refs = refs[11:]
    pc = Place(dims)
    width, rows = h_ref.shape
    qkv = w.shape[1]
    loads = load_qo(qo_all, w, wo, qsem)
    greet(pc, "all" if carry == "columns" else "mates", True)
    riders, refs = plan.board(pc, ins, outs, refs)
    if carry == "columns":
        part = lambda q: columns_of(parts_ref, q, pc.nf, out_ref.shape[2])
        hand_out = RowSends(pc, 1, rows_ref, refs[4:])
    else:
        part = lambda q: parts_ref.at[q]
    scatter = ReadyScatter(pc, part, *refs[:4])
    scatter.start()
    each(riders, "start")
    g1 = column(padded_t(small_ref[layer]), 0, width // 128)
    fill_masks(pc, mask, padded_t(meta_ref[...]), docs_ref[...])
    grl = g_ref[...].astype(BF)
    loads[1].wait()
    dmix[...] = nn(wo[...], grl).astype(BF).reshape(dmix.shape)
    dqo_ref[:, qkv:] = nt(mixed_ref[...].reshape(H * HD, rows), grl).astype(BF)
    scatter.diagonal()
    scatter.early()
    if carry == "columns":
        for f in range(pc.nf):
            hand_out.start(f, more_ref.at[f])
    cos_part = cos_ref[...]
    sin_part = sin_ref[...]
    half = HD // 2
    scale = HD**-0.5
    dkv[...] = jnp.zeros_like(dkv)

    def unturned(d1, d2):
        return (d1 * cos_part + d2 * sin_part, d2 * cos_part - d1 * sin_part)

    for g in range(KVH):
        keys_t = [kv_ref[j, g] for j in range(nk)]
        keys = [k.T for k in keys_t]
        values = [kv_ref[j, KVH + g].T for j in range(nk)]

        def one_head(i, carried):
            head = g * GROUP + i
            q = q_ref[head]
            do = dmix[head]
            lse = lse_ref[head]
            p = [jnp.exp(nn(keys[j], q) + mask[j] - lse) for j in range(nk)]
            dp = [nn(values[j], do) for j in range(nk)]
            delta = (p[0] * dp[0]).sum(axis=0, keepdims=True)
            for j in range(1, nk):
                delta = delta + (p[j] * dp[j]).sum(axis=0, keepdims=True)
            dq = jnp.zeros((HD, rows), F32)
            for j in range(nk):
                ds = (p[j] * (dp[j] - delta)).astype(BF)
                dkv[j, g] += nt(q, ds)
                dkv[j, KVH + g] += nt(do, p[j].astype(BF))
                dq = dq + nn(keys_t[j], ds)
            dq = dq * scale
            r1, r2 = unturned(dq[:half], dq[half:])
            gj[pl.ds(pl.multiple_of(head * HD, HD), half), :] = r1.astype(BF)
            gj[pl.ds(pl.multiple_of(head * HD + half, half), half), :] = r2.astype(BF)
            return carried

        lax.fori_loop(0, GROUP, one_head, 0)
        each(riders, "service")
        if g == 0:
            scatter.late()
    for j in range(1, nk):
        out_kv[j - 1] = dkv[j].astype(BF)
    sends = [
        remote(out_kv.at[j - 1], in_kv.at[j - 1], ssem.at[j - 1], rsem.at[j - 1],
               pc.along(pc.nb - j))
        for j in range(1, nk)
    ]
    for c in sends:
        c.start()
    for c in sends:
        c.wait()
    own = dkv[0]
    for j in range(1, nk):
        own = own + in_kv[j - 1].astype(F32)
    for g in range(KVH):
        r1, r2 = unturned(own[g, :half], own[g, half:])
        k0 = (H + g) * HD
        gj[k0 : k0 + half, :] = r1.astype(BF)
        gj[k0 + half : k0 + HD, :] = r2.astype(BF)
        v0 = (H + KVH + g) * HD
        gj[v0 : v0 + HD, :] = own[KVH + g].astype(BF)
    gjv = gj[...]
    n1 = width // 128
    dsmall_ref[n1 : n1 + qkv // 128, :] = rows_of(gjv.astype(F32))
    loads[0].wait()
    dqo_ref[:, :qkv] = nt(normed_ref[...], gjv).astype(BF)
    gn = nn(w[...], gjv)
    hidden = h_ref[...].astype(BF).astype(F32)
    scale_one = rms(hidden)
    unit = hidden * scale_one
    dsmall_ref[:n1, :] = rows_of(gn * unit)
    u = gn * g1
    gh_ref[...] = g_ref[...] + scale_one * (u - unit * jnp.mean(u * unit, axis=0, keepdims=True))

    def store(total):
        if carry == "columns":
            out_ref[...] = total.astype(BF)
        else:
            out_ref[...] = more_ref[...] + total

    scatter.finish(store)
    if carry == "columns":
        hand_out.finish(more_ref.at[0])
    each(riders, "finish")


def attention_backward(dims, nk, cid, layer, g, small, meta, docs, cos_part, sin_part, hidden,
                       normed, q, kv, lse, mixed, qo_all, plan, carry, late):
    width, rows = hidden.shape
    qkv = qo_all.shape[1] - width
    sds = jax.ShapeDtypeStruct
    outs = [
        sds((width, rows), F32),
        sds((width, qkv + width), BF),
        sds(((width + qkv) // 128, 128), F32),
    ] + plan.shapes
    dma = pltpu.SemaphoreType.DMA
    block = (2 * KVH, HD, rows)
    if carry == "columns":
        summed = (dims[1], late[0].shape[2], late[0].shape[3] // dims[0])
        outs += [sds(summed, BF), sds((dims[0] * dims[2],) + late[1].shape[1:], BF)]
        places = [VM, AN]
    else:
        summed = (width, rows)
        outs.append(sds(summed, F32))
        places = [VM]
    out = call(
        functools.partial(attention_backward_kernel, dims, nk, layer, plan, carry),
        "attention_backward",
        cid,
        tuple(outs),
        [VM] * 3 + plan.places + places,
        [VM] * 12 + [AN] + [VM] * len(late) + plan.places,
        [
            pltpu.VMEM((width, qkv), BF),
            pltpu.VMEM((width, width), BF),
            pltpu.VMEM((nk, rows, rows), F32),
            pltpu.VMEM((H, HD, rows), BF),
            pltpu.VMEM((nk,) + block, F32),
            pltpu.VMEM((nk - 1,) + block, BF),
            pltpu.VMEM((nk - 1,) + block, BF),
            pltpu.VMEM((qkv, rows), BF),
            dma((nk - 1,)),
            dma((nk - 1,)),
            dma((2,)),
        ]
        + plan.scratch
        + scatter_scratch(dims, *summed)[2:]
        + (row_scratch(dims) if carry == "columns" else []),
        (g, small, meta, docs, cos_part, sin_part, hidden, normed, q, kv, lse, mixed, qo_all,
         *late, *plan.arrays),
    )
    return (out[:3], out[3:])


def sequence_of(pc):
    if pc.two_level:
        return ((0, 1, 2, 3, 6, 7, 4, 5), 5, 7)
    return (tuple(range(pc.count)), pc.count - 1, pc.count - 1)


def lanes(slot, rows):
    return pl.ds(pl.multiple_of(slot * rows, rows), rows)


def transpose_into(dst, src):
    cols = src.shape[1]
    for c0 in range(0, cols, 128):
        c1 = min(c0 + 128, cols)
        dst[c0:c1, :] = src[:, c0:c1].T


def feed_forward_kernel(dims, plan, x_ref, res_ref, wgu_ref, wd_ref, *refs):
    n = plan.count
    ins, refs = (refs[:n], refs[n:])
    out_ref, x_all, gu_all = refs[:3]
    outs, refs = (refs[3 : 3 + n], refs[3 + n :])
    wgu_t, wd_t, gu, inner, near, away, back, hop, ss, sr, gs, gr = refs[:12]
    pc = Place(dims)
    width, rows = x_ref.shape
    ff = wd_ref.shape[0]
    greet(pc, "mates", n > 0)
    riders, _ = plan.board(pc, ins, outs, refs[12:])
    gather = PlaneGather(pc, lambda q: x_all.at[:, lanes(q, rows)], gs, gr)
    scatter = PlaneScatter(pc, near, away, back, hop, ss, sr)
    x_all[:, lanes(pc.me, rows)] = x_ref[...]
    gather.start()
    each(riders, "start")
    transpose_into(wgu_t, wgu_ref)
    transpose_into(wd_t, wd_ref)
    sequence, diagonal_at, early_at = sequence_of(pc)
    chunk = 32 if ff % 32 == 0 else 16

    def step_body(turn, carry):
        step = pick(turn, sequence)

        for k in range(pc.count):
            @pl.when(step == k)
            def _():
                gather.before(k)

        slot = pick(step, gather.order)
        sl = lanes(slot, rows)
        gu[...] = nn(wgu_t[...], x_all[:, sl])

        def act(i, c):
            r = pl.multiple_of(i * chunk, chunk)
            gate = gu[pl.ds(r, chunk), :]
            up = gu[pl.ds(ff + r, chunk), :]
            gu_all[pl.ds(r, chunk), sl] = gate.astype(BF)
            gu_all[pl.ds(ff + r, chunk), sl] = up.astype(BF)
            inner[pl.ds(r, chunk), :] = (gate * jax.nn.sigmoid(gate) * up).astype(BF)
            return c

        lax.fori_loop(0, ff // chunk, act, 0)
        scatter.put(step, nn(wd_t[...], inner[...]))

        @pl.when(turn == 3)
        def _():
            each(riders, "service")

        @pl.when(turn == diagonal_at)
        def _():
            scatter.diagonal()

        @pl.when(turn == early_at)
        def _():
            scatter.early()

        return carry

    lax.fori_loop(0, pc.count, step_body, 0)
    each(riders, "service")

    def store(total):
        out_ref[...] = res_ref[...] + total

    scatter.result(store)
    gather.finish()
    each(riders, "finish")


def feed_forward(dims, cid, x, residual, wgu, wd, plan):
    width, rows = x.shape
    count = dims[0] * dims[2]
    two_ff, ff = (wgu.shape[1], wd.shape[0])
    sds = jax.ShapeDtypeStruct
    dma = pltpu.SemaphoreType.DMA
    out = call(
        functools.partial(feed_forward_kernel, dims, plan),
        "feed_forward",
        cid,
        (
            sds((width, rows), F32),
            sds((width, count * rows), BF),
            sds((two_ff, count * rows), BF),
            *plan.shapes,
        ),
        [VM] * 3 + plan.places,
        [VM] * 4 + plan.places,
        [
            pltpu.VMEM((two_ff, width), BF),
            pltpu.VMEM((width, ff), BF),
            pltpu.VMEM((two_ff, rows), F32),
            pltpu.VMEM((ff, rows), BF),
        ]
        + scatter_scratch(dims, width, rows)
        + [dma((count - 1,)), dma((count - 1,))]
        + plan.scratch,
        (x, residual, wgu, wd, *plan.arrays),
    )
    return (out[:3], out[3:])


def feed_backward_kernel(
    dims, layer, plan, g_ref, res_ref, x_all, gu_all, wgu_ref, wd_ref, small_ref, *refs
):
    n = plan.count
    ins, refs = (refs[:n], refs[n:])
    gr_ref, dwgu_ref, dwd_ref, dsmall_ref = refs[:4]
    outs, refs = (refs[4 : 4 + n], refs[4 + n :])
    g_all, inner, ggu, gi, near, away, back, hop, ss, sr, gs, gr = refs[:12]
    pc = Place(dims)
    width, rows = g_ref.shape
    ff = wd_ref.shape[0]
    greet(pc, "mates", n > 0)
    riders, _ = plan.board(pc, ins, outs, refs[12:])
    gather = PlaneGather(pc, lambda q: g_all.at[:, lanes(q, rows)], gs, gr)
    scatter = PlaneScatter(pc, near, away, back, hop, ss, sr)
    g_all[:, lanes(pc.me, rows)] = g_ref[...].astype(BF)
    gather.start()
    each(riders, "start")
    sequence, diagonal_at, early_at = sequence_of(pc)
    chunk = 32 if ff % 32 == 0 else 16

    def step_body(turn, carry):
        step = pick(turn, sequence)

        for k in range(pc.count):
            @pl.when(step == k)
            def _():
                gather.before(k)

        slot = pick(step, gather.order)
        sl = lanes(slot, rows)
        gi[...] = nn(wd_ref[...], g_all[:, sl])

        def act(i, c):
            r = pl.multiple_of(i * chunk, chunk)
            gate = gu_all[pl.ds(r, chunk), sl].astype(F32)
            up = gu_all[pl.ds(ff + r, chunk), sl].astype(F32)
            grad = gi[pl.ds(r, chunk), :]
            sig = jax.nn.sigmoid(gate)
            silu = gate * sig
            inner[pl.ds(r, chunk), sl] = (silu * up).astype(BF)
            ggu[pl.ds(r, chunk), sl] = (grad * up * sig * (1.0 + gate * (1.0 - sig))).astype(BF)
            ggu[pl.ds(ff + r, chunk), sl] = (grad * silu).astype(BF)
            return c

        lax.fori_loop(0, ff // chunk, act, 0)
        scatter.put(step, nn(wgu_ref[...], ggu[:, sl]))

        @pl.when(turn == 3)
        def _():
            each(riders, "service")

        @pl.when(turn == diagonal_at)
        def _():
            scatter.diagonal()

        @pl.when(turn == early_at)
        def _():
            scatter.early()

        return carry

    lax.fori_loop(0, pc.count, step_body, 0)
    each(riders, "service")
    dwd_ref[...] = nt(inner[...], g_all[...]).astype(BF)
    scatter.late()
    part = width // 2
    for r in range(2):
        dwgu_ref[r * part : (r + 1) * part, :] = nt(
            x_all[r * part : (r + 1) * part, :], ggu[...]
        ).astype(BF)

    def store(total):
        residual = res_ref[...]
        scale_two = rms(residual)
        unit = residual * scale_two
        n1 = width // 128
        dsmall_ref[...] = rows_of(total * unit)
        u = total * column(padded_t(small_ref[layer]), n1, n1)
        gr_ref[...] = g_ref[...].astype(BF).astype(F32) + scale_two * (
            u - unit * jnp.mean(u * unit, axis=0, keepdims=True)
        )

    scatter.finish(store)
    gather.finish()
    each(riders, "finish")


def feed_backward(dims, cid, layer, g, residual, x_all, gu_all, wgu, wd, small, plan):
    width, rows = g.shape
    count = dims[0] * dims[2]
    two_ff, ff = (wgu.shape[1], wd.shape[0])
    sds = jax.ShapeDtypeStruct
    dma = pltpu.SemaphoreType.DMA
    out = call(
        functools.partial(feed_backward_kernel, dims, layer, plan),
        "feed_backward",
        cid,
        (
            sds((width, rows), F32),
            sds(wgu.shape, BF),
            sds(wd.shape, BF),
            sds((width // 128, 128), F32),
            *plan.shapes,
        ),
        [VM] * 4 + plan.places,
        [VM] * 7 + plan.places,
        [
            pltpu.VMEM((width, count * rows), BF),
            pltpu.VMEM((ff, count * rows), BF),
            pltpu.VMEM((two_ff, count * rows), BF),
            pltpu.VMEM((ff, rows), F32),
        ]
        + scatter_scratch(dims, width, rows)
        + [dma((count - 1,)), dma((count - 1,))]
        + plan.scratch,
        (g, residual, x_all, gu_all, wgu, wd, small, *plan.arrays),
    )
    return (out[:4], out[4:])


def feed_both_kernel(
    dims, layer, x_ref, res_ref, g_ref, g_all, wgu_ref, wd_ref, small_ref,
    gr_ref, dwgu_ref, dwd_ref, dsmall_ref, parts_ref,
    x_all, inner, ggu, wgu_t, wd_t, gu, gi, near, away, back, hop, ss, sr, gs, gr,
):
    pc = Place(dims)
    width, rows = g_ref.shape
    ff = wd_ref.shape[0]
    greet(pc, "mates", False)
    gather = PlaneGather(pc, lambda q: x_all.at[:, lanes(q, rows)], gs, gr)
    scatter = PlaneScatter(pc, near, away, back, hop, ss, sr)
    x_all[:, lanes(pc.me, rows)] = x_ref[...]
    gather.start()
    transpose_into(wgu_t, wgu_ref)
    transpose_into(wd_t, wd_ref)
    sequence, diagonal_at, early_at = sequence_of(pc)
    chunk = 32 if ff % 32 == 0 else 16

    def step_body(turn, carry):
        step = pick(turn, sequence)

        for k in range(pc.count):
            @pl.when(step == k)
            def _():
                gather.before(k)

        slot = pick(step, gather.order)
        sl = lanes(slot, rows)
        gu[...] = nn(wgu_t[...], x_all[:, sl])
        gi[...] = nn(wd_ref[...], g_all[:, sl])

        def act(i, c):
            r = pl.multiple_of(i * chunk, chunk)
            gate = gu[pl.ds(r, chunk), :]
            up = gu[pl.ds(ff + r, chunk), :]
            grad = gi[pl.ds(r, chunk), :]
            sig = jax.nn.sigmoid(gate)
            silu = gate * sig
            inner[pl.ds(r, chunk), sl] = (silu * up).astype(BF)
            ggu[pl.ds(r, chunk), sl] = (grad * up * sig * (1.0 + gate * (1.0 - sig))).astype(BF)
            ggu[pl.ds(ff + r, chunk), sl] = (grad * silu).astype(BF)
            return c

        lax.fori_loop(0, ff // chunk, act, 0)
        scatter.put(step, nn(wgu_ref[...], ggu[:, sl]))

        @pl.when(turn == diagonal_at)
        def _():
            scatter.diagonal()

        @pl.when(turn == early_at)
        def _():
            scatter.early()

        parts_ref[slot] = nn(wd_t[...], inner[:, sl]).astype(BF)
        return carry

    lax.fori_loop(0, pc.count, step_body, 0)
    dwd_ref[...] = nt(inner[...], g_all[...]).astype(BF)
    scatter.late()
    part = width // 2
    for r in range(2):
        dwgu_ref[r * part : (r + 1) * part, :] = nt(
            x_all[r * part : (r + 1) * part, :], ggu[...]
        ).astype(BF)

    def store(total):
        residual = res_ref[...]
        scale_two = rms(residual)
        unit = residual * scale_two
        n1 = width // 128
        dsmall_ref[...] = rows_of(total * unit)
        u = total * column(padded_t(small_ref[layer]), n1, n1)
        gr_ref[...] = g_ref[...].astype(BF).astype(F32) + scale_two * (
            u - unit * jnp.mean(u * unit, axis=0, keepdims=True)
        )

    scatter.finish(store)
    gather.finish()


def feed_both(dims, cid, layer, x, residual, g, g_all, wgu, wd, small):
    width, rows = g.shape
    count = dims[0] * dims[2]
    two_ff, ff = (wgu.shape[1], wd.shape[0])
    sds = jax.ShapeDtypeStruct
    dma = pltpu.SemaphoreType.DMA
    return call(
        functools.partial(feed_both_kernel, dims, layer),
        "feed_both",
        cid,
        (
            sds((width, rows), F32),
            sds(wgu.shape, BF),
            sds(wd.shape, BF),
            sds((width // 128, 128), F32),
            sds((count, width, rows), BF),
        ),
        [VM] * 5,
        [VM] * 7,
        [
            pltpu.VMEM((width, count * rows), BF),
            pltpu.VMEM((ff, count * rows), BF),
            pltpu.VMEM((two_ff, count * rows), BF),
            pltpu.VMEM((two_ff, width), BF),
            pltpu.VMEM((width, ff), BF),
            pltpu.VMEM((two_ff, rows), F32),
            pltpu.VMEM((ff, rows), F32),
        ]
        + scatter_scratch(dims, width, rows)
        + [dma((count - 1,)), dma((count - 1,))],
        (x, residual, g, g_all, wgu, wd, small),
    )


def reduce_kernel(
    dims, cut, qo, terms, sa0, sa1, sb0, sb1, wd1, wd0, gu0a, gu0,
    qo_out, small_out, gu_got, wd_got,
    gsum, small, sm_in, sm_mid, sm_line, z_out, mine, give,
    lsem, ws, wr, ls, lr, zs, zr, *rest
):
    pc = Place(dims)
    ns, nb, nf = dims
    greet(pc, "all", True)
    scatter = ReadyScatter(
        pc, lambda q: columns_of(qo, q, nf, z_out.shape[2]), *rest[15:19]
    )
    scatter.start()

    def keep(value):
        gsum[...] = value.astype(BF)

    def keep_of(l):
        def store(value):
            mine[l] = value

        return store

    line = LineReduce(pc, lambda t: gu0[t, cut:nf], keep, rest[0:4])
    ends = [
        LineReduce(pc, lambda t: z_out[t], keep_of(0), rest[4:8]),
        LineReduce(pc, lambda t: terms[t], keep_of(1), rest[8:12]),
    ]
    line.start()
    ends[1].start()
    n1 = sb0.shape[0]
    per = small.shape[0] // ns
    nr = sa0.shape[0] + n1
    small[...] = jnp.zeros_like(small)
    for l, (a, g) in enumerate(((sa0, sb0), (sa1, sb1))):
        small[l * per : l * per + n1] = a[0:n1]
        small[l * per + n1 : l * per + 2 * n1] = g[...]
        small[l * per + 2 * n1 : l * per + nr] = a[n1 : a.shape[0]]
    smalls = [
        remote(small, sm_in.at[e - 1], ls.at[e - 1], lr.at[e - 1], pc.plane(e))
        for e in range(1, pc.count)
    ]
    for c in smalls:
        c.start()
    scatter.diagonal()
    scatter.early()
    hand_out = RowSends(pc, 0, gu_got, rest[12:15])
    for f in range(cut):
        hand_out.start(f, gu0a.at[f])
    for l, ref in ((0, wd0), (1, wd1)):
        @pl.when(pc.s == l)
        def _():
            pltpu.make_async_copy(ref, wd_got.at[l], lsem.at[0]).start()

        @pl.when(pc.s != l)
        def _():
            remote(ref, wd_got.at[pc.s], ws.at[0], wr.at[0], (l, pc.b, pc.f)).start()

    ends[1].service()
    scatter.late()
    line.service()
    total = small[...]
    for e, c in enumerate(smalls):
        c.wait()
        total = total + sm_in[e]
    sm_mid[...] = total
    lines = [
        remote(sm_mid, sm_line.at[d - 1], zs.at[d - 1], zr.at[d - 1], pc.along(d))
        for d in range(1, nb)
    ]
    for c in lines:
        c.start()

    def store(value):
        z_out[...] = value.astype(BF)

    scatter.finish(store)
    ends[0].start()
    ends[1].finish()
    line.service()
    ends[0].finish()
    mate = (ns - 1 - pc.s, pc.b, pc.f)
    swap = remote(give.at[0], give.at[1], ws.at[1], wr.at[1], mate)
    give[0] = mine[ns - 1 - pc.s].astype(BF)
    swap.start()
    qo_out[pc.s] = mine[pc.s]
    line.finish()
    for f in range(cut, nf):
        hand_out.start(f, gsum.at[f - cut])
    total = sm_mid[...]
    for d, c in enumerate(lines):
        c.wait()
        total = total + sm_line[d]
    small_out[...] = total
    swap.wait()
    qo_out[ns - 1 - pc.s] = give[1].astype(F32)
    hand_out.finish(gsum.at[0])
    pltpu.make_async_copy(wd0, wd_got.at[pc.s], lsem.at[0]).wait()
    remote(wd0, wd_got.at[pc.s], ws.at[0], wr.at[0], mate).wait()


def reduce_gradients(dims, cid, cut, qo, terms, smalls, wd1, wd0, gu0a, gu0):
    ns, nb, nf = dims
    count = ns * nf
    dr, wide = terms.shape[1:]
    two_ff = gu0.shape[3]
    half, width = wd0.shape
    rows = smalls[0].shape[0] + smalls[2].shape[0]
    small = (ns * (-(-rows // 8) * 8), 128)
    sds = jax.ShapeDtypeStruct
    dma = pltpu.SemaphoreType.DMA
    return call(
        functools.partial(reduce_kernel, dims, cut),
        "reduce_gradients",
        cid,
        (
            sds((ns, dr, wide), F32),
            sds(small, F32),
            sds((count, dr, two_ff), BF),
            sds((ns, half, width), BF),
        ),
        [VM] * 4,
        [VM] * 10,
        [
            pltpu.VMEM((nf - cut, dr, two_ff), BF),
            pltpu.VMEM(small, F32),
            pltpu.VMEM((count - 1,) + small, F32),
            pltpu.VMEM(small, F32),
            pltpu.VMEM((nb - 1,) + small, F32),
            pltpu.VMEM((nb, dr, wide), BF),
            pltpu.VMEM((ns, dr, wide), F32),
            pltpu.VMEM((2, dr, wide), BF),
            dma((1,)),
            dma((2,)),
            dma((2,)),
            dma((count - 1,)),
            dma((count - 1,)),
            dma((nb - 1,)),
            dma((nb - 1,)),
        ]
        + reduce_scratch(dims, nf - cut, dr, two_ff)
        + reduce_scratch(dims, dr, wide) * 2
        + row_scratch(dims)
        + scatter_scratch(dims, nb, dr, wide)[2:],
        (qo, terms, *smalls, wd1, wd0, gu0a, gu0),
    )


def lay_out_kernel(
    dims, gu0, gu1, wd, qo, small, out0, out1, gh0, gh1, take_out, take_grad,
    block_out, input_grad, g1, wqkv, bqkv, wout, g2, wgu, wdn
):
    ns, nb, nf = dims
    half = wd.shape[1]
    s = lax.axis_index("section")
    qkv = wqkv.shape[2]
    width = wout.shape[2]
    full = jnp.concatenate([qo[y] for y in range(ns)], axis=1)
    wqkv[0] = full[:, :qkv]
    wout[0] = full[:, qkv:]
    for y in range(ns):
        wdn[0, y * half : (y + 1) * half, :] = wd[y].astype(F32)
    for l, gu in enumerate((gu0, gu1)):
        @pl.when(s == l)
        def _():
            for y in range(ns):
                for f in range(nf):
                    got = gu[y * nf + f].astype(F32)
                    for part in range(2):
                        for b in range(nb):
                            c0 = column_start(dims, part, b, f, y, half)
                            k0 = (part * nb + b) * half
                            wgu[0, :, c0 : c0 + half] = got[:, k0 : k0 + half]
    n1 = width // 128
    per = small.shape[0] // ns
    rows = small[pl.ds(pl.multiple_of(s * per, 8), per), :]
    for k in range(n1):
        g1[0:1, k * 128 : (k + 1) * 128] = rows[k : k + 1]
        g2[0:1, k * 128 : (k + 1) * 128] = rows[n1 + k : n1 + k + 1]
    for k in range(qkv // 128):
        bqkv[0:1, k * 128 : (k + 1) * 128] = rows[2 * n1 + k : 2 * n1 + k + 1]
    for out, pair, take in (
        (block_out, (out0, out1), take_out),
        (input_grad, (gh0, gh1), take_grad),
    ):
        for l in range(ns):
            @pl.when(s == l)
            def _():
                out[0, l] = pair[l][...].T
                out[0, 1 - l] = take[...].T.astype(F32)


def lay_out(dims, qkv, args):
    ns, nb, nf = dims
    gu, wd, qo = (args[0], args[2], args[3])
    width, rows = args[5].shape
    dr = qo.shape[1]
    sds = jax.ShapeDtypeStruct
    tokens = sds((1, ns, rows, width), F32)
    return pl.pallas_call(
        functools.partial(lay_out_kernel, dims),
        name="lay_out",
        out_shape=(
            tokens,
            tokens,
            sds((1, width), F32),
            sds((1, dr, qkv), F32),
            sds((1, qkv), F32),
            sds((1, dr, width), F32),
            sds((1, width), F32),
            sds((1, dr, gu.shape[0] * gu.shape[2]), F32),
            sds((1, ns * wd.shape[1], width), F32),
        ),
        in_specs=[VM] * len(args),
        out_specs=[VM] * 9,
        compiler_params=pltpu.CompilerParams(vmem_limit_bytes=VMEM_LIMIT),
    )(*args)


def shards(
    dims,
    tokens_in,
    positions,
    doc_ids,
    out_grad,
    norm1_gain,
    w_qkv,
    b_qkv,
    w_out,
    norm2_gain,
    w_gate_up,
    w_down,
):
    ns, nb, nf = dims
    seqs, rows, width = tokens_in.shape
    s = lax.axis_index("section")
    b = lax.axis_index("blk")
    dr = w_qkv.shape[1]
    qkv = w_qkv.shape[2]
    fr = w_down.shape[1]
    half = fr // ns
    ff = nb * half
    nk = min(nb, 1 + (LONGEST - 1 + rows - 1) // rows)

    tokens = lax.dynamic_index_in_dim(tokens_in, s, 0, keepdims=False)
    cot = lax.dynamic_index_in_dim(out_grad, s, 0, keepdims=False)
    pos = lax.dynamic_index_in_dim(positions, s, 0, keepdims=False)
    docs = lax.dynamic_index_in_dim(doc_ids, s, 0, keepdims=False).astype(F32)
    freq = jnp.exp(jnp.arange(HD // 2, dtype=F32) * (-2.0 / HD) * math.log(1000000.0))
    phase = freq[:, None] * pos.astype(F32)[None, :]
    cos_part, sin_part = (jnp.cos(phase), jnp.sin(phase))
    docs = docs.reshape(nb, rows)
    picked = (b - jnp.arange(nk) + nb) % nb
    meta = jnp.take(docs, picked, axis=0).reshape(nk * rows // 128, 128)
    query_docs = lax.dynamic_slice_in_dim(docs, b, 1)
    hidden = tokens.T.astype(F32)
    g = cot.T.astype(F32)

    wd = w_down[0].reshape(ns, half, width)
    small = jnp.concatenate([norm1_gain[0], norm2_gain[0], b_qkv[0]])
    total = -(-small.shape[0] // 1024) * 1024
    small = jnp.pad(small, (0, total - small.shape[0])).reshape(-1, 128)
    gup, wdp, gu_first, qo_first, qz, small_all = gather_weights(
        dims, w_gate_up, w_qkv, w_out, wd, small
    )
    cols = qkv + width
    wide = (width, 2 * ff)

    def ride(*pairs):
        return Riders(dims, tuple(a for a, _ in pairs), tuple(v for _, v in pairs))

    common = (small_all, meta, query_docs, cos_part, sin_part)
    qo0 = qo_first.reshape(width, cols)
    a0, (wd0, qo1) = attention_forward(
        dims, nk, 1, 0, hidden, *common, qo0, ride((("gather", 0), wdp)), "columns", qz
    )
    qo1 = qo1.reshape(width, cols)
    wd0 = wd0.reshape(ff, width)
    wgu0 = gu_first.reshape(wide)
    f0, (gu1,) = feed_forward(dims, 3, a0[6], a0[5], wgu0, wd0, ride((("gather", 1), gup)))
    wgu1 = gu1.reshape(wide)
    a1, (wd1, g_all) = attention_forward(
        dims, nk, 2, 1, f0[0], *common, qo1, ride((("gather", 1), wdp)), "lanes", cot.T
    )
    wd1 = wd1.reshape(ff, width)

    line_gu = (nb, nf, dr, 2 * ff)
    line_wd = (nb, half, width)
    line_qo = (nb, nf, dr, cols)
    everything = (0, half)
    cut = nf // 2
    b1 = feed_both(dims, 4, 1, a1[6], a1[5], g, g_all, wgu1, wd1, small_all)
    ab1, (dwd1, out1) = attention_backward(
        dims, nk, 7, 1, b1[0], *common, f0[0], *a1[:5], qo1,
        ride((("reduce", everything), b1[2].reshape(line_wd))), "sum", (b1[4], a1[5]),
    )
    b0, (dgu1,) = feed_backward(
        dims, 6, 0, ab1[0], a0[5], f0[1], f0[2], wgu0, wd0, small_all,
        ride((("reduce", (0, nf)), b1[1].reshape(line_gu))),
    )
    dgu0 = b0[1].reshape(line_gu)
    ab0, (dwd0, dgu0a, terms, gu_got1) = attention_backward(
        dims, nk, 8, 0, b0[0], *common, hidden, *a0[:5], qo0,
        ride((("reduce", everything), b0[2].reshape(line_wd)), (("reduce", (0, cut)), dgu0)),
        "columns", (ab1[1].reshape(line_qo), dgu1),
    )

    def swapped(values):
        give = jnp.where(s == 0, values[1], values[0]).astype(BF)
        return lax.ppermute(give, "section", [(0, 1), (1, 0)])

    take_out = swapped((f0[0], out1))
    take_grad = swapped((ab0[0], ab1[0]))
    grad_qo, small_sum, gu_got0, wd_got = reduce_gradients(
        dims, 9, cut, ab0[1].reshape(line_qo), terms,
        (ab0[2], ab1[2], b0[3], b1[3]), dwd1, dwd0, dgu0a, dgu0,
    )
    return lay_out(
        dims,
        qkv,
        (gu_got0, gu_got1, wd_got, grad_qo, small_sum, f0[0], out1, ab0[0], ab1[0], take_out,
         take_grad),
    )


def solution(mesh):
    dims = (mesh.shape["section"], mesh.shape["blk"], mesh.shape["fsdp"])
    return jax.shard_map(
        functools.partial(shards, dims),
        mesh=mesh,
        in_specs=(
            P("fsdp", "blk", None),
            P("fsdp", "blk"),
            P("fsdp", None),
            P("fsdp", "blk", None),
            P("section", None),
            P("section", ("blk", "fsdp"), None),
            P("section", None),
            P("section", ("blk", "fsdp"), None),
            P("section", None),
            P("section", ("blk", "fsdp"), None),
            P("section", ("blk", "fsdp"), None),
        ),
        out_specs=(
            P("section", "fsdp", "blk", None),
            P("section", "fsdp", "blk", None),
            P("section", None),
            P("section", ("blk", "fsdp"), None),
            P("section", None),
            P("section", ("blk", "fsdp"), None),
            P("section", None),
            P("section", ("blk", "fsdp"), None),
            P("section", ("blk", "fsdp"), None),
        ),
        check_vma=False,
    )
```

```python
import functools
import math

import jax
import jax.numpy as jnp
from jax import lax
from jax.experimental import pallas as pl
from jax.experimental.pallas import tpu as pltpu
from jax.sharding import PartitionSpec as P

H = 14
KVH = 2
HD = 64
GROUP = H // KVH
LONGEST = 512
NEG = -1e30
BF = jnp.bfloat16
F32 = jnp.float32
MESH = pl.DeviceIdType.MESH
VMEM_LIMIT = 60 * 2**20
VM = pl.BlockSpec(memory_space=pltpu.VMEM)
AN = pl.BlockSpec(memory_space=pl.ANY)


def nn(a, b):
    return lax.dot_general(a, b, (((1,), (0,)), ((), ())), preferred_element_type=F32)


def nt(a, b):
    return lax.dot_general(a, b, (((1,), (1,)), ((), ())), preferred_element_type=F32)


def tn(a, b):
    return lax.dot_general(a, b, (((0,), (0,)), ((), ())), preferred_element_type=F32)


def other(f):
    return f + 1 - 2 * (f % 2)


class Place:
    def __init__(self, dims):
        self.ns, self.nb, self.nf = dims
        self.count = self.ns * self.nf
        self.s = lax.axis_index("section")
        self.b = lax.axis_index("blk")
        self.f = lax.axis_index("fsdp")
        self.me = self.s * self.nf + self.f
        self.two_level = self.ns == 2 and self.nf == 4

    def plane(self, e):
        q = (self.me + e) % self.count
        return (q // self.nf, self.b, q % self.nf)

    def slot_from(self, e):
        return (self.me + self.count - e) % self.count

    def along(self, d):
        return (self.s, (self.b + d) % self.nb, self.f)

    def mates(self):
        s, b, f = (self.s, self.b, self.f)
        xf = (f + 2) % 4
        return ((s, b, other(f)), (s, b, xf), (1 - s, b, f))

    def slots(self):
        s, f = (self.s, self.f)
        xf = (f + 2) % 4
        t = 1 - s
        return (
            s * 4 + f,
            s * 4 + other(f),
            s * 4 + xf,
            t * 4 + f,
            s * 4 + other(xf),
            t * 4 + other(f),
            t * 4 + xf,
            t * 4 + other(xf),
        )


def pick(i, values):
    total = 0
    for k, v in enumerate(values):
        total = total + jnp.where(i == k, v, 0)
    return total


def greet(place, plane, along):
    barrier = pltpu.get_barrier_semaphore()
    count = 0
    if plane:
        if place.two_level and plane == "mates":
            targets = list(place.mates())
        else:
            targets = [place.plane(e) for e in range(1, place.count)]
        for t in targets:
            pl.semaphore_signal(barrier, 1, device_id=t, device_id_type=MESH)
        count += len(targets)
    if along:
        for d in range(1, place.nb):
            pl.semaphore_signal(barrier, 1, device_id=place.along(d), device_id_type=MESH)
        count += place.nb - 1
    pl.semaphore_wait(barrier, count)


def remote(src, dst, ssem, rsem, device):
    return pltpu.make_async_remote_copy(
        src_ref=src,
        dst_ref=dst,
        send_sem=ssem,
        recv_sem=rsem,
        device_id=device,
        device_id_type=MESH,
    )


def cut_in(parts, view, c):
    n = view.shape[0] // parts
    return view.at[pl.ds(c * n, n)]


def gather_sems(dims):
    n = 2 * (dims[0] * dims[2] - 1)
    return [pltpu.SemaphoreType.DMA((n,)), pltpu.SemaphoreType.DMA((n,))]


class PlaneGather:
    def __init__(self, place, slot, ssem, rsem):
        self.place, self.slot, self.ssem, self.rsem = (place, slot, ssem, rsem)
        self.parts = 2 if place.two_level else 1
        if place.two_level:
            self.order = place.slots()
        else:
            self.order = tuple(place.slot_from(e) for e in range(place.count))

    def copy(self, k, c, q, device):
        v = cut_in(self.parts, self.slot(q), c)
        i = k * self.parts + c
        return remote(v, v, self.ssem.at[i], self.rsem.at[i], device)

    def start(self):
        pc = self.place
        if pc.two_level:
            core, xm, ym = pc.mates()
            for c in range(2):
                self.copy(1, c, self.order[0], xm).start()
                self.copy(2, c, self.order[0], ym).start()
            for c in range(2):
                self.copy(0, c, self.order[0], core).start()
        else:
            for e in range(1, pc.count):
                self.copy(e - 1, 0, self.order[0], pc.plane(e)).start()

    def came(self, k, c):
        self.copy(k, c, self.order[k + 1], self.place.plane(1)).wait_recv()

    def before(self, step):
        if step == 0:
            return
        pc = self.place
        if not pc.two_level:
            self.came(step - 1, 0)
            return
        core, xm, ym = pc.mates()
        h = pc.f % 2
        if step == 2:
            which = h * self.order[3] + (1 - h) * self.order[2]
            far = (
                h * xm[0] + (1 - h) * ym[0],
                pc.b,
                h * xm[2] + (1 - h) * ym[2],
            )
            for c in range(2):
                self.came(1, c)
                self.came(2, c)
                self.copy(5, c, which, far).start()
                self.copy(3, c, self.order[2], core).start()
                self.copy(4, c, self.order[3], core).start()
        elif step == 3:
            return
        elif step == 6:
            for c in range(2):
                self.came(5, c)
                self.copy(6, c, self.order[6], core).start()
        else:
            for c in range(2):
                self.came(step - 1, c)

    def finish(self):
        n = self.place.count - 1
        for k in range(n):
            for c in range(self.parts):
                self.copy(k, c, self.order[0], self.place.plane(1)).wait_send()


class PlaneScatter:
    def __init__(self, place, near, away, back, hop, ssem, rsem):
        self.place = place
        self.near, self.away, self.back, self.hop = (near, away, back, hop)
        self.ssem, self.rsem = (ssem, rsem)

    def put(self, step, value):
        pc = self.place
        if not pc.two_level:
            @pl.when(step == 0)
            def _():
                self.near[0] = value

            @pl.when(step > 0)
            def _():
                e = pc.count - step
                self.away[e - 1] = value.astype(BF)
                q = (pc.me + e) % pc.count
                remote(
                    self.away.at[e - 1],
                    self.back.at[e - 1],
                    self.ssem.at[e - 1],
                    self.rsem.at[e - 1],
                    (q // pc.nf, pc.b, q % pc.nf),
                ).start()
            return
        core, xm, ym = pc.mates()
        here = (step == 0) | (step == 2) | (step == 3) | (step == 6)
        q = pick(step, (0, 0, 1, 2, 1, 2, 3, 3))

        @pl.when(here)
        def _():
            self.near[q] = value

        @pl.when(jnp.logical_not(here))
        def _():
            self.away[q] = value.astype(BF)
            self.core_copy(q).start()

    def core_copy(self, q):
        core = self.place.mates()[0]
        return remote(self.away.at[q], self.back.at[q], self.ssem.at[q], self.rsem.at[q], core)

    def far_copy(self, e):
        return remote(self.away.at[e - 1], self.back.at[e - 1], self.ssem.at[e - 1],
                      self.rsem.at[e - 1], self.place.plane(e))

    def hop_copy(self, k, c, device):
        i = 4 + 2 * k + c
        return remote(
            cut_in(2, self.hop.at[k], c),
            cut_in(2, self.hop.at[k + 3], c),
            self.ssem.at[i],
            self.rsem.at[i],
            device,
        )

    def rows(self, c):
        n = self.hop.shape[1] // 2
        return slice(c * n, (c + 1) * n)

    def targets(self):
        pc = self.place
        core, xm, ym = pc.mates()
        c = pc.f % 2
        first = (c * xm[0] + (1 - c) * ym[0], pc.b, c * xm[2] + (1 - c) * ym[2])
        second = (c * ym[0] + (1 - c) * xm[0], pc.b, c * ym[2] + (1 - c) * xm[2])
        return (first, second)

    def early(self):
        pc = self.place
        if not pc.two_level:
            return
        c = pc.f % 2
        first, second = self.targets()
        self.core_copy(1).wait_recv()
        self.core_copy(2).wait_recv()
        q = c * 1 + (1 - c) * 2
        for k in range(2):
            r = self.rows(k)
            self.hop[0, r] = (self.mine(q, r) + self.back[q, r].astype(F32)).astype(BF)
            self.hop_copy(0, k, first).start()

    def diagonal(self):
        pc = self.place
        if not pc.two_level:
            return
        first, second = self.targets()
        self.core_copy(3).wait_recv()
        for k in range(2):
            r = self.rows(k)
            self.hop[1, r] = (self.mine(3, r) + self.back[3, r].astype(F32)).astype(BF)
            self.hop_copy(1, k, first).start()

    def mine(self, q, r=slice(None)):
        return self.near[q, r]

    def result(self, store):
        self.late()
        self.finish(store)

    def late(self):
        pc = self.place
        if not pc.two_level:
            return
        c = pc.f % 2
        first, second = self.targets()
        q = c * 2 + (1 - c) * 1
        for k in range(2):
            r = self.rows(k)
            self.hop_copy(1, k, first).wait_recv()
            self.hop[2, r] = (
                self.mine(q, r) + self.back[q, r].astype(F32) + self.hop[4, r].astype(F32)
            ).astype(BF)
            self.hop_copy(2, k, second).start()

    def finish(self, store):
        pc = self.place
        if not pc.two_level:
            total = self.mine(0)
            for e in range(1, pc.count):
                self.far_copy(e).wait()
                total = total + self.back[e - 1].astype(F32)
            store(total)
            return
        first, second = self.targets()
        self.core_copy(0).wait_recv()
        for k in range(2):
            self.hop_copy(0, k, first).wait_recv()
            self.hop_copy(2, k, second).wait_recv()
        store(
            self.mine(0)
            + self.back[0].astype(F32)
            + self.hop[3].astype(F32)
            + self.hop[5].astype(F32)
        )
        for q in range(4):
            self.core_copy(q).wait_send()
        for k in range(2):
            self.hop_copy(0, k, first).wait_send()
            self.hop_copy(1, k, first).wait_send()
            self.hop_copy(2, k, second).wait_send()


class ReadyScatter(PlaneScatter):
    def __init__(self, place, part, back, hop, ssem, rsem):
        super().__init__(place, None, None, back, hop, ssem, rsem)
        self.part = part
        if place.two_level:
            o = place.slots()
            self.here = (o[0], o[2], o[3], o[6])
            self.gone = (o[1], o[4], o[5], o[7])

    def mine(self, q, r=slice(None)):
        if not self.place.two_level:
            return self.part(self.place.me)[...].astype(F32)
        return self.part(pick(q, self.here))[r].astype(F32)

    def core_copy(self, q):
        core = self.place.mates()[0]
        v = self.part(self.gone[q])
        return remote(v, self.back.at[q], self.ssem.at[q], self.rsem.at[q], core)

    def far_copy(self, e):
        pc = self.place
        v = self.part((pc.me + e) % pc.count)
        return remote(v, self.back.at[e - 1], self.ssem.at[e - 1], self.rsem.at[e - 1],
                      pc.plane(e))

    def start(self):
        pc = self.place
        if pc.two_level:
            for q in (3, 2, 1, 0):
                self.core_copy(q).start()
        else:
            for e in range(1, pc.count):
                self.far_copy(e).start()


class RowSends:
    def __init__(self, place, layer, out, sems):
        self.place, self.layer, self.out = (place, layer, out)
        self.lsem, self.ss, self.sr = sems

    def copies(self, f, src):
        pc = self.place
        e = (self.layer * pc.nf + f - pc.me + pc.count) % pc.count
        own = self.out.at[pc.me]
        k = (e + pc.count - 1) % pc.count
        away = remote(src, own, self.ss.at[f], self.sr.at[k], (self.layer, pc.b, f))
        return (e, away, pltpu.make_async_copy(src, own, self.lsem))

    def start(self, f, src):
        e, away, local = self.copies(f, src)

        @pl.when(e != 0)
        def _():
            away.start()

        @pl.when(e == 0)
        def _():
            local.start()

    def finish(self, src):
        pc = self.place
        for f in range(pc.nf):
            e, away, local = self.copies(f, src)

            @pl.when(e != 0)
            def _():
                away.wait_send()

            @pl.when(e == 0)
            def _():
                local.wait()

        @pl.when(pc.s == self.layer)
        def _():
            for e in range(1, pc.count):
                q = pc.slot_from(e)
                remote(src, self.out.at[q], self.ss.at[0], self.sr.at[e - 1], pc.plane(e)).wait_recv()


def row_scratch(dims):
    dma = pltpu.SemaphoreType.DMA
    return [dma(()), dma((dims[2],)), dma((dims[0] * dims[2],))]


class LineGather:
    def __init__(self, place, piece, out, sems, part=None):
        self.place, self.piece = (place, piece)
        self.view = lambda t: out.at[t] if part is None else out.at[t, part]
        self.lsem, self.ss, self.sr = sems
        self.k = 0

    def local(self):
        return pltpu.make_async_copy(self.piece, self.view(self.place.b), self.lsem)

    def hop(self, way, k, came):
        pc = self.place
        t = pc.b - way * (k - (0 if came else 1))
        src = self.piece if k == 1 and not came else self.view(t)
        i = k - 1 + (0 if way == 1 else pc.nb - 1)
        return remote(
            src, self.view(t), self.ss.at[i], self.sr.at[i], (pc.s, pc.b + way, pc.f)
        )

    def sends(self, way, k):
        b, nb = (self.place.b, self.place.nb)
        return (b >= k - 1) & (b < nb - 1) if way == 1 else (b <= nb - k) & (b > 0)

    def comes(self, way, k):
        b, nb = (self.place.b, self.place.nb)
        return b >= k if way == 1 else b <= nb - 1 - k

    def arrived(self, k):
        for way in (1, -1):
            @pl.when(self.comes(way, k))
            def _():
                self.hop(way, k, True).wait_recv()

    def start(self):
        self.local().start()
        self.service()

    def service(self):
        if self.k == self.place.nb - 1:
            return
        self.k += 1
        if self.k > 1:
            self.arrived(self.k - 1)
        for way in (1, -1):
            @pl.when(self.sends(way, self.k))
            def _():
                self.hop(way, self.k, False).start()

    def finish(self):
        last = self.place.nb - 1
        while self.k < last:
            self.service()
        self.arrived(last)
        for k in range(1, last + 1):
            for way in (1, -1):
                @pl.when(self.sends(way, k))
                def _():
                    self.hop(way, k, False).wait_send()
        self.local().wait()


class LineReduce:
    def __init__(self, place, terms, store, sems, load=None):
        self.place, self.terms, self.store, self.load = (place, terms, store, load)
        self.out, self.came, self.ss, self.sr = sems
        self.k = 0

    def index(self, way, k):
        return k - 1 + (0 if way == 1 else self.place.nb - 1)

    def hop(self, way, k):
        pc = self.place
        i = self.index(way, k)
        return remote(
            self.out.at[i], self.came.at[i], self.ss.at[i], self.sr.at[i],
            (pc.s, pc.b + way, pc.f),
        )

    def rank(self, way):
        pc = self.place
        return pc.b if way == 1 else pc.nb - 1 - pc.b

    def sends(self, way, k):
        r = self.rank(way)
        return (r < k) & (r < self.place.nb - 1)

    def start(self):
        if self.load is not None:
            self.load.wait()
        self.service()

    def service(self):
        nb = self.place.nb
        if self.k == nb - 1:
            return
        self.k += 1
        k = self.k
        for way in (1, -1):
            r = self.rank(way)
            t = nb - k + r if way == 1 else k - 1 - r
            i = self.index(way, k)

            @pl.when(self.sends(way, k) & (r == 0))
            def _():
                self.out[i] = self.terms(t)

            if k > 1:
                @pl.when(self.sends(way, k) & (r > 0))
                def _():
                    self.hop(way, k - 1).wait_recv()
                    total = self.terms(t).astype(F32) + self.came[i - 1].astype(F32)
                    self.out[i] = total.astype(BF)

            @pl.when(self.sends(way, k))
            def _():
                self.hop(way, k).start()

    def finish(self):
        pc = self.place
        last = pc.nb - 1
        while self.k < last:
            self.service()
        right, left = (self.index(1, last), self.index(-1, last))

        @pl.when(pc.b == 0)
        def _():
            self.hop(-1, last).wait_recv()
            self.store(self.terms(pc.b).astype(F32) + self.came[left].astype(F32))

        @pl.when(pc.b == last)
        def _():
            self.hop(1, last).wait_recv()
            self.store(self.terms(pc.b).astype(F32) + self.came[right].astype(F32))

        @pl.when((pc.b > 0) & (pc.b < last))
        def _():
            self.hop(1, last).wait_recv()
            self.hop(-1, last).wait_recv()
            self.store(
                self.terms(pc.b).astype(F32)
                + self.came[right].astype(F32)
                + self.came[left].astype(F32)
            )

        for k in range(1, last + 1):
            for way in (1, -1):
                @pl.when(self.sends(way, k))
                def _():
                    self.hop(way, k).wait_send()


def gather_scratch(dims):
    dma = pltpu.SemaphoreType.DMA
    return [dma(()), dma((2 * (dims[1] - 1),)), dma((2 * (dims[1] - 1),))]


def reduce_scratch(dims, *block):
    dma = pltpu.SemaphoreType.DMA
    n = 2 * (dims[1] - 1)
    return [pltpu.VMEM((n,) + block, BF), pltpu.VMEM((n,) + block, BF), dma((n,)), dma((n,))]


class Riders:
    def __init__(self, dims, specs, arrays):
        self.dims, self.specs, self.arrays = (dims, specs, arrays)
        self.shapes = []
        self.places = [AN] * len(specs)
        self.outs = []
        self.scratch = []
        self.sizes = []
        for spec, a in zip(specs, arrays):
            if spec[0] == "gather":
                shape = (dims[1],) + a.shape[1:]
                scratch = gather_scratch(dims)
            else:
                lo, hi = spec[1]
                shape = (hi - lo,) + a.shape[2:]
                scratch = reduce_scratch(dims, *shape)
                scratch += [
                    pltpu.VMEM((dims[1],) + shape, BF), pltpu.SemaphoreType.DMA(())
                ]
            self.outs.append(AN if spec[0] == "gather" else VM)
            self.shapes.append(jax.ShapeDtypeStruct(shape, a.dtype))
            self.scratch += scratch
            self.sizes.append(len(scratch))
        self.count = len(specs)

    def board(self, place, ins, outs, scratch):
        out = []
        for spec, size, a, o in zip(self.specs, self.sizes, ins, outs):
            mine, scratch = (scratch[:size], scratch[size:])
            if spec[0] == "gather":
                out.append(LineGather(place, a.at[spec[1]], o, mine))
            else:
                lo, hi = spec[1]

                def store(value, o=o):
                    o[...] = value.astype(BF)

                terms, sem = mine[4:]
                load = pltpu.make_async_copy(a.at[:, lo:hi], terms, sem)
                load.start()
                out.append(
                    LineReduce(place, lambda t, r=terms: r[t], store, mine[:4], load)
                )
        return (out, scratch)


def each(riders, what):
    for r in riders:
        getattr(r, what)()


def scatter_scratch(dims, *block):
    count = dims[0] * dims[2]
    if dims[0] == 2 and dims[2] == 4:
        near, away, hops, sems = (4, 4, 6, 10)
    else:
        near, away, hops, sems = (1, count - 1, 1, count - 1)
    return [
        pltpu.VMEM((near,) + block, F32),
        pltpu.VMEM((away,) + block, BF),
        pltpu.VMEM((away,) + block, BF),
        pltpu.VMEM((hops,) + block, BF),
        pltpu.SemaphoreType.DMA((sems,)),
        pltpu.SemaphoreType.DMA((sems,)),
    ]


def call(kernel, name, cid, outs, out_specs, in_specs, scratch, args):
    params = pltpu.CompilerParams(
        collective_id=cid, has_side_effects=True, vmem_limit_bytes=VMEM_LIMIT
    )
    return pl.pallas_call(
        kernel,
        name=name,
        out_shape=outs,
        in_specs=in_specs,
        out_specs=out_specs,
        scratch_shapes=scratch,
        compiler_params=params,
    )(*args)


def column_start(dims, part, b, f, y, half):
    ns, nb, nf = dims
    return part * nb * nf * ns * half + ((b * nf + f) * ns + y) * half


def columns_of(ref, q, nf, wide):
    return ref.at[:, q % nf, :, pl.ds(pl.multiple_of((q // nf) * wide, wide), wide)]


def gather_weights_kernel(
    dims, w_ref, wq_ref, wo_ref, wd, small, gup, wdp, gu_first, qo_first, qz, small_all,
    pack, qcol, qh, lsem, ps, pr, ms, mr, qs, qr, *rest
):
    pc = Place(dims)
    ns, nb, nf = dims
    half = wd.shape[1]
    wide = qh.shape[2]
    greet(pc, "all", True)
    qkv = wq_ref.shape[2]
    full = jnp.concatenate([wq_ref[0], wo_ref[0]], axis=1)
    for y in range(ns):
        qcol[y] = full[:, y * wide : (y + 1) * wide]
    across = []
    for d in range(1, ns):
        y = (pc.s + d) % ns
        t = (y, pc.b, pc.f)
        i = 3 * (d - 1)
        across.append(remote(qcol.at[y], qh.at[pc.s], ms.at[i], mr.at[i], t))
        across.append(remote(wd.at[y], wdp.at[pc.s], ms.at[i + 1], mr.at[i + 1], t))
        across.append(remote(small, small_all.at[pc.s], ms.at[i + 2], mr.at[i + 2], t))
    for c in across:
        c.start()
    qh[pc.s] = qcol[pc.s]
    local = [
        pltpu.make_async_copy(wd.at[pc.s], wdp.at[pc.s], lsem.at[0]),
        pltpu.make_async_copy(small, small_all.at[pc.s], lsem.at[1]),
    ]
    for c in local:
        c.start()
    own = pltpu.make_async_copy(pack.at[pc.s, pc.f], gup.at[pc.s, pc.f], lsem.at[2])

    def piece(y, f):
        e = (y * nf + f - pc.me + pc.count) % pc.count
        k = (e + pc.count - 1) % pc.count
        return (
            e,
            remote(pack.at[y, f], gup.at[pc.s, pc.f], ps.at[k], pr.at[k], (y, pc.b, f)),
        )

    for f in range(nf):
        for y in range(ns):
            pieces = []
            for part in range(2):
                for b in range(nb):
                    c0 = column_start(dims, part, b, f, y, half)
                    pieces.append(w_ref[0, :, c0 : c0 + half])
            pack[y, f] = jnp.concatenate(pieces, axis=1)
            e, c = piece(y, f)

            @pl.when(e != 0)
            def _():
                c.start()

    own.start()
    for d in range(ns - 1):
        across[3 * d].wait()
    line_q = LineGather(pc, qh, qz, rest[0:3])
    lines = [
        LineGather(pc, gup.at[0, f], gu_first, rest[3 + 3 * f : 6 + 3 * f], f) for f in range(nf)
    ]
    line_q.start()

    def arrived(y, f):
        e, c = piece(y, f)
        k = (2 * pc.count - e - 1) % pc.count

        @pl.when(e != 0)
        def _():
            remote(pack.at[0, 0], gup.at[y, f], ps.at[k], pr.at[k], (y, pc.b, f)).wait_recv()

    own.wait()
    line_q.service()
    for f in range(nf):
        arrived(0, f)
        lines[f].start()
    line_q.service()
    for line in lines:
        line.service()
    line_q.finish()
    gather = PlaneGather(pc, lambda q: columns_of(qo_first, q, nf, wide), qs, qr)
    columns_of(qo_first, pc.me, nf, wide)[...] = qz[:, 0]
    gather.start()
    for step in range(1, min(6, pc.count)):
        gather.before(step)
    for line in lines:
        line.service()
    for step in range(min(6, pc.count), pc.count):
        gather.before(step)
    gather.finish()
    for y in range(1, ns):
        for f in range(nf):
            arrived(y, f)
    for y in range(ns):
        for f in range(nf):
            e, c = piece(y, f)

            @pl.when(e != 0)
            def _():
                c.wait_send()

    for c in local:
        c.wait()
    for i, c in enumerate(across):
        if i % 3:
            c.wait()
    for line in lines:
        line.finish()


def gather_weights(dims, w, wq, wo, wd, small):
    ns, nb, nf = dims
    count = ns * nf
    half, width = wd.shape[1:]
    dr = wq.shape[1]
    cols = wq.shape[2] + wo.shape[2]
    wide = cols // ns
    two_ff = 2 * nb * half
    sds = jax.ShapeDtypeStruct
    outs = (
        sds((ns, nf, dr, two_ff), BF),
        sds((ns, half, width), BF),
        sds((nb, nf, dr, two_ff), BF),
        sds((nb, nf, dr, cols), BF),
        sds((nb, ns, dr, wide), BF),
        sds((ns,) + small.shape, F32),
    )
    dma = pltpu.SemaphoreType.DMA
    return call(
        functools.partial(gather_weights_kernel, dims),
        "gather_weights",
        0,
        outs,
        [AN, AN, AN, VM, VM, AN],
        [VM, VM, VM, AN, AN],
        [
            pltpu.VMEM((ns, nf, dr, two_ff), BF),
            pltpu.VMEM((ns, dr, wide), BF),
            pltpu.VMEM((ns, dr, wide), BF),
            dma((4,)),
            dma((count,)),
            dma((count,)),
            dma((3 * (ns - 1),)),
            dma((3 * (ns - 1),)),
        ]
        + gather_sems(dims)
        + gather_scratch(dims) * (1 + nf),
        (w, wq, wo, wd, small),
    )


def rms(values):
    return lax.rsqrt(jnp.mean(values * values, axis=0, keepdims=True) + 1e-06)


def column(rows_t, first, count):
    return jnp.concatenate([rows_t[:, k : k + 1] for k in range(first, first + count)], axis=0)


def rows_of(values):
    v = folded(values)
    return jnp.concatenate(
        [v[k : k + 128].T.sum(axis=0, keepdims=True) for k in range(0, v.shape[0], 128)], axis=0
    )


def folded(v):
    out = v[:, :128]
    for k in range(1, v.shape[1] // 128):
        out = out + v[:, k * 128 : (k + 1) * 128]
    return out


def fill_masks(pc, mask, meta_t, query_docs):
    nk, rows = mask.shape[:2]
    key_i = lax.broadcasted_iota(jnp.int32, (rows, rows), 0)
    query_i = lax.broadcasted_iota(jnp.int32, (rows, rows), 1)
    per = rows // 128
    for j in range(nk):
        same = column(meta_t, j * per, per) == query_docs
        if j == 0:
            live = same & (key_i <= query_i)
        else:
            live = same & (key_i < (pc.b - j + 1) * rows)
        mask[j] = jnp.where(live, 0.0, NEG)


def load_qo(qo, w, wo, sems):
    cols = w.shape[1]
    c1 = pltpu.make_async_copy(qo.at[:, 0:cols], w, sems.at[0])
    c2 = pltpu.make_async_copy(qo.at[:, cols : cols + wo.shape[1]], wo, sems.at[1])
    c1.start()
    c2.start()
    return (c1, c2)


def gains_of(small_t, width, qkv):
    n = width // 128
    return (
        column(small_t, 0, n),
        column(small_t, n, n),
        column(small_t, 2 * n, qkv // 128),
    )


def padded_t(v):
    n = v.shape[0]
    return jnp.concatenate([v, jnp.zeros((128 - n, 128), v.dtype)], axis=0).T


def attention_forward_kernel(
    dims, nk, layer, plan, carry, h_ref, small_ref, meta_ref, docs_ref, cos_ref, sin_ref, qo_all,
    *refs
):
    n = plan.count
    if carry:
        block_ref, refs = (refs[0], refs[1:])
    ins, refs = (refs[:n], refs[n:])
    normed_ref, q_ref, kv_ref, lse_ref, mixed_ref, res_ref, n2_ref = refs[:7]
    outs, refs = (refs[7 : 7 + n], refs[7 + n :])
    if carry:
        block_all, refs = (refs[0], refs[1:])
    w, wo, mask, joined, ssem, rsem, qsem = refs[:7]
    refs = refs[7:]
    pc = Place(dims)
    width, rows = h_ref.shape
    loads = load_qo(qo_all, w, wo, qsem)
    greet(pc, "mates" if carry else None, True)
    riders, refs = plan.board(pc, ins, outs, refs)
    if carry == "lanes":
        own = block_ref
        slot = lambda q: block_all.at[:, lanes(q, rows)]
    elif carry == "columns":
        own = block_ref.at[:, 1]
        slot = lambda q: columns_of(block_all, q, pc.nf, block_ref.shape[3])
    gather = None
    if carry:
        gather = PlaneGather(pc, slot, *refs)
        slot(pc.me)[...] = own[...]
        gather.start()
    each(riders, "start")
    g1, g2, bias = gains_of(padded_t(small_ref[layer]), width, w.shape[1])
    hidden = h_ref[...].astype(BF).astype(F32)
    normed = (hidden * rms(hidden) * g1).astype(BF)
    normed_ref[...] = normed
    fill_masks(pc, mask, padded_t(meta_ref[...]), docs_ref[...])
    loads[0].wait()
    joined[...] = tn(w[...], normed) + bias
    cos_part = cos_ref[...]
    sin_part = sin_ref[...]
    half = HD // 2

    def turned(row):
        u1 = joined[pl.ds(row, half), :]
        u2 = joined[pl.ds(row + half, half), :]
        return (u1 * cos_part - u2 * sin_part, u2 * cos_part + u1 * sin_part)

    for g in range(KVH):
        r1, r2 = turned((H + g) * HD)
        kv_ref[0, g, :half, :] = r1.astype(BF)
        kv_ref[0, g, half:, :] = r2.astype(BF)
        v0 = (H + KVH + g) * HD
        kv_ref[0, KVH + g] = joined[v0 : v0 + HD, :].astype(BF)
    sends = [
        remote(kv_ref.at[0], kv_ref.at[j], ssem.at[j - 1], rsem.at[j - 1], pc.along(j))
        for j in range(1, nk)
    ]
    for c in sends:
        c.start()
    scale = HD**-0.5
    for head in range(H):
        r1, r2 = turned(head * HD)
        q_ref[head, :half, :] = (r1 * scale).astype(BF)
        q_ref[head, half:, :] = (r2 * scale).astype(BF)
    for c in sends:
        c.wait()
    each(riders, "service")
    for g in range(KVH):
        keys = [kv_ref[j, g].T for j in range(nk)]
        values = [kv_ref[j, KVH + g] for j in range(nk)]

        def one_head(i, carried):
            head = g * GROUP + i
            q = q_ref[head]
            s = [nn(keys[j], q) + mask[j] for j in range(nk)]
            top = s[0].max(axis=0, keepdims=True)
            for j in range(1, nk):
                top = jnp.maximum(top, s[j].max(axis=0, keepdims=True))
            e = [jnp.exp(x - top) for x in s]
            total = e[0].sum(axis=0, keepdims=True)
            for j in range(1, nk):
                total = total + e[j].sum(axis=0, keepdims=True)
            out = nn(values[0], e[0].astype(BF))
            for j in range(1, nk):
                out = out + nn(values[j], e[j].astype(BF))
            lse_ref[head] = top + jnp.log(total)
            mixed_ref[head] = (out / total).astype(BF)
            return carried

        lax.fori_loop(0, GROUP, one_head, 0)
        each(riders, "service")
        if carry and g == 0:
            for step in range(1, min(6, pc.count)):
                gather.before(step)
    mixed = mixed_ref[...].reshape(H * HD, rows)
    loads[1].wait()
    residual = hidden + tn(wo[...], mixed)
    res_ref[...] = residual
    n2_ref[...] = (residual * rms(residual) * g2).astype(BF)
    if carry:
        for step in range(min(6, pc.count), pc.count):
            gather.before(step)
        gather.finish()
    each(riders, "finish")


def attention_forward(dims, nk, cid, layer, hidden, small, meta, docs, cos_part, sin_part, qo_all,
                      plan, carry, block):
    width, rows = hidden.shape
    ns, nb, nf = dims
    count = ns * nf
    qkv = qo_all.shape[1] - width
    sds = jax.ShapeDtypeStruct
    outs = [
        sds((width, rows), BF),
        sds((H, HD, rows), BF),
        sds((nk, 2 * KVH, HD, rows), BF),
        sds((H, 1, rows), F32),
        sds((H, HD, rows), BF),
        sds((width, rows), F32),
        sds((width, rows), BF),
    ] + plan.shapes
    dma = pltpu.SemaphoreType.DMA
    if carry == "lanes":
        outs.append(sds((width, count * rows), BF))
    else:
        outs.append(sds((nb, nf, block.shape[2], ns * block.shape[3]), BF))
    out = call(
        functools.partial(attention_forward_kernel, dims, nk, layer, plan, carry),
        "attention_forward",
        cid,
        tuple(outs),
        [VM] * 7 + plan.outs + [VM],
        [VM] * 6 + [AN, VM] + plan.places,
        [
            pltpu.VMEM((width, qkv), BF),
            pltpu.VMEM((width, width), BF),
            pltpu.VMEM((nk, rows, rows), F32),
            pltpu.VMEM((qkv, rows), F32),
            dma((nk - 1,)),
            dma((nk - 1,)),
            dma((2,)),
        ]
        + plan.scratch
        + gather_sems(dims),
        (hidden, small, meta, docs, cos_part, sin_part, qo_all, block, *plan.arrays),
    )
    return (out[:7], out[7:])


def attention_backward_kernel(
    dims, nk, layer, plan, carry, g_ref, small_ref, meta_ref, docs_ref, cos_ref, sin_ref,
    h_ref, normed_ref, q_ref, kv_ref, lse_ref, mixed_ref, qo_all, *refs
):
    n = plan.count
    parts_ref, more_ref, refs = (refs[0], refs[1], refs[2:])
    ins, refs = (refs[:n], refs[n:])
    gh_ref, dqo_ref, dsmall_ref = refs[:3]
    outs, refs = (refs[3 : 3 + n], refs[3 + n :])
    out_ref, refs = (refs[0], refs[1:])
    if carry == "columns":
        rows_ref, refs = (refs[0], refs[1:])
    w, wo, mask, dmix, dkv, out_kv, in_kv, gj, ssem, rsem, qsem = refs[:11]
    refs = refs[11:]
    pc = Place(dims)
    width, rows = h_ref.shape
    qkv = w.shape[1]
    loads = load_qo(qo_all, w, wo, qsem)
    riders, refs = plan.board(pc, ins, outs, refs)
    if carry == "columns":
        held, held_sem = refs[7:]
        coming = pltpu.make_async_copy(parts_ref, held, held_sem)
        coming.start()
    greet(pc, "all" if carry == "columns" else "mates", True)
    if carry == "columns":
        part = lambda q: columns_of(held, q, pc.nf, out_ref.shape[2])
        hand_out = RowSends(pc, 1, rows_ref, refs[4:7])
        coming.wait()
    else:
        part = lambda q: parts_ref.at[q]
    scatter = ReadyScatter(pc, part, *refs[:4])
    scatter.start()
    each(riders, "start")
    g1 = column(padded_t(small_ref[layer]), 0, width // 128)
    fill_masks(pc, mask, padded_t(meta_ref[...]), docs_ref[...])
    grl = g_ref[...].astype(BF)
    loads[1].wait()
    dmix[...] = nn(wo[...], grl).astype(BF).reshape(dmix.shape)
    dqo_ref[:, qkv:] = nt(mixed_ref[...].reshape(H * HD, rows), grl).astype(BF)
    scatter.diagonal()
    scatter.early()
    if carry == "columns":
        for f in range(pc.nf):
            hand_out.start(f, more_ref.at[f])
    cos_part = cos_ref[...]
    sin_part = sin_ref[...]
    half = HD // 2
    scale = HD**-0.5
    dkv[...] = jnp.zeros_like(dkv)

    def unturned(d1, d2):
        return (d1 * cos_part + d2 * sin_part, d2 * cos_part - d1 * sin_part)

    for g in range(KVH):
        keys_t = [kv_ref[j, g] for j in range(nk)]
        keys = [k.T for k in keys_t]
        values = [kv_ref[j, KVH + g].T for j in range(nk)]

        def one_head(i, carried):
            head = g * GROUP + i
            q = q_ref[head]
            do = dmix[head]
            lse = lse_ref[head]
            p = [jnp.exp(nn(keys[j], q) + mask[j] - lse) for j in range(nk)]
            dp = [nn(values[j], do) for j in range(nk)]
            delta = (p[0] * dp[0]).sum(axis=0, keepdims=True)
            for j in range(1, nk):
                delta = delta + (p[j] * dp[j]).sum(axis=0, keepdims=True)
            dq = jnp.zeros((HD, rows), F32)
            for j in range(nk):
                ds = (p[j] * (dp[j] - delta)).astype(BF)
                dkv[j, g] += nt(q, ds)
                dkv[j, KVH + g] += nt(do, p[j].astype(BF))
                dq = dq + nn(keys_t[j], ds)
            dq = dq * scale
            r1, r2 = unturned(dq[:half], dq[half:])
            gj[pl.ds(pl.multiple_of(head * HD, HD), half), :] = r1.astype(BF)
            gj[pl.ds(pl.multiple_of(head * HD + half, half), half), :] = r2.astype(BF)
            return carried

        lax.fori_loop(0, GROUP, one_head, 0)
        each(riders, "service")
        if g == 0:
            scatter.late()
    for j in range(1, nk):
        out_kv[j - 1] = dkv[j].astype(BF)
    sends = [
        remote(out_kv.at[j - 1], in_kv.at[j - 1], ssem.at[j - 1], rsem.at[j - 1],
               pc.along(pc.nb - j))
        for j in range(1, nk)
    ]
    for c in sends:
        c.start()
    for c in sends:
        c.wait()
    own = dkv[0]
    for j in range(1, nk):
        own = own + in_kv[j - 1].astype(F32)
    for g in range(KVH):
        r1, r2 = unturned(own[g, :half], own[g, half:])
        k0 = (H + g) * HD
        gj[k0 : k0 + half, :] = r1.astype(BF)
        gj[k0 + half : k0 + HD, :] = r2.astype(BF)
        v0 = (H + KVH + g) * HD
        gj[v0 : v0 + HD, :] = own[KVH + g].astype(BF)
    gjv = gj[...]
    n1 = width // 128
    dsmall_ref[n1 : n1 + qkv // 128, :] = rows_of(gjv.astype(F32))
    loads[0].wait()
    dqo_ref[:, :qkv] = nt(normed_ref[...], gjv).astype(BF)
    gn = nn(w[...], gjv)
    hidden = h_ref[...].astype(BF).astype(F32)
    scale_one = rms(hidden)
    unit = hidden * scale_one
    dsmall_ref[:n1, :] = rows_of(gn * unit)
    u = gn * g1
    gh_ref[...] = g_ref[...] + scale_one * (u - unit * jnp.mean(u * unit, axis=0, keepdims=True))

    def store(total):
        if carry == "columns":
            out_ref[...] = total.astype(BF)
        else:
            out_ref[...] = more_ref[...] + total

    scatter.finish(store)
    if carry == "columns":
        hand_out.finish(more_ref.at[0])
    each(riders, "finish")


def attention_backward(dims, nk, cid, layer, g, small, meta, docs, cos_part, sin_part, hidden,
                       normed, q, kv, lse, mixed, qo_all, plan, carry, late):
    width, rows = hidden.shape
    qkv = qo_all.shape[1] - width
    sds = jax.ShapeDtypeStruct
    outs = [
        sds((width, rows), F32),
        sds((width, qkv + width), BF),
        sds(((width + qkv) // 128, 128), F32),
    ] + plan.shapes
    dma = pltpu.SemaphoreType.DMA
    block = (2 * KVH, HD, rows)
    if carry == "columns":
        summed = (dims[1], late[0].shape[2], late[0].shape[3] // dims[0])
        outs += [sds(summed, BF), sds((dims[0] * dims[2],) + late[1].shape[1:], BF)]
        places = [VM, AN]
    else:
        summed = (width, rows)
        outs.append(sds(summed, F32))
        places = [VM]
    out = call(
        functools.partial(attention_backward_kernel, dims, nk, layer, plan, carry),
        "attention_backward",
        cid,
        tuple(outs),
        [VM] * 3 + plan.outs + places,
        [VM] * 12 + [AN] + [AN if carry == "columns" else VM, VM] + plan.places,
        [
            pltpu.VMEM((width, qkv), BF),
            pltpu.VMEM((width, width), BF),
            pltpu.VMEM((nk, rows, rows), F32),
            pltpu.VMEM((H, HD, rows), BF),
            pltpu.VMEM((nk,) + block, F32),
            pltpu.VMEM((nk - 1,) + block, BF),
            pltpu.VMEM((nk - 1,) + block, BF),
            pltpu.VMEM((qkv, rows), BF),
            dma((nk - 1,)),
            dma((nk - 1,)),
            dma((2,)),
        ]
        + plan.scratch
        + scatter_scratch(dims, *summed)[2:]
        + (
            row_scratch(dims) + [pltpu.VMEM(late[0].shape, BF), dma(())]
            if carry == "columns"
            else []
        ),
        (g, small, meta, docs, cos_part, sin_part, hidden, normed, q, kv, lse, mixed, qo_all,
         *late, *plan.arrays),
    )
    return (out[:3], out[3:])


def sequence_of(pc):
    if pc.two_level:
        return ((0, 1, 2, 3, 6, 7, 4, 5), 5, 7)
    return (tuple(range(pc.count)), pc.count - 1, pc.count - 1)


def lanes(slot, rows):
    return pl.ds(pl.multiple_of(slot * rows, rows), rows)


def transpose_into(dst, src):
    cols = src.shape[1]
    for c0 in range(0, cols, 128):
        c1 = min(c0 + 128, cols)
        dst[c0:c1, :] = src[:, c0:c1].T


def feed_forward_kernel(dims, plan, x_ref, res_ref, wgu_ref, wd_ref, *refs):
    n = plan.count
    ins, refs = (refs[:n], refs[n:])
    out_ref, x_out, gu_out = refs[:3]
    outs, refs = (refs[3 : 3 + n], refs[3 + n :])
    x_all, gu_all, lsem, wgu_t, wd_t, gu, inner, near, away, back, hop, ss, sr, gs, gr = refs[:15]
    pc = Place(dims)
    width, rows = x_ref.shape
    ff = wd_ref.shape[0]
    riders, _ = plan.board(pc, ins, outs, refs[15:])
    greet(pc, "mates", n > 0)
    gather = PlaneGather(pc, lambda q: x_all.at[:, lanes(q, rows)], gs, gr)
    scatter = PlaneScatter(pc, near, away, back, hop, ss, sr)
    x_all[:, lanes(pc.me, rows)] = x_ref[...]
    gather.start()
    each(riders, "start")
    transpose_into(wgu_t, wgu_ref)
    transpose_into(wd_t, wd_ref)
    sequence, diagonal_at, early_at = sequence_of(pc)
    chunk = 32 if ff % 32 == 0 else 16

    def step_body(turn, carry):
        step = pick(turn, sequence)

        for k in range(pc.count):
            @pl.when(step == k)
            def _():
                gather.before(k)

        slot = pick(step, gather.order)
        sl = lanes(slot, rows)
        gu[...] = nn(wgu_t[...], x_all[:, sl])

        def act(i, c):
            r = pl.multiple_of(i * chunk, chunk)
            gate = gu[pl.ds(r, chunk), :]
            up = gu[pl.ds(ff + r, chunk), :]
            gu_all[pl.ds(r, chunk), sl] = gate.astype(BF)
            gu_all[pl.ds(ff + r, chunk), sl] = up.astype(BF)
            inner[pl.ds(r, chunk), :] = (gate * jax.nn.sigmoid(gate) * up).astype(BF)
            return c

        lax.fori_loop(0, ff // chunk, act, 0)
        scatter.put(step, nn(wd_t[...], inner[...]))

        @pl.when(turn == 3)
        def _():
            each(riders, "service")

        @pl.when(turn == diagonal_at)
        def _():
            scatter.diagonal()

        @pl.when(turn == early_at)
        def _():
            scatter.early()

        return carry

    lax.fori_loop(0, pc.count, step_body, 0)
    leaving = [
        pltpu.make_async_copy(gu_all, gu_out, lsem.at[0]),
        pltpu.make_async_copy(x_all, x_out, lsem.at[1]),
    ]
    each(leaving, "start")
    each(riders, "service")

    def store(total):
        out_ref[...] = res_ref[...] + total

    scatter.result(store)
    gather.finish()
    each(leaving, "wait")
    each(riders, "finish")


def feed_forward(dims, cid, x, residual, wgu, wd, plan):
    width, rows = x.shape
    count = dims[0] * dims[2]
    two_ff, ff = (wgu.shape[1], wd.shape[0])
    sds = jax.ShapeDtypeStruct
    dma = pltpu.SemaphoreType.DMA
    out = call(
        functools.partial(feed_forward_kernel, dims, plan),
        "feed_forward",
        cid,
        (
            sds((width, rows), F32),
            sds((width, count * rows), BF),
            sds((two_ff, count * rows), BF),
            *plan.shapes,
        ),
        [VM, AN, AN] + plan.outs,
        [VM] * 4 + plan.places,
        [
            pltpu.VMEM((width, count * rows), BF),
            pltpu.VMEM((two_ff, count * rows), BF),
            dma((2,)),
            pltpu.VMEM((two_ff, width), BF),
            pltpu.VMEM((width, ff), BF),
            pltpu.VMEM((two_ff, rows), F32),
            pltpu.VMEM((ff, rows), BF),
        ]
        + scatter_scratch(dims, width, rows)
        + gather_sems(dims)
        + plan.scratch,
        (x, residual, wgu, wd, *plan.arrays),
    )
    return (out[:3], out[3:])


def feed_backward_kernel(
    dims, layer, plan, g_ref, res_ref, x_in, gu_in, wgu_ref, wd_ref, small_ref, *refs
):
    n = plan.count
    ins, refs = (refs[:n], refs[n:])
    gr_ref, dwgu_ref, dwd_ref, dsmall_ref = refs[:4]
    outs, refs = (refs[4 : 4 + n], refs[4 + n :])
    x_all, gu_all, lsem, g_all, inner, ggu, gi, near, away, back, hop, ss, sr, gs, gr = refs[:15]
    coming = [
        pltpu.make_async_copy(gu_in, gu_all, lsem.at[0]),
        pltpu.make_async_copy(x_in, x_all, lsem.at[1]),
    ]
    each(coming, "start")
    pc = Place(dims)
    width, rows = g_ref.shape
    ff = wd_ref.shape[0]
    riders, _ = plan.board(pc, ins, outs, refs[15:])
    greet(pc, "mates", n > 0)
    gather = PlaneGather(pc, lambda q: g_all.at[:, lanes(q, rows)], gs, gr)
    scatter = PlaneScatter(pc, near, away, back, hop, ss, sr)
    g_all[:, lanes(pc.me, rows)] = g_ref[...].astype(BF)
    gather.start()
    each(riders, "start")
    coming[0].wait()
    sequence, diagonal_at, early_at = sequence_of(pc)
    chunk = 32 if ff % 32 == 0 else 16

    def step_body(turn, carry):
        step = pick(turn, sequence)

        for k in range(pc.count):
            @pl.when(step == k)
            def _():
                gather.before(k)

        slot = pick(step, gather.order)
        sl = lanes(slot, rows)
        gi[...] = nn(wd_ref[...], g_all[:, sl])

        def act(i, c):
            r = pl.multiple_of(i * chunk, chunk)
            gate = gu_all[pl.ds(r, chunk), sl].astype(F32)
            up = gu_all[pl.ds(ff + r, chunk), sl].astype(F32)
            grad = gi[pl.ds(r, chunk), :]
            sig = jax.nn.sigmoid(gate)
            silu = gate * sig
            inner[pl.ds(r, chunk), sl] = (silu * up).astype(BF)
            ggu[pl.ds(r, chunk), sl] = (grad * up * sig * (1.0 + gate * (1.0 - sig))).astype(BF)
            ggu[pl.ds(ff + r, chunk), sl] = (grad * silu).astype(BF)
            return c

        lax.fori_loop(0, ff // chunk, act, 0)
        scatter.put(step, nn(wgu_ref[...], ggu[:, sl]))

        @pl.when(turn == 3)
        def _():
            each(riders, "service")

        @pl.when(turn == diagonal_at)
        def _():
            scatter.diagonal()

        @pl.when(turn == early_at)
        def _():
            scatter.early()

        return carry

    lax.fori_loop(0, pc.count, step_body, 0)
    each(riders, "service")
    dwd_ref[...] = nt(inner[...], g_all[...]).astype(BF)
    scatter.late()
    coming[1].wait()
    part = width // 2
    for r in range(2):
        dwgu_ref[r * part : (r + 1) * part, :] = nt(
            x_all[r * part : (r + 1) * part, :], ggu[...]
        ).astype(BF)

    def store(total):
        residual = res_ref[...]
        scale_two = rms(residual)
        unit = residual * scale_two
        n1 = width // 128
        dsmall_ref[...] = rows_of(total * unit)
        u = total * column(padded_t(small_ref[layer]), n1, n1)
        gr_ref[...] = g_ref[...].astype(BF).astype(F32) + scale_two * (
            u - unit * jnp.mean(u * unit, axis=0, keepdims=True)
        )

    scatter.finish(store)
    gather.finish()
    each(riders, "finish")


def feed_backward(dims, cid, layer, g, residual, x_all, gu_all, wgu, wd, small, plan):
    width, rows = g.shape
    count = dims[0] * dims[2]
    two_ff, ff = (wgu.shape[1], wd.shape[0])
    sds = jax.ShapeDtypeStruct
    dma = pltpu.SemaphoreType.DMA
    out = call(
        functools.partial(feed_backward_kernel, dims, layer, plan),
        "feed_backward",
        cid,
        (
            sds((width, rows), F32),
            sds(wgu.shape, BF),
            sds(wd.shape, BF),
            sds((width // 128, 128), F32),
            *plan.shapes,
        ),
        [VM] * 4 + plan.outs,
        [VM, VM, AN, AN, VM, VM, VM] + plan.places,
        [
            pltpu.VMEM((width, count * rows), BF),
            pltpu.VMEM((two_ff, count * rows), BF),
            dma((2,)),
            pltpu.VMEM((width, count * rows), BF),
            pltpu.VMEM((ff, count * rows), BF),
            pltpu.VMEM((two_ff, count * rows), BF),
            pltpu.VMEM((ff, rows), F32),
        ]
        + scatter_scratch(dims, width, rows)
        + gather_sems(dims)
        + plan.scratch,
        (g, residual, x_all, gu_all, wgu, wd, small, *plan.arrays),
    )
    return (out[:4], out[4:])


def feed_both_kernel(
    dims, layer, x_ref, res_ref, g_ref, g_all, wgu_ref, wd_ref, small_ref,
    gr_ref, dwgu_ref, dwd_ref, dsmall_ref, parts_ref,
    x_all, inner, ggu, wgu_t, wd_t, gu, gi, near, away, back, hop, ss, sr, gs, gr,
):
    pc = Place(dims)
    width, rows = g_ref.shape
    ff = wd_ref.shape[0]
    greet(pc, "mates", False)
    gather = PlaneGather(pc, lambda q: x_all.at[:, lanes(q, rows)], gs, gr)
    scatter = PlaneScatter(pc, near, away, back, hop, ss, sr)
    x_all[:, lanes(pc.me, rows)] = x_ref[...]
    gather.start()
    transpose_into(wgu_t, wgu_ref)
    transpose_into(wd_t, wd_ref)
    sequence, diagonal_at, early_at = sequence_of(pc)
    chunk = 32 if ff % 32 == 0 else 16

    def step_body(turn, carry):
        step = pick(turn, sequence)

        for k in range(pc.count):
            @pl.when(step == k)
            def _():
                gather.before(k)

        slot = pick(step, gather.order)
        sl = lanes(slot, rows)
        gu[...] = nn(wgu_t[...], x_all[:, sl])
        gi[...] = nn(wd_ref[...], g_all[:, sl])

        def act(i, c):
            r = pl.multiple_of(i * chunk, chunk)
            gate = gu[pl.ds(r, chunk), :]
            up = gu[pl.ds(ff + r, chunk), :]
            grad = gi[pl.ds(r, chunk), :]
            sig = jax.nn.sigmoid(gate)
            silu = gate * sig
            inner[pl.ds(r, chunk), sl] = (silu * up).astype(BF)
            ggu[pl.ds(r, chunk), sl] = (grad * up * sig * (1.0 + gate * (1.0 - sig))).astype(BF)
            ggu[pl.ds(ff + r, chunk), sl] = (grad * silu).astype(BF)
            return c

        lax.fori_loop(0, ff // chunk, act, 0)
        scatter.put(step, nn(wgu_ref[...], ggu[:, sl]))

        @pl.when(turn == diagonal_at)
        def _():
            scatter.diagonal()

        @pl.when(turn == early_at)
        def _():
            scatter.early()

        parts_ref[slot] = nn(wd_t[...], inner[:, sl]).astype(BF)
        return carry

    lax.fori_loop(0, pc.count, step_body, 0)
    dwd_ref[...] = nt(inner[...], g_all[...]).astype(BF)
    scatter.late()
    part = width // 2
    for r in range(2):
        dwgu_ref[r * part : (r + 1) * part, :] = nt(
            x_all[r * part : (r + 1) * part, :], ggu[...]
        ).astype(BF)

    def store(total):
        residual = res_ref[...]
        scale_two = rms(residual)
        unit = residual * scale_two
        n1 = width // 128
        dsmall_ref[...] = rows_of(total * unit)
        u = total * column(padded_t(small_ref[layer]), n1, n1)
        gr_ref[...] = g_ref[...].astype(BF).astype(F32) + scale_two * (
            u - unit * jnp.mean(u * unit, axis=0, keepdims=True)
        )

    scatter.finish(store)
    gather.finish()


def feed_both(dims, cid, layer, x, residual, g, g_all, wgu, wd, small):
    width, rows = g.shape
    count = dims[0] * dims[2]
    two_ff, ff = (wgu.shape[1], wd.shape[0])
    sds = jax.ShapeDtypeStruct
    dma = pltpu.SemaphoreType.DMA
    return call(
        functools.partial(feed_both_kernel, dims, layer),
        "feed_both",
        cid,
        (
            sds((width, rows), F32),
            sds(wgu.shape, BF),
            sds(wd.shape, BF),
            sds((width // 128, 128), F32),
            sds((count, width, rows), BF),
        ),
        [VM] * 5,
        [VM] * 7,
        [
            pltpu.VMEM((width, count * rows), BF),
            pltpu.VMEM((ff, count * rows), BF),
            pltpu.VMEM((two_ff, count * rows), BF),
            pltpu.VMEM((two_ff, width), BF),
            pltpu.VMEM((width, ff), BF),
            pltpu.VMEM((two_ff, rows), F32),
            pltpu.VMEM((ff, rows), F32),
        ]
        + scatter_scratch(dims, width, rows)
        + gather_sems(dims),
        (x, residual, g, g_all, wgu, wd, small),
    )


def reduce_kernel(
    dims, cut, qo, terms, sa0, sa1, sb0, sb1, wd1, wd0, gu0a, gu0,
    qo_out, small_out, gu_got, wd_got,
    gsum, small, sm_in, sm_mid, sm_line, z_out, mine, give,
    lsem, ws, wr, ls, lr, zs, zr, *rest
):
    pc = Place(dims)
    ns, nb, nf = dims
    greet(pc, "all", True)
    scatter = ReadyScatter(
        pc, lambda q: columns_of(qo, q, nf, z_out.shape[2]), *rest[15:19]
    )
    scatter.start()

    def keep(value):
        gsum[...] = value.astype(BF)

    def keep_of(l):
        def store(value):
            mine[l] = value

        return store

    line = LineReduce(pc, lambda t: gu0[t, cut:nf], keep, rest[0:4])
    ends = [
        LineReduce(pc, lambda t: z_out[t], keep_of(0), rest[4:8]),
        LineReduce(pc, lambda t: terms[t], keep_of(1), rest[8:12]),
    ]
    line.start()
    ends[1].start()
    n1 = sb0.shape[0]
    per = small.shape[0] // ns
    nr = sa0.shape[0] + n1
    small[...] = jnp.zeros_like(small)
    for l, (a, g) in enumerate(((sa0, sb0), (sa1, sb1))):
        small[l * per : l * per + n1] = a[0:n1]
        small[l * per + n1 : l * per + 2 * n1] = g[...]
        small[l * per + 2 * n1 : l * per + nr] = a[n1 : a.shape[0]]
    smalls = [
        remote(small, sm_in.at[e - 1], ls.at[e - 1], lr.at[e - 1], pc.plane(e))
        for e in range(1, pc.count)
    ]
    for c in smalls:
        c.start()
    scatter.diagonal()
    scatter.early()
    hand_out = RowSends(pc, 0, gu_got, rest[12:15])
    for f in range(cut):
        hand_out.start(f, gu0a.at[f])
    for l, ref in ((0, wd0), (1, wd1)):
        @pl.when(pc.s == l)
        def _():
            pltpu.make_async_copy(ref, wd_got.at[l], lsem.at[0]).start()

        @pl.when(pc.s != l)
        def _():
            remote(ref, wd_got.at[pc.s], ws.at[0], wr.at[0], (l, pc.b, pc.f)).start()

    ends[1].service()
    scatter.late()
    line.service()
    total = small[...]
    for e, c in enumerate(smalls):
        c.wait()
        total = total + sm_in[e]
    sm_mid[...] = total
    lines = [
        remote(sm_mid, sm_line.at[d - 1], zs.at[d - 1], zr.at[d - 1], pc.along(d))
        for d in range(1, nb)
    ]
    for c in lines:
        c.start()

    def store(value):
        z_out[...] = value.astype(BF)

    scatter.finish(store)
    ends[0].start()
    ends[1].finish()
    line.service()
    ends[0].finish()
    mate = (ns - 1 - pc.s, pc.b, pc.f)
    swap = remote(give.at[0], give.at[1], ws.at[1], wr.at[1], mate)
    give[0] = mine[ns - 1 - pc.s].astype(BF)
    swap.start()
    qo_out[pc.s] = mine[pc.s]
    line.finish()
    for f in range(cut, nf):
        hand_out.start(f, gsum.at[f - cut])
    total = sm_mid[...]
    for d, c in enumerate(lines):
        c.wait()
        total = total + sm_line[d]
    small_out[...] = total
    swap.wait()
    qo_out[ns - 1 - pc.s] = give[1].astype(F32)
    hand_out.finish(gsum.at[0])
    pltpu.make_async_copy(wd0, wd_got.at[pc.s], lsem.at[0]).wait()
    remote(wd0, wd_got.at[pc.s], ws.at[0], wr.at[0], mate).wait()


def reduce_gradients(dims, cid, cut, qo, terms, smalls, wd1, wd0, gu0a, gu0):
    ns, nb, nf = dims
    count = ns * nf
    dr, wide = terms.shape[1:]
    two_ff = gu0.shape[3]
    half, width = wd0.shape
    rows = smalls[0].shape[0] + smalls[2].shape[0]
    small = (ns * (-(-rows // 8) * 8), 128)
    sds = jax.ShapeDtypeStruct
    dma = pltpu.SemaphoreType.DMA
    return call(
        functools.partial(reduce_kernel, dims, cut),
        "reduce_gradients",
        cid,
        (
            sds((ns, dr, wide), F32),
            sds(small, F32),
            sds((count, dr, two_ff), BF),
            sds((ns, half, width), BF),
        ),
        [VM] * 4,
        [VM] * 10,
        [
            pltpu.VMEM((nf - cut, dr, two_ff), BF),
            pltpu.VMEM(small, F32),
            pltpu.VMEM((count - 1,) + small, F32),
            pltpu.VMEM(small, F32),
            pltpu.VMEM((nb - 1,) + small, F32),
            pltpu.VMEM((nb, dr, wide), BF),
            pltpu.VMEM((ns, dr, wide), F32),
            pltpu.VMEM((2, dr, wide), BF),
            dma((1,)),
            dma((2,)),
            dma((2,)),
            dma((count - 1,)),
            dma((count - 1,)),
            dma((nb - 1,)),
            dma((nb - 1,)),
        ]
        + reduce_scratch(dims, nf - cut, dr, two_ff)
        + reduce_scratch(dims, dr, wide) * 2
        + row_scratch(dims)
        + scatter_scratch(dims, nb, dr, wide)[2:],
        (qo, terms, *smalls, wd1, wd0, gu0a, gu0),
    )


def lay_out_kernel(
    dims, gu0, gu1, wd, qo, small, out0, out1, gh0, gh1, take_out, take_grad,
    block_out, input_grad, g1, wqkv, bqkv, wout, g2, wgu, wdn
):
    ns, nb, nf = dims
    half = wd.shape[1]
    s = lax.axis_index("section")
    qkv = wqkv.shape[2]
    width = wout.shape[2]
    full = jnp.concatenate([qo[y] for y in range(ns)], axis=1)
    wqkv[0] = full[:, :qkv]
    wout[0] = full[:, qkv:]
    for y in range(ns):
        wdn[0, y * half : (y + 1) * half, :] = wd[y].astype(F32)
    for l, gu in enumerate((gu0, gu1)):
        @pl.when(s == l)
        def _():
            for y in range(ns):
                for f in range(nf):
                    got = gu[y * nf + f].astype(F32)
                    for part in range(2):
                        for b in range(nb):
                            c0 = column_start(dims, part, b, f, y, half)
                            k0 = (part * nb + b) * half
                            wgu[0, :, c0 : c0 + half] = got[:, k0 : k0 + half]
    n1 = width // 128
    per = small.shape[0] // ns
    rows = small[pl.ds(pl.multiple_of(s * per, 8), per), :]
    for k in range(n1):
        g1[0:1, k * 128 : (k + 1) * 128] = rows[k : k + 1]
        g2[0:1, k * 128 : (k + 1) * 128] = rows[n1 + k : n1 + k + 1]
    for k in range(qkv // 128):
        bqkv[0:1, k * 128 : (k + 1) * 128] = rows[2 * n1 + k : 2 * n1 + k + 1]
    for out, pair, take in (
        (block_out, (out0, out1), take_out),
        (input_grad, (gh0, gh1), take_grad),
    ):
        for l in range(ns):
            @pl.when(s == l)
            def _():
                out[0, l] = pair[l][...].T
                out[0, 1 - l] = take[...].T.astype(F32)


def lay_out(dims, qkv, args):
    ns, nb, nf = dims
    gu, wd, qo = (args[0], args[2], args[3])
    width, rows = args[5].shape
    dr = qo.shape[1]
    sds = jax.ShapeDtypeStruct
    tokens = sds((1, ns, rows, width), F32)
    return pl.pallas_call(
        functools.partial(lay_out_kernel, dims),
        name="lay_out",
        out_shape=(
            tokens,
            tokens,
            sds((1, width), F32),
            sds((1, dr, qkv), F32),
            sds((1, qkv), F32),
            sds((1, dr, width), F32),
            sds((1, width), F32),
            sds((1, dr, gu.shape[0] * gu.shape[2]), F32),
            sds((1, ns * wd.shape[1], width), F32),
        ),
        in_specs=[VM] * len(args),
        out_specs=[VM] * 9,
        compiler_params=pltpu.CompilerParams(vmem_limit_bytes=VMEM_LIMIT),
    )(*args)


def shards(
    dims,
    tokens_in,
    positions,
    doc_ids,
    out_grad,
    norm1_gain,
    w_qkv,
    b_qkv,
    w_out,
    norm2_gain,
    w_gate_up,
    w_down,
):
    ns, nb, nf = dims
    seqs, rows, width = tokens_in.shape
    s = lax.axis_index("section")
    b = lax.axis_index("blk")
    dr = w_qkv.shape[1]
    qkv = w_qkv.shape[2]
    fr = w_down.shape[1]
    half = fr // ns
    ff = nb * half
    nk = min(nb, 1 + (LONGEST - 1 + rows - 1) // rows)

    tokens = lax.dynamic_index_in_dim(tokens_in, s, 0, keepdims=False)
    cot = lax.dynamic_index_in_dim(out_grad, s, 0, keepdims=False)
    pos = lax.dynamic_index_in_dim(positions, s, 0, keepdims=False)
    docs = lax.dynamic_index_in_dim(doc_ids, s, 0, keepdims=False).astype(F32)
    freq = jnp.exp(jnp.arange(HD // 2, dtype=F32) * (-2.0 / HD) * math.log(1000000.0))
    phase = freq[:, None] * pos.astype(F32)[None, :]
    cos_part, sin_part = (jnp.cos(phase), jnp.sin(phase))
    docs = docs.reshape(nb, rows)
    picked = (b - jnp.arange(nk) + nb) % nb
    meta = jnp.take(docs, picked, axis=0).reshape(nk * rows // 128, 128)
    query_docs = lax.dynamic_slice_in_dim(docs, b, 1)
    hidden = tokens.T.astype(F32)
    g = cot.T.astype(F32)

    wd = w_down[0].reshape(ns, half, width)
    small = jnp.concatenate([norm1_gain[0], norm2_gain[0], b_qkv[0]])
    total = -(-small.shape[0] // 1024) * 1024
    small = jnp.pad(small, (0, total - small.shape[0])).reshape(-1, 128)
    gup, wdp, gu_first, qo_first, qz, small_all = gather_weights(
        dims, w_gate_up, w_qkv, w_out, wd, small
    )
    cols = qkv + width
    wide = (width, 2 * ff)

    def ride(*pairs):
        return Riders(dims, tuple(a for a, _ in pairs), tuple(v for _, v in pairs))

    common = (small_all, meta, query_docs, cos_part, sin_part)
    qo0 = qo_first.reshape(width, cols)
    a0, (wd0, qo1) = attention_forward(
        dims, nk, 1, 0, hidden, *common, qo0, ride((("gather", 0), wdp)), "columns", qz
    )
    qo1 = qo1.reshape(width, cols)
    wd0 = wd0.reshape(ff, width)
    wgu0 = gu_first.reshape(wide)
    f0, (gu1,) = feed_forward(dims, 3, a0[6], a0[5], wgu0, wd0, ride((("gather", 1), gup)))
    wgu1 = gu1.reshape(wide)
    a1, (wd1, g_all) = attention_forward(
        dims, nk, 2, 1, f0[0], *common, qo1, ride((("gather", 1), wdp)), "lanes", cot.T
    )
    wd1 = wd1.reshape(ff, width)

    line_gu = (nb, nf, dr, 2 * ff)
    line_wd = (nb, half, width)
    line_qo = (nb, nf, dr, cols)
    everything = (0, half)
    cut = nf // 2
    b1 = feed_both(dims, 4, 1, a1[6], a1[5], g, g_all, wgu1, wd1, small_all)
    ab1, (dwd1, out1) = attention_backward(
        dims, nk, 7, 1, b1[0], *common, f0[0], *a1[:5], qo1,
        ride((("reduce", everything), b1[2].reshape(line_wd))), "sum", (b1[4], a1[5]),
    )
    b0, (dgu1,) = feed_backward(
        dims, 6, 0, ab1[0], a0[5], f0[1], f0[2], wgu0, wd0, small_all,
        ride((("reduce", (0, nf)), b1[1].reshape(line_gu))),
    )
    dgu0 = b0[1].reshape(line_gu)
    ab0, (dwd0, dgu0a, terms, gu_got1) = attention_backward(
        dims, nk, 8, 0, b0[0], *common, hidden, *a0[:5], qo0,
        ride((("reduce", everything), b0[2].reshape(line_wd)), (("reduce", (0, cut)), dgu0)),
        "columns", (ab1[1].reshape(line_qo), dgu1),
    )

    def swapped(values):
        give = jnp.where(s == 0, values[1], values[0]).astype(BF)
        return lax.ppermute(give, "section", [(0, 1), (1, 0)])

    take_out = swapped((f0[0], out1))
    take_grad = swapped((ab0[0], ab1[0]))
    grad_qo, small_sum, gu_got0, wd_got = reduce_gradients(
        dims, 9, cut, ab0[1].reshape(line_qo), terms,
        (ab0[2], ab1[2], b0[3], b1[3]), dwd1, dwd0, dgu0a, dgu0,
    )
    return lay_out(
        dims,
        qkv,
        (gu_got0, gu_got1, wd_got, grad_qo, small_sum, f0[0], out1, ab0[0], ab1[0], take_out,
         take_grad),
    )


def solution(mesh):
    dims = (mesh.shape["section"], mesh.shape["blk"], mesh.shape["fsdp"])
    return jax.shard_map(
        functools.partial(shards, dims),
        mesh=mesh,
        in_specs=(
            P("fsdp", "blk", None),
            P("fsdp", "blk"),
            P("fsdp", None),
            P("fsdp", "blk", None),
            P("section", None),
            P("section", ("blk", "fsdp"), None),
            P("section", None),
            P("section", ("blk", "fsdp"), None),
            P("section", None),
            P("section", ("blk", "fsdp"), None),
            P("section", ("blk", "fsdp"), None),
        ),
        out_specs=(
            P("section", "fsdp", "blk", None),
            P("section", "fsdp", "blk", None),
            P("section", None),
            P("section", ("blk", "fsdp"), None),
            P("section", None),
            P("section", ("blk", "fsdp"), None),
            P("section", None),
            P("section", ("blk", "fsdp"), None),
            P("section", ("blk", "fsdp"), None),
        ),
        check_vma=False,
    )
```

```python
import functools
import math

import jax
import jax.numpy as jnp
from jax import lax
from jax.experimental import pallas as pl
from jax.experimental.pallas import tpu as pltpu
from jax.sharding import PartitionSpec as P

H = 14
KVH = 2
HD = 64
GROUP = H // KVH
LONGEST = 512
NEG = -1e30
BF = jnp.bfloat16
F32 = jnp.float32
MESH = pl.DeviceIdType.MESH
VMEM_LIMIT = 60 * 2**20
VM = pl.BlockSpec(memory_space=pltpu.VMEM)
AN = pl.BlockSpec(memory_space=pl.ANY)


def nn(a, b):
    return lax.dot_general(a, b, (((1,), (0,)), ((), ())), preferred_element_type=F32)


def nt(a, b):
    return lax.dot_general(a, b, (((1,), (1,)), ((), ())), preferred_element_type=F32)


def tn(a, b):
    return lax.dot_general(a, b, (((0,), (0,)), ((), ())), preferred_element_type=F32)


def other(f):
    return f + 1 - 2 * (f % 2)


class Place:
    def __init__(self, dims):
        self.ns, self.nb, self.nf = dims
        self.count = self.ns * self.nf
        self.s = lax.axis_index("section")
        self.b = lax.axis_index("blk")
        self.f = lax.axis_index("fsdp")
        self.me = self.s * self.nf + self.f
        self.two_level = self.ns == 2 and self.nf == 4

    def plane(self, e):
        q = (self.me + e) % self.count
        return (q // self.nf, self.b, q % self.nf)

    def slot_from(self, e):
        return (self.me + self.count - e) % self.count

    def along(self, d):
        return (self.s, (self.b + d) % self.nb, self.f)

    def mates(self):
        s, b, f = (self.s, self.b, self.f)
        xf = (f + 2) % 4
        return ((s, b, other(f)), (s, b, xf), (1 - s, b, f))

    def slots(self):
        s, f = (self.s, self.f)
        xf = (f + 2) % 4
        t = 1 - s
        return (
            s * 4 + f,
            s * 4 + other(f),
            s * 4 + xf,
            t * 4 + f,
            s * 4 + other(xf),
            t * 4 + other(f),
            t * 4 + xf,
            t * 4 + other(xf),
        )


def pick(i, values):
    total = 0
    for k, v in enumerate(values):
        total = total + jnp.where(i == k, v, 0)
    return total


def greet(place, plane, along):
    barrier = pltpu.get_barrier_semaphore()
    count = 0
    if plane:
        if place.two_level and plane == "mates":
            targets = list(place.mates())
        else:
            targets = [place.plane(e) for e in range(1, place.count)]
        for t in targets:
            pl.semaphore_signal(barrier, 1, device_id=t, device_id_type=MESH)
        count += len(targets)
    if along:
        for d in range(1, place.nb):
            pl.semaphore_signal(barrier, 1, device_id=place.along(d), device_id_type=MESH)
        count += place.nb - 1
    pl.semaphore_wait(barrier, count)


def remote(src, dst, ssem, rsem, device):
    return pltpu.make_async_remote_copy(
        src_ref=src,
        dst_ref=dst,
        send_sem=ssem,
        recv_sem=rsem,
        device_id=device,
        device_id_type=MESH,
    )


def cut_in(parts, view, c):
    n = view.shape[0] // parts
    return view.at[pl.ds(c * n, n)]


def gather_sems(dims):
    n = 2 * (dims[0] * dims[2] - 1)
    return [pltpu.SemaphoreType.DMA((n,)), pltpu.SemaphoreType.DMA((n,))]


class PlaneGather:
    def __init__(self, place, slot, ssem, rsem):
        self.place, self.slot, self.ssem, self.rsem = (place, slot, ssem, rsem)
        self.parts = 2 if place.two_level else 1
        if place.two_level:
            self.order = place.slots()
        else:
            self.order = tuple(place.slot_from(e) for e in range(place.count))

    def copy(self, k, c, q, device):
        v = cut_in(self.parts, self.slot(q), c)
        i = k * self.parts + c
        return remote(v, v, self.ssem.at[i], self.rsem.at[i], device)

    def start(self):
        pc = self.place
        if pc.two_level:
            core, xm, ym = pc.mates()
            for c in range(2):
                self.copy(1, c, self.order[0], xm).start()
                self.copy(2, c, self.order[0], ym).start()
            for c in range(2):
                self.copy(0, c, self.order[0], core).start()
        else:
            for e in range(1, pc.count):
                self.copy(e - 1, 0, self.order[0], pc.plane(e)).start()

    def came(self, k, c):
        self.copy(k, c, self.order[k + 1], self.place.plane(1)).wait_recv()

    def before(self, step):
        if step == 0:
            return
        pc = self.place
        if not pc.two_level:
            self.came(step - 1, 0)
            return
        core, xm, ym = pc.mates()
        h = pc.f % 2
        if step == 2:
            which = h * self.order[3] + (1 - h) * self.order[2]
            far = (
                h * xm[0] + (1 - h) * ym[0],
                pc.b,
                h * xm[2] + (1 - h) * ym[2],
            )
            for c in range(2):
                self.came(1, c)
                self.came(2, c)
                self.copy(5, c, which, far).start()
                self.copy(3, c, self.order[2], core).start()
                self.copy(4, c, self.order[3], core).start()
        elif step == 3:
            return
        elif step == 6:
            for c in range(2):
                self.came(5, c)
                self.copy(6, c, self.order[6], core).start()
        else:
            for c in range(2):
                self.came(step - 1, c)

    def finish(self):
        n = self.place.count - 1
        for k in range(n):
            for c in range(self.parts):
                self.copy(k, c, self.order[0], self.place.plane(1)).wait_send()


class PlaneScatter:
    def __init__(self, place, near, away, back, hop, ssem, rsem):
        self.place = place
        self.near, self.away, self.back, self.hop = (near, away, back, hop)
        self.ssem, self.rsem = (ssem, rsem)

    def put(self, step, value):
        pc = self.place
        if not pc.two_level:
            @pl.when(step == 0)
            def _():
                self.near[0] = value

            @pl.when(step > 0)
            def _():
                e = pc.count - step
                self.away[e - 1] = value.astype(BF)
                q = (pc.me + e) % pc.count
                remote(
                    self.away.at[e - 1],
                    self.back.at[e - 1],
                    self.ssem.at[e - 1],
                    self.rsem.at[e - 1],
                    (q // pc.nf, pc.b, q % pc.nf),
                ).start()
            return
        core, xm, ym = pc.mates()
        here = (step == 0) | (step == 2) | (step == 3) | (step == 6)
        q = pick(step, (0, 0, 1, 2, 1, 2, 3, 3))

        @pl.when(here)
        def _():
            self.near[q] = value

        @pl.when(jnp.logical_not(here))
        def _():
            self.away[q] = value.astype(BF)
            self.core_copy(q).start()

    def core_copy(self, q):
        core = self.place.mates()[0]
        return remote(self.away.at[q], self.back.at[q], self.ssem.at[q], self.rsem.at[q], core)

    def far_copy(self, e):
        return remote(self.away.at[e - 1], self.back.at[e - 1], self.ssem.at[e - 1],
                      self.rsem.at[e - 1], self.place.plane(e))

    def hop_copy(self, k, c, device):
        i = 4 + 2 * k + c
        return remote(
            cut_in(2, self.hop.at[k], c),
            cut_in(2, self.hop.at[k + 3], c),
            self.ssem.at[i],
            self.rsem.at[i],
            device,
        )

    def rows(self, c):
        n = self.hop.shape[1] // 2
        return slice(c * n, (c + 1) * n)

    def targets(self):
        pc = self.place
        core, xm, ym = pc.mates()
        c = pc.f % 2
        first = (c * xm[0] + (1 - c) * ym[0], pc.b, c * xm[2] + (1 - c) * ym[2])
        second = (c * ym[0] + (1 - c) * xm[0], pc.b, c * ym[2] + (1 - c) * xm[2])
        return (first, second)

    def early(self):
        pc = self.place
        if not pc.two_level:
            return
        c = pc.f % 2
        first, second = self.targets()
        self.core_copy(1).wait_recv()
        self.core_copy(2).wait_recv()
        q = c * 1 + (1 - c) * 2
        for k in range(2):
            r = self.rows(k)
            self.hop[0, r] = (self.mine(q, r) + self.back[q, r].astype(F32)).astype(BF)
            self.hop_copy(0, k, first).start()

    def diagonal(self):
        pc = self.place
        if not pc.two_level:
            return
        first, second = self.targets()
        self.core_copy(3).wait_recv()
        for k in range(2):
            r = self.rows(k)
            self.hop[1, r] = (self.mine(3, r) + self.back[3, r].astype(F32)).astype(BF)
            self.hop_copy(1, k, first).start()

    def mine(self, q, r=slice(None)):
        return self.near[q, r]

    def result(self, store):
        self.late()
        self.finish(store)

    def late(self):
        pc = self.place
        if not pc.two_level:
            return
        c = pc.f % 2
        first, second = self.targets()
        q = c * 2 + (1 - c) * 1
        for k in range(2):
            r = self.rows(k)
            self.hop_copy(1, k, first).wait_recv()
            self.hop[2, r] = (
                self.mine(q, r) + self.back[q, r].astype(F32) + self.hop[4, r].astype(F32)
            ).astype(BF)
            self.hop_copy(2, k, second).start()

    def finish(self, store):
        pc = self.place
        if not pc.two_level:
            total = self.mine(0)
            for e in range(1, pc.count):
                self.far_copy(e).wait()
                total = total + self.back[e - 1].astype(F32)
            store(total)
            return
        first, second = self.targets()
        self.core_copy(0).wait_recv()
        for k in range(2):
            self.hop_copy(0, k, first).wait_recv()
            self.hop_copy(2, k, second).wait_recv()
        store(
            self.mine(0)
            + self.back[0].astype(F32)
            + self.hop[3].astype(F32)
            + self.hop[5].astype(F32)
        )
        for q in range(4):
            self.core_copy(q).wait_send()
        for k in range(2):
            self.hop_copy(0, k, first).wait_send()
            self.hop_copy(1, k, first).wait_send()
            self.hop_copy(2, k, second).wait_send()


class ReadyScatter(PlaneScatter):
    def __init__(self, place, part, back, hop, ssem, rsem):
        super().__init__(place, None, None, back, hop, ssem, rsem)
        self.part = part
        if place.two_level:
            o = place.slots()
            self.here = (o[0], o[2], o[3], o[6])
            self.gone = (o[1], o[4], o[5], o[7])

    def mine(self, q, r=slice(None)):
        if not self.place.two_level:
            return self.part(self.place.me)[...].astype(F32)
        return self.part(pick(q, self.here))[r].astype(F32)

    def core_copy(self, q):
        core = self.place.mates()[0]
        v = self.part(self.gone[q])
        return remote(v, self.back.at[q], self.ssem.at[q], self.rsem.at[q], core)

    def far_copy(self, e):
        pc = self.place
        v = self.part((pc.me + e) % pc.count)
        return remote(v, self.back.at[e - 1], self.ssem.at[e - 1], self.rsem.at[e - 1],
                      pc.plane(e))

    def start(self):
        pc = self.place
        if pc.two_level:
            for q in (3, 2, 1, 0):
                self.core_copy(q).start()
        else:
            for e in range(1, pc.count):
                self.far_copy(e).start()


class RowSends:
    def __init__(self, place, layer, out, sems):
        self.place, self.layer, self.out = (place, layer, out)
        self.lsem, self.ss, self.sr = sems

    def copies(self, f, src):
        pc = self.place
        e = (self.layer * pc.nf + f - pc.me + pc.count) % pc.count
        own = self.out.at[pc.me]
        k = (e + pc.count - 1) % pc.count
        away = remote(src, own, self.ss.at[f], self.sr.at[k], (self.layer, pc.b, f))
        return (e, away, pltpu.make_async_copy(src, own, self.lsem))

    def start(self, f, src):
        e, away, local = self.copies(f, src)

        @pl.when(e != 0)
        def _():
            away.start()

        @pl.when(e == 0)
        def _():
            local.start()

    def finish(self, src):
        pc = self.place
        for f in range(pc.nf):
            e, away, local = self.copies(f, src)

            @pl.when(e != 0)
            def _():
                away.wait_send()

            @pl.when(e == 0)
            def _():
                local.wait()

        @pl.when(pc.s == self.layer)
        def _():
            for e in range(1, pc.count):
                q = pc.slot_from(e)
                remote(src, self.out.at[q], self.ss.at[0], self.sr.at[e - 1], pc.plane(e)).wait_recv()


def row_scratch(dims):
    dma = pltpu.SemaphoreType.DMA
    return [dma(()), dma((dims[2],)), dma((dims[0] * dims[2],))]


class LineGather:
    def __init__(self, place, piece, out, sems, part=None):
        self.place, self.piece = (place, piece)
        self.view = lambda t: out.at[t] if part is None else out.at[t, part]
        self.lsem, self.ss, self.sr = sems
        self.k = 0

    def local(self):
        return pltpu.make_async_copy(self.piece, self.view(self.place.b), self.lsem)

    def hop(self, way, k, came):
        pc = self.place
        t = pc.b - way * (k - (0 if came else 1))
        src = self.piece if k == 1 and not came else self.view(t)
        i = k - 1 + (0 if way == 1 else pc.nb - 1)
        return remote(
            src, self.view(t), self.ss.at[i], self.sr.at[i], (pc.s, pc.b + way, pc.f)
        )

    def sends(self, way, k):
        b, nb = (self.place.b, self.place.nb)
        return (b >= k - 1) & (b < nb - 1) if way == 1 else (b <= nb - k) & (b > 0)

    def comes(self, way, k):
        b, nb = (self.place.b, self.place.nb)
        return b >= k if way == 1 else b <= nb - 1 - k

    def arrived(self, k):
        for way in (1, -1):
            @pl.when(self.comes(way, k))
            def _():
                self.hop(way, k, True).wait_recv()

    def start(self):
        self.local().start()
        self.service()

    def service(self):
        if self.k == self.place.nb - 1:
            return
        self.k += 1
        if self.k > 1:
            self.arrived(self.k - 1)
        for way in (1, -1):
            @pl.when(self.sends(way, self.k))
            def _():
                self.hop(way, self.k, False).start()

    def finish(self):
        last = self.place.nb - 1
        while self.k < last:
            self.service()
        self.arrived(last)
        for k in range(1, last + 1):
            for way in (1, -1):
                @pl.when(self.sends(way, k))
                def _():
                    self.hop(way, k, False).wait_send()
        self.local().wait()


class LineReduce:
    def __init__(self, place, terms, store, sems, load=None):
        self.place, self.terms, self.store, self.load = (place, terms, store, load)
        self.out, self.came, self.ss, self.sr = sems
        self.k = 0

    def index(self, way, k):
        return k - 1 + (0 if way == 1 else self.place.nb - 1)

    def hop(self, way, k):
        pc = self.place
        i = self.index(way, k)
        return remote(
            self.out.at[i], self.came.at[i], self.ss.at[i], self.sr.at[i],
            (pc.s, pc.b + way, pc.f),
        )

    def rank(self, way):
        pc = self.place
        return pc.b if way == 1 else pc.nb - 1 - pc.b

    def sends(self, way, k):
        r = self.rank(way)
        return (r < k) & (r < self.place.nb - 1)

    def start(self):
        if self.load is not None:
            self.load.wait()
        self.service()

    def service(self):
        nb = self.place.nb
        if self.k == nb - 1:
            return
        self.k += 1
        k = self.k
        for way in (1, -1):
            r = self.rank(way)
            t = nb - k + r if way == 1 else k - 1 - r
            i = self.index(way, k)

            @pl.when(self.sends(way, k) & (r == 0))
            def _():
                self.out[i] = self.terms(t)

            if k > 1:
                @pl.when(self.sends(way, k) & (r > 0))
                def _():
                    self.hop(way, k - 1).wait_recv()
                    total = self.terms(t).astype(F32) + self.came[i - 1].astype(F32)
                    self.out[i] = total.astype(BF)

            @pl.when(self.sends(way, k))
            def _():
                self.hop(way, k).start()

    def finish(self):
        pc = self.place
        last = pc.nb - 1
        while self.k < last:
            self.service()
        right, left = (self.index(1, last), self.index(-1, last))

        @pl.when(pc.b == 0)
        def _():
            self.hop(-1, last).wait_recv()
            self.store(self.terms(pc.b).astype(F32) + self.came[left].astype(F32))

        @pl.when(pc.b == last)
        def _():
            self.hop(1, last).wait_recv()
            self.store(self.terms(pc.b).astype(F32) + self.came[right].astype(F32))

        @pl.when((pc.b > 0) & (pc.b < last))
        def _():
            self.hop(1, last).wait_recv()
            self.hop(-1, last).wait_recv()
            self.store(
                self.terms(pc.b).astype(F32)
                + self.came[right].astype(F32)
                + self.came[left].astype(F32)
            )

        for k in range(1, last + 1):
            for way in (1, -1):
                @pl.when(self.sends(way, k))
                def _():
                    self.hop(way, k).wait_send()


def gather_scratch(dims):
    dma = pltpu.SemaphoreType.DMA
    return [dma(()), dma((2 * (dims[1] - 1),)), dma((2 * (dims[1] - 1),))]


def reduce_scratch(dims, *block):
    dma = pltpu.SemaphoreType.DMA
    n = 2 * (dims[1] - 1)
    return [pltpu.VMEM((n,) + block, BF), pltpu.VMEM((n,) + block, BF), dma((n,)), dma((n,))]


class Riders:
    def __init__(self, dims, specs, arrays):
        self.dims, self.specs, self.arrays = (dims, specs, arrays)
        self.shapes = []
        self.places = [AN] * len(specs)
        self.outs = []
        self.scratch = []
        self.sizes = []
        for spec, a in zip(specs, arrays):
            if spec[0] == "gather":
                shape = (dims[1],) + a.shape[1:]
                scratch = gather_scratch(dims)
            else:
                lo, hi = spec[1]
                shape = (hi - lo,) + a.shape[2:]
                scratch = reduce_scratch(dims, *shape)
                scratch += [
                    pltpu.VMEM((dims[1],) + shape, BF), pltpu.SemaphoreType.DMA(())
                ]
            self.outs.append(AN if spec[0] == "gather" else VM)
            self.shapes.append(jax.ShapeDtypeStruct(shape, a.dtype))
            self.scratch += scratch
            self.sizes.append(len(scratch))
        self.count = len(specs)

    def board(self, place, ins, outs, scratch):
        out = []
        for spec, size, a, o in zip(self.specs, self.sizes, ins, outs):
            mine, scratch = (scratch[:size], scratch[size:])
            if spec[0] == "gather":
                out.append(LineGather(place, a.at[spec[1]], o, mine))
            else:
                lo, hi = spec[1]

                def store(value, o=o):
                    o[...] = value.astype(BF)

                terms, sem = mine[4:]
                load = pltpu.make_async_copy(a.at[:, lo:hi], terms, sem)
                load.start()
                out.append(
                    LineReduce(place, lambda t, r=terms: r[t], store, mine[:4], load)
                )
        return (out, scratch)


def each(riders, what):
    for r in riders:
        getattr(r, what)()


def scatter_scratch(dims, *block):
    count = dims[0] * dims[2]
    if dims[0] == 2 and dims[2] == 4:
        near, away, hops, sems = (4, 4, 6, 10)
    else:
        near, away, hops, sems = (1, count - 1, 1, count - 1)
    return [
        pltpu.VMEM((near,) + block, F32),
        pltpu.VMEM((away,) + block, BF),
        pltpu.VMEM((away,) + block, BF),
        pltpu.VMEM((hops,) + block, BF),
        pltpu.SemaphoreType.DMA((sems,)),
        pltpu.SemaphoreType.DMA((sems,)),
    ]


def call(kernel, name, cid, outs, out_specs, in_specs, scratch, args):
    params = pltpu.CompilerParams(
        collective_id=cid, has_side_effects=True, vmem_limit_bytes=VMEM_LIMIT
    )
    return pl.pallas_call(
        kernel,
        name=name,
        out_shape=outs,
        in_specs=in_specs,
        out_specs=out_specs,
        scratch_shapes=scratch,
        compiler_params=params,
    )(*args)


def column_start(dims, part, b, f, y, half):
    ns, nb, nf = dims
    return part * nb * nf * ns * half + ((b * nf + f) * ns + y) * half


def columns_of(ref, q, nf, wide):
    return ref.at[:, q % nf, :, pl.ds(pl.multiple_of((q // nf) * wide, wide), wide)]


def gather_weights_kernel(
    dims, w_ref, wq_ref, wo_ref, wd, small, gup, wdp, gu_first, qo_first, qz, small_all,
    pack, qcol, qh, lsem, ps, pr, ms, mr, qs, qr, *rest
):
    pc = Place(dims)
    ns, nb, nf = dims
    half = wd.shape[1]
    wide = qh.shape[2]
    greet(pc, "all", True)
    qkv = wq_ref.shape[2]
    full = jnp.concatenate([wq_ref[0], wo_ref[0]], axis=1)
    for y in range(ns):
        qcol[y] = full[:, y * wide : (y + 1) * wide]
    across = []
    for d in range(1, ns):
        y = (pc.s + d) % ns
        t = (y, pc.b, pc.f)
        i = 3 * (d - 1)
        across.append(remote(qcol.at[y], qh.at[pc.s], ms.at[i], mr.at[i], t))
        across.append(remote(wd.at[y], wdp.at[pc.s], ms.at[i + 1], mr.at[i + 1], t))
        across.append(remote(small, small_all.at[pc.s], ms.at[i + 2], mr.at[i + 2], t))
    for c in across:
        c.start()
    qh[pc.s] = qcol[pc.s]
    local = [
        pltpu.make_async_copy(wd.at[pc.s], wdp.at[pc.s], lsem.at[0]),
        pltpu.make_async_copy(small, small_all.at[pc.s], lsem.at[1]),
    ]
    for c in local:
        c.start()
    own = pltpu.make_async_copy(pack.at[pc.s, pc.f], gup.at[pc.s, pc.f], lsem.at[2])

    def piece(y, f):
        e = (y * nf + f - pc.me + pc.count) % pc.count
        k = (e + pc.count - 1) % pc.count
        return (
            e,
            remote(pack.at[y, f], gup.at[pc.s, pc.f], ps.at[k], pr.at[k], (y, pc.b, f)),
        )

    for f in range(nf):
        for y in range(ns):
            pieces = []
            for part in range(2):
                for b in range(nb):
                    c0 = column_start(dims, part, b, f, y, half)
                    pieces.append(w_ref[0, :, c0 : c0 + half])
            pack[y, f] = jnp.concatenate(pieces, axis=1)
            e, c = piece(y, f)

            @pl.when(e != 0)
            def _():
                c.start()

    own.start()
    for d in range(ns - 1):
        across[3 * d].wait()
    line_q = LineGather(pc, qh, qz, rest[0:3])
    lines = [
        LineGather(pc, gup.at[0, f], gu_first, rest[3 + 3 * f : 6 + 3 * f], f) for f in range(nf)
    ]
    line_q.start()

    def arrived(y, f):
        e, c = piece(y, f)
        k = (2 * pc.count - e - 1) % pc.count

        @pl.when(e != 0)
        def _():
            remote(pack.at[0, 0], gup.at[y, f], ps.at[k], pr.at[k], (y, pc.b, f)).wait_recv()

    own.wait()
    line_q.service()
    for f in range(nf):
        arrived(0, f)
        lines[f].start()
    line_q.service()
    for line in lines:
        line.service()
    line_q.finish()
    gather = PlaneGather(pc, lambda q: columns_of(qo_first, q, nf, wide), qs, qr)
    columns_of(qo_first, pc.me, nf, wide)[...] = qz[:, 0]
    gather.start()
    for step in range(1, min(6, pc.count)):
        gather.before(step)
    for line in lines:
        line.service()
    for step in range(min(6, pc.count), pc.count):
        gather.before(step)
    gather.finish()
    for y in range(1, ns):
        for f in range(nf):
            arrived(y, f)
    for y in range(ns):
        for f in range(nf):
            e, c = piece(y, f)

            @pl.when(e != 0)
            def _():
                c.wait_send()

    for c in local:
        c.wait()
    for i, c in enumerate(across):
        if i % 3:
            c.wait()
    for line in lines:
        line.finish()


def gather_weights(dims, w, wq, wo, wd, small):
    ns, nb, nf = dims
    count = ns * nf
    half, width = wd.shape[1:]
    dr = wq.shape[1]
    cols = wq.shape[2] + wo.shape[2]
    wide = cols // ns
    two_ff = 2 * nb * half
    sds = jax.ShapeDtypeStruct
    outs = (
        sds((ns, nf, dr, two_ff), BF),
        sds((ns, half, width), BF),
        sds((nb, nf, dr, two_ff), BF),
        sds((nb, nf, dr, cols), BF),
        sds((nb, ns, dr, wide), BF),
        sds((ns,) + small.shape, F32),
    )
    dma = pltpu.SemaphoreType.DMA
    return call(
        functools.partial(gather_weights_kernel, dims),
        "gather_weights",
        0,
        outs,
        [AN, AN, AN, VM, VM, AN],
        [VM, VM, VM, AN, AN],
        [
            pltpu.VMEM((ns, nf, dr, two_ff), BF),
            pltpu.VMEM((ns, dr, wide), BF),
            pltpu.VMEM((ns, dr, wide), BF),
            dma((4,)),
            dma((count,)),
            dma((count,)),
            dma((3 * (ns - 1),)),
            dma((3 * (ns - 1),)),
        ]
        + gather_sems(dims)
        + gather_scratch(dims) * (1 + nf),
        (w, wq, wo, wd, small),
    )


def rms(values):
    return lax.rsqrt(jnp.mean(values * values, axis=0, keepdims=True) + 1e-06)


def column(rows_t, first, count):
    return jnp.concatenate([rows_t[:, k : k + 1] for k in range(first, first + count)], axis=0)


def rows_of(values):
    v = folded(values)
    return jnp.concatenate(
        [v[k : k + 128].T.sum(axis=0, keepdims=True) for k in range(0, v.shape[0], 128)], axis=0
    )


def folded(v):
    out = v[:, :128]
    for k in range(1, v.shape[1] // 128):
        out = out + v[:, k * 128 : (k + 1) * 128]
    return out


def fill_masks(pc, mask, meta_t, query_docs):
    nk, rows = mask.shape[:2]
    key_i = lax.broadcasted_iota(jnp.int32, (rows, rows), 0)
    query_i = lax.broadcasted_iota(jnp.int32, (rows, rows), 1)
    per = rows // 128
    for j in range(nk):
        same = column(meta_t, j * per, per) == query_docs
        if j == 0:
            live = same & (key_i <= query_i)
        else:
            live = same & (key_i < (pc.b - j + 1) * rows)
        mask[j] = jnp.where(live, 0.0, NEG)


def load_qo(qo, w, wo, sems):
    cols = w.shape[1]
    c1 = pltpu.make_async_copy(qo.at[:, 0:cols], w, sems.at[0])
    c2 = pltpu.make_async_copy(qo.at[:, cols : cols + wo.shape[1]], wo, sems.at[1])
    c1.start()
    c2.start()
    return (c1, c2)


def gains_of(small_t, width, qkv):
    n = width // 128
    return (
        column(small_t, 0, n),
        column(small_t, n, n),
        column(small_t, 2 * n, qkv // 128),
    )


def padded_t(v):
    n = v.shape[0]
    return jnp.concatenate([v, jnp.zeros((128 - n, 128), v.dtype)], axis=0).T


def attention_forward_kernel(
    dims, nk, layer, plan, carry, h_ref, small_ref, meta_ref, docs_ref, cos_ref, sin_ref, qo_all,
    *refs
):
    n = plan.count
    if carry:
        block_ref, refs = (refs[0], refs[1:])
    ins, refs = (refs[:n], refs[n:])
    normed_ref, q_ref, kv_ref, lse_ref, mixed_ref, res_ref, n2_ref = refs[:7]
    outs, refs = (refs[7 : 7 + n], refs[7 + n :])
    if carry:
        block_all, refs = (refs[0], refs[1:])
    w, wo, mask, joined, top_own, sum_own, out_own, ssem, rsem, qsem = refs[:10]
    refs = refs[10:]
    pc = Place(dims)
    width, rows = h_ref.shape
    loads = load_qo(qo_all, w, wo, qsem)
    greet(pc, "mates" if carry else None, True)
    riders, refs = plan.board(pc, ins, outs, refs)
    if carry == "lanes":
        own = block_ref
        slot = lambda q: block_all.at[:, lanes(q, rows)]
    elif carry == "columns":
        own = block_ref.at[:, 1]
        slot = lambda q: columns_of(block_all, q, pc.nf, block_ref.shape[3])
    gather = None
    if carry:
        gather = PlaneGather(pc, slot, *refs)
        slot(pc.me)[...] = own[...]
        gather.start()
    each(riders, "start")
    g1, g2, bias = gains_of(padded_t(small_ref[layer]), width, w.shape[1])
    hidden = h_ref[...].astype(BF).astype(F32)
    normed = (hidden * rms(hidden) * g1).astype(BF)
    normed_ref[...] = normed
    fill_masks(pc, mask, padded_t(meta_ref[...]), docs_ref[...])
    loads[0].wait()
    joined[...] = tn(w[...], normed) + bias
    cos_part = cos_ref[...]
    sin_part = sin_ref[...]
    half = HD // 2

    def turned(row):
        u1 = joined[pl.ds(row, half), :]
        u2 = joined[pl.ds(row + half, half), :]
        return (u1 * cos_part - u2 * sin_part, u2 * cos_part + u1 * sin_part)

    for g in range(KVH):
        r1, r2 = turned((H + g) * HD)
        kv_ref[0, g, :half, :] = r1.astype(BF)
        kv_ref[0, g, half:, :] = r2.astype(BF)
        v0 = (H + KVH + g) * HD
        kv_ref[0, KVH + g] = joined[v0 : v0 + HD, :].astype(BF)
    sends = [
        remote(kv_ref.at[0], kv_ref.at[j], ssem.at[j - 1], rsem.at[j - 1], pc.along(j))
        for j in range(1, nk)
    ]
    for c in sends:
        c.start()
    scale = HD**-0.5
    for head in range(H):
        r1, r2 = turned(head * HD)
        q_ref[head, :half, :] = (r1 * scale).astype(BF)
        q_ref[head, half:, :] = (r2 * scale).astype(BF)
    for g in range(KVH):
        keys = kv_ref[0, g].T
        values = kv_ref[0, KVH + g]

        def own_keys(i, carried):
            head = g * GROUP + i
            x = nn(keys, q_ref[head]) + mask[0]
            top = x.max(axis=0, keepdims=True)
            e = jnp.exp(x - top)
            top_own[head] = top
            sum_own[head] = e.sum(axis=0, keepdims=True)
            out_own[head] = nn(values, e.astype(BF))
            return carried

        lax.fori_loop(0, GROUP, own_keys, 0)
    for c in sends:
        c.wait()
    each(riders, "service")
    for g in range(KVH):
        keys = [kv_ref[j, g].T for j in range(1, nk)]
        values = [kv_ref[j, KVH + g] for j in range(1, nk)]

        def one_head(i, carried):
            head = g * GROUP + i
            q = q_ref[head]
            s = [nn(keys[j], q) + mask[j + 1] for j in range(nk - 1)]
            first = top_own[head]
            top = first
            for x in s:
                top = jnp.maximum(top, x.max(axis=0, keepdims=True))
            e = [jnp.exp(x - top) for x in s]
            fade = jnp.exp(first - top)
            total = sum_own[head] * fade
            out = out_own[head] * fade
            for j in range(nk - 1):
                total = total + e[j].sum(axis=0, keepdims=True)
                out = out + nn(values[j], e[j].astype(BF))
            lse_ref[head] = top + jnp.log(total)
            mixed_ref[head] = (out / total).astype(BF)
            return carried

        lax.fori_loop(0, GROUP, one_head, 0)
        if g == 0:
            for step in range(1, min(6, pc.count)):
                gather.before(step)
        else:
            each(riders, "service")
    mixed = mixed_ref[...].reshape(H * HD, rows)
    loads[1].wait()
    residual = hidden + tn(wo[...], mixed)
    res_ref[...] = residual
    n2_ref[...] = (residual * rms(residual) * g2).astype(BF)
    if carry:
        for step in range(min(6, pc.count), pc.count):
            gather.before(step)
        gather.finish()
    each(riders, "finish")


def attention_forward(dims, nk, cid, layer, hidden, small, meta, docs, cos_part, sin_part, qo_all,
                      plan, carry, block):
    width, rows = hidden.shape
    ns, nb, nf = dims
    count = ns * nf
    qkv = qo_all.shape[1] - width
    sds = jax.ShapeDtypeStruct
    outs = [
        sds((width, rows), BF),
        sds((H, HD, rows), BF),
        sds((nk, 2 * KVH, HD, rows), BF),
        sds((H, 1, rows), F32),
        sds((H, HD, rows), BF),
        sds((width, rows), F32),
        sds((width, rows), BF),
    ] + plan.shapes
    dma = pltpu.SemaphoreType.DMA
    if carry == "lanes":
        outs.append(sds((width, count * rows), BF))
    else:
        outs.append(sds((nb, nf, block.shape[2], ns * block.shape[3]), BF))
    out = call(
        functools.partial(attention_forward_kernel, dims, nk, layer, plan, carry),
        "attention_forward",
        cid,
        tuple(outs),
        [VM] * 7 + plan.outs + [VM],
        [VM] * 6 + [AN, VM] + plan.places,
        [
            pltpu.VMEM((width, qkv), BF),
            pltpu.VMEM((width, width), BF),
            pltpu.VMEM((nk, rows, rows), F32),
            pltpu.VMEM((qkv, rows), F32),
            pltpu.VMEM((H, 1, rows), F32),
            pltpu.VMEM((H, 1, rows), F32),
            pltpu.VMEM((H, HD, rows), F32),
            dma((nk - 1,)),
            dma((nk - 1,)),
            dma((2,)),
        ]
        + plan.scratch
        + gather_sems(dims),
        (hidden, small, meta, docs, cos_part, sin_part, qo_all, block, *plan.arrays),
    )
    return (out[:7], out[7:])


def attention_backward_kernel(
    dims, nk, layer, plan, carry, g_ref, small_ref, meta_ref, docs_ref, cos_ref, sin_ref,
    h_ref, normed_ref, q_ref, kv_ref, lse_ref, mixed_ref, qo_all, *refs
):
    n = plan.count
    parts_ref, more_ref, refs = (refs[0], refs[1], refs[2:])
    ins, refs = (refs[:n], refs[n:])
    gh_ref, dqo_ref, dsmall_ref = refs[:3]
    outs, refs = (refs[3 : 3 + n], refs[3 + n :])
    out_ref, refs = (refs[0], refs[1:])
    if carry == "columns":
        rows_ref, refs = (refs[0], refs[1:])
    w, wo, mask, dmix, dkv, delta, dq_some, out_kv, in_kv, gj, ssem, rsem, qsem = refs[:13]
    refs = refs[13:]
    pc = Place(dims)
    width, rows = h_ref.shape
    qkv = w.shape[1]
    loads = load_qo(qo_all, w, wo, qsem)
    riders, refs = plan.board(pc, ins, outs, refs)
    if carry == "columns":
        held, held_sem = refs[7:]
        coming = pltpu.make_async_copy(parts_ref, held, held_sem)
        coming.start()
    greet(pc, "all" if carry == "columns" else "mates", True)
    if carry == "columns":
        part = lambda q: columns_of(held, q, pc.nf, out_ref.shape[2])
        hand_out = RowSends(pc, 1, rows_ref, refs[4:7])
        coming.wait()
    else:
        part = lambda q: parts_ref.at[q]
    scatter = ReadyScatter(pc, part, *refs[:4])
    scatter.start()
    each(riders, "start")
    g1 = column(padded_t(small_ref[layer]), 0, width // 128)
    fill_masks(pc, mask, padded_t(meta_ref[...]), docs_ref[...])
    grl = g_ref[...].astype(BF)
    loads[1].wait()
    dmix[...] = nn(wo[...], grl).astype(BF).reshape(dmix.shape)
    dqo_ref[:, qkv:] = nt(mixed_ref[...].reshape(H * HD, rows), grl).astype(BF)
    scatter.diagonal()
    scatter.early()
    if carry == "columns":
        for f in range(pc.nf):
            hand_out.start(f, more_ref.at[f])
    cos_part = cos_ref[...]
    sin_part = sin_ref[...]
    half = HD // 2
    scale = HD**-0.5
    dkv[...] = jnp.zeros_like(dkv)

    def unturned(d1, d2):
        return (d1 * cos_part + d2 * sin_part, d2 * cos_part - d1 * sin_part)

    def of_block(j, g, head, keys, keys_t, values):
        q = q_ref[head]
        do = dmix[head]
        p = jnp.exp(nn(keys, q) + mask[j] - lse_ref[head])
        ds = (p * (nn(values, do) - delta[head])).astype(BF)
        dkv[j, g] += nt(q, ds)
        dkv[j, KVH + g] += nt(do, p.astype(BF))
        return nn(keys_t, ds)

    for g in range(KVH):
        keys_t = [kv_ref[j, g] for j in range(1, nk)]
        keys = [k.T for k in keys_t]
        values = [kv_ref[j, KVH + g].T for j in range(1, nk)]

        def earlier(i, carried):
            head = g * GROUP + i
            delta[head] = (dmix[head].astype(F32) * mixed_ref[head].astype(F32)).sum(
                axis=0, keepdims=True
            )
            dq = of_block(1, g, head, keys[0], keys_t[0], values[0])
            for j in range(2, nk):
                dq = dq + of_block(j, g, head, keys[j - 1], keys_t[j - 1], values[j - 1])
            dq_some[head] = dq
            return carried

        lax.fori_loop(0, GROUP, earlier, 0)
        if g == 0:
            scatter.late()
        if g == 1 or carry == "sum":
            each(riders, "service")
    for j in range(1, nk):
        out_kv[j - 1] = dkv[j].astype(BF)
    sends = [
        remote(out_kv.at[j - 1], in_kv.at[j - 1], ssem.at[j - 1], rsem.at[j - 1],
               pc.along(pc.nb - j))
        for j in range(1, nk)
    ]
    for c in sends:
        c.start()
    for g in range(KVH):
        keys_t = kv_ref[0, g]
        keys = keys_t.T
        values = kv_ref[0, KVH + g].T

        def own_keys(i, carried):
            head = g * GROUP + i
            dq = (dq_some[head] + of_block(0, g, head, keys, keys_t, values)) * scale
            r1, r2 = unturned(dq[:half], dq[half:])
            gj[pl.ds(pl.multiple_of(head * HD, HD), half), :] = r1.astype(BF)
            gj[pl.ds(pl.multiple_of(head * HD + half, half), half), :] = r2.astype(BF)
            return carried

        lax.fori_loop(0, GROUP, own_keys, 0)
    for c in sends:
        c.wait()
    each(riders, "service")
    own = dkv[0]
    for j in range(1, nk):
        own = own + in_kv[j - 1].astype(F32)
    for g in range(KVH):
        r1, r2 = unturned(own[g, :half], own[g, half:])
        k0 = (H + g) * HD
        gj[k0 : k0 + half, :] = r1.astype(BF)
        gj[k0 + half : k0 + HD, :] = r2.astype(BF)
        v0 = (H + KVH + g) * HD
        gj[v0 : v0 + HD, :] = own[KVH + g].astype(BF)
    gjv = gj[...]
    n1 = width // 128
    dsmall_ref[n1 : n1 + qkv // 128, :] = rows_of(gjv.astype(F32))
    loads[0].wait()
    dqo_ref[:, :qkv] = nt(normed_ref[...], gjv).astype(BF)
    gn = nn(w[...], gjv)
    hidden = h_ref[...].astype(BF).astype(F32)
    scale_one = rms(hidden)
    unit = hidden * scale_one
    dsmall_ref[:n1, :] = rows_of(gn * unit)
    u = gn * g1
    gh_ref[...] = g_ref[...] + scale_one * (u - unit * jnp.mean(u * unit, axis=0, keepdims=True))

    def store(total):
        if carry == "columns":
            out_ref[...] = total.astype(BF)
        else:
            out_ref[...] = more_ref[...] + total

    scatter.finish(store)
    if carry == "columns":
        hand_out.finish(more_ref.at[0])
    each(riders, "finish")


def attention_backward(dims, nk, cid, layer, g, small, meta, docs, cos_part, sin_part, hidden,
                       normed, q, kv, lse, mixed, qo_all, plan, carry, late):
    width, rows = hidden.shape
    qkv = qo_all.shape[1] - width
    sds = jax.ShapeDtypeStruct
    outs = [
        sds((width, rows), F32),
        sds((width, qkv + width), BF),
        sds(((width + qkv) // 128, 128), F32),
    ] + plan.shapes
    dma = pltpu.SemaphoreType.DMA
    block = (2 * KVH, HD, rows)
    if carry == "columns":
        summed = (dims[1], late[0].shape[2], late[0].shape[3] // dims[0])
        outs += [sds(summed, BF), sds((dims[0] * dims[2],) + late[1].shape[1:], BF)]
        places = [VM, AN]
    else:
        summed = (width, rows)
        outs.append(sds(summed, F32))
        places = [VM]
    out = call(
        functools.partial(attention_backward_kernel, dims, nk, layer, plan, carry),
        "attention_backward",
        cid,
        tuple(outs),
        [VM] * 3 + plan.outs + places,
        [VM] * 12 + [AN] + [AN if carry == "columns" else VM, VM] + plan.places,
        [
            pltpu.VMEM((width, qkv), BF),
            pltpu.VMEM((width, width), BF),
            pltpu.VMEM((nk, rows, rows), F32),
            pltpu.VMEM((H, HD, rows), BF),
            pltpu.VMEM((nk,) + block, F32),
            pltpu.VMEM((H, 1, rows), F32),
            pltpu.VMEM((H, HD, rows), F32),
            pltpu.VMEM((nk - 1,) + block, BF),
            pltpu.VMEM((nk - 1,) + block, BF),
            pltpu.VMEM((qkv, rows), BF),
            dma((nk - 1,)),
            dma((nk - 1,)),
            dma((2,)),
        ]
        + plan.scratch
        + scatter_scratch(dims, *summed)[2:]
        + (
            row_scratch(dims) + [pltpu.VMEM(late[0].shape, BF), dma(())]
            if carry == "columns"
            else []
        ),
        (g, small, meta, docs, cos_part, sin_part, hidden, normed, q, kv, lse, mixed, qo_all,
         *late, *plan.arrays),
    )
    return (out[:3], out[3:])


def sequence_of(pc):
    if pc.two_level:
        return ((0, 1, 2, 3, 6, 7, 4, 5), 5, 7)
    return (tuple(range(pc.count)), pc.count - 1, pc.count - 1)


def lanes(slot, rows):
    return pl.ds(pl.multiple_of(slot * rows, rows), rows)


def transpose_into(dst, src):
    cols = src.shape[1]
    for c0 in range(0, cols, 128):
        c1 = min(c0 + 128, cols)
        dst[c0:c1, :] = src[:, c0:c1].T


def feed_forward_kernel(dims, plan, x_ref, res_ref, wgu_ref, wd_ref, *refs):
    n = plan.count
    ins, refs = (refs[:n], refs[n:])
    out_ref, x_out, gu_out = refs[:3]
    outs, refs = (refs[3 : 3 + n], refs[3 + n :])
    x_all, gu_all, lsem, wgu_t, wd_t, gu, inner, near, away, back, hop, ss, sr, gs, gr = refs[:15]
    pc = Place(dims)
    width, rows = x_ref.shape
    ff = wd_ref.shape[0]
    riders, _ = plan.board(pc, ins, outs, refs[15:])
    greet(pc, "mates", n > 0)
    gather = PlaneGather(pc, lambda q: x_all.at[:, lanes(q, rows)], gs, gr)
    scatter = PlaneScatter(pc, near, away, back, hop, ss, sr)
    x_all[:, lanes(pc.me, rows)] = x_ref[...]
    gather.start()
    each(riders, "start")
    transpose_into(wgu_t, wgu_ref)
    transpose_into(wd_t, wd_ref)
    sequence, diagonal_at, early_at = sequence_of(pc)
    chunk = 32 if ff % 32 == 0 else 16

    def step_body(turn, carry):
        step = pick(turn, sequence)

        for k in range(pc.count):
            @pl.when(step == k)
            def _():
                gather.before(k)

        slot = pick(step, gather.order)
        sl = lanes(slot, rows)
        gu[...] = nn(wgu_t[...], x_all[:, sl])

        def act(i, c):
            r = pl.multiple_of(i * chunk, chunk)
            gate = gu[pl.ds(r, chunk), :]
            up = gu[pl.ds(ff + r, chunk), :]
            gu_all[pl.ds(r, chunk), sl] = gate.astype(BF)
            gu_all[pl.ds(ff + r, chunk), sl] = up.astype(BF)
            inner[pl.ds(r, chunk), :] = (gate * jax.nn.sigmoid(gate) * up).astype(BF)
            return c

        lax.fori_loop(0, ff // chunk, act, 0)
        scatter.put(step, nn(wd_t[...], inner[...]))

        @pl.when(turn == 3)
        def _():
            each(riders, "service")

        @pl.when(turn == diagonal_at)
        def _():
            scatter.diagonal()

        @pl.when(turn == early_at)
        def _():
            scatter.early()

        return carry

    lax.fori_loop(0, pc.count, step_body, 0)
    leaving = [
        pltpu.make_async_copy(gu_all, gu_out, lsem.at[0]),
        pltpu.make_async_copy(x_all, x_out, lsem.at[1]),
    ]
    each(leaving, "start")
    each(riders, "service")

    def store(total):
        out_ref[...] = res_ref[...] + total

    scatter.result(store)
    gather.finish()
    each(leaving, "wait")
    each(riders, "finish")


def feed_forward(dims, cid, x, residual, wgu, wd, plan):
    width, rows = x.shape
    count = dims[0] * dims[2]
    two_ff, ff = (wgu.shape[1], wd.shape[0])
    sds = jax.ShapeDtypeStruct
    dma = pltpu.SemaphoreType.DMA
    out = call(
        functools.partial(feed_forward_kernel, dims, plan),
        "feed_forward",
        cid,
        (
            sds((width, rows), F32),
            sds((width, count * rows), BF),
            sds((two_ff, count * rows), BF),
            *plan.shapes,
        ),
        [VM, AN, AN] + plan.outs,
        [VM] * 4 + plan.places,
        [
            pltpu.VMEM((width, count * rows), BF),
            pltpu.VMEM((two_ff, count * rows), BF),
            dma((2,)),
            pltpu.VMEM((two_ff, width), BF),
            pltpu.VMEM((width, ff), BF),
            pltpu.VMEM((two_ff, rows), F32),
            pltpu.VMEM((ff, rows), BF),
        ]
        + scatter_scratch(dims, width, rows)
        + gather_sems(dims)
        + plan.scratch,
        (x, residual, wgu, wd, *plan.arrays),
    )
    return (out[:3], out[3:])


def feed_backward_kernel(
    dims, layer, plan, g_ref, res_ref, x_in, gu_in, wgu_ref, wd_ref, small_ref, *refs
):
    n = plan.count
    ins, refs = (refs[:n], refs[n:])
    gr_ref, dwgu_ref, dwd_ref, dsmall_ref = refs[:4]
    outs, refs = (refs[4 : 4 + n], refs[4 + n :])
    x_all, gu_all, lsem, g_all, inner, ggu, gi, near, away, back, hop, ss, sr, gs, gr = refs[:15]
    coming = [
        pltpu.make_async_copy(gu_in, gu_all, lsem.at[0]),
        pltpu.make_async_copy(x_in, x_all, lsem.at[1]),
    ]
    each(coming, "start")
    pc = Place(dims)
    width, rows = g_ref.shape
    ff = wd_ref.shape[0]
    riders, _ = plan.board(pc, ins, outs, refs[15:])
    greet(pc, "mates", n > 0)
    gather = PlaneGather(pc, lambda q: g_all.at[:, lanes(q, rows)], gs, gr)
    scatter = PlaneScatter(pc, near, away, back, hop, ss, sr)
    g_all[:, lanes(pc.me, rows)] = g_ref[...].astype(BF)
    gather.start()
    each(riders, "start")
    coming[0].wait()
    sequence, diagonal_at, early_at = sequence_of(pc)
    chunk = 32 if ff % 32 == 0 else 16

    def step_body(turn, carry):
        step = pick(turn, sequence)

        for k in range(pc.count):
            @pl.when(step == k)
            def _():
                gather.before(k)

        slot = pick(step, gather.order)
        sl = lanes(slot, rows)
        gi[...] = nn(wd_ref[...], g_all[:, sl])

        def act(i, c):
            r = pl.multiple_of(i * chunk, chunk)
            gate = gu_all[pl.ds(r, chunk), sl].astype(F32)
            up = gu_all[pl.ds(ff + r, chunk), sl].astype(F32)
            grad = gi[pl.ds(r, chunk), :]
            sig = jax.nn.sigmoid(gate)
            silu = gate * sig
            inner[pl.ds(r, chunk), sl] = (silu * up).astype(BF)
            ggu[pl.ds(r, chunk), sl] = (grad * up * sig * (1.0 + gate * (1.0 - sig))).astype(BF)
            ggu[pl.ds(ff + r, chunk), sl] = (grad * silu).astype(BF)
            return c

        lax.fori_loop(0, ff // chunk, act, 0)
        scatter.put(step, nn(wgu_ref[...], ggu[:, sl]))

        @pl.when(turn == 3)
        def _():
            each(riders, "service")

        @pl.when(turn == diagonal_at)
        def _():
            scatter.diagonal()

        @pl.when(turn == early_at)
        def _():
            scatter.early()

        return carry

    lax.fori_loop(0, pc.count, step_body, 0)
    each(riders, "service")
    dwd_ref[...] = nt(inner[...], g_all[...]).astype(BF)
    scatter.late()
    coming[1].wait()
    part = width // 2
    for r in range(2):
        dwgu_ref[r * part : (r + 1) * part, :] = nt(
            x_all[r * part : (r + 1) * part, :], ggu[...]
        ).astype(BF)

    def store(total):
        residual = res_ref[...]
        scale_two = rms(residual)
        unit = residual * scale_two
        n1 = width // 128
        dsmall_ref[...] = rows_of(total * unit)
        u = total * column(padded_t(small_ref[layer]), n1, n1)
        gr_ref[...] = g_ref[...].astype(BF).astype(F32) + scale_two * (
            u - unit * jnp.mean(u * unit, axis=0, keepdims=True)
        )

    scatter.finish(store)
    gather.finish()
    each(riders, "finish")


def feed_backward(dims, cid, layer, g, residual, x_all, gu_all, wgu, wd, small, plan):
    width, rows = g.shape
    count = dims[0] * dims[2]
    two_ff, ff = (wgu.shape[1], wd.shape[0])
    sds = jax.ShapeDtypeStruct
    dma = pltpu.SemaphoreType.DMA
    out = call(
        functools.partial(feed_backward_kernel, dims, layer, plan),
        "feed_backward",
        cid,
        (
            sds((width, rows), F32),
            sds(wgu.shape, BF),
            sds(wd.shape, BF),
            sds((width // 128, 128), F32),
            *plan.shapes,
        ),
        [VM] * 4 + plan.outs,
        [VM, VM, AN, AN, VM, VM, VM] + plan.places,
        [
            pltpu.VMEM((width, count * rows), BF),
            pltpu.VMEM((two_ff, count * rows), BF),
            dma((2,)),
            pltpu.VMEM((width, count * rows), BF),
            pltpu.VMEM((ff, count * rows), BF),
            pltpu.VMEM((two_ff, count * rows), BF),
            pltpu.VMEM((ff, rows), F32),
        ]
        + scatter_scratch(dims, width, rows)
        + gather_sems(dims)
        + plan.scratch,
        (g, residual, x_all, gu_all, wgu, wd, small, *plan.arrays),
    )
    return (out[:4], out[4:])


def feed_both_kernel(
    dims, layer, x_ref, res_ref, g_ref, g_all, wgu_ref, wd_ref, small_ref,
    gr_ref, dwgu_ref, dwd_ref, dsmall_ref, parts_ref,
    x_all, inner, ggu, wgu_t, wd_t, gu, gi, near, away, back, hop, ss, sr, gs, gr,
):
    pc = Place(dims)
    width, rows = g_ref.shape
    ff = wd_ref.shape[0]
    greet(pc, "mates", False)
    gather = PlaneGather(pc, lambda q: x_all.at[:, lanes(q, rows)], gs, gr)
    scatter = PlaneScatter(pc, near, away, back, hop, ss, sr)
    x_all[:, lanes(pc.me, rows)] = x_ref[...]
    gather.start()
    transpose_into(wgu_t, wgu_ref)
    transpose_into(wd_t, wd_ref)
    sequence, diagonal_at, early_at = sequence_of(pc)
    chunk = 32 if ff % 32 == 0 else 16

    def step_body(turn, carry):
        step = pick(turn, sequence)

        for k in range(pc.count):
            @pl.when(step == k)
            def _():
                gather.before(k)

        slot = pick(step, gather.order)
        sl = lanes(slot, rows)
        gu[...] = nn(wgu_t[...], x_all[:, sl])
        gi[...] = nn(wd_ref[...], g_all[:, sl])

        def act(i, c):
            r = pl.multiple_of(i * chunk, chunk)
            gate = gu[pl.ds(r, chunk), :]
            up = gu[pl.ds(ff + r, chunk), :]
            grad = gi[pl.ds(r, chunk), :]
            sig = jax.nn.sigmoid(gate)
            silu = gate * sig
            inner[pl.ds(r, chunk), sl] = (silu * up).astype(BF)
            ggu[pl.ds(r, chunk), sl] = (grad * up * sig * (1.0 + gate * (1.0 - sig))).astype(BF)
            ggu[pl.ds(ff + r, chunk), sl] = (grad * silu).astype(BF)
            return c

        lax.fori_loop(0, ff // chunk, act, 0)
        scatter.put(step, nn(wgu_ref[...], ggu[:, sl]))

        @pl.when(turn == diagonal_at)
        def _():
            scatter.diagonal()

        @pl.when(turn == early_at)
        def _():
            scatter.early()

        parts_ref[slot] = nn(wd_t[...], inner[:, sl]).astype(BF)
        return carry

    lax.fori_loop(0, pc.count, step_body, 0)
    dwd_ref[...] = nt(inner[...], g_all[...]).astype(BF)
    scatter.late()
    part = width // 2
    for r in range(2):
        dwgu_ref[r * part : (r + 1) * part, :] = nt(
            x_all[r * part : (r + 1) * part, :], ggu[...]
        ).astype(BF)

    def store(total):
        residual = res_ref[...]
        scale_two = rms(residual)
        unit = residual * scale_two
        n1 = width // 128
        dsmall_ref[...] = rows_of(total * unit)
        u = total * column(padded_t(small_ref[layer]), n1, n1)
        gr_ref[...] = g_ref[...].astype(BF).astype(F32) + scale_two * (
            u - unit * jnp.mean(u * unit, axis=0, keepdims=True)
        )

    scatter.finish(store)
    gather.finish()


def feed_both(dims, cid, layer, x, residual, g, g_all, wgu, wd, small):
    width, rows = g.shape
    count = dims[0] * dims[2]
    two_ff, ff = (wgu.shape[1], wd.shape[0])
    sds = jax.ShapeDtypeStruct
    dma = pltpu.SemaphoreType.DMA
    return call(
        functools.partial(feed_both_kernel, dims, layer),
        "feed_both",
        cid,
        (
            sds((width, rows), F32),
            sds(wgu.shape, BF),
            sds(wd.shape, BF),
            sds((width // 128, 128), F32),
            sds((count, width, rows), BF),
        ),
        [VM] * 5,
        [VM] * 7,
        [
            pltpu.VMEM((width, count * rows), BF),
            pltpu.VMEM((ff, count * rows), BF),
            pltpu.VMEM((two_ff, count * rows), BF),
            pltpu.VMEM((two_ff, width), BF),
            pltpu.VMEM((width, ff), BF),
            pltpu.VMEM((two_ff, rows), F32),
            pltpu.VMEM((ff, rows), F32),
        ]
        + scatter_scratch(dims, width, rows)
        + gather_sems(dims),
        (x, residual, g, g_all, wgu, wd, small),
    )


def reduce_kernel(
    dims, qo, terms, sa0, sa1, sb0, sb1, wd1, gu0a, gu0, wd0,
    qo_out, small_out, gu_got, wd_got,
    held, rest_gu, gsum, wsum, small, sm_in, sm_mid, sm_line, z_out, mine, give,
    lsem, ws, wr, ls, lr, zs, zr, *rest
):
    pc = Place(dims)
    ns, nb, nf = dims
    coming = pltpu.make_async_copy(qo, held, lsem.at[1])
    coming.start()
    cut = gu0a.shape[0]
    coming_gu = pltpu.make_async_copy(gu0.at[:, cut:nf], rest_gu, lsem.at[2])
    coming_gu.start()
    n1 = sb0.shape[0]
    per = small.shape[0] // ns
    nr = sa0.shape[0] + n1
    small[...] = jnp.zeros_like(small)
    for l, (a, g) in enumerate(((sa0, sb0), (sa1, sb1))):
        small[l * per : l * per + n1] = a[0:n1]
        small[l * per + n1 : l * per + 2 * n1] = g[...]
        small[l * per + 2 * n1 : l * per + nr] = a[n1 : a.shape[0]]
    greet(pc, "all", True)

    def keep(value):
        wsum[...] = value.astype(BF)

    def keep_of(l):
        def store(value):
            mine[l] = value

        return store

    line = LineReduce(pc, lambda t: wd0[t], keep, rest[0:4])
    ends = [
        LineReduce(pc, lambda t: z_out[t], keep_of(0), rest[4:8]),
        LineReduce(pc, lambda t: terms[t], keep_of(1), rest[8:12]),
    ]
    def keep_gu(value):
        gsum[...] = value.astype(BF)

    line_gu = LineReduce(pc, lambda t: rest_gu[t], keep_gu, rest[19:23])
    ends[1].start()
    coming_gu.wait()
    line_gu.start()
    line.start()
    scatter = ReadyScatter(
        pc, lambda q: columns_of(held, q, nf, z_out.shape[2]), *rest[15:19]
    )
    coming.wait()
    scatter.start()
    smalls = [
        remote(small, sm_in.at[e - 1], ls.at[e - 1], lr.at[e - 1], pc.plane(e))
        for e in range(1, pc.count)
    ]
    for c in smalls:
        c.start()
    scatter.diagonal()
    scatter.early()
    hand_out = RowSends(pc, 0, gu_got, rest[12:15])
    for f in range(cut):
        hand_out.start(f, gu0a.at[f])

    def split(l, ref):
        @pl.when(pc.s == l)
        def _():
            pltpu.make_async_copy(ref, wd_got.at[l], lsem.at[0]).start()

        @pl.when(pc.s != l)
        def _():
            remote(ref, wd_got.at[pc.s], ws.at[0], wr.at[0], (l, pc.b, pc.f)).start()

    split(1, wd1)
    ends[1].service()
    line_gu.service()
    line.service()
    scatter.late()
    ends[1].service()
    total = small[...]
    for e, c in enumerate(smalls):
        c.wait()
        total = total + sm_in[e]
    sm_mid[...] = total
    lines = [
        remote(sm_mid, sm_line.at[d - 1], zs.at[d - 1], zr.at[d - 1], pc.along(d))
        for d in range(1, nb)
    ]
    for c in lines:
        c.start()
    line_gu.service()
    line.service()

    def store(value):
        z_out[...] = value.astype(BF)

    scatter.finish(store)
    ends[0].start()
    ends[1].finish()
    line_gu.finish()
    for f in range(cut, nf):
        hand_out.start(f, gsum.at[f - cut])
    ends[0].service()
    line.finish()
    split(0, wsum)
    ends[0].finish()
    mate = (ns - 1 - pc.s, pc.b, pc.f)
    swap = remote(give.at[0], give.at[1], ws.at[1], wr.at[1], mate)
    give[0] = mine[ns - 1 - pc.s].astype(BF)
    swap.start()
    qo_out[pc.s] = mine[pc.s]
    total = sm_mid[...]
    for d, c in enumerate(lines):
        c.wait()
        total = total + sm_line[d]
    small_out[...] = total
    hand_out.finish(gu0a.at[0])
    pltpu.make_async_copy(wsum, wd_got.at[pc.s], lsem.at[0]).wait()
    remote(wsum, wd_got.at[pc.s], ws.at[0], wr.at[0], mate).wait()
    swap.wait()
    qo_out[ns - 1 - pc.s] = give[1].astype(F32)


def reduce_gradients(dims, cid, qo, terms, smalls, wd1, gu0a, gu0, wd0):
    ns, nb, nf = dims
    count = ns * nf
    dr, wide = terms.shape[1:]
    two_ff = gu0.shape[3]
    cut = gu0a.shape[0]
    half, width = wd1.shape
    rows = smalls[0].shape[0] + smalls[2].shape[0]
    small = (ns * (-(-rows // 8) * 8), 128)
    sds = jax.ShapeDtypeStruct
    dma = pltpu.SemaphoreType.DMA
    return call(
        functools.partial(reduce_kernel, dims),
        "reduce_gradients",
        cid,
        (
            sds((ns, dr, wide), F32),
            sds(small, F32),
            sds((count, dr, two_ff), BF),
            sds((ns, half, width), BF),
        ),
        [VM] * 4,
        [AN] + [VM] * 7 + [AN, VM],
        [
            pltpu.VMEM(qo.shape, BF),
            pltpu.VMEM((nb, nf - cut, dr, two_ff), BF),
            pltpu.VMEM((nf - cut, dr, two_ff), BF),
            pltpu.VMEM((half, width), BF),
            pltpu.VMEM(small, F32),
            pltpu.VMEM((count - 1,) + small, F32),
            pltpu.VMEM(small, F32),
            pltpu.VMEM((nb - 1,) + small, F32),
            pltpu.VMEM((nb, dr, wide), BF),
            pltpu.VMEM((ns, dr, wide), F32),
            pltpu.VMEM((2, dr, wide), BF),
            dma((3,)),
            dma((2,)),
            dma((2,)),
            dma((count - 1,)),
            dma((count - 1,)),
            dma((nb - 1,)),
            dma((nb - 1,)),
        ]
        + reduce_scratch(dims, half, width)
        + reduce_scratch(dims, dr, wide) * 2
        + row_scratch(dims)
        + scatter_scratch(dims, nb, dr, wide)[2:]
        + reduce_scratch(dims, nf - cut, dr, two_ff),
        (qo, terms, *smalls, wd1, gu0a, gu0, wd0),
    )


def lay_out_kernel(
    dims, gu0, gu1, wd, qo, small, out0, out1, gh0, gh1, take_out, take_grad,
    block_out, input_grad, g1, wqkv, bqkv, wout, g2, wgu, wdn
):
    ns, nb, nf = dims
    half = wd.shape[1]
    s = lax.axis_index("section")
    qkv = wqkv.shape[2]
    width = wout.shape[2]
    full = jnp.concatenate([qo[y] for y in range(ns)], axis=1)
    wqkv[0] = full[:, :qkv]
    wout[0] = full[:, qkv:]
    for y in range(ns):
        wdn[0, y * half : (y + 1) * half, :] = wd[y].astype(F32)
    for l, gu in enumerate((gu0, gu1)):
        @pl.when(s == l)
        def _():
            for y in range(ns):
                for f in range(nf):
                    got = gu[y * nf + f].astype(F32)
                    for part in range(2):
                        for b in range(nb):
                            c0 = column_start(dims, part, b, f, y, half)
                            k0 = (part * nb + b) * half
                            wgu[0, :, c0 : c0 + half] = got[:, k0 : k0 + half]
    n1 = width // 128
    per = small.shape[0] // ns
    rows = small[pl.ds(pl.multiple_of(s * per, 8), per), :]
    for k in range(n1):
        g1[0:1, k * 128 : (k + 1) * 128] = rows[k : k + 1]
        g2[0:1, k * 128 : (k + 1) * 128] = rows[n1 + k : n1 + k + 1]
    for k in range(qkv // 128):
        bqkv[0:1, k * 128 : (k + 1) * 128] = rows[2 * n1 + k : 2 * n1 + k + 1]
    for out, pair, take in (
        (block_out, (out0, out1), take_out),
        (input_grad, (gh0, gh1), take_grad),
    ):
        for l in range(ns):
            @pl.when(s == l)
            def _():
                out[0, l] = pair[l][...].T
                out[0, 1 - l] = take[...].T.astype(F32)


def lay_out(dims, qkv, args):
    ns, nb, nf = dims
    gu, wd, qo = (args[0], args[2], args[3])
    width, rows = args[5].shape
    dr = qo.shape[1]
    sds = jax.ShapeDtypeStruct
    tokens = sds((1, ns, rows, width), F32)
    return pl.pallas_call(
        functools.partial(lay_out_kernel, dims),
        name="lay_out",
        out_shape=(
            tokens,
            tokens,
            sds((1, width), F32),
            sds((1, dr, qkv), F32),
            sds((1, qkv), F32),
            sds((1, dr, width), F32),
            sds((1, width), F32),
            sds((1, dr, gu.shape[0] * gu.shape[2]), F32),
            sds((1, ns * wd.shape[1], width), F32),
        ),
        in_specs=[VM] * len(args),
        out_specs=[VM] * 9,
        compiler_params=pltpu.CompilerParams(vmem_limit_bytes=VMEM_LIMIT),
    )(*args)


def shards(
    dims,
    tokens_in,
    positions,
    doc_ids,
    out_grad,
    norm1_gain,
    w_qkv,
    b_qkv,
    w_out,
    norm2_gain,
    w_gate_up,
    w_down,
):
    ns, nb, nf = dims
    seqs, rows, width = tokens_in.shape
    s = lax.axis_index("section")
    b = lax.axis_index("blk")
    dr = w_qkv.shape[1]
    qkv = w_qkv.shape[2]
    fr = w_down.shape[1]
    half = fr // ns
    ff = nb * half
    nk = min(nb, 1 + (LONGEST - 1 + rows - 1) // rows)

    tokens = lax.dynamic_index_in_dim(tokens_in, s, 0, keepdims=False)
    cot = lax.dynamic_index_in_dim(out_grad, s, 0, keepdims=False)
    pos = lax.dynamic_index_in_dim(positions, s, 0, keepdims=False)
    docs = lax.dynamic_index_in_dim(doc_ids, s, 0, keepdims=False).astype(F32)
    freq = jnp.exp(jnp.arange(HD // 2, dtype=F32) * (-2.0 / HD) * math.log(1000000.0))
    phase = freq[:, None] * pos.astype(F32)[None, :]
    cos_part, sin_part = (jnp.cos(phase), jnp.sin(phase))
    docs = docs.reshape(nb, rows)
    picked = (b - jnp.arange(nk) + nb) % nb
    meta = jnp.take(docs, picked, axis=0).reshape(nk * rows // 128, 128)
    query_docs = lax.dynamic_slice_in_dim(docs, b, 1)
    hidden = tokens.T.astype(F32)
    g = cot.T.astype(F32)

    wd = w_down[0].reshape(ns, half, width)
    small = jnp.concatenate([norm1_gain[0], norm2_gain[0], b_qkv[0]])
    total = -(-small.shape[0] // 1024) * 1024
    small = jnp.pad(small, (0, total - small.shape[0])).reshape(-1, 128)
    gup, wdp, gu_first, qo_first, qz, small_all = gather_weights(
        dims, w_gate_up, w_qkv, w_out, wd, small
    )
    cols = qkv + width
    wide = (width, 2 * ff)

    def ride(*pairs):
        return Riders(dims, tuple(a for a, _ in pairs), tuple(v for _, v in pairs))

    common = (small_all, meta, query_docs, cos_part, sin_part)
    qo0 = qo_first.reshape(width, cols)
    a0, (wd0, qo1) = attention_forward(
        dims, nk, 1, 0, hidden, *common, qo0, ride((("gather", 0), wdp)), "columns", qz
    )
    qo1 = qo1.reshape(width, cols)
    wd0 = wd0.reshape(ff, width)
    wgu0 = gu_first.reshape(wide)
    f0, (gu1,) = feed_forward(dims, 3, a0[6], a0[5], wgu0, wd0, ride((("gather", 1), gup)))
    wgu1 = gu1.reshape(wide)
    a1, (wd1, g_all) = attention_forward(
        dims, nk, 2, 1, f0[0], *common, qo1, ride((("gather", 1), wdp)), "lanes", cot.T
    )
    wd1 = wd1.reshape(ff, width)

    line_gu = (nb, nf, dr, 2 * ff)
    line_wd = (nb, half, width)
    line_qo = (nb, nf, dr, cols)
    everything = (0, half)
    b1 = feed_both(dims, 4, 1, a1[6], a1[5], g, g_all, wgu1, wd1, small_all)
    ab1, (dwd1, out1) = attention_backward(
        dims, nk, 7, 1, b1[0], *common, f0[0], *a1[:5], qo1,
        ride((("reduce", everything), b1[2].reshape(line_wd))), "sum", (b1[4], a1[5]),
    )
    b0, (dgu1,) = feed_backward(
        dims, 6, 0, ab1[0], a0[5], f0[1], f0[2], wgu0, wd0, small_all,
        ride((("reduce", (0, nf)), b1[1].reshape(line_gu))),
    )
    dgu0 = b0[1].reshape(line_gu)
    cut = nf - nf // 4
    ab0, (dgu0a, terms, gu_got1) = attention_backward(
        dims, nk, 8, 0, b0[0], *common, hidden, *a0[:5], qo0,
        ride((("reduce", (0, cut)), dgu0)),
        "columns", (ab1[1].reshape(line_qo), dgu1),
    )

    def swapped(values):
        give = jnp.where(s == 0, values[1], values[0]).astype(BF)
        return lax.ppermute(give, "section", [(0, 1), (1, 0)])

    take_out = swapped((f0[0], out1))
    take_grad = swapped((ab0[0], ab1[0]))
    grad_qo, small_sum, gu_got0, wd_got = reduce_gradients(
        dims, 9, ab0[1].reshape(line_qo), terms,
        (ab0[2], ab1[2], b0[3], b1[3]), dwd1, dgu0a, dgu0, b0[2].reshape(line_wd),
    )
    return lay_out(
        dims,
        qkv,
        (gu_got0, gu_got1, wd_got, grad_qo, small_sum, f0[0], out1, ab0[0], ab1[0], take_out,
         take_grad),
    )


def solution(mesh):
    dims = (mesh.shape["section"], mesh.shape["blk"], mesh.shape["fsdp"])
    return jax.shard_map(
        functools.partial(shards, dims),
        mesh=mesh,
        in_specs=(
            P("fsdp", "blk", None),
            P("fsdp", "blk"),
            P("fsdp", None),
            P("fsdp", "blk", None),
            P("section", None),
            P("section", ("blk", "fsdp"), None),
            P("section", None),
            P("section", ("blk", "fsdp"), None),
            P("section", None),
            P("section", ("blk", "fsdp"), None),
            P("section", ("blk", "fsdp"), None),
        ),
        out_specs=(
            P("section", "fsdp", "blk", None),
            P("section", "fsdp", "blk", None),
            P("section", None),
            P("section", ("blk", "fsdp"), None),
            P("section", None),
            P("section", ("blk", "fsdp"), None),
            P("section", None),
            P("section", ("blk", "fsdp"), None),
            P("section", ("blk", "fsdp"), None),
        ),
        check_vma=False,
    )
```

```python
import functools
import math

import jax
import jax.numpy as jnp
from jax import lax
from jax.experimental import pallas as pl
from jax.experimental.pallas import tpu as pltpu
from jax.sharding import PartitionSpec as P

H = 14
KVH = 2
HD = 64
GROUP = H // KVH
LONGEST = 512
NEG = -1e30
BF = jnp.bfloat16
F32 = jnp.float32
MESH = pl.DeviceIdType.MESH
VMEM_LIMIT = 60 * 2**20
VM = pl.BlockSpec(memory_space=pltpu.VMEM)
AN = pl.BlockSpec(memory_space=pl.ANY)


def nn(a, b):
    return lax.dot_general(a, b, (((1,), (0,)), ((), ())), preferred_element_type=F32)


def nt(a, b):
    return lax.dot_general(a, b, (((1,), (1,)), ((), ())), preferred_element_type=F32)


def tn(a, b):
    return lax.dot_general(a, b, (((0,), (0,)), ((), ())), preferred_element_type=F32)


def other(f):
    return f + 1 - 2 * (f % 2)


class Place:
    def __init__(self, dims):
        self.ns, self.nb, self.nf = dims
        self.count = self.ns * self.nf
        self.s = lax.axis_index("section")
        self.b = lax.axis_index("blk")
        self.f = lax.axis_index("fsdp")
        self.me = self.s * self.nf + self.f
        self.two_level = self.ns == 2 and self.nf == 4

    def plane(self, e):
        q = (self.me + e) % self.count
        return (q // self.nf, self.b, q % self.nf)

    def slot_from(self, e):
        return (self.me + self.count - e) % self.count

    def along(self, d):
        return (self.s, (self.b + d) % self.nb, self.f)

    def mates(self):
        s, b, f = (self.s, self.b, self.f)
        xf = (f + 2) % 4
        return ((s, b, other(f)), (s, b, xf), (1 - s, b, f))

    def slots(self):
        s, f = (self.s, self.f)
        xf = (f + 2) % 4
        t = 1 - s
        return (
            s * 4 + f,
            s * 4 + other(f),
            s * 4 + xf,
            t * 4 + f,
            s * 4 + other(xf),
            t * 4 + other(f),
            t * 4 + xf,
            t * 4 + other(xf),
        )


def pick(i, values):
    total = 0
    for k, v in enumerate(values):
        total = total + jnp.where(i == k, v, 0)
    return total


def greet(place, plane, along):
    barrier = pltpu.get_barrier_semaphore()
    count = 0
    if plane:
        if place.two_level and plane == "mates":
            targets = list(place.mates())
        else:
            targets = [place.plane(e) for e in range(1, place.count)]
        for t in targets:
            pl.semaphore_signal(barrier, 1, device_id=t, device_id_type=MESH)
        count += len(targets)
    if along:
        for d in range(1, place.nb):
            pl.semaphore_signal(barrier, 1, device_id=place.along(d), device_id_type=MESH)
        count += place.nb - 1
    pl.semaphore_wait(barrier, count)


def remote(src, dst, ssem, rsem, device):
    return pltpu.make_async_remote_copy(
        src_ref=src,
        dst_ref=dst,
        send_sem=ssem,
        recv_sem=rsem,
        device_id=device,
        device_id_type=MESH,
    )


def cut_in(parts, view, c):
    n = view.shape[0] // parts
    return view.at[pl.ds(c * n, n)]


def gather_sems(dims):
    n = 2 * (dims[0] * dims[2] - 1)
    return [pltpu.SemaphoreType.DMA((n,)), pltpu.SemaphoreType.DMA((n,))]


class PlaneGather:
    def __init__(self, place, slot, ssem, rsem):
        self.place, self.slot, self.ssem, self.rsem = (place, slot, ssem, rsem)
        self.parts = 2 if place.two_level else 1
        if place.two_level:
            self.order = place.slots()
        else:
            self.order = tuple(place.slot_from(e) for e in range(place.count))

    def copy(self, k, c, q, device):
        v = cut_in(self.parts, self.slot(q), c)
        i = k * self.parts + c
        return remote(v, v, self.ssem.at[i], self.rsem.at[i], device)

    def start(self):
        pc = self.place
        if pc.two_level:
            core, xm, ym = pc.mates()
            for c in range(2):
                self.copy(1, c, self.order[0], xm).start()
                self.copy(2, c, self.order[0], ym).start()
            for c in range(2):
                self.copy(0, c, self.order[0], core).start()
        else:
            for e in range(1, pc.count):
                self.copy(e - 1, 0, self.order[0], pc.plane(e)).start()

    def came(self, k, c):
        self.copy(k, c, self.order[k + 1], self.place.plane(1)).wait_recv()

    def before(self, step):
        if step == 0:
            return
        pc = self.place
        if not pc.two_level:
            self.came(step - 1, 0)
            return
        core, xm, ym = pc.mates()
        h = pc.f % 2
        if step == 2:
            which = h * self.order[3] + (1 - h) * self.order[2]
            far = (
                h * xm[0] + (1 - h) * ym[0],
                pc.b,
                h * xm[2] + (1 - h) * ym[2],
            )
            for c in range(2):
                self.came(1, c)
                self.came(2, c)
                self.copy(5, c, which, far).start()
                self.copy(3, c, self.order[2], core).start()
                self.copy(4, c, self.order[3], core).start()
        elif step == 3:
            return
        elif step == 6:
            for c in range(2):
                self.came(5, c)
                self.copy(6, c, self.order[6], core).start()
        else:
            for c in range(2):
                self.came(step - 1, c)

    def finish(self):
        n = self.place.count - 1
        for k in range(n):
            for c in range(self.parts):
                self.copy(k, c, self.order[0], self.place.plane(1)).wait_send()


class PlaneScatter:
    def __init__(self, place, near, away, back, hop, ssem, rsem):
        self.place = place
        self.near, self.away, self.back, self.hop = (near, away, back, hop)
        self.ssem, self.rsem = (ssem, rsem)

    def put(self, step, value):
        pc = self.place
        if not pc.two_level:
            @pl.when(step == 0)
            def _():
                self.near[0] = value

            @pl.when(step > 0)
            def _():
                e = pc.count - step
                self.away[e - 1] = value.astype(BF)
                q = (pc.me + e) % pc.count
                remote(
                    self.away.at[e - 1],
                    self.back.at[e - 1],
                    self.ssem.at[e - 1],
                    self.rsem.at[e - 1],
                    (q // pc.nf, pc.b, q % pc.nf),
                ).start()
            return
        core, xm, ym = pc.mates()
        here = (step == 0) | (step == 2) | (step == 3) | (step == 6)
        q = pick(step, (0, 0, 1, 2, 1, 2, 3, 3))

        @pl.when(here)
        def _():
            self.near[q] = value

        @pl.when(jnp.logical_not(here))
        def _():
            self.away[q] = value.astype(BF)
            self.core_copy(q).start()

    def core_copy(self, q):
        core = self.place.mates()[0]
        return remote(self.away.at[q], self.back.at[q], self.ssem.at[q], self.rsem.at[q], core)

    def far_copy(self, e):
        return remote(self.away.at[e - 1], self.back.at[e - 1], self.ssem.at[e - 1],
                      self.rsem.at[e - 1], self.place.plane(e))

    def hop_copy(self, k, c, device):
        i = 4 + 2 * k + c
        return remote(
            cut_in(2, self.hop.at[k], c),
            cut_in(2, self.hop.at[k + 3], c),
            self.ssem.at[i],
            self.rsem.at[i],
            device,
        )

    def rows(self, c):
        n = self.hop.shape[1] // 2
        return slice(c * n, (c + 1) * n)

    def targets(self):
        pc = self.place
        core, xm, ym = pc.mates()
        c = pc.f % 2
        first = (c * xm[0] + (1 - c) * ym[0], pc.b, c * xm[2] + (1 - c) * ym[2])
        second = (c * ym[0] + (1 - c) * xm[0], pc.b, c * ym[2] + (1 - c) * xm[2])
        return (first, second)

    def early(self):
        pc = self.place
        if not pc.two_level:
            return
        c = pc.f % 2
        first, second = self.targets()
        self.core_copy(1).wait_recv()
        self.core_copy(2).wait_recv()
        q = c * 1 + (1 - c) * 2
        for k in range(2):
            r = self.rows(k)
            self.hop[0, r] = (self.mine(q, r) + self.back[q, r].astype(F32)).astype(BF)
            self.hop_copy(0, k, first).start()

    def diagonal(self):
        pc = self.place
        if not pc.two_level:
            return
        first, second = self.targets()
        self.core_copy(3).wait_recv()
        for k in range(2):
            r = self.rows(k)
            self.hop[1, r] = (self.mine(3, r) + self.back[3, r].astype(F32)).astype(BF)
            self.hop_copy(1, k, first).start()

    def mine(self, q, r=slice(None)):
        return self.near[q, r]

    def result(self, store):
        self.late()
        self.finish(store)

    def late(self):
        pc = self.place
        if not pc.two_level:
            return
        c = pc.f % 2
        first, second = self.targets()
        q = c * 2 + (1 - c) * 1
        for k in range(2):
            r = self.rows(k)
            self.hop_copy(1, k, first).wait_recv()
            self.hop[2, r] = (
                self.mine(q, r) + self.back[q, r].astype(F32) + self.hop[4, r].astype(F32)
            ).astype(BF)
            self.hop_copy(2, k, second).start()

    def finish(self, store):
        pc = self.place
        if not pc.two_level:
            total = self.mine(0)
            for e in range(1, pc.count):
                self.far_copy(e).wait()
                total = total + self.back[e - 1].astype(F32)
            store(total)
            return
        first, second = self.targets()
        self.core_copy(0).wait_recv()
        for k in range(2):
            self.hop_copy(0, k, first).wait_recv()
            self.hop_copy(2, k, second).wait_recv()
        store(
            self.mine(0)
            + self.back[0].astype(F32)
            + self.hop[3].astype(F32)
            + self.hop[5].astype(F32)
        )
        for q in range(4):
            self.core_copy(q).wait_send()
        for k in range(2):
            self.hop_copy(0, k, first).wait_send()
            self.hop_copy(1, k, first).wait_send()
            self.hop_copy(2, k, second).wait_send()


class ReadyScatter(PlaneScatter):
    def __init__(self, place, part, back, hop, ssem, rsem):
        super().__init__(place, None, None, back, hop, ssem, rsem)
        self.part = part
        if place.two_level:
            o = place.slots()
            self.here = (o[0], o[2], o[3], o[6])
            self.gone = (o[1], o[4], o[5], o[7])

    def mine(self, q, r=slice(None)):
        if not self.place.two_level:
            return self.part(self.place.me)[...].astype(F32)
        return self.part(pick(q, self.here))[r].astype(F32)

    def core_copy(self, q):
        core = self.place.mates()[0]
        v = self.part(self.gone[q])
        return remote(v, self.back.at[q], self.ssem.at[q], self.rsem.at[q], core)

    def far_copy(self, e):
        pc = self.place
        v = self.part((pc.me + e) % pc.count)
        return remote(v, self.back.at[e - 1], self.ssem.at[e - 1], self.rsem.at[e - 1],
                      pc.plane(e))

    def start(self):
        pc = self.place
        if pc.two_level:
            for q in (3, 2, 1, 0):
                self.core_copy(q).start()
        else:
            for e in range(1, pc.count):
                self.far_copy(e).start()


class RowSends:
    def __init__(self, place, layer, out, sems):
        self.place, self.layer, self.out = (place, layer, out)
        self.lsem, self.ss, self.sr = sems

    def copies(self, f, src):
        pc = self.place
        e = (self.layer * pc.nf + f - pc.me + pc.count) % pc.count
        own = self.out.at[pc.me]
        k = (e + pc.count - 1) % pc.count
        away = remote(src, own, self.ss.at[f], self.sr.at[k], (self.layer, pc.b, f))
        return (e, away, pltpu.make_async_copy(src, own, self.lsem))

    def start(self, f, src):
        e, away, local = self.copies(f, src)

        @pl.when(e != 0)
        def _():
            away.start()

        @pl.when(e == 0)
        def _():
            local.start()

    def finish(self, src):
        pc = self.place
        for f in range(pc.nf):
            e, away, local = self.copies(f, src)

            @pl.when(e != 0)
            def _():
                away.wait_send()

            @pl.when(e == 0)
            def _():
                local.wait()

        @pl.when(pc.s == self.layer)
        def _():
            for e in range(1, pc.count):
                q = pc.slot_from(e)
                remote(src, self.out.at[q], self.ss.at[0], self.sr.at[e - 1], pc.plane(e)).wait_recv()


def row_scratch(dims):
    dma = pltpu.SemaphoreType.DMA
    return [dma(()), dma((dims[2],)), dma((dims[0] * dims[2],))]


class LineGather:
    def __init__(self, place, piece, out, sems, part=None):
        self.place, self.piece = (place, piece)
        self.view = lambda t: out.at[t] if part is None else out.at[t, part]
        self.lsem, self.ss, self.sr = sems
        self.k = 0

    def local(self):
        return pltpu.make_async_copy(self.piece, self.view(self.place.b), self.lsem)

    def hop(self, way, k, came):
        pc = self.place
        t = pc.b - way * (k - (0 if came else 1))
        src = self.piece if k == 1 and not came else self.view(t)
        i = k - 1 + (0 if way == 1 else pc.nb - 1)
        return remote(
            src, self.view(t), self.ss.at[i], self.sr.at[i], (pc.s, pc.b + way, pc.f)
        )

    def sends(self, way, k):
        b, nb = (self.place.b, self.place.nb)
        return (b >= k - 1) & (b < nb - 1) if way == 1 else (b <= nb - k) & (b > 0)

    def comes(self, way, k):
        b, nb = (self.place.b, self.place.nb)
        return b >= k if way == 1 else b <= nb - 1 - k

    def arrived(self, k):
        for way in (1, -1):
            @pl.when(self.comes(way, k))
            def _():
                self.hop(way, k, True).wait_recv()

    def start(self):
        self.local().start()
        self.service()

    def service(self):
        if self.k == self.place.nb - 1:
            return
        self.k += 1
        if self.k > 1:
            self.arrived(self.k - 1)
        for way in (1, -1):
            @pl.when(self.sends(way, self.k))
            def _():
                self.hop(way, self.k, False).start()

    def finish(self):
        last = self.place.nb - 1
        while self.k < last:
            self.service()
        self.arrived(last)
        for k in range(1, last + 1):
            for way in (1, -1):
                @pl.when(self.sends(way, k))
                def _():
                    self.hop(way, k, False).wait_send()
        self.local().wait()


class LineReduce:
    def __init__(self, place, terms, store, sems, load=None):
        self.place, self.terms, self.store, self.load = (place, terms, store, load)
        self.out, self.came, self.ss, self.sr = sems
        self.k = 0

    def index(self, way, k):
        return k - 1 + (0 if way == 1 else self.place.nb - 1)

    def hop(self, way, k):
        pc = self.place
        i = self.index(way, k)
        return remote(
            self.out.at[i], self.came.at[i], self.ss.at[i], self.sr.at[i],
            (pc.s, pc.b + way, pc.f),
        )

    def rank(self, way):
        pc = self.place
        return pc.b if way == 1 else pc.nb - 1 - pc.b

    def sends(self, way, k):
        r = self.rank(way)
        return (r < k) & (r < self.place.nb - 1)

    def start(self):
        if self.load is not None:
            self.load.wait()
        self.service()

    def service(self):
        nb = self.place.nb
        if self.k == nb - 1:
            return
        self.k += 1
        k = self.k
        for way in (1, -1):
            r = self.rank(way)
            t = nb - k + r if way == 1 else k - 1 - r
            i = self.index(way, k)

            @pl.when(self.sends(way, k) & (r == 0))
            def _():
                self.out[i] = self.terms(t)

            if k > 1:
                @pl.when(self.sends(way, k) & (r > 0))
                def _():
                    self.hop(way, k - 1).wait_recv()
                    total = self.terms(t).astype(F32) + self.came[i - 1].astype(F32)
                    self.out[i] = total.astype(BF)

            @pl.when(self.sends(way, k))
            def _():
                self.hop(way, k).start()

    def finish(self):
        pc = self.place
        last = pc.nb - 1
        while self.k < last:
            self.service()
        right, left = (self.index(1, last), self.index(-1, last))

        @pl.when(pc.b == 0)
        def _():
            self.hop(-1, last).wait_recv()
            self.store(self.terms(pc.b).astype(F32) + self.came[left].astype(F32))

        @pl.when(pc.b == last)
        def _():
            self.hop(1, last).wait_recv()
            self.store(self.terms(pc.b).astype(F32) + self.came[right].astype(F32))

        @pl.when((pc.b > 0) & (pc.b < last))
        def _():
            self.hop(1, last).wait_recv()
            self.hop(-1, last).wait_recv()
            self.store(
                self.terms(pc.b).astype(F32)
                + self.came[right].astype(F32)
                + self.came[left].astype(F32)
            )

        for k in range(1, last + 1):
            for way in (1, -1):
                @pl.when(self.sends(way, k))
                def _():
                    self.hop(way, k).wait_send()


def gather_scratch(dims):
    dma = pltpu.SemaphoreType.DMA
    return [dma(()), dma((2 * (dims[1] - 1),)), dma((2 * (dims[1] - 1),))]


def reduce_scratch(dims, *block):
    dma = pltpu.SemaphoreType.DMA
    n = 2 * (dims[1] - 1)
    return [pltpu.VMEM((n,) + block, BF), pltpu.VMEM((n,) + block, BF), dma((n,)), dma((n,))]


class Riders:
    def __init__(self, dims, specs, arrays):
        self.dims, self.specs, self.arrays = (dims, specs, arrays)
        self.shapes = []
        self.places = [AN] * len(specs)
        self.outs = []
        self.scratch = []
        self.sizes = []
        for spec, a in zip(specs, arrays):
            if spec[0] == "gather":
                shape = (dims[1],) + a.shape[1:]
                scratch = gather_scratch(dims)
            else:
                lo, hi = spec[1]
                shape = (hi - lo,) + a.shape[2:]
                scratch = reduce_scratch(dims, *shape)
                scratch += [
                    pltpu.VMEM((dims[1],) + shape, BF), pltpu.SemaphoreType.DMA(())
                ]
            self.outs.append(AN if spec[0] == "gather" else VM)
            self.shapes.append(jax.ShapeDtypeStruct(shape, a.dtype))
            self.scratch += scratch
            self.sizes.append(len(scratch))
        self.count = len(specs)

    def board(self, place, ins, outs, scratch):
        out = []
        for spec, size, a, o in zip(self.specs, self.sizes, ins, outs):
            mine, scratch = (scratch[:size], scratch[size:])
            if spec[0] == "gather":
                out.append(LineGather(place, a.at[spec[1]], o, mine))
            else:
                lo, hi = spec[1]

                def store(value, o=o):
                    o[...] = value.astype(BF)

                terms, sem = mine[4:]
                load = pltpu.make_async_copy(a.at[:, lo:hi], terms, sem)
                load.start()
                out.append(
                    LineReduce(place, lambda t, r=terms: r[t], store, mine[:4], load)
                )
        return (out, scratch)


def each(riders, what):
    for r in riders:
        getattr(r, what)()


def scatter_scratch(dims, *block):
    count = dims[0] * dims[2]
    if dims[0] == 2 and dims[2] == 4:
        near, away, hops, sems = (4, 4, 6, 10)
    else:
        near, away, hops, sems = (1, count - 1, 1, count - 1)
    return [
        pltpu.VMEM((near,) + block, F32),
        pltpu.VMEM((away,) + block, BF),
        pltpu.VMEM((away,) + block, BF),
        pltpu.VMEM((hops,) + block, BF),
        pltpu.SemaphoreType.DMA((sems,)),
        pltpu.SemaphoreType.DMA((sems,)),
    ]


def call(kernel, name, cid, outs, out_specs, in_specs, scratch, args):
    params = pltpu.CompilerParams(
        collective_id=cid, has_side_effects=True, vmem_limit_bytes=VMEM_LIMIT
    )
    return pl.pallas_call(
        kernel,
        name=name,
        out_shape=outs,
        in_specs=in_specs,
        out_specs=out_specs,
        scratch_shapes=scratch,
        compiler_params=params,
    )(*args)


def column_start(dims, part, b, f, y, half):
    ns, nb, nf = dims
    return part * nb * nf * ns * half + ((b * nf + f) * ns + y) * half


def columns_of(ref, q, nf, wide):
    return ref.at[:, q % nf, :, pl.ds(pl.multiple_of((q // nf) * wide, wide), wide)]


def gather_weights_kernel(
    dims, w_ref, wq_ref, wo_ref, wd, small, gup, wdp, gu_first, qo_first, qz, small_all,
    pack, qcol, qh, lsem, ps, pr, ms, mr, qs, qr, *rest
):
    pc = Place(dims)
    ns, nb, nf = dims
    half = wd.shape[1]
    wide = qh.shape[2]
    greet(pc, "all", True)
    qkv = wq_ref.shape[2]
    full = jnp.concatenate([wq_ref[0], wo_ref[0]], axis=1)
    for y in range(ns):
        qcol[y] = full[:, y * wide : (y + 1) * wide]
    across = []
    for d in range(1, ns):
        y = (pc.s + d) % ns
        t = (y, pc.b, pc.f)
        i = 3 * (d - 1)
        across.append(remote(qcol.at[y], qh.at[pc.s], ms.at[i], mr.at[i], t))
        across.append(remote(wd.at[y], wdp.at[pc.s], ms.at[i + 1], mr.at[i + 1], t))
        across.append(remote(small, small_all.at[pc.s], ms.at[i + 2], mr.at[i + 2], t))
    for c in across:
        c.start()
    qh[pc.s] = qcol[pc.s]
    local = [
        pltpu.make_async_copy(wd.at[pc.s], wdp.at[pc.s], lsem.at[0]),
        pltpu.make_async_copy(small, small_all.at[pc.s], lsem.at[1]),
    ]
    for c in local:
        c.start()
    own = pltpu.make_async_copy(pack.at[pc.s, pc.f], gup.at[pc.s, pc.f], lsem.at[2])

    def piece(y, f):
        e = (y * nf + f - pc.me + pc.count) % pc.count
        k = (e + pc.count - 1) % pc.count
        return (
            e,
            remote(pack.at[y, f], gup.at[pc.s, pc.f], ps.at[k], pr.at[k], (y, pc.b, f)),
        )

    for f in range(nf):
        for y in range(ns):
            pieces = []
            for part in range(2):
                for b in range(nb):
                    c0 = column_start(dims, part, b, f, y, half)
                    pieces.append(w_ref[0, :, c0 : c0 + half])
            pack[y, f] = jnp.concatenate(pieces, axis=1)
            e, c = piece(y, f)

            @pl.when(e != 0)
            def _():
                c.start()

    own.start()
    for d in range(ns - 1):
        across[3 * d].wait()
    line_q = LineGather(pc, qh, qz, rest[0:3])
    lines = [
        LineGather(pc, gup.at[0, f], gu_first, rest[3 + 3 * f : 6 + 3 * f], f) for f in range(nf)
    ]
    line_q.start()

    def arrived(y, f):
        e, c = piece(y, f)
        k = (2 * pc.count - e - 1) % pc.count

        @pl.when(e != 0)
        def _():
            remote(pack.at[0, 0], gup.at[y, f], ps.at[k], pr.at[k], (y, pc.b, f)).wait_recv()

    own.wait()
    line_q.service()
    for f in range(nf):
        arrived(0, f)
        lines[f].start()
    line_q.service()
    for line in lines:
        line.service()
    line_q.finish()
    gather = PlaneGather(pc, lambda q: columns_of(qo_first, q, nf, wide), qs, qr)
    columns_of(qo_first, pc.me, nf, wide)[...] = qz[:, 0]
    gather.start()
    for step in range(1, min(6, pc.count)):
        gather.before(step)
    for line in lines:
        line.service()
    for step in range(min(6, pc.count), pc.count):
        gather.before(step)
    gather.finish()
    for y in range(1, ns):
        for f in range(nf):
            arrived(y, f)
    for y in range(ns):
        for f in range(nf):
            e, c = piece(y, f)

            @pl.when(e != 0)
            def _():
                c.wait_send()

    for c in local:
        c.wait()
    for i, c in enumerate(across):
        if i % 3:
            c.wait()
    for line in lines:
        line.finish()


def gather_weights(dims, w, wq, wo, wd, small):
    ns, nb, nf = dims
    count = ns * nf
    half, width = wd.shape[1:]
    dr = wq.shape[1]
    cols = wq.shape[2] + wo.shape[2]
    wide = cols // ns
    two_ff = 2 * nb * half
    sds = jax.ShapeDtypeStruct
    outs = (
        sds((ns, nf, dr, two_ff), BF),
        sds((ns, half, width), BF),
        sds((nb, nf, dr, two_ff), BF),
        sds((nb, nf, dr, cols), BF),
        sds((nb, ns, dr, wide), BF),
        sds((ns,) + small.shape, F32),
    )
    dma = pltpu.SemaphoreType.DMA
    return call(
        functools.partial(gather_weights_kernel, dims),
        "gather_weights",
        0,
        outs,
        [AN, AN, AN, VM, VM, AN],
        [VM, VM, VM, AN, AN],
        [
            pltpu.VMEM((ns, nf, dr, two_ff), BF),
            pltpu.VMEM((ns, dr, wide), BF),
            pltpu.VMEM((ns, dr, wide), BF),
            dma((4,)),
            dma((count,)),
            dma((count,)),
            dma((3 * (ns - 1),)),
            dma((3 * (ns - 1),)),
        ]
        + gather_sems(dims)
        + gather_scratch(dims) * (1 + nf),
        (w, wq, wo, wd, small),
    )


def rms(values):
    return lax.rsqrt(jnp.mean(values * values, axis=0, keepdims=True) + 1e-06)


def column(rows_t, first, count):
    return jnp.concatenate([rows_t[:, k : k + 1] for k in range(first, first + count)], axis=0)


def rows_of(values):
    v = folded(values)
    return jnp.concatenate(
        [v[k : k + 128].T.sum(axis=0, keepdims=True) for k in range(0, v.shape[0], 128)], axis=0
    )


def folded(v):
    out = v[:, :128]
    for k in range(1, v.shape[1] // 128):
        out = out + v[:, k * 128 : (k + 1) * 128]
    return out


def fill_masks(pc, mask, meta_t, query_docs):
    nk, rows = mask.shape[:2]
    key_i = lax.broadcasted_iota(jnp.int32, (rows, rows), 0)
    query_i = lax.broadcasted_iota(jnp.int32, (rows, rows), 1)
    per = rows // 128
    for j in range(nk):
        same = column(meta_t, j * per, per) == query_docs
        if j == 0:
            live = same & (key_i <= query_i)
        else:
            live = same & (key_i < (pc.b - j + 1) * rows)
        mask[j] = jnp.where(live, 0.0, NEG)


def load_qo(qo, w, wo, sems):
    cols = w.shape[1]
    c1 = pltpu.make_async_copy(qo.at[:, 0:cols], w, sems.at[0])
    c2 = pltpu.make_async_copy(qo.at[:, cols : cols + wo.shape[1]], wo, sems.at[1])
    c1.start()
    c2.start()
    return (c1, c2)


def gains_of(small_t, width, qkv):
    n = width // 128
    return (
        column(small_t, 0, n),
        column(small_t, n, n),
        column(small_t, 2 * n, qkv // 128),
    )


def padded_t(v):
    n = v.shape[0]
    return jnp.concatenate([v, jnp.zeros((128 - n, 128), v.dtype)], axis=0).T


def attention_forward_kernel(dims, *args):
    pc = Place(dims)
    riders, gather = attention_forward_part(pc, *args)
    last_blocks(pc, gather)
    gather.finish()
    each(riders, "finish")


def last_blocks(pc, gather):
    for step in range(min(6, pc.count), pc.count):
        gather.before(step)


def attention_forward_part(
    pc, nk, layer, plan, carry, h_ref, small_ref, meta_ref, docs_ref, cos_ref, sin_ref, qo_all,
    *refs
):
    n = plan.count
    block_ref, refs = (refs[0], refs[1:])
    ins, refs = (refs[:n], refs[n:])
    normed_ref, q_ref, kv_ref, lse_ref, mixed_ref, res_ref, n2_ref = refs[:7]
    outs, refs = (refs[7 : 7 + n], refs[7 + n :])
    block_all, refs = (refs[0], refs[1:])
    w, wo, mask, joined, top_own, sum_own, out_own, ssem, rsem, qsem = refs[:10]
    refs = refs[10:]
    width, rows = h_ref.shape
    loads = load_qo(qo_all, w, wo, qsem)
    greet(pc, "mates", True)
    riders, refs = plan.board(pc, ins, outs, refs)
    if carry == "lanes":
        own = block_ref
        slot = lambda q: block_all.at[:, lanes(q, rows)]
    else:
        own = block_ref.at[:, 1]
        slot = lambda q: columns_of(block_all, q, pc.nf, block_ref.shape[3])
    gather = PlaneGather(pc, slot, *refs)
    slot(pc.me)[...] = own[...]
    gather.start()
    each(riders, "start")
    g1, g2, bias = gains_of(padded_t(small_ref[layer]), width, w.shape[1])
    hidden = h_ref[...].astype(BF).astype(F32)
    normed = (hidden * rms(hidden) * g1).astype(BF)
    normed_ref[...] = normed
    fill_masks(pc, mask, padded_t(meta_ref[...]), docs_ref[...])
    loads[0].wait()
    joined[...] = tn(w[...], normed) + bias
    cos_part = cos_ref[...]
    sin_part = sin_ref[...]
    half = HD // 2

    def turned(row):
        u1 = joined[pl.ds(row, half), :]
        u2 = joined[pl.ds(row + half, half), :]
        return (u1 * cos_part - u2 * sin_part, u2 * cos_part + u1 * sin_part)

    for g in range(KVH):
        r1, r2 = turned((H + g) * HD)
        kv_ref[0, g, :half, :] = r1.astype(BF)
        kv_ref[0, g, half:, :] = r2.astype(BF)
        v0 = (H + KVH + g) * HD
        kv_ref[0, KVH + g] = joined[v0 : v0 + HD, :].astype(BF)
    sends = [
        remote(kv_ref.at[0], kv_ref.at[j], ssem.at[j - 1], rsem.at[j - 1], pc.along(j))
        for j in range(1, nk)
    ]
    for c in sends:
        c.start()
    scale = HD**-0.5
    for head in range(H):
        r1, r2 = turned(head * HD)
        q_ref[head, :half, :] = (r1 * scale).astype(BF)
        q_ref[head, half:, :] = (r2 * scale).astype(BF)
    for g in range(KVH):
        keys = kv_ref[0, g].T
        values = kv_ref[0, KVH + g]

        def own_keys(i, carried):
            head = g * GROUP + i
            x = nn(keys, q_ref[head]) + mask[0]
            top = x.max(axis=0, keepdims=True)
            e = jnp.exp(x - top)
            top_own[head] = top
            sum_own[head] = e.sum(axis=0, keepdims=True)
            out_own[head] = nn(values, e.astype(BF))
            return carried

        lax.fori_loop(0, GROUP, own_keys, 0)
    for c in sends:
        c.wait()
    each(riders, "service")
    for g in range(KVH):
        keys = [kv_ref[j, g].T for j in range(1, nk)]
        values = [kv_ref[j, KVH + g] for j in range(1, nk)]

        def one_head(i, carried):
            head = g * GROUP + i
            q = q_ref[head]
            s = [nn(keys[j], q) + mask[j + 1] for j in range(nk - 1)]
            first = top_own[head]
            top = first
            for x in s:
                top = jnp.maximum(top, x.max(axis=0, keepdims=True))
            e = [jnp.exp(x - top) for x in s]
            fade = jnp.exp(first - top)
            total = sum_own[head] * fade
            out = out_own[head] * fade
            for j in range(nk - 1):
                total = total + e[j].sum(axis=0, keepdims=True)
                out = out + nn(values[j], e[j].astype(BF))
            lse_ref[head] = top + jnp.log(total)
            mixed_ref[head] = (out / total).astype(BF)
            return carried

        lax.fori_loop(0, GROUP, one_head, 0)
        if g == 0:
            for step in range(1, min(6, pc.count)):
                gather.before(step)
        else:
            each(riders, "service")
    mixed = mixed_ref[...].reshape(H * HD, rows)
    loads[1].wait()
    residual = hidden + tn(wo[...], mixed)
    res_ref[...] = residual
    n2_ref[...] = (residual * rms(residual) * g2).astype(BF)
    return (riders, gather)


def attention_scratch(dims, nk, width, rows, qkv):
    dma = pltpu.SemaphoreType.DMA
    return [
        pltpu.VMEM((width, qkv), BF),
        pltpu.VMEM((width, width), BF),
        pltpu.VMEM((nk, rows, rows), F32),
        pltpu.VMEM((qkv, rows), F32),
        pltpu.VMEM((H, 1, rows), F32),
        pltpu.VMEM((H, 1, rows), F32),
        pltpu.VMEM((H, HD, rows), F32),
        dma((nk - 1,)),
        dma((nk - 1,)),
        dma((2,)),
    ]


def attention_forward(dims, nk, cid, layer, hidden, small, meta, docs, cos_part, sin_part, qo_all,
                      plan, carry, block):
    width, rows = hidden.shape
    ns, nb, nf = dims
    count = ns * nf
    qkv = qo_all.shape[1] - width
    sds = jax.ShapeDtypeStruct
    outs = [
        sds((width, rows), BF),
        sds((H, HD, rows), BF),
        sds((nk, 2 * KVH, HD, rows), BF),
        sds((H, 1, rows), F32),
        sds((H, HD, rows), BF),
        sds((width, rows), F32),
        sds((width, rows), BF),
    ] + plan.shapes
    if carry == "lanes":
        outs.append(sds((width, count * rows), BF))
    else:
        outs.append(sds((nb, nf, block.shape[2], ns * block.shape[3]), BF))
    out = call(
        functools.partial(attention_forward_kernel, dims, nk, layer, plan, carry),
        "attention_forward",
        cid,
        tuple(outs),
        [VM] * 7 + plan.outs + [VM],
        [VM] * 6 + [AN, VM] + plan.places,
        attention_scratch(dims, nk, width, rows, qkv)
        + plan.scratch
        + gather_sems(dims),
        (hidden, small, meta, docs, cos_part, sin_part, qo_all, block, *plan.arrays),
    )
    return (out[:7], out[7:])


def attention_backward_kernel(
    dims, nk, layer, plan, carry, g_ref, small_ref, meta_ref, docs_ref, cos_ref, sin_ref,
    h_ref, normed_ref, q_ref, kv_ref, lse_ref, mixed_ref, qo_all, *refs
):
    n = plan.count
    parts_ref, more_ref, refs = (refs[0], refs[1], refs[2:])
    ins, refs = (refs[:n], refs[n:])
    gh_ref, dqo_ref, dsmall_ref = refs[:3]
    outs, refs = (refs[3 : 3 + n], refs[3 + n :])
    out_ref, refs = (refs[0], refs[1:])
    if carry == "columns":
        rows_ref, refs = (refs[0], refs[1:])
    w, wo, mask, dmix, dkv, delta, dq_some, out_kv, in_kv, gj, ssem, rsem, qsem = refs[:13]
    refs = refs[13:]
    pc = Place(dims)
    width, rows = h_ref.shape
    qkv = w.shape[1]
    loads = load_qo(qo_all, w, wo, qsem)
    riders, refs = plan.board(pc, ins, outs, refs)
    if carry == "columns":
        held, held_sem = refs[7:]
        coming = pltpu.make_async_copy(parts_ref, held, held_sem)
        coming.start()
    greet(pc, "all" if carry == "columns" else "mates", True)
    if carry == "columns":
        part = lambda q: columns_of(held, q, pc.nf, out_ref.shape[2])
        hand_out = RowSends(pc, 1, rows_ref, refs[4:7])
        coming.wait()
    else:
        part = lambda q: parts_ref.at[q]
    scatter = ReadyScatter(pc, part, *refs[:4])
    scatter.start()
    each(riders, "start")
    g1 = column(padded_t(small_ref[layer]), 0, width // 128)
    fill_masks(pc, mask, padded_t(meta_ref[...]), docs_ref[...])
    grl = g_ref[...].astype(BF)
    loads[1].wait()
    dmix[...] = nn(wo[...], grl).astype(BF).reshape(dmix.shape)
    dqo_ref[:, qkv:] = nt(mixed_ref[...].reshape(H * HD, rows), grl).astype(BF)
    scatter.diagonal()
    scatter.early()
    if carry == "columns":
        for f in range(pc.nf):
            hand_out.start(f, more_ref.at[f])
    cos_part = cos_ref[...]
    sin_part = sin_ref[...]
    half = HD // 2
    scale = HD**-0.5
    dkv[...] = jnp.zeros_like(dkv)

    def unturned(d1, d2):
        return (d1 * cos_part + d2 * sin_part, d2 * cos_part - d1 * sin_part)

    def of_block(j, g, head, keys, keys_t, values):
        q = q_ref[head]
        do = dmix[head]
        p = jnp.exp(nn(keys, q) + mask[j] - lse_ref[head])
        ds = (p * (nn(values, do) - delta[head])).astype(BF)
        dkv[j, g] += nt(q, ds)
        dkv[j, KVH + g] += nt(do, p.astype(BF))
        return nn(keys_t, ds)

    for g in range(KVH):
        keys_t = [kv_ref[j, g] for j in range(1, nk)]
        keys = [k.T for k in keys_t]
        values = [kv_ref[j, KVH + g].T for j in range(1, nk)]

        def earlier(i, carried):
            head = g * GROUP + i
            delta[head] = (dmix[head].astype(F32) * mixed_ref[head].astype(F32)).sum(
                axis=0, keepdims=True
            )
            dq = of_block(1, g, head, keys[0], keys_t[0], values[0])
            for j in range(2, nk):
                dq = dq + of_block(j, g, head, keys[j - 1], keys_t[j - 1], values[j - 1])
            dq_some[head] = dq
            return carried

        lax.fori_loop(0, GROUP, earlier, 0)
        if g == 0:
            scatter.late()
        if g == 1 or carry == "sum":
            each(riders, "service")
    for j in range(1, nk):
        out_kv[j - 1] = dkv[j].astype(BF)
    sends = [
        remote(out_kv.at[j - 1], in_kv.at[j - 1], ssem.at[j - 1], rsem.at[j - 1],
               pc.along(pc.nb - j))
        for j in range(1, nk)
    ]
    for c in sends:
        c.start()
    for g in range(KVH):
        keys_t = kv_ref[0, g]
        keys = keys_t.T
        values = kv_ref[0, KVH + g].T

        def own_keys(i, carried):
            head = g * GROUP + i
            dq = (dq_some[head] + of_block(0, g, head, keys, keys_t, values)) * scale
            r1, r2 = unturned(dq[:half], dq[half:])
            gj[pl.ds(pl.multiple_of(head * HD, HD), half), :] = r1.astype(BF)
            gj[pl.ds(pl.multiple_of(head * HD + half, half), half), :] = r2.astype(BF)
            return carried

        lax.fori_loop(0, GROUP, own_keys, 0)
    for c in sends:
        c.wait()
    each(riders, "service")
    own = dkv[0]
    for j in range(1, nk):
        own = own + in_kv[j - 1].astype(F32)
    for g in range(KVH):
        r1, r2 = unturned(own[g, :half], own[g, half:])
        k0 = (H + g) * HD
        gj[k0 : k0 + half, :] = r1.astype(BF)
        gj[k0 + half : k0 + HD, :] = r2.astype(BF)
        v0 = (H + KVH + g) * HD
        gj[v0 : v0 + HD, :] = own[KVH + g].astype(BF)
    gjv = gj[...]
    n1 = width // 128
    dsmall_ref[n1 : n1 + qkv // 128, :] = rows_of(gjv.astype(F32))
    loads[0].wait()
    dqo_ref[:, :qkv] = nt(normed_ref[...], gjv).astype(BF)
    gn = nn(w[...], gjv)
    hidden = h_ref[...].astype(BF).astype(F32)
    scale_one = rms(hidden)
    unit = hidden * scale_one
    dsmall_ref[:n1, :] = rows_of(gn * unit)
    u = gn * g1
    gh_ref[...] = g_ref[...] + scale_one * (u - unit * jnp.mean(u * unit, axis=0, keepdims=True))

    def store(total):
        if carry == "columns":
            out_ref[...] = total.astype(BF)
        else:
            out_ref[...] = more_ref[...] + total

    scatter.finish(store)
    if carry == "columns":
        hand_out.finish(more_ref.at[0])
    each(riders, "finish")


def attention_backward(dims, nk, cid, layer, g, small, meta, docs, cos_part, sin_part, hidden,
                       normed, q, kv, lse, mixed, qo_all, plan, carry, late):
    width, rows = hidden.shape
    qkv = qo_all.shape[1] - width
    sds = jax.ShapeDtypeStruct
    outs = [
        sds((width, rows), F32),
        sds((width, qkv + width), BF),
        sds(((width + qkv) // 128, 128), F32),
    ] + plan.shapes
    dma = pltpu.SemaphoreType.DMA
    block = (2 * KVH, HD, rows)
    if carry == "columns":
        summed = (dims[1], late[0].shape[2], late[0].shape[3] // dims[0])
        outs += [sds(summed, BF), sds((dims[0] * dims[2],) + late[1].shape[1:], BF)]
        places = [VM, AN]
    else:
        summed = (width, rows)
        outs.append(sds(summed, F32))
        places = [VM]
    out = call(
        functools.partial(attention_backward_kernel, dims, nk, layer, plan, carry),
        "attention_backward",
        cid,
        tuple(outs),
        [VM] * 3 + plan.outs + places,
        [VM] * 12 + [AN] + [AN if carry == "columns" else VM, VM] + plan.places,
        [
            pltpu.VMEM((width, qkv), BF),
            pltpu.VMEM((width, width), BF),
            pltpu.VMEM((nk, rows, rows), F32),
            pltpu.VMEM((H, HD, rows), BF),
            pltpu.VMEM((nk,) + block, F32),
            pltpu.VMEM((H, 1, rows), F32),
            pltpu.VMEM((H, HD, rows), F32),
            pltpu.VMEM((nk - 1,) + block, BF),
            pltpu.VMEM((nk - 1,) + block, BF),
            pltpu.VMEM((qkv, rows), BF),
            dma((nk - 1,)),
            dma((nk - 1,)),
            dma((2,)),
        ]
        + plan.scratch
        + scatter_scratch(dims, *summed)[2:]
        + (
            row_scratch(dims) + [pltpu.VMEM(late[0].shape, BF), dma(())]
            if carry == "columns"
            else []
        ),
        (g, small, meta, docs, cos_part, sin_part, hidden, normed, q, kv, lse, mixed, qo_all,
         *late, *plan.arrays),
    )
    return (out[:3], out[3:])


def sequence_of(pc):
    if pc.two_level:
        return ((0, 1, 2, 3, 6, 7, 4, 5), 5, 7)
    return (tuple(range(pc.count)), pc.count - 1, pc.count - 1)


def lanes(slot, rows):
    return pl.ds(pl.multiple_of(slot * rows, rows), rows)


def transpose_into(dst, src):
    cols = src.shape[1]
    for c0 in range(0, cols, 128):
        c1 = min(c0 + 128, cols)
        dst[c0:c1, :] = src[:, c0:c1].T


def feed_forward_kernel(dims, *args):
    pc = Place(dims)
    feed_forward_part(pc, lambda: greet(pc, "mates", True), lambda: None, *args)


def feed_forward_part(pc, enter, ready, plan, x_ref, res_ref, wgu_ref, wd_ref, *refs):
    n = plan.count
    ins, refs = (refs[:n], refs[n:])
    out_ref, x_out, gu_out = refs[:3]
    outs, refs = (refs[3 : 3 + n], refs[3 + n :])
    x_all, gu_all, lsem, wgu_t, wd_t, gu, inner, near, away, back, hop, ss, sr, gs, gr = refs[:15]
    width, rows = x_ref.shape
    ff = wd_ref.shape[0]
    riders, _ = plan.board(pc, ins, outs, refs[15:])
    enter()
    gather = PlaneGather(pc, lambda q: x_all.at[:, lanes(q, rows)], gs, gr)
    scatter = PlaneScatter(pc, near, away, back, hop, ss, sr)
    x_all[:, lanes(pc.me, rows)] = x_ref[...]
    gather.start()
    ready()
    each(riders, "start")
    transpose_into(wgu_t, wgu_ref)
    transpose_into(wd_t, wd_ref)
    sequence, diagonal_at, early_at = sequence_of(pc)
    chunk = 32 if ff % 32 == 0 else 16

    def step_body(turn, carry):
        step = pick(turn, sequence)

        for k in range(pc.count):
            @pl.when(step == k)
            def _():
                gather.before(k)

        slot = pick(step, gather.order)
        sl = lanes(slot, rows)
        gu[...] = nn(wgu_t[...], x_all[:, sl])

        def act(i, c):
            r = pl.multiple_of(i * chunk, chunk)
            gate = gu[pl.ds(r, chunk), :]
            up = gu[pl.ds(ff + r, chunk), :]
            gu_all[pl.ds(r, chunk), sl] = gate.astype(BF)
            gu_all[pl.ds(ff + r, chunk), sl] = up.astype(BF)
            inner[pl.ds(r, chunk), :] = (gate * jax.nn.sigmoid(gate) * up).astype(BF)
            return c

        lax.fori_loop(0, ff // chunk, act, 0)
        scatter.put(step, nn(wd_t[...], inner[...]))

        @pl.when(turn == 3)
        def _():
            each(riders, "service")

        @pl.when(turn == diagonal_at)
        def _():
            scatter.diagonal()

        @pl.when(turn == early_at)
        def _():
            scatter.early()

        return carry

    lax.fori_loop(0, pc.count, step_body, 0)
    leaving = [
        pltpu.make_async_copy(gu_all, gu_out, lsem.at[0]),
        pltpu.make_async_copy(x_all, x_out, lsem.at[1]),
    ]
    each(leaving, "start")
    each(riders, "service")

    def store(total):
        out_ref[...] = res_ref[...] + total

    scatter.result(store)
    gather.finish()
    each(leaving, "wait")
    each(riders, "finish")


def feed_forward(dims, cid, x, residual, wgu, wd, plan):
    width, rows = x.shape
    count = dims[0] * dims[2]
    two_ff, ff = (wgu.shape[1], wd.shape[0])
    sds = jax.ShapeDtypeStruct
    dma = pltpu.SemaphoreType.DMA
    out = call(
        functools.partial(feed_forward_kernel, dims, plan),
        "feed_forward",
        cid,
        (
            sds((width, rows), F32),
            sds((width, count * rows), BF),
            sds((two_ff, count * rows), BF),
            *plan.shapes,
        ),
        [VM, AN, AN] + plan.outs,
        [VM] * 4 + plan.places,
        [
            pltpu.VMEM((width, count * rows), BF),
            pltpu.VMEM((two_ff, count * rows), BF),
            dma((2,)),
            pltpu.VMEM((two_ff, width), BF),
            pltpu.VMEM((width, ff), BF),
            pltpu.VMEM((two_ff, rows), F32),
            pltpu.VMEM((ff, rows), BF),
        ]
        + scatter_scratch(dims, width, rows)
        + gather_sems(dims)
        + plan.scratch,
        (x, residual, wgu, wd, *plan.arrays),
    )
    return (out[:3], out[3:])


def feed_backward_kernel(
    dims, layer, plan, g_ref, res_ref, x_in, gu_in, wgu_ref, wd_ref, small_ref, *refs
):
    n = plan.count
    ins, refs = (refs[:n], refs[n:])
    gr_ref, dwgu_ref, dwd_ref, dsmall_ref = refs[:4]
    outs, refs = (refs[4 : 4 + n], refs[4 + n :])
    x_all, gu_all, lsem, g_all, inner, ggu, gi, near, away, back, hop, ss, sr, gs, gr = refs[:15]
    coming = [
        pltpu.make_async_copy(gu_in, gu_all, lsem.at[0]),
        pltpu.make_async_copy(x_in, x_all, lsem.at[1]),
    ]
    each(coming, "start")
    pc = Place(dims)
    width, rows = g_ref.shape
    ff = wd_ref.shape[0]
    riders, _ = plan.board(pc, ins, outs, refs[15:])
    greet(pc, "mates", n > 0)
    gather = PlaneGather(pc, lambda q: g_all.at[:, lanes(q, rows)], gs, gr)
    scatter = PlaneScatter(pc, near, away, back, hop, ss, sr)
    g_all[:, lanes(pc.me, rows)] = g_ref[...].astype(BF)
    gather.start()
    each(riders, "start")
    coming[0].wait()
    sequence, diagonal_at, early_at = sequence_of(pc)
    chunk = 32 if ff % 32 == 0 else 16

    def step_body(turn, carry):
        step = pick(turn, sequence)

        for k in range(pc.count):
            @pl.when(step == k)
            def _():
                gather.before(k)

        slot = pick(step, gather.order)
        sl = lanes(slot, rows)
        gi[...] = nn(wd_ref[...], g_all[:, sl])

        def act(i, c):
            r = pl.multiple_of(i * chunk, chunk)
            gate = gu_all[pl.ds(r, chunk), sl].astype(F32)
            up = gu_all[pl.ds(ff + r, chunk), sl].astype(F32)
            grad = gi[pl.ds(r, chunk), :]
            sig = jax.nn.sigmoid(gate)
            silu = gate * sig
            inner[pl.ds(r, chunk), sl] = (silu * up).astype(BF)
            ggu[pl.ds(r, chunk), sl] = (grad * up * sig * (1.0 + gate * (1.0 - sig))).astype(BF)
            ggu[pl.ds(ff + r, chunk), sl] = (grad * silu).astype(BF)
            return c

        lax.fori_loop(0, ff // chunk, act, 0)
        scatter.put(step, nn(wgu_ref[...], ggu[:, sl]))

        @pl.when(turn == 3)
        def _():
            each(riders, "service")

        @pl.when(turn == diagonal_at)
        def _():
            scatter.diagonal()

        @pl.when(turn == early_at)
        def _():
            scatter.early()

        return carry

    lax.fori_loop(0, pc.count, step_body, 0)
    each(riders, "service")
    dwd_ref[...] = nt(inner[...], g_all[...]).astype(BF)
    scatter.late()
    coming[1].wait()
    part = width // 2
    for r in range(2):
        dwgu_ref[r * part : (r + 1) * part, :] = nt(
            x_all[r * part : (r + 1) * part, :], ggu[...]
        ).astype(BF)

    def store(total):
        residual = res_ref[...]
        scale_two = rms(residual)
        unit = residual * scale_two
        n1 = width // 128
        dsmall_ref[...] = rows_of(total * unit)
        u = total * column(padded_t(small_ref[layer]), n1, n1)
        gr_ref[...] = g_ref[...].astype(BF).astype(F32) + scale_two * (
            u - unit * jnp.mean(u * unit, axis=0, keepdims=True)
        )

    scatter.finish(store)
    gather.finish()
    each(riders, "finish")


def feed_backward(dims, cid, layer, g, residual, x_all, gu_all, wgu, wd, small, plan):
    width, rows = g.shape
    count = dims[0] * dims[2]
    two_ff, ff = (wgu.shape[1], wd.shape[0])
    sds = jax.ShapeDtypeStruct
    dma = pltpu.SemaphoreType.DMA
    out = call(
        functools.partial(feed_backward_kernel, dims, layer, plan),
        "feed_backward",
        cid,
        (
            sds((width, rows), F32),
            sds(wgu.shape, BF),
            sds(wd.shape, BF),
            sds((width // 128, 128), F32),
            *plan.shapes,
        ),
        [VM] * 4 + plan.outs,
        [VM, VM, AN, AN, VM, VM, VM] + plan.places,
        [
            pltpu.VMEM((width, count * rows), BF),
            pltpu.VMEM((two_ff, count * rows), BF),
            dma((2,)),
            pltpu.VMEM((width, count * rows), BF),
            pltpu.VMEM((ff, count * rows), BF),
            pltpu.VMEM((two_ff, count * rows), BF),
            pltpu.VMEM((ff, rows), F32),
        ]
        + scatter_scratch(dims, width, rows)
        + gather_sems(dims)
        + plan.scratch,
        (g, residual, x_all, gu_all, wgu, wd, small, *plan.arrays),
    )
    return (out[:4], out[4:])


def feed_both_kernel(dims, *args):
    pc = Place(dims)
    feed_both_part(pc, lambda: greet(pc, "mates", False), lambda: None, *args)


def feed_both_part(
    pc, enter, ready, layer, x_ref, res_ref, g_ref, g_all, wgu_ref, wd_ref, small_ref,
    gr_ref, dwgu_ref, dwd_ref, dsmall_ref, parts_ref,
    x_all, inner, ggu, wgu_t, wd_t, gu, gi, near, away, back, hop, ss, sr, gs, gr,
):
    width, rows = g_ref.shape
    ff = wd_ref.shape[0]
    enter()
    gather = PlaneGather(pc, lambda q: x_all.at[:, lanes(q, rows)], gs, gr)
    scatter = PlaneScatter(pc, near, away, back, hop, ss, sr)
    x_all[:, lanes(pc.me, rows)] = x_ref[...]
    gather.start()
    ready()
    transpose_into(wgu_t, wgu_ref)
    transpose_into(wd_t, wd_ref)
    sequence, diagonal_at, early_at = sequence_of(pc)
    chunk = 32 if ff % 32 == 0 else 16

    def step_body(turn, carry):
        step = pick(turn, sequence)

        for k in range(pc.count):
            @pl.when(step == k)
            def _():
                gather.before(k)

        slot = pick(step, gather.order)
        sl = lanes(slot, rows)
        gu[...] = nn(wgu_t[...], x_all[:, sl])
        gi[...] = nn(wd_ref[...], g_all[:, sl])

        def act(i, c):
            r = pl.multiple_of(i * chunk, chunk)
            gate = gu[pl.ds(r, chunk), :]
            up = gu[pl.ds(ff + r, chunk), :]
            grad = gi[pl.ds(r, chunk), :]
            sig = jax.nn.sigmoid(gate)
            silu = gate * sig
            inner[pl.ds(r, chunk), sl] = (silu * up).astype(BF)
            ggu[pl.ds(r, chunk), sl] = (grad * up * sig * (1.0 + gate * (1.0 - sig))).astype(BF)
            ggu[pl.ds(ff + r, chunk), sl] = (grad * silu).astype(BF)
            return c

        lax.fori_loop(0, ff // chunk, act, 0)
        scatter.put(step, nn(wgu_ref[...], ggu[:, sl]))

        @pl.when(turn == diagonal_at)
        def _():
            scatter.diagonal()

        @pl.when(turn == early_at)
        def _():
            scatter.early()

        parts_ref[slot] = nn(wd_t[...], inner[:, sl]).astype(BF)
        return carry

    lax.fori_loop(0, pc.count, step_body, 0)
    dwd_ref[...] = nt(inner[...], g_all[...]).astype(BF)
    scatter.late()
    part = width // 2
    for r in range(2):
        dwgu_ref[r * part : (r + 1) * part, :] = nt(
            x_all[r * part : (r + 1) * part, :], ggu[...]
        ).astype(BF)

    def store(total):
        residual = res_ref[...]
        scale_two = rms(residual)
        unit = residual * scale_two
        n1 = width // 128
        dsmall_ref[...] = rows_of(total * unit)
        u = total * column(padded_t(small_ref[layer]), n1, n1)
        gr_ref[...] = g_ref[...].astype(BF).astype(F32) + scale_two * (
            u - unit * jnp.mean(u * unit, axis=0, keepdims=True)
        )

    scatter.finish(store)
    gather.finish()


def feed_both(dims, cid, layer, x, residual, g, g_all, wgu, wd, small):
    width, rows = g.shape
    count = dims[0] * dims[2]
    two_ff, ff = (wgu.shape[1], wd.shape[0])
    sds = jax.ShapeDtypeStruct
    dma = pltpu.SemaphoreType.DMA
    return call(
        functools.partial(feed_both_kernel, dims, layer),
        "feed_both",
        cid,
        (
            sds((width, rows), F32),
            sds(wgu.shape, BF),
            sds(wd.shape, BF),
            sds((width // 128, 128), F32),
            sds((count, width, rows), BF),
        ),
        [VM] * 5,
        [VM] * 7,
        [
            pltpu.VMEM((width, count * rows), BF),
            pltpu.VMEM((ff, count * rows), BF),
            pltpu.VMEM((two_ff, count * rows), BF),
            pltpu.VMEM((two_ff, width), BF),
            pltpu.VMEM((width, ff), BF),
            pltpu.VMEM((two_ff, rows), F32),
            pltpu.VMEM((ff, rows), F32),
        ]
        + scatter_scratch(dims, width, rows)
        + gather_sems(dims),
        (x, residual, g, g_all, wgu, wd, small),
    )


def wait_for_weights(pc, riders, gather, wd_all, pieces, wd, sem, others):
    last_blocks(pc, gather)
    each(riders, "finish")
    load = pltpu.make_async_copy(wd_all, pieces, sem)
    load.start()
    each(others, "wait")
    load.wait()
    half = pieces.shape[1]
    for t in range(pc.nb):
        wd[t * half : (t + 1) * half, :] = pieces[t]
    gather.finish()


def lower_kernel(dims, nk, plan_a, plan_f, *refs):
    pc = Place(dims)
    a_in, wgu_in, refs = (refs[:9], refs[9], refs[10:])
    f_in, refs = (refs[: plan_f.count], refs[plan_f.count :])
    a_out, wd_all, qo_next, refs = (refs[:6], refs[6], refs[7], refs[8:])
    f_out, refs = (refs[: 3 + plan_f.count], refs[3 + plan_f.count :])
    n2, wgu, pieces, wd, wsem, dsem, refs = (*refs[:6], refs[6:])
    a_scratch, f_scratch = (refs[: 10 + len(plan_a.scratch) + 2], refs[10 + len(plan_a.scratch) + 2 :])
    load = pltpu.make_async_copy(wgu_in, wgu, wsem)
    load.start()
    riders, gather = attention_forward_part(
        pc, nk, 0, plan_a, "columns", *a_in, *a_out, n2, wd_all, qo_next, *a_scratch
    )
    feed_forward_part(
        pc,
        lambda: None,
        lambda: wait_for_weights(pc, riders, gather, wd_all, pieces, wd, dsem, [load]),
        plan_f, n2, a_out[5], wgu, wd, *f_in, *f_out, *f_scratch,
    )


def lower_layer(dims, nk, cid, hidden, small, meta, docs, cos_part, sin_part, qo, plan_a, block,
                wgu, plan_f):
    ns, nb, nf = dims
    width, rows = hidden.shape
    count = ns * nf
    qkv = qo.shape[1] - width
    two_ff = wgu.shape[1]
    ff = two_ff // 2
    sds = jax.ShapeDtypeStruct
    dma = pltpu.SemaphoreType.DMA
    outs = [
        sds((width, rows), BF),
        sds((H, HD, rows), BF),
        sds((nk, 2 * KVH, HD, rows), BF),
        sds((H, 1, rows), F32),
        sds((H, HD, rows), BF),
        sds((width, rows), F32),
        *plan_a.shapes,
        sds((nb, nf, block.shape[2], ns * block.shape[3]), BF),
        sds((width, rows), F32),
        sds((width, count * rows), BF),
        sds((two_ff, count * rows), BF),
        *plan_f.shapes,
    ]
    out = call(
        functools.partial(lower_kernel, dims, nk, plan_a, plan_f),
        "lower_layer",
        cid,
        tuple(outs),
        [VM] * 6 + plan_a.outs + [VM] + [VM, AN, AN] + plan_f.outs,
        [VM] * 6 + [AN, VM] + plan_a.places + [AN] + plan_f.places,
        [
            pltpu.VMEM((width, rows), BF),
            pltpu.VMEM(wgu.shape, BF),
            pltpu.VMEM((nb, ff // nb, width), BF),
            pltpu.VMEM((ff, width), BF),
            dma(()),
            dma(()),
        ]
        + attention_scratch(dims, nk, width, rows, qkv)
        + plan_a.scratch
        + gather_sems(dims)
        + [
            pltpu.VMEM((width, count * rows), BF),
            pltpu.VMEM((two_ff, count * rows), BF),
            dma((2,)),
            pltpu.VMEM((two_ff, width), BF),
            pltpu.VMEM((width, ff), BF),
            pltpu.VMEM((two_ff, rows), F32),
            pltpu.VMEM((ff, rows), BF),
        ]
        + scatter_scratch(dims, width, rows)
        + gather_sems(dims)
        + plan_f.scratch,
        (hidden, small, meta, docs, cos_part, sin_part, qo, block, *plan_a.arrays, wgu,
         *plan_f.arrays),
    )
    return (out[:6], out[6], out[7], out[8:11], out[11:])


def upper_kernel(dims, nk, plan, *refs):
    pc = Place(dims)
    a_in, g_ref, wgu_in, refs = (refs[:9], refs[9], refs[10], refs[11:])
    a_out, wd_all, f_out, refs = (refs[:6], refs[6], refs[7:12], refs[12:])
    n2, g_all, wgu, pieces, wd, wsem, dsem, refs = (*refs[:7], refs[7:])
    a_scratch, f_scratch = (refs[: 10 + len(plan.scratch) + 2], refs[10 + len(plan.scratch) + 2 :])
    load = pltpu.make_async_copy(wgu_in, wgu, wsem)
    load.start()
    riders, gather = attention_forward_part(
        pc, nk, 1, plan, "lanes", *a_in, *a_out, n2, wd_all, g_all, *a_scratch
    )
    feed_both_part(
        pc,
        lambda: None,
        lambda: wait_for_weights(pc, riders, gather, wd_all, pieces, wd, dsem, [load]),
        1, n2, a_out[5], g_ref, g_all, wgu, wd, a_in[1], *f_out, *f_scratch,
    )


def upper_layer(dims, nk, cid, hidden, small, meta, docs, cos_part, sin_part, qo, plan, block, g,
                wgu):
    ns, nb, nf = dims
    width, rows = hidden.shape
    count = ns * nf
    qkv = qo.shape[1] - width
    two_ff = wgu.shape[1]
    ff = two_ff // 2
    sds = jax.ShapeDtypeStruct
    dma = pltpu.SemaphoreType.DMA
    outs = [
        sds((width, rows), BF),
        sds((H, HD, rows), BF),
        sds((nk, 2 * KVH, HD, rows), BF),
        sds((H, 1, rows), F32),
        sds((H, HD, rows), BF),
        sds((width, rows), F32),
        *plan.shapes,
        sds((width, rows), F32),
        sds(wgu.shape, BF),
        sds((ff, width), BF),
        sds((width // 128, 128), F32),
        sds((count, width, rows), BF),
    ]
    out = call(
        functools.partial(upper_kernel, dims, nk, plan),
        "upper_layer",
        cid,
        tuple(outs),
        [VM] * 6 + plan.outs + [VM] * 5,
        [VM] * 6 + [AN, VM] + plan.places + [VM, AN],
        [
            pltpu.VMEM((width, rows), BF),
            pltpu.VMEM((width, count * rows), BF),
            pltpu.VMEM(wgu.shape, BF),
            pltpu.VMEM((nb, ff // nb, width), BF),
            pltpu.VMEM((ff, width), BF),
            dma(()),
            dma(()),
        ]
        + attention_scratch(dims, nk, width, rows, qkv)
        + plan.scratch
        + gather_sems(dims)
        + [
            pltpu.VMEM((width, count * rows), BF),
            pltpu.VMEM((ff, count * rows), BF),
            pltpu.VMEM((two_ff, count * rows), BF),
            pltpu.VMEM((two_ff, width), BF),
            pltpu.VMEM((width, ff), BF),
            pltpu.VMEM((two_ff, rows), F32),
            pltpu.VMEM((ff, rows), F32),
        ]
        + scatter_scratch(dims, width, rows)
        + gather_sems(dims),
        (hidden, small, meta, docs, cos_part, sin_part, qo, block, *plan.arrays, g, wgu),
    )
    return (out[:6], out[7:])


def reduce_kernel(
    dims, qo, terms, sa0, sa1, sb0, sb1, wd1, gu0a, gu0, wd0,
    qo_out, small_out, gu_got, wd_got,
    held, rest_gu, gsum, wsum, small, sm_in, sm_mid, sm_line, z_out, mine, give,
    lsem, ws, wr, ls, lr, zs, zr, *rest
):
    pc = Place(dims)
    ns, nb, nf = dims
    coming = pltpu.make_async_copy(qo, held, lsem.at[1])
    coming.start()
    cut = gu0a.shape[0]
    coming_gu = pltpu.make_async_copy(gu0.at[:, cut:nf], rest_gu, lsem.at[2])
    coming_gu.start()
    n1 = sb0.shape[0]
    per = small.shape[0] // ns
    nr = sa0.shape[0] + n1
    small[...] = jnp.zeros_like(small)
    for l, (a, g) in enumerate(((sa0, sb0), (sa1, sb1))):
        small[l * per : l * per + n1] = a[0:n1]
        small[l * per + n1 : l * per + 2 * n1] = g[...]
        small[l * per + 2 * n1 : l * per + nr] = a[n1 : a.shape[0]]
    greet(pc, "all", True)

    def keep(value):
        wsum[...] = value.astype(BF)

    def keep_of(l):
        def store(value):
            mine[l] = value

        return store

    line = LineReduce(pc, lambda t: wd0[t], keep, rest[0:4])
    ends = [
        LineReduce(pc, lambda t: z_out[t], keep_of(0), rest[4:8]),
        LineReduce(pc, lambda t: terms[t], keep_of(1), rest[8:12]),
    ]
    def keep_gu(value):
        gsum[...] = value.astype(BF)

    line_gu = LineReduce(pc, lambda t: rest_gu[t], keep_gu, rest[19:23])
    ends[1].start()
    coming_gu.wait()
    line_gu.start()
    line.start()
    scatter = ReadyScatter(
        pc, lambda q: columns_of(held, q, nf, z_out.shape[2]), *rest[15:19]
    )
    coming.wait()
    scatter.start()
    smalls = [
        remote(small, sm_in.at[e - 1], ls.at[e - 1], lr.at[e - 1], pc.plane(e))
        for e in range(1, pc.count)
    ]
    for c in smalls:
        c.start()
    scatter.diagonal()
    scatter.early()
    hand_out = RowSends(pc, 0, gu_got, rest[12:15])
    for f in range(cut):
        hand_out.start(f, gu0a.at[f])

    def split(l, ref):
        @pl.when(pc.s == l)
        def _():
            pltpu.make_async_copy(ref, wd_got.at[l], lsem.at[0]).start()

        @pl.when(pc.s != l)
        def _():
            remote(ref, wd_got.at[pc.s], ws.at[0], wr.at[0], (l, pc.b, pc.f)).start()

    split(1, wd1)
    ends[1].service()
    line_gu.service()
    line.service()
    scatter.late()
    ends[1].service()
    total = small[...]
    for e, c in enumerate(smalls):
        c.wait()
        total = total + sm_in[e]
    sm_mid[...] = total
    lines = [
        remote(sm_mid, sm_line.at[d - 1], zs.at[d - 1], zr.at[d - 1], pc.along(d))
        for d in range(1, nb)
    ]
    for c in lines:
        c.start()
    line_gu.service()
    line.service()

    def store(value):
        z_out[...] = value.astype(BF)

    scatter.finish(store)
    ends[0].start()
    ends[1].finish()
    line_gu.finish()
    for f in range(cut, nf):
        hand_out.start(f, gsum.at[f - cut])
    ends[0].service()
    line.finish()
    split(0, wsum)
    ends[0].finish()
    mate = (ns - 1 - pc.s, pc.b, pc.f)
    swap = remote(give.at[0], give.at[1], ws.at[1], wr.at[1], mate)
    give[0] = mine[ns - 1 - pc.s].astype(BF)
    swap.start()
    qo_out[pc.s] = mine[pc.s]
    total = sm_mid[...]
    for d, c in enumerate(lines):
        c.wait()
        total = total + sm_line[d]
    small_out[...] = total
    hand_out.finish(gu0a.at[0])
    pltpu.make_async_copy(wsum, wd_got.at[pc.s], lsem.at[0]).wait()
    remote(wsum, wd_got.at[pc.s], ws.at[0], wr.at[0], mate).wait()
    swap.wait()
    qo_out[ns - 1 - pc.s] = give[1].astype(F32)


def reduce_gradients(dims, cid, qo, terms, smalls, wd1, gu0a, gu0, wd0):
    ns, nb, nf = dims
    count = ns * nf
    dr, wide = terms.shape[1:]
    two_ff = gu0.shape[3]
    cut = gu0a.shape[0]
    half, width = wd1.shape
    rows = smalls[0].shape[0] + smalls[2].shape[0]
    small = (ns * (-(-rows // 8) * 8), 128)
    sds = jax.ShapeDtypeStruct
    dma = pltpu.SemaphoreType.DMA
    return call(
        functools.partial(reduce_kernel, dims),
        "reduce_gradients",
        cid,
        (
            sds((ns, dr, wide), F32),
            sds(small, F32),
            sds((count, dr, two_ff), BF),
            sds((ns, half, width), BF),
        ),
        [VM] * 4,
        [AN] + [VM] * 7 + [AN, VM],
        [
            pltpu.VMEM(qo.shape, BF),
            pltpu.VMEM((nb, nf - cut, dr, two_ff), BF),
            pltpu.VMEM((nf - cut, dr, two_ff), BF),
            pltpu.VMEM((half, width), BF),
            pltpu.VMEM(small, F32),
            pltpu.VMEM((count - 1,) + small, F32),
            pltpu.VMEM(small, F32),
            pltpu.VMEM((nb - 1,) + small, F32),
            pltpu.VMEM((nb, dr, wide), BF),
            pltpu.VMEM((ns, dr, wide), F32),
            pltpu.VMEM((2, dr, wide), BF),
            dma((3,)),
            dma((2,)),
            dma((2,)),
            dma((count - 1,)),
            dma((count - 1,)),
            dma((nb - 1,)),
            dma((nb - 1,)),
        ]
        + reduce_scratch(dims, half, width)
        + reduce_scratch(dims, dr, wide) * 2
        + row_scratch(dims)
        + scatter_scratch(dims, nb, dr, wide)[2:]
        + reduce_scratch(dims, nf - cut, dr, two_ff),
        (qo, terms, *smalls, wd1, gu0a, gu0, wd0),
    )


def lay_out_kernel(
    dims, gu0, gu1, wd, qo, small, out0, out1, gh0, gh1, take_out, take_grad,
    block_out, input_grad, g1, wqkv, bqkv, wout, g2, wgu, wdn
):
    ns, nb, nf = dims
    half = wd.shape[1]
    s = lax.axis_index("section")
    qkv = wqkv.shape[2]
    width = wout.shape[2]
    full = jnp.concatenate([qo[y] for y in range(ns)], axis=1)
    wqkv[0] = full[:, :qkv]
    wout[0] = full[:, qkv:]
    for y in range(ns):
        wdn[0, y * half : (y + 1) * half, :] = wd[y].astype(F32)
    for l, gu in enumerate((gu0, gu1)):
        @pl.when(s == l)
        def _():
            for y in range(ns):
                for f in range(nf):
                    got = gu[y * nf + f].astype(F32)
                    for part in range(2):
                        for b in range(nb):
                            c0 = column_start(dims, part, b, f, y, half)
                            k0 = (part * nb + b) * half
                            wgu[0, :, c0 : c0 + half] = got[:, k0 : k0 + half]
    n1 = width // 128
    per = small.shape[0] // ns
    rows = small[pl.ds(pl.multiple_of(s * per, 8), per), :]
    for k in range(n1):
        g1[0:1, k * 128 : (k + 1) * 128] = rows[k : k + 1]
        g2[0:1, k * 128 : (k + 1) * 128] = rows[n1 + k : n1 + k + 1]
    for k in range(qkv // 128):
        bqkv[0:1, k * 128 : (k + 1) * 128] = rows[2 * n1 + k : 2 * n1 + k + 1]
    for out, pair, take in (
        (block_out, (out0, out1), take_out),
        (input_grad, (gh0, gh1), take_grad),
    ):
        for l in range(ns):
            @pl.when(s == l)
            def _():
                out[0, l] = pair[l][...].T
                out[0, 1 - l] = take[...].T.astype(F32)


def lay_out(dims, qkv, args):
    ns, nb, nf = dims
    gu, wd, qo = (args[0], args[2], args[3])
    width, rows = args[5].shape
    dr = qo.shape[1]
    sds = jax.ShapeDtypeStruct
    tokens = sds((1, ns, rows, width), F32)
    return pl.pallas_call(
        functools.partial(lay_out_kernel, dims),
        name="lay_out",
        out_shape=(
            tokens,
            tokens,
            sds((1, width), F32),
            sds((1, dr, qkv), F32),
            sds((1, qkv), F32),
            sds((1, dr, width), F32),
            sds((1, width), F32),
            sds((1, dr, gu.shape[0] * gu.shape[2]), F32),
            sds((1, ns * wd.shape[1], width), F32),
        ),
        in_specs=[VM] * len(args),
        out_specs=[VM] * 9,
        compiler_params=pltpu.CompilerParams(vmem_limit_bytes=VMEM_LIMIT),
    )(*args)


def shards(
    dims,
    tokens_in,
    positions,
    doc_ids,
    out_grad,
    norm1_gain,
    w_qkv,
    b_qkv,
    w_out,
    norm2_gain,
    w_gate_up,
    w_down,
):
    ns, nb, nf = dims
    seqs, rows, width = tokens_in.shape
    s = lax.axis_index("section")
    b = lax.axis_index("blk")
    dr = w_qkv.shape[1]
    qkv = w_qkv.shape[2]
    fr = w_down.shape[1]
    half = fr // ns
    ff = nb * half
    nk = min(nb, 1 + (LONGEST - 1 + rows - 1) // rows)

    tokens = lax.dynamic_index_in_dim(tokens_in, s, 0, keepdims=False)
    cot = lax.dynamic_index_in_dim(out_grad, s, 0, keepdims=False)
    pos = lax.dynamic_index_in_dim(positions, s, 0, keepdims=False)
    docs = lax.dynamic_index_in_dim(doc_ids, s, 0, keepdims=False).astype(F32)
    freq = jnp.exp(jnp.arange(HD // 2, dtype=F32) * (-2.0 / HD) * math.log(1000000.0))
    phase = freq[:, None] * pos.astype(F32)[None, :]
    cos_part, sin_part = (jnp.cos(phase), jnp.sin(phase))
    docs = docs.reshape(nb, rows)
    picked = (b - jnp.arange(nk) + nb) % nb
    meta = jnp.take(docs, picked, axis=0).reshape(nk * rows // 128, 128)
    query_docs = lax.dynamic_slice_in_dim(docs, b, 1)
    hidden = tokens.T.astype(F32)
    g = cot.T.astype(F32)

    wd = w_down[0].reshape(ns, half, width)
    small = jnp.concatenate([norm1_gain[0], norm2_gain[0], b_qkv[0]])
    total = -(-small.shape[0] // 1024) * 1024
    small = jnp.pad(small, (0, total - small.shape[0])).reshape(-1, 128)
    gup, wdp, gu_first, qo_first, qz, small_all = gather_weights(
        dims, w_gate_up, w_qkv, w_out, wd, small
    )
    cols = qkv + width
    wide = (width, 2 * ff)

    def ride(*pairs):
        return Riders(dims, tuple(a for a, _ in pairs), tuple(v for _, v in pairs))

    common = (small_all, meta, query_docs, cos_part, sin_part)
    qo0 = qo_first.reshape(width, cols)
    wgu0 = gu_first.reshape(wide)
    first = ride((("gather", 0), wdp))
    second = ride((("gather", 1), gup))
    third = ride((("gather", 1), wdp))
    together = half % 8 == 0
    if together:
        a0, wd0, qo1, f0, (gu1,) = lower_layer(
            dims, nk, 1, hidden, *common, qo0, first, qz, wgu0, second
        )
    else:
        a0, (wd0, qo1) = attention_forward(
            dims, nk, 1, 0, hidden, *common, qo0, first, "columns", qz
        )
        f0, (gu1,) = feed_forward(dims, 3, a0[6], a0[5], wgu0, wd0.reshape(ff, width), second)
    qo1 = qo1.reshape(width, cols)
    wd0 = wd0.reshape(ff, width)
    wgu1 = gu1.reshape(wide)
    if together:
        a1, b1 = upper_layer(dims, nk, 2, f0[0], *common, qo1, third, cot.T, g, wgu1)
    else:
        a1, (wd1, g_all) = attention_forward(
            dims, nk, 2, 1, f0[0], *common, qo1, third, "lanes", cot.T
        )
        wd1 = wd1.reshape(ff, width)
        b1 = feed_both(dims, 4, 1, a1[6], a1[5], g, g_all, wgu1, wd1, small_all)

    line_gu = (nb, nf, dr, 2 * ff)
    line_wd = (nb, half, width)
    line_qo = (nb, nf, dr, cols)
    everything = (0, half)
    ab1, (dwd1, out1) = attention_backward(
        dims, nk, 7, 1, b1[0], *common, f0[0], *a1[:5], qo1,
        ride((("reduce", everything), b1[2].reshape(line_wd))), "sum", (b1[4], a1[5]),
    )
    b0, (dgu1,) = feed_backward(
        dims, 6, 0, ab1[0], a0[5], f0[1], f0[2], wgu0, wd0, small_all,
        ride((("reduce", (0, nf)), b1[1].reshape(line_gu))),
    )
    dgu0 = b0[1].reshape(line_gu)
    cut = nf - nf // 4
    ab0, (dgu0a, terms, gu_got1) = attention_backward(
        dims, nk, 8, 0, b0[0], *common, hidden, *a0[:5], qo0,
        ride((("reduce", (0, cut)), dgu0)),
        "columns", (ab1[1].reshape(line_qo), dgu1),
    )

    def swapped(values):
        give = jnp.where(s == 0, values[1], values[0]).astype(BF)
        return lax.ppermute(give, "section", [(0, 1), (1, 0)])

    take_out = swapped((f0[0], out1))
    take_grad = swapped((ab0[0], ab1[0]))
    grad_qo, small_sum, gu_got0, wd_got = reduce_gradients(
        dims, 9, ab0[1].reshape(line_qo), terms,
        (ab0[2], ab1[2], b0[3], b1[3]), dwd1, dgu0a, dgu0, b0[2].reshape(line_wd),
    )
    return lay_out(
        dims,
        qkv,
        (gu_got0, gu_got1, wd_got, grad_qo, small_sum, f0[0], out1, ab0[0], ab1[0], take_out,
         take_grad),
    )


def solution(mesh):
    dims = (mesh.shape["section"], mesh.shape["blk"], mesh.shape["fsdp"])
    return jax.shard_map(
        functools.partial(shards, dims),
        mesh=mesh,
        in_specs=(
            P("fsdp", "blk", None),
            P("fsdp", "blk"),
            P("fsdp", None),
            P("fsdp", "blk", None),
            P("section", None),
            P("section", ("blk", "fsdp"), None),
            P("section", None),
            P("section", ("blk", "fsdp"), None),
            P("section", None),
            P("section", ("blk", "fsdp"), None),
            P("section", ("blk", "fsdp"), None),
        ),
        out_specs=(
            P("section", "fsdp", "blk", None),
            P("section", "fsdp", "blk", None),
            P("section", None),
            P("section", ("blk", "fsdp"), None),
            P("section", None),
            P("section", ("blk", "fsdp"), None),
            P("section", None),
            P("section", ("blk", "fsdp"), None),
            P("section", ("blk", "fsdp"), None),
        ),
        check_vma=False,
    )
```

```python
import functools
import math

import jax
import jax.numpy as jnp
from jax import lax
from jax.experimental import pallas as pl
from jax.experimental.pallas import tpu as pltpu
from jax.sharding import PartitionSpec as P

H = 14
KVH = 2
HD = 64
GROUP = H // KVH
LONGEST = 512
NEG = -1e30
BF = jnp.bfloat16
F32 = jnp.float32
MESH = pl.DeviceIdType.MESH
VMEM_LIMIT = 60 * 2**20
VM = pl.BlockSpec(memory_space=pltpu.VMEM)
AN = pl.BlockSpec(memory_space=pl.ANY)


def nn(a, b):
    return lax.dot_general(a, b, (((1,), (0,)), ((), ())), preferred_element_type=F32)


def nt(a, b):
    return lax.dot_general(a, b, (((1,), (1,)), ((), ())), preferred_element_type=F32)


def tn(a, b):
    return lax.dot_general(a, b, (((0,), (0,)), ((), ())), preferred_element_type=F32)


def other(f):
    return f + 1 - 2 * (f % 2)


class Place:
    def __init__(self, dims):
        self.ns, self.nb, self.nf = dims
        self.count = self.ns * self.nf
        self.s = lax.axis_index("section")
        self.b = lax.axis_index("blk")
        self.f = lax.axis_index("fsdp")
        self.me = self.s * self.nf + self.f
        self.two_level = self.ns == 2 and self.nf == 4

    def plane(self, e):
        q = (self.me + e) % self.count
        return (q // self.nf, self.b, q % self.nf)

    def slot_from(self, e):
        return (self.me + self.count - e) % self.count

    def along(self, d):
        return (self.s, (self.b + d) % self.nb, self.f)

    def mates(self):
        s, b, f = (self.s, self.b, self.f)
        xf = (f + 2) % 4
        return ((s, b, other(f)), (s, b, xf), (1 - s, b, f))

    def slots(self):
        s, f = (self.s, self.f)
        xf = (f + 2) % 4
        t = 1 - s
        return (
            s * 4 + f,
            s * 4 + other(f),
            s * 4 + xf,
            t * 4 + f,
            s * 4 + other(xf),
            t * 4 + other(f),
            t * 4 + xf,
            t * 4 + other(xf),
        )


def pick(i, values):
    total = 0
    for k, v in enumerate(values):
        total = total + jnp.where(i == k, v, 0)
    return total


def greet(place, plane, along):
    barrier = pltpu.get_barrier_semaphore()
    count = 0
    if plane:
        if place.two_level and plane == "mates":
            targets = list(place.mates())
        else:
            targets = [place.plane(e) for e in range(1, place.count)]
        for t in targets:
            pl.semaphore_signal(barrier, 1, device_id=t, device_id_type=MESH)
        count += len(targets)
    if along:
        for d in range(1, place.nb):
            pl.semaphore_signal(barrier, 1, device_id=place.along(d), device_id_type=MESH)
        count += place.nb - 1
    pl.semaphore_wait(barrier, count)


def remote(src, dst, ssem, rsem, device):
    return pltpu.make_async_remote_copy(
        src_ref=src,
        dst_ref=dst,
        send_sem=ssem,
        recv_sem=rsem,
        device_id=device,
        device_id_type=MESH,
    )


def cut_in(parts, view, c):
    n = view.shape[0] // parts
    return view.at[pl.ds(c * n, n)]


def gather_sems(dims):
    n = 2 * (dims[0] * dims[2] - 1)
    return [pltpu.SemaphoreType.DMA((n,)), pltpu.SemaphoreType.DMA((n,))]


class PlaneGather:
    def __init__(self, place, slot, ssem, rsem):
        self.place, self.slot, self.ssem, self.rsem = (place, slot, ssem, rsem)
        self.parts = 2 if place.two_level else 1
        if place.two_level:
            self.order = place.slots()
        else:
            self.order = tuple(place.slot_from(e) for e in range(place.count))

    def copy(self, k, c, q, device):
        v = cut_in(self.parts, self.slot(q), c)
        i = k * self.parts + c
        return remote(v, v, self.ssem.at[i], self.rsem.at[i], device)

    def start(self):
        pc = self.place
        if pc.two_level:
            core, xm, ym = pc.mates()
            for c in range(2):
                self.copy(1, c, self.order[0], xm).start()
                self.copy(2, c, self.order[0], ym).start()
            for c in range(2):
                self.copy(0, c, self.order[0], core).start()
        else:
            for e in range(1, pc.count):
                self.copy(e - 1, 0, self.order[0], pc.plane(e)).start()

    def came(self, k, c):
        self.copy(k, c, self.order[k + 1], self.place.plane(1)).wait_recv()

    def before(self, step):
        if step == 0:
            return
        pc = self.place
        if not pc.two_level:
            self.came(step - 1, 0)
            return
        core, xm, ym = pc.mates()
        h = pc.f % 2
        if step == 2:
            which = h * self.order[3] + (1 - h) * self.order[2]
            far = (
                h * xm[0] + (1 - h) * ym[0],
                pc.b,
                h * xm[2] + (1 - h) * ym[2],
            )
            for c in range(2):
                self.came(1, c)
                self.came(2, c)
                self.copy(5, c, which, far).start()
                self.copy(3, c, self.order[2], core).start()
                self.copy(4, c, self.order[3], core).start()
        elif step == 3:
            return
        elif step == 6:
            for c in range(2):
                self.came(5, c)
                self.copy(6, c, self.order[6], core).start()
        else:
            for c in range(2):
                self.came(step - 1, c)

    def finish(self):
        n = self.place.count - 1
        for k in range(n):
            for c in range(self.parts):
                self.copy(k, c, self.order[0], self.place.plane(1)).wait_send()


class PlaneScatter:
    def __init__(self, place, near, away, back, hop, ssem, rsem):
        self.place = place
        self.near, self.away, self.back, self.hop = (near, away, back, hop)
        self.ssem, self.rsem = (ssem, rsem)

    def put(self, step, value):
        pc = self.place
        if not pc.two_level:
            @pl.when(step == 0)
            def _():
                self.near[0] = value

            @pl.when(step > 0)
            def _():
                e = pc.count - step
                self.away[e - 1] = value.astype(BF)
                q = (pc.me + e) % pc.count
                remote(
                    self.away.at[e - 1],
                    self.back.at[e - 1],
                    self.ssem.at[e - 1],
                    self.rsem.at[e - 1],
                    (q // pc.nf, pc.b, q % pc.nf),
                ).start()
            return
        core, xm, ym = pc.mates()
        here = (step == 0) | (step == 2) | (step == 3) | (step == 6)
        q = pick(step, (0, 0, 1, 2, 1, 2, 3, 3))

        @pl.when(here)
        def _():
            self.near[q] = value

        @pl.when(jnp.logical_not(here))
        def _():
            self.away[q] = value.astype(BF)
            self.core_copy(q).start()

    def core_copy(self, q):
        core = self.place.mates()[0]
        return remote(self.away.at[q], self.back.at[q], self.ssem.at[q], self.rsem.at[q], core)

    def far_copy(self, e):
        return remote(self.away.at[e - 1], self.back.at[e - 1], self.ssem.at[e - 1],
                      self.rsem.at[e - 1], self.place.plane(e))

    def hop_copy(self, k, c, device):
        i = 4 + 2 * k + c
        return remote(
            cut_in(2, self.hop.at[k], c),
            cut_in(2, self.hop.at[k + 3], c),
            self.ssem.at[i],
            self.rsem.at[i],
            device,
        )

    def rows(self, c):
        n = self.hop.shape[1] // 2
        return slice(c * n, (c + 1) * n)

    def targets(self):
        pc = self.place
        core, xm, ym = pc.mates()
        c = pc.f % 2
        first = (c * xm[0] + (1 - c) * ym[0], pc.b, c * xm[2] + (1 - c) * ym[2])
        second = (c * ym[0] + (1 - c) * xm[0], pc.b, c * ym[2] + (1 - c) * xm[2])
        return (first, second)

    def early(self):
        pc = self.place
        if not pc.two_level:
            return
        c = pc.f % 2
        first, second = self.targets()
        self.core_copy(1).wait_recv()
        self.core_copy(2).wait_recv()
        q = c * 1 + (1 - c) * 2
        for k in range(2):
            r = self.rows(k)
            self.hop[0, r] = (self.mine(q, r) + self.back[q, r].astype(F32)).astype(BF)
            self.hop_copy(0, k, first).start()

    def diagonal(self):
        pc = self.place
        if not pc.two_level:
            return
        first, second = self.targets()
        self.core_copy(3).wait_recv()
        for k in range(2):
            r = self.rows(k)
            self.hop[1, r] = (self.mine(3, r) + self.back[3, r].astype(F32)).astype(BF)
            self.hop_copy(1, k, first).start()

    def mine(self, q, r=slice(None)):
        return self.near[q, r]

    def result(self, store):
        self.late()
        self.finish(store)

    def late(self):
        pc = self.place
        if not pc.two_level:
            return
        c = pc.f % 2
        first, second = self.targets()
        q = c * 2 + (1 - c) * 1
        for k in range(2):
            r = self.rows(k)
            self.hop_copy(1, k, first).wait_recv()
            self.hop[2, r] = (
                self.mine(q, r) + self.back[q, r].astype(F32) + self.hop[4, r].astype(F32)
            ).astype(BF)
            self.hop_copy(2, k, second).start()

    def finish(self, store):
        pc = self.place
        if not pc.two_level:
            total = self.mine(0)
            for e in range(1, pc.count):
                self.far_copy(e).wait()
                total = total + self.back[e - 1].astype(F32)
            store(total)
            return
        first, second = self.targets()
        self.core_copy(0).wait_recv()
        for k in range(2):
            self.hop_copy(0, k, first).wait_recv()
            self.hop_copy(2, k, second).wait_recv()
        store(
            self.mine(0)
            + self.back[0].astype(F32)
            + self.hop[3].astype(F32)
            + self.hop[5].astype(F32)
        )
        for q in range(4):
            self.core_copy(q).wait_send()
        for k in range(2):
            self.hop_copy(0, k, first).wait_send()
            self.hop_copy(1, k, first).wait_send()
            self.hop_copy(2, k, second).wait_send()


class ReadyScatter(PlaneScatter):
    def __init__(self, place, part, back, hop, ssem, rsem):
        super().__init__(place, None, None, back, hop, ssem, rsem)
        self.part = part
        if place.two_level:
            o = place.slots()
            self.here = (o[0], o[2], o[3], o[6])
            self.gone = (o[1], o[4], o[5], o[7])

    def mine(self, q, r=slice(None)):
        if not self.place.two_level:
            return self.part(self.place.me)[...].astype(F32)
        return self.part(pick(q, self.here))[r].astype(F32)

    def core_copy(self, q):
        core = self.place.mates()[0]
        v = self.part(self.gone[q])
        return remote(v, self.back.at[q], self.ssem.at[q], self.rsem.at[q], core)

    def far_copy(self, e):
        pc = self.place
        v = self.part((pc.me + e) % pc.count)
        return remote(v, self.back.at[e - 1], self.ssem.at[e - 1], self.rsem.at[e - 1],
                      pc.plane(e))

    def start(self):
        pc = self.place
        if pc.two_level:
            for q in (3, 2, 1, 0):
                self.core_copy(q).start()
        else:
            for e in range(1, pc.count):
                self.far_copy(e).start()


class RowSends:
    def __init__(self, place, layer, out, sems):
        self.place, self.layer, self.out = (place, layer, out)
        self.lsem, self.ss, self.sr = sems

    def copies(self, f, src):
        pc = self.place
        e = (self.layer * pc.nf + f - pc.me + pc.count) % pc.count
        own = self.out.at[pc.me]
        k = (e + pc.count - 1) % pc.count
        away = remote(src, own, self.ss.at[f], self.sr.at[k], (self.layer, pc.b, f))
        return (e, away, pltpu.make_async_copy(src, own, self.lsem))

    def start(self, f, src):
        e, away, local = self.copies(f, src)

        @pl.when(e != 0)
        def _():
            away.start()

        @pl.when(e == 0)
        def _():
            local.start()

    def finish(self, src):
        pc = self.place
        for f in range(pc.nf):
            e, away, local = self.copies(f, src)

            @pl.when(e != 0)
            def _():
                away.wait_send()

            @pl.when(e == 0)
            def _():
                local.wait()

        @pl.when(pc.s == self.layer)
        def _():
            for e in range(1, pc.count):
                q = pc.slot_from(e)
                remote(src, self.out.at[q], self.ss.at[0], self.sr.at[e - 1], pc.plane(e)).wait_recv()


def row_scratch(dims):
    dma = pltpu.SemaphoreType.DMA
    return [dma(()), dma((dims[2],)), dma((dims[0] * dims[2],))]


class LineGather:
    def __init__(self, place, piece, out, sems, part=None):
        self.place, self.piece = (place, piece)
        self.view = lambda t: out.at[t] if part is None else out.at[t, part]
        self.lsem, self.ss, self.sr = sems
        self.k = 0

    def local(self):
        return pltpu.make_async_copy(self.piece, self.view(self.place.b), self.lsem)

    def hop(self, way, k, came):
        pc = self.place
        t = pc.b - way * (k - (0 if came else 1))
        src = self.piece if k == 1 and not came else self.view(t)
        i = k - 1 + (0 if way == 1 else pc.nb - 1)
        return remote(
            src, self.view(t), self.ss.at[i], self.sr.at[i], (pc.s, pc.b + way, pc.f)
        )

    def sends(self, way, k):
        b, nb = (self.place.b, self.place.nb)
        return (b >= k - 1) & (b < nb - 1) if way == 1 else (b <= nb - k) & (b > 0)

    def comes(self, way, k):
        b, nb = (self.place.b, self.place.nb)
        return b >= k if way == 1 else b <= nb - 1 - k

    def arrived(self, k):
        for way in (1, -1):
            @pl.when(self.comes(way, k))
            def _():
                self.hop(way, k, True).wait_recv()

    def start(self):
        self.local().start()
        self.service()

    def service(self):
        if self.k == self.place.nb - 1:
            return
        self.k += 1
        if self.k > 1:
            self.arrived(self.k - 1)
        for way in (1, -1):
            @pl.when(self.sends(way, self.k))
            def _():
                self.hop(way, self.k, False).start()

    def finish(self):
        last = self.place.nb - 1
        while self.k < last:
            self.service()
        self.arrived(last)
        for k in range(1, last + 1):
            for way in (1, -1):
                @pl.when(self.sends(way, k))
                def _():
                    self.hop(way, k, False).wait_send()
        self.local().wait()


class LineReduce:
    def __init__(self, place, terms, store, sems, load=None):
        self.place, self.terms, self.store, self.load = (place, terms, store, load)
        self.out, self.came, self.ss, self.sr = sems
        self.k = 0

    def index(self, way, k):
        return k - 1 + (0 if way == 1 else self.place.nb - 1)

    def hop(self, way, k):
        pc = self.place
        i = self.index(way, k)
        return remote(
            self.out.at[i], self.came.at[i], self.ss.at[i], self.sr.at[i],
            (pc.s, pc.b + way, pc.f),
        )

    def rank(self, way):
        pc = self.place
        return pc.b if way == 1 else pc.nb - 1 - pc.b

    def sends(self, way, k):
        r = self.rank(way)
        return (r < k) & (r < self.place.nb - 1)

    def start(self):
        if self.load is not None:
            self.load.wait()
        self.service()

    def service(self):
        nb = self.place.nb
        if self.k == nb - 1:
            return
        self.k += 1
        k = self.k
        for way in (1, -1):
            r = self.rank(way)
            t = nb - k + r if way == 1 else k - 1 - r
            i = self.index(way, k)

            @pl.when(self.sends(way, k) & (r == 0))
            def _():
                self.out[i] = self.terms(t)

            if k > 1:
                @pl.when(self.sends(way, k) & (r > 0))
                def _():
                    self.hop(way, k - 1).wait_recv()
                    total = self.terms(t).astype(F32) + self.came[i - 1].astype(F32)
                    self.out[i] = total.astype(BF)

            @pl.when(self.sends(way, k))
            def _():
                self.hop(way, k).start()

    def finish(self):
        pc = self.place
        last = pc.nb - 1
        while self.k < last:
            self.service()
        right, left = (self.index(1, last), self.index(-1, last))

        @pl.when(pc.b == 0)
        def _():
            self.hop(-1, last).wait_recv()
            self.store(self.terms(pc.b).astype(F32) + self.came[left].astype(F32))

        @pl.when(pc.b == last)
        def _():
            self.hop(1, last).wait_recv()
            self.store(self.terms(pc.b).astype(F32) + self.came[right].astype(F32))

        @pl.when((pc.b > 0) & (pc.b < last))
        def _():
            self.hop(1, last).wait_recv()
            self.hop(-1, last).wait_recv()
            self.store(
                self.terms(pc.b).astype(F32)
                + self.came[right].astype(F32)
                + self.came[left].astype(F32)
            )

        for k in range(1, last + 1):
            for way in (1, -1):
                @pl.when(self.sends(way, k))
                def _():
                    self.hop(way, k).wait_send()


def gather_scratch(dims):
    dma = pltpu.SemaphoreType.DMA
    return [dma(()), dma((2 * (dims[1] - 1),)), dma((2 * (dims[1] - 1),))]


def reduce_scratch(dims, *block):
    dma = pltpu.SemaphoreType.DMA
    n = 2 * (dims[1] - 1)
    return [pltpu.VMEM((n,) + block, BF), pltpu.VMEM((n,) + block, BF), dma((n,)), dma((n,))]


class Riders:
    def __init__(self, dims, specs, arrays):
        self.dims, self.specs, self.arrays = (dims, specs, arrays)
        self.shapes = []
        self.places = [AN] * len(specs)
        self.outs = []
        self.scratch = []
        self.sizes = []
        for spec, a in zip(specs, arrays):
            if spec[0] == "gather":
                shape = (dims[1],) + a.shape[1:]
                scratch = gather_scratch(dims)
            else:
                lo, hi = spec[1]
                shape = (hi - lo,) + a.shape[2:]
                scratch = reduce_scratch(dims, *shape)
                scratch += [
                    pltpu.VMEM((dims[1],) + shape, BF), pltpu.SemaphoreType.DMA(())
                ]
            self.outs.append(AN if spec[0] == "gather" else VM)
            self.shapes.append(jax.ShapeDtypeStruct(shape, a.dtype))
            self.scratch += scratch
            self.sizes.append(len(scratch))
        self.count = len(specs)

    def board(self, place, ins, outs, scratch):
        out = []
        for spec, size, a, o in zip(self.specs, self.sizes, ins, outs):
            mine, scratch = (scratch[:size], scratch[size:])
            if spec[0] == "gather":
                out.append(LineGather(place, a.at[spec[1]], o, mine))
            else:
                lo, hi = spec[1]

                def store(value, o=o):
                    o[...] = value.astype(BF)

                terms, sem = mine[4:]
                load = pltpu.make_async_copy(a.at[:, lo:hi], terms, sem)
                load.start()
                out.append(
                    LineReduce(place, lambda t, r=terms: r[t], store, mine[:4], load)
                )
        return (out, scratch)


def each(riders, what):
    for r in riders:
        getattr(r, what)()


def scatter_scratch(dims, *block):
    count = dims[0] * dims[2]
    if dims[0] == 2 and dims[2] == 4:
        near, away, hops, sems = (4, 4, 6, 10)
    else:
        near, away, hops, sems = (1, count - 1, 1, count - 1)
    return [
        pltpu.VMEM((near,) + block, F32),
        pltpu.VMEM((away,) + block, BF),
        pltpu.VMEM((away,) + block, BF),
        pltpu.VMEM((hops,) + block, BF),
        pltpu.SemaphoreType.DMA((sems,)),
        pltpu.SemaphoreType.DMA((sems,)),
    ]


def call(kernel, name, cid, outs, out_specs, in_specs, scratch, args):
    params = pltpu.CompilerParams(
        collective_id=cid, has_side_effects=True, vmem_limit_bytes=VMEM_LIMIT
    )
    return pl.pallas_call(
        kernel,
        name=name,
        out_shape=outs,
        in_specs=in_specs,
        out_specs=out_specs,
        scratch_shapes=scratch,
        compiler_params=params,
    )(*args)


def column_start(dims, part, b, f, y, half):
    ns, nb, nf = dims
    return part * nb * nf * ns * half + ((b * nf + f) * ns + y) * half


def columns_of(ref, q, nf, wide):
    return ref.at[:, q % nf, :, pl.ds(pl.multiple_of((q // nf) * wide, wide), wide)]


def gather_weights_kernel(
    dims, w_ref, wq_ref, wo_ref, wd, small, gup, wdp, gu_first, qo_first, qz, small_all,
    pack, qcol, qh, lsem, ps, pr, ms, mr, qs, qr, *rest
):
    pc = Place(dims)
    ns, nb, nf = dims
    half = wd.shape[1]
    wide = qh.shape[2]
    greet(pc, "all", True)
    qkv = wq_ref.shape[2]
    full = jnp.concatenate([wq_ref[0], wo_ref[0]], axis=1)
    for y in range(ns):
        qcol[y] = full[:, y * wide : (y + 1) * wide]
    across = []
    for d in range(1, ns):
        y = (pc.s + d) % ns
        t = (y, pc.b, pc.f)
        i = 3 * (d - 1)
        across.append(remote(qcol.at[y], qh.at[pc.s], ms.at[i], mr.at[i], t))
        across.append(remote(wd.at[y], wdp.at[pc.s], ms.at[i + 1], mr.at[i + 1], t))
        across.append(remote(small, small_all.at[pc.s], ms.at[i + 2], mr.at[i + 2], t))
    for c in across:
        c.start()
    qh[pc.s] = qcol[pc.s]
    local = [
        pltpu.make_async_copy(wd.at[pc.s], wdp.at[pc.s], lsem.at[0]),
        pltpu.make_async_copy(small, small_all.at[pc.s], lsem.at[1]),
    ]
    for c in local:
        c.start()
    own = pltpu.make_async_copy(pack.at[pc.s, pc.f], gup.at[pc.s, pc.f], lsem.at[2])

    def piece(y, f):
        e = (y * nf + f - pc.me + pc.count) % pc.count
        k = (e + pc.count - 1) % pc.count
        return (
            e,
            remote(pack.at[y, f], gup.at[pc.s, pc.f], ps.at[k], pr.at[k], (y, pc.b, f)),
        )

    for f in range(nf):
        for y in range(ns):
            pieces = []
            for part in range(2):
                for b in range(nb):
                    c0 = column_start(dims, part, b, f, y, half)
                    pieces.append(w_ref[0, :, c0 : c0 + half])
            pack[y, f] = jnp.concatenate(pieces, axis=1)
            e, c = piece(y, f)

            @pl.when(e != 0)
            def _():
                c.start()

    own.start()
    for d in range(ns - 1):
        across[3 * d].wait()
    line_q = LineGather(pc, qh, qz, rest[0:3])
    lines = [
        LineGather(pc, gup.at[0, f], gu_first, rest[3 + 3 * f : 6 + 3 * f], f) for f in range(nf)
    ]
    line_q.start()

    def arrived(y, f):
        e, c = piece(y, f)
        k = (2 * pc.count - e - 1) % pc.count

        @pl.when(e != 0)
        def _():
            remote(pack.at[0, 0], gup.at[y, f], ps.at[k], pr.at[k], (y, pc.b, f)).wait_recv()

    own.wait()
    line_q.service()
    for f in range(nf):
        arrived(0, f)
        lines[f].start()
    line_q.service()
    for line in lines:
        line.service()
    line_q.finish()
    gather = PlaneGather(pc, lambda q: columns_of(qo_first, q, nf, wide), qs, qr)
    columns_of(qo_first, pc.me, nf, wide)[...] = qz[:, 0]
    gather.start()
    for step in range(1, min(6, pc.count)):
        gather.before(step)
    for line in lines:
        line.service()
    for step in range(min(6, pc.count), pc.count):
        gather.before(step)
    gather.finish()
    for y in range(1, ns):
        for f in range(nf):
            arrived(y, f)
    for y in range(ns):
        for f in range(nf):
            e, c = piece(y, f)

            @pl.when(e != 0)
            def _():
                c.wait_send()

    for c in local:
        c.wait()
    for i, c in enumerate(across):
        if i % 3:
            c.wait()
    for line in lines:
        line.finish()


def gather_weights(dims, w, wq, wo, wd, small):
    ns, nb, nf = dims
    count = ns * nf
    half, width = wd.shape[1:]
    dr = wq.shape[1]
    cols = wq.shape[2] + wo.shape[2]
    wide = cols // ns
    two_ff = 2 * nb * half
    sds = jax.ShapeDtypeStruct
    outs = (
        sds((ns, nf, dr, two_ff), BF),
        sds((ns, half, width), BF),
        sds((nb, nf, dr, two_ff), BF),
        sds((nb, nf, dr, cols), BF),
        sds((nb, ns, dr, wide), BF),
        sds((ns,) + small.shape, F32),
    )
    dma = pltpu.SemaphoreType.DMA
    return call(
        functools.partial(gather_weights_kernel, dims),
        "gather_weights",
        0,
        outs,
        [AN, AN, AN, VM, VM, AN],
        [VM, VM, VM, AN, AN],
        [
            pltpu.VMEM((ns, nf, dr, two_ff), BF),
            pltpu.VMEM((ns, dr, wide), BF),
            pltpu.VMEM((ns, dr, wide), BF),
            dma((4,)),
            dma((count,)),
            dma((count,)),
            dma((3 * (ns - 1),)),
            dma((3 * (ns - 1),)),
        ]
        + gather_sems(dims)
        + gather_scratch(dims) * (1 + nf),
        (w, wq, wo, wd, small),
    )


def rms(values):
    return lax.rsqrt(jnp.mean(values * values, axis=0, keepdims=True) + 1e-06)


def column(rows_t, first, count):
    return jnp.concatenate([rows_t[:, k : k + 1] for k in range(first, first + count)], axis=0)


def rows_of(values):
    v = folded(values)
    return jnp.concatenate(
        [v[k : k + 128].T.sum(axis=0, keepdims=True) for k in range(0, v.shape[0], 128)], axis=0
    )


def folded(v):
    out = v[:, :128]
    for k in range(1, v.shape[1] // 128):
        out = out + v[:, k * 128 : (k + 1) * 128]
    return out


def fill_masks(pc, mask, meta_t, query_docs):
    nk, rows = mask.shape[:2]
    key_i = lax.broadcasted_iota(jnp.int32, (rows, rows), 0)
    query_i = lax.broadcasted_iota(jnp.int32, (rows, rows), 1)
    per = rows // 128
    for j in range(nk):
        same = column(meta_t, j * per, per) == query_docs
        if j == 0:
            live = same & (key_i <= query_i)
        else:
            live = same & (key_i < (pc.b - j + 1) * rows)
        mask[j] = jnp.where(live, 0.0, NEG)


def load_qo(qo, w, wo, sems):
    cols = w.shape[1]
    c1 = pltpu.make_async_copy(qo.at[:, 0:cols], w, sems.at[0])
    c2 = pltpu.make_async_copy(qo.at[:, cols : cols + wo.shape[1]], wo, sems.at[1])
    c1.start()
    c2.start()
    return (c1, c2)


def gains_of(small_t, width, qkv):
    n = width // 128
    return (
        column(small_t, 0, n),
        column(small_t, n, n),
        column(small_t, 2 * n, qkv // 128),
    )


def padded_t(v):
    n = v.shape[0]
    return jnp.concatenate([v, jnp.zeros((128 - n, 128), v.dtype)], axis=0).T


def attention_forward_kernel(dims, *args):
    pc = Place(dims)
    riders, gather = attention_forward_part(pc, *args)
    last_blocks(pc, gather)
    gather.finish()
    each(riders, "finish")


def last_blocks(pc, gather):
    for step in range(min(6, pc.count), pc.count):
        gather.before(step)


def attention_forward_part(
    pc, nk, layer, plan, carry, h_ref, small_ref, meta_ref, docs_ref, cos_ref, sin_ref, qo_all,
    *refs
):
    n = plan.count
    block_ref, refs = (refs[0], refs[1:])
    ins, refs = (refs[:n], refs[n:])
    normed_ref, q_ref, kv_ref, lse_ref, mixed_ref, res_ref, n2_ref = refs[:7]
    outs, refs = (refs[7 : 7 + n], refs[7 + n :])
    block_all, refs = (refs[0], refs[1:])
    w, wo, mask, joined, top_own, sum_own, out_own, ssem, rsem, qsem = refs[:10]
    refs = refs[10:]
    width, rows = h_ref.shape
    loads = load_qo(qo_all, w, wo, qsem)
    greet(pc, "mates", True)
    riders, refs = plan.board(pc, ins, outs, refs)
    if carry == "lanes":
        own = block_ref
        slot = lambda q: block_all.at[:, lanes(q, rows)]
    else:
        own = block_ref.at[:, 1]
        slot = lambda q: columns_of(block_all, q, pc.nf, block_ref.shape[3])
    gather = PlaneGather(pc, slot, *refs)
    slot(pc.me)[...] = own[...]
    gather.start()
    each(riders, "start")
    g1, g2, bias = gains_of(padded_t(small_ref[layer]), width, w.shape[1])
    hidden = h_ref[...].astype(BF).astype(F32)
    normed = (hidden * rms(hidden) * g1).astype(BF)
    normed_ref[...] = normed
    fill_masks(pc, mask, padded_t(meta_ref[...]), docs_ref[...])
    loads[0].wait()
    joined[...] = tn(w[...], normed) + bias
    cos_part = cos_ref[...]
    sin_part = sin_ref[...]
    half = HD // 2

    def turned(row):
        u1 = joined[pl.ds(row, half), :]
        u2 = joined[pl.ds(row + half, half), :]
        return (u1 * cos_part - u2 * sin_part, u2 * cos_part + u1 * sin_part)

    for g in range(KVH):
        r1, r2 = turned((H + g) * HD)
        kv_ref[0, g, :half, :] = r1.astype(BF)
        kv_ref[0, g, half:, :] = r2.astype(BF)
        v0 = (H + KVH + g) * HD
        kv_ref[0, KVH + g] = joined[v0 : v0 + HD, :].astype(BF)
    sends = [
        remote(kv_ref.at[0], kv_ref.at[j], ssem.at[j - 1], rsem.at[j - 1], pc.along(j))
        for j in range(1, nk)
    ]
    for c in sends:
        c.start()
    scale = HD**-0.5
    for head in range(H):
        r1, r2 = turned(head * HD)
        q_ref[head, :half, :] = (r1 * scale).astype(BF)
        q_ref[head, half:, :] = (r2 * scale).astype(BF)
    for g in range(KVH):
        keys = kv_ref[0, g].T
        values = kv_ref[0, KVH + g]

        def own_keys(i, carried):
            head = g * GROUP + i
            x = nn(keys, q_ref[head]) + mask[0]
            top = x.max(axis=0, keepdims=True)
            e = jnp.exp(x - top)
            top_own[head] = top
            sum_own[head] = e.sum(axis=0, keepdims=True)
            out_own[head] = nn(values, e.astype(BF))
            return carried

        lax.fori_loop(0, GROUP, own_keys, 0, unroll=True)
    for c in sends:
        c.wait()
    each(riders, "service")
    for g in range(KVH):
        keys = [kv_ref[j, g].T for j in range(1, nk)]
        values = [kv_ref[j, KVH + g] for j in range(1, nk)]

        def one_head(i, carried):
            head = g * GROUP + i
            q = q_ref[head]
            s = [nn(keys[j], q) + mask[j + 1] for j in range(nk - 1)]
            first = top_own[head]
            top = first
            for x in s:
                top = jnp.maximum(top, x.max(axis=0, keepdims=True))
            e = [jnp.exp(x - top) for x in s]
            fade = jnp.exp(first - top)
            total = sum_own[head] * fade
            out = out_own[head] * fade
            for j in range(nk - 1):
                total = total + e[j].sum(axis=0, keepdims=True)
                out = out + nn(values[j], e[j].astype(BF))
            lse_ref[head] = top + jnp.log(total)
            mixed_ref[head] = (out / total).astype(BF)
            return carried

        lax.fori_loop(0, GROUP, one_head, 0, unroll=True)
        if g == 0:
            for step in range(1, min(6, pc.count)):
                gather.before(step)
        else:
            each(riders, "service")
    mixed = mixed_ref[...].reshape(H * HD, rows)
    loads[1].wait()
    residual = hidden + tn(wo[...], mixed)
    res_ref[...] = residual
    n2_ref[...] = (residual * rms(residual) * g2).astype(BF)
    return (riders, gather)


def attention_scratch(dims, nk, width, rows, qkv):
    dma = pltpu.SemaphoreType.DMA
    return [
        pltpu.VMEM((width, qkv), BF),
        pltpu.VMEM((width, width), BF),
        pltpu.VMEM((nk, rows, rows), F32),
        pltpu.VMEM((qkv, rows), F32),
        pltpu.VMEM((H, 1, rows), F32),
        pltpu.VMEM((H, 1, rows), F32),
        pltpu.VMEM((H, HD, rows), F32),
        dma((nk - 1,)),
        dma((nk - 1,)),
        dma((2,)),
    ]


def attention_forward(dims, nk, cid, layer, hidden, small, meta, docs, cos_part, sin_part, qo_all,
                      plan, carry, block):
    width, rows = hidden.shape
    ns, nb, nf = dims
    count = ns * nf
    qkv = qo_all.shape[1] - width
    sds = jax.ShapeDtypeStruct
    outs = [
        sds((width, rows), BF),
        sds((H, HD, rows), BF),
        sds((nk, 2 * KVH, HD, rows), BF),
        sds((H, 1, rows), F32),
        sds((H, HD, rows), BF),
        sds((width, rows), F32),
        sds((width, rows), BF),
    ] + plan.shapes
    if carry == "lanes":
        outs.append(sds((width, count * rows), BF))
    else:
        outs.append(sds((nb, nf, block.shape[2], ns * block.shape[3]), BF))
    out = call(
        functools.partial(attention_forward_kernel, dims, nk, layer, plan, carry),
        "attention_forward",
        cid,
        tuple(outs),
        [VM] * 7 + plan.outs + [VM],
        [VM] * 6 + [AN, VM] + plan.places,
        attention_scratch(dims, nk, width, rows, qkv)
        + plan.scratch
        + gather_sems(dims),
        (hidden, small, meta, docs, cos_part, sin_part, qo_all, block, *plan.arrays),
    )
    return (out[:7], out[7:])


def attention_backward_kernel(
    dims, nk, layer, plan, carry, g_ref, small_ref, meta_ref, docs_ref, cos_ref, sin_ref,
    h_ref, normed_ref, q_ref, kv_ref, lse_ref, mixed_ref, qo_all, *refs
):
    n = plan.count
    parts_ref, more_ref, refs = (refs[0], refs[1], refs[2:])
    ins, refs = (refs[:n], refs[n:])
    gh_ref, dqo_ref, dsmall_ref = refs[:3]
    outs, refs = (refs[3 : 3 + n], refs[3 + n :])
    out_ref, refs = (refs[0], refs[1:])
    if carry == "columns":
        rows_ref, refs = (refs[0], refs[1:])
    w, wo, mask, dmix, dkv, delta, dq_some, out_kv, in_kv, gj, ssem, rsem, qsem = refs[:13]
    refs = refs[13:]
    pc = Place(dims)
    width, rows = h_ref.shape
    qkv = w.shape[1]
    loads = load_qo(qo_all, w, wo, qsem)
    riders, refs = plan.board(pc, ins, outs, refs)
    if carry == "columns":
        held, held_sem = refs[7:]
        coming = pltpu.make_async_copy(parts_ref, held, held_sem)
        coming.start()
    greet(pc, "all" if carry == "columns" else "mates", True)
    if carry == "columns":
        part = lambda q: columns_of(held, q, pc.nf, out_ref.shape[2])
        hand_out = RowSends(pc, 1, rows_ref, refs[4:7])
        coming.wait()
    else:
        part = lambda q: parts_ref.at[q]
    scatter = ReadyScatter(pc, part, *refs[:4])
    scatter.start()
    each(riders, "start")
    g1 = column(padded_t(small_ref[layer]), 0, width // 128)
    fill_masks(pc, mask, padded_t(meta_ref[...]), docs_ref[...])
    grl = g_ref[...].astype(BF)
    loads[1].wait()
    dmix[...] = nn(wo[...], grl).astype(BF).reshape(dmix.shape)
    dqo_ref[:, qkv:] = nt(mixed_ref[...].reshape(H * HD, rows), grl).astype(BF)
    scatter.diagonal()
    scatter.early()
    if carry == "columns":
        for f in range(pc.nf):
            hand_out.start(f, more_ref.at[f])
    cos_part = cos_ref[...]
    sin_part = sin_ref[...]
    half = HD // 2
    scale = HD**-0.5
    dkv[...] = jnp.zeros_like(dkv)

    def unturned(d1, d2):
        return (d1 * cos_part + d2 * sin_part, d2 * cos_part - d1 * sin_part)

    def of_block(j, g, head, keys, keys_t, values):
        q = q_ref[head]
        do = dmix[head]
        p = jnp.exp(nn(keys, q) + mask[j] - lse_ref[head])
        ds = (p * (nn(values, do) - delta[head])).astype(BF)
        dkv[j, g] += nt(q, ds)
        dkv[j, KVH + g] += nt(do, p.astype(BF))
        return nn(keys_t, ds)

    for g in range(KVH):
        keys_t = [kv_ref[j, g] for j in range(1, nk)]
        keys = [k.T for k in keys_t]
        values = [kv_ref[j, KVH + g].T for j in range(1, nk)]

        def earlier(i, carried):
            head = g * GROUP + i
            delta[head] = (dmix[head].astype(F32) * mixed_ref[head].astype(F32)).sum(
                axis=0, keepdims=True
            )
            dq = of_block(1, g, head, keys[0], keys_t[0], values[0])
            for j in range(2, nk):
                dq = dq + of_block(j, g, head, keys[j - 1], keys_t[j - 1], values[j - 1])
            dq_some[head] = dq
            return carried

        lax.fori_loop(0, GROUP, earlier, 0, unroll=True)
        if g == 0:
            scatter.late()
        if g == 1 or carry == "sum":
            each(riders, "service")
    for j in range(1, nk):
        out_kv[j - 1] = dkv[j].astype(BF)
    sends = [
        remote(out_kv.at[j - 1], in_kv.at[j - 1], ssem.at[j - 1], rsem.at[j - 1],
               pc.along(pc.nb - j))
        for j in range(1, nk)
    ]
    for c in sends:
        c.start()
    for g in range(KVH):
        keys_t = kv_ref[0, g]
        keys = keys_t.T
        values = kv_ref[0, KVH + g].T

        def own_keys(i, carried):
            head = g * GROUP + i
            dq = (dq_some[head] + of_block(0, g, head, keys, keys_t, values)) * scale
            r1, r2 = unturned(dq[:half], dq[half:])
            gj[pl.ds(pl.multiple_of(head * HD, HD), half), :] = r1.astype(BF)
            gj[pl.ds(pl.multiple_of(head * HD + half, half), half), :] = r2.astype(BF)
            return carried

        lax.fori_loop(0, GROUP, own_keys, 0, unroll=True)
    for c in sends:
        c.wait()
    each(riders, "service")
    own = dkv[0]
    for j in range(1, nk):
        own = own + in_kv[j - 1].astype(F32)
    for g in range(KVH):
        r1, r2 = unturned(own[g, :half], own[g, half:])
        k0 = (H + g) * HD
        gj[k0 : k0 + half, :] = r1.astype(BF)
        gj[k0 + half : k0 + HD, :] = r2.astype(BF)
        v0 = (H + KVH + g) * HD
        gj[v0 : v0 + HD, :] = own[KVH + g].astype(BF)
    gjv = gj[...]
    n1 = width // 128
    dsmall_ref[n1 : n1 + qkv // 128, :] = rows_of(gjv.astype(F32))
    loads[0].wait()
    dqo_ref[:, :qkv] = nt(normed_ref[...], gjv).astype(BF)
    gn = nn(w[...], gjv)
    hidden = h_ref[...].astype(BF).astype(F32)
    scale_one = rms(hidden)
    unit = hidden * scale_one
    dsmall_ref[:n1, :] = rows_of(gn * unit)
    u = gn * g1
    gh_ref[...] = g_ref[...] + scale_one * (u - unit * jnp.mean(u * unit, axis=0, keepdims=True))

    def store(total):
        if carry == "columns":
            out_ref[...] = total.astype(BF)
        else:
            out_ref[...] = more_ref[...] + total

    scatter.finish(store)
    if carry == "columns":
        hand_out.finish(more_ref.at[0])
    each(riders, "finish")


def attention_backward(dims, nk, cid, layer, g, small, meta, docs, cos_part, sin_part, hidden,
                       normed, q, kv, lse, mixed, qo_all, plan, carry, late):
    width, rows = hidden.shape
    qkv = qo_all.shape[1] - width
    sds = jax.ShapeDtypeStruct
    outs = [
        sds((width, rows), F32),
        sds((width, qkv + width), BF),
        sds(((width + qkv) // 128, 128), F32),
    ] + plan.shapes
    dma = pltpu.SemaphoreType.DMA
    block = (2 * KVH, HD, rows)
    if carry == "columns":
        summed = (dims[1], late[0].shape[2], late[0].shape[3] // dims[0])
        outs += [sds(summed, BF), sds((dims[0] * dims[2],) + late[1].shape[1:], BF)]
        places = [VM, AN]
    else:
        summed = (width, rows)
        outs.append(sds(summed, F32))
        places = [VM]
    out = call(
        functools.partial(attention_backward_kernel, dims, nk, layer, plan, carry),
        "attention_backward",
        cid,
        tuple(outs),
        [VM] * 3 + plan.outs + places,
        [VM] * 12 + [AN] + [AN if carry == "columns" else VM, VM] + plan.places,
        [
            pltpu.VMEM((width, qkv), BF),
            pltpu.VMEM((width, width), BF),
            pltpu.VMEM((nk, rows, rows), F32),
            pltpu.VMEM((H, HD, rows), BF),
            pltpu.VMEM((nk,) + block, F32),
            pltpu.VMEM((H, 1, rows), F32),
            pltpu.VMEM((H, HD, rows), F32),
            pltpu.VMEM((nk - 1,) + block, BF),
            pltpu.VMEM((nk - 1,) + block, BF),
            pltpu.VMEM((qkv, rows), BF),
            dma((nk - 1,)),
            dma((nk - 1,)),
            dma((2,)),
        ]
        + plan.scratch
        + scatter_scratch(dims, *summed)[2:]
        + (
            row_scratch(dims) + [pltpu.VMEM(late[0].shape, BF), dma(())]
            if carry == "columns"
            else []
        ),
        (g, small, meta, docs, cos_part, sin_part, hidden, normed, q, kv, lse, mixed, qo_all,
         *late, *plan.arrays),
    )
    return (out[:3], out[3:])


def sequence_of(pc):
    if pc.two_level:
        return ((0, 1, 2, 3, 6, 7, 4, 5), 5, 7)
    return (tuple(range(pc.count)), pc.count - 1, pc.count - 1)


def lanes(slot, rows):
    return pl.ds(pl.multiple_of(slot * rows, rows), rows)


def transpose_into(dst, src):
    cols = src.shape[1]
    for c0 in range(0, cols, 128):
        c1 = min(c0 + 128, cols)
        dst[c0:c1, :] = src[:, c0:c1].T


def feed_forward_kernel(dims, *args):
    pc = Place(dims)
    feed_forward_part(pc, lambda: greet(pc, "mates", True), lambda: None, *args)


def feed_forward_part(pc, enter, ready, plan, x_ref, res_ref, wgu_ref, wd_ref, *refs):
    n = plan.count
    ins, refs = (refs[:n], refs[n:])
    out_ref, x_out, gu_out = refs[:3]
    outs, refs = (refs[3 : 3 + n], refs[3 + n :])
    x_all, gu_all, lsem, wgu_t, wd_t, gu, inner, near, away, back, hop, ss, sr, gs, gr = refs[:15]
    width, rows = x_ref.shape
    ff = wd_ref.shape[0]
    riders, _ = plan.board(pc, ins, outs, refs[15:])
    enter()
    gather = PlaneGather(pc, lambda q: x_all.at[:, lanes(q, rows)], gs, gr)
    scatter = PlaneScatter(pc, near, away, back, hop, ss, sr)
    x_all[:, lanes(pc.me, rows)] = x_ref[...]
    gather.start()
    ready()
    each(riders, "start")
    transpose_into(wgu_t, wgu_ref)
    transpose_into(wd_t, wd_ref)
    sequence, diagonal_at, early_at = sequence_of(pc)
    chunk = 32 if ff % 32 == 0 else 16

    def step_body(turn, carry):
        step = pick(turn, sequence)

        for k in range(pc.count):
            @pl.when(step == k)
            def _():
                gather.before(k)

        slot = pick(step, gather.order)
        sl = lanes(slot, rows)
        gu[...] = nn(wgu_t[...], x_all[:, sl])

        def act(i, c):
            r = pl.multiple_of(i * chunk, chunk)
            gate = gu[pl.ds(r, chunk), :]
            up = gu[pl.ds(ff + r, chunk), :]
            gu_all[pl.ds(r, chunk), sl] = gate.astype(BF)
            gu_all[pl.ds(ff + r, chunk), sl] = up.astype(BF)
            inner[pl.ds(r, chunk), :] = (gate * jax.nn.sigmoid(gate) * up).astype(BF)
            return c

        lax.fori_loop(0, ff // chunk, act, 0, unroll=True)
        scatter.put(step, nn(wd_t[...], inner[...]))

        @pl.when(turn == 3)
        def _():
            each(riders, "service")

        @pl.when(turn == diagonal_at)
        def _():
            scatter.diagonal()

        @pl.when(turn == early_at)
        def _():
            scatter.early()

        return carry

    lax.fori_loop(0, pc.count, step_body, 0)
    leaving = [
        pltpu.make_async_copy(gu_all, gu_out, lsem.at[0]),
        pltpu.make_async_copy(x_all, x_out, lsem.at[1]),
    ]
    each(leaving, "start")
    each(riders, "service")

    def store(total):
        out_ref[...] = res_ref[...] + total

    scatter.result(store)
    gather.finish()
    each(leaving, "wait")
    each(riders, "finish")


def feed_forward(dims, cid, x, residual, wgu, wd, plan):
    width, rows = x.shape
    count = dims[0] * dims[2]
    two_ff, ff = (wgu.shape[1], wd.shape[0])
    sds = jax.ShapeDtypeStruct
    dma = pltpu.SemaphoreType.DMA
    out = call(
        functools.partial(feed_forward_kernel, dims, plan),
        "feed_forward",
        cid,
        (
            sds((width, rows), F32),
            sds((width, count * rows), BF),
            sds((two_ff, count * rows), BF),
            *plan.shapes,
        ),
        [VM, AN, AN] + plan.outs,
        [VM] * 4 + plan.places,
        [
            pltpu.VMEM((width, count * rows), BF),
            pltpu.VMEM((two_ff, count * rows), BF),
            dma((2,)),
            pltpu.VMEM((two_ff, width), BF),
            pltpu.VMEM((width, ff), BF),
            pltpu.VMEM((two_ff, rows), F32),
            pltpu.VMEM((ff, rows), BF),
        ]
        + scatter_scratch(dims, width, rows)
        + gather_sems(dims)
        + plan.scratch,
        (x, residual, wgu, wd, *plan.arrays),
    )
    return (out[:3], out[3:])


def feed_backward_kernel(
    dims, layer, plan, g_ref, res_ref, x_in, gu_in, wgu_ref, wd_ref, small_ref, *refs
):
    n = plan.count
    ins, refs = (refs[:n], refs[n:])
    gr_ref, dwgu_ref, dwd_ref, dsmall_ref = refs[:4]
    outs, refs = (refs[4 : 4 + n], refs[4 + n :])
    x_all, gu_all, lsem, g_all, inner, ggu, gi, near, away, back, hop, ss, sr, gs, gr = refs[:15]
    coming = [
        pltpu.make_async_copy(gu_in, gu_all, lsem.at[0]),
        pltpu.make_async_copy(x_in, x_all, lsem.at[1]),
    ]
    each(coming, "start")
    pc = Place(dims)
    width, rows = g_ref.shape
    ff = wd_ref.shape[0]
    riders, _ = plan.board(pc, ins, outs, refs[15:])
    greet(pc, "mates", n > 0)
    gather = PlaneGather(pc, lambda q: g_all.at[:, lanes(q, rows)], gs, gr)
    scatter = PlaneScatter(pc, near, away, back, hop, ss, sr)
    g_all[:, lanes(pc.me, rows)] = g_ref[...].astype(BF)
    gather.start()
    each(riders, "start")
    coming[0].wait()
    sequence, diagonal_at, early_at = sequence_of(pc)
    chunk = 32 if ff % 32 == 0 else 16

    def step_body(turn, carry):
        step = pick(turn, sequence)

        for k in range(pc.count):
            @pl.when(step == k)
            def _():
                gather.before(k)

        slot = pick(step, gather.order)
        sl = lanes(slot, rows)
        gi[...] = nn(wd_ref[...], g_all[:, sl])

        def act(i, c):
            r = pl.multiple_of(i * chunk, chunk)
            gate = gu_all[pl.ds(r, chunk), sl].astype(F32)
            up = gu_all[pl.ds(ff + r, chunk), sl].astype(F32)
            grad = gi[pl.ds(r, chunk), :]
            sig = jax.nn.sigmoid(gate)
            silu = gate * sig
            inner[pl.ds(r, chunk), sl] = (silu * up).astype(BF)
            ggu[pl.ds(r, chunk), sl] = (grad * up * sig * (1.0 + gate * (1.0 - sig))).astype(BF)
            ggu[pl.ds(ff + r, chunk), sl] = (grad * silu).astype(BF)
            return c

        lax.fori_loop(0, ff // chunk, act, 0, unroll=True)
        scatter.put(step, nn(wgu_ref[...], ggu[:, sl]))

        @pl.when(turn == 3)
        def _():
            each(riders, "service")

        @pl.when(turn == diagonal_at)
        def _():
            scatter.diagonal()

        @pl.when(turn == early_at)
        def _():
            scatter.early()

        return carry

    lax.fori_loop(0, pc.count, step_body, 0)
    each(riders, "service")
    dwd_ref[...] = nt(inner[...], g_all[...]).astype(BF)
    scatter.late()
    coming[1].wait()
    part = width // 2
    for r in range(2):
        dwgu_ref[r * part : (r + 1) * part, :] = nt(
            x_all[r * part : (r + 1) * part, :], ggu[...]
        ).astype(BF)

    def store(total):
        residual = res_ref[...]
        scale_two = rms(residual)
        unit = residual * scale_two
        n1 = width // 128
        dsmall_ref[...] = rows_of(total * unit)
        u = total * column(padded_t(small_ref[layer]), n1, n1)
        gr_ref[...] = g_ref[...].astype(BF).astype(F32) + scale_two * (
            u - unit * jnp.mean(u * unit, axis=0, keepdims=True)
        )

    scatter.finish(store)
    gather.finish()
    each(riders, "finish")


def feed_backward(dims, cid, layer, g, residual, x_all, gu_all, wgu, wd, small, plan):
    width, rows = g.shape
    count = dims[0] * dims[2]
    two_ff, ff = (wgu.shape[1], wd.shape[0])
    sds = jax.ShapeDtypeStruct
    dma = pltpu.SemaphoreType.DMA
    out = call(
        functools.partial(feed_backward_kernel, dims, layer, plan),
        "feed_backward",
        cid,
        (
            sds((width, rows), F32),
            sds(wgu.shape, BF),
            sds(wd.shape, BF),
            sds((width // 128, 128), F32),
            *plan.shapes,
        ),
        [VM] * 4 + plan.outs,
        [VM, VM, AN, AN, VM, VM, VM] + plan.places,
        [
            pltpu.VMEM((width, count * rows), BF),
            pltpu.VMEM((two_ff, count * rows), BF),
            dma((2,)),
            pltpu.VMEM((width, count * rows), BF),
            pltpu.VMEM((ff, count * rows), BF),
            pltpu.VMEM((two_ff, count * rows), BF),
            pltpu.VMEM((ff, rows), F32),
        ]
        + scatter_scratch(dims, width, rows)
        + gather_sems(dims)
        + plan.scratch,
        (g, residual, x_all, gu_all, wgu, wd, small, *plan.arrays),
    )
    return (out[:4], out[4:])


def feed_both_kernel(dims, *args):
    pc = Place(dims)
    feed_both_part(pc, lambda: greet(pc, "mates", False), lambda: None, *args)


def feed_both_part(
    pc, enter, ready, layer, x_ref, res_ref, g_ref, g_all, wgu_ref, wd_ref, small_ref,
    gr_ref, dwgu_ref, dwd_ref, dsmall_ref, parts_ref,
    x_all, inner, ggu, wgu_t, wd_t, gu, gi, near, away, back, hop, ss, sr, gs, gr,
):
    width, rows = g_ref.shape
    ff = wd_ref.shape[0]
    enter()
    gather = PlaneGather(pc, lambda q: x_all.at[:, lanes(q, rows)], gs, gr)
    scatter = PlaneScatter(pc, near, away, back, hop, ss, sr)
    x_all[:, lanes(pc.me, rows)] = x_ref[...]
    gather.start()
    ready()
    transpose_into(wgu_t, wgu_ref)
    transpose_into(wd_t, wd_ref)
    sequence, diagonal_at, early_at = sequence_of(pc)
    chunk = 32 if ff % 32 == 0 else 16

    def step_body(turn, carry):
        step = pick(turn, sequence)

        for k in range(pc.count):
            @pl.when(step == k)
            def _():
                gather.before(k)

        slot = pick(step, gather.order)
        sl = lanes(slot, rows)
        gu[...] = nn(wgu_t[...], x_all[:, sl])
        gi[...] = nn(wd_ref[...], g_all[:, sl])

        def act(i, c):
            r = pl.multiple_of(i * chunk, chunk)
            gate = gu[pl.ds(r, chunk), :]
            up = gu[pl.ds(ff + r, chunk), :]
            grad = gi[pl.ds(r, chunk), :]
            sig = jax.nn.sigmoid(gate)
            silu = gate * sig
            inner[pl.ds(r, chunk), sl] = (silu * up).astype(BF)
            ggu[pl.ds(r, chunk), sl] = (grad * up * sig * (1.0 + gate * (1.0 - sig))).astype(BF)
            ggu[pl.ds(ff + r, chunk), sl] = (grad * silu).astype(BF)
            return c

        lax.fori_loop(0, ff // chunk, act, 0, unroll=True)
        scatter.put(step, nn(wgu_ref[...], ggu[:, sl]))

        @pl.when(turn == diagonal_at)
        def _():
            scatter.diagonal()

        @pl.when(turn == early_at)
        def _():
            scatter.early()

        parts_ref[slot] = nn(wd_t[...], inner[:, sl]).astype(BF)
        return carry

    lax.fori_loop(0, pc.count, step_body, 0)
    dwd_ref[...] = nt(inner[...], g_all[...]).astype(BF)
    scatter.late()
    part = width // 2
    for r in range(2):
        dwgu_ref[r * part : (r + 1) * part, :] = nt(
            x_all[r * part : (r + 1) * part, :], ggu[...]
        ).astype(BF)

    def store(total):
        residual = res_ref[...]
        scale_two = rms(residual)
        unit = residual * scale_two
        n1 = width // 128
        dsmall_ref[...] = rows_of(total * unit)
        u = total * column(padded_t(small_ref[layer]), n1, n1)
        gr_ref[...] = g_ref[...].astype(BF).astype(F32) + scale_two * (
            u - unit * jnp.mean(u * unit, axis=0, keepdims=True)
        )

    scatter.finish(store)
    gather.finish()


def feed_both(dims, cid, layer, x, residual, g, g_all, wgu, wd, small):
    width, rows = g.shape
    count = dims[0] * dims[2]
    two_ff, ff = (wgu.shape[1], wd.shape[0])
    sds = jax.ShapeDtypeStruct
    dma = pltpu.SemaphoreType.DMA
    return call(
        functools.partial(feed_both_kernel, dims, layer),
        "feed_both",
        cid,
        (
            sds((width, rows), F32),
            sds(wgu.shape, BF),
            sds(wd.shape, BF),
            sds((width // 128, 128), F32),
            sds((count, width, rows), BF),
        ),
        [VM] * 5,
        [VM] * 7,
        [
            pltpu.VMEM((width, count * rows), BF),
            pltpu.VMEM((ff, count * rows), BF),
            pltpu.VMEM((two_ff, count * rows), BF),
            pltpu.VMEM((two_ff, width), BF),
            pltpu.VMEM((width, ff), BF),
            pltpu.VMEM((two_ff, rows), F32),
            pltpu.VMEM((ff, rows), F32),
        ]
        + scatter_scratch(dims, width, rows)
        + gather_sems(dims),
        (x, residual, g, g_all, wgu, wd, small),
    )


def wait_for_weights(pc, riders, gather, wd_all, pieces, wd, sem, others):
    last_blocks(pc, gather)
    each(riders, "finish")
    load = pltpu.make_async_copy(wd_all, pieces, sem)
    load.start()
    each(others, "wait")
    load.wait()
    half = pieces.shape[1]
    for t in range(pc.nb):
        wd[t * half : (t + 1) * half, :] = pieces[t]
    gather.finish()


def lower_kernel(dims, nk, plan_a, plan_f, *refs):
    pc = Place(dims)
    a_in, wgu_in, refs = (refs[:9], refs[9], refs[10:])
    f_in, refs = (refs[: plan_f.count], refs[plan_f.count :])
    a_out, wd_all, qo_next, refs = (refs[:6], refs[6], refs[7], refs[8:])
    f_out, refs = (refs[: 3 + plan_f.count], refs[3 + plan_f.count :])
    n2, wgu, pieces, wd, wsem, dsem, refs = (*refs[:6], refs[6:])
    a_scratch, f_scratch = (refs[: 10 + len(plan_a.scratch) + 2], refs[10 + len(plan_a.scratch) + 2 :])
    load = pltpu.make_async_copy(wgu_in, wgu, wsem)
    load.start()
    riders, gather = attention_forward_part(
        pc, nk, 0, plan_a, "columns", *a_in, *a_out, n2, wd_all, qo_next, *a_scratch
    )
    feed_forward_part(
        pc,
        lambda: None,
        lambda: wait_for_weights(pc, riders, gather, wd_all, pieces, wd, dsem, [load]),
        plan_f, n2, a_out[5], wgu, wd, *f_in, *f_out, *f_scratch,
    )


def lower_layer(dims, nk, cid, hidden, small, meta, docs, cos_part, sin_part, qo, plan_a, block,
                wgu, plan_f):
    ns, nb, nf = dims
    width, rows = hidden.shape
    count = ns * nf
    qkv = qo.shape[1] - width
    two_ff = wgu.shape[1]
    ff = two_ff // 2
    sds = jax.ShapeDtypeStruct
    dma = pltpu.SemaphoreType.DMA
    outs = [
        sds((width, rows), BF),
        sds((H, HD, rows), BF),
        sds((nk, 2 * KVH, HD, rows), BF),
        sds((H, 1, rows), F32),
        sds((H, HD, rows), BF),
        sds((width, rows), F32),
        *plan_a.shapes,
        sds((nb, nf, block.shape[2], ns * block.shape[3]), BF),
        sds((width, rows), F32),
        sds((width, count * rows), BF),
        sds((two_ff, count * rows), BF),
        *plan_f.shapes,
    ]
    out = call(
        functools.partial(lower_kernel, dims, nk, plan_a, plan_f),
        "lower_layer",
        cid,
        tuple(outs),
        [VM] * 6 + plan_a.outs + [VM] + [VM, AN, AN] + plan_f.outs,
        [VM] * 6 + [AN, VM] + plan_a.places + [AN] + plan_f.places,
        [
            pltpu.VMEM((width, rows), BF),
            pltpu.VMEM(wgu.shape, BF),
            pltpu.VMEM((nb, ff // nb, width), BF),
            pltpu.VMEM((ff, width), BF),
            dma(()),
            dma(()),
        ]
        + attention_scratch(dims, nk, width, rows, qkv)
        + plan_a.scratch
        + gather_sems(dims)
        + [
            pltpu.VMEM((width, count * rows), BF),
            pltpu.VMEM((two_ff, count * rows), BF),
            dma((2,)),
            pltpu.VMEM((two_ff, width), BF),
            pltpu.VMEM((width, ff), BF),
            pltpu.VMEM((two_ff, rows), F32),
            pltpu.VMEM((ff, rows), BF),
        ]
        + scatter_scratch(dims, width, rows)
        + gather_sems(dims)
        + plan_f.scratch,
        (hidden, small, meta, docs, cos_part, sin_part, qo, block, *plan_a.arrays, wgu,
         *plan_f.arrays),
    )
    return (out[:6], out[6], out[7], out[8:11], out[11:])


def upper_kernel(dims, nk, plan, *refs):
    pc = Place(dims)
    a_in, g_ref, wgu_in, refs = (refs[:9], refs[9], refs[10], refs[11:])
    a_out, wd_all, f_out, refs = (refs[:6], refs[6], refs[7:12], refs[12:])
    n2, g_all, wgu, pieces, wd, wsem, dsem, refs = (*refs[:7], refs[7:])
    a_scratch, f_scratch = (refs[: 10 + len(plan.scratch) + 2], refs[10 + len(plan.scratch) + 2 :])
    load = pltpu.make_async_copy(wgu_in, wgu, wsem)
    load.start()
    riders, gather = attention_forward_part(
        pc, nk, 1, plan, "lanes", *a_in, *a_out, n2, wd_all, g_all, *a_scratch
    )
    feed_both_part(
        pc,
        lambda: None,
        lambda: wait_for_weights(pc, riders, gather, wd_all, pieces, wd, dsem, [load]),
        1, n2, a_out[5], g_ref, g_all, wgu, wd, a_in[1], *f_out, *f_scratch,
    )


def upper_layer(dims, nk, cid, hidden, small, meta, docs, cos_part, sin_part, qo, plan, block, g,
                wgu):
    ns, nb, nf = dims
    width, rows = hidden.shape
    count = ns * nf
    qkv = qo.shape[1] - width
    two_ff = wgu.shape[1]
    ff = two_ff // 2
    sds = jax.ShapeDtypeStruct
    dma = pltpu.SemaphoreType.DMA
    outs = [
        sds((width, rows), BF),
        sds((H, HD, rows), BF),
        sds((nk, 2 * KVH, HD, rows), BF),
        sds((H, 1, rows), F32),
        sds((H, HD, rows), BF),
        sds((width, rows), F32),
        *plan.shapes,
        sds((width, rows), F32),
        sds(wgu.shape, BF),
        sds((ff, width), BF),
        sds((width // 128, 128), F32),
        sds((count, width, rows), BF),
    ]
    out = call(
        functools.partial(upper_kernel, dims, nk, plan),
        "upper_layer",
        cid,
        tuple(outs),
        [VM] * 6 + plan.outs + [VM] * 5,
        [VM] * 6 + [AN, VM] + plan.places + [VM, AN],
        [
            pltpu.VMEM((width, rows), BF),
            pltpu.VMEM((width, count * rows), BF),
            pltpu.VMEM(wgu.shape, BF),
            pltpu.VMEM((nb, ff // nb, width), BF),
            pltpu.VMEM((ff, width), BF),
            dma(()),
            dma(()),
        ]
        + attention_scratch(dims, nk, width, rows, qkv)
        + plan.scratch
        + gather_sems(dims)
        + [
            pltpu.VMEM((width, count * rows), BF),
            pltpu.VMEM((ff, count * rows), BF),
            pltpu.VMEM((two_ff, count * rows), BF),
            pltpu.VMEM((two_ff, width), BF),
            pltpu.VMEM((width, ff), BF),
            pltpu.VMEM((two_ff, rows), F32),
            pltpu.VMEM((ff, rows), F32),
        ]
        + scatter_scratch(dims, width, rows)
        + gather_sems(dims),
        (hidden, small, meta, docs, cos_part, sin_part, qo, block, *plan.arrays, g, wgu),
    )
    return (out[:6], out[7:])


def reduce_kernel(
    dims, qo, terms, sa0, sa1, sb0, sb1, wd1, gu0a, gu0, wd0,
    qo_out, small_out, gu_got, wd_got,
    held, rest_gu, gsum, wsum, small, sm_in, sm_mid, sm_line, z_out, mine, give,
    lsem, ws, wr, ls, lr, zs, zr, *rest
):
    pc = Place(dims)
    ns, nb, nf = dims
    coming = pltpu.make_async_copy(qo, held, lsem.at[1])
    coming.start()
    cut = gu0a.shape[0]
    coming_gu = pltpu.make_async_copy(gu0.at[:, cut:nf], rest_gu, lsem.at[2])
    coming_gu.start()
    n1 = sb0.shape[0]
    per = small.shape[0] // ns
    nr = sa0.shape[0] + n1
    small[...] = jnp.zeros_like(small)
    for l, (a, g) in enumerate(((sa0, sb0), (sa1, sb1))):
        small[l * per : l * per + n1] = a[0:n1]
        small[l * per + n1 : l * per + 2 * n1] = g[...]
        small[l * per + 2 * n1 : l * per + nr] = a[n1 : a.shape[0]]
    greet(pc, "all", True)

    def keep(value):
        wsum[...] = value.astype(BF)

    def keep_of(l):
        def store(value):
            mine[l] = value

        return store

    line = LineReduce(pc, lambda t: wd0[t], keep, rest[0:4])
    ends = [
        LineReduce(pc, lambda t: z_out[t], keep_of(0), rest[4:8]),
        LineReduce(pc, lambda t: terms[t], keep_of(1), rest[8:12]),
    ]
    def keep_gu(value):
        gsum[...] = value.astype(BF)

    line_gu = LineReduce(pc, lambda t: rest_gu[t], keep_gu, rest[19:23])
    ends[1].start()
    coming_gu.wait()
    line_gu.start()
    line.start()
    scatter = ReadyScatter(
        pc, lambda q: columns_of(held, q, nf, z_out.shape[2]), *rest[15:19]
    )
    coming.wait()
    scatter.start()
    smalls = [
        remote(small, sm_in.at[e - 1], ls.at[e - 1], lr.at[e - 1], pc.plane(e))
        for e in range(1, pc.count)
    ]
    for c in smalls:
        c.start()
    scatter.diagonal()
    scatter.early()
    hand_out = RowSends(pc, 0, gu_got, rest[12:15])
    for f in range(cut):
        hand_out.start(f, gu0a.at[f])

    def split(l, ref):
        @pl.when(pc.s == l)
        def _():
            pltpu.make_async_copy(ref, wd_got.at[l], lsem.at[0]).start()

        @pl.when(pc.s != l)
        def _():
            remote(ref, wd_got.at[pc.s], ws.at[0], wr.at[0], (l, pc.b, pc.f)).start()

    split(1, wd1)
    ends[1].service()
    line_gu.service()
    line.service()
    scatter.late()
    ends[1].service()
    total = small[...]
    for e, c in enumerate(smalls):
        c.wait()
        total = total + sm_in[e]
    sm_mid[...] = total
    lines = [
        remote(sm_mid, sm_line.at[d - 1], zs.at[d - 1], zr.at[d - 1], pc.along(d))
        for d in range(1, nb)
    ]
    for c in lines:
        c.start()
    line_gu.service()
    line.service()

    def store(value):
        z_out[...] = value.astype(BF)

    scatter.finish(store)
    ends[0].start()
    ends[1].finish()
    line_gu.finish()
    for f in range(cut, nf):
        hand_out.start(f, gsum.at[f - cut])
    ends[0].service()
    line.finish()
    split(0, wsum)
    ends[0].finish()
    mate = (ns - 1 - pc.s, pc.b, pc.f)
    swap = remote(give.at[0], give.at[1], ws.at[1], wr.at[1], mate)
    give[0] = mine[ns - 1 - pc.s].astype(BF)
    swap.start()
    qo_out[pc.s] = mine[pc.s]
    total = sm_mid[...]
    for d, c in enumerate(lines):
        c.wait()
        total = total + sm_line[d]
    small_out[...] = total
    hand_out.finish(gu0a.at[0])
    pltpu.make_async_copy(wsum, wd_got.at[pc.s], lsem.at[0]).wait()
    remote(wsum, wd_got.at[pc.s], ws.at[0], wr.at[0], mate).wait()
    swap.wait()
    qo_out[ns - 1 - pc.s] = give[1].astype(F32)


def reduce_gradients(dims, cid, qo, terms, smalls, wd1, gu0a, gu0, wd0):
    ns, nb, nf = dims
    count = ns * nf
    dr, wide = terms.shape[1:]
    two_ff = gu0.shape[3]
    cut = gu0a.shape[0]
    half, width = wd1.shape
    rows = smalls[0].shape[0] + smalls[2].shape[0]
    small = (ns * (-(-rows // 8) * 8), 128)
    sds = jax.ShapeDtypeStruct
    dma = pltpu.SemaphoreType.DMA
    return call(
        functools.partial(reduce_kernel, dims),
        "reduce_gradients",
        cid,
        (
            sds((ns, dr, wide), F32),
            sds(small, F32),
            sds((count, dr, two_ff), BF),
            sds((ns, half, width), BF),
        ),
        [VM] * 4,
        [AN] + [VM] * 7 + [AN, VM],
        [
            pltpu.VMEM(qo.shape, BF),
            pltpu.VMEM((nb, nf - cut, dr, two_ff), BF),
            pltpu.VMEM((nf - cut, dr, two_ff), BF),
            pltpu.VMEM((half, width), BF),
            pltpu.VMEM(small, F32),
            pltpu.VMEM((count - 1,) + small, F32),
            pltpu.VMEM(small, F32),
            pltpu.VMEM((nb - 1,) + small, F32),
            pltpu.VMEM((nb, dr, wide), BF),
            pltpu.VMEM((ns, dr, wide), F32),
            pltpu.VMEM((2, dr, wide), BF),
            dma((3,)),
            dma((2,)),
            dma((2,)),
            dma((count - 1,)),
            dma((count - 1,)),
            dma((nb - 1,)),
            dma((nb - 1,)),
        ]
        + reduce_scratch(dims, half, width)
        + reduce_scratch(dims, dr, wide) * 2
        + row_scratch(dims)
        + scatter_scratch(dims, nb, dr, wide)[2:]
        + reduce_scratch(dims, nf - cut, dr, two_ff),
        (qo, terms, *smalls, wd1, gu0a, gu0, wd0),
    )


def lay_out_kernel(
    dims, gu0, gu1, wd, qo, small, out0, out1, gh0, gh1, take_out, take_grad,
    block_out, input_grad, g1, wqkv, bqkv, wout, g2, wgu, wdn
):
    ns, nb, nf = dims
    half = wd.shape[1]
    s = lax.axis_index("section")
    qkv = wqkv.shape[2]
    width = wout.shape[2]
    full = jnp.concatenate([qo[y] for y in range(ns)], axis=1)
    wqkv[0] = full[:, :qkv]
    wout[0] = full[:, qkv:]
    for y in range(ns):
        wdn[0, y * half : (y + 1) * half, :] = wd[y].astype(F32)
    for l, gu in enumerate((gu0, gu1)):
        @pl.when(s == l)
        def _():
            for y in range(ns):
                for f in range(nf):
                    got = gu[y * nf + f].astype(F32)
                    for part in range(2):
                        for b in range(nb):
                            c0 = column_start(dims, part, b, f, y, half)
                            k0 = (part * nb + b) * half
                            wgu[0, :, c0 : c0 + half] = got[:, k0 : k0 + half]
    n1 = width // 128
    per = small.shape[0] // ns
    rows = small[pl.ds(pl.multiple_of(s * per, 8), per), :]
    for k in range(n1):
        g1[0:1, k * 128 : (k + 1) * 128] = rows[k : k + 1]
        g2[0:1, k * 128 : (k + 1) * 128] = rows[n1 + k : n1 + k + 1]
    for k in range(qkv // 128):
        bqkv[0:1, k * 128 : (k + 1) * 128] = rows[2 * n1 + k : 2 * n1 + k + 1]
    for out, pair, take in (
        (block_out, (out0, out1), take_out),
        (input_grad, (gh0, gh1), take_grad),
    ):
        for l in range(ns):
            @pl.when(s == l)
            def _():
                out[0, l] = pair[l][...].T
                out[0, 1 - l] = take[...].T.astype(F32)


def lay_out(dims, qkv, args):
    ns, nb, nf = dims
    gu, wd, qo = (args[0], args[2], args[3])
    width, rows = args[5].shape
    dr = qo.shape[1]
    sds = jax.ShapeDtypeStruct
    tokens = sds((1, ns, rows, width), F32)
    return pl.pallas_call(
        functools.partial(lay_out_kernel, dims),
        name="lay_out",
        out_shape=(
            tokens,
            tokens,
            sds((1, width), F32),
            sds((1, dr, qkv), F32),
            sds((1, qkv), F32),
            sds((1, dr, width), F32),
            sds((1, width), F32),
            sds((1, dr, gu.shape[0] * gu.shape[2]), F32),
            sds((1, ns * wd.shape[1], width), F32),
        ),
        in_specs=[VM] * len(args),
        out_specs=[VM] * 9,
        compiler_params=pltpu.CompilerParams(vmem_limit_bytes=VMEM_LIMIT),
    )(*args)


def shards(
    dims,
    tokens_in,
    positions,
    doc_ids,
    out_grad,
    norm1_gain,
    w_qkv,
    b_qkv,
    w_out,
    norm2_gain,
    w_gate_up,
    w_down,
):
    ns, nb, nf = dims
    seqs, rows, width = tokens_in.shape
    s = lax.axis_index("section")
    b = lax.axis_index("blk")
    dr = w_qkv.shape[1]
    qkv = w_qkv.shape[2]
    fr = w_down.shape[1]
    half = fr // ns
    ff = nb * half
    nk = min(nb, 1 + (LONGEST - 1 + rows - 1) // rows)

    tokens = lax.dynamic_index_in_dim(tokens_in, s, 0, keepdims=False)
    cot = lax.dynamic_index_in_dim(out_grad, s, 0, keepdims=False)
    pos = lax.dynamic_index_in_dim(positions, s, 0, keepdims=False)
    docs = lax.dynamic_index_in_dim(doc_ids, s, 0, keepdims=False).astype(F32)
    freq = jnp.exp(jnp.arange(HD // 2, dtype=F32) * (-2.0 / HD) * math.log(1000000.0))
    phase = freq[:, None] * pos.astype(F32)[None, :]
    cos_part, sin_part = (jnp.cos(phase), jnp.sin(phase))
    docs = docs.reshape(nb, rows)
    picked = (b - jnp.arange(nk) + nb) % nb
    meta = jnp.take(docs, picked, axis=0).reshape(nk * rows // 128, 128)
    query_docs = lax.dynamic_slice_in_dim(docs, b, 1)
    hidden = tokens.T.astype(F32)
    g = cot.T.astype(F32)

    wd = w_down[0].reshape(ns, half, width)
    small = jnp.concatenate([norm1_gain[0], norm2_gain[0], b_qkv[0]])
    total = -(-small.shape[0] // 1024) * 1024
    small = jnp.pad(small, (0, total - small.shape[0])).reshape(-1, 128)
    gup, wdp, gu_first, qo_first, qz, small_all = gather_weights(
        dims, w_gate_up, w_qkv, w_out, wd, small
    )
    cols = qkv + width
    wide = (width, 2 * ff)

    def ride(*pairs):
        return Riders(dims, tuple(a for a, _ in pairs), tuple(v for _, v in pairs))

    common = (small_all, meta, query_docs, cos_part, sin_part)
    qo0 = qo_first.reshape(width, cols)
    wgu0 = gu_first.reshape(wide)
    first = ride((("gather", 0), wdp))
    second = ride((("gather", 1), gup))
    third = ride((("gather", 1), wdp))
    together = half % 8 == 0
    if together:
        a0, wd0, qo1, f0, (gu1,) = lower_layer(
            dims, nk, 1, hidden, *common, qo0, first, qz, wgu0, second
        )
    else:
        a0, (wd0, qo1) = attention_forward(
            dims, nk, 1, 0, hidden, *common, qo0, first, "columns", qz
        )
        f0, (gu1,) = feed_forward(dims, 3, a0[6], a0[5], wgu0, wd0.reshape(ff, width), second)
    qo1 = qo1.reshape(width, cols)
    wd0 = wd0.reshape(ff, width)
    wgu1 = gu1.reshape(wide)
    if together:
        a1, b1 = upper_layer(dims, nk, 2, f0[0], *common, qo1, third, cot.T, g, wgu1)
    else:
        a1, (wd1, g_all) = attention_forward(
            dims, nk, 2, 1, f0[0], *common, qo1, third, "lanes", cot.T
        )
        wd1 = wd1.reshape(ff, width)
        b1 = feed_both(dims, 4, 1, a1[6], a1[5], g, g_all, wgu1, wd1, small_all)

    line_gu = (nb, nf, dr, 2 * ff)
    line_wd = (nb, half, width)
    line_qo = (nb, nf, dr, cols)
    everything = (0, half)
    ab1, (dwd1, out1) = attention_backward(
        dims, nk, 7, 1, b1[0], *common, f0[0], *a1[:5], qo1,
        ride((("reduce", everything), b1[2].reshape(line_wd))), "sum", (b1[4], a1[5]),
    )
    b0, (dgu1,) = feed_backward(
        dims, 6, 0, ab1[0], a0[5], f0[1], f0[2], wgu0, wd0, small_all,
        ride((("reduce", (0, nf)), b1[1].reshape(line_gu))),
    )
    dgu0 = b0[1].reshape(line_gu)
    cut = nf - nf // 4
    ab0, (dgu0a, terms, gu_got1) = attention_backward(
        dims, nk, 8, 0, b0[0], *common, hidden, *a0[:5], qo0,
        ride((("reduce", (0, cut)), dgu0)),
        "columns", (ab1[1].reshape(line_qo), dgu1),
    )

    def swapped(values):
        give = jnp.where(s == 0, values[1], values[0]).astype(BF)
        return lax.ppermute(give, "section", [(0, 1), (1, 0)])

    take_out = swapped((f0[0], out1))
    take_grad = swapped((ab0[0], ab1[0]))
    grad_qo, small_sum, gu_got0, wd_got = reduce_gradients(
        dims, 9, ab0[1].reshape(line_qo), terms,
        (ab0[2], ab1[2], b0[3], b1[3]), dwd1, dgu0a, dgu0, b0[2].reshape(line_wd),
    )
    return lay_out(
        dims,
        qkv,
        (gu_got0, gu_got1, wd_got, grad_qo, small_sum, f0[0], out1, ab0[0], ab1[0], take_out,
         take_grad),
    )


def solution(mesh):
    dims = (mesh.shape["section"], mesh.shape["blk"], mesh.shape["fsdp"])
    return jax.shard_map(
        functools.partial(shards, dims),
        mesh=mesh,
        in_specs=(
            P("fsdp", "blk", None),
            P("fsdp", "blk"),
            P("fsdp", None),
            P("fsdp", "blk", None),
            P("section", None),
            P("section", ("blk", "fsdp"), None),
            P("section", None),
            P("section", ("blk", "fsdp"), None),
            P("section", None),
            P("section", ("blk", "fsdp"), None),
            P("section", ("blk", "fsdp"), None),
        ),
        out_specs=(
            P("section", "fsdp", "blk", None),
            P("section", "fsdp", "blk", None),
            P("section", None),
            P("section", ("blk", "fsdp"), None),
            P("section", None),
            P("section", ("blk", "fsdp"), None),
            P("section", None),
            P("section", ("blk", "fsdp"), None),
            P("section", ("blk", "fsdp"), None),
        ),
        check_vma=False,
    )
```

```python
import functools
import math

import jax
import jax.numpy as jnp
from jax import lax
from jax.experimental import pallas as pl
from jax.experimental.pallas import tpu as pltpu
from jax.sharding import PartitionSpec as P

H = 14
KVH = 2
HD = 64
GROUP = H // KVH
LONGEST = 512
NEG = -1e30
BF = jnp.bfloat16
F32 = jnp.float32
MESH = pl.DeviceIdType.MESH
VMEM_LIMIT = 60 * 2**20
VM = pl.BlockSpec(memory_space=pltpu.VMEM)
AN = pl.BlockSpec(memory_space=pl.ANY)


def nn(a, b):
    return lax.dot_general(a, b, (((1,), (0,)), ((), ())), preferred_element_type=F32)


def nt(a, b):
    return lax.dot_general(a, b, (((1,), (1,)), ((), ())), preferred_element_type=F32)


def tn(a, b):
    return lax.dot_general(a, b, (((0,), (0,)), ((), ())), preferred_element_type=F32)


def other(f):
    return f + 1 - 2 * (f % 2)


class Place:
    def __init__(self, dims):
        self.ns, self.nb, self.nf = dims
        self.count = self.ns * self.nf
        self.s = lax.axis_index("section")
        self.b = lax.axis_index("blk")
        self.f = lax.axis_index("fsdp")
        self.me = self.s * self.nf + self.f
        self.two_level = self.ns == 2 and self.nf == 4

    def plane(self, e):
        q = (self.me + e) % self.count
        return (q // self.nf, self.b, q % self.nf)

    def slot_from(self, e):
        return (self.me + self.count - e) % self.count

    def along(self, d):
        return (self.s, (self.b + d) % self.nb, self.f)

    def mates(self):
        s, b, f = (self.s, self.b, self.f)
        xf = (f + 2) % 4
        return ((s, b, other(f)), (s, b, xf), (1 - s, b, f))

    def slots(self):
        s, f = (self.s, self.f)
        xf = (f + 2) % 4
        t = 1 - s
        return (
            s * 4 + f,
            s * 4 + other(f),
            s * 4 + xf,
            t * 4 + f,
            s * 4 + other(xf),
            t * 4 + other(f),
            t * 4 + xf,
            t * 4 + other(xf),
        )


def pick(i, values):
    total = 0
    for k, v in enumerate(values):
        total = total + jnp.where(i == k, v, 0)
    return total


def greet(place, plane, along):
    barrier = pltpu.get_barrier_semaphore()
    count = 0
    if plane:
        if place.two_level and plane == "mates":
            targets = list(place.mates())
        else:
            targets = [place.plane(e) for e in range(1, place.count)]
        for t in targets:
            pl.semaphore_signal(barrier, 1, device_id=t, device_id_type=MESH)
        count += len(targets)
    if along:
        for d in range(1, place.nb):
            pl.semaphore_signal(barrier, 1, device_id=place.along(d), device_id_type=MESH)
        count += place.nb - 1
    pl.semaphore_wait(barrier, count)


def remote(src, dst, ssem, rsem, device):
    return pltpu.make_async_remote_copy(
        src_ref=src,
        dst_ref=dst,
        send_sem=ssem,
        recv_sem=rsem,
        device_id=device,
        device_id_type=MESH,
    )


def cut_in(parts, view, c):
    n = view.shape[0] // parts
    return view.at[pl.ds(c * n, n)]


def gather_sems(dims):
    n = 2 * (dims[0] * dims[2] - 1)
    return [pltpu.SemaphoreType.DMA((n,)), pltpu.SemaphoreType.DMA((n,))]


class PlaneGather:
    def __init__(self, place, slot, ssem, rsem):
        self.place, self.slot, self.ssem, self.rsem = (place, slot, ssem, rsem)
        self.parts = 2 if place.two_level else 1
        if place.two_level:
            self.order = place.slots()
        else:
            self.order = tuple(place.slot_from(e) for e in range(place.count))

    def copy(self, k, c, q, device):
        v = cut_in(self.parts, self.slot(q), c)
        i = k * self.parts + c
        return remote(v, v, self.ssem.at[i], self.rsem.at[i], device)

    def start(self):
        pc = self.place
        if pc.two_level:
            core, xm, ym = pc.mates()
            for c in range(2):
                self.copy(1, c, self.order[0], xm).start()
                self.copy(2, c, self.order[0], ym).start()
            for c in range(2):
                self.copy(0, c, self.order[0], core).start()
        else:
            for e in range(1, pc.count):
                self.copy(e - 1, 0, self.order[0], pc.plane(e)).start()

    def came(self, k, c):
        self.copy(k, c, self.order[k + 1], self.place.plane(1)).wait_recv()

    def before(self, step):
        if step == 0:
            return
        pc = self.place
        if not pc.two_level:
            self.came(step - 1, 0)
            return
        core, xm, ym = pc.mates()
        h = pc.f % 2
        if step == 2:
            which = h * self.order[3] + (1 - h) * self.order[2]
            far = (
                h * xm[0] + (1 - h) * ym[0],
                pc.b,
                h * xm[2] + (1 - h) * ym[2],
            )
            for c in range(2):
                self.came(1, c)
                self.came(2, c)
                self.copy(5, c, which, far).start()
                self.copy(3, c, self.order[2], core).start()
                self.copy(4, c, self.order[3], core).start()
        elif step == 3:
            return
        elif step == 6:
            for c in range(2):
                self.came(5, c)
                self.copy(6, c, self.order[6], core).start()
        else:
            for c in range(2):
                self.came(step - 1, c)

    def finish(self):
        n = self.place.count - 1
        for k in range(n):
            for c in range(self.parts):
                self.copy(k, c, self.order[0], self.place.plane(1)).wait_send()


class PlaneScatter:
    def __init__(self, place, near, away, back, hop, ssem, rsem):
        self.place = place
        self.near, self.away, self.back, self.hop = (near, away, back, hop)
        self.ssem, self.rsem = (ssem, rsem)

    def put(self, step, value):
        pc = self.place
        if not pc.two_level:
            @pl.when(step == 0)
            def _():
                self.near[0] = value

            @pl.when(step > 0)
            def _():
                e = pc.count - step
                self.away[e - 1] = value.astype(BF)
                q = (pc.me + e) % pc.count
                remote(
                    self.away.at[e - 1],
                    self.back.at[e - 1],
                    self.ssem.at[e - 1],
                    self.rsem.at[e - 1],
                    (q // pc.nf, pc.b, q % pc.nf),
                ).start()
            return
        core, xm, ym = pc.mates()
        here = (step == 0) | (step == 2) | (step == 3) | (step == 6)
        q = pick(step, (0, 0, 1, 2, 1, 2, 3, 3))

        @pl.when(here)
        def _():
            self.near[q] = value

        @pl.when(jnp.logical_not(here))
        def _():
            self.away[q] = value.astype(BF)
            self.core_copy(q).start()

    def core_copy(self, q):
        core = self.place.mates()[0]
        return remote(self.away.at[q], self.back.at[q], self.ssem.at[q], self.rsem.at[q], core)

    def far_copy(self, e):
        return remote(self.away.at[e - 1], self.back.at[e - 1], self.ssem.at[e - 1],
                      self.rsem.at[e - 1], self.place.plane(e))

    def hop_copy(self, k, c, device):
        i = 4 + 2 * k + c
        return remote(
            cut_in(2, self.hop.at[k], c),
            cut_in(2, self.hop.at[k + 3], c),
            self.ssem.at[i],
            self.rsem.at[i],
            device,
        )

    def rows(self, c):
        n = self.hop.shape[1] // 2
        return slice(c * n, (c + 1) * n)

    def targets(self):
        pc = self.place
        core, xm, ym = pc.mates()
        c = pc.f % 2
        first = (c * xm[0] + (1 - c) * ym[0], pc.b, c * xm[2] + (1 - c) * ym[2])
        second = (c * ym[0] + (1 - c) * xm[0], pc.b, c * ym[2] + (1 - c) * xm[2])
        return (first, second)

    def early(self):
        pc = self.place
        if not pc.two_level:
            return
        c = pc.f % 2
        first, second = self.targets()
        self.core_copy(1).wait_recv()
        self.core_copy(2).wait_recv()
        q = c * 1 + (1 - c) * 2
        for k in range(2):
            r = self.rows(k)
            self.hop[0, r] = (self.mine(q, r) + self.back[q, r].astype(F32)).astype(BF)
            self.hop_copy(0, k, first).start()

    def diagonal(self):
        pc = self.place
        if not pc.two_level:
            return
        first, second = self.targets()
        self.core_copy(3).wait_recv()
        for k in range(2):
            r = self.rows(k)
            self.hop[1, r] = (self.mine(3, r) + self.back[3, r].astype(F32)).astype(BF)
            self.hop_copy(1, k, first).start()

    def mine(self, q, r=slice(None)):
        return self.near[q, r]

    def result(self, store):
        self.late()
        self.finish(store)

    def late(self):
        pc = self.place
        if not pc.two_level:
            return
        c = pc.f % 2
        first, second = self.targets()
        q = c * 2 + (1 - c) * 1
        for k in range(2):
            r = self.rows(k)
            self.hop_copy(1, k, first).wait_recv()
            self.hop[2, r] = (
                self.mine(q, r) + self.back[q, r].astype(F32) + self.hop[4, r].astype(F32)
            ).astype(BF)
            self.hop_copy(2, k, second).start()

    def finish(self, store):
        pc = self.place
        if not pc.two_level:
            total = self.mine(0)
            for e in range(1, pc.count):
                self.far_copy(e).wait()
                total = total + self.back[e - 1].astype(F32)
            store(total)
            return
        first, second = self.targets()
        self.core_copy(0).wait_recv()
        for k in range(2):
            self.hop_copy(0, k, first).wait_recv()
            self.hop_copy(2, k, second).wait_recv()
        store(
            self.mine(0)
            + self.back[0].astype(F32)
            + self.hop[3].astype(F32)
            + self.hop[5].astype(F32)
        )
        for q in range(4):
            self.core_copy(q).wait_send()
        for k in range(2):
            self.hop_copy(0, k, first).wait_send()
            self.hop_copy(1, k, first).wait_send()
            self.hop_copy(2, k, second).wait_send()


class ReadyScatter(PlaneScatter):
    def __init__(self, place, part, back, hop, ssem, rsem):
        super().__init__(place, None, None, back, hop, ssem, rsem)
        self.part = part
        if place.two_level:
            o = place.slots()
            self.here = (o[0], o[2], o[3], o[6])
            self.gone = (o[1], o[4], o[5], o[7])

    def mine(self, q, r=slice(None)):
        if not self.place.two_level:
            return self.part(self.place.me)[...].astype(F32)
        return self.part(pick(q, self.here))[r].astype(F32)

    def core_copy(self, q):
        core = self.place.mates()[0]
        v = self.part(self.gone[q])
        return remote(v, self.back.at[q], self.ssem.at[q], self.rsem.at[q], core)

    def far_copy(self, e):
        pc = self.place
        v = self.part((pc.me + e) % pc.count)
        return remote(v, self.back.at[e - 1], self.ssem.at[e - 1], self.rsem.at[e - 1],
                      pc.plane(e))

    def start(self):
        pc = self.place
        if pc.two_level:
            for q in (3, 2, 1, 0):
                self.core_copy(q).start()
        else:
            for e in range(1, pc.count):
                self.far_copy(e).start()


class RowSends:
    def __init__(self, place, layer, out, sems):
        self.place, self.layer, self.out = (place, layer, out)
        self.lsem, self.ss, self.sr = sems

    def copies(self, f, src):
        pc = self.place
        e = (self.layer * pc.nf + f - pc.me + pc.count) % pc.count
        own = self.out.at[pc.me]
        k = (e + pc.count - 1) % pc.count
        away = remote(src, own, self.ss.at[f], self.sr.at[k], (self.layer, pc.b, f))
        return (e, away, pltpu.make_async_copy(src, own, self.lsem))

    def start(self, f, src):
        e, away, local = self.copies(f, src)

        @pl.when(e != 0)
        def _():
            away.start()

        @pl.when(e == 0)
        def _():
            local.start()

    def finish(self, src):
        pc = self.place
        for f in range(pc.nf):
            e, away, local = self.copies(f, src)

            @pl.when(e != 0)
            def _():
                away.wait_send()

            @pl.when(e == 0)
            def _():
                local.wait()

        @pl.when(pc.s == self.layer)
        def _():
            for e in range(1, pc.count):
                q = pc.slot_from(e)
                remote(src, self.out.at[q], self.ss.at[0], self.sr.at[e - 1], pc.plane(e)).wait_recv()


def row_scratch(dims):
    dma = pltpu.SemaphoreType.DMA
    return [dma(()), dma((dims[2],)), dma((dims[0] * dims[2],))]


class LineGather:
    def __init__(self, place, piece, out, sems, part=None):
        self.place, self.piece = (place, piece)
        self.view = lambda t: out.at[t] if part is None else out.at[t, part]
        self.lsem, self.ss, self.sr = sems
        self.k = 0

    def local(self):
        return pltpu.make_async_copy(self.piece, self.view(self.place.b), self.lsem)

    def hop(self, way, k, came):
        pc = self.place
        t = pc.b - way * (k - (0 if came else 1))
        src = self.piece if k == 1 and not came else self.view(t)
        i = k - 1 + (0 if way == 1 else pc.nb - 1)
        return remote(
            src, self.view(t), self.ss.at[i], self.sr.at[i], (pc.s, pc.b + way, pc.f)
        )

    def sends(self, way, k):
        b, nb = (self.place.b, self.place.nb)
        return (b >= k - 1) & (b < nb - 1) if way == 1 else (b <= nb - k) & (b > 0)

    def comes(self, way, k):
        b, nb = (self.place.b, self.place.nb)
        return b >= k if way == 1 else b <= nb - 1 - k

    def arrived(self, k):
        for way in (1, -1):
            @pl.when(self.comes(way, k))
            def _():
                self.hop(way, k, True).wait_recv()

    def start(self):
        self.local().start()
        self.service()

    def service(self):
        if self.k == self.place.nb - 1:
            return
        self.k += 1
        if self.k > 1:
            self.arrived(self.k - 1)
        for way in (1, -1):
            @pl.when(self.sends(way, self.k))
            def _():
                self.hop(way, self.k, False).start()

    def finish(self):
        last = self.place.nb - 1
        while self.k < last:
            self.service()
        self.arrived(last)
        for k in range(1, last + 1):
            for way in (1, -1):
                @pl.when(self.sends(way, k))
                def _():
                    self.hop(way, k, False).wait_send()
        self.local().wait()


class LineReduce:
    def __init__(self, place, terms, store, sems, load=None):
        self.place, self.terms, self.store, self.load = (place, terms, store, load)
        self.out, self.came, self.ss, self.sr = sems
        self.k = 0

    def index(self, way, k):
        return k - 1 + (0 if way == 1 else self.place.nb - 1)

    def hop(self, way, k):
        pc = self.place
        i = self.index(way, k)
        return remote(
            self.out.at[i], self.came.at[i], self.ss.at[i], self.sr.at[i],
            (pc.s, pc.b + way, pc.f),
        )

    def rank(self, way):
        pc = self.place
        return pc.b if way == 1 else pc.nb - 1 - pc.b

    def sends(self, way, k):
        r = self.rank(way)
        return (r < k) & (r < self.place.nb - 1)

    def start(self):
        if self.load is not None:
            self.load.wait()
        self.service()

    def service(self):
        nb = self.place.nb
        if self.k == nb - 1:
            return
        self.k += 1
        k = self.k
        for way in (1, -1):
            r = self.rank(way)
            t = nb - k + r if way == 1 else k - 1 - r
            i = self.index(way, k)

            @pl.when(self.sends(way, k) & (r == 0))
            def _():
                self.out[i] = self.terms(t)

            if k > 1:
                @pl.when(self.sends(way, k) & (r > 0))
                def _():
                    self.hop(way, k - 1).wait_recv()
                    total = self.terms(t).astype(F32) + self.came[i - 1].astype(F32)
                    self.out[i] = total.astype(BF)

            @pl.when(self.sends(way, k))
            def _():
                self.hop(way, k).start()

    def finish(self):
        pc = self.place
        last = pc.nb - 1
        while self.k < last:
            self.service()
        right, left = (self.index(1, last), self.index(-1, last))

        @pl.when(pc.b == 0)
        def _():
            self.hop(-1, last).wait_recv()
            self.store(self.terms(pc.b).astype(F32) + self.came[left].astype(F32))

        @pl.when(pc.b == last)
        def _():
            self.hop(1, last).wait_recv()
            self.store(self.terms(pc.b).astype(F32) + self.came[right].astype(F32))

        @pl.when((pc.b > 0) & (pc.b < last))
        def _():
            self.hop(1, last).wait_recv()
            self.hop(-1, last).wait_recv()
            self.store(
                self.terms(pc.b).astype(F32)
                + self.came[right].astype(F32)
                + self.came[left].astype(F32)
            )

        for k in range(1, last + 1):
            for way in (1, -1):
                @pl.when(self.sends(way, k))
                def _():
                    self.hop(way, k).wait_send()


def gather_scratch(dims):
    dma = pltpu.SemaphoreType.DMA
    return [dma(()), dma((2 * (dims[1] - 1),)), dma((2 * (dims[1] - 1),))]


def reduce_scratch(dims, *block):
    dma = pltpu.SemaphoreType.DMA
    n = 2 * (dims[1] - 1)
    return [pltpu.VMEM((n,) + block, BF), pltpu.VMEM((n,) + block, BF), dma((n,)), dma((n,))]


class Riders:
    def __init__(self, dims, specs, arrays):
        self.dims, self.specs, self.arrays = (dims, specs, arrays)
        self.shapes = []
        self.places = [AN] * len(specs)
        self.outs = []
        self.scratch = []
        self.sizes = []
        for spec, a in zip(specs, arrays):
            if spec[0] == "gather":
                shape = (dims[1],) + a.shape[1:]
                scratch = gather_scratch(dims)
            else:
                lo, hi = spec[1]
                shape = (hi - lo,) + a.shape[2:]
                scratch = reduce_scratch(dims, *shape)
                scratch += [
                    pltpu.VMEM((dims[1],) + shape, BF), pltpu.SemaphoreType.DMA(())
                ]
            self.outs.append(AN if spec[0] == "gather" else VM)
            self.shapes.append(jax.ShapeDtypeStruct(shape, a.dtype))
            self.scratch += scratch
            self.sizes.append(len(scratch))
        self.count = len(specs)

    def board(self, place, ins, outs, scratch):
        out = []
        for spec, size, a, o in zip(self.specs, self.sizes, ins, outs):
            mine, scratch = (scratch[:size], scratch[size:])
            if spec[0] == "gather":
                out.append(LineGather(place, a.at[spec[1]], o, mine))
            else:
                lo, hi = spec[1]

                def store(value, o=o):
                    o[...] = value.astype(BF)

                terms, sem = mine[4:]
                load = pltpu.make_async_copy(a.at[:, lo:hi], terms, sem)
                load.start()
                out.append(
                    LineReduce(place, lambda t, r=terms: r[t], store, mine[:4], load)
                )
        return (out, scratch)


def each(riders, what):
    for r in riders:
        getattr(r, what)()


def scatter_scratch(dims, *block):
    count = dims[0] * dims[2]
    if dims[0] == 2 and dims[2] == 4:
        near, away, hops, sems = (4, 4, 6, 10)
    else:
        near, away, hops, sems = (1, count - 1, 1, count - 1)
    return [
        pltpu.VMEM((near,) + block, F32),
        pltpu.VMEM((away,) + block, BF),
        pltpu.VMEM((away,) + block, BF),
        pltpu.VMEM((hops,) + block, BF),
        pltpu.SemaphoreType.DMA((sems,)),
        pltpu.SemaphoreType.DMA((sems,)),
    ]


def call(kernel, name, cid, outs, out_specs, in_specs, scratch, args):
    params = pltpu.CompilerParams(
        collective_id=cid, has_side_effects=True, vmem_limit_bytes=VMEM_LIMIT
    )
    return pl.pallas_call(
        kernel,
        name=name,
        out_shape=outs,
        in_specs=in_specs,
        out_specs=out_specs,
        scratch_shapes=scratch,
        compiler_params=params,
    )(*args)


def column_start(dims, part, b, f, y, half):
    ns, nb, nf = dims
    return part * nb * nf * ns * half + ((b * nf + f) * ns + y) * half


def columns_of(ref, q, nf, wide):
    return ref.at[:, q % nf, :, pl.ds(pl.multiple_of((q // nf) * wide, wide), wide)]


def gather_weights_kernel(
    dims, w_ref, wq_ref, wo_ref, wd, small, gup, wdp, gu_first, qo_first, qz, small_all,
    pack, qcol, qh, lsem, ps, pr, ms, mr, qs, qr, *rest
):
    pc = Place(dims)
    ns, nb, nf = dims
    half = wd.shape[1]
    wide = qh.shape[2]
    greet(pc, "all", True)
    qkv = wq_ref.shape[2]
    full = jnp.concatenate([wq_ref[0], wo_ref[0]], axis=1)
    for y in range(ns):
        qcol[y] = full[:, y * wide : (y + 1) * wide]
    across = []
    for d in range(1, ns):
        y = (pc.s + d) % ns
        t = (y, pc.b, pc.f)
        i = 3 * (d - 1)
        across.append(remote(qcol.at[y], qh.at[pc.s], ms.at[i], mr.at[i], t))
        across.append(remote(wd.at[y], wdp.at[pc.s], ms.at[i + 1], mr.at[i + 1], t))
        across.append(remote(small, small_all.at[pc.s], ms.at[i + 2], mr.at[i + 2], t))
    for c in across:
        c.start()
    qh[pc.s] = qcol[pc.s]
    local = [
        pltpu.make_async_copy(wd.at[pc.s], wdp.at[pc.s], lsem.at[0]),
        pltpu.make_async_copy(small, small_all.at[pc.s], lsem.at[1]),
    ]
    for c in local:
        c.start()
    own = pltpu.make_async_copy(pack.at[pc.s, pc.f], gup.at[pc.s, pc.f], lsem.at[2])

    def piece(y, f):
        e = (y * nf + f - pc.me + pc.count) % pc.count
        k = (e + pc.count - 1) % pc.count
        return (
            e,
            remote(pack.at[y, f], gup.at[pc.s, pc.f], ps.at[k], pr.at[k], (y, pc.b, f)),
        )

    for f in range(nf):
        for y in range(ns):
            pieces = []
            for part in range(2):
                for b in range(nb):
                    c0 = column_start(dims, part, b, f, y, half)
                    pieces.append(w_ref[0, :, c0 : c0 + half])
            pack[y, f] = jnp.concatenate(pieces, axis=1)
            e, c = piece(y, f)

            @pl.when(e != 0)
            def _():
                c.start()

    own.start()
    for d in range(ns - 1):
        across[3 * d].wait()
    line_q = LineGather(pc, qh, qz, rest[0:3])
    lines = [
        LineGather(pc, gup.at[0, f], gu_first, rest[3 + 3 * f : 6 + 3 * f], f) for f in range(nf)
    ]
    line_q.start()

    def arrived(y, f):
        e, c = piece(y, f)
        k = (2 * pc.count - e - 1) % pc.count

        @pl.when(e != 0)
        def _():
            remote(pack.at[0, 0], gup.at[y, f], ps.at[k], pr.at[k], (y, pc.b, f)).wait_recv()

    own.wait()
    line_q.service()
    for f in range(nf):
        arrived(0, f)
        lines[f].start()
    line_q.service()
    for line in lines:
        line.service()
    line_q.finish()
    gather = PlaneGather(pc, lambda q: columns_of(qo_first, q, nf, wide), qs, qr)
    columns_of(qo_first, pc.me, nf, wide)[...] = qz[:, 0]
    gather.start()
    for step in range(1, min(6, pc.count)):
        gather.before(step)
    for line in lines:
        line.service()
    for step in range(min(6, pc.count), pc.count):
        gather.before(step)
    gather.finish()
    for y in range(1, ns):
        for f in range(nf):
            arrived(y, f)
    for y in range(ns):
        for f in range(nf):
            e, c = piece(y, f)

            @pl.when(e != 0)
            def _():
                c.wait_send()

    for c in local:
        c.wait()
    for i, c in enumerate(across):
        if i % 3:
            c.wait()
    for line in lines:
        line.finish()


def gather_weights(dims, w, wq, wo, wd, small):
    ns, nb, nf = dims
    count = ns * nf
    half, width = wd.shape[1:]
    dr = wq.shape[1]
    cols = wq.shape[2] + wo.shape[2]
    wide = cols // ns
    two_ff = 2 * nb * half
    sds = jax.ShapeDtypeStruct
    outs = (
        sds((ns, nf, dr, two_ff), BF),
        sds((ns, half, width), BF),
        sds((nb, nf, dr, two_ff), BF),
        sds((nb, nf, dr, cols), BF),
        sds((nb, ns, dr, wide), BF),
        sds((ns,) + small.shape, F32),
    )
    dma = pltpu.SemaphoreType.DMA
    return call(
        functools.partial(gather_weights_kernel, dims),
        "gather_weights",
        0,
        outs,
        [AN, AN, AN, VM, VM, AN],
        [VM, VM, VM, AN, AN],
        [
            pltpu.VMEM((ns, nf, dr, two_ff), BF),
            pltpu.VMEM((ns, dr, wide), BF),
            pltpu.VMEM((ns, dr, wide), BF),
            dma((4,)),
            dma((count,)),
            dma((count,)),
            dma((3 * (ns - 1),)),
            dma((3 * (ns - 1),)),
        ]
        + gather_sems(dims)
        + gather_scratch(dims) * (1 + nf),
        (w, wq, wo, wd, small),
    )


def rms(values):
    return lax.rsqrt(jnp.mean(values * values, axis=0, keepdims=True) + 1e-06)


def column(rows_t, first, count):
    return jnp.concatenate([rows_t[:, k : k + 1] for k in range(first, first + count)], axis=0)


def rows_of(values):
    v = folded(values)
    return jnp.concatenate(
        [v[k : k + 128].T.sum(axis=0, keepdims=True) for k in range(0, v.shape[0], 128)], axis=0
    )


def folded(v):
    out = v[:, :128]
    for k in range(1, v.shape[1] // 128):
        out = out + v[:, k * 128 : (k + 1) * 128]
    return out


def fill_masks(pc, mask, meta_t, query_docs):
    nk, rows = mask.shape[:2]
    key_i = lax.broadcasted_iota(jnp.int32, (rows, rows), 0)
    query_i = lax.broadcasted_iota(jnp.int32, (rows, rows), 1)
    per = rows // 128
    for j in range(nk):
        same = column(meta_t, j * per, per) == query_docs
        if j == 0:
            live = same & (key_i <= query_i)
        else:
            live = same & (key_i < (pc.b - j + 1) * rows)
        mask[j] = jnp.where(live, 0.0, NEG)


def load_qo(qo, w, wo, sems):
    cols = w.shape[1]
    c1 = pltpu.make_async_copy(qo.at[:, 0:cols], w, sems.at[0])
    c2 = pltpu.make_async_copy(qo.at[:, cols : cols + wo.shape[1]], wo, sems.at[1])
    c1.start()
    c2.start()
    return (c1, c2)


def gains_of(small_t, width, qkv):
    n = width // 128
    return (
        column(small_t, 0, n),
        column(small_t, n, n),
        column(small_t, 2 * n, qkv // 128),
    )


def padded_t(v):
    n = v.shape[0]
    return jnp.concatenate([v, jnp.zeros((128 - n, 128), v.dtype)], axis=0).T


def attention_forward_kernel(dims, *args):
    pc = Place(dims)
    riders, gather = attention_forward_part(pc, *args)
    last_blocks(pc, gather)
    gather.finish()
    each(riders, "finish")


def last_blocks(pc, gather):
    for step in range(min(6, pc.count), pc.count):
        gather.before(step)


def attention_forward_part(
    pc, nk, layer, plan, carry, h_ref, small_ref, meta_ref, docs_ref, cos_ref, sin_ref, qo_all,
    *refs
):
    n = plan.count
    block_ref, refs = (refs[0], refs[1:])
    ins, refs = (refs[:n], refs[n:])
    normed_ref, q_ref, kv_ref, lse_ref, mixed_ref, res_ref, n2_ref = refs[:7]
    outs, refs = (refs[7 : 7 + n], refs[7 + n :])
    block_all, refs = (refs[0], refs[1:])
    w, wo, mask, joined, top_own, sum_own, out_own, ssem, rsem, qsem = refs[:10]
    refs = refs[10:]
    width, rows = h_ref.shape
    loads = load_qo(qo_all, w, wo, qsem)
    greet(pc, "mates", True)
    riders, refs = plan.board(pc, ins, outs, refs)
    if carry == "lanes":
        own = block_ref
        slot = lambda q: block_all.at[:, lanes(q, rows)]
    else:
        own = block_ref.at[:, 1]
        slot = lambda q: columns_of(block_all, q, pc.nf, block_ref.shape[3])
    gather = PlaneGather(pc, slot, *refs)
    slot(pc.me)[...] = own[...]
    gather.start()
    each(riders, "start")
    g1, g2, bias = gains_of(padded_t(small_ref[layer]), width, w.shape[1])
    hidden = h_ref[...].astype(BF).astype(F32)
    normed = (hidden * rms(hidden) * g1).astype(BF)
    normed_ref[...] = normed
    fill_masks(pc, mask, padded_t(meta_ref[...]), docs_ref[...])
    loads[0].wait()
    joined[...] = tn(w[...], normed) + bias
    cos_part = cos_ref[...]
    sin_part = sin_ref[...]
    half = HD // 2

    def turned(row):
        u1 = joined[pl.ds(row, half), :]
        u2 = joined[pl.ds(row + half, half), :]
        return (u1 * cos_part - u2 * sin_part, u2 * cos_part + u1 * sin_part)

    for g in range(KVH):
        r1, r2 = turned((H + g) * HD)
        kv_ref[0, g, :half, :] = r1.astype(BF)
        kv_ref[0, g, half:, :] = r2.astype(BF)
        v0 = (H + KVH + g) * HD
        kv_ref[0, KVH + g] = joined[v0 : v0 + HD, :].astype(BF)
    sends = [
        remote(kv_ref.at[0], kv_ref.at[j], ssem.at[j - 1], rsem.at[j - 1], pc.along(j))
        for j in range(1, nk)
    ]
    for c in sends:
        c.start()
    scale = HD**-0.5
    for head in range(H):
        r1, r2 = turned(head * HD)
        q_ref[head, :half, :] = (r1 * scale).astype(BF)
        q_ref[head, half:, :] = (r2 * scale).astype(BF)
    for g in range(KVH):
        keys = kv_ref[0, g].T
        values = kv_ref[0, KVH + g]

        def own_keys(i, carried):
            head = g * GROUP + i
            x = nn(keys, q_ref[head]) + mask[0]
            top = x.max(axis=0, keepdims=True)
            e = jnp.exp(x - top)
            top_own[head] = top
            sum_own[head] = e.sum(axis=0, keepdims=True)
            out_own[head] = nn(values, e.astype(BF))
            return carried

        lax.fori_loop(0, GROUP, own_keys, 0, unroll=True)
    for c in sends:
        c.wait()
    each(riders, "service")
    for g in range(KVH):
        keys = [kv_ref[j, g].T for j in range(1, nk)]
        values = [kv_ref[j, KVH + g] for j in range(1, nk)]

        def one_head(i, carried):
            head = g * GROUP + i
            q = q_ref[head]
            s = [nn(keys[j], q) + mask[j + 1] for j in range(nk - 1)]
            first = top_own[head]
            top = first
            for x in s:
                top = jnp.maximum(top, x.max(axis=0, keepdims=True))
            e = [jnp.exp(x - top) for x in s]
            fade = jnp.exp(first - top)
            total = sum_own[head] * fade
            out = out_own[head] * fade
            for j in range(nk - 1):
                total = total + e[j].sum(axis=0, keepdims=True)
                out = out + nn(values[j], e[j].astype(BF))
            lse_ref[head] = top + jnp.log(total)
            mixed_ref[head] = (out / total).astype(BF)
            return carried

        lax.fori_loop(0, GROUP, one_head, 0, unroll=True)
        if g == 0:
            for step in range(1, min(6, pc.count)):
                gather.before(step)
        else:
            each(riders, "service")
    mixed = mixed_ref[...].reshape(H * HD, rows)
    loads[1].wait()
    residual = hidden + tn(wo[...], mixed)
    res_ref[...] = residual
    n2_ref[...] = (residual * rms(residual) * g2).astype(BF)
    return (riders, gather)


def attention_scratch(dims, nk, width, rows, qkv):
    dma = pltpu.SemaphoreType.DMA
    return [
        pltpu.VMEM((width, qkv), BF),
        pltpu.VMEM((width, width), BF),
        pltpu.VMEM((nk, rows, rows), F32),
        pltpu.VMEM((qkv, rows), F32),
        pltpu.VMEM((H, 1, rows), F32),
        pltpu.VMEM((H, 1, rows), F32),
        pltpu.VMEM((H, HD, rows), F32),
        dma((nk - 1,)),
        dma((nk - 1,)),
        dma((2,)),
    ]


def attention_forward(dims, nk, cid, layer, hidden, small, meta, docs, cos_part, sin_part, qo_all,
                      plan, carry, block):
    width, rows = hidden.shape
    ns, nb, nf = dims
    count = ns * nf
    qkv = qo_all.shape[1] - width
    sds = jax.ShapeDtypeStruct
    outs = [
        sds((width, rows), BF),
        sds((H, HD, rows), BF),
        sds((nk, 2 * KVH, HD, rows), BF),
        sds((H, 1, rows), F32),
        sds((H, HD, rows), BF),
        sds((width, rows), F32),
        sds((width, rows), BF),
    ] + plan.shapes
    if carry == "lanes":
        outs.append(sds((width, count * rows), BF))
    else:
        outs.append(sds((nb, nf, block.shape[2], ns * block.shape[3]), BF))
    out = call(
        functools.partial(attention_forward_kernel, dims, nk, layer, plan, carry),
        "attention_forward",
        cid,
        tuple(outs),
        [VM] * 7 + plan.outs + [VM],
        [VM] * 6 + [AN, VM] + plan.places,
        attention_scratch(dims, nk, width, rows, qkv)
        + plan.scratch
        + gather_sems(dims),
        (hidden, small, meta, docs, cos_part, sin_part, qo_all, block, *plan.arrays),
    )
    return (out[:7], out[7:])


def attention_backward_kernel(dims, *args):
    pc = Place(dims)
    riders = attention_backward_part(pc, lambda: None, None, *args)
    each(riders, "finish")


def attention_backward_part(
    pc, begun, cut_rows, nk, layer, plan, carry, g_ref, small_ref, meta_ref, docs_ref, cos_ref, sin_ref,
    h_ref, normed_ref, q_ref, kv_ref, lse_ref, mixed_ref, qo_all, *refs
):
    n = plan.count
    parts_ref, more_ref, refs = (refs[0], refs[1], refs[2:])
    ins, refs = (refs[:n], refs[n:])
    gh_ref, dqo_ref, dsmall_ref = refs[:3]
    outs, refs = (refs[3 : 3 + n], refs[3 + n :])
    out_ref, refs = (refs[0], refs[1:])
    if carry == "columns":
        rows_ref, refs = (refs[0], refs[1:])
    w, wo, mask, dmix, dkv, delta, dq_some, out_kv, in_kv, gj, ssem, rsem, qsem = refs[:13]
    refs = refs[13:]
    width, rows = h_ref.shape
    qkv = w.shape[1]
    loads = load_qo(qo_all, w, wo, qsem)
    riders, refs = plan.board(pc, ins, outs, refs)
    if carry == "columns":
        held, held_sem = refs[7:]
        coming = pltpu.make_async_copy(parts_ref, held, held_sem)
        coming.start()
    greet(pc, "all" if carry == "columns" else "mates", True)
    if carry == "columns":
        part = lambda q: columns_of(held, q, pc.nf, out_ref.shape[2])
        hand_out = RowSends(pc, 1, rows_ref, refs[4:7])
        coming.wait()
    else:
        part = lambda q: parts_ref.at[q]
    scatter = ReadyScatter(pc, part, *refs[:4])
    scatter.start()
    each(riders, "start")
    begun()

    def put(c0, c1, value):
        if cut_rows is None:
            dqo_ref[:, c0:c1] = value.astype(BF)
        else:
            for t in range(pc.nb):
                for f in range(pc.nf):
                    r = (t * pc.nf + f) * cut_rows
                    dqo_ref[t, f, :, c0:c1] = value[r : r + cut_rows].astype(BF)

    g1 = column(padded_t(small_ref[layer]), 0, width // 128)
    fill_masks(pc, mask, padded_t(meta_ref[...]), docs_ref[...])
    grl = g_ref[...].astype(BF)
    loads[1].wait()
    dmix[...] = nn(wo[...], grl).astype(BF).reshape(dmix.shape)
    put(qkv, qkv + width, nt(mixed_ref[...].reshape(H * HD, rows), grl))
    scatter.diagonal()
    scatter.early()
    if carry == "columns":
        for f in range(pc.nf):
            hand_out.start(f, more_ref.at[f])
    cos_part = cos_ref[...]
    sin_part = sin_ref[...]
    half = HD // 2
    scale = HD**-0.5
    dkv[...] = jnp.zeros_like(dkv)

    def unturned(d1, d2):
        return (d1 * cos_part + d2 * sin_part, d2 * cos_part - d1 * sin_part)

    def of_block(j, g, head, keys, keys_t, values):
        q = q_ref[head]
        do = dmix[head]
        p = jnp.exp(nn(keys, q) + mask[j] - lse_ref[head])
        ds = (p * (nn(values, do) - delta[head])).astype(BF)
        dkv[j, g] += nt(q, ds)
        dkv[j, KVH + g] += nt(do, p.astype(BF))
        return nn(keys_t, ds)

    for g in range(KVH):
        keys_t = [kv_ref[j, g] for j in range(1, nk)]
        keys = [k.T for k in keys_t]
        values = [kv_ref[j, KVH + g].T for j in range(1, nk)]

        def earlier(i, carried):
            head = g * GROUP + i
            delta[head] = (dmix[head].astype(F32) * mixed_ref[head].astype(F32)).sum(
                axis=0, keepdims=True
            )
            dq = of_block(1, g, head, keys[0], keys_t[0], values[0])
            for j in range(2, nk):
                dq = dq + of_block(j, g, head, keys[j - 1], keys_t[j - 1], values[j - 1])
            dq_some[head] = dq
            return carried

        lax.fori_loop(0, GROUP, earlier, 0, unroll=True)
        if g == 0:
            scatter.late()
        if g == 1 or carry == "sum":
            each(riders, "service")
    for j in range(1, nk):
        out_kv[j - 1] = dkv[j].astype(BF)
    sends = [
        remote(out_kv.at[j - 1], in_kv.at[j - 1], ssem.at[j - 1], rsem.at[j - 1],
               pc.along(pc.nb - j))
        for j in range(1, nk)
    ]
    for c in sends:
        c.start()
    for g in range(KVH):
        keys_t = kv_ref[0, g]
        keys = keys_t.T
        values = kv_ref[0, KVH + g].T

        def own_keys(i, carried):
            head = g * GROUP + i
            dq = (dq_some[head] + of_block(0, g, head, keys, keys_t, values)) * scale
            r1, r2 = unturned(dq[:half], dq[half:])
            gj[pl.ds(pl.multiple_of(head * HD, HD), half), :] = r1.astype(BF)
            gj[pl.ds(pl.multiple_of(head * HD + half, half), half), :] = r2.astype(BF)
            return carried

        lax.fori_loop(0, GROUP, own_keys, 0, unroll=True)
    for c in sends:
        c.wait()
    if cut_rows is None:
        each(riders, "service")
    own = dkv[0]
    for j in range(1, nk):
        own = own + in_kv[j - 1].astype(F32)
    for g in range(KVH):
        r1, r2 = unturned(own[g, :half], own[g, half:])
        k0 = (H + g) * HD
        gj[k0 : k0 + half, :] = r1.astype(BF)
        gj[k0 + half : k0 + HD, :] = r2.astype(BF)
        v0 = (H + KVH + g) * HD
        gj[v0 : v0 + HD, :] = own[KVH + g].astype(BF)
    gjv = gj[...]
    n1 = width // 128
    dsmall_ref[n1 : n1 + qkv // 128, :] = rows_of(gjv.astype(F32))
    loads[0].wait()
    put(0, qkv, nt(normed_ref[...], gjv))
    gn = nn(w[...], gjv)
    hidden = h_ref[...].astype(BF).astype(F32)
    scale_one = rms(hidden)
    unit = hidden * scale_one
    dsmall_ref[:n1, :] = rows_of(gn * unit)
    u = gn * g1
    gh_ref[...] = g_ref[...] + scale_one * (u - unit * jnp.mean(u * unit, axis=0, keepdims=True))

    def store(total):
        if carry == "columns":
            out_ref[...] = total.astype(BF)
        else:
            out_ref[...] = more_ref[...] + total

    if cut_rows is not None:
        each(riders, "service")
    scatter.finish(store)
    if carry == "columns":
        hand_out.finish(more_ref.at[0])
    return riders


def backward_scratch(nk, width, rows, qkv):
    dma = pltpu.SemaphoreType.DMA
    block = (2 * KVH, HD, rows)
    return [
        pltpu.VMEM((width, qkv), BF),
        pltpu.VMEM((width, width), BF),
        pltpu.VMEM((nk, rows, rows), F32),
        pltpu.VMEM((H, HD, rows), BF),
        pltpu.VMEM((nk,) + block, F32),
        pltpu.VMEM((H, 1, rows), F32),
        pltpu.VMEM((H, HD, rows), F32),
        pltpu.VMEM((nk - 1,) + block, BF),
        pltpu.VMEM((nk - 1,) + block, BF),
        pltpu.VMEM((qkv, rows), BF),
        dma((nk - 1,)),
        dma((nk - 1,)),
        dma((2,)),
    ]


def attention_backward(dims, nk, cid, layer, g, small, meta, docs, cos_part, sin_part, hidden,
                       normed, q, kv, lse, mixed, qo_all, plan, carry, late):
    width, rows = hidden.shape
    qkv = qo_all.shape[1] - width
    sds = jax.ShapeDtypeStruct
    outs = [
        sds((width, rows), F32),
        sds((width, qkv + width), BF),
        sds(((width + qkv) // 128, 128), F32),
    ] + plan.shapes
    dma = pltpu.SemaphoreType.DMA
    if carry == "columns":
        summed = (dims[1], late[0].shape[2], late[0].shape[3] // dims[0])
        outs += [sds(summed, BF), sds((dims[0] * dims[2],) + late[1].shape[1:], BF)]
        places = [VM, AN]
    else:
        summed = (width, rows)
        outs.append(sds(summed, F32))
        places = [VM]
    out = call(
        functools.partial(attention_backward_kernel, dims, nk, layer, plan, carry),
        "attention_backward",
        cid,
        tuple(outs),
        [VM] * 3 + plan.outs + places,
        [VM] * 12 + [AN] + [AN if carry == "columns" else VM, VM] + plan.places,
        backward_scratch(nk, width, rows, qkv)
        + plan.scratch
        + scatter_scratch(dims, *summed)[2:]
        + (
            row_scratch(dims) + [pltpu.VMEM(late[0].shape, BF), dma(())]
            if carry == "columns"
            else []
        ),
        (g, small, meta, docs, cos_part, sin_part, hidden, normed, q, kv, lse, mixed, qo_all,
         *late, *plan.arrays),
    )
    return (out[:3], out[3:])


def sequence_of(pc):
    if pc.two_level:
        return ((0, 1, 2, 3, 6, 7, 4, 5), 5, 7)
    return (tuple(range(pc.count)), pc.count - 1, pc.count - 1)


def lanes(slot, rows):
    return pl.ds(pl.multiple_of(slot * rows, rows), rows)


def transpose_into(dst, src):
    cols = src.shape[1]
    for c0 in range(0, cols, 128):
        c1 = min(c0 + 128, cols)
        dst[c0:c1, :] = src[:, c0:c1].T


def feed_forward_kernel(dims, *args):
    pc = Place(dims)
    feed_forward_part(pc, lambda: greet(pc, "mates", True), lambda: None, *args)


def feed_forward_part(pc, enter, ready, plan, x_ref, res_ref, wgu_ref, wd_ref, *refs):
    n = plan.count
    ins, refs = (refs[:n], refs[n:])
    out_ref, x_out, gu_out = refs[:3]
    outs, refs = (refs[3 : 3 + n], refs[3 + n :])
    x_all, gu_all, lsem, wgu_t, wd_t, gu, inner, near, away, back, hop, ss, sr, gs, gr = refs[:15]
    width, rows = x_ref.shape
    ff = wd_ref.shape[0]
    riders, _ = plan.board(pc, ins, outs, refs[15:])
    enter()
    gather = PlaneGather(pc, lambda q: x_all.at[:, lanes(q, rows)], gs, gr)
    scatter = PlaneScatter(pc, near, away, back, hop, ss, sr)
    x_all[:, lanes(pc.me, rows)] = x_ref[...]
    gather.start()
    ready()
    each(riders, "start")
    transpose_into(wgu_t, wgu_ref)
    transpose_into(wd_t, wd_ref)
    sequence, diagonal_at, early_at = sequence_of(pc)
    chunk = 32 if ff % 32 == 0 else 16

    def step_body(turn, carry):
        step = pick(turn, sequence)

        for k in range(pc.count):
            @pl.when(step == k)
            def _():
                gather.before(k)

        slot = pick(step, gather.order)
        sl = lanes(slot, rows)
        gu[...] = nn(wgu_t[...], x_all[:, sl])

        def act(i, c):
            r = pl.multiple_of(i * chunk, chunk)
            gate = gu[pl.ds(r, chunk), :]
            up = gu[pl.ds(ff + r, chunk), :]
            gu_all[pl.ds(r, chunk), sl] = gate.astype(BF)
            gu_all[pl.ds(ff + r, chunk), sl] = up.astype(BF)
            inner[pl.ds(r, chunk), :] = (gate * jax.nn.sigmoid(gate) * up).astype(BF)
            return c

        lax.fori_loop(0, ff // chunk, act, 0, unroll=True)
        scatter.put(step, nn(wd_t[...], inner[...]))

        @pl.when(turn == 3)
        def _():
            each(riders, "service")

        @pl.when(turn == diagonal_at)
        def _():
            scatter.diagonal()

        @pl.when(turn == early_at)
        def _():
            scatter.early()

        return carry

    lax.fori_loop(0, pc.count, step_body, 0)
    leaving = [
        pltpu.make_async_copy(gu_all, gu_out, lsem.at[0]),
        pltpu.make_async_copy(x_all, x_out, lsem.at[1]),
    ]
    each(leaving, "start")
    each(riders, "service")

    def store(total):
        out_ref[...] = res_ref[...] + total

    scatter.result(store)
    gather.finish()
    each(leaving, "wait")
    each(riders, "finish")


def feed_forward(dims, cid, x, residual, wgu, wd, plan):
    width, rows = x.shape
    count = dims[0] * dims[2]
    two_ff, ff = (wgu.shape[1], wd.shape[0])
    sds = jax.ShapeDtypeStruct
    dma = pltpu.SemaphoreType.DMA
    out = call(
        functools.partial(feed_forward_kernel, dims, plan),
        "feed_forward",
        cid,
        (
            sds((width, rows), F32),
            sds((width, count * rows), BF),
            sds((two_ff, count * rows), BF),
            *plan.shapes,
        ),
        [VM, AN, AN] + plan.outs,
        [VM] * 4 + plan.places,
        [
            pltpu.VMEM((width, count * rows), BF),
            pltpu.VMEM((two_ff, count * rows), BF),
            dma((2,)),
            pltpu.VMEM((two_ff, width), BF),
            pltpu.VMEM((width, ff), BF),
            pltpu.VMEM((two_ff, rows), F32),
            pltpu.VMEM((ff, rows), BF),
        ]
        + scatter_scratch(dims, width, rows)
        + gather_sems(dims)
        + plan.scratch,
        (x, residual, wgu, wd, *plan.arrays),
    )
    return (out[:3], out[3:])


def feed_backward_kernel(
    dims, layer, plan, g_ref, res_ref, x_in, gu_in, wgu_ref, wd_ref, small_ref, *refs
):
    n = plan.count
    ins, refs = (refs[:n], refs[n:])
    gr_ref, dwgu_ref, dwd_ref, dsmall_ref = refs[:4]
    outs, refs = (refs[4 : 4 + n], refs[4 + n :])
    x_all, gu_all, lsem, g_all, inner, ggu, gi, near, away, back, hop, ss, sr, gs, gr = refs[:15]
    coming = [
        pltpu.make_async_copy(gu_in, gu_all, lsem.at[0]),
        pltpu.make_async_copy(x_in, x_all, lsem.at[1]),
    ]
    each(coming, "start")
    pc = Place(dims)
    width, rows = g_ref.shape
    ff = wd_ref.shape[0]
    riders, _ = plan.board(pc, ins, outs, refs[15:])
    greet(pc, "mates", n > 0)
    gather = PlaneGather(pc, lambda q: g_all.at[:, lanes(q, rows)], gs, gr)
    scatter = PlaneScatter(pc, near, away, back, hop, ss, sr)
    g_all[:, lanes(pc.me, rows)] = g_ref[...].astype(BF)
    gather.start()
    each(riders, "start")
    coming[0].wait()
    sequence, diagonal_at, early_at = sequence_of(pc)
    chunk = 32 if ff % 32 == 0 else 16

    def step_body(turn, carry):
        step = pick(turn, sequence)

        for k in range(pc.count):
            @pl.when(step == k)
            def _():
                gather.before(k)

        slot = pick(step, gather.order)
        sl = lanes(slot, rows)
        gi[...] = nn(wd_ref[...], g_all[:, sl])

        def act(i, c):
            r = pl.multiple_of(i * chunk, chunk)
            gate = gu_all[pl.ds(r, chunk), sl].astype(F32)
            up = gu_all[pl.ds(ff + r, chunk), sl].astype(F32)
            grad = gi[pl.ds(r, chunk), :]
            sig = jax.nn.sigmoid(gate)
            silu = gate * sig
            inner[pl.ds(r, chunk), sl] = (silu * up).astype(BF)
            ggu[pl.ds(r, chunk), sl] = (grad * up * sig * (1.0 + gate * (1.0 - sig))).astype(BF)
            ggu[pl.ds(ff + r, chunk), sl] = (grad * silu).astype(BF)
            return c

        lax.fori_loop(0, ff // chunk, act, 0, unroll=True)
        scatter.put(step, nn(wgu_ref[...], ggu[:, sl]))

        @pl.when(turn == 3)
        def _():
            each(riders, "service")

        @pl.when(turn == diagonal_at)
        def _():
            scatter.diagonal()

        @pl.when(turn == early_at)
        def _():
            scatter.early()

        return carry

    lax.fori_loop(0, pc.count, step_body, 0)
    each(riders, "service")
    dwd_ref[...] = nt(inner[...], g_all[...]).astype(BF)
    scatter.late()
    coming[1].wait()
    part = width // 2
    for r in range(2):
        dwgu_ref[r * part : (r + 1) * part, :] = nt(
            x_all[r * part : (r + 1) * part, :], ggu[...]
        ).astype(BF)

    def store(total):
        residual = res_ref[...]
        scale_two = rms(residual)
        unit = residual * scale_two
        n1 = width // 128
        dsmall_ref[...] = rows_of(total * unit)
        u = total * column(padded_t(small_ref[layer]), n1, n1)
        gr_ref[...] = g_ref[...].astype(BF).astype(F32) + scale_two * (
            u - unit * jnp.mean(u * unit, axis=0, keepdims=True)
        )

    scatter.finish(store)
    gather.finish()
    each(riders, "finish")


def feed_backward(dims, cid, layer, g, residual, x_all, gu_all, wgu, wd, small, plan):
    width, rows = g.shape
    count = dims[0] * dims[2]
    two_ff, ff = (wgu.shape[1], wd.shape[0])
    sds = jax.ShapeDtypeStruct
    dma = pltpu.SemaphoreType.DMA
    out = call(
        functools.partial(feed_backward_kernel, dims, layer, plan),
        "feed_backward",
        cid,
        (
            sds((width, rows), F32),
            sds(wgu.shape, BF),
            sds(wd.shape, BF),
            sds((width // 128, 128), F32),
            *plan.shapes,
        ),
        [VM] * 4 + plan.outs,
        [VM, VM, AN, AN, VM, VM, VM] + plan.places,
        [
            pltpu.VMEM((width, count * rows), BF),
            pltpu.VMEM((two_ff, count * rows), BF),
            dma((2,)),
            pltpu.VMEM((width, count * rows), BF),
            pltpu.VMEM((ff, count * rows), BF),
            pltpu.VMEM((two_ff, count * rows), BF),
            pltpu.VMEM((ff, rows), F32),
        ]
        + scatter_scratch(dims, width, rows)
        + gather_sems(dims)
        + plan.scratch,
        (g, residual, x_all, gu_all, wgu, wd, small, *plan.arrays),
    )
    return (out[:4], out[4:])


def feed_both_kernel(dims, *args):
    pc = Place(dims)
    feed_both_part(pc, lambda: greet(pc, "mates", False), lambda: None, *args)


def feed_both_part(
    pc, enter, ready, layer, x_ref, res_ref, g_ref, g_all, wgu_ref, wd_ref, small_ref,
    gr_ref, dwgu_ref, dwd_ref, dsmall_ref, parts_ref,
    x_all, inner, ggu, wgu_t, wd_t, gu, gi, near, away, back, hop, ss, sr, gs, gr,
):
    width, rows = g_ref.shape
    ff = wd_ref.shape[0]
    enter()
    gather = PlaneGather(pc, lambda q: x_all.at[:, lanes(q, rows)], gs, gr)
    scatter = PlaneScatter(pc, near, away, back, hop, ss, sr)
    x_all[:, lanes(pc.me, rows)] = x_ref[...]
    gather.start()
    ready()
    transpose_into(wgu_t, wgu_ref)
    transpose_into(wd_t, wd_ref)
    sequence, diagonal_at, early_at = sequence_of(pc)
    chunk = 32 if ff % 32 == 0 else 16

    def step_body(turn, carry):
        step = pick(turn, sequence)

        for k in range(pc.count):
            @pl.when(step == k)
            def _():
                gather.before(k)

        slot = pick(step, gather.order)
        sl = lanes(slot, rows)
        gu[...] = nn(wgu_t[...], x_all[:, sl])
        gi[...] = nn(wd_ref[...], g_all[:, sl])

        def act(i, c):
            r = pl.multiple_of(i * chunk, chunk)
            gate = gu[pl.ds(r, chunk), :]
            up = gu[pl.ds(ff + r, chunk), :]
            grad = gi[pl.ds(r, chunk), :]
            sig = jax.nn.sigmoid(gate)
            silu = gate * sig
            inner[pl.ds(r, chunk), sl] = (silu * up).astype(BF)
            ggu[pl.ds(r, chunk), sl] = (grad * up * sig * (1.0 + gate * (1.0 - sig))).astype(BF)
            ggu[pl.ds(ff + r, chunk), sl] = (grad * silu).astype(BF)
            return c

        lax.fori_loop(0, ff // chunk, act, 0, unroll=True)
        scatter.put(step, nn(wgu_ref[...], ggu[:, sl]))

        @pl.when(turn == diagonal_at)
        def _():
            scatter.diagonal()

        @pl.when(turn == early_at)
        def _():
            scatter.early()

        parts_ref[slot] = nn(wd_t[...], inner[:, sl]).astype(BF)
        return carry

    lax.fori_loop(0, pc.count, step_body, 0)
    dwd_ref[...] = nt(inner[...], g_all[...]).astype(BF)
    scatter.late()
    part = width // 2
    for r in range(2):
        dwgu_ref[r * part : (r + 1) * part, :] = nt(
            x_all[r * part : (r + 1) * part, :], ggu[...]
        ).astype(BF)

    def store(total):
        residual = res_ref[...]
        scale_two = rms(residual)
        unit = residual * scale_two
        n1 = width // 128
        dsmall_ref[...] = rows_of(total * unit)
        u = total * column(padded_t(small_ref[layer]), n1, n1)
        gr_ref[...] = g_ref[...].astype(BF).astype(F32) + scale_two * (
            u - unit * jnp.mean(u * unit, axis=0, keepdims=True)
        )

    scatter.finish(store)
    gather.finish()


def feed_both(dims, cid, layer, x, residual, g, g_all, wgu, wd, small):
    width, rows = g.shape
    count = dims[0] * dims[2]
    two_ff, ff = (wgu.shape[1], wd.shape[0])
    sds = jax.ShapeDtypeStruct
    dma = pltpu.SemaphoreType.DMA
    return call(
        functools.partial(feed_both_kernel, dims, layer),
        "feed_both",
        cid,
        (
            sds((width, rows), F32),
            sds(wgu.shape, BF),
            sds(wd.shape, BF),
            sds((width // 128, 128), F32),
            sds((count, width, rows), BF),
        ),
        [VM] * 5,
        [VM] * 7,
        [
            pltpu.VMEM((width, count * rows), BF),
            pltpu.VMEM((ff, count * rows), BF),
            pltpu.VMEM((two_ff, count * rows), BF),
            pltpu.VMEM((two_ff, width), BF),
            pltpu.VMEM((width, ff), BF),
            pltpu.VMEM((two_ff, rows), F32),
            pltpu.VMEM((ff, rows), F32),
        ]
        + scatter_scratch(dims, width, rows)
        + gather_sems(dims),
        (x, residual, g, g_all, wgu, wd, small),
    )


def wait_for_weights(pc, riders, gather, wd_all, pieces, wd, sem, others):
    last_blocks(pc, gather)
    each(riders, "finish")
    load = pltpu.make_async_copy(wd_all, pieces, sem)
    load.start()
    each(others, "wait")
    load.wait()
    half = pieces.shape[1]
    for t in range(pc.nb):
        wd[t * half : (t + 1) * half, :] = pieces[t]
    gather.finish()


def lower_kernel(dims, nk, plan_a, plan_f, *refs):
    pc = Place(dims)
    a_in, wgu_in, refs = (refs[:9], refs[9], refs[10:])
    f_in, refs = (refs[: plan_f.count], refs[plan_f.count :])
    a_out, wd_all, qo_next, refs = (refs[:6], refs[6], refs[7], refs[8:])
    f_out, refs = (refs[: 3 + plan_f.count], refs[3 + plan_f.count :])
    n2, wgu, pieces, wd, wsem, dsem, refs = (*refs[:6], refs[6:])
    a_scratch, f_scratch = (refs[: 10 + len(plan_a.scratch) + 2], refs[10 + len(plan_a.scratch) + 2 :])
    load = pltpu.make_async_copy(wgu_in, wgu, wsem)
    load.start()
    riders, gather = attention_forward_part(
        pc, nk, 0, plan_a, "columns", *a_in, *a_out, n2, wd_all, qo_next, *a_scratch
    )
    feed_forward_part(
        pc,
        lambda: None,
        lambda: wait_for_weights(pc, riders, gather, wd_all, pieces, wd, dsem, [load]),
        plan_f, n2, a_out[5], wgu, wd, *f_in, *f_out, *f_scratch,
    )


def lower_layer(dims, nk, cid, hidden, small, meta, docs, cos_part, sin_part, qo, plan_a, block,
                wgu, plan_f):
    ns, nb, nf = dims
    width, rows = hidden.shape
    count = ns * nf
    qkv = qo.shape[1] - width
    two_ff = wgu.shape[1]
    ff = two_ff // 2
    sds = jax.ShapeDtypeStruct
    dma = pltpu.SemaphoreType.DMA
    outs = [
        sds((width, rows), BF),
        sds((H, HD, rows), BF),
        sds((nk, 2 * KVH, HD, rows), BF),
        sds((H, 1, rows), F32),
        sds((H, HD, rows), BF),
        sds((width, rows), F32),
        *plan_a.shapes,
        sds((nb, nf, block.shape[2], ns * block.shape[3]), BF),
        sds((width, rows), F32),
        sds((width, count * rows), BF),
        sds((two_ff, count * rows), BF),
        *plan_f.shapes,
    ]
    out = call(
        functools.partial(lower_kernel, dims, nk, plan_a, plan_f),
        "lower_layer",
        cid,
        tuple(outs),
        [VM] * 6 + plan_a.outs + [VM] + [VM, AN, AN] + plan_f.outs,
        [VM] * 6 + [AN, VM] + plan_a.places + [AN] + plan_f.places,
        [
            pltpu.VMEM((width, rows), BF),
            pltpu.VMEM(wgu.shape, BF),
            pltpu.VMEM((nb, ff // nb, width), BF),
            pltpu.VMEM((ff, width), BF),
            dma(()),
            dma(()),
        ]
        + attention_scratch(dims, nk, width, rows, qkv)
        + plan_a.scratch
        + gather_sems(dims)
        + [
            pltpu.VMEM((width, count * rows), BF),
            pltpu.VMEM((two_ff, count * rows), BF),
            dma((2,)),
            pltpu.VMEM((two_ff, width), BF),
            pltpu.VMEM((width, ff), BF),
            pltpu.VMEM((two_ff, rows), F32),
            pltpu.VMEM((ff, rows), BF),
        ]
        + scatter_scratch(dims, width, rows)
        + gather_sems(dims)
        + plan_f.scratch,
        (hidden, small, meta, docs, cos_part, sin_part, qo, block, *plan_a.arrays, wgu,
         *plan_f.arrays),
    )
    return (out[:6], out[6], out[7], out[8:11], out[11:])


def upper_kernel(dims, nk, plan, *refs):
    pc = Place(dims)
    a_in, g_ref, wgu_in, refs = (refs[:9], refs[9], refs[10], refs[11:])
    a_out, wd_all, f_out, refs = (refs[:6], refs[6], refs[7:12], refs[12:])
    n2, g_all, wgu, pieces, wd, wsem, dsem, refs = (*refs[:7], refs[7:])
    a_scratch, f_scratch = (refs[: 10 + len(plan.scratch) + 2], refs[10 + len(plan.scratch) + 2 :])
    load = pltpu.make_async_copy(wgu_in, wgu, wsem)
    load.start()
    riders, gather = attention_forward_part(
        pc, nk, 1, plan, "lanes", *a_in, *a_out, n2, wd_all, g_all, *a_scratch
    )
    feed_both_part(
        pc,
        lambda: None,
        lambda: wait_for_weights(pc, riders, gather, wd_all, pieces, wd, dsem, [load]),
        1, n2, a_out[5], g_ref, g_all, wgu, wd, a_in[1], *f_out, *f_scratch,
    )


def upper_layer(dims, nk, cid, hidden, small, meta, docs, cos_part, sin_part, qo, plan, block, g,
                wgu):
    ns, nb, nf = dims
    width, rows = hidden.shape
    count = ns * nf
    qkv = qo.shape[1] - width
    two_ff = wgu.shape[1]
    ff = two_ff // 2
    sds = jax.ShapeDtypeStruct
    dma = pltpu.SemaphoreType.DMA
    outs = [
        sds((width, rows), BF),
        sds((H, HD, rows), BF),
        sds((nk, 2 * KVH, HD, rows), BF),
        sds((H, 1, rows), F32),
        sds((H, HD, rows), BF),
        sds((width, rows), F32),
        *plan.shapes,
        sds((width, rows), F32),
        sds(wgu.shape, BF),
        sds((ff, width), BF),
        sds((width // 128, 128), F32),
        sds((count, width, rows), BF),
    ]
    out = call(
        functools.partial(upper_kernel, dims, nk, plan),
        "upper_layer",
        cid,
        tuple(outs),
        [VM] * 6 + plan.outs + [VM] * 5,
        [VM] * 6 + [AN, VM] + plan.places + [VM, AN],
        [
            pltpu.VMEM((width, rows), BF),
            pltpu.VMEM((width, count * rows), BF),
            pltpu.VMEM(wgu.shape, BF),
            pltpu.VMEM((nb, ff // nb, width), BF),
            pltpu.VMEM((ff, width), BF),
            dma(()),
            dma(()),
        ]
        + attention_scratch(dims, nk, width, rows, qkv)
        + plan.scratch
        + gather_sems(dims)
        + [
            pltpu.VMEM((width, count * rows), BF),
            pltpu.VMEM((ff, count * rows), BF),
            pltpu.VMEM((two_ff, count * rows), BF),
            pltpu.VMEM((two_ff, width), BF),
            pltpu.VMEM((width, ff), BF),
            pltpu.VMEM((two_ff, rows), F32),
            pltpu.VMEM((ff, rows), F32),
        ]
        + scatter_scratch(dims, width, rows)
        + gather_sems(dims),
        (hidden, small, meta, docs, cos_part, sin_part, qo, block, *plan.arrays, g, wgu),
    )
    return (out[:6], out[7:])


def reduce_kernel(
    dims, qo, terms, sa0, sa1, sb0, sb1, wd1, gu0a, gu0, wd0,
    qo_out, small_out, gu_got, wd_got,
    held, rest_gu, gsum, wsum, small, sm_in, sm_mid, sm_line, z_out, mine, give,
    lsem, ws, wr, ls, lr, zs, zr, *rest
):
    pc = Place(dims)
    ns, nb, nf = dims
    coming = pltpu.make_async_copy(qo, held, lsem.at[1])
    coming.start()
    cut = gu0a.shape[0]
    coming_gu = pltpu.make_async_copy(gu0.at[:, cut:nf], rest_gu, lsem.at[2])
    coming_gu.start()
    n1 = sb0.shape[0]
    per = small.shape[0] // ns
    nr = sa0.shape[0] + n1
    small[...] = jnp.zeros_like(small)
    for l, (a, g) in enumerate(((sa0, sb0), (sa1, sb1))):
        small[l * per : l * per + n1] = a[0:n1]
        small[l * per + n1 : l * per + 2 * n1] = g[...]
        small[l * per + 2 * n1 : l * per + nr] = a[n1 : a.shape[0]]
    greet(pc, "all", True)

    def keep(value):
        wsum[...] = value.astype(BF)

    def keep_of(l):
        def store(value):
            mine[l] = value

        return store

    line = LineReduce(pc, lambda t: wd0[t], keep, rest[0:4])
    ends = [
        LineReduce(pc, lambda t: z_out[t], keep_of(0), rest[4:8]),
        LineReduce(pc, lambda t: terms[t], keep_of(1), rest[8:12]),
    ]
    def keep_gu(value):
        gsum[...] = value.astype(BF)

    line_gu = LineReduce(pc, lambda t: rest_gu[t], keep_gu, rest[19:23])
    ends[1].start()
    coming_gu.wait()
    line_gu.start()
    line.start()
    scatter = ReadyScatter(
        pc, lambda q: columns_of(held, q, nf, z_out.shape[2]), *rest[15:19]
    )
    coming.wait()
    scatter.start()
    smalls = [
        remote(small, sm_in.at[e - 1], ls.at[e - 1], lr.at[e - 1], pc.plane(e))
        for e in range(1, pc.count)
    ]
    for c in smalls:
        c.start()
    scatter.diagonal()
    scatter.early()
    hand_out = RowSends(pc, 0, gu_got, rest[12:15])
    for f in range(cut):
        hand_out.start(f, gu0a.at[f])

    def split(l, ref):
        @pl.when(pc.s == l)
        def _():
            pltpu.make_async_copy(ref, wd_got.at[l], lsem.at[0]).start()

        @pl.when(pc.s != l)
        def _():
            remote(ref, wd_got.at[pc.s], ws.at[0], wr.at[0], (l, pc.b, pc.f)).start()

    split(1, wd1)
    ends[1].service()
    line_gu.service()
    line.service()
    scatter.late()
    ends[1].service()
    total = small[...]
    for e, c in enumerate(smalls):
        c.wait()
        total = total + sm_in[e]
    sm_mid[...] = total
    lines = [
        remote(sm_mid, sm_line.at[d - 1], zs.at[d - 1], zr.at[d - 1], pc.along(d))
        for d in range(1, nb)
    ]
    for c in lines:
        c.start()
    line_gu.service()
    line.service()

    def store(value):
        z_out[...] = value.astype(BF)

    scatter.finish(store)
    ends[0].start()
    ends[1].finish()
    line_gu.finish()
    for f in range(cut, nf):
        hand_out.start(f, gsum.at[f - cut])
    ends[0].service()
    line.finish()
    split(0, wsum)
    ends[0].finish()
    mate = (ns - 1 - pc.s, pc.b, pc.f)
    swap = remote(give.at[0], give.at[1], ws.at[1], wr.at[1], mate)
    give[0] = mine[ns - 1 - pc.s].astype(BF)
    swap.start()
    qo_out[pc.s] = mine[pc.s]
    total = sm_mid[...]
    for d, c in enumerate(lines):
        c.wait()
        total = total + sm_line[d]
    small_out[...] = total
    hand_out.finish(gu0a.at[0])
    pltpu.make_async_copy(wsum, wd_got.at[pc.s], lsem.at[0]).wait()
    remote(wsum, wd_got.at[pc.s], ws.at[0], wr.at[0], mate).wait()
    swap.wait()
    qo_out[ns - 1 - pc.s] = give[1].astype(F32)


def reduce_gradients(dims, cid, qo, terms, smalls, wd1, gu0a, gu0, wd0):
    ns, nb, nf = dims
    count = ns * nf
    dr, wide = terms.shape[1:]
    two_ff = gu0.shape[3]
    cut = gu0a.shape[0]
    half, width = wd1.shape
    rows = smalls[0].shape[0] + smalls[2].shape[0]
    small = (ns * (-(-rows // 8) * 8), 128)
    sds = jax.ShapeDtypeStruct
    dma = pltpu.SemaphoreType.DMA
    return call(
        functools.partial(reduce_kernel, dims),
        "reduce_gradients",
        cid,
        (
            sds((ns, dr, wide), F32),
            sds(small, F32),
            sds((count, dr, two_ff), BF),
            sds((ns, half, width), BF),
        ),
        [VM] * 4,
        [AN] + [VM] * 7 + [AN, VM],
        [
            pltpu.VMEM(qo.shape, BF),
            pltpu.VMEM((nb, nf - cut, dr, two_ff), BF),
            pltpu.VMEM((nf - cut, dr, two_ff), BF),
            pltpu.VMEM((half, width), BF),
            pltpu.VMEM(small, F32),
            pltpu.VMEM((count - 1,) + small, F32),
            pltpu.VMEM(small, F32),
            pltpu.VMEM((nb - 1,) + small, F32),
            pltpu.VMEM((nb, dr, wide), BF),
            pltpu.VMEM((ns, dr, wide), F32),
            pltpu.VMEM((2, dr, wide), BF),
            dma((3,)),
            dma((2,)),
            dma((2,)),
            dma((count - 1,)),
            dma((count - 1,)),
            dma((nb - 1,)),
            dma((nb - 1,)),
        ]
        + reduce_scratch(dims, half, width)
        + reduce_scratch(dims, dr, wide) * 2
        + row_scratch(dims)
        + scatter_scratch(dims, nb, dr, wide)[2:]
        + reduce_scratch(dims, nf - cut, dr, two_ff),
        (qo, terms, *smalls, wd1, gu0a, gu0, wd0),
    )


def last_kernel(dims, nk, plan, *refs):
    pc = Place(dims)
    ns, nb, nf = dims
    a_in, refs = (refs[:15], refs[15:])
    ab_in, refs = (refs[: plan.count], refs[plan.count :])
    sa1, sb0, sb1, wd1, wd0, give_out, gh1, refs = (*refs[:7], refs[7:])
    gh_ref, gu_got1, qo_out, small_out, gu_got, wd_got, take_out, take_grad = refs[:8]
    refs = refs[8:]
    held, sa0, gu0, terms, refs = (*refs[:4], refs[4:])
    wsum, small, sm_in, sm_mid, sm_line, z_out, mine, give, give_grad = refs[:9]
    lsem, ws, wr, ls, lr, zs, zr, refs = (*refs[9:16], refs[16:])
    n = 13 + len(plan.scratch) + 4 + 3 + 2
    ab_scratch, rest = (refs[:n], refs[n:])
    mate = (ns - 1 - pc.s, pc.b, pc.f)
    outs = remote(give_out, take_out, ws.at[2], wr.at[2], mate)
    grads = remote(give_grad, take_grad, ws.at[3], wr.at[3], mate)
    riders = attention_backward_part(
        pc, outs.start, held.shape[2], nk, 0, plan, "columns",
        *a_in, *ab_in, gh_ref, held, sa0, gu0, terms, gu_got1, *ab_scratch,
    )
    line_gu = riders[0]

    def keep(value):
        wsum[...] = value.astype(BF)

    def keep_of(l):
        def store(value):
            mine[l] = value

        return store

    line = LineReduce(pc, lambda t: wd0[t], keep, rest[0:4])
    ends = [
        LineReduce(pc, lambda t: z_out[t], keep_of(0), rest[4:8]),
        LineReduce(pc, lambda t: terms[t], keep_of(1), rest[8:12]),
    ]
    scatter = ReadyScatter(
        pc, lambda q: columns_of(held, q, nf, z_out.shape[2]), *rest[15:19]
    )
    scatter.start()
    ends[1].start()
    n1 = sb0.shape[0]
    per = small.shape[0] // ns
    nr = sa0.shape[0] + n1
    small[...] = jnp.zeros_like(small)
    for l, (a, g) in enumerate(((sa0, sb0), (sa1, sb1))):
        small[l * per : l * per + n1] = a[0:n1]
        small[l * per + n1 : l * per + 2 * n1] = g[...]
        small[l * per + 2 * n1 : l * per + nr] = a[n1 : a.shape[0]]
    smalls = [
        remote(small, sm_in.at[e - 1], ls.at[e - 1], lr.at[e - 1], pc.plane(e))
        for e in range(1, pc.count)
    ]
    for c in smalls:
        c.start()
    scatter.diagonal()
    scatter.early()

    @pl.when(pc.s == 0)
    def _():
        give_grad[...] = gh1[...].astype(BF)

    @pl.when(pc.s != 0)
    def _():
        give_grad[...] = gh_ref[...].astype(BF)

    def split(l, ref):
        @pl.when(pc.s == l)
        def _():
            pltpu.make_async_copy(ref, wd_got.at[l], lsem.at[0]).start()

        @pl.when(pc.s != l)
        def _():
            remote(ref, wd_got.at[pc.s], ws.at[0], wr.at[0], (l, pc.b, pc.f)).start()

    split(1, wd1)
    ends[1].service()
    scatter.late()
    grads.start()
    line.start()
    ends[1].service()
    line_gu.finish()
    hand_out = RowSends(pc, 0, gu_got, rest[12:15])
    for f in range(nf):
        hand_out.start(f, gu0.at[f])
    total = small[...]
    for e, c in enumerate(smalls):
        c.wait()
        total = total + sm_in[e]
    sm_mid[...] = total
    lines = [
        remote(sm_mid, sm_line.at[d - 1], zs.at[d - 1], zr.at[d - 1], pc.along(d))
        for d in range(1, nb)
    ]
    for c in lines:
        c.start()

    def store(value):
        z_out[...] = value.astype(BF)

    scatter.finish(store)
    ends[0].start()
    ends[1].finish()
    line.service()
    ends[0].service()
    ends[0].service()
    line.service()
    ends[0].finish()
    swap = remote(give.at[0], give.at[1], ws.at[1], wr.at[1], mate)
    give[0] = mine[ns - 1 - pc.s].astype(BF)
    swap.start()
    qo_out[pc.s] = mine[pc.s]
    total = sm_mid[...]
    for d, c in enumerate(lines):
        c.wait()
        total = total + sm_line[d]
    small_out[...] = total
    line.finish()
    split(0, wsum)
    hand_out.finish(gu0.at[0])
    outs.wait()
    grads.wait()
    swap.wait()
    qo_out[ns - 1 - pc.s] = give[1].astype(F32)
    pltpu.make_async_copy(wsum, wd_got.at[pc.s], lsem.at[0]).wait()
    remote(wsum, wd_got.at[pc.s], ws.at[0], wr.at[0], mate).wait()


def last_layer(dims, nk, cid, a_in, late, plan, smalls, wd1, wd0, give_out, gh1):
    ns, nb, nf = dims
    count = ns * nf
    width, rows = gh1.shape
    qkv = a_in[-1].shape[1] - width
    dr, cols = late[0].shape[2:]
    wide = cols // ns
    two_ff = late[1].shape[2]
    half = wd1.shape[0]
    n_small = smalls[0].shape[0] + smalls[1].shape[0]
    small = (ns * (-(-n_small // 8) * 8), 128)
    sds = jax.ShapeDtypeStruct
    dma = pltpu.SemaphoreType.DMA
    rows_all = sds((count, dr, two_ff), BF)
    return call(
        functools.partial(last_kernel, dims, nk, plan),
        "last_layer",
        cid,
        (
            sds((width, rows), F32),
            rows_all,
            sds((ns, dr, wide), F32),
            sds(small, F32),
            rows_all,
            sds((ns, half, width), BF),
            sds((width, rows), BF),
            sds((width, rows), BF),
        ),
        [VM, AN] + [VM] * 6,
        [VM] * 12 + [AN, AN, VM] + plan.places + [VM] * 7,
        [
            pltpu.VMEM(late[0].shape, BF),
            pltpu.VMEM(smalls[0].shape, F32),
            pltpu.VMEM((nf, dr, two_ff), BF),
            pltpu.VMEM((nb, dr, wide), BF),
            pltpu.VMEM((half, width), BF),
            pltpu.VMEM(small, F32),
            pltpu.VMEM((count - 1,) + small, F32),
            pltpu.VMEM(small, F32),
            pltpu.VMEM((nb - 1,) + small, F32),
            pltpu.VMEM((nb, dr, wide), BF),
            pltpu.VMEM((ns, dr, wide), F32),
            pltpu.VMEM((2, dr, wide), BF),
            pltpu.VMEM((width, rows), BF),
            dma((1,)),
            dma((4,)),
            dma((4,)),
            dma((count - 1,)),
            dma((count - 1,)),
            dma((nb - 1,)),
            dma((nb - 1,)),
        ]
        + backward_scratch(nk, width, rows, qkv)
        + plan.scratch
        + scatter_scratch(dims, nb, dr, wide)[2:]
        + row_scratch(dims)
        + [pltpu.VMEM(late[0].shape, BF), dma(())]
        + reduce_scratch(dims, half, width)
        + reduce_scratch(dims, dr, wide) * 2
        + row_scratch(dims)
        + scatter_scratch(dims, nb, dr, wide)[2:],
        (*a_in, *late, *plan.arrays, *smalls[0:1], *smalls[1:], wd1, wd0, give_out, gh1),
    )


def lay_out_kernel(
    dims, gu0, gu1, wd, qo, small, out0, out1, gh0, gh1, take_out, take_grad,
    block_out, input_grad, g1, wqkv, bqkv, wout, g2, wgu, wdn
):
    ns, nb, nf = dims
    half = wd.shape[1]
    s = lax.axis_index("section")
    qkv = wqkv.shape[2]
    width = wout.shape[2]
    full = jnp.concatenate([qo[y] for y in range(ns)], axis=1)
    wqkv[0] = full[:, :qkv]
    wout[0] = full[:, qkv:]
    for y in range(ns):
        wdn[0, y * half : (y + 1) * half, :] = wd[y].astype(F32)
    for l, gu in enumerate((gu0, gu1)):
        @pl.when(s == l)
        def _():
            for y in range(ns):
                for f in range(nf):
                    got = gu[y * nf + f].astype(F32)
                    for part in range(2):
                        for b in range(nb):
                            c0 = column_start(dims, part, b, f, y, half)
                            k0 = (part * nb + b) * half
                            wgu[0, :, c0 : c0 + half] = got[:, k0 : k0 + half]
    n1 = width // 128
    per = small.shape[0] // ns
    rows = small[pl.ds(pl.multiple_of(s * per, 8), per), :]
    for k in range(n1):
        g1[0:1, k * 128 : (k + 1) * 128] = rows[k : k + 1]
        g2[0:1, k * 128 : (k + 1) * 128] = rows[n1 + k : n1 + k + 1]
    for k in range(qkv // 128):
        bqkv[0:1, k * 128 : (k + 1) * 128] = rows[2 * n1 + k : 2 * n1 + k + 1]
    for out, pair, take in (
        (block_out, (out0, out1), take_out),
        (input_grad, (gh0, gh1), take_grad),
    ):
        for l in range(ns):
            @pl.when(s == l)
            def _():
                out[0, l] = pair[l][...].T
                out[0, 1 - l] = take[...].T.astype(F32)


def lay_out(dims, qkv, args):
    ns, nb, nf = dims
    gu, wd, qo = (args[0], args[2], args[3])
    width, rows = args[5].shape
    dr = qo.shape[1]
    sds = jax.ShapeDtypeStruct
    tokens = sds((1, ns, rows, width), F32)
    return pl.pallas_call(
        functools.partial(lay_out_kernel, dims),
        name="lay_out",
        out_shape=(
            tokens,
            tokens,
            sds((1, width), F32),
            sds((1, dr, qkv), F32),
            sds((1, qkv), F32),
            sds((1, dr, width), F32),
            sds((1, width), F32),
            sds((1, dr, gu.shape[0] * gu.shape[2]), F32),
            sds((1, ns * wd.shape[1], width), F32),
        ),
        in_specs=[VM] * len(args),
        out_specs=[VM] * 9,
        compiler_params=pltpu.CompilerParams(vmem_limit_bytes=VMEM_LIMIT),
    )(*args)


def shards(
    dims,
    tokens_in,
    positions,
    doc_ids,
    out_grad,
    norm1_gain,
    w_qkv,
    b_qkv,
    w_out,
    norm2_gain,
    w_gate_up,
    w_down,
):
    ns, nb, nf = dims
    seqs, rows, width = tokens_in.shape
    s = lax.axis_index("section")
    b = lax.axis_index("blk")
    dr = w_qkv.shape[1]
    qkv = w_qkv.shape[2]
    fr = w_down.shape[1]
    half = fr // ns
    ff = nb * half
    nk = min(nb, 1 + (LONGEST - 1 + rows - 1) // rows)

    tokens = lax.dynamic_index_in_dim(tokens_in, s, 0, keepdims=False)
    cot = lax.dynamic_index_in_dim(out_grad, s, 0, keepdims=False)
    pos = lax.dynamic_index_in_dim(positions, s, 0, keepdims=False)
    docs = lax.dynamic_index_in_dim(doc_ids, s, 0, keepdims=False).astype(F32)
    freq = jnp.exp(jnp.arange(HD // 2, dtype=F32) * (-2.0 / HD) * math.log(1000000.0))
    phase = freq[:, None] * pos.astype(F32)[None, :]
    cos_part, sin_part = (jnp.cos(phase), jnp.sin(phase))
    docs = docs.reshape(nb, rows)
    picked = (b - jnp.arange(nk) + nb) % nb
    meta = jnp.take(docs, picked, axis=0).reshape(nk * rows // 128, 128)
    query_docs = lax.dynamic_slice_in_dim(docs, b, 1)
    hidden = tokens.T.astype(F32)
    g = cot.T.astype(F32)

    wd = w_down[0].reshape(ns, half, width)
    small = jnp.concatenate([norm1_gain[0], norm2_gain[0], b_qkv[0]])
    total = -(-small.shape[0] // 1024) * 1024
    small = jnp.pad(small, (0, total - small.shape[0])).reshape(-1, 128)
    gup, wdp, gu_first, qo_first, qz, small_all = gather_weights(
        dims, w_gate_up, w_qkv, w_out, wd, small
    )
    cols = qkv + width
    wide = (width, 2 * ff)

    def ride(*pairs):
        return Riders(dims, tuple(a for a, _ in pairs), tuple(v for _, v in pairs))

    common = (small_all, meta, query_docs, cos_part, sin_part)
    qo0 = qo_first.reshape(width, cols)
    wgu0 = gu_first.reshape(wide)
    first = ride((("gather", 0), wdp))
    second = ride((("gather", 1), gup))
    third = ride((("gather", 1), wdp))
    together = half % 8 == 0
    if together:
        a0, wd0, qo1, f0, (gu1,) = lower_layer(
            dims, nk, 1, hidden, *common, qo0, first, qz, wgu0, second
        )
    else:
        a0, (wd0, qo1) = attention_forward(
            dims, nk, 1, 0, hidden, *common, qo0, first, "columns", qz
        )
        f0, (gu1,) = feed_forward(dims, 3, a0[6], a0[5], wgu0, wd0.reshape(ff, width), second)
    qo1 = qo1.reshape(width, cols)
    wd0 = wd0.reshape(ff, width)
    wgu1 = gu1.reshape(wide)
    if together:
        a1, b1 = upper_layer(dims, nk, 2, f0[0], *common, qo1, third, cot.T, g, wgu1)
    else:
        a1, (wd1, g_all) = attention_forward(
            dims, nk, 2, 1, f0[0], *common, qo1, third, "lanes", cot.T
        )
        wd1 = wd1.reshape(ff, width)
        b1 = feed_both(dims, 4, 1, a1[6], a1[5], g, g_all, wgu1, wd1, small_all)

    line_gu = (nb, nf, dr, 2 * ff)
    line_wd = (nb, half, width)
    line_qo = (nb, nf, dr, cols)
    everything = (0, half)
    ab1, (dwd1, out1) = attention_backward(
        dims, nk, 7, 1, b1[0], *common, f0[0], *a1[:5], qo1,
        ride((("reduce", everything), b1[2].reshape(line_wd))), "sum", (b1[4], a1[5]),
    )
    b0, (dgu1,) = feed_backward(
        dims, 6, 0, ab1[0], a0[5], f0[1], f0[2], wgu0, wd0, small_all,
        ride((("reduce", (0, nf)), b1[1].reshape(line_gu))),
    )
    dgu0 = b0[1].reshape(line_gu)
    swaps = [(0, 1), (1, 0)]
    give_out = jnp.where(s == 0, out1, f0[0]).astype(BF)
    if together and dr % 8 == 0:
        gh0, gu_got1, grad_qo, small_sum, gu_got0, wd_got, take_out, take_grad = last_layer(
            dims, nk, 8, (b0[0], *common, hidden, *a0[:5], qo0),
            (ab1[1].reshape(line_qo), dgu1), ride((("reduce", (0, nf)), dgu0)),
            (ab1[2], b0[3], b1[3]), dwd1, b0[2].reshape(line_wd), give_out, ab1[0],
        )
    else:
        cut = nf - nf // 4
        ab0, (dgu0a, terms, gu_got1) = attention_backward(
            dims, nk, 8, 0, b0[0], *common, hidden, *a0[:5], qo0,
            ride((("reduce", (0, cut)), dgu0)), "columns", (ab1[1].reshape(line_qo), dgu1),
        )
        gh0 = ab0[0]
        take_out = lax.ppermute(give_out, "section", swaps)
        take_grad = lax.ppermute(jnp.where(s == 0, ab1[0], gh0).astype(BF), "section", swaps)
        grad_qo, small_sum, gu_got0, wd_got = reduce_gradients(
            dims, 9, ab0[1].reshape(line_qo), terms,
            (ab0[2], ab1[2], b0[3], b1[3]), dwd1, dgu0a, dgu0, b0[2].reshape(line_wd),
        )
    return lay_out(
        dims,
        qkv,
        (gu_got0, gu_got1, wd_got, grad_qo, small_sum, f0[0], out1, gh0, ab1[0], take_out,
         take_grad),
    )


def solution(mesh):
    dims = (mesh.shape["section"], mesh.shape["blk"], mesh.shape["fsdp"])
    return jax.shard_map(
        functools.partial(shards, dims),
        mesh=mesh,
        in_specs=(
            P("fsdp", "blk", None),
            P("fsdp", "blk"),
            P("fsdp", None),
            P("fsdp", "blk", None),
            P("section", None),
            P("section", ("blk", "fsdp"), None),
            P("section", None),
            P("section", ("blk", "fsdp"), None),
            P("section", None),
            P("section", ("blk", "fsdp"), None),
            P("section", ("blk", "fsdp"), None),
        ),
        out_specs=(
            P("section", "fsdp", "blk", None),
            P("section", "fsdp", "blk", None),
            P("section", None),
            P("section", ("blk", "fsdp"), None),
            P("section", None),
            P("section", ("blk", "fsdp"), None),
            P("section", None),
            P("section", ("blk", "fsdp"), None),
            P("section", ("blk", "fsdp"), None),
        ),
        check_vma=False,
    )
```

```python
import functools
import math

import jax
import jax.numpy as jnp
from jax import lax
from jax.experimental import pallas as pl
from jax.experimental.pallas import tpu as pltpu
from jax.sharding import PartitionSpec as P

H = 14
KVH = 2
HD = 64
GROUP = H // KVH
LONGEST = 512
NEG = -1e30
BF = jnp.bfloat16
F32 = jnp.float32
MESH = pl.DeviceIdType.MESH
VMEM_LIMIT = 60 * 2**20
VM = pl.BlockSpec(memory_space=pltpu.VMEM)
AN = pl.BlockSpec(memory_space=pl.ANY)


def nn(a, b):
    return lax.dot_general(a, b, (((1,), (0,)), ((), ())), preferred_element_type=F32)


def nt(a, b):
    return lax.dot_general(a, b, (((1,), (1,)), ((), ())), preferred_element_type=F32)


def tn(a, b):
    return lax.dot_general(a, b, (((0,), (0,)), ((), ())), preferred_element_type=F32)


def other(f):
    return f + 1 - 2 * (f % 2)


class Place:
    def __init__(self, dims):
        self.ns, self.nb, self.nf = dims
        self.count = self.ns * self.nf
        self.s = lax.axis_index("section")
        self.b = lax.axis_index("blk")
        self.f = lax.axis_index("fsdp")
        self.me = self.s * self.nf + self.f
        self.two_level = self.ns == 2 and self.nf == 4

    def plane(self, e):
        q = (self.me + e) % self.count
        return (q // self.nf, self.b, q % self.nf)

    def slot_from(self, e):
        return (self.me + self.count - e) % self.count

    def along(self, d):
        return (self.s, (self.b + d) % self.nb, self.f)

    def mates(self):
        s, b, f = (self.s, self.b, self.f)
        xf = (f + 2) % 4
        return ((s, b, other(f)), (s, b, xf), (1 - s, b, f))

    def slots(self):
        s, f = (self.s, self.f)
        xf = (f + 2) % 4
        t = 1 - s
        return (
            s * 4 + f,
            s * 4 + other(f),
            s * 4 + xf,
            t * 4 + f,
            s * 4 + other(xf),
            t * 4 + other(f),
            t * 4 + xf,
            t * 4 + other(xf),
        )


def pick(i, values):
    total = 0
    for k, v in enumerate(values):
        total = total + jnp.where(i == k, v, 0)
    return total


def greet(place, plane, along):
    barrier = pltpu.get_barrier_semaphore()
    count = 0
    if plane:
        if place.two_level and plane == "mates":
            targets = list(place.mates())
        else:
            targets = [place.plane(e) for e in range(1, place.count)]
        for t in targets:
            pl.semaphore_signal(barrier, 1, device_id=t, device_id_type=MESH)
        count += len(targets)
    if along:
        for d in range(1, place.nb):
            pl.semaphore_signal(barrier, 1, device_id=place.along(d), device_id_type=MESH)
        count += place.nb - 1
    pl.semaphore_wait(barrier, count)


def remote(src, dst, ssem, rsem, device):
    return pltpu.make_async_remote_copy(
        src_ref=src,
        dst_ref=dst,
        send_sem=ssem,
        recv_sem=rsem,
        device_id=device,
        device_id_type=MESH,
    )


def cut_in(parts, view, c):
    n = view.shape[0] // parts
    return view.at[pl.ds(c * n, n)]


def gather_sems(dims):
    n = 2 * (dims[0] * dims[2] - 1)
    return [pltpu.SemaphoreType.DMA((n,)), pltpu.SemaphoreType.DMA((n,))]


class PlaneGather:
    def __init__(self, place, slot, ssem, rsem):
        self.place, self.slot, self.ssem, self.rsem = (place, slot, ssem, rsem)
        self.parts = 2 if place.two_level else 1
        if place.two_level:
            self.order = place.slots()
        else:
            self.order = tuple(place.slot_from(e) for e in range(place.count))

    def copy(self, k, c, q, device):
        v = cut_in(self.parts, self.slot(q), c)
        i = k * self.parts + c
        return remote(v, v, self.ssem.at[i], self.rsem.at[i], device)

    def start(self):
        pc = self.place
        if pc.two_level:
            core, xm, ym = pc.mates()
            for c in range(2):
                self.copy(1, c, self.order[0], xm).start()
                self.copy(2, c, self.order[0], ym).start()
            for c in range(2):
                self.copy(0, c, self.order[0], core).start()
        else:
            for e in range(1, pc.count):
                self.copy(e - 1, 0, self.order[0], pc.plane(e)).start()

    def came(self, k, c):
        self.copy(k, c, self.order[k + 1], self.place.plane(1)).wait_recv()

    def before(self, step):
        if step == 0:
            return
        pc = self.place
        if not pc.two_level:
            self.came(step - 1, 0)
            return
        core, xm, ym = pc.mates()
        h = pc.f % 2
        if step == 2:
            which = h * self.order[3] + (1 - h) * self.order[2]
            far = (
                h * xm[0] + (1 - h) * ym[0],
                pc.b,
                h * xm[2] + (1 - h) * ym[2],
            )
            for c in range(2):
                self.came(1, c)
                self.came(2, c)
                self.copy(5, c, which, far).start()
                self.copy(3, c, self.order[2], core).start()
                self.copy(4, c, self.order[3], core).start()
        elif step == 3:
            return
        elif step == 6:
            for c in range(2):
                self.came(5, c)
                self.copy(6, c, self.order[6], core).start()
        else:
            for c in range(2):
                self.came(step - 1, c)

    def finish(self):
        n = self.place.count - 1
        for k in range(n):
            for c in range(self.parts):
                self.copy(k, c, self.order[0], self.place.plane(1)).wait_send()


class PlaneScatter:
    def __init__(self, place, near, away, back, hop, ssem, rsem):
        self.place = place
        self.near, self.away, self.back, self.hop = (near, away, back, hop)
        self.ssem, self.rsem = (ssem, rsem)

    def put(self, step, value):
        pc = self.place
        if not pc.two_level:
            @pl.when(step == 0)
            def _():
                self.near[0] = value

            @pl.when(step > 0)
            def _():
                e = pc.count - step
                self.away[e - 1] = value.astype(BF)
                q = (pc.me + e) % pc.count
                remote(
                    self.away.at[e - 1],
                    self.back.at[e - 1],
                    self.ssem.at[e - 1],
                    self.rsem.at[e - 1],
                    (q // pc.nf, pc.b, q % pc.nf),
                ).start()
            return
        core, xm, ym = pc.mates()
        here = (step == 0) | (step == 2) | (step == 3) | (step == 6)
        q = pick(step, (0, 0, 1, 2, 1, 2, 3, 3))

        @pl.when(here)
        def _():
            self.near[q] = value

        @pl.when(jnp.logical_not(here))
        def _():
            self.away[q] = value.astype(BF)
            self.core_copy(q).start()

    def core_copy(self, q):
        core = self.place.mates()[0]
        return remote(self.away.at[q], self.back.at[q], self.ssem.at[q], self.rsem.at[q], core)

    def far_copy(self, e):
        return remote(self.away.at[e - 1], self.back.at[e - 1], self.ssem.at[e - 1],
                      self.rsem.at[e - 1], self.place.plane(e))

    def hop_copy(self, k, c, device):
        i = 4 + 2 * k + c
        return remote(
            cut_in(2, self.hop.at[k], c),
            cut_in(2, self.hop.at[k + 3], c),
            self.ssem.at[i],
            self.rsem.at[i],
            device,
        )

    def rows(self, c):
        n = self.hop.shape[1] // 2
        return slice(c * n, (c + 1) * n)

    def targets(self):
        pc = self.place
        core, xm, ym = pc.mates()
        c = pc.f % 2
        first = (c * xm[0] + (1 - c) * ym[0], pc.b, c * xm[2] + (1 - c) * ym[2])
        second = (c * ym[0] + (1 - c) * xm[0], pc.b, c * ym[2] + (1 - c) * xm[2])
        return (first, second)

    def early(self):
        pc = self.place
        if not pc.two_level:
            return
        c = pc.f % 2
        first, second = self.targets()
        self.core_copy(1).wait_recv()
        self.core_copy(2).wait_recv()
        q = c * 1 + (1 - c) * 2
        for k in range(2):
            r = self.rows(k)
            self.hop[0, r] = (self.mine(q, r) + self.back[q, r].astype(F32)).astype(BF)
            self.hop_copy(0, k, first).start()

    def diagonal(self):
        pc = self.place
        if not pc.two_level:
            return
        first, second = self.targets()
        self.core_copy(3).wait_recv()
        for k in range(2):
            r = self.rows(k)
            self.hop[1, r] = (self.mine(3, r) + self.back[3, r].astype(F32)).astype(BF)
            self.hop_copy(1, k, first).start()

    def mine(self, q, r=slice(None)):
        return self.near[q, r]

    def result(self, store):
        self.late()
        self.finish(store)

    def late(self):
        pc = self.place
        if not pc.two_level:
            return
        c = pc.f % 2
        first, second = self.targets()
        q = c * 2 + (1 - c) * 1
        for k in range(2):
            r = self.rows(k)
            self.hop_copy(1, k, first).wait_recv()
            self.hop[2, r] = (
                self.mine(q, r) + self.back[q, r].astype(F32) + self.hop[4, r].astype(F32)
            ).astype(BF)
            self.hop_copy(2, k, second).start()

    def finish(self, store):
        pc = self.place
        if not pc.two_level:
            total = self.mine(0)
            for e in range(1, pc.count):
                self.far_copy(e).wait()
                total = total + self.back[e - 1].astype(F32)
            store(total)
            return
        first, second = self.targets()
        self.core_copy(0).wait_recv()
        for k in range(2):
            self.hop_copy(0, k, first).wait_recv()
            self.hop_copy(2, k, second).wait_recv()
        store(
            self.mine(0)
            + self.back[0].astype(F32)
            + self.hop[3].astype(F32)
            + self.hop[5].astype(F32)
        )
        for q in range(4):
            self.core_copy(q).wait_send()
        for k in range(2):
            self.hop_copy(0, k, first).wait_send()
            self.hop_copy(1, k, first).wait_send()
            self.hop_copy(2, k, second).wait_send()


class ReadyScatter(PlaneScatter):
    def __init__(self, place, part, back, hop, ssem, rsem):
        super().__init__(place, None, None, back, hop, ssem, rsem)
        self.part = part
        if place.two_level:
            o = place.slots()
            self.here = (o[0], o[2], o[3], o[6])
            self.gone = (o[1], o[4], o[5], o[7])

    def mine(self, q, r=slice(None)):
        if not self.place.two_level:
            return self.part(self.place.me)[...].astype(F32)
        return self.part(pick(q, self.here))[r].astype(F32)

    def core_copy(self, q):
        core = self.place.mates()[0]
        v = self.part(self.gone[q])
        return remote(v, self.back.at[q], self.ssem.at[q], self.rsem.at[q], core)

    def far_copy(self, e):
        pc = self.place
        v = self.part((pc.me + e) % pc.count)
        return remote(v, self.back.at[e - 1], self.ssem.at[e - 1], self.rsem.at[e - 1],
                      pc.plane(e))

    def start(self):
        pc = self.place
        if pc.two_level:
            for q in (3, 2, 1, 0):
                self.core_copy(q).start()
        else:
            for e in range(1, pc.count):
                self.far_copy(e).start()


class RowSends:
    def __init__(self, place, layer, out, sems):
        self.place, self.layer, self.out = (place, layer, out)
        self.lsem, self.ss, self.sr = sems

    def copies(self, f, src):
        pc = self.place
        e = (self.layer * pc.nf + f - pc.me + pc.count) % pc.count
        own = self.out.at[pc.me]
        k = (e + pc.count - 1) % pc.count
        away = remote(src, own, self.ss.at[f], self.sr.at[k], (self.layer, pc.b, f))
        return (e, away, pltpu.make_async_copy(src, own, self.lsem))

    def start(self, f, src):
        e, away, local = self.copies(f, src)

        @pl.when(e != 0)
        def _():
            away.start()

        @pl.when(e == 0)
        def _():
            local.start()

    def finish(self, src):
        pc = self.place
        for f in range(pc.nf):
            e, away, local = self.copies(f, src)

            @pl.when(e != 0)
            def _():
                away.wait_send()

            @pl.when(e == 0)
            def _():
                local.wait()

        @pl.when(pc.s == self.layer)
        def _():
            for e in range(1, pc.count):
                q = pc.slot_from(e)
                remote(src, self.out.at[q], self.ss.at[0], self.sr.at[e - 1], pc.plane(e)).wait_recv()


def row_scratch(dims):
    dma = pltpu.SemaphoreType.DMA
    return [dma(()), dma((dims[2],)), dma((dims[0] * dims[2],))]


class LineGather:
    def __init__(self, place, piece, out, sems, part=None):
        self.place, self.piece = (place, piece)
        self.view = lambda t: out.at[t] if part is None else out.at[t, part]
        self.lsem, self.ss, self.sr = sems
        self.k = 0

    def local(self):
        return pltpu.make_async_copy(self.piece, self.view(self.place.b), self.lsem)

    def hop(self, way, k, came):
        pc = self.place
        t = pc.b - way * (k - (0 if came else 1))
        src = self.piece if k == 1 and not came else self.view(t)
        i = k - 1 + (0 if way == 1 else pc.nb - 1)
        return remote(
            src, self.view(t), self.ss.at[i], self.sr.at[i], (pc.s, pc.b + way, pc.f)
        )

    def sends(self, way, k):
        b, nb = (self.place.b, self.place.nb)
        return (b >= k - 1) & (b < nb - 1) if way == 1 else (b <= nb - k) & (b > 0)

    def comes(self, way, k):
        b, nb = (self.place.b, self.place.nb)
        return b >= k if way == 1 else b <= nb - 1 - k

    def arrived(self, k):
        for way in (1, -1):
            @pl.when(self.comes(way, k))
            def _():
                self.hop(way, k, True).wait_recv()

    def start(self):
        self.local().start()
        self.service()

    def service(self):
        if self.k == self.place.nb - 1:
            return
        self.k += 1
        if self.k > 1:
            self.arrived(self.k - 1)
        for way in (1, -1):
            @pl.when(self.sends(way, self.k))
            def _():
                self.hop(way, self.k, False).start()

    def finish(self):
        last = self.place.nb - 1
        while self.k < last:
            self.service()
        self.arrived(last)
        for k in range(1, last + 1):
            for way in (1, -1):
                @pl.when(self.sends(way, k))
                def _():
                    self.hop(way, k, False).wait_send()
        self.local().wait()


class LineReduce:
    def __init__(self, place, terms, store, sems, load=None):
        self.place, self.terms, self.store, self.load = (place, terms, store, load)
        self.out, self.came, self.ss, self.sr = sems
        self.k = 0

    def index(self, way, k):
        return k - 1 + (0 if way == 1 else self.place.nb - 1)

    def hop(self, way, k):
        pc = self.place
        i = self.index(way, k)
        return remote(
            self.out.at[i], self.came.at[i], self.ss.at[i], self.sr.at[i],
            (pc.s, pc.b + way, pc.f),
        )

    def rank(self, way):
        pc = self.place
        return pc.b if way == 1 else pc.nb - 1 - pc.b

    def sends(self, way, k):
        r = self.rank(way)
        return (r < k) & (r < self.place.nb - 1)

    def start(self):
        if self.load is not None:
            self.load.wait()
        self.service()

    def service(self):
        nb = self.place.nb
        if self.k == nb - 1:
            return
        self.k += 1
        k = self.k
        for way in (1, -1):
            r = self.rank(way)
            t = nb - k + r if way == 1 else k - 1 - r
            i = self.index(way, k)

            @pl.when(self.sends(way, k) & (r == 0))
            def _():
                self.out[i] = self.terms(t)

            if k > 1:
                @pl.when(self.sends(way, k) & (r > 0))
                def _():
                    self.hop(way, k - 1).wait_recv()
                    total = self.terms(t).astype(F32) + self.came[i - 1].astype(F32)
                    self.out[i] = total.astype(BF)

            @pl.when(self.sends(way, k))
            def _():
                self.hop(way, k).start()

    def finish(self):
        pc = self.place
        last = pc.nb - 1
        while self.k < last:
            self.service()
        right, left = (self.index(1, last), self.index(-1, last))

        @pl.when(pc.b == 0)
        def _():
            self.hop(-1, last).wait_recv()
            self.store(self.terms(pc.b).astype(F32) + self.came[left].astype(F32))

        @pl.when(pc.b == last)
        def _():
            self.hop(1, last).wait_recv()
            self.store(self.terms(pc.b).astype(F32) + self.came[right].astype(F32))

        @pl.when((pc.b > 0) & (pc.b < last))
        def _():
            self.hop(1, last).wait_recv()
            self.hop(-1, last).wait_recv()
            self.store(
                self.terms(pc.b).astype(F32)
                + self.came[right].astype(F32)
                + self.came[left].astype(F32)
            )

        for k in range(1, last + 1):
            for way in (1, -1):
                @pl.when(self.sends(way, k))
                def _():
                    self.hop(way, k).wait_send()


def gather_scratch(dims):
    dma = pltpu.SemaphoreType.DMA
    return [dma(()), dma((2 * (dims[1] - 1),)), dma((2 * (dims[1] - 1),))]


def reduce_scratch(dims, *block):
    dma = pltpu.SemaphoreType.DMA
    n = 2 * (dims[1] - 1)
    return [pltpu.VMEM((n,) + block, BF), pltpu.VMEM((n,) + block, BF), dma((n,)), dma((n,))]


class Riders:
    def __init__(self, dims, specs, arrays):
        self.dims, self.specs, self.arrays = (dims, specs, arrays)
        self.shapes = []
        self.places = [AN] * len(specs)
        self.outs = []
        self.scratch = []
        self.sizes = []
        for spec, a in zip(specs, arrays):
            if spec[0] == "gather":
                shape = (dims[1],) + a.shape[1:]
                scratch = gather_scratch(dims)
            else:
                lo, hi = spec[1]
                shape = (hi - lo,) + a.shape[2:]
                scratch = reduce_scratch(dims, *shape)
                scratch += [
                    pltpu.VMEM((dims[1],) + shape, BF), pltpu.SemaphoreType.DMA(())
                ]
            self.outs.append(AN if spec[0] == "gather" else VM)
            self.shapes.append(jax.ShapeDtypeStruct(shape, a.dtype))
            self.scratch += scratch
            self.sizes.append(len(scratch))
        self.count = len(specs)

    def board(self, place, ins, outs, scratch):
        out = []
        for spec, size, a, o in zip(self.specs, self.sizes, ins, outs):
            mine, scratch = (scratch[:size], scratch[size:])
            if spec[0] == "gather":
                out.append(LineGather(place, a.at[spec[1]], o, mine))
            else:
                lo, hi = spec[1]

                def store(value, o=o):
                    o[...] = value.astype(BF)

                terms, sem = mine[4:]
                load = pltpu.make_async_copy(a.at[:, lo:hi], terms, sem)
                load.start()
                out.append(
                    LineReduce(place, lambda t, r=terms: r[t], store, mine[:4], load)
                )
        return (out, scratch)


def each(riders, what):
    for r in riders:
        getattr(r, what)()


def scatter_scratch(dims, *block):
    count = dims[0] * dims[2]
    if dims[0] == 2 and dims[2] == 4:
        near, away, hops, sems = (4, 4, 6, 10)
    else:
        near, away, hops, sems = (1, count - 1, 1, count - 1)
    return [
        pltpu.VMEM((near,) + block, F32),
        pltpu.VMEM((away,) + block, BF),
        pltpu.VMEM((away,) + block, BF),
        pltpu.VMEM((hops,) + block, BF),
        pltpu.SemaphoreType.DMA((sems,)),
        pltpu.SemaphoreType.DMA((sems,)),
    ]


def call(kernel, name, cid, outs, out_specs, in_specs, scratch, args):
    params = pltpu.CompilerParams(
        collective_id=cid, has_side_effects=True, vmem_limit_bytes=VMEM_LIMIT
    )
    return pl.pallas_call(
        kernel,
        name=name,
        out_shape=outs,
        in_specs=in_specs,
        out_specs=out_specs,
        scratch_shapes=scratch,
        compiler_params=params,
    )(*args)


def column_start(dims, part, b, f, y, half):
    ns, nb, nf = dims
    return part * nb * nf * ns * half + ((b * nf + f) * ns + y) * half


def columns_of(ref, q, nf, wide):
    return ref.at[:, q % nf, :, pl.ds(pl.multiple_of((q // nf) * wide, wide), wide)]


def gather_weights_kernel(
    dims, w_ref, wq_ref, wo_ref, wd, g1_ref, g2_ref, bias_ref,
    gup, wdp, gu_first, qo_first, qz, small_all,
    small, pack, qcol, qh, lsem, ps, pr, ms, mr, qs, qr, *rest
):
    pc = Place(dims)
    ns, nb, nf = dims
    half = wd.shape[1]
    wide = qh.shape[2]
    greet(pc, "all", True)
    small[...] = jnp.zeros_like(small)
    r = 0
    for ref in (g1_ref, g2_ref, bias_ref):
        for k in range(0, ref.shape[1], 128):
            small[r : r + 1, :] = ref[0:1, k : k + 128]
            r += 1
    qkv = wq_ref.shape[2]
    full = jnp.concatenate([wq_ref[0], wo_ref[0]], axis=1)
    for y in range(ns):
        qcol[y] = full[:, y * wide : (y + 1) * wide]
    across = []
    for d in range(1, ns):
        y = (pc.s + d) % ns
        t = (y, pc.b, pc.f)
        i = 3 * (d - 1)
        across.append(remote(qcol.at[y], qh.at[pc.s], ms.at[i], mr.at[i], t))
        across.append(remote(wd.at[y], wdp.at[pc.s], ms.at[i + 1], mr.at[i + 1], t))
        across.append(remote(small, small_all.at[pc.s], ms.at[i + 2], mr.at[i + 2], t))
    for c in across:
        c.start()
    qh[pc.s] = qcol[pc.s]
    local = [
        pltpu.make_async_copy(wd.at[pc.s], wdp.at[pc.s], lsem.at[0]),
        pltpu.make_async_copy(small, small_all.at[pc.s], lsem.at[1]),
    ]
    for c in local:
        c.start()
    own = pltpu.make_async_copy(pack.at[pc.s, pc.f], gup.at[pc.s, pc.f], lsem.at[2])

    def piece(y, f):
        e = (y * nf + f - pc.me + pc.count) % pc.count
        k = (e + pc.count - 1) % pc.count
        return (
            e,
            remote(pack.at[y, f], gup.at[pc.s, pc.f], ps.at[k], pr.at[k], (y, pc.b, f)),
        )

    for f in range(nf):
        for y in range(ns):
            pieces = []
            for part in range(2):
                for b in range(nb):
                    c0 = column_start(dims, part, b, f, y, half)
                    pieces.append(w_ref[0, :, c0 : c0 + half])
            pack[y, f] = jnp.concatenate(pieces, axis=1)
            e, c = piece(y, f)

            @pl.when(e != 0)
            def _():
                c.start()

    own.start()
    for d in range(ns - 1):
        across[3 * d].wait()
    line_q = LineGather(pc, qh, qz, rest[0:3])
    lines = [
        LineGather(pc, gup.at[0, f], gu_first, rest[3 + 3 * f : 6 + 3 * f], f) for f in range(nf)
    ]
    line_q.start()

    def arrived(y, f):
        e, c = piece(y, f)
        k = (2 * pc.count - e - 1) % pc.count

        @pl.when(e != 0)
        def _():
            remote(pack.at[0, 0], gup.at[y, f], ps.at[k], pr.at[k], (y, pc.b, f)).wait_recv()

    own.wait()
    line_q.service()
    for f in range(nf):
        arrived(0, f)
        lines[f].start()
    line_q.service()
    for line in lines:
        line.service()
    line_q.finish()
    gather = PlaneGather(pc, lambda q: columns_of(qo_first, q, nf, wide), qs, qr)
    columns_of(qo_first, pc.me, nf, wide)[...] = qz[:, 0]
    gather.start()
    for step in range(1, min(6, pc.count)):
        gather.before(step)
    for line in lines:
        line.service()
    for step in range(min(6, pc.count), pc.count):
        gather.before(step)
    gather.finish()
    for y in range(1, ns):
        for f in range(nf):
            arrived(y, f)
    for y in range(ns):
        for f in range(nf):
            e, c = piece(y, f)

            @pl.when(e != 0)
            def _():
                c.wait_send()

    for c in local:
        c.wait()
    for i, c in enumerate(across):
        if i % 3:
            c.wait()
    for line in lines:
        line.finish()


def gather_weights(dims, w, wq, wo, wd, vectors):
    ns, nb, nf = dims
    count = ns * nf
    half, width = wd.shape[1:]
    dr = wq.shape[1]
    cols = wq.shape[2] + wo.shape[2]
    wide = cols // ns
    two_ff = 2 * nb * half
    small = (-(-sum(v.shape[1] for v in vectors) // 1024) * 8, 128)
    sds = jax.ShapeDtypeStruct
    outs = (
        sds((ns, nf, dr, two_ff), BF),
        sds((ns, half, width), BF),
        sds((nb, nf, dr, two_ff), BF),
        sds((nb, nf, dr, cols), BF),
        sds((nb, ns, dr, wide), BF),
        sds((ns,) + small, F32),
    )
    dma = pltpu.SemaphoreType.DMA
    return call(
        functools.partial(gather_weights_kernel, dims),
        "gather_weights",
        0,
        outs,
        [AN, AN, AN, VM, VM, AN],
        [VM, VM, VM, AN, VM, VM, VM],
        [
            pltpu.VMEM(small, F32),
            pltpu.VMEM((ns, nf, dr, two_ff), BF),
            pltpu.VMEM((ns, dr, wide), BF),
            pltpu.VMEM((ns, dr, wide), BF),
            dma((4,)),
            dma((count,)),
            dma((count,)),
            dma((3 * (ns - 1),)),
            dma((3 * (ns - 1),)),
        ]
        + gather_sems(dims)
        + gather_scratch(dims) * (1 + nf),
        (w, wq, wo, wd, *vectors),
    )


def rms(values):
    return lax.rsqrt(jnp.mean(values * values, axis=0, keepdims=True) + 1e-06)


def column(rows_t, first, count):
    return jnp.concatenate([rows_t[:, k : k + 1] for k in range(first, first + count)], axis=0)


def rows_of(values):
    v = folded(values)
    return jnp.concatenate(
        [v[k : k + 128].T.sum(axis=0, keepdims=True) for k in range(0, v.shape[0], 128)], axis=0
    )


def folded(v):
    out = v[:, :128]
    for k in range(1, v.shape[1] // 128):
        out = out + v[:, k * 128 : (k + 1) * 128]
    return out


def fill_masks(pc, mask, docs_ref):
    nk, rows = mask.shape[:2]
    picked = []
    for j in range(nk):
        start = pl.multiple_of((pc.b - j + pc.nb) % pc.nb * rows, rows)
        row = jnp.zeros((1, rows), F32)
        for t in range(pc.ns):
            mine = jnp.where(pc.s == t, 1.0, 0.0)
            row = row + docs_ref[t : t + 1, pl.ds(start, rows)].astype(F32) * mine
        picked.append(row)
    query_docs = picked[0]
    meta_t = padded_t(
        jnp.concatenate(
            [row[:, k : k + 128] for row in picked for k in range(0, rows, 128)], axis=0
        )
    )
    key_i = lax.broadcasted_iota(jnp.int32, (rows, rows), 0)
    query_i = lax.broadcasted_iota(jnp.int32, (rows, rows), 1)
    per = rows // 128
    for j in range(nk):
        same = column(meta_t, j * per, per) == query_docs
        if j == 0:
            live = same & (key_i <= query_i)
        else:
            live = same & (key_i < (pc.b - j + 1) * rows)
        mask[j] = jnp.where(live, 0.0, NEG)


def load_qo(qo, w, wo, sems):
    cols = w.shape[1]
    c1 = pltpu.make_async_copy(qo.at[:, 0:cols], w, sems.at[0])
    c2 = pltpu.make_async_copy(qo.at[:, cols : cols + wo.shape[1]], wo, sems.at[1])
    c1.start()
    c2.start()
    return (c1, c2)


def gains_of(small_t, width, qkv):
    n = width // 128
    return (
        column(small_t, 0, n),
        column(small_t, n, n),
        column(small_t, 2 * n, qkv // 128),
    )


def padded_t(v):
    n = v.shape[0]
    return jnp.concatenate([v, jnp.zeros((128 - n, 128), v.dtype)], axis=0).T


def attention_forward_kernel(dims, *args):
    pc = Place(dims)
    riders, gather = attention_forward_part(pc, *args)
    last_blocks(pc, gather)
    gather.finish()
    each(riders, "finish")


def last_blocks(pc, gather):
    for step in range(min(6, pc.count), pc.count):
        gather.before(step)


def attention_forward_part(
    pc, nk, layer, plan, carry, h_ref, small_ref, docs_ref, cos_ref, sin_ref, qo_all,
    *refs
):
    n = plan.count
    block_ref, refs = (refs[0], refs[1:])
    ins, refs = (refs[:n], refs[n:])
    normed_ref, q_ref, kv_ref, lse_ref, mixed_ref, res_ref, n2_ref = refs[:7]
    outs, refs = (refs[7 : 7 + n], refs[7 + n :])
    block_all, refs = (refs[0], refs[1:])
    w, wo, mask, joined, top_own, sum_own, out_own, ssem, rsem, qsem = refs[:10]
    refs = refs[10:]
    width, rows = h_ref.shape
    loads = load_qo(qo_all, w, wo, qsem)
    greet(pc, "mates", True)
    riders, refs = plan.board(pc, ins, outs, refs)
    if carry == "lanes":
        own = block_ref
        slot = lambda q: block_all.at[:, lanes(q, rows)]
    else:
        own = block_ref.at[:, 1]
        slot = lambda q: columns_of(block_all, q, pc.nf, block_ref.shape[3])
    gather = PlaneGather(pc, slot, *refs)
    slot(pc.me)[...] = own[...]
    gather.start()
    each(riders, "start")
    g1, g2, bias = gains_of(padded_t(small_ref[layer]), width, w.shape[1])
    hidden = h_ref[...].astype(BF).astype(F32)
    normed = (hidden * rms(hidden) * g1).astype(BF)
    normed_ref[...] = normed
    fill_masks(pc, mask, docs_ref)
    loads[0].wait()
    joined[...] = tn(w[...], normed) + bias
    cos_part = cos_ref[...]
    sin_part = sin_ref[...]
    half = HD // 2

    def turned(row):
        u1 = joined[pl.ds(row, half), :]
        u2 = joined[pl.ds(row + half, half), :]
        return (u1 * cos_part - u2 * sin_part, u2 * cos_part + u1 * sin_part)

    for g in range(KVH):
        r1, r2 = turned((H + g) * HD)
        kv_ref[0, g, :half, :] = r1.astype(BF)
        kv_ref[0, g, half:, :] = r2.astype(BF)
        v0 = (H + KVH + g) * HD
        kv_ref[0, KVH + g] = joined[v0 : v0 + HD, :].astype(BF)
    sends = [
        remote(kv_ref.at[0], kv_ref.at[j], ssem.at[j - 1], rsem.at[j - 1], pc.along(j))
        for j in range(1, nk)
    ]
    for c in sends:
        c.start()
    scale = HD**-0.5
    for head in range(H):
        r1, r2 = turned(head * HD)
        q_ref[head, :half, :] = (r1 * scale).astype(BF)
        q_ref[head, half:, :] = (r2 * scale).astype(BF)
    for g in range(KVH):
        keys = kv_ref[0, g].T
        values = kv_ref[0, KVH + g]

        def own_keys(i, carried):
            head = g * GROUP + i
            x = nn(keys, q_ref[head]) + mask[0]
            top = x.max(axis=0, keepdims=True)
            e = jnp.exp(x - top)
            top_own[head] = top
            sum_own[head] = e.sum(axis=0, keepdims=True)
            out_own[head] = nn(values, e.astype(BF))
            return carried

        lax.fori_loop(0, GROUP, own_keys, 0, unroll=True)
    for c in sends:
        c.wait()
    each(riders, "service")
    for g in range(KVH):
        keys = [kv_ref[j, g].T for j in range(1, nk)]
        values = [kv_ref[j, KVH + g] for j in range(1, nk)]

        def one_head(i, carried):
            head = g * GROUP + i
            q = q_ref[head]
            s = [nn(keys[j], q) + mask[j + 1] for j in range(nk - 1)]
            first = top_own[head]
            top = first
            for x in s:
                top = jnp.maximum(top, x.max(axis=0, keepdims=True))
            e = [jnp.exp(x - top) for x in s]
            fade = jnp.exp(first - top)
            total = sum_own[head] * fade
            out = out_own[head] * fade
            for j in range(nk - 1):
                total = total + e[j].sum(axis=0, keepdims=True)
                out = out + nn(values[j], e[j].astype(BF))
            lse_ref[head] = top + jnp.log(total)
            mixed_ref[head] = (out / total).astype(BF)
            return carried

        lax.fori_loop(0, GROUP, one_head, 0, unroll=True)
        if g == 0:
            for step in range(1, min(6, pc.count)):
                gather.before(step)
        else:
            each(riders, "service")
    mixed = mixed_ref[...].reshape(H * HD, rows)
    loads[1].wait()
    residual = hidden + tn(wo[...], mixed)
    res_ref[...] = residual
    n2_ref[...] = (residual * rms(residual) * g2).astype(BF)
    return (riders, gather)


def attention_scratch(dims, nk, width, rows, qkv):
    dma = pltpu.SemaphoreType.DMA
    return [
        pltpu.VMEM((width, qkv), BF),
        pltpu.VMEM((width, width), BF),
        pltpu.VMEM((nk, rows, rows), F32),
        pltpu.VMEM((qkv, rows), F32),
        pltpu.VMEM((H, 1, rows), F32),
        pltpu.VMEM((H, 1, rows), F32),
        pltpu.VMEM((H, HD, rows), F32),
        dma((nk - 1,)),
        dma((nk - 1,)),
        dma((2,)),
    ]


def attention_forward(dims, nk, cid, layer, hidden, small, docs, cos_part, sin_part, qo_all,
                      plan, carry, block):
    width, rows = hidden.shape
    ns, nb, nf = dims
    count = ns * nf
    qkv = qo_all.shape[1] - width
    sds = jax.ShapeDtypeStruct
    outs = [
        sds((width, rows), BF),
        sds((H, HD, rows), BF),
        sds((nk, 2 * KVH, HD, rows), BF),
        sds((H, 1, rows), F32),
        sds((H, HD, rows), BF),
        sds((width, rows), F32),
        sds((width, rows), BF),
    ] + plan.shapes
    if carry == "lanes":
        outs.append(sds((width, count * rows), BF))
    else:
        outs.append(sds((nb, nf, block.shape[2], ns * block.shape[3]), BF))
    out = call(
        functools.partial(attention_forward_kernel, dims, nk, layer, plan, carry),
        "attention_forward",
        cid,
        tuple(outs),
        [VM] * 7 + plan.outs + [VM],
        [VM] * 5 + [AN, VM] + plan.places,
        attention_scratch(dims, nk, width, rows, qkv)
        + plan.scratch
        + gather_sems(dims),
        (hidden, small, docs, cos_part, sin_part, qo_all, block, *plan.arrays),
    )
    return (out[:7], out[7:])


def attention_backward_kernel(dims, *args):
    pc = Place(dims)
    riders = attention_backward_part(pc, lambda: None, None, *args)
    each(riders, "finish")


def attention_backward_part(
    pc, begun, cut_rows, nk, layer, plan, carry, g_ref, small_ref, docs_ref, cos_ref, sin_ref,
    h_ref, normed_ref, q_ref, kv_ref, lse_ref, mixed_ref, qo_all, *refs
):
    n = plan.count
    parts_ref, more_ref, refs = (refs[0], refs[1], refs[2:])
    ins, refs = (refs[:n], refs[n:])
    gh_ref, dqo_ref, dsmall_ref = refs[:3]
    outs, refs = (refs[3 : 3 + n], refs[3 + n :])
    out_ref, refs = (refs[0], refs[1:])
    if carry == "columns":
        rows_ref, refs = (refs[0], refs[1:])
    w, wo, mask, dmix, dkv, delta, dq_some, out_kv, in_kv, gj, ssem, rsem, qsem = refs[:13]
    refs = refs[13:]
    width, rows = h_ref.shape
    qkv = w.shape[1]
    loads = load_qo(qo_all, w, wo, qsem)
    riders, refs = plan.board(pc, ins, outs, refs)
    if carry == "columns":
        held, held_sem = refs[7:]
        coming = pltpu.make_async_copy(parts_ref, held, held_sem)
        coming.start()
    greet(pc, "all" if carry == "columns" else "mates", True)
    if carry == "columns":
        part = lambda q: columns_of(held, q, pc.nf, out_ref.shape[2])
        hand_out = RowSends(pc, 1, rows_ref, refs[4:7])
        coming.wait()
    else:
        part = lambda q: parts_ref.at[q]
    scatter = ReadyScatter(pc, part, *refs[:4])
    scatter.start()
    each(riders, "start")
    begun()

    def put(c0, c1, value):
        if cut_rows is None:
            dqo_ref[:, c0:c1] = value.astype(BF)
        else:
            for t in range(pc.nb):
                for f in range(pc.nf):
                    r = (t * pc.nf + f) * cut_rows
                    dqo_ref[t, f, :, c0:c1] = value[r : r + cut_rows].astype(BF)

    g1 = column(padded_t(small_ref[layer]), 0, width // 128)
    fill_masks(pc, mask, docs_ref)
    grl = g_ref[...].astype(BF)
    loads[1].wait()
    dmix[...] = nn(wo[...], grl).astype(BF).reshape(dmix.shape)
    put(qkv, qkv + width, nt(mixed_ref[...].reshape(H * HD, rows), grl))
    scatter.diagonal()
    scatter.early()
    if carry == "columns":
        for f in range(pc.nf):
            hand_out.start(f, more_ref.at[f])
    cos_part = cos_ref[...]
    sin_part = sin_ref[...]
    half = HD // 2
    scale = HD**-0.5
    dkv[...] = jnp.zeros_like(dkv)

    def unturned(d1, d2):
        return (d1 * cos_part + d2 * sin_part, d2 * cos_part - d1 * sin_part)

    def of_block(j, g, head, keys, keys_t, values):
        q = q_ref[head]
        do = dmix[head]
        p = jnp.exp(nn(keys, q) + mask[j] - lse_ref[head])
        ds = (p * (nn(values, do) - delta[head])).astype(BF)
        dkv[j, g] += nt(q, ds)
        dkv[j, KVH + g] += nt(do, p.astype(BF))
        return nn(keys_t, ds)

    for g in range(KVH):
        keys_t = [kv_ref[j, g] for j in range(1, nk)]
        keys = [k.T for k in keys_t]
        values = [kv_ref[j, KVH + g].T for j in range(1, nk)]

        def earlier(i, carried):
            head = g * GROUP + i
            delta[head] = (dmix[head].astype(F32) * mixed_ref[head].astype(F32)).sum(
                axis=0, keepdims=True
            )
            dq = of_block(1, g, head, keys[0], keys_t[0], values[0])
            for j in range(2, nk):
                dq = dq + of_block(j, g, head, keys[j - 1], keys_t[j - 1], values[j - 1])
            dq_some[head] = dq
            return carried

        lax.fori_loop(0, GROUP, earlier, 0, unroll=True)
        if g == 0:
            scatter.late()
        if (g == 1) == (carry == "columns"):
            each(riders, "service")
    for j in range(1, nk):
        out_kv[j - 1] = dkv[j].astype(BF)
    sends = [
        remote(out_kv.at[j - 1], in_kv.at[j - 1], ssem.at[j - 1], rsem.at[j - 1],
               pc.along(pc.nb - j))
        for j in range(1, nk)
    ]
    for c in sends:
        c.start()
    for g in range(KVH):
        keys_t = kv_ref[0, g]
        keys = keys_t.T
        values = kv_ref[0, KVH + g].T

        def own_keys(i, carried):
            head = g * GROUP + i
            dq = (dq_some[head] + of_block(0, g, head, keys, keys_t, values)) * scale
            r1, r2 = unturned(dq[:half], dq[half:])
            gj[pl.ds(pl.multiple_of(head * HD, HD), half), :] = r1.astype(BF)
            gj[pl.ds(pl.multiple_of(head * HD + half, half), half), :] = r2.astype(BF)
            return carried

        lax.fori_loop(0, GROUP, own_keys, 0, unroll=True)
    for c in sends:
        c.wait()
    each(riders, "service")
    own = dkv[0]
    for j in range(1, nk):
        own = own + in_kv[j - 1].astype(F32)
    for g in range(KVH):
        r1, r2 = unturned(own[g, :half], own[g, half:])
        k0 = (H + g) * HD
        gj[k0 : k0 + half, :] = r1.astype(BF)
        gj[k0 + half : k0 + HD, :] = r2.astype(BF)
        v0 = (H + KVH + g) * HD
        gj[v0 : v0 + HD, :] = own[KVH + g].astype(BF)
    gjv = gj[...]
    n1 = width // 128
    dsmall_ref[n1 : n1 + qkv // 128, :] = rows_of(gjv.astype(F32))
    loads[0].wait()
    put(0, qkv, nt(normed_ref[...], gjv))
    gn = nn(w[...], gjv)
    hidden = h_ref[...].astype(BF).astype(F32)
    scale_one = rms(hidden)
    unit = hidden * scale_one
    dsmall_ref[:n1, :] = rows_of(gn * unit)
    u = gn * g1
    gh_ref[...] = g_ref[...] + scale_one * (u - unit * jnp.mean(u * unit, axis=0, keepdims=True))

    def store(total):
        if carry == "columns":
            out_ref[...] = total.astype(BF)
        else:
            out_ref[...] = more_ref[...] + total

    if cut_rows is not None:
        each(riders, "service")
    scatter.finish(store)
    if carry == "columns":
        hand_out.finish(more_ref.at[0])
    return riders


def backward_scratch(nk, width, rows, qkv):
    dma = pltpu.SemaphoreType.DMA
    block = (2 * KVH, HD, rows)
    return [
        pltpu.VMEM((width, qkv), BF),
        pltpu.VMEM((width, width), BF),
        pltpu.VMEM((nk, rows, rows), F32),
        pltpu.VMEM((H, HD, rows), BF),
        pltpu.VMEM((nk,) + block, F32),
        pltpu.VMEM((H, 1, rows), F32),
        pltpu.VMEM((H, HD, rows), F32),
        pltpu.VMEM((nk - 1,) + block, BF),
        pltpu.VMEM((nk - 1,) + block, BF),
        pltpu.VMEM((qkv, rows), BF),
        dma((nk - 1,)),
        dma((nk - 1,)),
        dma((2,)),
    ]


def attention_backward(dims, nk, cid, layer, g, small, docs, cos_part, sin_part, hidden,
                       normed, q, kv, lse, mixed, qo_all, plan, carry, late):
    width, rows = hidden.shape
    qkv = qo_all.shape[1] - width
    sds = jax.ShapeDtypeStruct
    outs = [
        sds((width, rows), F32),
        sds((width, qkv + width), BF),
        sds(((width + qkv) // 128, 128), F32),
    ] + plan.shapes
    dma = pltpu.SemaphoreType.DMA
    if carry == "columns":
        summed = (dims[1], late[0].shape[2], late[0].shape[3] // dims[0])
        outs += [sds(summed, BF), sds((dims[0] * dims[2],) + late[1].shape[1:], BF)]
        places = [VM, AN]
    else:
        summed = (width, rows)
        outs.append(sds(summed, F32))
        places = [VM]
    out = call(
        functools.partial(attention_backward_kernel, dims, nk, layer, plan, carry),
        "attention_backward",
        cid,
        tuple(outs),
        [VM] * 3 + plan.outs + places,
        [VM] * 11 + [AN] + [AN if carry == "columns" else VM, VM] + plan.places,
        backward_scratch(nk, width, rows, qkv)
        + plan.scratch
        + scatter_scratch(dims, *summed)[2:]
        + (
            row_scratch(dims) + [pltpu.VMEM(late[0].shape, BF), dma(())]
            if carry == "columns"
            else []
        ),
        (g, small, docs, cos_part, sin_part, hidden, normed, q, kv, lse, mixed, qo_all,
         *late, *plan.arrays),
    )
    return (out[:3], out[3:])


def sequence_of(pc):
    if pc.two_level:
        return ((0, 1, 2, 3, 6, 7, 4, 5), 5, 7)
    return (tuple(range(pc.count)), pc.count - 1, pc.count - 1)


def lanes(slot, rows):
    return pl.ds(pl.multiple_of(slot * rows, rows), rows)


def transpose_into(dst, src):
    cols = src.shape[1]
    for c0 in range(0, cols, 128):
        c1 = min(c0 + 128, cols)
        dst[c0:c1, :] = src[:, c0:c1].T


def feed_forward_kernel(dims, *args):
    pc = Place(dims)
    feed_forward_part(pc, lambda: greet(pc, "mates", True), lambda: None, *args)


def feed_forward_part(pc, enter, ready, plan, x_ref, res_ref, wgu_ref, wd_ref, *refs):
    n = plan.count
    ins, refs = (refs[:n], refs[n:])
    out_ref, x_out, gu_out = refs[:3]
    outs, refs = (refs[3 : 3 + n], refs[3 + n :])
    x_all, gu_all, lsem, wgu_t, wd_t, gu, inner, near, away, back, hop, ss, sr, gs, gr = refs[:15]
    width, rows = x_ref.shape
    ff = wd_ref.shape[0]
    riders, _ = plan.board(pc, ins, outs, refs[15:])
    enter()
    gather = PlaneGather(pc, lambda q: x_all.at[:, lanes(q, rows)], gs, gr)
    scatter = PlaneScatter(pc, near, away, back, hop, ss, sr)
    x_all[:, lanes(pc.me, rows)] = x_ref[...]
    gather.start()
    ready()
    each(riders, "start")
    transpose_into(wgu_t, wgu_ref)
    transpose_into(wd_t, wd_ref)
    sequence, diagonal_at, early_at = sequence_of(pc)
    chunk = 32 if ff % 32 == 0 else 16

    def step_body(turn, carry):
        step = pick(turn, sequence)

        for k in range(pc.count):
            @pl.when(step == k)
            def _():
                gather.before(k)

        slot = pick(step, gather.order)
        sl = lanes(slot, rows)
        gu[...] = nn(wgu_t[...], x_all[:, sl])

        def act(i, c):
            r = pl.multiple_of(i * chunk, chunk)
            gate = gu[pl.ds(r, chunk), :]
            up = gu[pl.ds(ff + r, chunk), :]
            gu_all[pl.ds(r, chunk), sl] = gate.astype(BF)
            gu_all[pl.ds(ff + r, chunk), sl] = up.astype(BF)
            inner[pl.ds(r, chunk), :] = (gate * jax.nn.sigmoid(gate) * up).astype(BF)
            return c

        lax.fori_loop(0, ff // chunk, act, 0, unroll=True)
        scatter.put(step, nn(wd_t[...], inner[...]))

        @pl.when(turn == 3)
        def _():
            each(riders, "service")

        @pl.when(turn == diagonal_at)
        def _():
            scatter.diagonal()

        @pl.when(turn == early_at)
        def _():
            scatter.early()

        return carry

    lax.fori_loop(0, pc.count, step_body, 0)
    leaving = [
        pltpu.make_async_copy(gu_all, gu_out, lsem.at[0]),
        pltpu.make_async_copy(x_all, x_out, lsem.at[1]),
    ]
    each(leaving, "start")
    each(riders, "service")

    def store(total):
        out_ref[...] = res_ref[...] + total

    scatter.result(store)
    gather.finish()
    each(leaving, "wait")
    each(riders, "finish")


def feed_forward(dims, cid, x, residual, wgu, wd, plan):
    width, rows = x.shape
    count = dims[0] * dims[2]
    two_ff, ff = (wgu.shape[1], wd.shape[0])
    sds = jax.ShapeDtypeStruct
    dma = pltpu.SemaphoreType.DMA
    out = call(
        functools.partial(feed_forward_kernel, dims, plan),
        "feed_forward",
        cid,
        (
            sds((width, rows), F32),
            sds((width, count * rows), BF),
            sds((two_ff, count * rows), BF),
            *plan.shapes,
        ),
        [VM, AN, AN] + plan.outs,
        [VM] * 4 + plan.places,
        [
            pltpu.VMEM((width, count * rows), BF),
            pltpu.VMEM((two_ff, count * rows), BF),
            dma((2,)),
            pltpu.VMEM((two_ff, width), BF),
            pltpu.VMEM((width, ff), BF),
            pltpu.VMEM((two_ff, rows), F32),
            pltpu.VMEM((ff, rows), BF),
        ]
        + scatter_scratch(dims, width, rows)
        + gather_sems(dims)
        + plan.scratch,
        (x, residual, wgu, wd, *plan.arrays),
    )
    return (out[:3], out[3:])


def feed_backward_kernel(
    dims, layer, plan, g_ref, res_ref, x_in, gu_in, wgu_ref, wd_ref, small_ref, *refs
):
    n = plan.count
    ins, refs = (refs[:n], refs[n:])
    gr_ref, dwgu_ref, dwd_ref, dsmall_ref = refs[:4]
    outs, refs = (refs[4 : 4 + n], refs[4 + n :])
    x_all, gu_all, lsem, g_all, inner, ggu, gi, near, away, back, hop, ss, sr, gs, gr = refs[:15]
    coming = [
        pltpu.make_async_copy(gu_in, gu_all, lsem.at[0]),
        pltpu.make_async_copy(x_in, x_all, lsem.at[1]),
    ]
    each(coming, "start")
    pc = Place(dims)
    width, rows = g_ref.shape
    ff = wd_ref.shape[0]
    riders, _ = plan.board(pc, ins, outs, refs[15:])
    greet(pc, "mates", n > 0)
    gather = PlaneGather(pc, lambda q: g_all.at[:, lanes(q, rows)], gs, gr)
    scatter = PlaneScatter(pc, near, away, back, hop, ss, sr)
    g_all[:, lanes(pc.me, rows)] = g_ref[...].astype(BF)
    gather.start()
    each(riders, "start")
    coming[0].wait()
    sequence, diagonal_at, early_at = sequence_of(pc)
    chunk = 32 if ff % 32 == 0 else 16

    def step_body(turn, carry):
        step = pick(turn, sequence)

        for k in range(pc.count):
            @pl.when(step == k)
            def _():
                gather.before(k)

        slot = pick(step, gather.order)
        sl = lanes(slot, rows)
        gi[...] = nn(wd_ref[...], g_all[:, sl])

        def act(i, c):
            r = pl.multiple_of(i * chunk, chunk)
            gate = gu_all[pl.ds(r, chunk), sl].astype(F32)
            up = gu_all[pl.ds(ff + r, chunk), sl].astype(F32)
            grad = gi[pl.ds(r, chunk), :]
            sig = jax.nn.sigmoid(gate)
            silu = gate * sig
            inner[pl.ds(r, chunk), sl] = (silu * up).astype(BF)
            ggu[pl.ds(r, chunk), sl] = (grad * up * sig * (1.0 + gate * (1.0 - sig))).astype(BF)
            ggu[pl.ds(ff + r, chunk), sl] = (grad * silu).astype(BF)
            return c

        lax.fori_loop(0, ff // chunk, act, 0, unroll=True)
        scatter.put(step, nn(wgu_ref[...], ggu[:, sl]))

        @pl.when(turn == 3)
        def _():
            each(riders, "service")

        @pl.when(turn == diagonal_at)
        def _():
            scatter.diagonal()

        @pl.when(turn == early_at)
        def _():
            scatter.early()

        return carry

    lax.fori_loop(0, pc.count, step_body, 0)
    each(riders, "service")
    dwd_ref[...] = nt(inner[...], g_all[...]).astype(BF)
    scatter.late()
    coming[1].wait()
    part = width // 2
    for r in range(2):
        dwgu_ref[r * part : (r + 1) * part, :] = nt(
            x_all[r * part : (r + 1) * part, :], ggu[...]
        ).astype(BF)

    def store(total):
        residual = res_ref[...]
        scale_two = rms(residual)
        unit = residual * scale_two
        n1 = width // 128
        dsmall_ref[...] = rows_of(total * unit)
        u = total * column(padded_t(small_ref[layer]), n1, n1)
        gr_ref[...] = g_ref[...].astype(BF).astype(F32) + scale_two * (
            u - unit * jnp.mean(u * unit, axis=0, keepdims=True)
        )

    scatter.finish(store)
    gather.finish()
    each(riders, "finish")


def feed_backward(dims, cid, layer, g, residual, x_all, gu_all, wgu, wd, small, plan):
    width, rows = g.shape
    count = dims[0] * dims[2]
    two_ff, ff = (wgu.shape[1], wd.shape[0])
    sds = jax.ShapeDtypeStruct
    dma = pltpu.SemaphoreType.DMA
    out = call(
        functools.partial(feed_backward_kernel, dims, layer, plan),
        "feed_backward",
        cid,
        (
            sds((width, rows), F32),
            sds(wgu.shape, BF),
            sds(wd.shape, BF),
            sds((width // 128, 128), F32),
            *plan.shapes,
        ),
        [VM] * 4 + plan.outs,
        [VM, VM, AN, AN, VM, VM, VM] + plan.places,
        [
            pltpu.VMEM((width, count * rows), BF),
            pltpu.VMEM((two_ff, count * rows), BF),
            dma((2,)),
            pltpu.VMEM((width, count * rows), BF),
            pltpu.VMEM((ff, count * rows), BF),
            pltpu.VMEM((two_ff, count * rows), BF),
            pltpu.VMEM((ff, rows), F32),
        ]
        + scatter_scratch(dims, width, rows)
        + gather_sems(dims)
        + plan.scratch,
        (g, residual, x_all, gu_all, wgu, wd, small, *plan.arrays),
    )
    return (out[:4], out[4:])


def feed_both_kernel(dims, *args):
    pc = Place(dims)
    feed_both_part(pc, lambda: greet(pc, "mates", False), lambda: None, *args)


def feed_both_part(
    pc, enter, ready, layer, x_ref, res_ref, g_ref, g_all, wgu_ref, wd_ref, small_ref,
    gr_ref, dwgu_ref, dwd_ref, dsmall_ref, parts_ref,
    x_all, inner, ggu, wgu_t, wd_t, gu, gi, near, away, back, hop, ss, sr, gs, gr,
):
    width, rows = g_ref.shape
    ff = wd_ref.shape[0]
    enter()
    gather = PlaneGather(pc, lambda q: x_all.at[:, lanes(q, rows)], gs, gr)
    scatter = PlaneScatter(pc, near, away, back, hop, ss, sr)
    x_all[:, lanes(pc.me, rows)] = x_ref[...]
    gather.start()
    ready()
    transpose_into(wgu_t, wgu_ref)
    transpose_into(wd_t, wd_ref)
    sequence, diagonal_at, early_at = sequence_of(pc)
    chunk = 32 if ff % 32 == 0 else 16

    def step_body(turn, carry):
        step = pick(turn, sequence)

        for k in range(pc.count):
            @pl.when(step == k)
            def _():
                gather.before(k)

        slot = pick(step, gather.order)
        sl = lanes(slot, rows)
        gu[...] = nn(wgu_t[...], x_all[:, sl])
        gi[...] = nn(wd_ref[...], g_all[:, sl])

        def act(i, c):
            r = pl.multiple_of(i * chunk, chunk)
            gate = gu[pl.ds(r, chunk), :]
            up = gu[pl.ds(ff + r, chunk), :]
            grad = gi[pl.ds(r, chunk), :]
            sig = jax.nn.sigmoid(gate)
            silu = gate * sig
            inner[pl.ds(r, chunk), sl] = (silu * up).astype(BF)
            ggu[pl.ds(r, chunk), sl] = (grad * up * sig * (1.0 + gate * (1.0 - sig))).astype(BF)
            ggu[pl.ds(ff + r, chunk), sl] = (grad * silu).astype(BF)
            return c

        lax.fori_loop(0, ff // chunk, act, 0, unroll=True)
        scatter.put(step, nn(wgu_ref[...], ggu[:, sl]))

        @pl.when(turn == diagonal_at)
        def _():
            scatter.diagonal()

        @pl.when(turn == early_at)
        def _():
            scatter.early()

        parts_ref[slot] = nn(wd_t[...], inner[:, sl]).astype(BF)
        return carry

    lax.fori_loop(0, pc.count, step_body, 0)
    dwd_ref[...] = nt(inner[...], g_all[...]).astype(BF)
    scatter.late()
    part = width // 2
    for r in range(2):
        dwgu_ref[r * part : (r + 1) * part, :] = nt(
            x_all[r * part : (r + 1) * part, :], ggu[...]
        ).astype(BF)

    def store(total):
        residual = res_ref[...]
        scale_two = rms(residual)
        unit = residual * scale_two
        n1 = width // 128
        dsmall_ref[...] = rows_of(total * unit)
        u = total * column(padded_t(small_ref[layer]), n1, n1)
        gr_ref[...] = g_ref[...].astype(BF).astype(F32) + scale_two * (
            u - unit * jnp.mean(u * unit, axis=0, keepdims=True)
        )

    scatter.finish(store)
    gather.finish()


def feed_both(dims, cid, layer, x, residual, g, g_all, wgu, wd, small):
    width, rows = g.shape
    count = dims[0] * dims[2]
    two_ff, ff = (wgu.shape[1], wd.shape[0])
    sds = jax.ShapeDtypeStruct
    dma = pltpu.SemaphoreType.DMA
    return call(
        functools.partial(feed_both_kernel, dims, layer),
        "feed_both",
        cid,
        (
            sds((width, rows), F32),
            sds(wgu.shape, BF),
            sds(wd.shape, BF),
            sds((width // 128, 128), F32),
            sds((count, width, rows), BF),
        ),
        [VM] * 5,
        [VM] * 7,
        [
            pltpu.VMEM((width, count * rows), BF),
            pltpu.VMEM((ff, count * rows), BF),
            pltpu.VMEM((two_ff, count * rows), BF),
            pltpu.VMEM((two_ff, width), BF),
            pltpu.VMEM((width, ff), BF),
            pltpu.VMEM((two_ff, rows), F32),
            pltpu.VMEM((ff, rows), F32),
        ]
        + scatter_scratch(dims, width, rows)
        + gather_sems(dims),
        (x, residual, g, g_all, wgu, wd, small),
    )


def wait_for_weights(pc, riders, gather, wd_all, pieces, wd, sem, others):
    last_blocks(pc, gather)
    each(riders, "finish")
    load = pltpu.make_async_copy(wd_all, pieces, sem)
    load.start()
    each(others, "wait")
    load.wait()
    half = pieces.shape[1]
    for t in range(pc.nb):
        wd[t * half : (t + 1) * half, :] = pieces[t]
    gather.finish()


def lower_kernel(dims, nk, plan_a, plan_f, *refs):
    pc = Place(dims)
    a_in, wgu_in, refs = (refs[:8], refs[8], refs[9:])
    f_in, refs = (refs[: plan_f.count], refs[plan_f.count :])
    a_out, wd_all, qo_next, refs = (refs[:6], refs[6], refs[7], refs[8:])
    f_out, refs = (refs[: 3 + plan_f.count], refs[3 + plan_f.count :])
    n2, wgu, pieces, wd, wsem, dsem, refs = (*refs[:6], refs[6:])
    a_scratch, f_scratch = (refs[: 10 + len(plan_a.scratch) + 2], refs[10 + len(plan_a.scratch) + 2 :])
    load = pltpu.make_async_copy(wgu_in, wgu, wsem)
    load.start()
    riders, gather = attention_forward_part(
        pc, nk, 0, plan_a, "columns", *a_in, *a_out, n2, wd_all, qo_next, *a_scratch
    )
    feed_forward_part(
        pc,
        lambda: None,
        lambda: wait_for_weights(pc, riders, gather, wd_all, pieces, wd, dsem, [load]),
        plan_f, n2, a_out[5], wgu, wd, *f_in, *f_out, *f_scratch,
    )


def lower_layer(dims, nk, cid, hidden, small, docs, cos_part, sin_part, qo, plan_a, block,
                wgu, plan_f):
    ns, nb, nf = dims
    width, rows = hidden.shape
    count = ns * nf
    qkv = qo.shape[1] - width
    two_ff = wgu.shape[1]
    ff = two_ff // 2
    sds = jax.ShapeDtypeStruct
    dma = pltpu.SemaphoreType.DMA
    outs = [
        sds((width, rows), BF),
        sds((H, HD, rows), BF),
        sds((nk, 2 * KVH, HD, rows), BF),
        sds((H, 1, rows), F32),
        sds((H, HD, rows), BF),
        sds((width, rows), F32),
        *plan_a.shapes,
        sds((nb, nf, block.shape[2], ns * block.shape[3]), BF),
        sds((width, rows), F32),
        sds((width, count * rows), BF),
        sds((two_ff, count * rows), BF),
        *plan_f.shapes,
    ]
    out = call(
        functools.partial(lower_kernel, dims, nk, plan_a, plan_f),
        "lower_layer",
        cid,
        tuple(outs),
        [VM] * 6 + plan_a.outs + [VM] + [VM, AN, AN] + plan_f.outs,
        [VM] * 5 + [AN, VM] + plan_a.places + [AN] + plan_f.places,
        [
            pltpu.VMEM((width, rows), BF),
            pltpu.VMEM(wgu.shape, BF),
            pltpu.VMEM((nb, ff // nb, width), BF),
            pltpu.VMEM((ff, width), BF),
            dma(()),
            dma(()),
        ]
        + attention_scratch(dims, nk, width, rows, qkv)
        + plan_a.scratch
        + gather_sems(dims)
        + [
            pltpu.VMEM((width, count * rows), BF),
            pltpu.VMEM((two_ff, count * rows), BF),
            dma((2,)),
            pltpu.VMEM((two_ff, width), BF),
            pltpu.VMEM((width, ff), BF),
            pltpu.VMEM((two_ff, rows), F32),
            pltpu.VMEM((ff, rows), BF),
        ]
        + scatter_scratch(dims, width, rows)
        + gather_sems(dims)
        + plan_f.scratch,
        (hidden, small, docs, cos_part, sin_part, qo, block, *plan_a.arrays, wgu,
         *plan_f.arrays),
    )
    return (out[:6], out[6], out[7], out[8:11], out[11:])


def upper_kernel(dims, nk, plan, *refs):
    pc = Place(dims)
    a_in, g_ref, wgu_in, refs = (refs[:8], refs[8], refs[9], refs[10:])
    a_out, wd_all, f_out, refs = (refs[:6], refs[6], refs[7:12], refs[12:])
    n2, g_all, wgu, pieces, wd, wsem, dsem, refs = (*refs[:7], refs[7:])
    a_scratch, f_scratch = (refs[: 10 + len(plan.scratch) + 2], refs[10 + len(plan.scratch) + 2 :])
    load = pltpu.make_async_copy(wgu_in, wgu, wsem)
    load.start()
    riders, gather = attention_forward_part(
        pc, nk, 1, plan, "lanes", *a_in, *a_out, n2, wd_all, g_all, *a_scratch
    )
    feed_both_part(
        pc,
        lambda: None,
        lambda: wait_for_weights(pc, riders, gather, wd_all, pieces, wd, dsem, [load]),
        1, n2, a_out[5], g_ref, g_all, wgu, wd, a_in[1], *f_out, *f_scratch,
    )


def upper_layer(dims, nk, cid, hidden, small, docs, cos_part, sin_part, qo, plan, block, g,
                wgu):
    ns, nb, nf = dims
    width, rows = hidden.shape
    count = ns * nf
    qkv = qo.shape[1] - width
    two_ff = wgu.shape[1]
    ff = two_ff // 2
    sds = jax.ShapeDtypeStruct
    dma = pltpu.SemaphoreType.DMA
    outs = [
        sds((width, rows), BF),
        sds((H, HD, rows), BF),
        sds((nk, 2 * KVH, HD, rows), BF),
        sds((H, 1, rows), F32),
        sds((H, HD, rows), BF),
        sds((width, rows), F32),
        *plan.shapes,
        sds((width, rows), F32),
        sds(wgu.shape, BF),
        sds((ff, width), BF),
        sds((width // 128, 128), F32),
        sds((count, width, rows), BF),
    ]
    out = call(
        functools.partial(upper_kernel, dims, nk, plan),
        "upper_layer",
        cid,
        tuple(outs),
        [VM] * 6 + plan.outs + [VM] * 5,
        [VM] * 5 + [AN, VM] + plan.places + [VM, AN],
        [
            pltpu.VMEM((width, rows), BF),
            pltpu.VMEM((width, count * rows), BF),
            pltpu.VMEM(wgu.shape, BF),
            pltpu.VMEM((nb, ff // nb, width), BF),
            pltpu.VMEM((ff, width), BF),
            dma(()),
            dma(()),
        ]
        + attention_scratch(dims, nk, width, rows, qkv)
        + plan.scratch
        + gather_sems(dims)
        + [
            pltpu.VMEM((width, count * rows), BF),
            pltpu.VMEM((ff, count * rows), BF),
            pltpu.VMEM((two_ff, count * rows), BF),
            pltpu.VMEM((two_ff, width), BF),
            pltpu.VMEM((width, ff), BF),
            pltpu.VMEM((two_ff, rows), F32),
            pltpu.VMEM((ff, rows), F32),
        ]
        + scatter_scratch(dims, width, rows)
        + gather_sems(dims),
        (hidden, small, docs, cos_part, sin_part, qo, block, *plan.arrays, g, wgu),
    )
    return (out[:6], out[7:])


def reduce_kernel(
    dims, qo, terms, sa0, sa1, sb0, sb1, wd1, gu0a, gu0, wd0,
    qo_out, small_out, gu_got, wd_got,
    held, rest_gu, gsum, wsum, small, sm_in, sm_mid, sm_line, z_out, mine, give,
    lsem, ws, wr, ls, lr, zs, zr, *rest
):
    pc = Place(dims)
    ns, nb, nf = dims
    coming = pltpu.make_async_copy(qo, held, lsem.at[1])
    coming.start()
    cut = gu0a.shape[0]
    coming_gu = pltpu.make_async_copy(gu0.at[:, cut:nf], rest_gu, lsem.at[2])
    coming_gu.start()
    n1 = sb0.shape[0]
    per = small.shape[0] // ns
    nr = sa0.shape[0] + n1
    small[...] = jnp.zeros_like(small)
    for l, (a, g) in enumerate(((sa0, sb0), (sa1, sb1))):
        small[l * per : l * per + n1] = a[0:n1]
        small[l * per + n1 : l * per + 2 * n1] = g[...]
        small[l * per + 2 * n1 : l * per + nr] = a[n1 : a.shape[0]]
    greet(pc, "all", True)

    def keep(value):
        wsum[...] = value.astype(BF)

    def keep_of(l):
        def store(value):
            mine[l] = value

        return store

    line = LineReduce(pc, lambda t: wd0[t], keep, rest[0:4])
    ends = [
        LineReduce(pc, lambda t: z_out[t], keep_of(0), rest[4:8]),
        LineReduce(pc, lambda t: terms[t], keep_of(1), rest[8:12]),
    ]
    def keep_gu(value):
        gsum[...] = value.astype(BF)

    line_gu = LineReduce(pc, lambda t: rest_gu[t], keep_gu, rest[19:23])
    ends[1].start()
    coming_gu.wait()
    line_gu.start()
    line.start()
    scatter = ReadyScatter(
        pc, lambda q: columns_of(held, q, nf, z_out.shape[2]), *rest[15:19]
    )
    coming.wait()
    scatter.start()
    smalls = [
        remote(small, sm_in.at[e - 1], ls.at[e - 1], lr.at[e - 1], pc.plane(e))
        for e in range(1, pc.count)
    ]
    for c in smalls:
        c.start()
    scatter.diagonal()
    scatter.early()
    hand_out = RowSends(pc, 0, gu_got, rest[12:15])
    for f in range(cut):
        hand_out.start(f, gu0a.at[f])

    def split(l, ref):
        @pl.when(pc.s == l)
        def _():
            pltpu.make_async_copy(ref, wd_got.at[l], lsem.at[0]).start()

        @pl.when(pc.s != l)
        def _():
            remote(ref, wd_got.at[pc.s], ws.at[0], wr.at[0], (l, pc.b, pc.f)).start()

    split(1, wd1)
    ends[1].service()
    line_gu.service()
    line.service()
    scatter.late()
    ends[1].service()
    total = small[...]
    for e, c in enumerate(smalls):
        c.wait()
        total = total + sm_in[e]
    sm_mid[...] = total
    lines = [
        remote(sm_mid, sm_line.at[d - 1], zs.at[d - 1], zr.at[d - 1], pc.along(d))
        for d in range(1, nb)
    ]
    for c in lines:
        c.start()
    line_gu.service()
    line.service()

    def store(value):
        z_out[...] = value.astype(BF)

    scatter.finish(store)
    ends[0].start()
    ends[1].finish()
    line_gu.finish()
    for f in range(cut, nf):
        hand_out.start(f, gsum.at[f - cut])
    ends[0].service()
    line.finish()
    split(0, wsum)
    ends[0].finish()
    mate = (ns - 1 - pc.s, pc.b, pc.f)
    swap = remote(give.at[0], give.at[1], ws.at[1], wr.at[1], mate)
    give[0] = mine[ns - 1 - pc.s].astype(BF)
    swap.start()
    qo_out[pc.s] = mine[pc.s]
    total = sm_mid[...]
    for d, c in enumerate(lines):
        c.wait()
        total = total + sm_line[d]
    small_out[...] = total
    hand_out.finish(gu0a.at[0])
    pltpu.make_async_copy(wsum, wd_got.at[pc.s], lsem.at[0]).wait()
    remote(wsum, wd_got.at[pc.s], ws.at[0], wr.at[0], mate).wait()
    swap.wait()
    qo_out[ns - 1 - pc.s] = give[1].astype(F32)


def reduce_gradients(dims, cid, qo, terms, smalls, wd1, gu0a, gu0, wd0):
    ns, nb, nf = dims
    count = ns * nf
    dr, wide = terms.shape[1:]
    two_ff = gu0.shape[3]
    cut = gu0a.shape[0]
    half, width = wd1.shape
    rows = smalls[0].shape[0] + smalls[2].shape[0]
    small = (ns * (-(-rows // 8) * 8), 128)
    sds = jax.ShapeDtypeStruct
    dma = pltpu.SemaphoreType.DMA
    return call(
        functools.partial(reduce_kernel, dims),
        "reduce_gradients",
        cid,
        (
            sds((ns, dr, wide), F32),
            sds(small, F32),
            sds((count, dr, two_ff), BF),
            sds((ns, half, width), BF),
        ),
        [VM] * 4,
        [AN] + [VM] * 7 + [AN, VM],
        [
            pltpu.VMEM(qo.shape, BF),
            pltpu.VMEM((nb, nf - cut, dr, two_ff), BF),
            pltpu.VMEM((nf - cut, dr, two_ff), BF),
            pltpu.VMEM((half, width), BF),
            pltpu.VMEM(small, F32),
            pltpu.VMEM((count - 1,) + small, F32),
            pltpu.VMEM(small, F32),
            pltpu.VMEM((nb - 1,) + small, F32),
            pltpu.VMEM((nb, dr, wide), BF),
            pltpu.VMEM((ns, dr, wide), F32),
            pltpu.VMEM((2, dr, wide), BF),
            dma((3,)),
            dma((2,)),
            dma((2,)),
            dma((count - 1,)),
            dma((count - 1,)),
            dma((nb - 1,)),
            dma((nb - 1,)),
        ]
        + reduce_scratch(dims, half, width)
        + reduce_scratch(dims, dr, wide) * 2
        + row_scratch(dims)
        + scatter_scratch(dims, nb, dr, wide)[2:]
        + reduce_scratch(dims, nf - cut, dr, two_ff),
        (qo, terms, *smalls, wd1, gu0a, gu0, wd0),
    )


def last_kernel(dims, nk, plan, *refs):
    pc = Place(dims)
    ns, nb, nf = dims
    a_in, refs = (refs[:14], refs[14:])
    ab_in, refs = (refs[: plan.count], refs[plan.count :])
    sa1, sb0, sb1, wd1, wd0, give_out, gh1, refs = (*refs[:7], refs[7:])
    gh_ref, gu_got1, qo_out, small_out, gu_got, wd_got, take_out, take_grad = refs[:8]
    refs = refs[8:]
    held, sa0, gu0, terms, refs = (*refs[:4], refs[4:])
    wsum, small, sm_in, sm_mid, sm_line, z_out, mine, give, give_grad = refs[:9]
    lsem, ws, wr, ls, lr, zs, zr, refs = (*refs[9:16], refs[16:])
    n = 13 + len(plan.scratch) + 4 + 3 + 2
    ab_scratch, rest = (refs[:n], refs[n:])
    mate = (ns - 1 - pc.s, pc.b, pc.f)
    outs = remote(give_out, take_out, ws.at[2], wr.at[2], mate)
    grads = remote(give_grad, take_grad, ws.at[3], wr.at[3], mate)
    riders = attention_backward_part(
        pc, outs.start, held.shape[2], nk, 0, plan, "columns",
        *a_in, *ab_in, gh_ref, held, sa0, gu0, terms, gu_got1, *ab_scratch,
    )
    line_gu = riders[0]

    def keep(value):
        wsum[...] = value.astype(BF)

    def keep_of(l):
        def store(value):
            mine[l] = value

        return store

    line = LineReduce(pc, lambda t: wd0[t], keep, rest[0:4])
    ends = [
        LineReduce(pc, lambda t: z_out[t], keep_of(0), rest[4:8]),
        LineReduce(pc, lambda t: terms[t], keep_of(1), rest[8:12]),
    ]
    scatter = ReadyScatter(
        pc, lambda q: columns_of(held, q, nf, z_out.shape[2]), *rest[15:19]
    )
    scatter.start()
    ends[1].start()
    n1 = sb0.shape[0]
    per = small.shape[0] // ns
    nr = sa0.shape[0] + n1
    small[...] = jnp.zeros_like(small)
    for l, (a, g) in enumerate(((sa0, sb0), (sa1, sb1))):
        small[l * per : l * per + n1] = a[0:n1]
        small[l * per + n1 : l * per + 2 * n1] = g[...]
        small[l * per + 2 * n1 : l * per + nr] = a[n1 : a.shape[0]]
    smalls = [
        remote(small, sm_in.at[e - 1], ls.at[e - 1], lr.at[e - 1], pc.plane(e))
        for e in range(1, pc.count)
    ]
    for c in smalls:
        c.start()
    scatter.diagonal()
    scatter.early()

    @pl.when(pc.s == 0)
    def _():
        give_grad[...] = gh1[...].astype(BF)

    @pl.when(pc.s != 0)
    def _():
        give_grad[...] = gh_ref[...].astype(BF)

    def split(l, ref):
        @pl.when(pc.s == l)
        def _():
            pltpu.make_async_copy(ref, wd_got.at[l], lsem.at[0]).start()

        @pl.when(pc.s != l)
        def _():
            remote(ref, wd_got.at[pc.s], ws.at[0], wr.at[0], (l, pc.b, pc.f)).start()

    split(1, wd1)
    ends[1].service()
    scatter.late()
    grads.start()
    line.start()
    ends[1].service()
    line_gu.finish()
    hand_out = RowSends(pc, 0, gu_got, rest[12:15])
    for f in range(nf):
        hand_out.start(f, gu0.at[f])
    total = small[...]
    for e, c in enumerate(smalls):
        c.wait()
        total = total + sm_in[e]
    sm_mid[...] = total
    lines = [
        remote(sm_mid, sm_line.at[d - 1], zs.at[d - 1], zr.at[d - 1], pc.along(d))
        for d in range(1, nb)
    ]
    for c in lines:
        c.start()

    def store(value):
        z_out[...] = value.astype(BF)

    scatter.finish(store)
    ends[0].start()
    ends[1].finish()
    line.service()
    ends[0].service()
    ends[0].service()
    line.service()
    ends[0].finish()
    swap = remote(give.at[0], give.at[1], ws.at[1], wr.at[1], mate)
    give[0] = mine[ns - 1 - pc.s].astype(BF)
    swap.start()
    qo_out[pc.s] = mine[pc.s]
    total = sm_mid[...]
    for d, c in enumerate(lines):
        c.wait()
        total = total + sm_line[d]
    small_out[...] = total
    line.finish()
    split(0, wsum)
    hand_out.finish(gu0.at[0])
    outs.wait()
    grads.wait()
    swap.wait()
    qo_out[ns - 1 - pc.s] = give[1].astype(F32)
    pltpu.make_async_copy(wsum, wd_got.at[pc.s], lsem.at[0]).wait()
    remote(wsum, wd_got.at[pc.s], ws.at[0], wr.at[0], mate).wait()


def last_layer(dims, nk, cid, a_in, late, plan, smalls, wd1, wd0, give_out, gh1):
    ns, nb, nf = dims
    count = ns * nf
    width, rows = gh1.shape
    qkv = a_in[-1].shape[1] - width
    dr, cols = late[0].shape[2:]
    wide = cols // ns
    two_ff = late[1].shape[2]
    half = wd1.shape[0]
    n_small = smalls[0].shape[0] + smalls[1].shape[0]
    small = (ns * (-(-n_small // 8) * 8), 128)
    sds = jax.ShapeDtypeStruct
    dma = pltpu.SemaphoreType.DMA
    rows_all = sds((count, dr, two_ff), BF)
    return call(
        functools.partial(last_kernel, dims, nk, plan),
        "last_layer",
        cid,
        (
            sds((width, rows), F32),
            rows_all,
            sds((ns, dr, wide), F32),
            sds(small, F32),
            rows_all,
            sds((ns, half, width), BF),
            sds((width, rows), BF),
            sds((width, rows), BF),
        ),
        [VM, AN] + [VM] * 6,
        [VM] * 11 + [AN, AN, VM] + plan.places + [VM] * 7,
        [
            pltpu.VMEM(late[0].shape, BF),
            pltpu.VMEM(smalls[0].shape, F32),
            pltpu.VMEM((nf, dr, two_ff), BF),
            pltpu.VMEM((nb, dr, wide), BF),
            pltpu.VMEM((half, width), BF),
            pltpu.VMEM(small, F32),
            pltpu.VMEM((count - 1,) + small, F32),
            pltpu.VMEM(small, F32),
            pltpu.VMEM((nb - 1,) + small, F32),
            pltpu.VMEM((nb, dr, wide), BF),
            pltpu.VMEM((ns, dr, wide), F32),
            pltpu.VMEM((2, dr, wide), BF),
            pltpu.VMEM((width, rows), BF),
            dma((1,)),
            dma((4,)),
            dma((4,)),
            dma((count - 1,)),
            dma((count - 1,)),
            dma((nb - 1,)),
            dma((nb - 1,)),
        ]
        + backward_scratch(nk, width, rows, qkv)
        + plan.scratch
        + scatter_scratch(dims, nb, dr, wide)[2:]
        + row_scratch(dims)
        + [pltpu.VMEM(late[0].shape, BF), dma(())]
        + reduce_scratch(dims, half, width)
        + reduce_scratch(dims, dr, wide) * 2
        + row_scratch(dims)
        + scatter_scratch(dims, nb, dr, wide)[2:],
        (*a_in, *late, *plan.arrays, *smalls[0:1], *smalls[1:], wd1, wd0, give_out, gh1),
    )


def lay_out_kernel(
    dims, gu0, gu1, wd, qo, small, out0, out1, gh0, gh1, take_out, take_grad,
    block_out, input_grad, g1, wqkv, bqkv, wout, g2, wgu, wdn
):
    ns, nb, nf = dims
    half = wd.shape[1]
    s = lax.axis_index("section")
    qkv = wqkv.shape[2]
    width = wout.shape[2]
    full = jnp.concatenate([qo[y] for y in range(ns)], axis=1)
    wqkv[0] = full[:, :qkv]
    wout[0] = full[:, qkv:]
    for y in range(ns):
        wdn[0, y * half : (y + 1) * half, :] = wd[y].astype(F32)
    for l, gu in enumerate((gu0, gu1)):
        @pl.when(s == l)
        def _():
            for y in range(ns):
                for f in range(nf):
                    got = gu[y * nf + f].astype(F32)
                    for part in range(2):
                        for b in range(nb):
                            c0 = column_start(dims, part, b, f, y, half)
                            k0 = (part * nb + b) * half
                            wgu[0, :, c0 : c0 + half] = got[:, k0 : k0 + half]
    n1 = width // 128
    per = small.shape[0] // ns
    rows = small[pl.ds(pl.multiple_of(s * per, 8), per), :]
    for k in range(n1):
        g1[0:1, k * 128 : (k + 1) * 128] = rows[k : k + 1]
        g2[0:1, k * 128 : (k + 1) * 128] = rows[n1 + k : n1 + k + 1]
    for k in range(qkv // 128):
        bqkv[0:1, k * 128 : (k + 1) * 128] = rows[2 * n1 + k : 2 * n1 + k + 1]
    for out, pair, take in (
        (block_out, (out0, out1), take_out),
        (input_grad, (gh0, gh1), take_grad),
    ):
        for l in range(ns):
            @pl.when(s == l)
            def _():
                out[0, l] = pair[l][...].T
                out[0, 1 - l] = take[...].T.astype(F32)


def lay_out(dims, qkv, args):
    ns, nb, nf = dims
    gu, wd, qo = (args[0], args[2], args[3])
    width, rows = args[5].shape
    dr = qo.shape[1]
    sds = jax.ShapeDtypeStruct
    tokens = sds((1, ns, rows, width), F32)
    return pl.pallas_call(
        functools.partial(lay_out_kernel, dims),
        name="lay_out",
        out_shape=(
            tokens,
            tokens,
            sds((1, width), F32),
            sds((1, dr, qkv), F32),
            sds((1, qkv), F32),
            sds((1, dr, width), F32),
            sds((1, width), F32),
            sds((1, dr, gu.shape[0] * gu.shape[2]), F32),
            sds((1, ns * wd.shape[1], width), F32),
        ),
        in_specs=[VM] * len(args),
        out_specs=[VM] * 9,
        compiler_params=pltpu.CompilerParams(vmem_limit_bytes=VMEM_LIMIT),
    )(*args)


def shards(
    dims,
    tokens_in,
    positions,
    doc_ids,
    out_grad,
    norm1_gain,
    w_qkv,
    b_qkv,
    w_out,
    norm2_gain,
    w_gate_up,
    w_down,
):
    ns, nb, nf = dims
    seqs, rows, width = tokens_in.shape
    s = lax.axis_index("section")
    dr = w_qkv.shape[1]
    qkv = w_qkv.shape[2]
    fr = w_down.shape[1]
    half = fr // ns
    ff = nb * half
    nk = min(nb, 1 + (LONGEST - 1 + rows - 1) // rows)

    tokens = lax.dynamic_index_in_dim(tokens_in, s, 0, keepdims=False)
    cot = lax.dynamic_index_in_dim(out_grad, s, 0, keepdims=False)
    pos = lax.dynamic_index_in_dim(positions, s, 0, keepdims=False)
    freq = jnp.exp(jnp.arange(HD // 2, dtype=F32) * (-2.0 / HD) * math.log(1000000.0))
    phase = freq[:, None] * pos.astype(F32)[None, :]
    cos_part, sin_part = (jnp.cos(phase), jnp.sin(phase))
    hidden = tokens.T.astype(F32)
    g = cot.T.astype(F32)

    wd = w_down[0].reshape(ns, half, width)
    gup, wdp, gu_first, qo_first, qz, small_all = gather_weights(
        dims, w_gate_up, w_qkv, w_out, wd, (norm1_gain, norm2_gain, b_qkv)
    )
    cols = qkv + width
    wide = (width, 2 * ff)

    def ride(*pairs):
        return Riders(dims, tuple(a for a, _ in pairs), tuple(v for _, v in pairs))

    common = (small_all, doc_ids, cos_part, sin_part)
    qo0 = qo_first.reshape(width, cols)
    wgu0 = gu_first.reshape(wide)
    first = ride((("gather", 0), wdp))
    second = ride((("gather", 1), gup))
    third = ride((("gather", 1), wdp))
    together = half % 8 == 0
    if together:
        a0, wd0, qo1, f0, (gu1,) = lower_layer(
            dims, nk, 1, hidden, *common, qo0, first, qz, wgu0, second
        )
    else:
        a0, (wd0, qo1) = attention_forward(
            dims, nk, 1, 0, hidden, *common, qo0, first, "columns", qz
        )
        f0, (gu1,) = feed_forward(dims, 3, a0[6], a0[5], wgu0, wd0.reshape(ff, width), second)
    qo1 = qo1.reshape(width, cols)
    wd0 = wd0.reshape(ff, width)
    wgu1 = gu1.reshape(wide)
    if together:
        a1, b1 = upper_layer(dims, nk, 2, f0[0], *common, qo1, third, cot.T, g, wgu1)
    else:
        a1, (wd1, g_all) = attention_forward(
            dims, nk, 2, 1, f0[0], *common, qo1, third, "lanes", cot.T
        )
        wd1 = wd1.reshape(ff, width)
        b1 = feed_both(dims, 4, 1, a1[6], a1[5], g, g_all, wgu1, wd1, small_all)

    line_gu = (nb, nf, dr, 2 * ff)
    line_wd = (nb, half, width)
    line_qo = (nb, nf, dr, cols)
    everything = (0, half)
    ab1, (dwd1, out1) = attention_backward(
        dims, nk, 7, 1, b1[0], *common, f0[0], *a1[:5], qo1,
        ride((("reduce", everything), b1[2].reshape(line_wd))), "sum", (b1[4], a1[5]),
    )
    b0, (dgu1,) = feed_backward(
        dims, 6, 0, ab1[0], a0[5], f0[1], f0[2], wgu0, wd0, small_all,
        ride((("reduce", (0, nf)), b1[1].reshape(line_gu))),
    )
    dgu0 = b0[1].reshape(line_gu)
    swaps = [(0, 1), (1, 0)]
    give_out = jnp.where(s == 0, out1, f0[0]).astype(BF)
    if together and dr % 8 == 0:
        gh0, gu_got1, grad_qo, small_sum, gu_got0, wd_got, take_out, take_grad = last_layer(
            dims, nk, 8, (b0[0], *common, hidden, *a0[:5], qo0),
            (ab1[1].reshape(line_qo), dgu1), ride((("reduce", (0, nf)), dgu0)),
            (ab1[2], b0[3], b1[3]), dwd1, b0[2].reshape(line_wd), give_out, ab1[0],
        )
    else:
        cut = nf - nf // 4
        ab0, (dgu0a, terms, gu_got1) = attention_backward(
            dims, nk, 8, 0, b0[0], *common, hidden, *a0[:5], qo0,
            ride((("reduce", (0, cut)), dgu0)), "columns", (ab1[1].reshape(line_qo), dgu1),
        )
        gh0 = ab0[0]
        take_out = lax.ppermute(give_out, "section", swaps)
        take_grad = lax.ppermute(jnp.where(s == 0, ab1[0], gh0).astype(BF), "section", swaps)
        grad_qo, small_sum, gu_got0, wd_got = reduce_gradients(
            dims, 9, ab0[1].reshape(line_qo), terms,
            (ab0[2], ab1[2], b0[3], b1[3]), dwd1, dgu0a, dgu0, b0[2].reshape(line_wd),
        )
    return lay_out(
        dims,
        qkv,
        (gu_got0, gu_got1, wd_got, grad_qo, small_sum, f0[0], out1, gh0, ab1[0], take_out,
         take_grad),
    )


def solution(mesh):
    dims = (mesh.shape["section"], mesh.shape["blk"], mesh.shape["fsdp"])
    return jax.shard_map(
        functools.partial(shards, dims),
        mesh=mesh,
        in_specs=(
            P("fsdp", "blk", None),
            P("fsdp", "blk"),
            P("fsdp", None),
            P("fsdp", "blk", None),
            P("section", None),
            P("section", ("blk", "fsdp"), None),
            P("section", None),
            P("section", ("blk", "fsdp"), None),
            P("section", None),
            P("section", ("blk", "fsdp"), None),
            P("section", ("blk", "fsdp"), None),
        ),
        out_specs=(
            P("section", "fsdp", "blk", None),
            P("section", "fsdp", "blk", None),
            P("section", None),
            P("section", ("blk", "fsdp"), None),
            P("section", None),
            P("section", ("blk", "fsdp"), None),
            P("section", None),
            P("section", ("blk", "fsdp"), None),
            P("section", ("blk", "fsdp"), None),
        ),
        check_vma=False,
    )
```

```python
import functools
import math

import jax
import jax.numpy as jnp
from jax import lax
from jax.experimental import pallas as pl
from jax.experimental.pallas import tpu as pltpu
from jax.sharding import PartitionSpec as P

H = 14
KVH = 2
HD = 64
GROUP = H // KVH
LONGEST = 512
NEG = -1e30
BF = jnp.bfloat16
F32 = jnp.float32
MESH = pl.DeviceIdType.MESH
VMEM_LIMIT = 60 * 2**20
VM = pl.BlockSpec(memory_space=pltpu.VMEM)
AN = pl.BlockSpec(memory_space=pl.ANY)


def nn(a, b):
    return lax.dot_general(a, b, (((1,), (0,)), ((), ())), preferred_element_type=F32)


def nt(a, b):
    return lax.dot_general(a, b, (((1,), (1,)), ((), ())), preferred_element_type=F32)


def tn(a, b):
    return lax.dot_general(a, b, (((0,), (0,)), ((), ())), preferred_element_type=F32)


def other(f):
    return f + 1 - 2 * (f % 2)


class Place:
    def __init__(self, dims):
        self.ns, self.nb, self.nf = dims
        self.count = self.ns * self.nf
        self.s = lax.axis_index("section")
        self.b = lax.axis_index("blk")
        self.f = lax.axis_index("fsdp")
        self.me = self.s * self.nf + self.f
        self.two_level = self.ns == 2 and self.nf == 4

    def plane(self, e):
        q = (self.me + e) % self.count
        return (q // self.nf, self.b, q % self.nf)

    def slot_from(self, e):
        return (self.me + self.count - e) % self.count

    def along(self, d):
        return (self.s, (self.b + d) % self.nb, self.f)

    def mates(self):
        s, b, f = (self.s, self.b, self.f)
        xf = (f + 2) % 4
        return ((s, b, other(f)), (s, b, xf), (1 - s, b, f))

    def slots(self):
        s, f = (self.s, self.f)
        xf = (f + 2) % 4
        t = 1 - s
        return (
            s * 4 + f,
            s * 4 + other(f),
            s * 4 + xf,
            t * 4 + f,
            s * 4 + other(xf),
            t * 4 + other(f),
            t * 4 + xf,
            t * 4 + other(xf),
        )


def pick(i, values):
    total = 0
    for k, v in enumerate(values):
        total = total + jnp.where(i == k, v, 0)
    return total


def greet(place, plane, along):
    barrier = pltpu.get_barrier_semaphore()
    count = 0
    if plane:
        if place.two_level and plane == "mates":
            targets = list(place.mates())
        else:
            targets = [place.plane(e) for e in range(1, place.count)]
        for t in targets:
            pl.semaphore_signal(barrier, 1, device_id=t, device_id_type=MESH)
        count += len(targets)
    if along:
        for d in range(1, place.nb):
            pl.semaphore_signal(barrier, 1, device_id=place.along(d), device_id_type=MESH)
        count += place.nb - 1
    pl.semaphore_wait(barrier, count)


def remote(src, dst, ssem, rsem, device):
    return pltpu.make_async_remote_copy(
        src_ref=src,
        dst_ref=dst,
        send_sem=ssem,
        recv_sem=rsem,
        device_id=device,
        device_id_type=MESH,
    )


def cut_in(parts, view, c):
    n = view.shape[0] // parts
    return view.at[pl.ds(c * n, n)]


def gather_sems(dims):
    n = 2 * (dims[0] * dims[2] - 1)
    return [pltpu.SemaphoreType.DMA((n,)), pltpu.SemaphoreType.DMA((n,))]


class PlaneGather:
    def __init__(self, place, slot, ssem, rsem):
        self.place, self.slot, self.ssem, self.rsem = (place, slot, ssem, rsem)
        self.parts = 2 if place.two_level else 1
        if place.two_level:
            self.order = place.slots()
        else:
            self.order = tuple(place.slot_from(e) for e in range(place.count))

    def copy(self, k, c, q, device):
        v = cut_in(self.parts, self.slot(q), c)
        i = k * self.parts + c
        return remote(v, v, self.ssem.at[i], self.rsem.at[i], device)

    def start(self):
        pc = self.place
        if pc.two_level:
            core, xm, ym = pc.mates()
            for c in range(2):
                self.copy(1, c, self.order[0], xm).start()
                self.copy(2, c, self.order[0], ym).start()
            for c in range(2):
                self.copy(0, c, self.order[0], core).start()
        else:
            for e in range(1, pc.count):
                self.copy(e - 1, 0, self.order[0], pc.plane(e)).start()

    def came(self, k, c):
        self.copy(k, c, self.order[k + 1], self.place.plane(1)).wait_recv()

    def before(self, step):
        if step == 0:
            return
        pc = self.place
        if not pc.two_level:
            self.came(step - 1, 0)
            return
        core, xm, ym = pc.mates()
        h = pc.f % 2
        if step == 2:
            which = h * self.order[3] + (1 - h) * self.order[2]
            far = (
                h * xm[0] + (1 - h) * ym[0],
                pc.b,
                h * xm[2] + (1 - h) * ym[2],
            )
            for c in range(2):
                self.came(1, c)
                self.came(2, c)
                self.copy(5, c, which, far).start()
                self.copy(3, c, self.order[2], core).start()
                self.copy(4, c, self.order[3], core).start()
        elif step == 3:
            return
        elif step == 6:
            for c in range(2):
                self.came(5, c)
                self.copy(6, c, self.order[6], core).start()
        else:
            for c in range(2):
                self.came(step - 1, c)

    def finish(self):
        n = self.place.count - 1
        for k in range(n):
            for c in range(self.parts):
                self.copy(k, c, self.order[0], self.place.plane(1)).wait_send()


class PlaneScatter:
    def __init__(self, place, near, away, back, hop, ssem, rsem):
        self.place = place
        self.near, self.away, self.back, self.hop = (near, away, back, hop)
        self.ssem, self.rsem = (ssem, rsem)

    def put(self, step, value):
        pc = self.place
        if not pc.two_level:
            @pl.when(step == 0)
            def _():
                self.near[0] = value

            @pl.when(step > 0)
            def _():
                e = pc.count - step
                self.away[e - 1] = value.astype(BF)
                q = (pc.me + e) % pc.count
                remote(
                    self.away.at[e - 1],
                    self.back.at[e - 1],
                    self.ssem.at[e - 1],
                    self.rsem.at[e - 1],
                    (q // pc.nf, pc.b, q % pc.nf),
                ).start()
            return
        core, xm, ym = pc.mates()
        here = (step == 0) | (step == 2) | (step == 3) | (step == 6)
        q = pick(step, (0, 0, 1, 2, 1, 2, 3, 3))

        @pl.when(here)
        def _():
            self.near[q] = value

        @pl.when(jnp.logical_not(here))
        def _():
            self.away[q] = value.astype(BF)
            self.core_copy(q).start()

    def core_copy(self, q):
        core = self.place.mates()[0]
        return remote(self.away.at[q], self.back.at[q], self.ssem.at[q], self.rsem.at[q], core)

    def far_copy(self, e):
        return remote(self.away.at[e - 1], self.back.at[e - 1], self.ssem.at[e - 1],
                      self.rsem.at[e - 1], self.place.plane(e))

    def hop_copy(self, k, c, device):
        i = 4 + 2 * k + c
        return remote(
            cut_in(2, self.hop.at[k], c),
            cut_in(2, self.hop.at[k + 3], c),
            self.ssem.at[i],
            self.rsem.at[i],
            device,
        )

    def rows(self, c):
        n = self.hop.shape[1] // 2
        return slice(c * n, (c + 1) * n)

    def targets(self):
        pc = self.place
        core, xm, ym = pc.mates()
        c = pc.f % 2
        first = (c * xm[0] + (1 - c) * ym[0], pc.b, c * xm[2] + (1 - c) * ym[2])
        second = (c * ym[0] + (1 - c) * xm[0], pc.b, c * ym[2] + (1 - c) * xm[2])
        return (first, second)

    def early(self):
        pc = self.place
        if not pc.two_level:
            return
        c = pc.f % 2
        first, second = self.targets()
        self.core_copy(1).wait_recv()
        self.core_copy(2).wait_recv()
        q = c * 1 + (1 - c) * 2
        for k in range(2):
            r = self.rows(k)
            self.hop[0, r] = (self.mine(q, r) + self.back[q, r].astype(F32)).astype(BF)
            self.hop_copy(0, k, first).start()

    def diagonal(self):
        pc = self.place
        if not pc.two_level:
            return
        first, second = self.targets()
        self.core_copy(3).wait_recv()
        for k in range(2):
            r = self.rows(k)
            self.hop[1, r] = (self.mine(3, r) + self.back[3, r].astype(F32)).astype(BF)
            self.hop_copy(1, k, first).start()

    def mine(self, q, r=slice(None)):
        return self.near[q, r]

    def result(self, store):
        self.late()
        self.finish(store)

    def late(self):
        pc = self.place
        if not pc.two_level:
            return
        c = pc.f % 2
        first, second = self.targets()
        q = c * 2 + (1 - c) * 1
        for k in range(2):
            r = self.rows(k)
            self.hop_copy(1, k, first).wait_recv()
            self.hop[2, r] = (
                self.mine(q, r) + self.back[q, r].astype(F32) + self.hop[4, r].astype(F32)
            ).astype(BF)
            self.hop_copy(2, k, second).start()

    def finish(self, store):
        pc = self.place
        if not pc.two_level:
            total = self.mine(0)
            for e in range(1, pc.count):
                self.far_copy(e).wait()
                total = total + self.back[e - 1].astype(F32)
            store(total)
            return
        first, second = self.targets()
        self.core_copy(0).wait_recv()
        for k in range(2):
            self.hop_copy(0, k, first).wait_recv()
            self.hop_copy(2, k, second).wait_recv()
        store(
            self.mine(0)
            + self.back[0].astype(F32)
            + self.hop[3].astype(F32)
            + self.hop[5].astype(F32)
        )
        for q in range(4):
            self.core_copy(q).wait_send()
        for k in range(2):
            self.hop_copy(0, k, first).wait_send()
            self.hop_copy(1, k, first).wait_send()
            self.hop_copy(2, k, second).wait_send()


class ReadyScatter(PlaneScatter):
    def __init__(self, place, part, back, hop, ssem, rsem):
        super().__init__(place, None, None, back, hop, ssem, rsem)
        self.part = part
        if place.two_level:
            o = place.slots()
            self.here = (o[0], o[2], o[3], o[6])
            self.gone = (o[1], o[4], o[5], o[7])

    def mine(self, q, r=slice(None)):
        if not self.place.two_level:
            return self.part(self.place.me)[...].astype(F32)
        return self.part(pick(q, self.here))[r].astype(F32)

    def core_copy(self, q):
        core = self.place.mates()[0]
        v = self.part(self.gone[q])
        return remote(v, self.back.at[q], self.ssem.at[q], self.rsem.at[q], core)

    def far_copy(self, e):
        pc = self.place
        v = self.part((pc.me + e) % pc.count)
        return remote(v, self.back.at[e - 1], self.ssem.at[e - 1], self.rsem.at[e - 1],
                      pc.plane(e))

    def start(self):
        pc = self.place
        if pc.two_level:
            for q in (3, 2, 1, 0):
                self.core_copy(q).start()
        else:
            for e in range(1, pc.count):
                self.far_copy(e).start()


class RowSends:
    def __init__(self, place, layer, out, sems):
        self.place, self.layer, self.out = (place, layer, out)
        self.lsem, self.ss, self.sr = sems

    def copies(self, f, src):
        pc = self.place
        e = (self.layer * pc.nf + f - pc.me + pc.count) % pc.count
        own = self.out.at[pc.me]
        k = (e + pc.count - 1) % pc.count
        away = remote(src, own, self.ss.at[f], self.sr.at[k], (self.layer, pc.b, f))
        return (e, away, pltpu.make_async_copy(src, own, self.lsem))

    def start(self, f, src):
        e, away, local = self.copies(f, src)

        @pl.when(e != 0)
        def _():
            away.start()

        @pl.when(e == 0)
        def _():
            local.start()

    def finish(self, src):
        pc = self.place
        for f in range(pc.nf):
            e, away, local = self.copies(f, src)

            @pl.when(e != 0)
            def _():
                away.wait_send()

            @pl.when(e == 0)
            def _():
                local.wait()

        @pl.when(pc.s == self.layer)
        def _():
            for e in range(1, pc.count):
                q = pc.slot_from(e)
                remote(src, self.out.at[q], self.ss.at[0], self.sr.at[e - 1], pc.plane(e)).wait_recv()


def row_scratch(dims):
    dma = pltpu.SemaphoreType.DMA
    return [dma(()), dma((dims[2],)), dma((dims[0] * dims[2],))]


class LineGather:
    def __init__(self, place, piece, out, sems, part=None):
        self.place, self.piece = (place, piece)
        self.view = lambda t: out.at[t] if part is None else out.at[t, part]
        self.lsem, self.ss, self.sr = sems
        self.k = 0

    def local(self):
        return pltpu.make_async_copy(self.piece, self.view(self.place.b), self.lsem)

    def hop(self, way, k, came):
        pc = self.place
        t = pc.b - way * (k - (0 if came else 1))
        src = self.piece if k == 1 and not came else self.view(t)
        i = k - 1 + (0 if way == 1 else pc.nb - 1)
        return remote(
            src, self.view(t), self.ss.at[i], self.sr.at[i], (pc.s, pc.b + way, pc.f)
        )

    def sends(self, way, k):
        b, nb = (self.place.b, self.place.nb)
        return (b >= k - 1) & (b < nb - 1) if way == 1 else (b <= nb - k) & (b > 0)

    def comes(self, way, k):
        b, nb = (self.place.b, self.place.nb)
        return b >= k if way == 1 else b <= nb - 1 - k

    def arrived(self, k):
        for way in (1, -1):
            @pl.when(self.comes(way, k))
            def _():
                self.hop(way, k, True).wait_recv()

    def start(self):
        self.local().start()
        self.service()

    def service(self):
        if self.k == self.place.nb - 1:
            return
        self.k += 1
        if self.k > 1:
            self.arrived(self.k - 1)
        for way in (1, -1):
            @pl.when(self.sends(way, self.k))
            def _():
                self.hop(way, self.k, False).start()

    def finish(self):
        last = self.place.nb - 1
        while self.k < last:
            self.service()
        self.arrived(last)
        for k in range(1, last + 1):
            for way in (1, -1):
                @pl.when(self.sends(way, k))
                def _():
                    self.hop(way, k, False).wait_send()
        self.local().wait()


class LineReduce:
    def __init__(self, place, terms, store, sems, load=None):
        self.place, self.terms, self.store, self.load = (place, terms, store, load)
        self.out, self.came, self.ss, self.sr = sems
        self.k = 0

    def index(self, way, k):
        return k - 1 + (0 if way == 1 else self.place.nb - 1)

    def hop(self, way, k):
        pc = self.place
        i = self.index(way, k)
        return remote(
            self.out.at[i], self.came.at[i], self.ss.at[i], self.sr.at[i],
            (pc.s, pc.b + way, pc.f),
        )

    def rank(self, way):
        pc = self.place
        return pc.b if way == 1 else pc.nb - 1 - pc.b

    def sends(self, way, k):
        r = self.rank(way)
        return (r < k) & (r < self.place.nb - 1)

    def start(self):
        if self.load is not None:
            self.load.wait()
        self.service()

    def service(self):
        nb = self.place.nb
        if self.k == nb - 1:
            return
        self.k += 1
        k = self.k
        for way in (1, -1):
            r = self.rank(way)
            t = nb - k + r if way == 1 else k - 1 - r
            i = self.index(way, k)

            @pl.when(self.sends(way, k) & (r == 0))
            def _():
                self.out[i] = self.terms(t)

            if k > 1:
                @pl.when(self.sends(way, k) & (r > 0))
                def _():
                    self.hop(way, k - 1).wait_recv()
                    total = self.terms(t).astype(F32) + self.came[i - 1].astype(F32)
                    self.out[i] = total.astype(BF)

            @pl.when(self.sends(way, k))
            def _():
                self.hop(way, k).start()

    def finish(self):
        pc = self.place
        last = pc.nb - 1
        while self.k < last:
            self.service()
        right, left = (self.index(1, last), self.index(-1, last))

        @pl.when(pc.b == 0)
        def _():
            self.hop(-1, last).wait_recv()
            self.store(self.terms(pc.b).astype(F32) + self.came[left].astype(F32))

        @pl.when(pc.b == last)
        def _():
            self.hop(1, last).wait_recv()
            self.store(self.terms(pc.b).astype(F32) + self.came[right].astype(F32))

        @pl.when((pc.b > 0) & (pc.b < last))
        def _():
            self.hop(1, last).wait_recv()
            self.hop(-1, last).wait_recv()
            self.store(
                self.terms(pc.b).astype(F32)
                + self.came[right].astype(F32)
                + self.came[left].astype(F32)
            )

        for k in range(1, last + 1):
            for way in (1, -1):
                @pl.when(self.sends(way, k))
                def _():
                    self.hop(way, k).wait_send()


def gather_scratch(dims):
    dma = pltpu.SemaphoreType.DMA
    return [dma(()), dma((2 * (dims[1] - 1),)), dma((2 * (dims[1] - 1),))]


def reduce_scratch(dims, *block):
    dma = pltpu.SemaphoreType.DMA
    n = 2 * (dims[1] - 1)
    return [pltpu.VMEM((n,) + block, BF), pltpu.VMEM((n,) + block, BF), dma((n,)), dma((n,))]


class Riders:
    def __init__(self, dims, specs, arrays):
        self.dims, self.specs, self.arrays = (dims, specs, arrays)
        self.shapes = []
        self.places = [AN] * len(specs)
        self.outs = []
        self.scratch = []
        self.sizes = []
        for spec, a in zip(specs, arrays):
            if spec[0] == "gather":
                shape = (dims[1],) + a.shape[1:]
                scratch = gather_scratch(dims)
            else:
                lo, hi = spec[1]
                shape = (hi - lo,) + a.shape[2:]
                scratch = reduce_scratch(dims, *shape)
                scratch += [
                    pltpu.VMEM((dims[1],) + shape, BF), pltpu.SemaphoreType.DMA(())
                ]
            self.outs.append(AN if spec[0] == "gather" else VM)
            self.shapes.append(jax.ShapeDtypeStruct(shape, a.dtype))
            self.scratch += scratch
            self.sizes.append(len(scratch))
        self.count = len(specs)

    def board(self, place, ins, outs, scratch):
        out = []
        for spec, size, a, o in zip(self.specs, self.sizes, ins, outs):
            mine, scratch = (scratch[:size], scratch[size:])
            if spec[0] == "gather":
                out.append(LineGather(place, a.at[spec[1]], o, mine))
            else:
                lo, hi = spec[1]

                def store(value, o=o):
                    o[...] = value.astype(BF)

                terms, sem = mine[4:]
                load = pltpu.make_async_copy(a.at[:, lo:hi], terms, sem)
                load.start()
                out.append(
                    LineReduce(place, lambda t, r=terms: r[t], store, mine[:4], load)
                )
        return (out, scratch)


def each(riders, what):
    for r in riders:
        getattr(r, what)()


def scatter_scratch(dims, *block):
    count = dims[0] * dims[2]
    if dims[0] == 2 and dims[2] == 4:
        near, away, hops, sems = (4, 4, 6, 10)
    else:
        near, away, hops, sems = (1, count - 1, 1, count - 1)
    return [
        pltpu.VMEM((near,) + block, F32),
        pltpu.VMEM((away,) + block, BF),
        pltpu.VMEM((away,) + block, BF),
        pltpu.VMEM((hops,) + block, BF),
        pltpu.SemaphoreType.DMA((sems,)),
        pltpu.SemaphoreType.DMA((sems,)),
    ]


def call(kernel, name, cid, outs, out_specs, in_specs, scratch, args):
    params = pltpu.CompilerParams(
        collective_id=cid, has_side_effects=True, vmem_limit_bytes=VMEM_LIMIT
    )
    return pl.pallas_call(
        kernel,
        name=name,
        out_shape=outs,
        in_specs=in_specs,
        out_specs=out_specs,
        scratch_shapes=scratch,
        compiler_params=params,
    )(*args)


def column_start(dims, part, b, f, y, half):
    ns, nb, nf = dims
    return part * nb * nf * ns * half + ((b * nf + f) * ns + y) * half


def columns_of(ref, q, nf, wide):
    return ref.at[:, q % nf, :, pl.ds(pl.multiple_of((q // nf) * wide, wide), wide)]


def gather_weights_kernel(
    dims, w_ref, wq_ref, wo_ref, wd, g1_ref, g2_ref, bias_ref,
    gup, wdp, gu_first, qo_first, qz, small_all,
    small, pack, qcol, qh, lsem, ps, pr, ms, mr, qs, qr, *rest
):
    pc = Place(dims)
    ns, nb, nf = dims
    half = wd.shape[1]
    wide = qh.shape[2]
    greet(pc, "all", True)
    small[...] = jnp.zeros_like(small)
    r = 0
    for ref in (g1_ref, g2_ref, bias_ref):
        for k in range(0, ref.shape[1], 128):
            small[r : r + 1, :] = ref[0:1, k : k + 128]
            r += 1
    qkv = wq_ref.shape[2]
    full = jnp.concatenate([wq_ref[0], wo_ref[0]], axis=1)
    for y in range(ns):
        qcol[y] = full[:, y * wide : (y + 1) * wide]
    across = []
    for d in range(1, ns):
        y = (pc.s + d) % ns
        t = (y, pc.b, pc.f)
        i = 3 * (d - 1)
        across.append(remote(qcol.at[y], qh.at[pc.s], ms.at[i], mr.at[i], t))
        across.append(remote(wd.at[y], wdp.at[pc.s], ms.at[i + 1], mr.at[i + 1], t))
        across.append(remote(small, small_all.at[pc.s], ms.at[i + 2], mr.at[i + 2], t))
    for c in across:
        c.start()
    qh[pc.s] = qcol[pc.s]
    local = [
        pltpu.make_async_copy(wd.at[pc.s], wdp.at[pc.s], lsem.at[0]),
        pltpu.make_async_copy(small, small_all.at[pc.s], lsem.at[1]),
    ]
    for c in local:
        c.start()
    own = pltpu.make_async_copy(pack.at[pc.s, pc.f], gup.at[pc.s, pc.f], lsem.at[2])

    def piece(y, f):
        e = (y * nf + f - pc.me + pc.count) % pc.count
        k = (e + pc.count - 1) % pc.count
        return (
            e,
            remote(pack.at[y, f], gup.at[pc.s, pc.f], ps.at[k], pr.at[k], (y, pc.b, f)),
        )

    for f in range(nf):
        for y in range(ns):
            pieces = []
            for part in range(2):
                for b in range(nb):
                    c0 = column_start(dims, part, b, f, y, half)
                    pieces.append(w_ref[0, :, c0 : c0 + half])
            pack[y, f] = jnp.concatenate(pieces, axis=1)
            e, c = piece(y, f)

            @pl.when(e != 0)
            def _():
                c.start()

    own.start()
    for d in range(ns - 1):
        across[3 * d].wait()
    line_q = LineGather(pc, qh, qz, rest[0:3])
    lines = [
        LineGather(pc, gup.at[0, f], gu_first, rest[3 + 3 * f : 6 + 3 * f], f) for f in range(nf)
    ]
    line_q.start()

    def arrived(y, f):
        e, c = piece(y, f)
        k = (2 * pc.count - e - 1) % pc.count

        @pl.when(e != 0)
        def _():
            remote(pack.at[0, 0], gup.at[y, f], ps.at[k], pr.at[k], (y, pc.b, f)).wait_recv()

    own.wait()
    line_q.service()
    for f in range(nf):
        arrived(0, f)
        lines[f].start()
    line_q.service()
    for line in lines:
        line.service()
    line_q.finish()
    gather = PlaneGather(pc, lambda q: columns_of(qo_first, q, nf, wide), qs, qr)
    columns_of(qo_first, pc.me, nf, wide)[...] = qz[:, 0]
    gather.start()
    for step in range(1, min(6, pc.count)):
        gather.before(step)
    for line in lines:
        line.service()
    for step in range(min(6, pc.count), pc.count):
        gather.before(step)
    gather.finish()
    for y in range(1, ns):
        for f in range(nf):
            arrived(y, f)
    for y in range(ns):
        for f in range(nf):
            e, c = piece(y, f)

            @pl.when(e != 0)
            def _():
                c.wait_send()

    for c in local:
        c.wait()
    for i, c in enumerate(across):
        if i % 3:
            c.wait()
    for line in lines:
        line.finish()


def gather_weights(dims, w, wq, wo, wd, vectors):
    ns, nb, nf = dims
    count = ns * nf
    half, width = wd.shape[1:]
    dr = wq.shape[1]
    cols = wq.shape[2] + wo.shape[2]
    wide = cols // ns
    two_ff = 2 * nb * half
    small = (-(-sum(v.shape[1] for v in vectors) // 1024) * 8, 128)
    sds = jax.ShapeDtypeStruct
    outs = (
        sds((ns, nf, dr, two_ff), BF),
        sds((ns, half, width), BF),
        sds((nb, nf, dr, two_ff), BF),
        sds((nb, nf, dr, cols), BF),
        sds((nb, ns, dr, wide), BF),
        sds((ns,) + small, F32),
    )
    dma = pltpu.SemaphoreType.DMA
    return call(
        functools.partial(gather_weights_kernel, dims),
        "gather_weights",
        0,
        outs,
        [AN, AN, AN, VM, VM, AN],
        [VM, VM, VM, AN, VM, VM, VM],
        [
            pltpu.VMEM(small, F32),
            pltpu.VMEM((ns, nf, dr, two_ff), BF),
            pltpu.VMEM((ns, dr, wide), BF),
            pltpu.VMEM((ns, dr, wide), BF),
            dma((4,)),
            dma((count,)),
            dma((count,)),
            dma((3 * (ns - 1),)),
            dma((3 * (ns - 1),)),
        ]
        + gather_sems(dims)
        + gather_scratch(dims) * (1 + nf),
        (w, wq, wo, wd, *vectors),
    )


def rms(values):
    return lax.rsqrt(jnp.mean(values * values, axis=0, keepdims=True) + 1e-06)


def column(rows_t, first, count):
    return jnp.concatenate([rows_t[:, k : k + 1] for k in range(first, first + count)], axis=0)


def rows_of(values):
    v = folded(values)
    return jnp.concatenate(
        [v[k : k + 128].T.sum(axis=0, keepdims=True) for k in range(0, v.shape[0], 128)], axis=0
    )


def folded(v):
    out = v[:, :128]
    for k in range(1, v.shape[1] // 128):
        out = out + v[:, k * 128 : (k + 1) * 128]
    return out


def fill_masks(pc, mask, docs_ref):
    nk, rows = mask.shape[:2]
    picked = []
    for j in range(nk):
        start = pl.multiple_of((pc.b - j + pc.nb) % pc.nb * rows, rows)
        row = jnp.zeros((1, rows), F32)
        for t in range(pc.ns):
            mine = jnp.where(pc.s == t, 1.0, 0.0)
            row = row + docs_ref[t : t + 1, pl.ds(start, rows)].astype(F32) * mine
        picked.append(row)
    query_docs = picked[0]
    meta_t = padded_t(
        jnp.concatenate(
            [row[:, k : k + 128] for row in picked for k in range(0, rows, 128)], axis=0
        )
    )
    key_i = lax.broadcasted_iota(jnp.int32, (rows, rows), 0)
    query_i = lax.broadcasted_iota(jnp.int32, (rows, rows), 1)
    per = rows // 128
    for j in range(nk):
        same = column(meta_t, j * per, per) == query_docs
        if j == 0:
            live = same & (key_i <= query_i)
        else:
            live = same & (key_i < (pc.b - j + 1) * rows)
        mask[j] = jnp.where(live, 0.0, NEG)


def load_qo(qo, w, wo, sems):
    cols = w.shape[1]
    c1 = pltpu.make_async_copy(qo.at[:, 0:cols], w, sems.at[0])
    c2 = pltpu.make_async_copy(qo.at[:, cols : cols + wo.shape[1]], wo, sems.at[1])
    c1.start()
    c2.start()
    return (c1, c2)


def gains_of(small_t, width, qkv):
    n = width // 128
    return (
        column(small_t, 0, n),
        column(small_t, n, n),
        column(small_t, 2 * n, qkv // 128),
    )


def padded_t(v):
    n = v.shape[0]
    return jnp.concatenate([v, jnp.zeros((128 - n, 128), v.dtype)], axis=0).T


def attention_forward_kernel(dims, *args):
    pc = Place(dims)
    riders, gather = attention_forward_part(pc, *args)
    last_blocks(pc, gather)
    gather.finish()
    each(riders, "finish")


def last_blocks(pc, gather):
    for step in range(min(6, pc.count), pc.count):
        gather.before(step)


def attention_forward_part(
    pc, nk, layer, plan, carry, h_ref, small_ref, docs_ref, cos_ref, sin_ref, qo_all,
    *refs
):
    n = plan.count
    block_ref, refs = (refs[0], refs[1:])
    ins, refs = (refs[:n], refs[n:])
    normed_ref, q_ref, kv_ref, lse_ref, mixed_ref, res_ref, n2_ref = refs[:7]
    outs, refs = (refs[7 : 7 + n], refs[7 + n :])
    block_all, refs = (refs[0], refs[1:])
    w, wo, mask, joined, top_own, sum_own, out_own, ssem, rsem, qsem = refs[:10]
    refs = refs[10:]
    width, rows = h_ref.shape
    loads = load_qo(qo_all, w, wo, qsem)
    greet(pc, "mates", True)
    riders, refs = plan.board(pc, ins, outs, refs)
    if carry == "lanes":
        own = block_ref
        slot = lambda q: block_all.at[:, lanes(q, rows)]
    else:
        own = block_ref.at[:, 1]
        slot = lambda q: columns_of(block_all, q, pc.nf, block_ref.shape[3])
    gather = PlaneGather(pc, slot, *refs)
    slot(pc.me)[...] = own[...]
    gather.start()
    each(riders, "start")
    g1, g2, bias = gains_of(padded_t(small_ref[layer]), width, w.shape[1])
    hidden = h_ref[...].astype(BF).astype(F32)
    normed = (hidden * rms(hidden) * g1).astype(BF)
    normed_ref[...] = normed
    fill_masks(pc, mask, docs_ref)
    loads[0].wait()
    joined[...] = tn(w[...], normed) + bias
    cos_part = cos_ref[...]
    sin_part = sin_ref[...]
    half = HD // 2

    def turned(row):
        u1 = joined[pl.ds(row, half), :]
        u2 = joined[pl.ds(row + half, half), :]
        return (u1 * cos_part - u2 * sin_part, u2 * cos_part + u1 * sin_part)

    for g in range(KVH):
        r1, r2 = turned((H + g) * HD)
        kv_ref[0, g, :half, :] = r1.astype(BF)
        kv_ref[0, g, half:, :] = r2.astype(BF)
        v0 = (H + KVH + g) * HD
        kv_ref[0, KVH + g] = joined[v0 : v0 + HD, :].astype(BF)
    sends = [
        remote(kv_ref.at[0], kv_ref.at[j], ssem.at[j - 1], rsem.at[j - 1], pc.along(j))
        for j in range(1, nk)
    ]
    for c in sends:
        c.start()
    scale = HD**-0.5
    for head in range(H):
        r1, r2 = turned(head * HD)
        q_ref[head, :half, :] = (r1 * scale).astype(BF)
        q_ref[head, half:, :] = (r2 * scale).astype(BF)
    for g in range(KVH):
        keys = kv_ref[0, g].T
        values = kv_ref[0, KVH + g]

        def own_keys(i, carried):
            head = g * GROUP + i
            x = nn(keys, q_ref[head]) + mask[0]
            top = x.max(axis=0, keepdims=True)
            e = jnp.exp(x - top)
            top_own[head] = top
            sum_own[head] = e.sum(axis=0, keepdims=True)
            out_own[head] = nn(values, e.astype(BF))
            return carried

        lax.fori_loop(0, GROUP, own_keys, 0, unroll=True)
    for c in sends:
        c.wait()
    each(riders, "service")
    for g in range(KVH):
        keys = [kv_ref[j, g].T for j in range(1, nk)]
        values = [kv_ref[j, KVH + g] for j in range(1, nk)]

        def one_head(i, carried):
            head = g * GROUP + i
            q = q_ref[head]
            s = [nn(keys[j], q) + mask[j + 1] for j in range(nk - 1)]
            first = top_own[head]
            top = first
            for x in s:
                top = jnp.maximum(top, x.max(axis=0, keepdims=True))
            e = [jnp.exp(x - top) for x in s]
            fade = jnp.exp(first - top)
            total = sum_own[head] * fade
            out = out_own[head] * fade
            for j in range(nk - 1):
                total = total + e[j].sum(axis=0, keepdims=True)
                out = out + nn(values[j], e[j].astype(BF))
            lse_ref[head] = top + jnp.log(total)
            mixed_ref[head] = (out / total).astype(BF)
            return carried

        lax.fori_loop(0, GROUP, one_head, 0, unroll=True)
        if g == 0:
            for step in range(1, min(6, pc.count)):
                gather.before(step)
            each(riders, "service")
    mixed = mixed_ref[...].reshape(H * HD, rows)
    loads[1].wait()
    residual = hidden + tn(wo[...], mixed)
    res_ref[...] = residual
    n2_ref[...] = (residual * rms(residual) * g2).astype(BF)
    return (riders, gather)


def attention_scratch(dims, nk, width, rows, qkv):
    dma = pltpu.SemaphoreType.DMA
    return [
        pltpu.VMEM((width, qkv), BF),
        pltpu.VMEM((width, width), BF),
        pltpu.VMEM((nk, rows, rows), F32),
        pltpu.VMEM((qkv, rows), F32),
        pltpu.VMEM((H, 1, rows), F32),
        pltpu.VMEM((H, 1, rows), F32),
        pltpu.VMEM((H, HD, rows), F32),
        dma((nk - 1,)),
        dma((nk - 1,)),
        dma((2,)),
    ]


def attention_forward(dims, nk, cid, layer, hidden, small, docs, cos_part, sin_part, qo_all,
                      plan, carry, block):
    width, rows = hidden.shape
    ns, nb, nf = dims
    count = ns * nf
    qkv = qo_all.shape[1] - width
    sds = jax.ShapeDtypeStruct
    outs = [
        sds((width, rows), BF),
        sds((H, HD, rows), BF),
        sds((nk, 2 * KVH, HD, rows), BF),
        sds((H, 1, rows), F32),
        sds((H, HD, rows), BF),
        sds((width, rows), F32),
        sds((width, rows), BF),
    ] + plan.shapes
    if carry == "lanes":
        outs.append(sds((width, count * rows), BF))
    else:
        outs.append(sds((nb, nf, block.shape[2], ns * block.shape[3]), BF))
    out = call(
        functools.partial(attention_forward_kernel, dims, nk, layer, plan, carry),
        "attention_forward",
        cid,
        tuple(outs),
        [VM] * 7 + plan.outs + [VM],
        [VM] * 5 + [AN, VM] + plan.places,
        attention_scratch(dims, nk, width, rows, qkv)
        + plan.scratch
        + gather_sems(dims),
        (hidden, small, docs, cos_part, sin_part, qo_all, block, *plan.arrays),
    )
    return (out[:7], out[7:])


def attention_backward_kernel(dims, *args):
    pc = Place(dims)
    riders = attention_backward_part(pc, lambda: None, None, *args)
    each(riders, "finish")


def attention_backward_part(
    pc, begun, cut_rows, nk, layer, plan, carry, g_ref, small_ref, docs_ref, cos_ref, sin_ref,
    h_ref, normed_ref, q_ref, kv_ref, lse_ref, mixed_ref, qo_all, *refs
):
    n = plan.count
    parts_ref, more_ref, refs = (refs[0], refs[1], refs[2:])
    ins, refs = (refs[:n], refs[n:])
    gh_ref, dqo_ref, dsmall_ref = refs[:3]
    outs, refs = (refs[3 : 3 + n], refs[3 + n :])
    out_ref, refs = (refs[0], refs[1:])
    if carry == "columns":
        rows_ref, refs = (refs[0], refs[1:])
    w, wo, mask, dmix, dkv, delta, dq_some, out_kv, in_kv, gj, ssem, rsem, qsem = refs[:13]
    refs = refs[13:]
    width, rows = h_ref.shape
    qkv = w.shape[1]
    loads = load_qo(qo_all, w, wo, qsem)
    riders, refs = plan.board(pc, ins, outs, refs)
    if carry == "columns":
        held, held_sem = refs[7:]
        coming = pltpu.make_async_copy(parts_ref, held, held_sem)
        coming.start()
    greet(pc, "all" if carry == "columns" else "mates", True)
    if carry == "columns":
        part = lambda q: columns_of(held, q, pc.nf, out_ref.shape[2])
        hand_out = RowSends(pc, 1, rows_ref, refs[4:7])
        coming.wait()
    else:
        part = lambda q: parts_ref.at[q]
    scatter = ReadyScatter(pc, part, *refs[:4])
    scatter.start()
    each(riders, "start")
    begun()

    def put(c0, c1, value):
        if cut_rows is None:
            dqo_ref[:, c0:c1] = value.astype(BF)
        else:
            for t in range(pc.nb):
                for f in range(pc.nf):
                    r = (t * pc.nf + f) * cut_rows
                    dqo_ref[t, f, :, c0:c1] = value[r : r + cut_rows].astype(BF)

    g1 = column(padded_t(small_ref[layer]), 0, width // 128)
    fill_masks(pc, mask, docs_ref)
    grl = g_ref[...].astype(BF)
    loads[1].wait()
    dmix[...] = nn(wo[...], grl).astype(BF).reshape(dmix.shape)
    put(qkv, qkv + width, nt(mixed_ref[...].reshape(H * HD, rows), grl))
    scatter.diagonal()
    scatter.early()
    if carry == "columns":
        for f in range(pc.nf):
            hand_out.start(f, more_ref.at[f])
    cos_part = cos_ref[...]
    sin_part = sin_ref[...]
    half = HD // 2
    scale = HD**-0.5
    dkv[...] = jnp.zeros_like(dkv)

    def unturned(d1, d2):
        return (d1 * cos_part + d2 * sin_part, d2 * cos_part - d1 * sin_part)

    def of_block(j, g, head, keys, keys_t, values):
        q = q_ref[head]
        do = dmix[head]
        p = jnp.exp(nn(keys, q) + mask[j] - lse_ref[head])
        ds = (p * (nn(values, do) - delta[head])).astype(BF)
        dkv[j, g] += nt(q, ds)
        dkv[j, KVH + g] += nt(do, p.astype(BF))
        return nn(keys_t, ds)

    for g in range(KVH):
        keys_t = [kv_ref[j, g] for j in range(1, nk)]
        keys = [k.T for k in keys_t]
        values = [kv_ref[j, KVH + g].T for j in range(1, nk)]

        def earlier(i, carried):
            head = g * GROUP + i
            delta[head] = (dmix[head].astype(F32) * mixed_ref[head].astype(F32)).sum(
                axis=0, keepdims=True
            )
            dq = of_block(1, g, head, keys[0], keys_t[0], values[0])
            for j in range(2, nk):
                dq = dq + of_block(j, g, head, keys[j - 1], keys_t[j - 1], values[j - 1])
            dq_some[head] = dq
            return carried

        lax.fori_loop(0, GROUP, earlier, 0, unroll=True)
        if g == 0:
            scatter.late()
        if (g == 1) == (carry == "columns"):
            each(riders, "service")
    for j in range(1, nk):
        out_kv[j - 1] = dkv[j].astype(BF)
    sends = [
        remote(out_kv.at[j - 1], in_kv.at[j - 1], ssem.at[j - 1], rsem.at[j - 1],
               pc.along(pc.nb - j))
        for j in range(1, nk)
    ]
    for c in sends:
        c.start()
    for g in range(KVH):
        keys_t = kv_ref[0, g]
        keys = keys_t.T
        values = kv_ref[0, KVH + g].T

        def own_keys(i, carried):
            head = g * GROUP + i
            dq = (dq_some[head] + of_block(0, g, head, keys, keys_t, values)) * scale
            r1, r2 = unturned(dq[:half], dq[half:])
            gj[pl.ds(pl.multiple_of(head * HD, HD), half), :] = r1.astype(BF)
            gj[pl.ds(pl.multiple_of(head * HD + half, half), half), :] = r2.astype(BF)
            return carried

        lax.fori_loop(0, GROUP, own_keys, 0, unroll=True)
    for c in sends:
        c.wait()
    each(riders, "service")
    own = dkv[0]
    for j in range(1, nk):
        own = own + in_kv[j - 1].astype(F32)
    for g in range(KVH):
        r1, r2 = unturned(own[g, :half], own[g, half:])
        k0 = (H + g) * HD
        gj[k0 : k0 + half, :] = r1.astype(BF)
        gj[k0 + half : k0 + HD, :] = r2.astype(BF)
        v0 = (H + KVH + g) * HD
        gj[v0 : v0 + HD, :] = own[KVH + g].astype(BF)
    gjv = gj[...]
    n1 = width // 128
    dsmall_ref[n1 : n1 + qkv // 128, :] = rows_of(gjv.astype(F32))
    loads[0].wait()
    put(0, qkv, nt(normed_ref[...], gjv))
    gn = nn(w[...], gjv)
    hidden = h_ref[...].astype(BF).astype(F32)
    scale_one = rms(hidden)
    unit = hidden * scale_one
    dsmall_ref[:n1, :] = rows_of(gn * unit)
    u = gn * g1
    gh_ref[...] = g_ref[...] + scale_one * (u - unit * jnp.mean(u * unit, axis=0, keepdims=True))

    def store(total):
        if carry == "columns":
            out_ref[...] = total.astype(BF)
        else:
            out_ref[...] = more_ref[...] + total

    if cut_rows is not None:
        each(riders, "service")
    scatter.finish(store)
    if carry == "columns":
        hand_out.finish(more_ref.at[0])
    return riders


def backward_scratch(nk, width, rows, qkv):
    dma = pltpu.SemaphoreType.DMA
    block = (2 * KVH, HD, rows)
    return [
        pltpu.VMEM((width, qkv), BF),
        pltpu.VMEM((width, width), BF),
        pltpu.VMEM((nk, rows, rows), F32),
        pltpu.VMEM((H, HD, rows), BF),
        pltpu.VMEM((nk,) + block, F32),
        pltpu.VMEM((H, 1, rows), F32),
        pltpu.VMEM((H, HD, rows), F32),
        pltpu.VMEM((nk - 1,) + block, BF),
        pltpu.VMEM((nk - 1,) + block, BF),
        pltpu.VMEM((qkv, rows), BF),
        dma((nk - 1,)),
        dma((nk - 1,)),
        dma((2,)),
    ]


def attention_backward(dims, nk, cid, layer, g, small, docs, cos_part, sin_part, hidden,
                       normed, q, kv, lse, mixed, qo_all, plan, carry, late):
    width, rows = hidden.shape
    qkv = qo_all.shape[1] - width
    sds = jax.ShapeDtypeStruct
    outs = [
        sds((width, rows), F32),
        sds((width, qkv + width), BF),
        sds(((width + qkv) // 128, 128), F32),
    ] + plan.shapes
    dma = pltpu.SemaphoreType.DMA
    if carry == "columns":
        summed = (dims[1], late[0].shape[2], late[0].shape[3] // dims[0])
        outs += [sds(summed, BF), sds((dims[0] * dims[2],) + late[1].shape[1:], BF)]
        places = [VM, AN]
    else:
        summed = (width, rows)
        outs.append(sds(summed, F32))
        places = [VM]
    out = call(
        functools.partial(attention_backward_kernel, dims, nk, layer, plan, carry),
        "attention_backward",
        cid,
        tuple(outs),
        [VM] * 3 + plan.outs + places,
        [VM] * 11 + [AN] + [AN if carry == "columns" else VM, VM] + plan.places,
        backward_scratch(nk, width, rows, qkv)
        + plan.scratch
        + scatter_scratch(dims, *summed)[2:]
        + (
            row_scratch(dims) + [pltpu.VMEM(late[0].shape, BF), dma(())]
            if carry == "columns"
            else []
        ),
        (g, small, docs, cos_part, sin_part, hidden, normed, q, kv, lse, mixed, qo_all,
         *late, *plan.arrays),
    )
    return (out[:3], out[3:])


def sequence_of(pc):
    if pc.two_level:
        return ((0, 1, 2, 3, 6, 7, 4, 5), 5, 7)
    return (tuple(range(pc.count)), pc.count - 1, pc.count - 1)


def lanes(slot, rows):
    return pl.ds(pl.multiple_of(slot * rows, rows), rows)


def transpose_into(dst, src):
    cols = src.shape[1]
    for c0 in range(0, cols, 128):
        c1 = min(c0 + 128, cols)
        dst[c0:c1, :] = src[:, c0:c1].T


def feed_forward_kernel(dims, *args):
    pc = Place(dims)
    feed_forward_part(pc, lambda: greet(pc, "mates", True), lambda: None, *args)


def feed_forward_part(pc, enter, ready, plan, x_ref, res_ref, wgu_ref, wd_ref, *refs):
    n = plan.count
    ins, refs = (refs[:n], refs[n:])
    out_ref, x_out, gu_out = refs[:3]
    outs, refs = (refs[3 : 3 + n], refs[3 + n :])
    x_all, gu_all, lsem, wgu_t, wd_t, gu, inner, near, away, back, hop, ss, sr, gs, gr = refs[:15]
    width, rows = x_ref.shape
    ff = wd_ref.shape[0]
    riders, _ = plan.board(pc, ins, outs, refs[15:])
    enter()
    gather = PlaneGather(pc, lambda q: x_all.at[:, lanes(q, rows)], gs, gr)
    scatter = PlaneScatter(pc, near, away, back, hop, ss, sr)
    x_all[:, lanes(pc.me, rows)] = x_ref[...]
    gather.start()
    ready()
    each(riders, "start")
    transpose_into(wgu_t, wgu_ref)
    transpose_into(wd_t, wd_ref)
    sequence, diagonal_at, early_at = sequence_of(pc)
    chunk = 32 if ff % 32 == 0 else 16

    def step_body(turn, carry):
        step = pick(turn, sequence)

        for k in range(pc.count):
            @pl.when(step == k)
            def _():
                gather.before(k)

        slot = pick(step, gather.order)
        sl = lanes(slot, rows)
        gu[...] = nn(wgu_t[...], x_all[:, sl])

        def act(i, c):
            r = pl.multiple_of(i * chunk, chunk)
            gate = gu[pl.ds(r, chunk), :]
            up = gu[pl.ds(ff + r, chunk), :]
            gu_all[pl.ds(r, chunk), sl] = gate.astype(BF)
            gu_all[pl.ds(ff + r, chunk), sl] = up.astype(BF)
            inner[pl.ds(r, chunk), :] = (gate * jax.nn.sigmoid(gate) * up).astype(BF)
            return c

        lax.fori_loop(0, ff // chunk, act, 0, unroll=True)
        scatter.put(step, nn(wd_t[...], inner[...]))

        @pl.when(turn == 3)
        def _():
            each(riders, "service")

        @pl.when(turn == diagonal_at)
        def _():
            scatter.diagonal()

        @pl.when(turn == early_at)
        def _():
            scatter.early()

        return carry

    lax.fori_loop(0, pc.count, step_body, 0)
    leaving = [
        pltpu.make_async_copy(gu_all, gu_out, lsem.at[0]),
        pltpu.make_async_copy(x_all, x_out, lsem.at[1]),
    ]
    each(leaving, "start")
    each(riders, "service")

    def store(total):
        out_ref[...] = res_ref[...] + total

    scatter.result(store)
    gather.finish()
    each(leaving, "wait")
    each(riders, "finish")


def feed_forward(dims, cid, x, residual, wgu, wd, plan):
    width, rows = x.shape
    count = dims[0] * dims[2]
    two_ff, ff = (wgu.shape[1], wd.shape[0])
    sds = jax.ShapeDtypeStruct
    dma = pltpu.SemaphoreType.DMA
    out = call(
        functools.partial(feed_forward_kernel, dims, plan),
        "feed_forward",
        cid,
        (
            sds((width, rows), F32),
            sds((width, count * rows), BF),
            sds((two_ff, count * rows), BF),
            *plan.shapes,
        ),
        [VM, AN, AN] + plan.outs,
        [VM] * 4 + plan.places,
        [
            pltpu.VMEM((width, count * rows), BF),
            pltpu.VMEM((two_ff, count * rows), BF),
            dma((2,)),
            pltpu.VMEM((two_ff, width), BF),
            pltpu.VMEM((width, ff), BF),
            pltpu.VMEM((two_ff, rows), F32),
            pltpu.VMEM((ff, rows), BF),
        ]
        + scatter_scratch(dims, width, rows)
        + gather_sems(dims)
        + plan.scratch,
        (x, residual, wgu, wd, *plan.arrays),
    )
    return (out[:3], out[3:])


def feed_backward_kernel(
    dims, layer, plan, g_ref, res_ref, x_in, gu_in, wgu_ref, wd_ref, small_ref, *refs
):
    n = plan.count
    ins, refs = (refs[:n], refs[n:])
    gr_ref, dwgu_ref, dwd_ref, dsmall_ref = refs[:4]
    outs, refs = (refs[4 : 4 + n], refs[4 + n :])
    x_all, gu_all, lsem, g_all, inner, ggu, gi, near, away, back, hop, ss, sr, gs, gr = refs[:15]
    coming = [
        pltpu.make_async_copy(gu_in, gu_all, lsem.at[0]),
        pltpu.make_async_copy(x_in, x_all, lsem.at[1]),
    ]
    each(coming, "start")
    pc = Place(dims)
    width, rows = g_ref.shape
    ff = wd_ref.shape[0]
    riders, _ = plan.board(pc, ins, outs, refs[15:])
    greet(pc, "mates", n > 0)
    gather = PlaneGather(pc, lambda q: g_all.at[:, lanes(q, rows)], gs, gr)
    scatter = PlaneScatter(pc, near, away, back, hop, ss, sr)
    g_all[:, lanes(pc.me, rows)] = g_ref[...].astype(BF)
    gather.start()
    each(riders, "start")
    coming[0].wait()
    sequence, diagonal_at, early_at = sequence_of(pc)
    chunk = 32 if ff % 32 == 0 else 16

    def step_body(turn, carry):
        step = pick(turn, sequence)

        for k in range(pc.count):
            @pl.when(step == k)
            def _():
                gather.before(k)

        slot = pick(step, gather.order)
        sl = lanes(slot, rows)
        gi[...] = nn(wd_ref[...], g_all[:, sl])

        def act(i, c):
            r = pl.multiple_of(i * chunk, chunk)
            gate = gu_all[pl.ds(r, chunk), sl].astype(F32)
            up = gu_all[pl.ds(ff + r, chunk), sl].astype(F32)
            grad = gi[pl.ds(r, chunk), :]
            sig = jax.nn.sigmoid(gate)
            silu = gate * sig
            inner[pl.ds(r, chunk), sl] = (silu * up).astype(BF)
            ggu[pl.ds(r, chunk), sl] = (grad * up * sig * (1.0 + gate * (1.0 - sig))).astype(BF)
            ggu[pl.ds(ff + r, chunk), sl] = (grad * silu).astype(BF)
            return c

        lax.fori_loop(0, ff // chunk, act, 0, unroll=True)
        scatter.put(step, nn(wgu_ref[...], ggu[:, sl]))

        @pl.when(turn == 3)
        def _():
            each(riders, "service")

        @pl.when(turn == diagonal_at)
        def _():
            scatter.diagonal()

        @pl.when(turn == early_at)
        def _():
            scatter.early()

        return carry

    lax.fori_loop(0, pc.count, step_body, 0)
    each(riders, "service")
    dwd_ref[...] = nt(inner[...], g_all[...]).astype(BF)
    scatter.late()
    coming[1].wait()
    part = width // 2
    for r in range(2):
        dwgu_ref[r * part : (r + 1) * part, :] = nt(
            x_all[r * part : (r + 1) * part, :], ggu[...]
        ).astype(BF)

    def store(total):
        residual = res_ref[...]
        scale_two = rms(residual)
        unit = residual * scale_two
        n1 = width // 128
        dsmall_ref[...] = rows_of(total * unit)
        u = total * column(padded_t(small_ref[layer]), n1, n1)
        gr_ref[...] = g_ref[...].astype(BF).astype(F32) + scale_two * (
            u - unit * jnp.mean(u * unit, axis=0, keepdims=True)
        )

    scatter.finish(store)
    gather.finish()
    each(riders, "finish")


def feed_backward(dims, cid, layer, g, residual, x_all, gu_all, wgu, wd, small, plan):
    width, rows = g.shape
    count = dims[0] * dims[2]
    two_ff, ff = (wgu.shape[1], wd.shape[0])
    sds = jax.ShapeDtypeStruct
    dma = pltpu.SemaphoreType.DMA
    out = call(
        functools.partial(feed_backward_kernel, dims, layer, plan),
        "feed_backward",
        cid,
        (
            sds((width, rows), F32),
            sds(wgu.shape, BF),
            sds(wd.shape, BF),
            sds((width // 128, 128), F32),
            *plan.shapes,
        ),
        [VM] * 4 + plan.outs,
        [VM, VM, AN, AN, VM, VM, VM] + plan.places,
        [
            pltpu.VMEM((width, count * rows), BF),
            pltpu.VMEM((two_ff, count * rows), BF),
            dma((2,)),
            pltpu.VMEM((width, count * rows), BF),
            pltpu.VMEM((ff, count * rows), BF),
            pltpu.VMEM((two_ff, count * rows), BF),
            pltpu.VMEM((ff, rows), F32),
        ]
        + scatter_scratch(dims, width, rows)
        + gather_sems(dims)
        + plan.scratch,
        (g, residual, x_all, gu_all, wgu, wd, small, *plan.arrays),
    )
    return (out[:4], out[4:])


def feed_both_kernel(dims, *args):
    pc = Place(dims)
    feed_both_part(pc, lambda: greet(pc, "mates", False), lambda: None, *args)


def feed_both_part(
    pc, enter, ready, layer, x_ref, res_ref, g_ref, g_all, wgu_ref, wd_ref, small_ref,
    gr_ref, dwgu_ref, dwd_ref, dsmall_ref, parts_ref,
    x_all, inner, ggu, wgu_t, wd_t, gu, gi, near, away, back, hop, ss, sr, gs, gr,
):
    width, rows = g_ref.shape
    ff = wd_ref.shape[0]
    enter()
    gather = PlaneGather(pc, lambda q: x_all.at[:, lanes(q, rows)], gs, gr)
    scatter = PlaneScatter(pc, near, away, back, hop, ss, sr)
    x_all[:, lanes(pc.me, rows)] = x_ref[...]
    gather.start()
    ready()
    transpose_into(wgu_t, wgu_ref)
    transpose_into(wd_t, wd_ref)
    sequence, diagonal_at, early_at = sequence_of(pc)
    chunk = 32 if ff % 32 == 0 else 16

    def step_body(turn, carry):
        step = pick(turn, sequence)

        for k in range(pc.count):
            @pl.when(step == k)
            def _():
                gather.before(k)

        slot = pick(step, gather.order)
        sl = lanes(slot, rows)
        gu[...] = nn(wgu_t[...], x_all[:, sl])
        gi[...] = nn(wd_ref[...], g_all[:, sl])

        def act(i, c):
            r = pl.multiple_of(i * chunk, chunk)
            gate = gu[pl.ds(r, chunk), :]
            up = gu[pl.ds(ff + r, chunk), :]
            grad = gi[pl.ds(r, chunk), :]
            sig = jax.nn.sigmoid(gate)
            silu = gate * sig
            inner[pl.ds(r, chunk), sl] = (silu * up).astype(BF)
            ggu[pl.ds(r, chunk), sl] = (grad * up * sig * (1.0 + gate * (1.0 - sig))).astype(BF)
            ggu[pl.ds(ff + r, chunk), sl] = (grad * silu).astype(BF)
            return c

        lax.fori_loop(0, ff // chunk, act, 0, unroll=True)
        scatter.put(step, nn(wgu_ref[...], ggu[:, sl]))

        @pl.when(turn == diagonal_at)
        def _():
            scatter.diagonal()

        @pl.when(turn == early_at)
        def _():
            scatter.early()

        parts_ref[slot] = nn(wd_t[...], inner[:, sl]).astype(BF)
        return carry

    lax.fori_loop(0, pc.count, step_body, 0)
    dwd_ref[...] = nt(inner[...], g_all[...]).astype(BF)
    scatter.late()
    part = width // 2
    for r in range(2):
        dwgu_ref[r * part : (r + 1) * part, :] = nt(
            x_all[r * part : (r + 1) * part, :], ggu[...]
        ).astype(BF)

    def store(total):
        residual = res_ref[...]
        scale_two = rms(residual)
        unit = residual * scale_two
        n1 = width // 128
        dsmall_ref[...] = rows_of(total * unit)
        u = total * column(padded_t(small_ref[layer]), n1, n1)
        gr_ref[...] = g_ref[...].astype(BF).astype(F32) + scale_two * (
            u - unit * jnp.mean(u * unit, axis=0, keepdims=True)
        )

    scatter.finish(store)
    gather.finish()


def feed_both(dims, cid, layer, x, residual, g, g_all, wgu, wd, small):
    width, rows = g.shape
    count = dims[0] * dims[2]
    two_ff, ff = (wgu.shape[1], wd.shape[0])
    sds = jax.ShapeDtypeStruct
    dma = pltpu.SemaphoreType.DMA
    return call(
        functools.partial(feed_both_kernel, dims, layer),
        "feed_both",
        cid,
        (
            sds((width, rows), F32),
            sds(wgu.shape, BF),
            sds(wd.shape, BF),
            sds((width // 128, 128), F32),
            sds((count, width, rows), BF),
        ),
        [VM] * 5,
        [VM] * 7,
        [
            pltpu.VMEM((width, count * rows), BF),
            pltpu.VMEM((ff, count * rows), BF),
            pltpu.VMEM((two_ff, count * rows), BF),
            pltpu.VMEM((two_ff, width), BF),
            pltpu.VMEM((width, ff), BF),
            pltpu.VMEM((two_ff, rows), F32),
            pltpu.VMEM((ff, rows), F32),
        ]
        + scatter_scratch(dims, width, rows)
        + gather_sems(dims),
        (x, residual, g, g_all, wgu, wd, small),
    )


def wait_for_weights(pc, riders, gather, wd_all, pieces, wd, sem, others):
    last_blocks(pc, gather)
    each(riders, "finish")
    load = pltpu.make_async_copy(wd_all, pieces, sem)
    load.start()
    each(others, "wait")
    load.wait()
    half = pieces.shape[1]
    for t in range(pc.nb):
        wd[t * half : (t + 1) * half, :] = pieces[t]
    gather.finish()


def lower_kernel(dims, nk, plan_a, plan_f, *refs):
    pc = Place(dims)
    a_in, wgu_in, refs = (refs[:8], refs[8], refs[9:])
    f_in, refs = (refs[: plan_f.count], refs[plan_f.count :])
    a_out, wd_all, qo_next, refs = (refs[:6], refs[6], refs[7], refs[8:])
    f_out, refs = (refs[: 3 + plan_f.count], refs[3 + plan_f.count :])
    n2, wgu, pieces, wd, wsem, dsem, refs = (*refs[:6], refs[6:])
    a_scratch, f_scratch = (refs[: 10 + len(plan_a.scratch) + 2], refs[10 + len(plan_a.scratch) + 2 :])
    load = pltpu.make_async_copy(wgu_in, wgu, wsem)
    load.start()
    riders, gather = attention_forward_part(
        pc, nk, 0, plan_a, "columns", *a_in, *a_out, n2, wd_all, qo_next, *a_scratch
    )
    feed_forward_part(
        pc,
        lambda: None,
        lambda: wait_for_weights(pc, riders, gather, wd_all, pieces, wd, dsem, [load]),
        plan_f, n2, a_out[5], wgu, wd, *f_in, *f_out, *f_scratch,
    )


def lower_layer(dims, nk, cid, hidden, small, docs, cos_part, sin_part, qo, plan_a, block,
                wgu, plan_f):
    ns, nb, nf = dims
    width, rows = hidden.shape
    count = ns * nf
    qkv = qo.shape[1] - width
    two_ff = wgu.shape[1]
    ff = two_ff // 2
    sds = jax.ShapeDtypeStruct
    dma = pltpu.SemaphoreType.DMA
    outs = [
        sds((width, rows), BF),
        sds((H, HD, rows), BF),
        sds((nk, 2 * KVH, HD, rows), BF),
        sds((H, 1, rows), F32),
        sds((H, HD, rows), BF),
        sds((width, rows), F32),
        *plan_a.shapes,
        sds((nb, nf, block.shape[2], ns * block.shape[3]), BF),
        sds((width, rows), F32),
        sds((width, count * rows), BF),
        sds((two_ff, count * rows), BF),
        *plan_f.shapes,
    ]
    out = call(
        functools.partial(lower_kernel, dims, nk, plan_a, plan_f),
        "lower_layer",
        cid,
        tuple(outs),
        [VM] * 6 + plan_a.outs + [VM] + [VM, AN, AN] + plan_f.outs,
        [VM] * 5 + [AN, VM] + plan_a.places + [AN] + plan_f.places,
        [
            pltpu.VMEM((width, rows), BF),
            pltpu.VMEM(wgu.shape, BF),
            pltpu.VMEM((nb, ff // nb, width), BF),
            pltpu.VMEM((ff, width), BF),
            dma(()),
            dma(()),
        ]
        + attention_scratch(dims, nk, width, rows, qkv)
        + plan_a.scratch
        + gather_sems(dims)
        + [
            pltpu.VMEM((width, count * rows), BF),
            pltpu.VMEM((two_ff, count * rows), BF),
            dma((2,)),
            pltpu.VMEM((two_ff, width), BF),
            pltpu.VMEM((width, ff), BF),
            pltpu.VMEM((two_ff, rows), F32),
            pltpu.VMEM((ff, rows), BF),
        ]
        + scatter_scratch(dims, width, rows)
        + gather_sems(dims)
        + plan_f.scratch,
        (hidden, small, docs, cos_part, sin_part, qo, block, *plan_a.arrays, wgu,
         *plan_f.arrays),
    )
    return (out[:6], out[6], out[7], out[8:11], out[11:])


def upper_kernel(dims, nk, plan, *refs):
    pc = Place(dims)
    a_in, g_ref, wgu_in, refs = (refs[:8], refs[8], refs[9], refs[10:])
    a_out, wd_all, f_out, refs = (refs[:6], refs[6], refs[7:12], refs[12:])
    n2, g_all, wgu, pieces, wd, wsem, dsem, refs = (*refs[:7], refs[7:])
    a_scratch, f_scratch = (refs[: 10 + len(plan.scratch) + 2], refs[10 + len(plan.scratch) + 2 :])
    load = pltpu.make_async_copy(wgu_in, wgu, wsem)
    load.start()
    riders, gather = attention_forward_part(
        pc, nk, 1, plan, "lanes", *a_in, *a_out, n2, wd_all, g_all, *a_scratch
    )
    feed_both_part(
        pc,
        lambda: None,
        lambda: wait_for_weights(pc, riders, gather, wd_all, pieces, wd, dsem, [load]),
        1, n2, a_out[5], g_ref, g_all, wgu, wd, a_in[1], *f_out, *f_scratch,
    )


def upper_layer(dims, nk, cid, hidden, small, docs, cos_part, sin_part, qo, plan, block, g,
                wgu):
    ns, nb, nf = dims
    width, rows = hidden.shape
    count = ns * nf
    qkv = qo.shape[1] - width
    two_ff = wgu.shape[1]
    ff = two_ff // 2
    sds = jax.ShapeDtypeStruct
    dma = pltpu.SemaphoreType.DMA
    outs = [
        sds((width, rows), BF),
        sds((H, HD, rows), BF),
        sds((nk, 2 * KVH, HD, rows), BF),
        sds((H, 1, rows), F32),
        sds((H, HD, rows), BF),
        sds((width, rows), F32),
        *plan.shapes,
        sds((width, rows), F32),
        sds(wgu.shape, BF),
        sds((ff, width), BF),
        sds((width // 128, 128), F32),
        sds((count, width, rows), BF),
    ]
    out = call(
        functools.partial(upper_kernel, dims, nk, plan),
        "upper_layer",
        cid,
        tuple(outs),
        [VM] * 6 + plan.outs + [VM] * 5,
        [VM] * 5 + [AN, VM] + plan.places + [VM, AN],
        [
            pltpu.VMEM((width, rows), BF),
            pltpu.VMEM((width, count * rows), BF),
            pltpu.VMEM(wgu.shape, BF),
            pltpu.VMEM((nb, ff // nb, width), BF),
            pltpu.VMEM((ff, width), BF),
            dma(()),
            dma(()),
        ]
        + attention_scratch(dims, nk, width, rows, qkv)
        + plan.scratch
        + gather_sems(dims)
        + [
            pltpu.VMEM((width, count * rows), BF),
            pltpu.VMEM((ff, count * rows), BF),
            pltpu.VMEM((two_ff, count * rows), BF),
            pltpu.VMEM((two_ff, width), BF),
            pltpu.VMEM((width, ff), BF),
            pltpu.VMEM((two_ff, rows), F32),
            pltpu.VMEM((ff, rows), F32),
        ]
        + scatter_scratch(dims, width, rows)
        + gather_sems(dims),
        (hidden, small, docs, cos_part, sin_part, qo, block, *plan.arrays, g, wgu),
    )
    return (out[:6], out[7:])


def reduce_kernel(
    dims, qo, terms, sa0, sa1, sb0, sb1, wd1, gu0a, gu0, wd0,
    qo_out, small_out, gu_got, wd_got,
    held, rest_gu, gsum, wsum, small, sm_in, sm_mid, sm_line, z_out, mine, give,
    lsem, ws, wr, ls, lr, zs, zr, *rest
):
    pc = Place(dims)
    ns, nb, nf = dims
    coming = pltpu.make_async_copy(qo, held, lsem.at[1])
    coming.start()
    cut = gu0a.shape[0]
    coming_gu = pltpu.make_async_copy(gu0.at[:, cut:nf], rest_gu, lsem.at[2])
    coming_gu.start()
    n1 = sb0.shape[0]
    per = small.shape[0] // ns
    nr = sa0.shape[0] + n1
    small[...] = jnp.zeros_like(small)
    for l, (a, g) in enumerate(((sa0, sb0), (sa1, sb1))):
        small[l * per : l * per + n1] = a[0:n1]
        small[l * per + n1 : l * per + 2 * n1] = g[...]
        small[l * per + 2 * n1 : l * per + nr] = a[n1 : a.shape[0]]
    greet(pc, "all", True)

    def keep(value):
        wsum[...] = value.astype(BF)

    def keep_of(l):
        def store(value):
            mine[l] = value

        return store

    line = LineReduce(pc, lambda t: wd0[t], keep, rest[0:4])
    ends = [
        LineReduce(pc, lambda t: z_out[t], keep_of(0), rest[4:8]),
        LineReduce(pc, lambda t: terms[t], keep_of(1), rest[8:12]),
    ]
    def keep_gu(value):
        gsum[...] = value.astype(BF)

    line_gu = LineReduce(pc, lambda t: rest_gu[t], keep_gu, rest[19:23])
    ends[1].start()
    coming_gu.wait()
    line_gu.start()
    line.start()
    scatter = ReadyScatter(
        pc, lambda q: columns_of(held, q, nf, z_out.shape[2]), *rest[15:19]
    )
    coming.wait()
    scatter.start()
    smalls = [
        remote(small, sm_in.at[e - 1], ls.at[e - 1], lr.at[e - 1], pc.plane(e))
        for e in range(1, pc.count)
    ]
    for c in smalls:
        c.start()
    scatter.diagonal()
    scatter.early()
    hand_out = RowSends(pc, 0, gu_got, rest[12:15])
    for f in range(cut):
        hand_out.start(f, gu0a.at[f])

    def split(l, ref):
        @pl.when(pc.s == l)
        def _():
            pltpu.make_async_copy(ref, wd_got.at[l], lsem.at[0]).start()

        @pl.when(pc.s != l)
        def _():
            remote(ref, wd_got.at[pc.s], ws.at[0], wr.at[0], (l, pc.b, pc.f)).start()

    split(1, wd1)
    ends[1].service()
    line_gu.service()
    line.service()
    scatter.late()
    ends[1].service()
    total = small[...]
    for e, c in enumerate(smalls):
        c.wait()
        total = total + sm_in[e]
    sm_mid[...] = total
    lines = [
        remote(sm_mid, sm_line.at[d - 1], zs.at[d - 1], zr.at[d - 1], pc.along(d))
        for d in range(1, nb)
    ]
    for c in lines:
        c.start()
    line_gu.service()
    line.service()

    def store(value):
        z_out[...] = value.astype(BF)

    scatter.finish(store)
    ends[0].start()
    ends[1].finish()
    line_gu.finish()
    for f in range(cut, nf):
        hand_out.start(f, gsum.at[f - cut])
    ends[0].service()
    line.finish()
    split(0, wsum)
    ends[0].finish()
    mate = (ns - 1 - pc.s, pc.b, pc.f)
    swap = remote(give.at[0], give.at[1], ws.at[1], wr.at[1], mate)
    give[0] = mine[ns - 1 - pc.s].astype(BF)
    swap.start()
    qo_out[pc.s] = mine[pc.s]
    total = sm_mid[...]
    for d, c in enumerate(lines):
        c.wait()
        total = total + sm_line[d]
    small_out[...] = total
    hand_out.finish(gu0a.at[0])
    pltpu.make_async_copy(wsum, wd_got.at[pc.s], lsem.at[0]).wait()
    remote(wsum, wd_got.at[pc.s], ws.at[0], wr.at[0], mate).wait()
    swap.wait()
    qo_out[ns - 1 - pc.s] = give[1].astype(F32)


def reduce_gradients(dims, cid, qo, terms, smalls, wd1, gu0a, gu0, wd0):
    ns, nb, nf = dims
    count = ns * nf
    dr, wide = terms.shape[1:]
    two_ff = gu0.shape[3]
    cut = gu0a.shape[0]
    half, width = wd1.shape
    rows = smalls[0].shape[0] + smalls[2].shape[0]
    small = (ns * (-(-rows // 8) * 8), 128)
    sds = jax.ShapeDtypeStruct
    dma = pltpu.SemaphoreType.DMA
    return call(
        functools.partial(reduce_kernel, dims),
        "reduce_gradients",
        cid,
        (
            sds((ns, dr, wide), F32),
            sds(small, F32),
            sds((count, dr, two_ff), BF),
            sds((ns, half, width), BF),
        ),
        [VM] * 4,
        [AN] + [VM] * 7 + [AN, VM],
        [
            pltpu.VMEM(qo.shape, BF),
            pltpu.VMEM((nb, nf - cut, dr, two_ff), BF),
            pltpu.VMEM((nf - cut, dr, two_ff), BF),
            pltpu.VMEM((half, width), BF),
            pltpu.VMEM(small, F32),
            pltpu.VMEM((count - 1,) + small, F32),
            pltpu.VMEM(small, F32),
            pltpu.VMEM((nb - 1,) + small, F32),
            pltpu.VMEM((nb, dr, wide), BF),
            pltpu.VMEM((ns, dr, wide), F32),
            pltpu.VMEM((2, dr, wide), BF),
            dma((3,)),
            dma((2,)),
            dma((2,)),
            dma((count - 1,)),
            dma((count - 1,)),
            dma((nb - 1,)),
            dma((nb - 1,)),
        ]
        + reduce_scratch(dims, half, width)
        + reduce_scratch(dims, dr, wide) * 2
        + row_scratch(dims)
        + scatter_scratch(dims, nb, dr, wide)[2:]
        + reduce_scratch(dims, nf - cut, dr, two_ff),
        (qo, terms, *smalls, wd1, gu0a, gu0, wd0),
    )


def last_kernel(dims, nk, plan, *refs):
    pc = Place(dims)
    ns, nb, nf = dims
    a_in, refs = (refs[:14], refs[14:])
    ab_in, refs = (refs[: plan.count], refs[plan.count :])
    sa1, sb0, sb1, wd1, wd0, give_out, gh1, refs = (*refs[:7], refs[7:])
    gh_ref, gu_got1, qo_out, small_out, gu_got, wd_got, take_out, take_grad = refs[:8]
    refs = refs[8:]
    held, sa0, gu0, terms, refs = (*refs[:4], refs[4:])
    wsum, small, sm_in, sm_mid, sm_line, z_out, mine, give, give_grad = refs[:9]
    lsem, ws, wr, ls, lr, zs, zr, refs = (*refs[9:16], refs[16:])
    n = 13 + len(plan.scratch) + 4 + 3 + 2
    ab_scratch, rest = (refs[:n], refs[n:])
    mate = (ns - 1 - pc.s, pc.b, pc.f)
    outs = remote(give_out, take_out, ws.at[2], wr.at[2], mate)
    grads = remote(give_grad, take_grad, ws.at[3], wr.at[3], mate)
    riders = attention_backward_part(
        pc, outs.start, held.shape[2], nk, 0, plan, "columns",
        *a_in, *ab_in, gh_ref, held, sa0, gu0, terms, gu_got1, *ab_scratch,
    )
    line_gu = riders[0]

    def keep(value):
        wsum[...] = value.astype(BF)

    def keep_of(l):
        def store(value):
            mine[l] = value

        return store

    line = LineReduce(pc, lambda t: wd0[t], keep, rest[0:4])
    ends = [
        LineReduce(pc, lambda t: z_out[t], keep_of(0), rest[4:8]),
        LineReduce(pc, lambda t: terms[t], keep_of(1), rest[8:12]),
    ]
    scatter = ReadyScatter(
        pc, lambda q: columns_of(held, q, nf, z_out.shape[2]), *rest[15:19]
    )
    scatter.start()
    ends[1].start()
    n1 = sb0.shape[0]
    per = small.shape[0] // ns
    nr = sa0.shape[0] + n1
    small[...] = jnp.zeros_like(small)
    for l, (a, g) in enumerate(((sa0, sb0), (sa1, sb1))):
        small[l * per : l * per + n1] = a[0:n1]
        small[l * per + n1 : l * per + 2 * n1] = g[...]
        small[l * per + 2 * n1 : l * per + nr] = a[n1 : a.shape[0]]
    smalls = [
        remote(small, sm_in.at[e - 1], ls.at[e - 1], lr.at[e - 1], pc.plane(e))
        for e in range(1, pc.count)
    ]
    for c in smalls:
        c.start()
    scatter.diagonal()
    scatter.early()

    @pl.when(pc.s == 0)
    def _():
        give_grad[...] = gh1[...].astype(BF)

    @pl.when(pc.s != 0)
    def _():
        give_grad[...] = gh_ref[...].astype(BF)

    def split(l, ref):
        @pl.when(pc.s == l)
        def _():
            pltpu.make_async_copy(ref, wd_got.at[l], lsem.at[0]).start()

        @pl.when(pc.s != l)
        def _():
            remote(ref, wd_got.at[pc.s], ws.at[0], wr.at[0], (l, pc.b, pc.f)).start()

    split(1, wd1)
    ends[1].service()
    scatter.late()
    grads.start()
    line.start()
    ends[1].service()
    line_gu.finish()
    hand_out = RowSends(pc, 0, gu_got, rest[12:15])
    for f in range(nf):
        hand_out.start(f, gu0.at[f])
    total = small[...]
    for e, c in enumerate(smalls):
        c.wait()
        total = total + sm_in[e]
    sm_mid[...] = total
    lines = [
        remote(sm_mid, sm_line.at[d - 1], zs.at[d - 1], zr.at[d - 1], pc.along(d))
        for d in range(1, nb)
    ]
    for c in lines:
        c.start()

    def store(value):
        z_out[...] = value.astype(BF)

    scatter.finish(store)
    ends[0].start()
    ends[1].finish()
    line.service()
    ends[0].service()
    ends[0].service()
    line.service()
    ends[0].finish()
    swap = remote(give.at[0], give.at[1], ws.at[1], wr.at[1], mate)
    give[0] = mine[ns - 1 - pc.s].astype(BF)
    swap.start()
    qo_out[pc.s] = mine[pc.s]
    total = sm_mid[...]
    for d, c in enumerate(lines):
        c.wait()
        total = total + sm_line[d]
    small_out[...] = total
    line.finish()
    split(0, wsum)
    hand_out.finish(gu0.at[0])
    outs.wait()
    grads.wait()
    swap.wait()
    qo_out[ns - 1 - pc.s] = give[1].astype(F32)
    pltpu.make_async_copy(wsum, wd_got.at[pc.s], lsem.at[0]).wait()
    remote(wsum, wd_got.at[pc.s], ws.at[0], wr.at[0], mate).wait()


def last_layer(dims, nk, cid, a_in, late, plan, smalls, wd1, wd0, give_out, gh1):
    ns, nb, nf = dims
    count = ns * nf
    width, rows = gh1.shape
    qkv = a_in[-1].shape[1] - width
    dr, cols = late[0].shape[2:]
    wide = cols // ns
    two_ff = late[1].shape[2]
    half = wd1.shape[0]
    n_small = smalls[0].shape[0] + smalls[1].shape[0]
    small = (ns * (-(-n_small // 8) * 8), 128)
    sds = jax.ShapeDtypeStruct
    dma = pltpu.SemaphoreType.DMA
    rows_all = sds((count, dr, two_ff), BF)
    return call(
        functools.partial(last_kernel, dims, nk, plan),
        "last_layer",
        cid,
        (
            sds((width, rows), F32),
            rows_all,
            sds((ns, dr, wide), F32),
            sds(small, F32),
            rows_all,
            sds((ns, half, width), BF),
            sds((width, rows), BF),
            sds((width, rows), BF),
        ),
        [VM, AN] + [VM] * 6,
        [VM] * 11 + [AN, AN, VM] + plan.places + [VM] * 7,
        [
            pltpu.VMEM(late[0].shape, BF),
            pltpu.VMEM(smalls[0].shape, F32),
            pltpu.VMEM((nf, dr, two_ff), BF),
            pltpu.VMEM((nb, dr, wide), BF),
            pltpu.VMEM((half, width), BF),
            pltpu.VMEM(small, F32),
            pltpu.VMEM((count - 1,) + small, F32),
            pltpu.VMEM(small, F32),
            pltpu.VMEM((nb - 1,) + small, F32),
            pltpu.VMEM((nb, dr, wide), BF),
            pltpu.VMEM((ns, dr, wide), F32),
            pltpu.VMEM((2, dr, wide), BF),
            pltpu.VMEM((width, rows), BF),
            dma((1,)),
            dma((4,)),
            dma((4,)),
            dma((count - 1,)),
            dma((count - 1,)),
            dma((nb - 1,)),
            dma((nb - 1,)),
        ]
        + backward_scratch(nk, width, rows, qkv)
        + plan.scratch
        + scatter_scratch(dims, nb, dr, wide)[2:]
        + row_scratch(dims)
        + [pltpu.VMEM(late[0].shape, BF), dma(())]
        + reduce_scratch(dims, half, width)
        + reduce_scratch(dims, dr, wide) * 2
        + row_scratch(dims)
        + scatter_scratch(dims, nb, dr, wide)[2:],
        (*a_in, *late, *plan.arrays, *smalls[0:1], *smalls[1:], wd1, wd0, give_out, gh1),
    )


def lay_out_kernel(
    dims, gu0, gu1, wd, qo, small, out0, out1, gh0, gh1, take_out, take_grad,
    block_out, input_grad, g1, wqkv, bqkv, wout, g2, wgu, wdn
):
    ns, nb, nf = dims
    half = wd.shape[1]
    s = lax.axis_index("section")
    qkv = wqkv.shape[2]
    width = wout.shape[2]
    full = jnp.concatenate([qo[y] for y in range(ns)], axis=1)
    wqkv[0] = full[:, :qkv]
    wout[0] = full[:, qkv:]
    for y in range(ns):
        wdn[0, y * half : (y + 1) * half, :] = wd[y].astype(F32)
    for l, gu in enumerate((gu0, gu1)):
        @pl.when(s == l)
        def _():
            for y in range(ns):
                for f in range(nf):
                    got = gu[y * nf + f].astype(F32)
                    for part in range(2):
                        for b in range(nb):
                            c0 = column_start(dims, part, b, f, y, half)
                            k0 = (part * nb + b) * half
                            wgu[0, :, c0 : c0 + half] = got[:, k0 : k0 + half]
    n1 = width // 128
    per = small.shape[0] // ns
    rows = small[pl.ds(pl.multiple_of(s * per, 8), per), :]
    for k in range(n1):
        g1[0:1, k * 128 : (k + 1) * 128] = rows[k : k + 1]
        g2[0:1, k * 128 : (k + 1) * 128] = rows[n1 + k : n1 + k + 1]
    for k in range(qkv // 128):
        bqkv[0:1, k * 128 : (k + 1) * 128] = rows[2 * n1 + k : 2 * n1 + k + 1]
    for out, pair, take in (
        (block_out, (out0, out1), take_out),
        (input_grad, (gh0, gh1), take_grad),
    ):
        for l in range(ns):
            @pl.when(s == l)
            def _():
                out[0, l] = pair[l][...].T
                out[0, 1 - l] = take[...].T.astype(F32)


def lay_out(dims, qkv, args):
    ns, nb, nf = dims
    gu, wd, qo = (args[0], args[2], args[3])
    width, rows = args[5].shape
    dr = qo.shape[1]
    sds = jax.ShapeDtypeStruct
    tokens = sds((1, ns, rows, width), F32)
    return pl.pallas_call(
        functools.partial(lay_out_kernel, dims),
        name="lay_out",
        out_shape=(
            tokens,
            tokens,
            sds((1, width), F32),
            sds((1, dr, qkv), F32),
            sds((1, qkv), F32),
            sds((1, dr, width), F32),
            sds((1, width), F32),
            sds((1, dr, gu.shape[0] * gu.shape[2]), F32),
            sds((1, ns * wd.shape[1], width), F32),
        ),
        in_specs=[VM] * len(args),
        out_specs=[VM] * 9,
        compiler_params=pltpu.CompilerParams(vmem_limit_bytes=VMEM_LIMIT),
    )(*args)


def shards(
    dims,
    tokens_in,
    positions,
    doc_ids,
    out_grad,
    norm1_gain,
    w_qkv,
    b_qkv,
    w_out,
    norm2_gain,
    w_gate_up,
    w_down,
):
    ns, nb, nf = dims
    seqs, rows, width = tokens_in.shape
    s = lax.axis_index("section")
    dr = w_qkv.shape[1]
    qkv = w_qkv.shape[2]
    fr = w_down.shape[1]
    half = fr // ns
    ff = nb * half
    nk = min(nb, 1 + (LONGEST - 1 + rows - 1) // rows)

    tokens = lax.dynamic_index_in_dim(tokens_in, s, 0, keepdims=False)
    cot = lax.dynamic_index_in_dim(out_grad, s, 0, keepdims=False)
    pos = lax.dynamic_index_in_dim(positions, s, 0, keepdims=False)
    freq = jnp.exp(jnp.arange(HD // 2, dtype=F32) * (-2.0 / HD) * math.log(1000000.0))
    phase = freq[:, None] * pos.astype(F32)[None, :]
    cos_part, sin_part = (jnp.cos(phase), jnp.sin(phase))
    hidden = tokens.T.astype(F32)
    g = cot.T.astype(F32)

    wd = w_down[0].reshape(ns, half, width)
    gup, wdp, gu_first, qo_first, qz, small_all = gather_weights(
        dims, w_gate_up, w_qkv, w_out, wd, (norm1_gain, norm2_gain, b_qkv)
    )
    cols = qkv + width
    wide = (width, 2 * ff)

    def ride(*pairs):
        return Riders(dims, tuple(a for a, _ in pairs), tuple(v for _, v in pairs))

    common = (small_all, doc_ids, cos_part, sin_part)
    qo0 = qo_first.reshape(width, cols)
    wgu0 = gu_first.reshape(wide)
    first = ride((("gather", 0), wdp))
    second = ride((("gather", 1), gup))
    third = ride((("gather", 1), wdp))
    together = half % 8 == 0
    if together:
        a0, wd0, qo1, f0, (gu1,) = lower_layer(
            dims, nk, 1, hidden, *common, qo0, first, qz, wgu0, second
        )
    else:
        a0, (wd0, qo1) = attention_forward(
            dims, nk, 1, 0, hidden, *common, qo0, first, "columns", qz
        )
        f0, (gu1,) = feed_forward(dims, 3, a0[6], a0[5], wgu0, wd0.reshape(ff, width), second)
    qo1 = qo1.reshape(width, cols)
    wd0 = wd0.reshape(ff, width)
    wgu1 = gu1.reshape(wide)
    if together:
        a1, b1 = upper_layer(dims, nk, 2, f0[0], *common, qo1, third, cot.T, g, wgu1)
    else:
        a1, (wd1, g_all) = attention_forward(
            dims, nk, 2, 1, f0[0], *common, qo1, third, "lanes", cot.T
        )
        wd1 = wd1.reshape(ff, width)
        b1 = feed_both(dims, 4, 1, a1[6], a1[5], g, g_all, wgu1, wd1, small_all)

    line_gu = (nb, nf, dr, 2 * ff)
    line_wd = (nb, half, width)
    line_qo = (nb, nf, dr, cols)
    everything = (0, half)
    ab1, (dwd1, out1) = attention_backward(
        dims, nk, 7, 1, b1[0], *common, f0[0], *a1[:5], qo1,
        ride((("reduce", everything), b1[2].reshape(line_wd))), "sum", (b1[4], a1[5]),
    )
    b0, (dgu1,) = feed_backward(
        dims, 6, 0, ab1[0], a0[5], f0[1], f0[2], wgu0, wd0, small_all,
        ride((("reduce", (0, nf)), b1[1].reshape(line_gu))),
    )
    dgu0 = b0[1].reshape(line_gu)
    swaps = [(0, 1), (1, 0)]
    give_out = jnp.where(s == 0, out1, f0[0]).astype(BF)
    if together and dr % 8 == 0:
        gh0, gu_got1, grad_qo, small_sum, gu_got0, wd_got, take_out, take_grad = last_layer(
            dims, nk, 8, (b0[0], *common, hidden, *a0[:5], qo0),
            (ab1[1].reshape(line_qo), dgu1), ride((("reduce", (0, nf)), dgu0)),
            (ab1[2], b0[3], b1[3]), dwd1, b0[2].reshape(line_wd), give_out, ab1[0],
        )
    else:
        cut = nf - nf // 4
        ab0, (dgu0a, terms, gu_got1) = attention_backward(
            dims, nk, 8, 0, b0[0], *common, hidden, *a0[:5], qo0,
            ride((("reduce", (0, cut)), dgu0)), "columns", (ab1[1].reshape(line_qo), dgu1),
        )
        gh0 = ab0[0]
        take_out = lax.ppermute(give_out, "section", swaps)
        take_grad = lax.ppermute(jnp.where(s == 0, ab1[0], gh0).astype(BF), "section", swaps)
        grad_qo, small_sum, gu_got0, wd_got = reduce_gradients(
            dims, 9, ab0[1].reshape(line_qo), terms,
            (ab0[2], ab1[2], b0[3], b1[3]), dwd1, dgu0a, dgu0, b0[2].reshape(line_wd),
        )
    return lay_out(
        dims,
        qkv,
        (gu_got0, gu_got1, wd_got, grad_qo, small_sum, f0[0], out1, gh0, ab1[0], take_out,
         take_grad),
    )


def solution(mesh):
    dims = (mesh.shape["section"], mesh.shape["blk"], mesh.shape["fsdp"])
    return jax.shard_map(
        functools.partial(shards, dims),
        mesh=mesh,
        in_specs=(
            P("fsdp", "blk", None),
            P("fsdp", "blk"),
            P("fsdp", None),
            P("fsdp", "blk", None),
            P("section", None),
            P("section", ("blk", "fsdp"), None),
            P("section", None),
            P("section", ("blk", "fsdp"), None),
            P("section", None),
            P("section", ("blk", "fsdp"), None),
            P("section", ("blk", "fsdp"), None),
        ),
        out_specs=(
            P("section", "fsdp", "blk", None),
            P("section", "fsdp", "blk", None),
            P("section", None),
            P("section", ("blk", "fsdp"), None),
            P("section", None),
            P("section", ("blk", "fsdp"), None),
            P("section", None),
            P("section", ("blk", "fsdp"), None),
            P("section", ("blk", "fsdp"), None),
        ),
        check_vma=False,
    )
```
